32 devices in a mesh: dp: 4 (over y, x), context: 2 (over core), tensor: 4 (over z).
Axes of the slice: x: 2, y: 2, z: 4, core: 2. Of those that a mesh axis runs over, the one named last changes fastest.
Arguments:
- inputs: bfloat16 [8, 1024, 2048], P('dp', 'context'), may hold values from -6 to 6
- cotangent: bfloat16 [8, 1024, 2048], P('dp', 'context'), may hold values from -6 to 6
- lengths: int32 [8], P('dp'), may hold values from 256 to 1024, as said below
- w_query: bfloat16 [2048, 2048], P(('dp', 'context'), 'tensor'), may hold values from -0.125 to 0.125
- key_projection_weight: bfloat16 [2048, 512], P(('dp', 'context'), 'tensor'), may hold values from -0.125 to 0.125
- value_projection_weight: bfloat16 [2048, 512], P(('dp', 'context'), 'tensor'), may hold values from -0.125 to 0.125
- w_output: bfloat16 [2048, 2048], P('tensor', ('dp', 'context')), may hold values from -2 to 2
- w_gate: bfloat16 [2048, 8192], P(('dp', 'context'), 'tensor'), may hold values from -0.125 to 0.125
- w_up: bfloat16 [2048, 8192], P(('dp', 'context'), 'tensor'), may hold values from -0.125 to 0.125
- w_down: bfloat16 [8192, 2048], P('tensor', ('dp', 'context')), may hold values from -0.0625 to 0.0625
- attn_gain: bfloat16 [2048], P(('dp', 'context')), may hold values from 0.5 to 1.5
- ffn_gain: bfloat16 [2048], P(('dp', 'context')), may hold values from 0.5 to 1.5
- query_gain: bfloat16 [64], replicated, may hold values from 0.5 to 1.5
- key_gain: bfloat16 [64], replicated, may hold values from 0.5 to 1.5
Outputs:
- output: bfloat16 [8, 1024, 2048], P('dp', ('context', 'tensor'))
- grad_inputs: float32 [8, 1024, 2048], P('dp', ('context', 'tensor'))
- grad_w_query: float32 [2048, 2048], P(('dp', 'context'), 'tensor')
- grad_w_key: float32 [2048, 512], P(('dp', 'context'), 'tensor')
- grad_w_value: float32 [2048, 512], P(('dp', 'context'), 'tensor')
- grad_w_output: float32 [2048, 2048], P('tensor', ('dp', 'context'))
- grad_w_gate: float32 [2048, 8192], P(('dp', 'context'), 'tensor')
- grad_w_up: float32 [2048, 8192], P(('dp', 'context'), 'tensor')
- grad_w_down: float32 [8192, 2048], P('tensor', ('dp', 'context'))
- grad_attn_gain: float32 [2048], P(('dp', 'context'))
- grad_ffn_gain: float32 [2048], P(('dp', 'context'))
- grad_query_gain: float32 [64], replicated
- grad_key_gain: float32 [64], replicated
- rms_values: float32 [3], replicated
The draws below stay inside these ranges and needn't reach their ends.
Inputs may be any that keep to these rules, and one draw needn't show every extreme that they name: `lengths`: in every draw one sequence, drawn from the seed, has all 1024 slots valid.
All inputs are finite; a program needn't handle non-finite values.
Results may differ from the reference program's by a relative error of at most 0.014.
Values may be sent and summed in bfloat16 or wider, within the bound.
A program may use at most 320 MiB of HBM per device.

```python
import math
import jax
import jax.numpy as jnp
from jax import lax

MODEL_WIDTH = 2048
QUERY_HEADS = 32
KEY_VALUE_HEADS = 8
HEAD_DIM = 64
FF = 8192
SEQUENCE_SLOTS = 1024
MIN_LEN = 256
NSEQ = 8


def draw_lengths(key, part):
    key = jax.random.fold_in(key, 11)
    values = jax.random.randint(key, (NSEQ,), MIN_LEN, SEQUENCE_SLOTS + 1, dtype=jnp.int32)
    chosen = jax.random.randint(jax.random.fold_in(key, 1), (), 0, NSEQ, dtype=jnp.int32)
    return jnp.where(jnp.arange(NSEQ, dtype=jnp.int32) == chosen, SEQUENCE_SLOTS, values).astype(jnp.int32)


def block_levels(rng, shape, shards, smallest, largest):
    level = 1.0
    for axis_at, parts in shards:
        steps = jax.random.uniform(jax.random.fold_in(jax.random.fold_in(rng, 6), axis_at), (parts,), jnp.float32, smallest / len(shards), largest / len(shards))
        level = level * jnp.repeat(jnp.exp(steps), shape[axis_at] // parts).reshape((-1,) + (1,) * (len(shape) - 1 - axis_at))
    return level


def noise(key, dims, spread, most, pieces=(), kind=jnp.bfloat16):
    drawn = spread * jax.random.normal(key, dims, jnp.float32)
    if pieces:
        drawn = drawn * block_levels(key, dims, pieces, -0.22, 0.18)
    return jnp.clip(drawn, -most, most).astype(kind)


def setup_inputs(seed: int = 0) -> dict:
    key_list = jax.random.split(jax.random.key(seed), 15)
    return {
        "inputs": noise(key_list[0], (NSEQ, SEQUENCE_SLOTS, MODEL_WIDTH), 1.0, 6.0, ((0, 4), (1, 2))),
        "cotangent": noise(key_list[1], (NSEQ, SEQUENCE_SLOTS, MODEL_WIDTH), 1.0, 6.0, ((0, 4), (1, 2))),
        "lengths": draw_lengths(jax.random.fold_in(key_list[14], 71), 0),
        "w_query": noise(key_list[3], (MODEL_WIDTH, QUERY_HEADS * HEAD_DIM), MODEL_WIDTH ** -0.5, 0.125, ((0, 8), (1, 4))),
        "key_projection_weight": noise(key_list[4], (MODEL_WIDTH, KEY_VALUE_HEADS * HEAD_DIM), MODEL_WIDTH ** -0.5, 0.125, ((0, 8), (1, 4))),
        "value_projection_weight": noise(key_list[5], (MODEL_WIDTH, KEY_VALUE_HEADS * HEAD_DIM), MODEL_WIDTH ** -0.5, 0.125, ((0, 8), (1, 4))),
        "w_output": noise(key_list[6], (QUERY_HEADS * HEAD_DIM, MODEL_WIDTH), (QUERY_HEADS * HEAD_DIM * 4 // SEQUENCE_SLOTS) ** -0.5, 2.0, ((0, 4), (1, 8))),
        "w_gate": noise(key_list[7], (MODEL_WIDTH, FF), MODEL_WIDTH ** -0.5, 0.125, ((0, 8), (1, 4))),
        "w_up": noise(key_list[8], (MODEL_WIDTH, FF), MODEL_WIDTH ** -0.5, 0.125, ((0, 8), (1, 4))),
        "w_down": noise(key_list[9], (FF, MODEL_WIDTH), FF ** -0.5, 0.0625, ((0, 4), (1, 8))),
        "attn_gain": jnp.clip(1.0 + 0.1 * jax.random.normal(key_list[10], (MODEL_WIDTH,), jnp.float32), 0.5, 1.5).astype(jnp.bfloat16),
        "ffn_gain": jnp.clip(1.0 + 0.1 * jax.random.normal(key_list[11], (MODEL_WIDTH,), jnp.float32), 0.5, 1.5).astype(jnp.bfloat16),
        "query_gain": jnp.clip(1.0 + 0.1 * jax.random.normal(key_list[12], (HEAD_DIM,), jnp.float32), 0.5, 1.5).astype(jnp.bfloat16),
        "key_gain": jnp.clip(1.0 + 0.1 * jax.random.normal(key_list[13], (HEAD_DIM,), jnp.float32), 0.5, 1.5).astype(jnp.bfloat16),
    }


epsilon = 1e-05
rope_base = 1000000.0
masked_score = -1e+30
highest = lax.Precision.HIGHEST

@jax.custom_vjp
def reduced_precision(v):
    return lax.optimization_barrier(v.astype(jnp.bfloat16)).astype(jnp.float32)

@jax.custom_vjp
def reduced_backward(v):
    return v

def low_keep(v):
    return (reduced_precision(v), None)

def low_pass(kept, grad):
    return (grad,)

def back_keep(v):
    return (v, None)

def back_low(kept, grad):
    return (reduced_precision(grad),)
reduced_precision.defvjp(low_keep, low_pass)
reduced_backward.defvjp(back_keep, back_low)

def matrix_product(left, right):
    return jnp.dot(left, right, precision=highest, preferred_element_type=jnp.float32)

def rms_norm(values, gain):
    return values * lax.rsqrt(lax.optimization_barrier(jnp.mean(values * values, axis=-1, keepdims=True)) + epsilon) * gain

def rope_angles(positions, width):
    half = width // 2
    freqs = rope_base ** (-(jnp.arange(half, dtype=jnp.float32) * (2.0 / width)))
    angles = positions.astype(jnp.float32)[:, None] * freqs[None, :]
    return (jnp.cos(angles), jnp.sin(angles))

def rotate(values, cosine, sine):
    half = values.shape[-1] // 2
    first = values[..., :half]
    second = values[..., half:]
    return jnp.concatenate([first * cosine - second * sine, second * cosine + first * sine], axis=-1)

def block_forward(params, values, length):
    w_query, key_projection_weight, value_projection_weight, w_output, w_gate, w_up, w_down, attn_gain, ffn_gain, query_gain, key_gain = params
    positions = jnp.arange(SEQUENCE_SLOTS, dtype=jnp.int32)
    cosine, sine = rope_angles(positions, HEAD_DIM)
    cosine = cosine[:, None, :]
    sine = sine[:, None, :]
    first_normed = reduced_precision(rms_norm(values, attn_gain))
    query_pre = reduced_backward(matrix_product(first_normed, w_query)).reshape(SEQUENCE_SLOTS, QUERY_HEADS, HEAD_DIM)
    key_before_norm = reduced_backward(matrix_product(first_normed, key_projection_weight)).reshape(SEQUENCE_SLOTS, KEY_VALUE_HEADS, HEAD_DIM)
    value_expanded = reduced_precision(reduced_backward(matrix_product(first_normed, value_projection_weight))).reshape(SEQUENCE_SLOTS, KEY_VALUE_HEADS, HEAD_DIM)
    query_reduced = reduced_precision(rotate(rms_norm(query_pre, query_gain), cosine, sine))
    key_low = reduced_precision(rotate(rms_norm(key_before_norm, key_gain), cosine, sine))
    allowed = (positions[None, :] <= positions[:, None]) & (positions[None, :] < length)
    queries_per_group = QUERY_HEADS // KEY_VALUE_HEADS
    score_scale = 1.0 / math.sqrt(HEAD_DIM)
    grouped_queries = query_reduced.reshape(SEQUENCE_SLOTS, KEY_VALUE_HEADS, queries_per_group, HEAD_DIM).transpose(1, 0, 2, 3)
    key_groups = key_low.transpose(1, 0, 2)
    value_groups = value_expanded.transpose(1, 0, 2)

    def attend(packed):
        query_part, key_part, value_part = packed
        scores = jnp.einsum('qre,ke->rqk', query_part, key_part, precision=highest, preferred_element_type=jnp.float32)
        scores = reduced_backward(scores * score_scale)
        scores = jnp.where(allowed[None], scores, masked_score)
        probs = reduced_precision(jax.nn.softmax(scores, axis=-1))
        return jnp.einsum('rqk,ke->qre', probs, value_part, precision=highest, preferred_element_type=jnp.float32)
    attended = lax.map(jax.checkpoint(attend), (grouped_queries, key_groups, value_groups))
    attended = reduced_precision(reduced_backward(attended.transpose(1, 0, 2, 3).reshape(SEQUENCE_SLOTS, QUERY_HEADS * HEAD_DIM)))
    attn_branch = reduced_backward(matrix_product(attended, w_output))
    hidden_state = values + attn_branch
    normed2 = reduced_precision(rms_norm(hidden_state, ffn_gain))
    gate_value = reduced_backward(matrix_product(normed2, w_gate))
    up_value = reduced_backward(matrix_product(normed2, w_up))
    inner = reduced_precision(jax.nn.silu(gate_value) * up_value)
    ffn_branch = reduced_backward(matrix_product(inner, w_down))
    return (hidden_state + ffn_branch, (attn_branch, ffn_branch))

def reference(inputs, cotangent, lengths, w_query, key_projection_weight, value_projection_weight, w_output, w_gate, w_up, w_down, attn_gain, ffn_gain, query_gain, key_gain):
    params = tuple((item.astype(jnp.float32) for item in (w_query, key_projection_weight, value_projection_weight, w_output, w_gate, w_up, w_down, attn_gain, ffn_gain, query_gain, key_gain)))
    zero_grads = tuple((jnp.zeros(item.shape, jnp.float32) for item in params))

    def per_sequence(carry, packed):
        totals, squares = carry
        seq_inputs, seq_cot, length = packed
        values = seq_inputs.astype(jnp.float32)
        row_mask = (jnp.arange(SEQUENCE_SLOTS, dtype=jnp.int32) < length).astype(jnp.float32)[:, None]

        def forward(weights, acts):
            return block_forward(weights, acts, length)
        result, pullback, branches = jax.vjp(forward, params, values, has_aux=True)
        grads, grad_values = pullback(seq_cot.astype(jnp.float32) * row_mask)
        totals = tuple((first + second for first, second in zip(totals, grads)))
        attn_branch, ffn_branch = branches
        squares = squares + jnp.stack([jnp.sum(row_mask * values * values), jnp.sum(row_mask * attn_branch * attn_branch), jnp.sum(row_mask * ffn_branch * ffn_branch)])
        return ((totals, squares), (result.astype(jnp.bfloat16), grad_values))
    (totals, squares), (output, grad_inputs) = lax.scan(per_sequence, (zero_grads, jnp.zeros((3,), jnp.float32)), (inputs, cotangent, lengths))
    count = jnp.sum(lengths).astype(jnp.float32) * MODEL_WIDTH
    rms_values = jnp.sqrt(squares / count)
    return (output, grad_inputs, totals[0], totals[1], totals[2], totals[3], totals[4], totals[5], totals[6], totals[7], totals[8], totals[9], totals[10], rms_values)
```

```python
import functools
import math

import jax
import jax.numpy as jnp
from jax import lax
from jax.experimental import pallas as pl
from jax.experimental.pallas import tpu as pltpu
from jax.sharding import PartitionSpec as P

F32 = jnp.float32
BF16 = jnp.bfloat16
epsilon = 1e-05
rope_base = 1000000.0
log2e = 1.4426950408889634
VMEM_BYTES = 60 * 1024 * 1024
PARAMS = pltpu.CompilerParams(vmem_limit_bytes=VMEM_BYTES)
SMEM = pl.BlockSpec(memory_space=pltpu.SMEM)
SWAP = ((0, 1), (1, 0))


def shape(dims, dtype):
    return jax.ShapeDtypeStruct(tuple(dims), dtype)


def cost(flops, size, exps=0):
    return pl.CostEstimate(flops=int(flops), bytes_accessed=int(size), transcendentals=int(exps))


def dot_nn(a, b):
    return lax.dot_general(a, b, (((1,), (0,)), ((), ())), preferred_element_type=F32)


def dot_nt(a, b):
    return lax.dot_general(a, b, (((1,), (1,)), ((), ())), preferred_element_type=F32)


def dot_tn(a, b):
    return lax.dot_general(a, b, (((0,), (0,)), ((), ())), preferred_element_type=F32)


def inverse_rms(values):
    return lax.rsqrt(jnp.mean(values * values, axis=-1, keepdims=True) + epsilon)


def tie(value, *others):
    return lax.optimization_barrier((value,) + others)[0]


def block_order(dp, row, core):
    if dp == 4:
        return jnp.stack([(row ^ k) * 2 + (core ^ o) for o in range(2) for k in range(dp)]).astype(jnp.int32)
    return jnp.stack([jnp.int32(k) * 2 + (core ^ o) for o in range(2) for k in range(dp)]).astype(jnp.int32)


def to_relative(values, dp, core):
    lead = values.shape[:-1]
    parts = values.reshape(lead + (dp, 2, -1))
    parts = jnp.where(core == 0, parts, parts[..., ::-1, :])
    return jnp.swapaxes(parts, -3, -2).reshape(values.shape)


def to_absolute(values, dp, core):
    lead = values.shape[:-1]
    parts = jnp.swapaxes(values.reshape(lead + (2, dp, -1)), -3, -2)
    return jnp.where(core == 0, parts, parts[..., ::-1, :]).reshape(values.shape)


def over_x(value):
    return lax.ppermute(value, "dp", [(i, i ^ 1) for i in range(4)])


def over_y(value):
    return lax.ppermute(value, "dp", [(i, i ^ 2) for i in range(4)])


def over_core(value):
    return lax.ppermute(value, "context", SWAP)


def gather_blocks(weight, axis, dp):
    if dp == 4:
        from_x = over_x(weight)
        from_y = over_y(weight)
        half = weight.shape[0] // 2
        first = over_x(from_y[:half])
        second = over_y(from_x[half:])
        if axis == 0:
            own = jnp.concatenate([weight, from_x, from_y, first, second], axis=0)
        else:
            diagonal = jnp.concatenate([first, second], axis=0)
            own = jnp.concatenate([weight, from_x, from_y, diagonal], axis=1)
        mark = from_x
    else:
        own = lax.all_gather(weight, "dp", axis=axis, tiled=True)
        mark = own
    return own, over_core(own), mark


def scatter_blocks(total, axis, dp):
    if dp != 4:
        return lax.psum_scatter(total, "dp", scatter_dimension=axis, tiled=True).astype(F32)
    piece = total.shape[axis] // 4
    half = piece // 2 if axis == 0 else total.shape[0] // 2

    def block(k):
        return lax.slice_in_dim(total, k * piece, (k + 1) * piece, axis=axis)

    diagonal = block(3)
    from_x = over_x(diagonal[:half])
    from_y = over_y(diagonal[half:])
    to_y = block(2)
    to_x = block(1)
    to_y = jnp.concatenate([to_y[:half].astype(F32) + from_x.astype(F32), to_y[half:].astype(F32)], axis=0).astype(BF16)
    to_x = jnp.concatenate([to_x[:half].astype(F32), to_x[half:].astype(F32) + from_y.astype(F32)], axis=0).astype(BF16)
    got_x = over_x(to_x)
    got_y = over_y(to_y)
    return block(0).astype(F32) + got_x.astype(F32) + got_y.astype(F32)


def sum_terms(part, tensor):
    if tensor != 4:
        return [lax.psum(part, "tensor")]
    inward = lax.ppermute(part, "tensor", [(0, 1), (3, 2)])
    pair = (part.astype(F32) + inward.astype(F32)).astype(BF16)
    across = lax.ppermute(pair, "tensor", [(1, 2), (2, 1)])
    rest = (part.astype(F32) + across.astype(F32)).astype(BF16)
    outward = lax.ppermute(rest, "tensor", [(1, 0), (2, 3)])
    return [part, inward, across, outward]


def ring_scatter(piece, tensor, rank):
    ring = [(i, (i + 1) % tensor) for i in range(tensor)]
    moving = piece((rank + tensor - 1) % tensor)
    for step in range(1, tensor):
        moving = lax.ppermute(moving, "tensor", ring)
        if step < tensor - 1:
            moving = (moving.astype(F32) + piece((rank + tensor - 1 - step) % tensor).astype(F32)).astype(BF16)
    return moving


def begin_kernel(order, x_ref, cot_ref, gain_ref, scal_ref, xr_ref, n1_ref, gf_ref):
    seq, tile = pl.program_id(0), pl.program_id(1)
    rows, width = x_ref.shape[1:]
    seqs = pl.num_programs(0)
    place = scal_ref[seqs] + tile * rows + lax.broadcasted_iota(jnp.int32, (rows, 1), 0)
    valid = (place < scal_ref[seq]).astype(F32)
    x = x_ref[0].astype(F32)
    inv = inverse_rms(x)
    piece = width // order
    for k in range(order):
        src = pl.ds(pl.multiple_of(scal_ref[seqs + 1 + k] * piece, piece), piece) if order > 1 else slice(0, width)
        dst = slice(k * piece, (k + 1) * piece)
        part = x_ref[0, :, src]
        xr_ref[0, :, dst] = part
        n1_ref[0, :, dst] = (part.astype(F32) * inv * gain_ref[:, dst]).astype(BF16)
        gf_ref[0, :, dst] = (cot_ref[0, :, src].astype(F32) * valid).astype(BF16)


def begin(x, cot, gain, scalars, order):
    seqs, span, width = x.shape
    rows = min(256, span)
    spec = pl.BlockSpec((1, rows, width), lambda s, i: (s, i, 0))
    return pl.pallas_call(
        functools.partial(begin_kernel, order),
        grid=(seqs, span // rows),
        in_specs=[spec, spec, pl.BlockSpec((1, width), lambda s, i: (0, 0)), SMEM],
        out_specs=[spec] * 3,
        out_shape=[shape(x.shape, BF16)] * 3,
        compiler_params=PARAMS,
        cost_estimate=cost(8 * x.size, 10 * x.size),
        name="first_norm",
    )(x, cot, gain, scalars)


def heads_kernel(hd, nq, nk, n1_ref, wo_ref, wx_ref, cos_ref, sin_ref, qg_ref, kg_ref, core_ref, pre_ref, own_ref, oth_ref):
    half = wo_ref.shape[0]
    x = n1_ref[0]
    flat = dot_nn(x[:, :half], wo_ref[...]) + dot_nn(x[:, half:], wx_ref[...])
    turned = flat.T
    span = turned.shape[1]
    normed = turned[: (nq + nk) * hd]
    pre_ref[...] = normed
    core = core_ref[0]
    cosine, sine = cos_ref[...], sin_ref[...]
    done = []
    for h in range(nq + nk):
        v = normed[h * hd : (h + 1) * hd]
        inv = lax.rsqrt(jnp.mean(v * v, axis=0, keepdims=True) + epsilon)
        v = v * inv * (qg_ref[...] if h < nq else kg_ref[...])
        a, b = v[: hd // 2], v[hd // 2 :]
        done.append(jnp.concatenate([a * cosine - b * sine, b * cosine + a * sine], axis=0))
    for h in range(nk):
        lo = (nq + nk + h) * hd
        done.append(turned[lo : lo + hd])
    parts = [[], []]
    for start, count in ((0, nq), (nq, nk), (nq + nk, nk)):
        for side in range(2):
            parts[side] += done[start + side * count // 2 : start + (side + 1) * count // 2]
    low = jnp.concatenate(parts[0], axis=0)
    high = jnp.concatenate(parts[1], axis=0)
    first = core == 0
    own_ref[...] = jnp.where(first, low, high).astype(BF16)
    oth_ref[...] = jnp.where(first, high, low).astype(BF16)


def heads(n1, seq, w_own, w_oth, cosine, sine, qgain, kgain, core, hd, nq, nk):
    span, width = n1.shape[1:]
    sides = (nq + 2 * nk) * hd // 2
    full = pl.BlockSpec(memory_space=pltpu.VMEM)
    whole = lambda a: pl.BlockSpec(a.shape, lambda i: (0,) * a.ndim)
    outs = [shape(((nq + nk) * hd, span), F32), shape((sides, span), BF16), shape((sides, span), BF16)]
    return pl.pallas_call(
        functools.partial(heads_kernel, hd, nq, nk),
        grid=(1,),
        in_specs=[pl.BlockSpec((1, span, width), lambda i: (seq, 0, 0))]
        + [whole(a) for a in (w_own, w_oth, cosine, sine, qgain, kgain)]
        + [SMEM],
        out_specs=[whole(o) for o in outs],
        out_shape=outs,
        compiler_params=PARAMS,
        cost_estimate=cost(2 * span * width * w_own.shape[1], 2 * span * width + 4 * w_own.size),
        name="query_key_value",
    )(n1, w_own, w_oth, cosine, sine, qgain, kgain, core)


def join_positions(core, own, oth):
    first = core == 0
    return jnp.where(first, own, oth), jnp.where(first, oth, own)


def attend_kernel(block, groups, scal_ref, own_ref, got_ref, all_ref, att_ref, inv_ref, ao_ref, ax_ref):
    span = own_ref.shape[1]
    hd = own_ref.shape[0] // (groups + 2)
    length, core = scal_ref[0], scal_ref[1]
    low, high = join_positions(core, own_ref[...], got_ref[...])
    all_ref[:, :span] = low
    all_ref[:, span:] = high
    scale = log2e / math.sqrt(hd)
    krow = lax.broadcasted_iota(jnp.int32, (block, groups * block), 0)
    qcol = lax.broadcasted_iota(jnp.int32, (block, groups * block), 1) % block
    base = groups * hd
    for i in range(2 * span // block):
        cut = slice(i * block, (i + 1) * block)
        q = jnp.concatenate([all_ref[g * hd : (g + 1) * hd, cut] for g in range(groups)], axis=1)
        acc = jnp.zeros((hd, groups * block), F32)
        total = jnp.zeros((1, groups * block), F32)
        for j in range(i + 1):
            kcut = slice(j * block, (j + 1) * block)
            s = dot_tn(all_ref[base : base + hd, kcut], q) * scale
            ok = (krow + j * block) < length
            if j == i:
                ok = ok & (krow <= qcol)
            e = jnp.where(ok, jnp.exp2(s), 0.0)
            total = total + jnp.sum(e, axis=0, keepdims=True)
            acc = acc + dot_nn(all_ref[base + hd : base + 2 * hd, kcut], e.astype(BF16))
        inv = 1.0 / total
        att = (acc * inv).astype(BF16)
        for g in range(groups):
            att_ref[g * hd : (g + 1) * hd, cut] = att[:, g * block : (g + 1) * block]
            inv_ref[g : g + 1, cut] = inv[:, g * block : (g + 1) * block]
    mine, theirs = join_positions(core, att_ref[:, :span], att_ref[:, span:])
    ao_ref[...] = mine
    ax_ref[...] = theirs


def attend(scalars, own, got, groups):
    rows, span = own.shape
    hd = rows // (groups + 2)
    block = min(256, span)
    full = pl.BlockSpec(memory_space=pltpu.VMEM)
    return pl.pallas_call(
        functools.partial(attend_kernel, block, groups),
        in_specs=[SMEM, full, full],
        out_specs=[full] * 5,
        out_shape=[
            shape((rows, 2 * span), BF16),
            shape((groups * hd, 2 * span), BF16),
            shape((groups, 2 * span), F32),
            shape((groups * hd, span), BF16),
            shape((groups * hd, span), BF16),
        ],
        compiler_params=PARAMS,
        cost_estimate=cost(60 * groups * hd * span * span, 12 * rows * span, 4 * groups * span * span),
        name="attend_forward",
    )(scalars, own, got)


def branch_kernel(own_ref, got_ref, wo_ref, wx_ref, core_ref, att_ref, *outs):
    half = wo_ref.shape[1]
    low, high = join_positions(core_ref[0], own_ref[...], got_ref[...])
    att = jnp.concatenate([low, high], axis=0)
    att_ref[...] = att
    rows = outs[0].shape[0]
    for k, out in enumerate(outs):
        part = att[:, k * rows : (k + 1) * rows]
        out[:, :half] = dot_tn(part, wo_ref[...]).astype(BF16)
        out[:, half:] = dot_tn(part, wx_ref[...]).astype(BF16)


def branch(own, got, w_own, w_oth, core, chunks):
    rows, span = own.shape
    width = 2 * w_own.shape[1]
    full = pl.BlockSpec(memory_space=pltpu.VMEM)
    return pl.pallas_call(
        branch_kernel,
        in_specs=[full] * 4 + [SMEM],
        out_specs=[full] * (1 + chunks),
        out_shape=[shape((2 * rows, span), BF16)] + [shape((span // chunks, width), BF16)] * chunks,
        compiler_params=PARAMS,
        cost_estimate=cost(4 * rows * span * width, 4 * rows * width + 2 * span * width),
        name="attention_branch",
    )(own, got, w_own, w_oth, core)


def second_norm_kernel(terms, scal_ref, x_ref, gain_ref, *refs):
    term_refs, (hidden_ref, n2_ref, stat_ref) = refs[:terms], refs[terms:]
    rows = hidden_ref.shape[0]
    branch_sum = term_refs[0][...].astype(F32)
    for ref in term_refs[1:]:
        branch_sum = branch_sum + ref[...].astype(F32)
    resid = x_ref[0].astype(F32)
    hidden = resid + branch_sum
    hidden_ref[...] = hidden
    n2_ref[...] = (hidden * inverse_rms(hidden) * gain_ref[...]).astype(BF16)
    place = scal_ref[1] + lax.broadcasted_iota(jnp.int32, (rows, 1), 0)
    valid = (place < scal_ref[0]).astype(F32)
    first = jnp.sum(valid * resid * resid, keepdims=True)
    second = jnp.sum(valid * branch_sum * branch_sum, keepdims=True)
    line = lax.broadcasted_iota(jnp.int32, (8, 128), 0)
    stat_ref[...] = jnp.where(line == 0, first, second)


def second_norm(scalars, xr, seq, part, gain, terms):
    rows, width = terms[0].shape
    flat = pl.BlockSpec((rows, width), lambda i: (0, 0))
    return pl.pallas_call(
        functools.partial(second_norm_kernel, len(terms)),
        grid=(1,),
        in_specs=[SMEM, pl.BlockSpec((1, rows, width), lambda i: (seq, part, 0)), pl.BlockSpec((1, width), lambda i: (0, 0))]
        + [flat] * len(terms),
        out_specs=[flat, flat, pl.BlockSpec((8, 128), lambda i: (0, 0))],
        out_shape=[shape((rows, width), F32), shape((rows, width), BF16), shape((8, 128), F32)],
        compiler_params=PARAMS,
        cost_estimate=cost(20 * rows * width, (8 + 2 * len(terms)) * rows * width),
        name="second_norm",
    )(scalars, xr, gain, *terms)


def feed_kernel(n_ref, g_ref, wgo, wgx, wuo, wux, wdo, wdx, inner_ref, gg_ref, gu_ref, ffn_ref, gn_ref, facc, gacc):
    step = pl.program_id(0)
    half = wgo.shape[0]
    no, nx = n_ref[:, :half], n_ref[:, half:]
    gate = dot_nn(no, wgo[...]) + dot_nn(nx, wgx[...])
    up = dot_nn(no, wuo[...]) + dot_nn(nx, wux[...])
    gi = dot_nt(g_ref[0, :, :half], wdo[...]) + dot_nt(g_ref[0, :, half:], wdx[...])
    sig = jax.nn.sigmoid(gate)
    silu = gate * sig
    inner = (silu * up).astype(BF16)
    gg = (gi * up * sig * (1.0 + gate * (1.0 - sig))).astype(BF16)
    gu = (gi * silu).astype(BF16)
    inner_ref[...] = inner
    gg_ref[...] = gg
    gu_ref[...] = gu

    @pl.when(step == 0)
    def _():
        facc[...] = jnp.zeros_like(facc)
        gacc[...] = jnp.zeros_like(gacc)

    facc[:, :half] += dot_nn(inner, wdo[...])
    facc[:, half:] += dot_nn(inner, wdx[...])
    gacc[:, :half] += dot_nt(gg, wgo[...]) + dot_nt(gu, wuo[...])
    gacc[:, half:] += dot_nt(gg, wgx[...]) + dot_nt(gu, wux[...])

    @pl.when(step == pl.num_programs(0) - 1)
    def _():
        ffn_ref[...] = facc[...].astype(BF16)
        gn_ref[...] = gacc[...].astype(BF16)


def feed(n2, gf, seq, part, wgo, wgx, wuo, wux, wdo, wdx):
    rows, width = n2.shape
    half, hidden = wgo.shape
    hb = min(512, hidden)
    row = pl.BlockSpec((half, hb), lambda h: (0, h))
    col = pl.BlockSpec((hb, half), lambda h: (h, 0))
    whole = pl.BlockSpec((rows, width), lambda h: (0, 0))
    tile = pl.BlockSpec((rows, hb), lambda h: (0, h))
    return pl.pallas_call(
        feed_kernel,
        grid=(hidden // hb,),
        in_specs=[whole, pl.BlockSpec((1, rows, width), lambda h: (seq, part, 0)), row, row, row, row, col, col],
        out_specs=[tile, tile, tile, whole, whole],
        out_shape=[shape((rows, hidden), BF16)] * 3 + [shape((rows, width), BF16)] * 2,
        scratch_shapes=[pltpu.VMEM((rows, width), F32), pltpu.VMEM((rows, width), F32)],
        compiler_params=PARAMS,
        cost_estimate=cost(12 * rows * width * hidden, 12 * half * hidden + 14 * rows * width, rows * hidden),
        name="feed_forward",
    )(n2, gf, wgo, wgx, wuo, wux, wdo, wdx)


def second_back_kernel(terms, hidden_ref, gf_ref, gain_ref, *refs):
    term_refs, (gb_ref, gh_ref, gain_out) = refs[:terms], refs[terms:]
    e = term_refs[0][...].astype(F32)
    for ref in term_refs[1:]:
        e = e + ref[...].astype(F32)
    hidden = hidden_ref[...]
    inv = inverse_rms(hidden)
    hat = hidden * inv
    eg = e * gain_ref[...]
    gh = gf_ref[0].astype(F32) + inv * (eg - hat * jnp.mean(eg * hat, axis=-1, keepdims=True))
    gh_ref[...] = gh
    gb_ref[...] = gh.astype(BF16)
    gain_out[...] = jnp.sum(e * hat, axis=0, keepdims=True)


def second_back(hidden, gf, seq, part, gain, terms):
    rows, width = hidden.shape
    flat = pl.BlockSpec((rows, width), lambda i: (0, 0))
    line = pl.BlockSpec((1, width), lambda i: (0, 0))
    return pl.pallas_call(
        functools.partial(second_back_kernel, len(terms)),
        grid=(1,),
        in_specs=[flat, pl.BlockSpec((1, rows, width), lambda i: (seq, part, 0)), line] + [flat] * len(terms),
        out_specs=[flat, flat, line],
        out_shape=[shape((rows, width), BF16), shape((rows, width), F32), shape((1, width), F32)],
        compiler_params=PARAMS,
        cost_estimate=cost(20 * rows * width, (12 + 2 * len(terms)) * rows * width),
        name="second_norm_back",
    )(hidden, gf, gain, *terms)


def branch_back_kernel(chunks, *refs):
    gb_refs, (wo_ref, wx_ref, core_ref, own_ref, oth_ref) = refs[:chunks], refs[chunks:]
    half = wo_ref.shape[1]
    rows = gb_refs[0].shape[0]
    heads_half = own_ref.shape[0]
    first = core_ref[0] == 0
    for k, ref in enumerate(gb_refs):
        da = dot_nt(wo_ref[...], ref[:, :half]) + dot_nt(wx_ref[...], ref[:, half:])
        da = da.astype(BF16)
        low, high = da[:heads_half], da[heads_half:]
        cut = slice(k * rows, (k + 1) * rows)
        own_ref[:, cut] = jnp.where(first, low, high)
        oth_ref[:, cut] = jnp.where(first, high, low)


def branch_back(gbs, w_own, w_oth, core):
    chunks = len(gbs)
    rows, width = gbs[0].shape
    dim = w_own.shape[0]
    full = pl.BlockSpec(memory_space=pltpu.VMEM)
    return pl.pallas_call(
        functools.partial(branch_back_kernel, chunks),
        in_specs=[full] * (chunks + 2) + [SMEM],
        out_specs=[full] * 2,
        out_shape=[shape((dim // 2, chunks * rows), BF16)] * 2,
        compiler_params=PARAMS,
        cost_estimate=cost(2 * dim * chunks * rows * width, 2 * dim * width + 2 * chunks * rows * width),
        name="attention_branch_back",
    )(*gbs, w_own, w_oth, core)


def attend_back_kernel(block, groups, scal_ref, all_ref, att_ref, inv_ref, own_ref, got_ref, out_own, out_oth, da_all, grads):
    span = own_ref.shape[1]
    hd = all_ref.shape[0] // (groups + 2)
    length, core = scal_ref[0], scal_ref[1]
    low, high = join_positions(core, own_ref[...], got_ref[...])
    da_all[:, :span] = low
    da_all[:, span:] = high
    scale = log2e / math.sqrt(hd)
    back = 1.0 / math.sqrt(hd)
    krow = lax.broadcasted_iota(jnp.int32, (block, groups * block), 0)
    qcol = lax.broadcasted_iota(jnp.int32, (block, groups * block), 1) % block
    base = groups * hd
    grads[base:, :] = jnp.zeros((2 * hd, 2 * span), F32)
    for i in range(2 * span // block):
        cut = slice(i * block, (i + 1) * block)

        def rows(ref):
            return jnp.concatenate([ref[g * hd : (g + 1) * hd, cut] for g in range(groups)], axis=1)

        q = rows(all_ref)
        da = rows(da_all)
        inv = jnp.concatenate([inv_ref[g : g + 1, cut] for g in range(groups)], axis=1)
        delta = jnp.sum(rows(att_ref).astype(F32) * da.astype(F32), axis=0, keepdims=True)
        dq = jnp.zeros((hd, groups * block), F32)
        for j in range(i + 1):
            kcut = slice(j * block, (j + 1) * block)
            key = all_ref[base : base + hd, kcut]
            s = dot_tn(key, q) * scale
            ok = (krow + j * block) < length
            if j == i:
                ok = ok & (krow <= qcol)
            p = jnp.where(ok, jnp.exp2(s) * inv, 0.0)
            dp = dot_tn(all_ref[base + hd : base + 2 * hd, kcut], da)
            ds = (p * (dp - delta)).astype(BF16)
            dq = dq + dot_nn(key, ds)
            grads[base : base + hd, kcut] += dot_nt(q, ds) * back
            grads[base + hd : base + 2 * hd, kcut] += dot_nt(da, p.astype(BF16))
        dq = dq * back
        for g in range(groups):
            grads[g * hd : (g + 1) * hd, cut] = dq[:, g * block : (g + 1) * block]
    mine, theirs = join_positions(core, grads[:, :span], grads[:, span:])
    out_own[...] = mine.astype(BF16)
    out_oth[...] = theirs.astype(BF16)


def attend_back(scalars, everything, att, inv, own, got, groups):
    rows, slots = everything.shape
    span = slots // 2
    block = min(256, span)
    full = pl.BlockSpec(memory_space=pltpu.VMEM)
    return pl.pallas_call(
        functools.partial(attend_back_kernel, block, groups),
        in_specs=[SMEM] + [full] * 5,
        out_specs=[full] * 2,
        out_shape=[shape((rows, span), BF16)] * 2,
        scratch_shapes=[pltpu.VMEM(att.shape, BF16), pltpu.VMEM((rows, slots), F32)],
        compiler_params=PARAMS,
        cost_estimate=cost(30 * att.shape[0] * slots * slots, 12 * rows * slots, groups * slots * slots),
        name="attend_backward",
    )(scalars, everything, att, inv, own, got)


def heads_back_kernel(hd, nq, nk, own_ref, got_ref, pre_ref, cos_ref, sin_ref, qg_ref, kg_ref, x_ref, wo_ref, wx_ref, core_ref, dpre_ref, first_ref, gain_ref, hgain_ref):
    half = wo_ref.shape[0]
    low, high = join_positions(core_ref[0], own_ref[...].astype(F32), got_ref[...].astype(F32))
    sides = (nq // 2, nk // 2, nk // 2)
    grads = [[], [], []]
    for side in (low, high):
        at = 0
        for kind, count in enumerate(sides):
            for h in range(count):
                grads[kind].append(side[at : at + hd])
                at += hd
    cosine, sine = cos_ref[...], sin_ref[...]
    done = []
    sums = [0.0, 0.0]
    for h in range(nq + nk):
        kind = 0 if h < nq else 1
        g = grads[kind][h - kind * nq]
        a, b = g[: hd // 2], g[hd // 2 :]
        g = jnp.concatenate([a * cosine + b * sine, b * cosine - a * sine], axis=0)
        v = pre_ref[h * hd : (h + 1) * hd, :]
        inv = lax.rsqrt(jnp.mean(v * v, axis=0, keepdims=True) + epsilon)
        hat = v * inv
        sums[kind] = sums[kind] + jnp.sum(g * hat, axis=1, keepdims=True)
        gg = g * (qg_ref[...] if kind == 0 else kg_ref[...])
        done.append(inv * (gg - hat * jnp.mean(gg * hat, axis=0, keepdims=True)))
    done += grads[2]
    hgain_ref[:hd, :] = jnp.broadcast_to(sums[0], (hd, 128))
    hgain_ref[hd:, :] = jnp.broadcast_to(sums[1], (hd, 128))
    dpre = jnp.concatenate(done, axis=0).T.astype(BF16)
    dpre_ref[...] = dpre
    x = x_ref[0].astype(F32)
    hat = x * inverse_rms(x)
    for k, ref in enumerate((wo_ref, wx_ref)):
        cut = slice(k * half, (k + 1) * half)
        part = dot_nt(dpre, ref[...])
        first_ref[:, cut] = part.astype(BF16)
        gain_ref[:, cut] = jnp.sum(part * hat[:, cut], axis=0, keepdims=True)


def heads_back(own, got, pre, cosine, sine, qgain, kgain, xr, seq, w_own, w_oth, core, hd, nq, nk):
    span = own.shape[1]
    half, cols = w_own.shape
    width = 2 * half
    whole = lambda a: pl.BlockSpec(a.shape, lambda i: (0,) * len(a.shape))
    outs = [shape((span, cols), BF16), shape((span, width), BF16), shape((1, width), F32), shape((2 * hd, 128), F32)]
    return pl.pallas_call(
        functools.partial(heads_back_kernel, hd, nq, nk),
        grid=(1,),
        in_specs=[whole(a) for a in (own, got, pre, cosine, sine, qgain, kgain)]
        + [pl.BlockSpec((1, span, width), lambda i: (seq, 0, 0)), whole(w_own), whole(w_oth), SMEM],
        out_specs=[whole(o) for o in outs],
        out_shape=outs,
        compiler_params=PARAMS,
        cost_estimate=cost(2 * span * width * cols, 4 * span * width + 4 * half * cols),
        name="query_key_value_back",
    )(own, got, pre, cosine, sine, qgain, kgain, xr, w_own, w_oth, core)


def place_blocks(order, ids, first_id, value, out_ref):
    piece = value.shape[-1] // order
    for k in range(order):
        if order == 1:
            out_ref[...] = value
        else:
            dst = pl.ds(pl.multiple_of(ids[first_id + k] * piece, piece), piece)
            out_ref[:, dst] = value[:, k * piece : (k + 1) * piece]


def output_kernel(order, scal_ref, got_ref, f0_ref, f1_ref, h0_ref, h1_ref, out_ref, stat_ref):
    low = scal_ref[0] * 2 < scal_ref[3]
    rows = out_ref.shape[0]
    ffn = got_ref[...].astype(F32) + jnp.where(low, f0_ref[...], f1_ref[...]).astype(F32)
    hidden = jnp.where(low, h0_ref[...], h1_ref[...])
    place = scal_ref[2] + lax.broadcasted_iota(jnp.int32, (rows, 1), 0)
    valid = (place < scal_ref[1]).astype(F32)
    stat_ref[...] = jnp.broadcast_to(jnp.sum(valid * ffn * ffn, keepdims=True), (8, 128))
    place_blocks(order, scal_ref, 4, (hidden + ffn).astype(BF16), out_ref)


def share_specs(rows, width, per):
    return [
        pl.BlockSpec((rows, width), lambda i, s: (jnp.minimum(s[0], per - 1), 0)),
        pl.BlockSpec((rows, width), lambda i, s: (jnp.maximum(s[0] - per, 0), 0)),
    ]


def output_share(scalars, got, ffns, hiddens, order):
    rows, width = got.shape
    pair = share_specs(rows, width, ffns[0].shape[0] // rows)
    flat = pl.BlockSpec((rows, width), lambda i, s: (0, 0))
    return pl.pallas_call(
        functools.partial(output_kernel, order),
        grid_spec=pltpu.PrefetchScalarGridSpec(
            num_scalar_prefetch=1,
            grid=(1,),
            in_specs=[flat] + pair + pair,
            out_specs=[flat, pl.BlockSpec((8, 128), lambda i, s: (0, 0))],
        ),
        out_shape=[shape((rows, width), BF16), shape((8, 128), F32)],
        compiler_params=PARAMS,
        cost_estimate=cost(6 * rows * width, 16 * rows * width),
        name="output_share",
    )(scalars, got, *ffns, *hiddens)


def input_kernel(order, scal_ref, got_ref, part_ref, g0_ref, g1_ref, x_ref, gain_ref, out_ref):
    low = scal_ref[0] * 2 < scal_ref[3]
    e = got_ref[...].astype(F32) + part_ref[...].astype(F32)
    gh = jnp.where(low, g0_ref[...], g1_ref[...])
    x = x_ref[0].astype(F32)
    inv = inverse_rms(x)
    hat = x * inv
    eg = e * gain_ref[...]
    value = gh + inv * (eg - hat * jnp.mean(eg * hat, axis=-1, keepdims=True))
    place_blocks(order, scal_ref, 4, value, out_ref)


def input_share(scalars, got, part, ghs, xr, seq, gain, order):
    rows, width = got.shape
    pair = share_specs(rows, width, ghs[0].shape[0] // rows)
    flat = pl.BlockSpec((rows, width), lambda i, s: (0, 0))
    return pl.pallas_call(
        functools.partial(input_kernel, order),
        grid_spec=pltpu.PrefetchScalarGridSpec(
            num_scalar_prefetch=1,
            grid=(1,),
            in_specs=[flat, pl.BlockSpec((rows, width), lambda i, s: (s[0], 0))]
            + pair
            + [pl.BlockSpec((1, rows, width), lambda i, s: (seq, s[0], 0)), pl.BlockSpec((1, width), lambda i, s: (0, 0))],
            out_specs=flat,
        ),
        out_shape=shape((rows, width), F32),
        compiler_params=PARAMS,
        cost_estimate=cost(12 * rows * width, 20 * rows * width),
        name="input_share",
    )(scalars, got, part, *ghs, xr, gain)


def weight_grad_kernel(count, extra, *refs):
    a_refs, b_refs, out = refs[:count], refs[count : 2 * count], refs[-1]
    total = dot_tn(a_refs[0][...], b_refs[0][...])
    for a, b in zip(a_refs[1:], b_refs[1:]):
        total = total + dot_tn(a[...], b[...])
    if extra:
        total = total + refs[2 * count][...].astype(F32)
    out[...] = total.astype(BF16)


def weight_grad(lefts, rights, side, axis, add=None):
    count = len(lefts)
    rows_all, cols_all = lefts[0].shape[1], rights[0].shape[1]
    dims = [rows_all, cols_all]
    dims[axis] //= 2
    rows, cols = min(512, dims[0]), min(2048, dims[1])
    row_at = side * (dims[0] // rows) if axis == 0 else 0
    col_at = side * (dims[1] // cols) if axis == 1 else 0
    specs = [pl.BlockSpec((a.shape[0], rows), lambda j, i: (0, i + row_at)) for a in lefts]
    specs += [pl.BlockSpec((b.shape[0], cols), lambda j, i: (0, j + col_at)) for b in rights]
    tile = pl.BlockSpec((rows, cols), lambda j, i: (i, j))
    tokens = sum(a.shape[0] for a in lefts)
    return pl.pallas_call(
        functools.partial(weight_grad_kernel, count, add is not None),
        grid=(dims[1] // cols, dims[0] // rows),
        in_specs=specs + ([tile] if add is not None else []),
        out_specs=tile,
        out_shape=shape(dims, BF16),
        compiler_params=PARAMS,
        cost_estimate=cost(2 * tokens * dims[0] * dims[1], 2 * tokens * sum(dims) + 2 * dims[0] * dims[1]),
        name="weight_grad",
    )(*lefts, *rights, *([add] if add is not None else []))


def per_device(
    inputs,
    cotangent,
    lengths,
    w_query,
    key_projection_weight,
    value_projection_weight,
    w_output,
    w_gate,
    w_up,
    w_down,
    attn_gain,
    ffn_gain,
    query_gain,
    key_gain,
):
    seqs, span, width = inputs.shape
    hd = query_gain.shape[0]
    nq = w_query.shape[1] // hd
    nk = key_projection_weight.shape[1] // hd
    groups = nq // nk
    dp = lax.axis_size("dp")
    tensor = lax.axis_size("tensor")
    row = lax.axis_index("dp")
    core = lax.axis_index("context")
    rank = lax.axis_index("tensor")
    chunks = 2
    rows = span // chunks
    share = span // tensor
    lengths = lengths.astype(jnp.int32)
    start = (core * span).astype(jnp.int32)
    core1 = core.astype(jnp.int32).reshape(1)
    ids = block_order(dp, row, core)
    order = 2 * dp if (width // (2 * dp)) % 128 == 0 else 1

    positions = start + jnp.arange(span, dtype=jnp.int32)
    freqs = rope_base ** (-(jnp.arange(hd // 2, dtype=F32) * (2.0 / hd)))
    angles = freqs[:, None] * positions.astype(F32)[None, :]
    cosine, sine = jnp.cos(angles), jnp.sin(angles)
    qgain = query_gain.astype(F32).reshape(hd, 1)
    kgain = key_gain.astype(F32).reshape(hd, 1)

    gains = jnp.stack([attn_gain, ffn_gain])
    g_own, g_oth, _ = gather_blocks(gains, 1, dp)
    gains = jnp.concatenate([g_own, g_oth], axis=1).astype(F32)
    gain1, gain2 = gains[0:1], gains[1:2]
    w_qkv = jnp.concatenate([w_query, key_projection_weight, value_projection_weight], axis=1)
    qkv_own, qkv_oth, mark = gather_blocks(w_qkv, 0, dp)
    out_own, out_oth, mark = gather_blocks(tie(w_output, mark), 1, dp)
    gate_own, gate_oth, mark = gather_blocks(tie(w_gate, mark), 0, dp)
    up_own, up_oth, mark = gather_blocks(tie(w_up, mark), 0, dp)
    down_own, down_oth, mark = gather_blocks(tie(w_down, mark), 1, dp)

    scal = jnp.concatenate([lengths, start.reshape(1), ids])
    x_in, cot_in = inputs, cotangent
    if order == 1:
        x_in, cot_in = to_relative(x_in, dp, core), to_relative(cot_in, dp, core)
    xr, n1, gf = begin(x_in, cot_in, gain1, scal, order)

    saved = []
    parts = []
    for s in range(seqs):
        pre, own, oth = heads(n1, s, qkv_own, qkv_oth, cosine, sine, qgain, kgain, core1, hd, nq, nk)
        seq_scal = jnp.stack([lengths[s], core.astype(jnp.int32)])
        everything, att, inv, mine, theirs = attend(seq_scal, own, over_core(oth), groups)
        branched = branch(mine, over_core(theirs), out_own, out_oth, core1, chunks)
        saved.append((pre, everything, att, inv, seq_scal, branched[0]))
        parts.append(branched[1:])

    stats = jnp.zeros((2,), F32)
    ffn_squares = jnp.zeros((), F32)
    hidden, n2, inner, gg, gu, ffn, gn = [[[None] * chunks for _ in range(seqs)] for _ in range(7)]
    out_shares = []
    for s in range(seqs):
        for k in range(chunks):
            terms = sum_terms(parts[s][k], tensor)
            place = jnp.stack([lengths[s], start + k * rows])
            hidden[s][k], n2[s][k], stat = second_norm(place, xr, s, k, gain2, terms)
            stats = stats + stat[:2, 0]
            inner[s][k], gg[s][k], gu[s][k], ffn[s][k], gn[s][k] = feed(
                n2[s][k], gf, s, k, gate_own, gate_oth, up_own, up_oth, down_own, down_oth
            )

    def piece_of(arrays):
        per = arrays[0].shape[0] // share

        def piece(k):
            found = lax.dynamic_slice_in_dim(arrays[0], jnp.minimum(k, per - 1) * share, share, 0)
            for m in range(1, len(arrays)):
                here = lax.dynamic_slice_in_dim(arrays[m], jnp.clip(k - m * per, 0, per - 1) * share, share, 0)
                found = jnp.where(k >= m * per, here, found)
            return found

        return piece

    def share_scalars(s):
        head = jnp.stack([rank.astype(jnp.int32), lengths[s], start + rank.astype(jnp.int32) * share, jnp.int32(tensor)])
        return jnp.concatenate([head, ids])

    gain2_grad = jnp.zeros((1, width), F32)
    gb, gh = [[[None] * chunks for _ in range(seqs)] for _ in range(2)]
    for s in range(seqs):
        for k in range(chunks):
            terms = sum_terms(gn[s][k], tensor)
            gb[s][k], gh[s][k], gain_part = second_back(hidden[s][k], gf, s, k, gain2, terms)
            gain2_grad = gain2_grad + gain_part
    for s in range(seqs):
        got = ring_scatter(piece_of(ffn[s]), tensor, rank)
        out, stat = output_share(share_scalars(s), got, ffn[s], hidden[s], order)
        out_shares.append(out)
        ffn_squares = ffn_squares + stat[0, 0]

    def flat(nested):
        return [item for inner_list in nested for item in inner_list]

    def reduced(lefts, rights, axis):
        oth = weight_grad(lefts, rights, 1, axis)
        own = weight_grad(lefts, rights, 0, axis, over_core(oth))
        return scatter_blocks(own, axis, dp)

    gf_chunks = [gf[s] for s in range(seqs)]
    inner_seq = flat(inner)
    gf_flat = [gf[s, k * rows : (k + 1) * rows] for s in range(seqs) for k in range(chunks)]
    grad_w_down = reduced(inner_seq, gf_flat, 1)
    grad_w_gate = reduced(flat(n2), flat(gg), 0)
    grad_w_up = reduced(flat(n2), flat(gu), 0)

    gain1_grad = jnp.zeros((1, width), F32)
    head_gain = jnp.zeros((2 * hd,), F32)
    dpres, in_shares = [], []
    for s in range(seqs):
        pre, everything, att, inv, seq_scal, att_rows = saved[s]
        da_own, da_oth = branch_back(gb[s], out_own, out_oth, core1)
        d_own, d_oth = attend_back(seq_scal, everything, att, inv, da_own, over_core(da_oth), groups)
        dpre, first, gain_part, hg = heads_back(
            d_own, over_core(d_oth), pre, cosine, sine, qgain, kgain, xr, s, qkv_own, qkv_oth, core1, hd, nq, nk
        )
        gain1_grad = gain1_grad + gain_part
        head_gain = head_gain + hg[:, 0]
        dpres.append(dpre)
        got = ring_scatter(piece_of([first]), tensor, rank)
        in_shares.append(input_share(share_scalars(s), got, first, gh[s], xr, s, gain1, order))

    att_rows = jnp.concatenate([jnp.swapaxes(saved[s][5], 0, 1) for s in range(seqs)], axis=0)
    att_list = [att_rows[i * rows : (i + 1) * rows] for i in range(seqs * chunks)]
    grad_w_output = reduced(att_list, flat(gb), 1)
    grad_qkv = reduced([n1[s] for s in range(seqs)], dpres, 0)
    nqc, nkc = nq * hd, nk * hd
    grad_w_query = grad_qkv[:, :nqc]
    grad_w_key = grad_qkv[:, nqc : nqc + nkc]
    grad_w_value = grad_qkv[:, nqc + nkc :]

    gain2_grad = gain2_grad / tensor
    counts = jnp.sum(jnp.clip(lengths - start, 0, span)).astype(F32) / tensor
    small = jnp.concatenate([head_gain, stats / tensor, ffn_squares.reshape(1), counts.reshape(1)])
    small = jnp.pad(small, (0, (-small.shape[0]) % 128)).reshape(1, -1)
    lines = jnp.concatenate([gain1_grad, gain2_grad], axis=0)
    if dp == 4 and tensor == 4:
        half = width // 2
        quarter = half // 4

        def join(part):
            return jnp.concatenate([part.reshape(1, -1), small], axis=1)

        got = over_core(join(lines[:, half:]))
        lines = lines[:, :half] + got[:, : 2 * half].reshape(2, half)
        small = small + got[:, 2 * half :]
        lines = lines.reshape(2, 4, quarter)
        got = over_x(join(lines[:, 1::2]))
        lines = lines[:, 0::2] + got[:, : 4 * quarter].reshape(2, 2, quarter)
        small = small + got[:, 4 * quarter :]
        got = over_y(join(lines[:, 1]))
        lines = lines[:, 0] + got[:, : 2 * quarter].reshape(2, quarter)
        small = small + got[:, 2 * quarter :]
        for step in (1, 2):
            got = lax.ppermute(join(lines), "tensor", [(i, i ^ step) for i in range(4)])
            lines = lines + got[:, : 2 * quarter].reshape(2, quarter)
            small = small + got[:, 2 * quarter :]
    else:
        piece = width // (2 * dp)
        lines = to_absolute(lines, dp, core) if dp != 4 else lines.reshape(2, 2 * dp, piece)[:, jnp.argsort(ids)].reshape(2, width)
        lines, small = lax.psum((lines, small), ("dp", "context", "tensor"))
        lines = lax.dynamic_slice_in_dim(lines, lax.axis_index(("dp", "context")) * piece, piece, 1)
    small = small[0]
    rms_values = jnp.sqrt(small[2 * hd : 2 * hd + 3] / (small[2 * hd + 3] * width))

    output = jnp.stack(out_shares)
    grad_inputs = jnp.stack(in_shares)
    if order == 1:
        output, grad_inputs = to_absolute(output, dp, core), to_absolute(grad_inputs, dp, core)
    return (
        output,
        grad_inputs,
        grad_w_query,
        grad_w_key,
        grad_w_value,
        grad_w_output,
        grad_w_gate,
        grad_w_up,
        grad_w_down,
        lines[0],
        lines[1],
        small[:hd],
        small[hd : 2 * hd],
        rms_values,
    )


def solution(mesh):
    both = ("dp", "context")
    rows = P(both, "tensor")
    cols = P("tensor", both)
    shares = P("dp", ("context", "tensor"), None)
    acts = P("dp", "context", None)
    return jax.shard_map(
        per_device,
        mesh=mesh,
        in_specs=(acts, acts, P("dp"), rows, rows, rows, cols, rows, rows, cols, P(both), P(both), P(), P()),
        out_specs=(shares, shares, rows, rows, rows, cols, rows, rows, cols, P(both), P(both), P(), P(), P()),
        check_vma=False,
    )
```

```python
import functools
import math

import jax
import jax.numpy as jnp
from jax import lax
from jax.experimental import pallas as pl
from jax.experimental.pallas import tpu as pltpu
from jax.sharding import PartitionSpec as P

F32 = jnp.float32
BF16 = jnp.bfloat16
epsilon = 1e-05
rope_base = 1000000.0
log2e = 1.4426950408889634
VMEM_BYTES = 60 * 1024 * 1024
PARAMS = pltpu.CompilerParams(vmem_limit_bytes=VMEM_BYTES)
SMEM = pl.BlockSpec(memory_space=pltpu.SMEM)
SWAP = ((0, 1), (1, 0))


def shape(dims, dtype):
    return jax.ShapeDtypeStruct(tuple(dims), dtype)


def cost(flops, size, exps=0):
    return pl.CostEstimate(flops=int(flops), bytes_accessed=int(size), transcendentals=int(exps))


def dot_nn(a, b):
    return lax.dot_general(a, b, (((1,), (0,)), ((), ())), preferred_element_type=F32)


def dot_nt(a, b):
    return lax.dot_general(a, b, (((1,), (1,)), ((), ())), preferred_element_type=F32)


def dot_tn(a, b):
    return lax.dot_general(a, b, (((0,), (0,)), ((), ())), preferred_element_type=F32)


def inverse_rms(values):
    return lax.rsqrt(jnp.mean(values * values, axis=-1, keepdims=True) + epsilon)


def tie(value, *others):
    return lax.optimization_barrier((value,) + others)[0]


def block_order(dp, row, core):
    if dp == 4:
        return jnp.stack([(row ^ k) * 2 + (core ^ o) for o in range(2) for k in range(dp)]).astype(jnp.int32)
    return jnp.stack([jnp.int32(k) * 2 + (core ^ o) for o in range(2) for k in range(dp)]).astype(jnp.int32)


def to_relative(values, dp, core):
    lead = values.shape[:-1]
    parts = values.reshape(lead + (dp, 2, -1))
    parts = jnp.where(core == 0, parts, parts[..., ::-1, :])
    return jnp.swapaxes(parts, -3, -2).reshape(values.shape)


def to_absolute(values, dp, core):
    lead = values.shape[:-1]
    parts = jnp.swapaxes(values.reshape(lead + (2, dp, -1)), -3, -2)
    return jnp.where(core == 0, parts, parts[..., ::-1, :]).reshape(values.shape)


def over_x(value):
    return lax.ppermute(value, "dp", [(i, i ^ 1) for i in range(4)])


def over_y(value):
    return lax.ppermute(value, "dp", [(i, i ^ 2) for i in range(4)])


def over_core(value):
    return lax.ppermute(value, "context", SWAP)


def gather_blocks(weight, axis, dp):
    if dp == 4:
        from_x = over_x(weight)
        from_y = over_y(weight)
        half = weight.shape[0] // 2
        first = over_x(from_y[:half])
        second = over_y(from_x[half:])
        if axis == 0:
            own = jnp.concatenate([weight, from_x, from_y, first, second], axis=0)
        else:
            diagonal = jnp.concatenate([first, second], axis=0)
            own = jnp.concatenate([weight, from_x, from_y, diagonal], axis=1)
        mark = from_x
    else:
        own = lax.all_gather(weight, "dp", axis=axis, tiled=True)
        mark = own
    return jnp.stack([own, over_core(own)]), mark


def scatter_blocks(total, axis, dp):
    if dp != 4:
        return lax.psum_scatter(total, "dp", scatter_dimension=axis, tiled=True).astype(F32)
    piece = total.shape[axis] // 4
    half = piece // 2 if axis == 0 else total.shape[0] // 2

    def block(k):
        return lax.slice_in_dim(total, k * piece, (k + 1) * piece, axis=axis)

    diagonal = block(3)
    from_x = over_x(diagonal[:half])
    from_y = over_y(diagonal[half:])
    to_y = block(2)
    to_x = block(1)
    to_y = jnp.concatenate([to_y[:half].astype(F32) + from_x.astype(F32), to_y[half:].astype(F32)], axis=0).astype(BF16)
    to_x = jnp.concatenate([to_x[:half].astype(F32), to_x[half:].astype(F32) + from_y.astype(F32)], axis=0).astype(BF16)
    got_x = over_x(to_x)
    got_y = over_y(to_y)
    return block(0).astype(F32) + got_x.astype(F32) + got_y.astype(F32)


def sum_terms(part, tensor):
    if tensor != 4:
        return [lax.psum(part, "tensor")]
    inward = lax.ppermute(part, "tensor", [(0, 1), (3, 2)])
    pair = (part.astype(F32) + inward.astype(F32)).astype(BF16)
    across = lax.ppermute(pair, "tensor", [(1, 2), (2, 1)])
    rest = (part.astype(F32) + across.astype(F32)).astype(BF16)
    outward = lax.ppermute(rest, "tensor", [(1, 0), (2, 3)])
    return [part, inward, across, outward]


def ring_scatter(piece, tensor, rank):
    ring = [(i, (i + 1) % tensor) for i in range(tensor)]
    moving = piece((rank + tensor - 1) % tensor)
    for step in range(1, tensor):
        moving = lax.ppermute(moving, "tensor", ring)
        if step < tensor - 1:
            moving = (moving.astype(F32) + piece((rank + tensor - 1 - step) % tensor).astype(F32)).astype(BF16)
    return moving


def begin_kernel(order, x_ref, cot_ref, gain_ref, scal_ref, xr_ref, n1_ref, gf_ref):
    seq, tile = pl.program_id(0), pl.program_id(1)
    rows, width = x_ref.shape[1:]
    seqs = pl.num_programs(0)
    place = scal_ref[seqs] + tile * rows + lax.broadcasted_iota(jnp.int32, (rows, 1), 0)
    valid = (place < scal_ref[seq]).astype(F32)
    x = x_ref[0].astype(F32)
    inv = inverse_rms(x)
    piece = width // order
    for k in range(order):
        src = pl.ds(pl.multiple_of(scal_ref[seqs + 1 + k] * piece, piece), piece) if order > 1 else slice(0, width)
        dst = slice(k * piece, (k + 1) * piece)
        part = x_ref[0, :, src]
        xr_ref[0, :, dst] = part
        n1_ref[0, :, dst] = (part.astype(F32) * inv * gain_ref[:, dst]).astype(BF16)
        gf_ref[0, :, dst] = (cot_ref[0, :, src].astype(F32) * valid).astype(BF16)


def begin(x, cot, gain, scalars, order):
    seqs, span, width = x.shape
    rows = min(256, span)
    spec = pl.BlockSpec((1, rows, width), lambda s, i: (s, i, 0))
    return pl.pallas_call(
        functools.partial(begin_kernel, order),
        grid=(seqs, span // rows),
        in_specs=[spec, spec, pl.BlockSpec((1, width), lambda s, i: (0, 0)), SMEM],
        out_specs=[spec] * 3,
        out_shape=[shape(x.shape, BF16)] * 3,
        compiler_params=PARAMS,
        cost_estimate=cost(8 * x.size, 10 * x.size),
        name="first_norm",
    )(x, cot, gain, scalars)


def heads_kernel(hd, nq, nk, n1_ref, w_ref, cos_ref, sin_ref, qg_ref, kg_ref, core_ref, pre_ref, own_ref, oth_ref):
    half = w_ref.shape[1]
    x = n1_ref[0]
    flat = dot_nn(x[:, :half], w_ref[0]) + dot_nn(x[:, half:], w_ref[1])
    turned = flat.T
    span = turned.shape[1]
    normed = turned[: (nq + nk) * hd]
    pre_ref[...] = normed
    core = core_ref[0]
    cosine, sine = cos_ref[...], sin_ref[...]
    done = []
    for h in range(nq + nk):
        v = normed[h * hd : (h + 1) * hd]
        inv = lax.rsqrt(jnp.mean(v * v, axis=0, keepdims=True) + epsilon)
        v = v * inv * (qg_ref[...] if h < nq else kg_ref[...])
        a, b = v[: hd // 2], v[hd // 2 :]
        done.append(jnp.concatenate([a * cosine - b * sine, b * cosine + a * sine], axis=0))
    for h in range(nk):
        lo = (nq + nk + h) * hd
        done.append(turned[lo : lo + hd])
    parts = [[], []]
    for start, count in ((0, nq), (nq, nk), (nq + nk, nk)):
        for side in range(2):
            parts[side] += done[start + side * count // 2 : start + (side + 1) * count // 2]
    low = jnp.concatenate(parts[0], axis=0)
    high = jnp.concatenate(parts[1], axis=0)
    first = core == 0
    own_ref[...] = jnp.where(first, low, high).astype(BF16)
    oth_ref[...] = jnp.where(first, high, low).astype(BF16)


def heads(n1, seq, weight, cosine, sine, qgain, kgain, core, hd, nq, nk):
    span, width = n1.shape[1:]
    sides = (nq + 2 * nk) * hd // 2
    full = pl.BlockSpec(memory_space=pltpu.VMEM)
    whole = lambda a: pl.BlockSpec(a.shape, lambda i: (0,) * a.ndim)
    outs = [shape(((nq + nk) * hd, span), F32), shape((sides, span), BF16), shape((sides, span), BF16)]
    return pl.pallas_call(
        functools.partial(heads_kernel, hd, nq, nk),
        grid=(1,),
        in_specs=[pl.BlockSpec((1, span, width), lambda i: (seq, 0, 0))]
        + [whole(a) for a in (weight, cosine, sine, qgain, kgain)]
        + [SMEM],
        out_specs=[whole(o) for o in outs],
        out_shape=outs,
        compiler_params=PARAMS,
        cost_estimate=cost(2 * span * width * weight.shape[2], 2 * span * width + 2 * weight.size),
        name="query_key_value",
    )(n1, weight, cosine, sine, qgain, kgain, core)


def join_positions(core, own, oth):
    first = core == 0
    return jnp.where(first, own, oth), jnp.where(first, oth, own)


def attend_kernel(block, groups, scal_ref, own_ref, got_ref, all_ref, att_ref, inv_ref, ao_ref, ax_ref):
    span = own_ref.shape[1]
    hd = own_ref.shape[0] // (groups + 2)
    length, core = scal_ref[0], scal_ref[1]
    low, high = join_positions(core, own_ref[...], got_ref[...])
    all_ref[:, :span] = low
    all_ref[:, span:] = high
    scale = log2e / math.sqrt(hd)
    krow = lax.broadcasted_iota(jnp.int32, (block, groups * block), 0)
    qcol = lax.broadcasted_iota(jnp.int32, (block, groups * block), 1) % block
    base = groups * hd
    for i in range(2 * span // block):
        cut = slice(i * block, (i + 1) * block)
        q = jnp.concatenate([all_ref[g * hd : (g + 1) * hd, cut] for g in range(groups)], axis=1)
        acc = jnp.zeros((hd, groups * block), F32)
        total = jnp.zeros((1, groups * block), F32)
        for j in range(i + 1):
            kcut = slice(j * block, (j + 1) * block)
            s = dot_tn(all_ref[base : base + hd, kcut], q) * scale
            ok = (krow + j * block) < length
            if j == i:
                ok = ok & (krow <= qcol)
            e = jnp.where(ok, jnp.exp2(s), 0.0)
            total = total + jnp.sum(e, axis=0, keepdims=True)
            acc = acc + dot_nn(all_ref[base + hd : base + 2 * hd, kcut], e.astype(BF16))
        inv = 1.0 / total
        att = (acc * inv).astype(BF16)
        for g in range(groups):
            att_ref[g * hd : (g + 1) * hd, cut] = att[:, g * block : (g + 1) * block]
            inv_ref[g : g + 1, cut] = inv[:, g * block : (g + 1) * block]
    mine, theirs = join_positions(core, att_ref[:, :span], att_ref[:, span:])
    ao_ref[...] = mine
    ax_ref[...] = theirs


def attend(scalars, own, got, groups):
    rows, span = own.shape
    hd = rows // (groups + 2)
    block = min(256, span)
    full = pl.BlockSpec(memory_space=pltpu.VMEM)
    return pl.pallas_call(
        functools.partial(attend_kernel, block, groups),
        in_specs=[SMEM, full, full],
        out_specs=[full] * 5,
        out_shape=[
            shape((rows, 2 * span), BF16),
            shape((groups * hd, 2 * span), BF16),
            shape((groups, 2 * span), F32),
            shape((groups * hd, span), BF16),
            shape((groups * hd, span), BF16),
        ],
        compiler_params=PARAMS,
        cost_estimate=cost(60 * groups * hd * span * span, 12 * rows * span, 4 * groups * span * span),
        name="attend_forward",
    )(scalars, own, got)


def branch_kernel(own_ref, got_ref, w_ref, core_ref, att_ref, *outs):
    half = w_ref.shape[2]
    low, high = join_positions(core_ref[0], own_ref[...], got_ref[...])
    att = jnp.concatenate([low, high], axis=0)
    att_ref[...] = att
    rows = outs[0].shape[0]
    for k, out in enumerate(outs):
        part = att[:, k * rows : (k + 1) * rows]
        out[:, :half] = dot_tn(part, w_ref[0]).astype(BF16)
        out[:, half:] = dot_tn(part, w_ref[1]).astype(BF16)


def branch(own, got, weight, core, chunks):
    rows, span = own.shape
    width = 2 * weight.shape[2]
    full = pl.BlockSpec(memory_space=pltpu.VMEM)
    return pl.pallas_call(
        branch_kernel,
        in_specs=[full] * 3 + [SMEM],
        out_specs=[full] * (1 + chunks),
        out_shape=[shape((2 * rows, span), BF16)] + [shape((span // chunks, width), BF16)] * chunks,
        compiler_params=PARAMS,
        cost_estimate=cost(4 * rows * span * width, 4 * rows * width + 2 * span * width),
        name="attention_branch",
    )(own, got, weight, core)


def second_norm_kernel(terms, scal_ref, x_ref, gain_ref, *refs):
    term_refs, (hidden_ref, n2_ref, stat_ref) = refs[:terms], refs[terms:]
    rows = hidden_ref.shape[0]
    branch_sum = term_refs[0][...].astype(F32)
    for ref in term_refs[1:]:
        branch_sum = branch_sum + ref[...].astype(F32)
    resid = x_ref[0].astype(F32)
    hidden = resid + branch_sum
    hidden_ref[...] = hidden
    n2_ref[...] = (hidden * inverse_rms(hidden) * gain_ref[...]).astype(BF16)
    place = scal_ref[1] + lax.broadcasted_iota(jnp.int32, (rows, 1), 0)
    valid = (place < scal_ref[0]).astype(F32)
    first = jnp.sum(valid * resid * resid, keepdims=True)
    second = jnp.sum(valid * branch_sum * branch_sum, keepdims=True)
    line = lax.broadcasted_iota(jnp.int32, (8, 128), 0)
    stat_ref[...] = jnp.where(line == 0, first, second)


def second_norm(scalars, xr, seq, part, gain, terms):
    rows, width = terms[0].shape
    flat = pl.BlockSpec((rows, width), lambda i: (0, 0))
    return pl.pallas_call(
        functools.partial(second_norm_kernel, len(terms)),
        grid=(1,),
        in_specs=[SMEM, pl.BlockSpec((1, rows, width), lambda i: (seq, part, 0)), pl.BlockSpec((1, width), lambda i: (0, 0))]
        + [flat] * len(terms),
        out_specs=[flat, flat, pl.BlockSpec((8, 128), lambda i: (0, 0))],
        out_shape=[shape((rows, width), F32), shape((rows, width), BF16), shape((8, 128), F32)],
        compiler_params=PARAMS,
        cost_estimate=cost(20 * rows * width, (8 + 2 * len(terms)) * rows * width),
        name="second_norm",
    )(scalars, xr, gain, *terms)


def feed_kernel(n_ref, g_ref, wgo, wgx, wuo, wux, wdo, wdx, inner_ref, gg_ref, gu_ref, ffn_ref, gn_ref, facc, gacc):
    step = pl.program_id(0)
    half = wgo.shape[0]
    no, nx = n_ref[:, :half], n_ref[:, half:]
    gate = dot_nn(no, wgo[...]) + dot_nn(nx, wgx[...])
    up = dot_nn(no, wuo[...]) + dot_nn(nx, wux[...])
    gi = dot_nt(g_ref[0, :, :half], wdo[...]) + dot_nt(g_ref[0, :, half:], wdx[...])
    sig = jax.nn.sigmoid(gate)
    silu = gate * sig
    inner = (silu * up).astype(BF16)
    gg = (gi * up * sig * (1.0 + gate * (1.0 - sig))).astype(BF16)
    gu = (gi * silu).astype(BF16)
    inner_ref[...] = inner
    gg_ref[...] = gg
    gu_ref[...] = gu

    @pl.when(step == 0)
    def _():
        facc[...] = jnp.zeros_like(facc)
        gacc[...] = jnp.zeros_like(gacc)

    facc[:, :half] += dot_nn(inner, wdo[...])
    facc[:, half:] += dot_nn(inner, wdx[...])
    gacc[:, :half] += dot_nt(gg, wgo[...]) + dot_nt(gu, wuo[...])
    gacc[:, half:] += dot_nt(gg, wgx[...]) + dot_nt(gu, wux[...])

    @pl.when(step == pl.num_programs(0) - 1)
    def _():
        ffn_ref[...] = facc[...].astype(BF16)
        gn_ref[...] = gacc[...].astype(BF16)


def feed(n2, chunk, rows, gf, seq, part, gate, up, down):
    width = n2.shape[1]
    _, half, hidden = gate.shape
    hb = min(512, hidden)
    row = [pl.BlockSpec((None, half, hb), lambda h, side=side: (side, 0, h)) for side in range(2)]
    col = [pl.BlockSpec((None, hb, half), lambda h, side=side: (side, h, 0)) for side in range(2)]
    whole = pl.BlockSpec((rows, width), lambda h: (0, 0))
    tile = pl.BlockSpec((rows, hb), lambda h: (0, h))
    return pl.pallas_call(
        feed_kernel,
        grid=(hidden // hb,),
        in_specs=[pl.BlockSpec((rows, width), lambda h: (chunk, 0)), pl.BlockSpec((1, rows, width), lambda h: (seq, part, 0))] + row + row + col,
        out_specs=[tile, tile, tile, whole, whole],
        out_shape=[shape((rows, hidden), BF16)] * 3 + [shape((rows, width), BF16)] * 2,
        scratch_shapes=[pltpu.VMEM((rows, width), F32), pltpu.VMEM((rows, width), F32)],
        compiler_params=PARAMS,
        cost_estimate=cost(12 * rows * width * hidden, 12 * half * hidden + 14 * rows * width, rows * hidden),
        name="feed_forward",
    )(n2, gf, gate, gate, up, up, down, down)


def second_back_kernel(terms, hidden_ref, gf_ref, gain_ref, *refs):
    term_refs, (gb_ref, gh_ref, gain_out) = refs[:terms], refs[terms:]
    e = term_refs[0][...].astype(F32)
    for ref in term_refs[1:]:
        e = e + ref[...].astype(F32)
    hidden = hidden_ref[...]
    inv = inverse_rms(hidden)
    hat = hidden * inv
    eg = e * gain_ref[...]
    gh = gf_ref[0].astype(F32) + inv * (eg - hat * jnp.mean(eg * hat, axis=-1, keepdims=True))
    gh_ref[...] = gh
    gb_ref[...] = gh.astype(BF16)
    gain_out[...] = jnp.sum(e * hat, axis=0, keepdims=True)


def second_back(hidden, chunk, gf, seq, part, gain, terms):
    rows, width = terms[0].shape
    flat = pl.BlockSpec((rows, width), lambda i: (0, 0))
    line = pl.BlockSpec((1, width), lambda i: (0, 0))
    return pl.pallas_call(
        functools.partial(second_back_kernel, len(terms)),
        grid=(1,),
        in_specs=[pl.BlockSpec((rows, width), lambda i: (chunk, 0)), pl.BlockSpec((1, rows, width), lambda i: (seq, part, 0)), line]
        + [flat] * len(terms),
        out_specs=[flat, flat, line],
        out_shape=[shape((rows, width), BF16), shape((rows, width), F32), shape((1, width), F32)],
        compiler_params=PARAMS,
        cost_estimate=cost(20 * rows * width, (12 + 2 * len(terms)) * rows * width),
        name="second_norm_back",
    )(hidden, gf, gain, *terms)


def branch_back_kernel(chunks, *refs):
    gb_refs, (w_ref, core_ref, own_ref, oth_ref) = refs[:chunks], refs[chunks:]
    half = w_ref.shape[2]
    rows = gb_refs[0].shape[0]
    heads_half = own_ref.shape[0]
    first = core_ref[0] == 0
    for k, ref in enumerate(gb_refs):
        da = dot_nt(w_ref[0], ref[:, :half]) + dot_nt(w_ref[1], ref[:, half:])
        da = da.astype(BF16)
        low, high = da[:heads_half], da[heads_half:]
        cut = slice(k * rows, (k + 1) * rows)
        own_ref[:, cut] = jnp.where(first, low, high)
        oth_ref[:, cut] = jnp.where(first, high, low)


def branch_back(gbs, weight, core):
    chunks = len(gbs)
    rows, width = gbs[0].shape
    dim = weight.shape[1]
    full = pl.BlockSpec(memory_space=pltpu.VMEM)
    return pl.pallas_call(
        functools.partial(branch_back_kernel, chunks),
        in_specs=[full] * (chunks + 1) + [SMEM],
        out_specs=[full] * 2,
        out_shape=[shape((dim // 2, chunks * rows), BF16)] * 2,
        compiler_params=PARAMS,
        cost_estimate=cost(2 * dim * chunks * rows * width, 2 * dim * width + 2 * chunks * rows * width),
        name="attention_branch_back",
    )(*gbs, weight, core)


def attend_back_kernel(block, groups, scal_ref, all_ref, att_ref, inv_ref, own_ref, got_ref, out_own, out_oth, da_all, grads):
    span = own_ref.shape[1]
    hd = all_ref.shape[0] // (groups + 2)
    length, core = scal_ref[0], scal_ref[1]
    low, high = join_positions(core, own_ref[...], got_ref[...])
    da_all[:, :span] = low
    da_all[:, span:] = high
    scale = log2e / math.sqrt(hd)
    back = 1.0 / math.sqrt(hd)
    krow = lax.broadcasted_iota(jnp.int32, (block, groups * block), 0)
    qcol = lax.broadcasted_iota(jnp.int32, (block, groups * block), 1) % block
    base = groups * hd
    grads[base:, :] = jnp.zeros((2 * hd, 2 * span), F32)
    for i in range(2 * span // block):
        cut = slice(i * block, (i + 1) * block)

        def rows(ref):
            return jnp.concatenate([ref[g * hd : (g + 1) * hd, cut] for g in range(groups)], axis=1)

        q = rows(all_ref)
        da = rows(da_all)
        inv = jnp.concatenate([inv_ref[g : g + 1, cut] for g in range(groups)], axis=1)
        delta = jnp.sum(rows(att_ref).astype(F32) * da.astype(F32), axis=0, keepdims=True)
        dq = jnp.zeros((hd, groups * block), F32)
        for j in range(i + 1):
            kcut = slice(j * block, (j + 1) * block)
            key = all_ref[base : base + hd, kcut]
            s = dot_tn(key, q) * scale
            ok = (krow + j * block) < length
            if j == i:
                ok = ok & (krow <= qcol)
            p = jnp.where(ok, jnp.exp2(s) * inv, 0.0)
            dp = dot_tn(all_ref[base + hd : base + 2 * hd, kcut], da)
            ds = (p * (dp - delta)).astype(BF16)
            dq = dq + dot_nn(key, ds)
            grads[base : base + hd, kcut] += dot_nt(q, ds) * back
            grads[base + hd : base + 2 * hd, kcut] += dot_nt(da, p.astype(BF16))
        dq = dq * back
        for g in range(groups):
            grads[g * hd : (g + 1) * hd, cut] = dq[:, g * block : (g + 1) * block]
    mine, theirs = join_positions(core, grads[:, :span], grads[:, span:])
    out_own[...] = mine.astype(BF16)
    out_oth[...] = theirs.astype(BF16)


def attend_back(scalars, everything, att, inv, own, got, groups):
    rows, slots = everything.shape
    span = slots // 2
    block = min(256, span)
    full = pl.BlockSpec(memory_space=pltpu.VMEM)
    return pl.pallas_call(
        functools.partial(attend_back_kernel, block, groups),
        in_specs=[SMEM] + [full] * 5,
        out_specs=[full] * 2,
        out_shape=[shape((rows, span), BF16)] * 2,
        scratch_shapes=[pltpu.VMEM(att.shape, BF16), pltpu.VMEM((rows, slots), F32)],
        compiler_params=PARAMS,
        cost_estimate=cost(30 * att.shape[0] * slots * slots, 12 * rows * slots, groups * slots * slots),
        name="attend_backward",
    )(scalars, everything, att, inv, own, got)


def heads_back_kernel(hd, nq, nk, own_ref, got_ref, pre_ref, cos_ref, sin_ref, qg_ref, kg_ref, x_ref, w_ref, core_ref, dpre_ref, first_ref, gain_ref, hgain_ref):
    half = w_ref.shape[1]
    low, high = join_positions(core_ref[0], own_ref[...].astype(F32), got_ref[...].astype(F32))
    sides = (nq // 2, nk // 2, nk // 2)
    grads = [[], [], []]
    for side in (low, high):
        at = 0
        for kind, count in enumerate(sides):
            for h in range(count):
                grads[kind].append(side[at : at + hd])
                at += hd
    cosine, sine = cos_ref[...], sin_ref[...]
    done = []
    sums = [0.0, 0.0]
    for h in range(nq + nk):
        kind = 0 if h < nq else 1
        g = grads[kind][h - kind * nq]
        a, b = g[: hd // 2], g[hd // 2 :]
        g = jnp.concatenate([a * cosine + b * sine, b * cosine - a * sine], axis=0)
        v = pre_ref[h * hd : (h + 1) * hd, :]
        inv = lax.rsqrt(jnp.mean(v * v, axis=0, keepdims=True) + epsilon)
        hat = v * inv
        sums[kind] = sums[kind] + jnp.sum(g * hat, axis=1, keepdims=True)
        gg = g * (qg_ref[...] if kind == 0 else kg_ref[...])
        done.append(inv * (gg - hat * jnp.mean(gg * hat, axis=0, keepdims=True)))
    done += grads[2]
    hgain_ref[:hd, :] = jnp.broadcast_to(sums[0], (hd, 128))
    hgain_ref[hd:, :] = jnp.broadcast_to(sums[1], (hd, 128))
    dpre = jnp.concatenate(done, axis=0).T.astype(BF16)
    dpre_ref[...] = dpre
    x = x_ref[0].astype(F32)
    hat = x * inverse_rms(x)
    for k in range(2):
        cut = slice(k * half, (k + 1) * half)
        part = dot_nt(dpre, w_ref[k])
        first_ref[:, cut] = part.astype(BF16)
        gain_ref[:, cut] = jnp.sum(part * hat[:, cut], axis=0, keepdims=True)


def heads_back(own, got, pre, cosine, sine, qgain, kgain, xr, seq, weight, core, hd, nq, nk):
    span = own.shape[1]
    _, half, cols = weight.shape
    width = 2 * half
    whole = lambda a: pl.BlockSpec(a.shape, lambda i: (0,) * len(a.shape))
    outs = [shape((span, cols), BF16), shape((span, width), BF16), shape((1, width), F32), shape((2 * hd, 128), F32)]
    return pl.pallas_call(
        functools.partial(heads_back_kernel, hd, nq, nk),
        grid=(1,),
        in_specs=[whole(a) for a in (own, got, pre, cosine, sine, qgain, kgain)]
        + [pl.BlockSpec((1, span, width), lambda i: (seq, 0, 0)), whole(weight), SMEM],
        out_specs=[whole(o) for o in outs],
        out_shape=outs,
        compiler_params=PARAMS,
        cost_estimate=cost(2 * span * width * cols, 4 * span * width + 4 * half * cols),
        name="query_key_value_back",
    )(own, got, pre, cosine, sine, qgain, kgain, xr, weight, core)


def place_blocks(order, ids, first_id, value, out_ref):
    piece = value.shape[-1] // order
    for k in range(order):
        if order == 1:
            out_ref[...] = value
        else:
            dst = pl.ds(pl.multiple_of(ids[first_id + k] * piece, piece), piece)
            out_ref[:, dst] = value[:, k * piece : (k + 1) * piece]


def output_kernel(order, scal_ref, got_ref, f0_ref, f1_ref, h0_ref, h1_ref, out_ref, stat_ref):
    low = scal_ref[0] * 2 < scal_ref[3]
    rows = out_ref.shape[0]
    ffn = got_ref[...].astype(F32) + jnp.where(low, f0_ref[...], f1_ref[...]).astype(F32)
    hidden = jnp.where(low, h0_ref[...], h1_ref[...])
    place = scal_ref[2] + lax.broadcasted_iota(jnp.int32, (rows, 1), 0)
    valid = (place < scal_ref[1]).astype(F32)
    stat_ref[...] = jnp.broadcast_to(jnp.sum(valid * ffn * ffn, keepdims=True), (8, 128))
    place_blocks(order, scal_ref, 4, (hidden + ffn).astype(BF16), out_ref)


def share_specs(rows, width, per):
    return [
        pl.BlockSpec((rows, width), lambda i, s: (jnp.minimum(s[0], per - 1), 0)),
        pl.BlockSpec((rows, width), lambda i, s: (jnp.maximum(s[0] - per, 0), 0)),
    ]


def output_share(scalars, got, ffns, hiddens, order):
    rows, width = got.shape
    pair = share_specs(rows, width, ffns[0].shape[0] // rows)
    flat = pl.BlockSpec((rows, width), lambda i, s: (0, 0))
    return pl.pallas_call(
        functools.partial(output_kernel, order),
        grid_spec=pltpu.PrefetchScalarGridSpec(
            num_scalar_prefetch=1,
            grid=(1,),
            in_specs=[flat] + pair + pair,
            out_specs=[flat, pl.BlockSpec((8, 128), lambda i, s: (0, 0))],
        ),
        out_shape=[shape((rows, width), BF16), shape((8, 128), F32)],
        compiler_params=PARAMS,
        cost_estimate=cost(6 * rows * width, 16 * rows * width),
        name="output_share",
    )(scalars, got, *ffns, *hiddens)


def input_kernel(order, scal_ref, got_ref, part_ref, g0_ref, g1_ref, x_ref, gain_ref, out_ref):
    low = scal_ref[0] * 2 < scal_ref[3]
    e = got_ref[...].astype(F32) + part_ref[...].astype(F32)
    gh = jnp.where(low, g0_ref[...], g1_ref[...])
    x = x_ref[0].astype(F32)
    inv = inverse_rms(x)
    hat = x * inv
    eg = e * gain_ref[...]
    value = gh + inv * (eg - hat * jnp.mean(eg * hat, axis=-1, keepdims=True))
    place_blocks(order, scal_ref, 4, value, out_ref)


def input_share(scalars, got, part, ghs, xr, seq, gain, order):
    rows, width = got.shape
    pair = share_specs(rows, width, ghs[0].shape[0] // rows)
    flat = pl.BlockSpec((rows, width), lambda i, s: (0, 0))
    return pl.pallas_call(
        functools.partial(input_kernel, order),
        grid_spec=pltpu.PrefetchScalarGridSpec(
            num_scalar_prefetch=1,
            grid=(1,),
            in_specs=[flat, pl.BlockSpec((rows, width), lambda i, s: (s[0], 0))]
            + pair
            + [pl.BlockSpec((1, rows, width), lambda i, s: (seq, s[0], 0)), pl.BlockSpec((1, width), lambda i, s: (0, 0))],
            out_specs=flat,
        ),
        out_shape=shape((rows, width), F32),
        compiler_params=PARAMS,
        cost_estimate=cost(12 * rows * width, 20 * rows * width),
        name="input_share",
    )(scalars, got, part, *ghs, xr, gain)


def weight_grad_kernel(count, extra, *refs):
    a_refs, b_refs, out = refs[:count], refs[count : 2 * count], refs[-1]
    total = dot_tn(a_refs[0][...], b_refs[0][...])
    for a, b in zip(a_refs[1:], b_refs[1:]):
        total = total + dot_tn(a[...], b[...])
    if extra:
        total = total + refs[2 * count][...].astype(F32)
    out[...] = total.astype(BF16)


def weight_grad(lefts, rights, side, axis, add=None):
    count = len(lefts)
    rows_all, cols_all = lefts[0].shape[1], rights[0].shape[1]
    dims = [rows_all, cols_all]
    dims[axis] //= 2
    rows, cols = min(512, dims[0]), min(2048, dims[1])
    row_at = side * (dims[0] // rows) if axis == 0 else 0
    col_at = side * (dims[1] // cols) if axis == 1 else 0
    specs = [pl.BlockSpec((a.shape[0], rows), lambda j, i: (0, i + row_at)) for a in lefts]
    specs += [pl.BlockSpec((b.shape[0], cols), lambda j, i: (0, j + col_at)) for b in rights]
    tile = pl.BlockSpec((rows, cols), lambda j, i: (i, j))
    tokens = sum(a.shape[0] for a in lefts)
    return pl.pallas_call(
        functools.partial(weight_grad_kernel, count, add is not None),
        grid=(dims[1] // cols, dims[0] // rows),
        in_specs=specs + ([tile] if add is not None else []),
        out_specs=tile,
        out_shape=shape(dims, BF16),
        compiler_params=PARAMS,
        cost_estimate=cost(2 * tokens * dims[0] * dims[1], 2 * tokens * sum(dims) + 2 * dims[0] * dims[1]),
        name="weight_grad",
    )(*lefts, *rights, *([add] if add is not None else []))


def xor_one(index):
    return index + 1 - 2 * (index % 2)


def remote(src, dst, send, recv, device):
    return pltpu.make_async_remote_copy(
        src_ref=src, dst_ref=dst, send_sem=send, recv_sem=recv, device_id=device, device_id_type=pl.DeviceIdType.MESH
    )


def greet(others):
    barrier = pltpu.get_barrier_semaphore()
    count = 0
    for needed, device in others:
        if needed is None:
            pl.semaphore_signal(barrier, inc=1, device_id=device, device_id_type=pl.DeviceIdType.MESH)
            count = count + 1
        else:

            @pl.when(needed)
            def _():
                pl.semaphore_signal(barrier, inc=1, device_id=device, device_id_type=pl.DeviceIdType.MESH)

            count = count + jnp.where(needed, 1, 0)
    pl.semaphore_wait(barrier, count)


class Gather:
    def __init__(self, shard, dst, axis, send, recv, local, near_x, near_y, near_core):
        piece = shard.shape[axis]
        half = shard.shape[0] // 2

        def block(side, k):
            cut = pl.ds(k * piece, piece)
            return dst.at[side, cut, :] if axis == 0 else dst.at[side, :, cut]

        def part(k, h):
            if axis == 0:
                return dst.at[0, pl.ds(k * piece + h * half, half), :]
            return dst.at[0, pl.ds(h * half, half), pl.ds(k * piece, piece)]

        sem = lambda k: (send.at[k], recv.at[k])
        self.local = pltpu.make_async_copy(shard, block(0, 0), local)
        self.x = remote(shard, block(0, 1), *sem(0), near_x)
        self.y = remote(shard, block(0, 2), *sem(1), near_y)
        self.dx = remote(part(2, 0), part(3, 0), *sem(2), near_x)
        self.dy = remote(part(1, 1), part(3, 1), *sem(3), near_y)
        self.cores = [remote(shard, block(1, 0), *sem(4), near_core)]
        self.cores += [remote(block(0, k), block(1, k), *sem(4 + k), near_core) for k in (1, 2, 3)]

    def first(self):
        self.x.start()
        self.y.start()
        self.cores[0].start()
        self.local.start()

    def second(self):
        self.y.wait_recv()
        self.dx.start()
        self.cores[2].start()
        self.x.wait_recv()
        self.dy.start()
        self.cores[1].start()

    def third(self):
        self.dx.wait_recv()
        self.dy.wait_recv()
        self.cores[3].start()

    def arrived(self):
        self.local.wait()
        for copy in self.cores:
            copy.wait_recv()

    def sent(self):
        for copy in [self.x, self.y, self.dx, self.dy] + self.cores:
            copy.wait_send()


def forward_kernel(
    hd, nq, nk, block, sub,
    len_ref, x_hbm, cot_hbm, wqkv, wout, wgate, wup, wdown, gain_ref, cos_ref, sin_ref, qg_ref, kg_ref,
    xr_hbm, n1_hbm, gf_hbm, qkv_hbm, out_hbm, gate_hbm, up_hbm, down_hbm, hidden_hbm, n2_hbm,
    gains_ref, pre_ref, all_ref, att_ref, inv_ref, tok_ref, stat_ref,
    xr_v, cot_v, n1_v, qkv_v, out_v, ex_own, ex_send, ex_got, at_own, at_send, at_got,
    part_v, in_v, back_v, pair_v, total_v, hid_v, norm_v,
    load_sem, store_sem, wsend, wrecv, wloc, gsend, grecv, exsend, exrecv, zsend, zrecv, hid_sem,
):
    seqs, span, width = xr_v.shape
    groups = nq // nk
    row, core, rank = lax.axis_index("dp"), lax.axis_index("context"), lax.axis_index("tensor")
    start = core * span
    near = [row, xor_one(row), (row + 2) % 4, 3 - row]
    inner = (rank % 3) != 0
    outer = (rank % 3) == 0
    near_x, near_y, near_core = {"dp": near[1]}, {"dp": near[2]}, {"context": 1 - core}
    z_side, z_mid = {"tensor": xor_one(rank)}, {"tensor": 3 - rank}
    piece = width // 8
    total_subs = part_v.shape[0]
    per = span // sub
    first_core = core == 0

    loads = []
    for at, (src, dst) in enumerate(((x_hbm, xr_v), (cot_hbm, cot_v))):
        for s in range(seqs):
            for o in range(2):
                for k in range(4):
                    b = near[k] * 2 + (core if o == 0 else 1 - core)
                    cut = pl.ds(pl.multiple_of(b * piece, piece), piece)
                    loads.append(
                        pltpu.make_async_copy(
                            src.at[s, :, cut], dst.at[s, :, pl.ds((o * 4 + k) * piece, piece)], load_sem.at[at, s, o * 4 + k]
                        )
                    )
    for copy in loads:
        copy.start()

    others = []
    for o in range(2):
        for k in range(4):
            if o or k:
                others.append((o * 4 + k, {"dp": near[k], "context": core if o == 0 else 1 - core}))
    greet([(None, d) for _, d in others] + [(None, z_side), (inner, z_mid)])

    gains = [remote(gain_ref, gains_ref.at[b], gsend.at[b], grecv.at[b], d) for b, d in others]
    for copy in gains:
        copy.start()
    weights = [
        Gather(shard, dst, axis, wsend.at[i], wrecv.at[i], wloc.at[i], near_x, near_y, near_core)
        for i, (shard, dst, axis) in enumerate(
            ((wqkv, qkv_v, 0), (wout, out_v, 1), (wgate, gate_hbm, 0), (wup, up_hbm, 0), (wdown, down_hbm, 1))
        )
    ]
    w_qkv, w_out, w_gate, w_up, w_down = weights
    w_qkv.first()
    w_out.first()
    gains_ref[0] = gain_ref[...]

    for copy in loads[len(loads) // 2 :]:
        copy.wait()

    def mask_rows(i, carry):
        s, t = i // per, i % per
        cut = pl.ds(pl.multiple_of(t * sub, sub), sub)
        place = start + t * sub + lax.broadcasted_iota(jnp.int32, (sub, 1), 0)
        length = len_ref[s]
        valid = (place < length).astype(F32)
        cot_v[s, cut, :] = (cot_v[s, cut, :].astype(F32) * valid).astype(BF16)
        return carry

    lax.fori_loop(0, total_subs, mask_rows, 0)
    store_gf = pltpu.make_async_copy(cot_v, gf_hbm, store_sem.at[0])
    store_gf.start()
    for copy in loads[: len(loads) // 2]:
        copy.wait()
    store_xr = pltpu.make_async_copy(xr_v, xr_hbm, store_sem.at[1])
    store_xr.start()
    for copy in gains:
        copy.wait_recv()
    gain1 = jnp.concatenate([gains_ref[b, 0:1, :] for b in range(8)], axis=1).astype(F32)
    gain2 = jnp.concatenate([gains_ref[b, 1:2, :] for b in range(8)], axis=1).astype(F32)

    def norm_rows(i, carry):
        s, t = i // per, i % per
        cut = pl.ds(pl.multiple_of(t * sub, sub), sub)
        x = xr_v[s, cut, :].astype(F32)
        n1_v[s, cut, :] = (x * inverse_rms(x) * gain1).astype(BF16)
        return carry

    lax.fori_loop(0, total_subs, norm_rows, 0)
    store_n1 = pltpu.make_async_copy(n1_v, n1_hbm, store_sem.at[2])
    store_n1.start()
    w_qkv.second()
    w_out.second()
    w_gate.first()
    w_qkv.third()
    w_out.third()
    w_qkv.arrived()
    w_up.first()

    cosine, sine = cos_ref[...], sin_ref[...]
    half = width // 2

    def exchange(s):
        return remote(ex_send.at[s], ex_got.at[s], exsend.at[0, s], exrecv.at[0, s], near_core)

    def project(s, carry):
        x = n1_v[s]
        flat = dot_nn(x[:, :half], qkv_v[0]) + dot_nn(x[:, half:], qkv_v[1])
        turned = flat.T
        pre_ref[s] = turned[: (nq + nk) * hd]
        done = []
        for h in range(nq + nk):
            v = turned[h * hd : (h + 1) * hd]
            inv = lax.rsqrt(jnp.mean(v * v, axis=0, keepdims=True) + epsilon)
            v = v * inv * (qg_ref[...] if h < nq else kg_ref[...])
            a, b = v[: hd // 2], v[hd // 2 :]
            done.append(jnp.concatenate([a * cosine - b * sine, b * cosine + a * sine], axis=0))
        for h in range(nk):
            lo = (nq + nk + h) * hd
            done.append(turned[lo : lo + hd])
        parts = [[], []]
        for begin_at, count in ((0, nq), (nq, nk), (nq + nk, nk)):
            for side in range(2):
                parts[side] += done[begin_at + side * count // 2 : begin_at + (side + 1) * count // 2]
        low = jnp.concatenate(parts[0], axis=0)
        high = jnp.concatenate(parts[1], axis=0)
        ex_own[s] = jnp.where(first_core, low, high).astype(BF16)
        ex_send[s] = jnp.where(first_core, high, low).astype(BF16)
        exchange(s).start()
        return carry

    lax.fori_loop(0, seqs, project, 0)
    store_qkv = pltpu.make_async_copy(qkv_v, qkv_hbm, store_sem.at[3])
    store_qkv.start()

    scale = log2e / math.sqrt(hd)
    krow = lax.broadcasted_iota(jnp.int32, (block, groups * block), 0)
    qcol = lax.broadcasted_iota(jnp.int32, (block, groups * block), 1) % block
    base = groups * hd

    def give(s):
        return remote(at_send.at[s], at_got.at[s], exsend.at[1, s], exrecv.at[1, s], near_core)

    def attention(s, carry):
        exchange(s).wait_recv()
        low, high = join_positions(core, ex_own[s], ex_got[s])
        all_ref[s, :, :span] = low
        all_ref[s, :, span:] = high
        length = len_ref[s]
        for i in range(2 * span // block):
            cut = slice(i * block, (i + 1) * block)
            q = jnp.concatenate([all_ref[s, g * hd : (g + 1) * hd, cut] for g in range(groups)], axis=1)
            acc = jnp.zeros((hd, groups * block), F32)
            total = jnp.zeros((1, groups * block), F32)
            for j in range(i + 1):
                kcut = slice(j * block, (j + 1) * block)
                score = dot_tn(all_ref[s, base : base + hd, kcut], q) * scale
                ok = (krow + j * block) < length
                if j == i:
                    ok = ok & (krow <= qcol)
                e = jnp.where(ok, jnp.exp2(score), 0.0)
                total = total + jnp.sum(e, axis=0, keepdims=True)
                acc = acc + dot_nn(all_ref[s, base + hd : base + 2 * hd, kcut], e.astype(BF16))
            inv = 1.0 / total
            att = (acc * inv).astype(BF16)
            for g in range(groups):
                att_ref[s, g * hd : (g + 1) * hd, cut] = att[:, g * block : (g + 1) * block]
                inv_ref[s, g : g + 1, cut] = inv[:, g * block : (g + 1) * block]
        mine, theirs = join_positions(core, att_ref[s, :, :span], att_ref[s, :, span:])
        at_own[s] = mine
        at_send[s] = theirs
        give(s).start()
        return carry

    lax.fori_loop(0, seqs, attention, 0)
    w_out.arrived()
    store_out = pltpu.make_async_copy(out_v, out_hbm, store_sem.at[4])
    store_out.start()

    def hop_in(u):
        return remote(part_v.at[u], in_v.at[u], zsend.at[0, u], zrecv.at[0, u], z_side)

    def hop_mid(u):
        return remote(pair_v.at[u], back_v.at[u], zsend.at[1, u], zrecv.at[1, u], z_mid)

    def hop_out(u):
        return remote(in_v.at[u], back_v.at[u], zsend.at[2, u], zrecv.at[2, u], z_side)

    def branch_rows(s, carry):
        give(s).wait_recv()
        low, high = join_positions(core, at_own[s], at_got[s])
        att = jnp.concatenate([low, high], axis=0).T
        tok_ref[s] = att
        for k in range(per):
            u = s * per + k
            rows = att[k * sub : (k + 1) * sub]
            part_v[u, :, :half] = dot_nn(rows, out_v[0]).astype(BF16)
            part_v[u, :, half:] = dot_nn(rows, out_v[1]).astype(BF16)

            @pl.when(outer)
            def _():
                hop_in(u).start()

        return carry

    lax.fori_loop(0, seqs, branch_rows, 0)
    w_gate.second()
    w_down.first()
    stat_ref[...] = jnp.zeros_like(stat_ref)
    line = lax.broadcasted_iota(jnp.int32, (8, 128), 0)

    def hidden_store(u):
        cut = pl.ds(pl.multiple_of(u * sub, sub), sub)
        return (
            pltpu.make_async_copy(hid_v.at[u % 2], hidden_hbm.at[cut, :], hid_sem.at[0, u % 2]),
            pltpu.make_async_copy(norm_v.at[u % 2], n2_hbm.at[cut, :], hid_sem.at[1, u % 2]),
        )

    def finish(u):
        s, t = u // per, u % per
        cut = pl.ds(pl.multiple_of(t * sub, sub), sub)

        @pl.when(inner)
        def _():
            total_v[...] = pair_v[u].astype(F32) + back_v[u].astype(F32)

        @pl.when(outer)
        def _():
            hop_out(u).wait_recv()
            total_v[...] = part_v[u].astype(F32) + back_v[u].astype(F32)

        @pl.when(u >= 2)
        def _():
            for copy in hidden_store(u - 2):
                copy.wait()

        total = total_v[...]
        resid = xr_v[s, cut, :].astype(F32)
        hidden = resid + total
        hid_v[u % 2] = hidden
        norm_v[u % 2] = (hidden * inverse_rms(hidden) * gain2).astype(BF16)
        for copy in hidden_store(u):
            copy.start()
        length = len_ref[s]
        place = start + t * sub + lax.broadcasted_iota(jnp.int32, (sub, 1), 0)
        valid = (place < length).astype(F32)
        one = jnp.sum(valid * resid * resid, keepdims=True)
        two = jnp.sum(valid * total * total, keepdims=True)
        stat_ref[...] += jnp.where(line == 0, one, jnp.where(line == 1, two, 0.0))

    def chain(i, carry):
        @pl.when((i < total_subs) & inner)
        def _():
            hop_in(i).wait_recv()
            pair_v[i] = (part_v[i].astype(F32) + in_v[i].astype(F32)).astype(BF16)
            hop_mid(i).start()

        @pl.when((i >= 1) & (i < total_subs + 1) & inner)
        def _():
            u = i - 1
            hop_mid(u).wait_recv()
            in_v[u] = (part_v[u].astype(F32) + back_v[u].astype(F32)).astype(BF16)
            hop_out(u).start()

        @pl.when(i >= 2)
        def _():
            finish(i - 2)

        @pl.when(i == total_subs // 2 - 2)
        def _():
            w_gate.third()
            w_up.second()

        @pl.when(i == total_subs - 1)
        def _():
            w_up.third()
            w_down.second()

        return carry

    lax.fori_loop(0, total_subs + 2, chain, 0)
    w_down.third()
    for u in (total_subs - 2, total_subs - 1):
        for copy in hidden_store(u):
            copy.wait()

    def settle(u, carry):
        @pl.when(outer)
        def _():
            hop_in(u).wait_send()

        @pl.when(inner)
        def _():
            hop_mid(u).wait_send()
            hop_out(u).wait_send()

        return carry

    lax.fori_loop(0, total_subs, settle, 0)
    for s in range(seqs):
        exchange(s).wait_send()
        give(s).wait_send()
    for copy in gains:
        copy.wait_send()
    for w in weights[2:]:
        w.arrived()
    for w in weights:
        w.sent()
    for copy in (store_gf, store_xr, store_n1, store_qkv, store_out):
        copy.wait()


def forward(lengths, x, cot, w_qkv, w_out, w_gate, w_up, w_down, gains, cosine, sine, qgain, kgain, hd, nq, nk):
    seqs, span, width = x.shape
    half = width // 2
    groups = nq // nk
    sub = min(128, span)
    subs = seqs * span // sub
    block = min(256, span)
    hidden = w_gate.shape[1]
    cols = w_qkv.shape[1]
    rows = cols // 2
    any_space = pl.BlockSpec(memory_space=pl.ANY)
    vmem = pl.BlockSpec(memory_space=pltpu.VMEM)
    wide = (seqs, span, width)
    large = [
        shape(wide, BF16), shape(wide, BF16), shape(wide, BF16),
        shape((2, half, cols), BF16), shape((2, w_out.shape[0], half), BF16),
        shape((2, half, hidden), BF16), shape((2, half, hidden), BF16), shape((2, hidden, half), BF16),
        shape((seqs * span, width), F32), shape((seqs * span, width), BF16),
    ]
    small = [
        shape((8,) + gains.shape, BF16), shape((seqs, (nq + nk) * hd, span), F32), shape((seqs, rows, 2 * span), BF16),
        shape((seqs, groups * hd, 2 * span), BF16), shape((seqs, groups, 2 * span), F32), shape((seqs, span, nq * hd), BF16),
        shape((8, 128), F32),
    ]
    dma = pltpu.SemaphoreType.DMA
    ex = pltpu.VMEM((seqs, rows, span), BF16)
    at = pltpu.VMEM((seqs, groups * hd, span), BF16)
    moving = pltpu.VMEM((subs, sub, width), BF16)
    flops = 2 * seqs * span * width * (cols + nq * hd) + 16 * seqs * nq * hd * span * span
    return pl.pallas_call(
        functools.partial(forward_kernel, hd, nq, nk, block, sub),
        in_specs=[SMEM] + [any_space] * 7 + [vmem] * 5,
        out_specs=[any_space] * len(large) + [vmem] * len(small),
        out_shape=large + small,
        scratch_shapes=[
            pltpu.VMEM(wide, BF16), pltpu.VMEM(wide, BF16), pltpu.VMEM(wide, BF16),
            pltpu.VMEM((2, half, cols), BF16), pltpu.VMEM((2, w_out.shape[0], half), BF16),
            ex, ex, ex, at, at, at,
            moving, moving, moving, moving,
            pltpu.VMEM((sub, width), F32), pltpu.VMEM((2, sub, width), F32), pltpu.VMEM((2, sub, width), BF16),
            dma((2, seqs, 8)), dma((5,)), dma((5, 8)), dma((5, 8)), dma((5,)), dma((8,)), dma((8,)),
            dma((2, seqs)), dma((2, seqs)), dma((3, subs)), dma((3, subs)), dma((2, 2)),
        ],
        compiler_params=pltpu.CompilerParams(vmem_limit_bytes=VMEM_BYTES, collective_id=1, has_side_effects=True),
        cost_estimate=cost(flops, 80 * seqs * span * width),
        name="attention_forward",
    )(lengths, x, cot, w_qkv, w_out, w_gate, w_up, w_down, gains, cosine, sine, qgain, kgain)


def per_device(
    inputs,
    cotangent,
    lengths,
    w_query,
    key_projection_weight,
    value_projection_weight,
    w_output,
    w_gate,
    w_up,
    w_down,
    attn_gain,
    ffn_gain,
    query_gain,
    key_gain,
):
    seqs, span, width = inputs.shape
    hd = query_gain.shape[0]
    nq = w_query.shape[1] // hd
    nk = key_projection_weight.shape[1] // hd
    groups = nq // nk
    dp = lax.axis_size("dp")
    tensor = lax.axis_size("tensor")
    row = lax.axis_index("dp")
    core = lax.axis_index("context")
    rank = lax.axis_index("tensor")
    chunks = 2
    rows = span // chunks
    share = span // tensor
    lengths = lengths.astype(jnp.int32)
    start = (core * span).astype(jnp.int32)
    core1 = core.astype(jnp.int32).reshape(1)
    ids = block_order(dp, row, core)
    order = 2 * dp if (width // (2 * dp)) % 128 == 0 else 1

    positions = start + jnp.arange(span, dtype=jnp.int32)
    freqs = rope_base ** (-(jnp.arange(hd // 2, dtype=F32) * (2.0 / hd)))
    angles = freqs[:, None] * positions.astype(F32)[None, :]
    cosine, sine = jnp.cos(angles), jnp.sin(angles)
    qgain = query_gain.astype(F32).reshape(hd, 1)
    kgain = key_gain.astype(F32).reshape(hd, 1)

    w_qkv = jnp.concatenate([w_query, key_projection_weight, value_projection_weight], axis=1)
    saved = []
    if dp == 4 and tensor == 4 and order == 8:
        gains = jnp.pad(jnp.stack([attn_gain, ffn_gain]), ((0, 14), (0, 0)))
        (xr, n1, gf, qkv, out_w, gate, up, down, hidden_all, n2_all, gains, pre_all, everything_all, att_all, inv_all, tok, stat) = forward(
            lengths, inputs, cotangent, w_qkv, w_output, w_gate, w_up, w_down, gains, cosine, sine, qgain, kgain, hd, nq, nk
        )
        gains = jnp.swapaxes(gains[:, :2], 0, 1).reshape(2, width).astype(F32)
        gain1, gain2 = gains[0:1], gains[1:2]
        stats = stat[:2, 0]
        for s in range(seqs):
            seq_scal = jnp.stack([lengths[s], core.astype(jnp.int32)])
            saved.append((pre_all[s], everything_all[s], att_all[s], inv_all[s], seq_scal))
        tok = tok.reshape(seqs * span, nq * hd)
    else:
        gains, _ = gather_blocks(jnp.stack([attn_gain, ffn_gain]), 1, dp)
        gains = jnp.concatenate([gains[0], gains[1]], axis=1).astype(F32)
        gain1, gain2 = gains[0:1], gains[1:2]
        qkv, mark = gather_blocks(w_qkv, 0, dp)
        out_w, mark = gather_blocks(tie(w_output, mark), 1, dp)
        gate, mark = gather_blocks(tie(w_gate, mark), 0, dp)
        up, mark = gather_blocks(tie(w_up, mark), 0, dp)
        down, mark = gather_blocks(tie(w_down, mark), 1, dp)

        scal = jnp.concatenate([lengths, start.reshape(1), ids])
        x_in, cot_in = inputs, cotangent
        if order == 1:
            x_in, cot_in = to_relative(x_in, dp, core), to_relative(cot_in, dp, core)
        xr, n1, gf = begin(x_in, cot_in, gain1, scal, order)

        parts, tok = [], []
        for s in range(seqs):
            pre, own, oth = heads(n1, s, qkv, cosine, sine, qgain, kgain, core1, hd, nq, nk)
            seq_scal = jnp.stack([lengths[s], core.astype(jnp.int32)])
            everything, att, inv, mine, theirs = attend(seq_scal, own, over_core(oth), groups)
            branched = branch(mine, over_core(theirs), out_w, core1, chunks)
            saved.append((pre, everything, att, inv, seq_scal))
            tok.append(jnp.swapaxes(branched[0], 0, 1))
            parts.append(branched[1:])
        tok = jnp.concatenate(tok, axis=0)

        stats = jnp.zeros((2,), F32)
        hidden_all, n2_all = [], []
        for s in range(seqs):
            for k in range(chunks):
                terms = sum_terms(parts[s][k], tensor)
                place = jnp.stack([lengths[s], start + k * rows])
                hidden, n2, stat = second_norm(place, xr, s, k, gain2, terms)
                hidden_all.append(hidden)
                n2_all.append(n2)
                stats = stats + stat[:2, 0]
        hidden_all, n2_all = jnp.concatenate(hidden_all), jnp.concatenate(n2_all)

    ffn_squares = jnp.zeros((), F32)
    inner, gg, gu, ffn, gn = [[[None] * chunks for _ in range(seqs)] for _ in range(5)]
    out_shares = []
    for s in range(seqs):
        for k in range(chunks):
            inner[s][k], gg[s][k], gu[s][k], ffn[s][k], gn[s][k] = feed(n2_all, s * chunks + k, rows, gf, s, k, gate, up, down)

    def piece_of(arrays):
        per = arrays[0].shape[0] // share

        def piece(k):
            found = lax.dynamic_slice_in_dim(arrays[0], jnp.minimum(k, per - 1) * share, share, 0)
            for m in range(1, len(arrays)):
                here = lax.dynamic_slice_in_dim(arrays[m], jnp.clip(k - m * per, 0, per - 1) * share, share, 0)
                found = jnp.where(k >= m * per, here, found)
            return found

        return piece

    def share_scalars(s):
        head = jnp.stack([rank.astype(jnp.int32), lengths[s], start + rank.astype(jnp.int32) * share, jnp.int32(tensor)])
        return jnp.concatenate([head, ids])

    gain2_grad = jnp.zeros((1, width), F32)
    gb, gh = [[[None] * chunks for _ in range(seqs)] for _ in range(2)]
    for s in range(seqs):
        for k in range(chunks):
            terms = sum_terms(gn[s][k], tensor)
            gb[s][k], gh[s][k], gain_part = second_back(hidden_all, s * chunks + k, gf, s, k, gain2, terms)
            gain2_grad = gain2_grad + gain_part
    for s in range(seqs):
        got = ring_scatter(piece_of(ffn[s]), tensor, rank)
        halves = [hidden_all[(s * chunks + k) * rows : (s * chunks + k + 1) * rows] for k in range(chunks)]
        out, stat = output_share(share_scalars(s), got, ffn[s], halves, order)
        out_shares.append(out)
        ffn_squares = ffn_squares + stat[0, 0]

    def flat(nested):
        return [item for inner_list in nested for item in inner_list]

    def reduced(lefts, rights, axis):
        oth = weight_grad(lefts, rights, 1, axis)
        own = weight_grad(lefts, rights, 0, axis, over_core(oth))
        return scatter_blocks(own, axis, dp)

    gf_chunks = [gf[s] for s in range(seqs)]
    inner_seq = flat(inner)
    gf_flat = [gf[s, k * rows : (k + 1) * rows] for s in range(seqs) for k in range(chunks)]
    grad_w_down = reduced(inner_seq, gf_flat, 1)
    n2_list = [n2_all[i * rows : (i + 1) * rows] for i in range(seqs * chunks)]
    grad_w_gate = reduced(n2_list, flat(gg), 0)
    grad_w_up = reduced(n2_list, flat(gu), 0)

    gain1_grad = jnp.zeros((1, width), F32)
    head_gain = jnp.zeros((2 * hd,), F32)
    dpres, in_shares = [], []
    for s in range(seqs):
        pre, everything, att, inv, seq_scal = saved[s]
        da_own, da_oth = branch_back(gb[s], out_w, core1)
        d_own, d_oth = attend_back(seq_scal, everything, att, inv, da_own, over_core(da_oth), groups)
        dpre, first, gain_part, hg = heads_back(
            d_own, over_core(d_oth), pre, cosine, sine, qgain, kgain, xr, s, qkv, core1, hd, nq, nk
        )
        gain1_grad = gain1_grad + gain_part
        head_gain = head_gain + hg[:, 0]
        dpres.append(dpre)
        got = ring_scatter(piece_of([first]), tensor, rank)
        in_shares.append(input_share(share_scalars(s), got, first, gh[s], xr, s, gain1, order))

    att_list = [tok[i * rows : (i + 1) * rows] for i in range(seqs * chunks)]
    grad_w_output = reduced(att_list, flat(gb), 1)
    grad_qkv = reduced([n1[s] for s in range(seqs)], dpres, 0)
    nqc, nkc = nq * hd, nk * hd
    grad_w_query = grad_qkv[:, :nqc]
    grad_w_key = grad_qkv[:, nqc : nqc + nkc]
    grad_w_value = grad_qkv[:, nqc + nkc :]

    gain2_grad = gain2_grad / tensor
    counts = jnp.sum(jnp.clip(lengths - start, 0, span)).astype(F32) / tensor
    small = jnp.concatenate([head_gain, stats / tensor, ffn_squares.reshape(1), counts.reshape(1)])
    small = jnp.pad(small, (0, (-small.shape[0]) % 128)).reshape(1, -1)
    lines = jnp.concatenate([gain1_grad, gain2_grad], axis=0)
    if dp == 4 and tensor == 4:
        half = width // 2
        quarter = half // 4

        def join(part):
            return jnp.concatenate([part.reshape(1, -1), small], axis=1)

        got = over_core(join(lines[:, half:]))
        lines = lines[:, :half] + got[:, : 2 * half].reshape(2, half)
        small = small + got[:, 2 * half :]
        lines = lines.reshape(2, 4, quarter)
        got = over_x(join(lines[:, 1::2]))
        lines = lines[:, 0::2] + got[:, : 4 * quarter].reshape(2, 2, quarter)
        small = small + got[:, 4 * quarter :]
        got = over_y(join(lines[:, 1]))
        lines = lines[:, 0] + got[:, : 2 * quarter].reshape(2, quarter)
        small = small + got[:, 2 * quarter :]
        for step in (1, 2):
            got = lax.ppermute(join(lines), "tensor", [(i, i ^ step) for i in range(4)])
            lines = lines + got[:, : 2 * quarter].reshape(2, quarter)
            small = small + got[:, 2 * quarter :]
    else:
        piece = width // (2 * dp)
        lines = to_absolute(lines, dp, core) if dp != 4 else lines.reshape(2, 2 * dp, piece)[:, jnp.argsort(ids)].reshape(2, width)
        lines, small = lax.psum((lines, small), ("dp", "context", "tensor"))
        lines = lax.dynamic_slice_in_dim(lines, lax.axis_index(("dp", "context")) * piece, piece, 1)
    small = small[0]
    rms_values = jnp.sqrt(small[2 * hd : 2 * hd + 3] / (small[2 * hd + 3] * width))

    output = jnp.stack(out_shares)
    grad_inputs = jnp.stack(in_shares)
    if order == 1:
        output, grad_inputs = to_absolute(output, dp, core), to_absolute(grad_inputs, dp, core)
    return (
        output,
        grad_inputs,
        grad_w_query,
        grad_w_key,
        grad_w_value,
        grad_w_output,
        grad_w_gate,
        grad_w_up,
        grad_w_down,
        lines[0],
        lines[1],
        small[:hd],
        small[hd : 2 * hd],
        rms_values,
    )


def solution(mesh):
    both = ("dp", "context")
    rows = P(both, "tensor")
    cols = P("tensor", both)
    shares = P("dp", ("context", "tensor"), None)
    acts = P("dp", "context", None)
    return jax.shard_map(
        per_device,
        mesh=mesh,
        in_specs=(acts, acts, P("dp"), rows, rows, rows, cols, rows, rows, cols, P(both), P(both), P(), P()),
        out_specs=(shares, shares, rows, rows, rows, cols, rows, rows, cols, P(both), P(both), P(), P(), P()),
        check_vma=False,
    )
```

```python
import functools
import math

import jax
import jax.numpy as jnp
from jax import lax
from jax.experimental import pallas as pl
from jax.experimental.pallas import tpu as pltpu
from jax.sharding import PartitionSpec as P

F32 = jnp.float32
BF16 = jnp.bfloat16
epsilon = 1e-05
rope_base = 1000000.0
log2e = 1.4426950408889634
VMEM_BYTES = 60 * 1024 * 1024
VMEM_MOST = 63 * 1024 * 1024
PARAMS = pltpu.CompilerParams(vmem_limit_bytes=VMEM_BYTES)
SMEM = pl.BlockSpec(memory_space=pltpu.SMEM)
SWAP = ((0, 1), (1, 0))


def shape(dims, dtype):
    return jax.ShapeDtypeStruct(tuple(dims), dtype)


def cost(flops, size, exps=0):
    return pl.CostEstimate(flops=int(flops), bytes_accessed=int(size), transcendentals=int(exps))


def dot_nn(a, b):
    return lax.dot_general(a, b, (((1,), (0,)), ((), ())), preferred_element_type=F32)


def dot_nt(a, b):
    return lax.dot_general(a, b, (((1,), (1,)), ((), ())), preferred_element_type=F32)


def dot_tn(a, b):
    return lax.dot_general(a, b, (((0,), (0,)), ((), ())), preferred_element_type=F32)


def inverse_rms(values):
    return lax.rsqrt(jnp.mean(values * values, axis=-1, keepdims=True) + epsilon)


def tie(value, *others):
    return lax.optimization_barrier((value,) + others)[0]


def block_order(dp, row, core):
    if dp == 4:
        return jnp.stack([(row ^ k) * 2 + (core ^ o) for o in range(2) for k in range(dp)]).astype(jnp.int32)
    return jnp.stack([jnp.int32(k) * 2 + (core ^ o) for o in range(2) for k in range(dp)]).astype(jnp.int32)


def to_relative(values, dp, core):
    lead = values.shape[:-1]
    parts = values.reshape(lead + (dp, 2, -1))
    parts = jnp.where(core == 0, parts, parts[..., ::-1, :])
    return jnp.swapaxes(parts, -3, -2).reshape(values.shape)


def to_absolute(values, dp, core):
    lead = values.shape[:-1]
    parts = jnp.swapaxes(values.reshape(lead + (2, dp, -1)), -3, -2)
    return jnp.where(core == 0, parts, parts[..., ::-1, :]).reshape(values.shape)


def over_x(value):
    return lax.ppermute(value, "dp", [(i, i ^ 1) for i in range(4)])


def over_y(value):
    return lax.ppermute(value, "dp", [(i, i ^ 2) for i in range(4)])


def over_core(value):
    return lax.ppermute(value, "context", SWAP)


def gather_blocks(weight, axis, dp):
    if dp == 4:
        from_x = over_x(weight)
        from_y = over_y(weight)
        half = weight.shape[0] // 2
        first = over_x(from_y[:half])
        second = over_y(from_x[half:])
        if axis == 0:
            own = jnp.concatenate([weight, from_x, from_y, first, second], axis=0)
        else:
            diagonal = jnp.concatenate([first, second], axis=0)
            own = jnp.concatenate([weight, from_x, from_y, diagonal], axis=1)
        mark = from_x
    else:
        own = lax.all_gather(weight, "dp", axis=axis, tiled=True)
        mark = own
    return jnp.stack([own, over_core(own)]), mark


def scatter_blocks(total, axis, dp):
    if dp != 4:
        return lax.psum_scatter(total, "dp", scatter_dimension=axis, tiled=True).astype(F32)
    piece = total.shape[axis] // 4
    half = piece // 2 if axis == 0 else total.shape[0] // 2

    def block(k):
        return lax.slice_in_dim(total, k * piece, (k + 1) * piece, axis=axis)

    diagonal = block(3)
    from_x = over_x(diagonal[:half])
    from_y = over_y(diagonal[half:])
    to_y = block(2)
    to_x = block(1)
    to_y = jnp.concatenate([to_y[:half].astype(F32) + from_x.astype(F32), to_y[half:].astype(F32)], axis=0).astype(BF16)
    to_x = jnp.concatenate([to_x[:half].astype(F32), to_x[half:].astype(F32) + from_y.astype(F32)], axis=0).astype(BF16)
    got_x = over_x(to_x)
    got_y = over_y(to_y)
    return block(0).astype(F32) + got_x.astype(F32) + got_y.astype(F32)


def sum_terms(part, tensor):
    if tensor != 4:
        return [lax.psum(part, "tensor")]
    inward = lax.ppermute(part, "tensor", [(0, 1), (3, 2)])
    pair = (part.astype(F32) + inward.astype(F32)).astype(BF16)
    across = lax.ppermute(pair, "tensor", [(1, 2), (2, 1)])
    rest = (part.astype(F32) + across.astype(F32)).astype(BF16)
    outward = lax.ppermute(rest, "tensor", [(1, 0), (2, 3)])
    return [part, inward, across, outward]


def ring_scatter(piece, tensor, rank):
    ring = [(i, (i + 1) % tensor) for i in range(tensor)]
    moving = piece((rank + tensor - 1) % tensor)
    for step in range(1, tensor):
        moving = lax.ppermute(moving, "tensor", ring)
        if step < tensor - 1:
            moving = (moving.astype(F32) + piece((rank + tensor - 1 - step) % tensor).astype(F32)).astype(BF16)
    return moving


def begin_kernel(order, x_ref, cot_ref, gain_ref, scal_ref, xr_ref, n1_ref, gf_ref):
    seq, tile = pl.program_id(0), pl.program_id(1)
    rows, width = x_ref.shape[1:]
    seqs = pl.num_programs(0)
    place = scal_ref[seqs] + tile * rows + lax.broadcasted_iota(jnp.int32, (rows, 1), 0)
    valid = (place < scal_ref[seq]).astype(F32)
    x = x_ref[0].astype(F32)
    inv = inverse_rms(x)
    piece = width // order
    for k in range(order):
        src = pl.ds(pl.multiple_of(scal_ref[seqs + 1 + k] * piece, piece), piece) if order > 1 else slice(0, width)
        dst = slice(k * piece, (k + 1) * piece)
        part = x_ref[0, :, src]
        xr_ref[0, :, dst] = part
        n1_ref[0, :, dst] = (part.astype(F32) * inv * gain_ref[:, dst]).astype(BF16)
        gf_ref[0, :, dst] = (cot_ref[0, :, src].astype(F32) * valid).astype(BF16)


def begin(x, cot, gain, scalars, order):
    seqs, span, width = x.shape
    rows = min(256, span)
    spec = pl.BlockSpec((1, rows, width), lambda s, i: (s, i, 0))
    return pl.pallas_call(
        functools.partial(begin_kernel, order),
        grid=(seqs, span // rows),
        in_specs=[spec, spec, pl.BlockSpec((1, width), lambda s, i: (0, 0)), SMEM],
        out_specs=[spec] * 3,
        out_shape=[shape(x.shape, BF16)] * 3,
        compiler_params=PARAMS,
        cost_estimate=cost(8 * x.size, 10 * x.size),
        name="first_norm",
    )(x, cot, gain, scalars)


def heads_kernel(hd, nq, nk, n1_ref, w_ref, cos_ref, sin_ref, qg_ref, kg_ref, core_ref, pre_ref, own_ref, oth_ref):
    half = w_ref.shape[1]
    x = n1_ref[0]
    flat = dot_nn(x[:, :half], w_ref[0]) + dot_nn(x[:, half:], w_ref[1])
    turned = flat.T
    span = turned.shape[1]
    normed = turned[: (nq + nk) * hd]
    pre_ref[...] = normed
    core = core_ref[0]
    cosine, sine = cos_ref[...], sin_ref[...]
    done = []
    for h in range(nq + nk):
        v = normed[h * hd : (h + 1) * hd]
        inv = lax.rsqrt(jnp.mean(v * v, axis=0, keepdims=True) + epsilon)
        v = v * inv * (qg_ref[...] if h < nq else kg_ref[...])
        a, b = v[: hd // 2], v[hd // 2 :]
        done.append(jnp.concatenate([a * cosine - b * sine, b * cosine + a * sine], axis=0))
    for h in range(nk):
        lo = (nq + nk + h) * hd
        done.append(turned[lo : lo + hd])
    parts = [[], []]
    for start, count in ((0, nq), (nq, nk), (nq + nk, nk)):
        for side in range(2):
            parts[side] += done[start + side * count // 2 : start + (side + 1) * count // 2]
    low = jnp.concatenate(parts[0], axis=0)
    high = jnp.concatenate(parts[1], axis=0)
    first = core == 0
    own_ref[...] = jnp.where(first, low, high).astype(BF16)
    oth_ref[...] = jnp.where(first, high, low).astype(BF16)


def heads(n1, seq, weight, cosine, sine, qgain, kgain, core, hd, nq, nk):
    span, width = n1.shape[1:]
    sides = (nq + 2 * nk) * hd // 2
    full = pl.BlockSpec(memory_space=pltpu.VMEM)
    whole = lambda a: pl.BlockSpec(a.shape, lambda i: (0,) * a.ndim)
    outs = [shape(((nq + nk) * hd, span), F32), shape((sides, span), BF16), shape((sides, span), BF16)]
    return pl.pallas_call(
        functools.partial(heads_kernel, hd, nq, nk),
        grid=(1,),
        in_specs=[pl.BlockSpec((1, span, width), lambda i: (seq, 0, 0))]
        + [whole(a) for a in (weight, cosine, sine, qgain, kgain)]
        + [SMEM],
        out_specs=[whole(o) for o in outs],
        out_shape=outs,
        compiler_params=PARAMS,
        cost_estimate=cost(2 * span * width * weight.shape[2], 2 * span * width + 2 * weight.size),
        name="query_key_value",
    )(n1, weight, cosine, sine, qgain, kgain, core)


def join_positions(core, own, oth):
    first = core == 0
    return jnp.where(first, own, oth), jnp.where(first, oth, own)


def attend_kernel(block, groups, scal_ref, own_ref, got_ref, all_ref, att_ref, inv_ref, ao_ref, ax_ref):
    span = own_ref.shape[1]
    hd = own_ref.shape[0] // (groups + 2)
    length, core = scal_ref[0], scal_ref[1]
    low, high = join_positions(core, own_ref[...], got_ref[...])
    all_ref[:, :span] = low
    all_ref[:, span:] = high
    scale = log2e / math.sqrt(hd)
    krow = lax.broadcasted_iota(jnp.int32, (block, groups * block), 0)
    qcol = lax.broadcasted_iota(jnp.int32, (block, groups * block), 1) % block
    base = groups * hd
    for i in range(2 * span // block):
        cut = slice(i * block, (i + 1) * block)
        q = jnp.concatenate([all_ref[g * hd : (g + 1) * hd, cut] for g in range(groups)], axis=1)
        acc = jnp.zeros((hd, groups * block), F32)
        total = jnp.zeros((1, groups * block), F32)
        for j in range(i + 1):
            kcut = slice(j * block, (j + 1) * block)
            s = dot_tn(all_ref[base : base + hd, kcut], q) * scale
            ok = (krow + j * block) < length
            if j == i:
                ok = ok & (krow <= qcol)
            e = jnp.where(ok, jnp.exp2(s), 0.0)
            total = total + jnp.sum(e, axis=0, keepdims=True)
            acc = acc + dot_nn(all_ref[base + hd : base + 2 * hd, kcut], e.astype(BF16))
        inv = 1.0 / total
        att = (acc * inv).astype(BF16)
        for g in range(groups):
            att_ref[g * hd : (g + 1) * hd, cut] = att[:, g * block : (g + 1) * block]
            inv_ref[g : g + 1, cut] = inv[:, g * block : (g + 1) * block]
    mine, theirs = join_positions(core, att_ref[:, :span], att_ref[:, span:])
    ao_ref[...] = mine
    ax_ref[...] = theirs


def attend(scalars, own, got, groups):
    rows, span = own.shape
    hd = rows // (groups + 2)
    block = min(256, span)
    full = pl.BlockSpec(memory_space=pltpu.VMEM)
    return pl.pallas_call(
        functools.partial(attend_kernel, block, groups),
        in_specs=[SMEM, full, full],
        out_specs=[full] * 5,
        out_shape=[
            shape((rows, 2 * span), BF16),
            shape((groups * hd, 2 * span), BF16),
            shape((groups, 2 * span), F32),
            shape((groups * hd, span), BF16),
            shape((groups * hd, span), BF16),
        ],
        compiler_params=PARAMS,
        cost_estimate=cost(60 * groups * hd * span * span, 12 * rows * span, 4 * groups * span * span),
        name="attend_forward",
    )(scalars, own, got)


def branch_kernel(own_ref, got_ref, w_ref, core_ref, att_ref, *outs):
    half = w_ref.shape[2]
    low, high = join_positions(core_ref[0], own_ref[...], got_ref[...])
    att = jnp.concatenate([low, high], axis=0)
    att_ref[...] = att
    rows = outs[0].shape[0]
    for k, out in enumerate(outs):
        part = att[:, k * rows : (k + 1) * rows]
        out[:, :half] = dot_tn(part, w_ref[0]).astype(BF16)
        out[:, half:] = dot_tn(part, w_ref[1]).astype(BF16)


def branch(own, got, weight, core, chunks):
    rows, span = own.shape
    width = 2 * weight.shape[2]
    full = pl.BlockSpec(memory_space=pltpu.VMEM)
    return pl.pallas_call(
        branch_kernel,
        in_specs=[full] * 3 + [SMEM],
        out_specs=[full] * (1 + chunks),
        out_shape=[shape((2 * rows, span), BF16)] + [shape((span // chunks, width), BF16)] * chunks,
        compiler_params=PARAMS,
        cost_estimate=cost(4 * rows * span * width, 4 * rows * width + 2 * span * width),
        name="attention_branch",
    )(own, got, weight, core)


def second_norm_kernel(terms, scal_ref, x_ref, gain_ref, *refs):
    term_refs, (hidden_ref, n2_ref, stat_ref) = refs[:terms], refs[terms:]
    rows = hidden_ref.shape[0]
    branch_sum = term_refs[0][...].astype(F32)
    for ref in term_refs[1:]:
        branch_sum = branch_sum + ref[...].astype(F32)
    resid = x_ref[0].astype(F32)
    hidden = resid + branch_sum
    hidden_ref[...] = hidden
    n2_ref[...] = (hidden * inverse_rms(hidden) * gain_ref[...]).astype(BF16)
    place = scal_ref[1] + lax.broadcasted_iota(jnp.int32, (rows, 1), 0)
    valid = (place < scal_ref[0]).astype(F32)
    first = jnp.sum(valid * resid * resid, keepdims=True)
    second = jnp.sum(valid * branch_sum * branch_sum, keepdims=True)
    line = lax.broadcasted_iota(jnp.int32, (8, 128), 0)
    stat_ref[...] = jnp.where(line == 0, first, second)


def second_norm(scalars, xr, seq, part, gain, terms):
    rows, width = terms[0].shape
    flat = pl.BlockSpec((rows, width), lambda i: (0, 0))
    return pl.pallas_call(
        functools.partial(second_norm_kernel, len(terms)),
        grid=(1,),
        in_specs=[SMEM, pl.BlockSpec((1, rows, width), lambda i: (seq, part, 0)), pl.BlockSpec((1, width), lambda i: (0, 0))]
        + [flat] * len(terms),
        out_specs=[flat, flat, pl.BlockSpec((8, 128), lambda i: (0, 0))],
        out_shape=[shape((rows, width), F32), shape((rows, width), BF16), shape((8, 128), F32)],
        compiler_params=PARAMS,
        cost_estimate=cost(20 * rows * width, (8 + 2 * len(terms)) * rows * width),
        name="second_norm",
    )(scalars, xr, gain, *terms)


def feed_kernel(n_ref, g_ref, wgo, wgx, wuo, wux, wdo, wdx, inner_ref, gg_ref, gu_ref, ffn_ref, gn_ref, facc, gacc):
    step = pl.program_id(0)
    half = wgo.shape[0]
    no, nx = n_ref[:, :half], n_ref[:, half:]
    gate = dot_nn(no, wgo[...]) + dot_nn(nx, wgx[...])
    up = dot_nn(no, wuo[...]) + dot_nn(nx, wux[...])
    gi = dot_nt(g_ref[0, :, :half], wdo[...]) + dot_nt(g_ref[0, :, half:], wdx[...])
    sig = jax.nn.sigmoid(gate)
    silu = gate * sig
    inner = (silu * up).astype(BF16)
    gg = (gi * up * sig * (1.0 + gate * (1.0 - sig))).astype(BF16)
    gu = (gi * silu).astype(BF16)
    inner_ref[...] = inner
    gg_ref[...] = gg
    gu_ref[...] = gu

    @pl.when(step == 0)
    def _():
        facc[...] = jnp.zeros_like(facc)
        gacc[...] = jnp.zeros_like(gacc)

    facc[:, :half] += dot_nn(inner, wdo[...])
    facc[:, half:] += dot_nn(inner, wdx[...])
    gacc[:, :half] += dot_nt(gg, wgo[...]) + dot_nt(gu, wuo[...])
    gacc[:, half:] += dot_nt(gg, wgx[...]) + dot_nt(gu, wux[...])

    @pl.when(step == pl.num_programs(0) - 1)
    def _():
        ffn_ref[...] = facc[...].astype(BF16)
        gn_ref[...] = gacc[...].astype(BF16)


def feed(n2, chunk, rows, gf, seq, part, gate, up, down):
    width = n2.shape[1]
    _, half, hidden = gate.shape
    hb = min(512, hidden)
    row = [pl.BlockSpec((None, half, hb), lambda h, side=side: (side, 0, h)) for side in range(2)]
    col = [pl.BlockSpec((None, hb, half), lambda h, side=side: (side, h, 0)) for side in range(2)]
    whole = pl.BlockSpec((rows, width), lambda h: (0, 0))
    tile = pl.BlockSpec((rows, hb), lambda h: (0, h))
    return pl.pallas_call(
        feed_kernel,
        grid=(hidden // hb,),
        in_specs=[pl.BlockSpec((rows, width), lambda h: (chunk, 0)), pl.BlockSpec((1, rows, width), lambda h: (seq, part, 0))] + row + row + col,
        out_specs=[tile, tile, tile, whole, whole],
        out_shape=[shape((rows, hidden), BF16)] * 3 + [shape((rows, width), BF16)] * 2,
        scratch_shapes=[pltpu.VMEM((rows, width), F32), pltpu.VMEM((rows, width), F32)],
        compiler_params=PARAMS,
        cost_estimate=cost(12 * rows * width * hidden, 12 * half * hidden + 14 * rows * width, rows * hidden),
        name="feed_forward",
    )(n2, gf, gate, gate, up, up, down, down)


def second_back_kernel(terms, hidden_ref, gf_ref, gain_ref, *refs):
    term_refs, (gb_ref, gh_ref, gain_out) = refs[:terms], refs[terms:]
    e = term_refs[0][...].astype(F32)
    for ref in term_refs[1:]:
        e = e + ref[...].astype(F32)
    hidden = hidden_ref[...]
    inv = inverse_rms(hidden)
    hat = hidden * inv
    eg = e * gain_ref[...]
    gh = gf_ref[0].astype(F32) + inv * (eg - hat * jnp.mean(eg * hat, axis=-1, keepdims=True))
    gh_ref[...] = gh
    gb_ref[...] = gh.astype(BF16)
    gain_out[...] = jnp.sum(e * hat, axis=0, keepdims=True)


def second_back(hidden, chunk, gf, seq, part, gain, terms):
    rows, width = terms[0].shape
    flat = pl.BlockSpec((rows, width), lambda i: (0, 0))
    line = pl.BlockSpec((1, width), lambda i: (0, 0))
    return pl.pallas_call(
        functools.partial(second_back_kernel, len(terms)),
        grid=(1,),
        in_specs=[pl.BlockSpec((rows, width), lambda i: (chunk, 0)), pl.BlockSpec((1, rows, width), lambda i: (seq, part, 0)), line]
        + [flat] * len(terms),
        out_specs=[flat, flat, line],
        out_shape=[shape((rows, width), BF16), shape((rows, width), F32), shape((1, width), F32)],
        compiler_params=PARAMS,
        cost_estimate=cost(20 * rows * width, (12 + 2 * len(terms)) * rows * width),
        name="second_norm_back",
    )(hidden, gf, gain, *terms)


def branch_back_kernel(chunks, *refs):
    gb_refs, (w_ref, core_ref, own_ref, oth_ref) = refs[:chunks], refs[chunks:]
    half = w_ref.shape[2]
    rows = gb_refs[0].shape[0]
    heads_half = own_ref.shape[0]
    first = core_ref[0] == 0
    for k, ref in enumerate(gb_refs):
        da = dot_nt(w_ref[0], ref[:, :half]) + dot_nt(w_ref[1], ref[:, half:])
        da = da.astype(BF16)
        low, high = da[:heads_half], da[heads_half:]
        cut = slice(k * rows, (k + 1) * rows)
        own_ref[:, cut] = jnp.where(first, low, high)
        oth_ref[:, cut] = jnp.where(first, high, low)


def branch_back(gbs, weight, core):
    chunks = len(gbs)
    rows, width = gbs[0].shape
    dim = weight.shape[1]
    full = pl.BlockSpec(memory_space=pltpu.VMEM)
    return pl.pallas_call(
        functools.partial(branch_back_kernel, chunks),
        in_specs=[full] * (chunks + 1) + [SMEM],
        out_specs=[full] * 2,
        out_shape=[shape((dim // 2, chunks * rows), BF16)] * 2,
        compiler_params=PARAMS,
        cost_estimate=cost(2 * dim * chunks * rows * width, 2 * dim * width + 2 * chunks * rows * width),
        name="attention_branch_back",
    )(*gbs, weight, core)


def attend_back_kernel(block, groups, scal_ref, all_ref, att_ref, inv_ref, own_ref, got_ref, out_own, out_oth, da_all, grads):
    span = own_ref.shape[1]
    hd = all_ref.shape[0] // (groups + 2)
    length, core = scal_ref[0], scal_ref[1]
    low, high = join_positions(core, own_ref[...], got_ref[...])
    da_all[:, :span] = low
    da_all[:, span:] = high
    scale = log2e / math.sqrt(hd)
    back = 1.0 / math.sqrt(hd)
    krow = lax.broadcasted_iota(jnp.int32, (block, groups * block), 0)
    qcol = lax.broadcasted_iota(jnp.int32, (block, groups * block), 1) % block
    base = groups * hd
    grads[base:, :] = jnp.zeros((2 * hd, 2 * span), F32)
    for i in range(2 * span // block):
        cut = slice(i * block, (i + 1) * block)

        def rows(ref):
            return jnp.concatenate([ref[g * hd : (g + 1) * hd, cut] for g in range(groups)], axis=1)

        q = rows(all_ref)
        da = rows(da_all)
        inv = jnp.concatenate([inv_ref[g : g + 1, cut] for g in range(groups)], axis=1)
        delta = jnp.sum(rows(att_ref).astype(F32) * da.astype(F32), axis=0, keepdims=True)
        dq = jnp.zeros((hd, groups * block), F32)
        for j in range(i + 1):
            kcut = slice(j * block, (j + 1) * block)
            key = all_ref[base : base + hd, kcut]
            s = dot_tn(key, q) * scale
            ok = (krow + j * block) < length
            if j == i:
                ok = ok & (krow <= qcol)
            p = jnp.where(ok, jnp.exp2(s) * inv, 0.0)
            dp = dot_tn(all_ref[base + hd : base + 2 * hd, kcut], da)
            ds = (p * (dp - delta)).astype(BF16)
            dq = dq + dot_nn(key, ds)
            grads[base : base + hd, kcut] += dot_nt(q, ds) * back
            grads[base + hd : base + 2 * hd, kcut] += dot_nt(da, p.astype(BF16))
        dq = dq * back
        for g in range(groups):
            grads[g * hd : (g + 1) * hd, cut] = dq[:, g * block : (g + 1) * block]
    mine, theirs = join_positions(core, grads[:, :span], grads[:, span:])
    out_own[...] = mine.astype(BF16)
    out_oth[...] = theirs.astype(BF16)


def attend_back(scalars, everything, att, inv, own, got, groups):
    rows, slots = everything.shape
    span = slots // 2
    block = min(256, span)
    full = pl.BlockSpec(memory_space=pltpu.VMEM)
    return pl.pallas_call(
        functools.partial(attend_back_kernel, block, groups),
        in_specs=[SMEM] + [full] * 5,
        out_specs=[full] * 2,
        out_shape=[shape((rows, span), BF16)] * 2,
        scratch_shapes=[pltpu.VMEM(att.shape, BF16), pltpu.VMEM((rows, slots), F32)],
        compiler_params=PARAMS,
        cost_estimate=cost(30 * att.shape[0] * slots * slots, 12 * rows * slots, groups * slots * slots),
        name="attend_backward",
    )(scalars, everything, att, inv, own, got)


def heads_back_kernel(hd, nq, nk, own_ref, got_ref, pre_ref, cos_ref, sin_ref, qg_ref, kg_ref, x_ref, w_ref, core_ref, dpre_ref, first_ref, gain_ref, hgain_ref):
    half = w_ref.shape[1]
    low, high = join_positions(core_ref[0], own_ref[...].astype(F32), got_ref[...].astype(F32))
    sides = (nq // 2, nk // 2, nk // 2)
    grads = [[], [], []]
    for side in (low, high):
        at = 0
        for kind, count in enumerate(sides):
            for h in range(count):
                grads[kind].append(side[at : at + hd])
                at += hd
    cosine, sine = cos_ref[...], sin_ref[...]
    done = []
    sums = [0.0, 0.0]
    for h in range(nq + nk):
        kind = 0 if h < nq else 1
        g = grads[kind][h - kind * nq]
        a, b = g[: hd // 2], g[hd // 2 :]
        g = jnp.concatenate([a * cosine + b * sine, b * cosine - a * sine], axis=0)
        v = pre_ref[h * hd : (h + 1) * hd, :]
        inv = lax.rsqrt(jnp.mean(v * v, axis=0, keepdims=True) + epsilon)
        hat = v * inv
        sums[kind] = sums[kind] + jnp.sum(g * hat, axis=1, keepdims=True)
        gg = g * (qg_ref[...] if kind == 0 else kg_ref[...])
        done.append(inv * (gg - hat * jnp.mean(gg * hat, axis=0, keepdims=True)))
    done += grads[2]
    hgain_ref[:hd, :] = jnp.broadcast_to(sums[0], (hd, 128))
    hgain_ref[hd:, :] = jnp.broadcast_to(sums[1], (hd, 128))
    dpre = jnp.concatenate(done, axis=0).T.astype(BF16)
    dpre_ref[...] = dpre
    x = x_ref[0].astype(F32)
    hat = x * inverse_rms(x)
    for k in range(2):
        cut = slice(k * half, (k + 1) * half)
        part = dot_nt(dpre, w_ref[k])
        first_ref[:, cut] = part.astype(BF16)
        gain_ref[:, cut] = jnp.sum(part * hat[:, cut], axis=0, keepdims=True)


def heads_back(own, got, pre, cosine, sine, qgain, kgain, xr, seq, weight, core, hd, nq, nk):
    span = own.shape[1]
    _, half, cols = weight.shape
    width = 2 * half
    whole = lambda a: pl.BlockSpec(a.shape, lambda i: (0,) * len(a.shape))
    outs = [shape((span, cols), BF16), shape((span, width), BF16), shape((1, width), F32), shape((2 * hd, 128), F32)]
    return pl.pallas_call(
        functools.partial(heads_back_kernel, hd, nq, nk),
        grid=(1,),
        in_specs=[whole(a) for a in (own, got, pre, cosine, sine, qgain, kgain)]
        + [pl.BlockSpec((1, span, width), lambda i: (seq, 0, 0)), whole(weight), SMEM],
        out_specs=[whole(o) for o in outs],
        out_shape=outs,
        compiler_params=PARAMS,
        cost_estimate=cost(2 * span * width * cols, 4 * span * width + 4 * half * cols),
        name="query_key_value_back",
    )(own, got, pre, cosine, sine, qgain, kgain, xr, weight, core)


def place_blocks(order, ids, first_id, value, out_ref):
    piece = value.shape[-1] // order
    for k in range(order):
        if order == 1:
            out_ref[...] = value
        else:
            dst = pl.ds(pl.multiple_of(ids[first_id + k] * piece, piece), piece)
            out_ref[:, dst] = value[:, k * piece : (k + 1) * piece]


def output_kernel(order, scal_ref, got_ref, f0_ref, f1_ref, h0_ref, h1_ref, out_ref, stat_ref):
    low = scal_ref[0] * 2 < scal_ref[3]
    rows = out_ref.shape[0]
    ffn = got_ref[...].astype(F32) + jnp.where(low, f0_ref[...], f1_ref[...]).astype(F32)
    hidden = jnp.where(low, h0_ref[...], h1_ref[...])
    place = scal_ref[2] + lax.broadcasted_iota(jnp.int32, (rows, 1), 0)
    valid = (place < scal_ref[1]).astype(F32)
    stat_ref[...] = jnp.broadcast_to(jnp.sum(valid * ffn * ffn, keepdims=True), (8, 128))
    place_blocks(order, scal_ref, 4, (hidden + ffn).astype(BF16), out_ref)


def share_specs(rows, width, per):
    return [
        pl.BlockSpec((rows, width), lambda i, s: (jnp.minimum(s[0], per - 1), 0)),
        pl.BlockSpec((rows, width), lambda i, s: (jnp.maximum(s[0] - per, 0), 0)),
    ]


def output_share(scalars, got, ffns, hiddens, order):
    rows, width = got.shape
    pair = share_specs(rows, width, ffns[0].shape[0] // rows)
    flat = pl.BlockSpec((rows, width), lambda i, s: (0, 0))
    return pl.pallas_call(
        functools.partial(output_kernel, order),
        grid_spec=pltpu.PrefetchScalarGridSpec(
            num_scalar_prefetch=1,
            grid=(1,),
            in_specs=[flat] + pair + pair,
            out_specs=[flat, pl.BlockSpec((8, 128), lambda i, s: (0, 0))],
        ),
        out_shape=[shape((rows, width), BF16), shape((8, 128), F32)],
        compiler_params=PARAMS,
        cost_estimate=cost(6 * rows * width, 16 * rows * width),
        name="output_share",
    )(scalars, got, *ffns, *hiddens)


def input_kernel(order, scal_ref, got_ref, part_ref, g0_ref, g1_ref, x_ref, gain_ref, out_ref):
    low = scal_ref[0] * 2 < scal_ref[3]
    e = got_ref[...].astype(F32) + part_ref[...].astype(F32)
    gh = jnp.where(low, g0_ref[...], g1_ref[...])
    x = x_ref[0].astype(F32)
    inv = inverse_rms(x)
    hat = x * inv
    eg = e * gain_ref[...]
    value = gh + inv * (eg - hat * jnp.mean(eg * hat, axis=-1, keepdims=True))
    place_blocks(order, scal_ref, 4, value, out_ref)


def input_share(scalars, got, part, ghs, xr, seq, gain, order):
    rows, width = got.shape
    pair = share_specs(rows, width, ghs[0].shape[0] // rows)
    flat = pl.BlockSpec((rows, width), lambda i, s: (0, 0))
    return pl.pallas_call(
        functools.partial(input_kernel, order),
        grid_spec=pltpu.PrefetchScalarGridSpec(
            num_scalar_prefetch=1,
            grid=(1,),
            in_specs=[flat, pl.BlockSpec((rows, width), lambda i, s: (s[0], 0))]
            + pair
            + [pl.BlockSpec((1, rows, width), lambda i, s: (seq, s[0], 0)), pl.BlockSpec((1, width), lambda i, s: (0, 0))],
            out_specs=flat,
        ),
        out_shape=shape((rows, width), F32),
        compiler_params=PARAMS,
        cost_estimate=cost(12 * rows * width, 20 * rows * width),
        name="input_share",
    )(scalars, got, part, *ghs, xr, gain)


def weight_grad_kernel(count, extra, *refs):
    a_refs, b_refs, out = refs[:count], refs[count : 2 * count], refs[-1]
    total = dot_tn(a_refs[0][...], b_refs[0][...])
    for a, b in zip(a_refs[1:], b_refs[1:]):
        total = total + dot_tn(a[...], b[...])
    if extra:
        total = total + refs[2 * count][...].astype(F32)
    out[...] = total.astype(BF16)


def weight_grad(lefts, rights, side, axis, add=None):
    count = len(lefts)
    rows_all, cols_all = lefts[0].shape[1], rights[0].shape[1]
    dims = [rows_all, cols_all]
    dims[axis] //= 2
    rows, cols = min(512, dims[0]), min(2048, dims[1])
    row_at = side * (dims[0] // rows) if axis == 0 else 0
    col_at = side * (dims[1] // cols) if axis == 1 else 0
    specs = [pl.BlockSpec((a.shape[0], rows), lambda j, i: (0, i + row_at)) for a in lefts]
    specs += [pl.BlockSpec((b.shape[0], cols), lambda j, i: (0, j + col_at)) for b in rights]
    tile = pl.BlockSpec((rows, cols), lambda j, i: (i, j))
    tokens = sum(a.shape[0] for a in lefts)
    return pl.pallas_call(
        functools.partial(weight_grad_kernel, count, add is not None),
        grid=(dims[1] // cols, dims[0] // rows),
        in_specs=specs + ([tile] if add is not None else []),
        out_specs=tile,
        out_shape=shape(dims, BF16),
        compiler_params=PARAMS,
        cost_estimate=cost(2 * tokens * dims[0] * dims[1], 2 * tokens * sum(dims) + 2 * dims[0] * dims[1]),
        name="weight_grad",
    )(*lefts, *rights, *([add] if add is not None else []))


def xor_one(index):
    return index + 1 - 2 * (index % 2)


def remote(src, dst, send, recv, device):
    return pltpu.make_async_remote_copy(
        src_ref=src, dst_ref=dst, send_sem=send, recv_sem=recv, device_id=device, device_id_type=pl.DeviceIdType.MESH
    )


def greet(others):
    barrier = pltpu.get_barrier_semaphore()
    count = 0
    for needed, device in others:
        if needed is None:
            pl.semaphore_signal(barrier, inc=1, device_id=device, device_id_type=pl.DeviceIdType.MESH)
            count = count + 1
        else:

            @pl.when(needed)
            def _():
                pl.semaphore_signal(barrier, inc=1, device_id=device, device_id_type=pl.DeviceIdType.MESH)

            count = count + jnp.where(needed, 1, 0)
    pl.semaphore_wait(barrier, count)


class Gather:
    def __init__(self, shard, dst, axis, send, recv, local, near_x, near_y, near_core):
        piece = shard.shape[axis]
        half = shard.shape[0] // 2

        def block(side, k):
            cut = pl.ds(k * piece, piece)
            return dst.at[side, cut, :] if axis == 0 else dst.at[side, :, cut]

        def part(k, h):
            if axis == 0:
                return dst.at[0, pl.ds(k * piece + h * half, half), :]
            return dst.at[0, pl.ds(h * half, half), pl.ds(k * piece, piece)]

        sem = lambda k: (send.at[k], recv.at[k])
        self.local = pltpu.make_async_copy(shard, block(0, 0), local)
        self.x = remote(shard, block(0, 1), *sem(0), near_x)
        self.y = remote(shard, block(0, 2), *sem(1), near_y)
        self.dx = remote(part(2, 0), part(3, 0), *sem(2), near_x)
        self.dy = remote(part(1, 1), part(3, 1), *sem(3), near_y)
        self.cores = [remote(shard, block(1, 0), *sem(4), near_core)]
        self.cores += [remote(block(0, k), block(1, k), *sem(4 + k), near_core) for k in (1, 2, 3)]

    def first(self):
        self.x.start()
        self.y.start()
        self.cores[0].start()
        self.local.start()

    def second(self):
        self.y.wait_recv()
        self.dx.start()
        self.cores[2].start()
        self.x.wait_recv()
        self.dy.start()
        self.cores[1].start()

    def third(self):
        self.dx.wait_recv()
        self.dy.wait_recv()
        self.cores[3].start()

    def arrived(self):
        self.local.wait()
        for copy in self.cores:
            copy.wait_recv()

    def sent(self):
        for copy in [self.x, self.y, self.dx, self.dy] + self.cores:
            copy.wait_send()


def forward_kernel(
    hd, nq, nk, block, sub,
    len_ref, x_hbm, cot_hbm, wqkv, wout, wgate, wup, wdown, gain_ref, cos_ref, sin_ref, qg_ref, kg_ref,
    xr_hbm, n1_hbm, gf_hbm, qkv_hbm, out_hbm, gate_hbm, up_hbm, down_hbm, hidden_hbm, n2_hbm,
    gains_ref, pre_ref, all_ref, att_ref, inv_ref, tok_ref, stat_ref,
    xr_v, cot_v, n1_v, qkv_v, out_v, ex_own, ex_send, ex_got, at_own, at_send, at_got,
    part_v, in_v, back_v, total_v, hid_v, norm_v,
    load_sem, store_sem, wsend, wrecv, wloc, gsend, grecv, exsend, exrecv, zsend, zrecv, hid_sem,
):
    seqs, span, width = xr_v.shape
    groups = nq // nk
    row, core, rank = lax.axis_index("dp"), lax.axis_index("context"), lax.axis_index("tensor")
    start = core * span
    near = [row, xor_one(row), (row + 2) % 4, 3 - row]
    inner = (rank % 3) != 0
    near_x, near_y, near_core = {"dp": near[1]}, {"dp": near[2]}, {"context": 1 - core}
    z_side, z_mid = {"tensor": xor_one(rank)}, {"tensor": 3 - rank}
    piece = width // 8
    total_subs = part_v.shape[0]
    per = span // sub
    first_core = core == 0

    loads = []
    for at, (src, dst) in enumerate(((x_hbm, xr_v), (cot_hbm, cot_v))):
        for s in range(seqs):
            for o in range(2):
                for k in range(4):
                    b = near[k] * 2 + (core if o == 0 else 1 - core)
                    cut = pl.ds(pl.multiple_of(b * piece, piece), piece)
                    loads.append(
                        pltpu.make_async_copy(
                            src.at[s, :, cut], dst.at[s, :, pl.ds((o * 4 + k) * piece, piece)], load_sem.at[at, s, o * 4 + k]
                        )
                    )
    for copy in loads:
        copy.start()

    others = []
    for o in range(2):
        for k in range(4):
            if o or k:
                others.append((o * 4 + k, {"dp": near[k], "context": core if o == 0 else 1 - core}))
    greet([(None, d) for _, d in others] + [(None, z_side), (inner, z_mid)])

    gains = [remote(gain_ref, gains_ref.at[b], gsend.at[b], grecv.at[b], d) for b, d in others]
    for copy in gains:
        copy.start()
    weights = [
        Gather(shard, dst, axis, wsend.at[i], wrecv.at[i], wloc.at[i], near_x, near_y, near_core)
        for i, (shard, dst, axis) in enumerate(
            ((wqkv, qkv_v, 0), (wout, out_v, 1), (wgate, gate_hbm, 0), (wup, up_hbm, 0), (wdown, down_hbm, 1))
        )
    ]
    w_qkv, w_out, w_gate, w_up, w_down = weights
    w_qkv.first()
    w_out.first()
    gains_ref[0] = gain_ref[...]

    for copy in loads[len(loads) // 2 :]:
        copy.wait()

    def mask_rows(i, carry):
        s, t = i // (span // 16), i % (span // 16)
        cut = pl.ds(pl.multiple_of(t * 16, 16), 16)
        place = start + t * 16 + lax.broadcasted_iota(jnp.int32, (16, 1), 0)
        valid = (place < len_ref[s]).astype(F32)
        cot_v[s, cut, :] = (cot_v[s, cut, :].astype(F32) * valid).astype(BF16)
        return carry

    lax.fori_loop(0, seqs * span // 16, mask_rows, 0)
    store_gf = pltpu.make_async_copy(cot_v, gf_hbm, store_sem.at[0])
    store_gf.start()
    for copy in loads[: len(loads) // 2]:
        copy.wait()
    store_xr = pltpu.make_async_copy(xr_v, xr_hbm, store_sem.at[1])
    store_xr.start()
    for copy in gains:
        copy.wait_recv()
    gain1 = jnp.concatenate([gains_ref[b, 0:1, :] for b in range(8)], axis=1).astype(F32)
    gain2 = jnp.concatenate([gains_ref[b, 1:2, :] for b in range(8)], axis=1).astype(F32)

    def norm_rows(i, carry):
        s, t = i // (span // 16), i % (span // 16)
        cut = pl.ds(pl.multiple_of(t * 16, 16), 16)
        x = xr_v[s, cut, :].astype(F32)
        n1_v[s, cut, :] = (x * inverse_rms(x) * gain1).astype(BF16)
        return carry

    lax.fori_loop(0, seqs * span // 16, norm_rows, 0)
    store_n1 = pltpu.make_async_copy(n1_v, n1_hbm, store_sem.at[2])
    store_n1.start()
    w_qkv.second()
    w_out.second()
    w_gate.first()
    w_qkv.third()
    w_out.third()
    w_qkv.arrived()
    w_up.first()

    cosine, sine = cos_ref[...], sin_ref[...]
    half = width // 2

    def exchange(s):
        return remote(ex_send.at[s], ex_got.at[s], exsend.at[0, s], exrecv.at[0, s], near_core)

    def project(s, carry):
        x = n1_v[s]
        flat = dot_nn(x[:, :half], qkv_v[0]) + dot_nn(x[:, half:], qkv_v[1])
        turned = flat.T
        pre_ref[s] = turned[: (nq + nk) * hd]
        done = []
        for h in range(nq + nk):
            v = turned[h * hd : (h + 1) * hd]
            inv = lax.rsqrt(jnp.mean(v * v, axis=0, keepdims=True) + epsilon)
            v = v * inv * (qg_ref[...] if h < nq else kg_ref[...])
            a, b = v[: hd // 2], v[hd // 2 :]
            done.append(jnp.concatenate([a * cosine - b * sine, b * cosine + a * sine], axis=0))
        for h in range(nk):
            lo = (nq + nk + h) * hd
            done.append(turned[lo : lo + hd])
        parts = [[], []]
        for begin_at, count in ((0, nq), (nq, nk), (nq + nk, nk)):
            for side in range(2):
                parts[side] += done[begin_at + side * count // 2 : begin_at + (side + 1) * count // 2]
        low = jnp.concatenate(parts[0], axis=0)
        high = jnp.concatenate(parts[1], axis=0)
        ex_own[s] = jnp.where(first_core, low, high).astype(BF16)
        ex_send[s] = jnp.where(first_core, high, low).astype(BF16)
        exchange(s).start()
        return carry

    lax.fori_loop(0, seqs, project, 0)
    store_qkv = pltpu.make_async_copy(qkv_v, qkv_hbm, store_sem.at[3])
    store_qkv.start()

    scale = log2e / math.sqrt(hd)
    krow = lax.broadcasted_iota(jnp.int32, (block, groups * block), 0)
    qcol = lax.broadcasted_iota(jnp.int32, (block, groups * block), 1) % block
    base = groups * hd

    def give(s):
        return remote(at_send.at[s], at_got.at[s], exsend.at[1, s], exrecv.at[1, s], near_core)

    def attention(s, carry):
        exchange(s).wait_recv()
        low, high = join_positions(core, ex_own[s], ex_got[s])
        all_ref[s, :, :span] = low
        all_ref[s, :, span:] = high
        length = len_ref[s]
        for i in range(2 * span // block):
            cut = slice(i * block, (i + 1) * block)
            q = jnp.concatenate([all_ref[s, g * hd : (g + 1) * hd, cut] for g in range(groups)], axis=1)
            acc = jnp.zeros((hd, groups * block), F32)
            total = jnp.zeros((1, groups * block), F32)
            for j in range(i + 1):
                kcut = slice(j * block, (j + 1) * block)
                score = dot_tn(all_ref[s, base : base + hd, kcut], q) * scale
                ok = (krow + j * block) < length
                if j == i:
                    ok = ok & (krow <= qcol)
                e = jnp.where(ok, jnp.exp2(score), 0.0)
                total = total + jnp.sum(e, axis=0, keepdims=True)
                acc = acc + dot_nn(all_ref[s, base + hd : base + 2 * hd, kcut], e.astype(BF16))
            inv = 1.0 / total
            att = (acc * inv).astype(BF16)
            for g in range(groups):
                att_ref[s, g * hd : (g + 1) * hd, cut] = att[:, g * block : (g + 1) * block]
                inv_ref[s, g : g + 1, cut] = inv[:, g * block : (g + 1) * block]
        mine, theirs = join_positions(core, att_ref[s, :, :span], att_ref[s, :, span:])
        at_own[s] = mine
        at_send[s] = theirs
        give(s).start()
        return carry

    lax.fori_loop(0, seqs, attention, 0)
    w_out.arrived()
    store_out = pltpu.make_async_copy(out_v, out_hbm, store_sem.at[4])
    store_out.start()

    moving = Chain(rank, part_v, in_v, back_v, zsend, zrecv)

    def branch_rows(s, carry):
        give(s).wait_recv()
        low, high = join_positions(core, at_own[s], at_got[s])
        att = jnp.concatenate([low, high], axis=0).T
        tok_ref[s] = att
        for k in range(per):
            u = s * per + k
            rows = att[k * sub : (k + 1) * sub]
            part_v[u, :, :half] = dot_nn(rows, out_v[0]).astype(BF16)
            part_v[u, :, half:] = dot_nn(rows, out_v[1]).astype(BF16)

            moving.begin(u)
        return carry

    lax.fori_loop(0, seqs, branch_rows, 0)
    w_gate.second()
    w_down.first()
    stat_ref[...] = jnp.zeros_like(stat_ref)

    def hidden_store(u):
        cut = pl.ds(pl.multiple_of(u * sub, sub), sub)
        return (
            pltpu.make_async_copy(hid_v.at[u % 2], hidden_hbm.at[cut, :], hid_sem.at[0, u % 2]),
            pltpu.make_async_copy(norm_v.at[u % 2], n2_hbm.at[cut, :], hid_sem.at[1, u % 2]),
        )

    def finish(u):
        s, t = u // per, u % per
        cut = pl.ds(pl.multiple_of(t * sub, sub), sub)

        moving.total(u, total_v)

        @pl.when(u >= 2)
        def _():
            for copy in hidden_store(u - 2):
                copy.wait()

        length = len_ref[s]

        def body(piece_rows, first):
            total = total_v[piece_rows, :]
            resid = xr_v[s, pl.ds(pl.multiple_of(t * sub + first, 16), 16), :].astype(F32)
            hidden = resid + total
            hid_v[u % 2, piece_rows, :] = hidden
            norm_v[u % 2, piece_rows, :] = (hidden * inverse_rms(hidden) * gain2).astype(BF16)
            place = start + t * sub + first + lax.broadcasted_iota(jnp.int32, (16, 1), 0)
            valid = (place < length).astype(F32)
            stat_ref[0] += fold_lanes(valid * resid * resid)
            stat_ref[1] += fold_lanes(valid * total * total)

        by_pieces(sub, body)
        for copy in hidden_store(u):
            copy.start()

    def chain(i, carry):
        moving.middle(i)
        moving.outward(i - 1)

        @pl.when(i >= 2)
        def _():
            finish(i - 2)

        @pl.when(i == total_subs // 2 - 2)
        def _():
            w_gate.third()
            w_up.second()

        @pl.when(i == total_subs - 1)
        def _():
            w_up.third()
            w_down.second()

        return carry

    lax.fori_loop(0, total_subs + 2, chain, 0)
    w_down.third()
    for u in (total_subs - 2, total_subs - 1):
        for copy in hidden_store(u):
            copy.wait()

    moving.settle()
    for s in range(seqs):
        exchange(s).wait_send()
        give(s).wait_send()
    for copy in gains:
        copy.wait_send()
    for w in weights[2:]:
        w.arrived()
    for w in weights:
        w.sent()
    for copy in (store_gf, store_xr, store_n1, store_qkv, store_out):
        copy.wait()


def forward(lengths, x, cot, w_qkv, w_out, w_gate, w_up, w_down, gains, cosine, sine, qgain, kgain, hd, nq, nk):
    seqs, span, width = x.shape
    half = width // 2
    groups = nq // nk
    sub = min(128, span)
    subs = seqs * span // sub
    block = min(256, span)
    hidden = w_gate.shape[1]
    cols = w_qkv.shape[1]
    rows = cols // 2
    any_space = pl.BlockSpec(memory_space=pl.ANY)
    vmem = pl.BlockSpec(memory_space=pltpu.VMEM)
    wide = (seqs, span, width)
    large = [
        shape(wide, BF16), shape(wide, BF16), shape(wide, BF16),
        shape((2, half, cols), BF16), shape((2, w_out.shape[0], half), BF16),
        shape((2, half, hidden), BF16), shape((2, half, hidden), BF16), shape((2, hidden, half), BF16),
        shape((seqs * span, width), F32), shape((seqs * span, width), BF16),
    ]
    small = [
        shape((8,) + gains.shape, BF16), shape((seqs, (nq + nk) * hd, span), F32), shape((seqs, rows, 2 * span), BF16),
        shape((seqs, groups * hd, 2 * span), BF16), shape((seqs, groups, 2 * span), F32), shape((seqs, span, nq * hd), BF16),
        shape((2, 8, 128), F32),
    ]
    dma = pltpu.SemaphoreType.DMA
    ex = pltpu.VMEM((seqs, rows, span), BF16)
    at = pltpu.VMEM((seqs, groups * hd, span), BF16)
    moving = pltpu.VMEM((subs, sub, width), BF16)
    flops = 2 * seqs * span * width * (cols + nq * hd) + 16 * seqs * nq * hd * span * span
    return pl.pallas_call(
        functools.partial(forward_kernel, hd, nq, nk, block, sub),
        in_specs=[SMEM] + [any_space] * 7 + [vmem] * 5,
        out_specs=[any_space] * len(large) + [vmem] * len(small),
        out_shape=large + small,
        scratch_shapes=[
            pltpu.VMEM(wide, BF16), pltpu.VMEM(wide, BF16), pltpu.VMEM(wide, BF16),
            pltpu.VMEM((2, half, cols), BF16), pltpu.VMEM((2, w_out.shape[0], half), BF16),
            ex, ex, ex, at, at, at,
            moving, moving, moving,
            pltpu.VMEM((sub, width), F32), pltpu.VMEM((2, sub, width), F32), pltpu.VMEM((2, sub, width), BF16),
            dma((2, seqs, 8)), dma((5,)), dma((5, 8)), dma((5, 8)), dma((5,)), dma((8,)), dma((8,)),
            dma((2, seqs)), dma((2, seqs)), dma((3, subs)), dma((3, subs)), dma((2, 2)),
        ],
        compiler_params=pltpu.CompilerParams(vmem_limit_bytes=VMEM_BYTES, collective_id=1, has_side_effects=True),
        cost_estimate=cost(flops, 80 * seqs * span * width),
        name="attention_forward",
    )(lengths, x, cot, w_qkv, w_out, w_gate, w_up, w_down, gains, cosine, sine, qgain, kgain)


def by_pieces(count, body, size=16):
    def one(p, carry):
        body(pl.ds(pl.multiple_of(p * size, size), size), p * size)
        return carry

    lax.fori_loop(0, count // size, one, 0)


def fold_lanes(values):
    tiles = values[:8] + values[8:]
    return sum(tiles[:, k * 128 : (k + 1) * 128] for k in range(tiles.shape[1] // 128))


class Chain:
    def __init__(self, rank, part, arrive, back, send, recv):
        self.inner = (rank % 3) != 0
        self.outer = (rank % 3) == 0
        self.part, self.arrive, self.back = part, arrive, back
        self.send, self.recv = send, recv
        self.side, self.mid = {"tensor": xor_one(rank)}, {"tensor": 3 - rank}
        self.count = part.shape[0]

    def hop_in(self, u):
        return remote(self.part.at[u], self.arrive.at[u], self.send.at[0, u], self.recv.at[0, u], self.side)

    def hop_mid(self, u):
        return remote(self.arrive.at[u], self.back.at[u], self.send.at[1, u], self.recv.at[1, u], self.mid)

    def hop_out(self, u):
        return remote(self.part.at[u], self.back.at[u], self.send.at[2, u], self.recv.at[2, u], self.side)

    def add(self, into, one, two, u):
        def body(cut, first):
            into[u, cut, :] = (one[u, cut, :].astype(F32) + two[u, cut, :].astype(F32)).astype(BF16)

        by_pieces(self.part.shape[1], body)

    def begin(self, u):
        @pl.when(self.outer)
        def _():
            self.hop_in(u).start()

    def middle(self, u):
        @pl.when((u >= 0) & (u < self.count) & self.inner)
        def _():
            self.hop_in(u).wait_recv()
            self.add(self.arrive, self.part, self.arrive, u)
            self.hop_mid(u).start()

    def outward(self, u):
        @pl.when((u >= 0) & (u < self.count) & self.inner)
        def _():
            self.hop_mid(u).wait_recv()
            self.add(self.part, self.part, self.back, u)
            self.hop_out(u).start()

    def total(self, u, into):
        @pl.when(self.inner)
        def _():
            def body(cut, first):
                into[cut, :] = self.arrive[u, cut, :].astype(F32) + self.back[u, cut, :].astype(F32)

            by_pieces(self.part.shape[1], body)

        @pl.when(self.outer)
        def _():
            self.hop_out(u).wait_recv()

            def body(cut, first):
                into[cut, :] = self.part[u, cut, :].astype(F32) + self.back[u, cut, :].astype(F32)

            by_pieces(self.part.shape[1], body)

    def settle(self):
        def one(u, carry):
            @pl.when(self.outer)
            def _():
                self.hop_in(u).wait_send()

            @pl.when(self.inner)
            def _():
                self.hop_mid(u).wait_send()
                self.hop_out(u).wait_send()

            return carry

        lax.fori_loop(0, self.count, one, 0)


def feed_both_kernel(
    hb, sub, rows,
    n2_hbm, gf_hbm, gate_hbm, up_hbm, down_hbm, hidden_hbm, gain_ref,
    ffn_hbm, gb_hbm, gh_hbm, dgate_hbm, dup_hbm, ddown_hbm, gain_out,
    n2_v, gf_v, inner_v, gg_v, gu_v, facc, gacc, wrow, wcol, part_v, in_v, back_v, total_v, hid_v, gh_v, gb_v, ffn_v, stage_row, stage_col,
    load_sem, wsem, zsend, zrecv, hid_sem, out_sem, ffn_sem, csend, crecv, store_sem, free_sem,
):
    core, rank = lax.axis_index("context"), lax.axis_index("tensor")
    near_core = {"context": 1 - core}
    tokens, width = n2_v.shape
    half = width // 2
    hidden = inner_v.shape[1]
    hsteps = hidden // hb
    steps = tokens // rows * hsteps
    per = rows // sub
    chain = Chain(rank, part_v, in_v, back_v, zsend, zrecv)
    subs = chain.count

    def load_weights(i):
        slot, h = i % 2, i % hsteps
        cut = pl.ds(pl.multiple_of(h * hb, hb), hb)
        copies = []
        for side in range(2):
            copies.append(pltpu.make_async_copy(gate_hbm.at[side, :, cut], wrow.at[slot, 0, side], wsem.at[slot, side]))
            copies.append(pltpu.make_async_copy(up_hbm.at[side, :, cut], wrow.at[slot, 1, side], wsem.at[slot, 2 + side]))
            copies.append(pltpu.make_async_copy(down_hbm.at[side, cut, :], wcol.at[slot, side], wsem.at[slot, 4 + side]))
        return copies

    def load_hidden(u):
        cut = pl.ds(pl.multiple_of(u * sub, sub), sub)
        return pltpu.make_async_copy(hidden_hbm.at[cut, :], hid_v.at[u % 2], hid_sem.at[u % 2])

    loads = [pltpu.make_async_copy(n2_hbm, n2_v, load_sem.at[0]), pltpu.make_async_copy(gf_hbm, gf_v, load_sem.at[1])]
    for copy in loads + load_weights(0):
        copy.start()
    for u in range(2):
        load_hidden(u).start()
    greet([(None, chain.side), (chain.inner, chain.mid), (None, near_core)])
    gain_out[...] = jnp.zeros_like(gain_out)
    for copy in loads:
        copy.wait()

    def stores(u):
        cut = pl.ds(pl.multiple_of(u * sub, sub), sub)
        return (
            pltpu.make_async_copy(gh_v.at[u % 2], gh_hbm.at[cut, :], out_sem.at[0, u % 2]),
            pltpu.make_async_copy(gb_v.at[u % 2], gb_hbm.at[cut, :], out_sem.at[1, u % 2]),
        )

    def finish(u):
        chain.total(u, total_v)
        load_hidden(u).wait()

        @pl.when(u >= 2)
        def _():
            for copy in stores(u - 2):
                copy.wait()

        def body(piece_rows, first):
            e = total_v[piece_rows, :]
            hidden_rows = hid_v[u % 2, piece_rows, :]
            inv = inverse_rms(hidden_rows)
            hat = hidden_rows * inv
            eg = e * gain_ref[...]
            grad = gf_v[pl.ds(pl.multiple_of(u * sub + first, 16), 16), :].astype(F32)
            gh = grad + inv * (eg - hat * jnp.mean(eg * hat, axis=-1, keepdims=True))
            gh_v[u % 2, piece_rows, :] = gh
            gb_v[u % 2, piece_rows, :] = gh.astype(BF16)
            both = e * hat
            gain_out[...] += both[:8] + both[8:]

        by_pieces(sub, body)
        for copy in stores(u):
            copy.start()

        @pl.when(u + 2 < subs)
        def _():
            load_hidden(u + 2).start()

    def serve(k):
        chain.middle(k - 3)
        chain.outward(k - 4)

        @pl.when((k >= 5) & (k < 5 + subs))
        def _():
            finish(k - 5)

    def store_ffn(c):
        return pltpu.make_async_copy(ffn_v, ffn_hbm.at[pl.ds(pl.multiple_of(c * rows, rows), rows), :], ffn_sem)

    def step(i, carry):
        slot, c, h = i % 2, i // hsteps, i % hsteps
        for copy in load_weights(i):
            copy.wait()

        @pl.when(i + 1 < steps)
        def _():
            for copy in load_weights(i + 1):
                copy.start()

        here = pl.ds(pl.multiple_of(c * rows, rows), rows)
        cols = pl.ds(pl.multiple_of(h * hb, hb), hb)
        n, g = n2_v[here, :], gf_v[here, :]
        wide = min(256, hb)
        for q in range(hb // wide):
            part = slice(q * wide, (q + 1) * wide)
            gate = dot_nn(n[:, :half], wrow[slot, 0, 0, :, part]) + dot_nn(n[:, half:], wrow[slot, 0, 1, :, part])
            up = dot_nn(n[:, :half], wrow[slot, 1, 0, :, part]) + dot_nn(n[:, half:], wrow[slot, 1, 1, :, part])
            gi = dot_nt(g[:, :half], wcol[slot, 0, part, :]) + dot_nt(g[:, half:], wcol[slot, 1, part, :])
            sig = jax.nn.sigmoid(gate)
            silu = gate * sig
            at = pl.ds(pl.multiple_of(h * hb + q * wide, wide), wide)
            inner_v[here, at] = (silu * up).astype(BF16)
            gg_v[here, at] = (gi * up * sig * (1.0 + gate * (1.0 - sig))).astype(BF16)
            gu_v[here, at] = (gi * silu).astype(BF16)

        @pl.when(h == 0)
        def _():
            facc[...] = jnp.zeros_like(facc)
            gacc[...] = jnp.zeros_like(gacc)

        inner, gg, gu = inner_v[here, cols], gg_v[here, cols], gu_v[here, cols]
        span = min(512, half)
        for side in range(2):
            for q in range(half // span):
                part = slice(q * span, (q + 1) * span)
                cut = slice(side * half + q * span, side * half + (q + 1) * span)
                facc[:, cut] += dot_nn(inner, wcol[slot, side, :, part])
                gacc[:, cut] += dot_nt(gg, wrow[slot, 0, side, part, :]) + dot_nt(gu, wrow[slot, 1, side, part, :])

        @pl.when(h == hsteps - 1)
        def _():
            for k in range(per):
                part_v[c * per + k] = gacc[k * sub : (k + 1) * sub, :].astype(BF16)
                chain.begin(c * per + k)

            @pl.when(c > 0)
            def _():
                store_ffn(c - 1).wait()

            ffn_v[...] = facc[...].astype(BF16)
            store_ffn(c).start()

        @pl.when(i % 2 == 0)
        def _():
            serve(i // 2)

        return carry

    lax.fori_loop(0, steps, step, 0)

    pl.semaphore_signal(free_sem, inc=1, device_id=near_core, device_id_type=pl.DeviceIdType.MESH)
    outs = (dgate_hbm, dup_hbm, ddown_hbm)

    def landing(w, t):
        return wrow.at[t // 2, w, t % 2] if w < 2 else wcol.at[t // 2, t % 2]

    def landed(w, t, piece):
        return wrow[t // 2, w, t % 2, piece, :] if w < 2 else wcol[t // 2, t % 2, piece, :]

    def staging(w):
        return stage_row if w < 2 else stage_col

    def ship(w, t):
        return remote(staging(w).at[t % 2], landing(w, t), csend.at[w, t], crecv.at[w, t], near_core)

    def keep(w, t):
        cut = pl.ds(pl.multiple_of(t * hb, hb), hb)
        dst = outs[w].at[:, cut] if w < 2 else outs[w].at[cut, :]
        return pltpu.make_async_copy(staging(w).at[t % 2], dst, store_sem.at[w, t])

    def release(kind, w, t):
        if kind == 1:
            ship(w, t).wait_send()
        else:
            keep(w, t).wait()

    def group(kind, w, before):
        def one(t, carry):
            cut = pl.ds(pl.multiple_of(t * hb, hb), hb)
            mine = slice(kind * half, (kind + 1) * half)
            @pl.when(t >= 2)
            def _():
                release(kind, w, t - 2)

            if before is not None:

                @pl.when(t < 2)
                def _():
                    release(before[0], before[1], t + hsteps - 2)

            if kind == 0:
                ship(w, t).wait_recv()
            tall = staging(w).shape[1]
            size = min(256, tall)
            for q in range(tall // size):
                piece = slice(q * size, (q + 1) * size)
                if w == 2:
                    left = inner_v[:, pl.ds(pl.multiple_of(t * hb + q * size, size), size)]
                    value = dot_tn(left, gf_v[:, mine])
                else:
                    value = dot_tn(n2_v[:, kind * half + q * size : kind * half + (q + 1) * size], (gg_v, gu_v)[w][:, cut])
                if kind == 0:
                    value = value + landed(w, t, piece).astype(F32)
                staging(w)[t % 2, piece, :] = value.astype(BF16)
            if kind == 1:
                ship(w, t).start()
            else:
                keep(w, t).start()
            return carry

        lax.fori_loop(0, hsteps, one, 0)

    done = steps // 2
    serve(done)
    pl.semaphore_wait(free_sem, 1)
    group(1, 0, None)
    serve(done + 1)
    group(1, 1, (1, 0))
    group(0, 0, (1, 1))
    serve(done + 2)
    group(1, 2, None)
    group(0, 1, (0, 0))
    serve(done + 3)
    group(0, 2, (1, 2))
    for k in range(done + 4, 5 + subs):
        serve(k)
    for t in range(hsteps - 2, hsteps):
        keep(1, t).wait()
        keep(2, t).wait()
    store_ffn(steps // hsteps - 1).wait()
    for u in range(subs - 2, subs):
        for copy in stores(u):
            copy.wait()
    chain.settle()


def feed_both(n2, gf, gate, up, down, hidden_rows, gain):
    tokens, width = n2.shape
    _, half, hidden = gate.shape
    hb = hidden // 4
    sub, rows = tokens // 8, tokens // 4
    any_space = pl.BlockSpec(memory_space=pl.ANY)
    vmem = pl.BlockSpec(memory_space=pltpu.VMEM)
    dma = pltpu.SemaphoreType.DMA
    moving = pltpu.VMEM((8, sub, width), BF16)
    act = pltpu.VMEM((tokens, hidden), BF16)
    return pl.pallas_call(
        functools.partial(feed_both_kernel, hb, sub, rows),
        in_specs=[any_space] * 6 + [vmem],
        out_specs=[any_space] * 6 + [vmem],
        out_shape=[
            shape((tokens, width), BF16), shape((tokens, width), BF16), shape((tokens, width), F32),
            shape((half, hidden), BF16), shape((half, hidden), BF16), shape((hidden, half), BF16), shape((8, width), F32),
        ],
        scratch_shapes=[
            pltpu.VMEM((tokens, width), BF16), pltpu.VMEM((tokens, width), BF16), act, act, act,
            pltpu.VMEM((rows, width), F32), pltpu.VMEM((rows, width), F32),
            pltpu.VMEM((2, 2, 2, half, hb), BF16), pltpu.VMEM((2, 2, hb, half), BF16),
            moving, moving, moving, pltpu.VMEM((sub, width), F32),
            pltpu.VMEM((2, sub, width), F32), pltpu.VMEM((2, sub, width), F32), pltpu.VMEM((2, sub, width), BF16),
            pltpu.VMEM((rows, width), BF16), pltpu.VMEM((2, half, hb), BF16), pltpu.VMEM((2, hb, half), BF16),
            dma((2,)), dma((2, 6)), dma((3, 8)), dma((3, 8)), dma((2,)), dma((2, 2)), dma(()), dma((3, 4)), dma((3, 4)),
            dma((3, 4)), pltpu.SemaphoreType.REGULAR,
        ],
        compiler_params=pltpu.CompilerParams(vmem_limit_bytes=VMEM_MOST, collective_id=2, has_side_effects=True),
        cost_estimate=cost(18 * tokens * width * hidden, 60 * tokens * width),
        name="feed_forward_both",
    )(n2, gf, gate, up, down, hidden_rows, gain)


def per_device(
    inputs,
    cotangent,
    lengths,
    w_query,
    key_projection_weight,
    value_projection_weight,
    w_output,
    w_gate,
    w_up,
    w_down,
    attn_gain,
    ffn_gain,
    query_gain,
    key_gain,
):
    seqs, span, width = inputs.shape
    hd = query_gain.shape[0]
    nq = w_query.shape[1] // hd
    nk = key_projection_weight.shape[1] // hd
    groups = nq // nk
    dp = lax.axis_size("dp")
    tensor = lax.axis_size("tensor")
    row = lax.axis_index("dp")
    core = lax.axis_index("context")
    rank = lax.axis_index("tensor")
    chunks = 2
    rows = span // chunks
    share = span // tensor
    lengths = lengths.astype(jnp.int32)
    start = (core * span).astype(jnp.int32)
    core1 = core.astype(jnp.int32).reshape(1)
    ids = block_order(dp, row, core)
    order = 2 * dp if (width // (2 * dp)) % 128 == 0 else 1

    positions = start + jnp.arange(span, dtype=jnp.int32)
    freqs = rope_base ** (-(jnp.arange(hd // 2, dtype=F32) * (2.0 / hd)))
    angles = freqs[:, None] * positions.astype(F32)[None, :]
    cosine, sine = jnp.cos(angles), jnp.sin(angles)
    qgain = query_gain.astype(F32).reshape(hd, 1)
    kgain = key_gain.astype(F32).reshape(hd, 1)

    w_qkv = jnp.concatenate([w_query, key_projection_weight, value_projection_weight], axis=1)
    saved = []
    if dp == 4 and tensor == 4 and order == 8:
        gains = jnp.pad(jnp.stack([attn_gain, ffn_gain]), ((0, 14), (0, 0)))
        (xr, n1, gf, qkv, out_w, gate, up, down, hidden_all, n2_all, gains, pre_all, everything_all, att_all, inv_all, tok, stat) = forward(
            lengths, inputs, cotangent, w_qkv, w_output, w_gate, w_up, w_down, gains, cosine, sine, qgain, kgain, hd, nq, nk
        )
        gains = jnp.swapaxes(gains[:, :2], 0, 1).reshape(2, width).astype(F32)
        gain1, gain2 = gains[0:1], gains[1:2]
        stats = jnp.sum(stat, axis=(1, 2))
        for s in range(seqs):
            seq_scal = jnp.stack([lengths[s], core.astype(jnp.int32)])
            saved.append((pre_all[s], everything_all[s], att_all[s], inv_all[s], seq_scal))
        tok = tok.reshape(seqs * span, nq * hd)
    else:
        gains, _ = gather_blocks(jnp.stack([attn_gain, ffn_gain]), 1, dp)
        gains = jnp.concatenate([gains[0], gains[1]], axis=1).astype(F32)
        gain1, gain2 = gains[0:1], gains[1:2]
        qkv, mark = gather_blocks(w_qkv, 0, dp)
        out_w, mark = gather_blocks(tie(w_output, mark), 1, dp)
        gate, mark = gather_blocks(tie(w_gate, mark), 0, dp)
        up, mark = gather_blocks(tie(w_up, mark), 0, dp)
        down, mark = gather_blocks(tie(w_down, mark), 1, dp)

        scal = jnp.concatenate([lengths, start.reshape(1), ids])
        x_in, cot_in = inputs, cotangent
        if order == 1:
            x_in, cot_in = to_relative(x_in, dp, core), to_relative(cot_in, dp, core)
        xr, n1, gf = begin(x_in, cot_in, gain1, scal, order)

        parts, tok = [], []
        for s in range(seqs):
            pre, own, oth = heads(n1, s, qkv, cosine, sine, qgain, kgain, core1, hd, nq, nk)
            seq_scal = jnp.stack([lengths[s], core.astype(jnp.int32)])
            everything, att, inv, mine, theirs = attend(seq_scal, own, over_core(oth), groups)
            branched = branch(mine, over_core(theirs), out_w, core1, chunks)
            saved.append((pre, everything, att, inv, seq_scal))
            tok.append(jnp.swapaxes(branched[0], 0, 1))
            parts.append(branched[1:])
        tok = jnp.concatenate(tok, axis=0)

        stats = jnp.zeros((2,), F32)
        hidden_all, n2_all = [], []
        for s in range(seqs):
            for k in range(chunks):
                terms = sum_terms(parts[s][k], tensor)
                place = jnp.stack([lengths[s], start + k * rows])
                hidden, n2, stat = second_norm(place, xr, s, k, gain2, terms)
                hidden_all.append(hidden)
                n2_all.append(n2)
                stats = stats + stat[:2, 0]
        hidden_all, n2_all = jnp.concatenate(hidden_all), jnp.concatenate(n2_all)

    ffn_squares = jnp.zeros((), F32)
    out_shares = []

    def piece_of(arrays):
        per = arrays[0].shape[0] // share

        def piece(k):
            found = lax.dynamic_slice_in_dim(arrays[0], jnp.minimum(k, per - 1) * share, share, 0)
            for m in range(1, len(arrays)):
                here = lax.dynamic_slice_in_dim(arrays[m], jnp.clip(k - m * per, 0, per - 1) * share, share, 0)
                found = jnp.where(k >= m * per, here, found)
            return found

        return piece

    def share_scalars(s):
        head = jnp.stack([rank.astype(jnp.int32), lengths[s], start + rank.astype(jnp.int32) * share, jnp.int32(tensor)])
        return jnp.concatenate([head, ids])

    def flat(nested):
        return [item for inner_list in nested for item in inner_list]

    def slices(array, count):
        size = array.shape[0] // count
        return [array[i * size : (i + 1) * size] for i in range(count)]

    def reduced(lefts, rights, axis):
        oth = weight_grad(lefts, rights, 1, axis)
        own = weight_grad(lefts, rights, 0, axis, over_core(oth))
        return scatter_blocks(own, axis, dp)

    if dp == 4 and tensor == 4 and order == 8:
        ffn_all, gb_all, gh_all, d_gate, d_up, d_down, gain2_grad = feed_both(
            n2_all, gf.reshape(seqs * span, width), gate, up, down, hidden_all, gain2
        )
        gain2_grad = jnp.sum(gain2_grad, axis=0, keepdims=True)
        ffn, gb, gh = [[[a[(s * chunks + k) * rows : (s * chunks + k + 1) * rows] for k in range(chunks)] for s in range(seqs)] for a in (ffn_all, gb_all, gh_all)]
        grad_w_gate = scatter_blocks(d_gate, 0, dp)
        grad_w_up = scatter_blocks(d_up, 0, dp)
        grad_w_down = scatter_blocks(d_down, 1, dp)
    else:
        inner, gg, gu, ffn, gn = [[[None] * chunks for _ in range(seqs)] for _ in range(5)]
        for s in range(seqs):
            for k in range(chunks):
                inner[s][k], gg[s][k], gu[s][k], ffn[s][k], gn[s][k] = feed(
                    n2_all, s * chunks + k, rows, gf, s, k, gate, up, down
                )
        gain2_grad = jnp.zeros((1, width), F32)
        gb, gh = [[[None] * chunks for _ in range(seqs)] for _ in range(2)]
        for s in range(seqs):
            for k in range(chunks):
                terms = sum_terms(gn[s][k], tensor)
                gb[s][k], gh[s][k], gain_part = second_back(hidden_all, s * chunks + k, gf, s, k, gain2, terms)
                gain2_grad = gain2_grad + gain_part
        gf_list = slices(gf.reshape(seqs * span, width), seqs * chunks)
        n2_list = slices(n2_all, seqs * chunks)
        grad_w_down = reduced(flat(inner), gf_list, 1)
        grad_w_gate = reduced(n2_list, flat(gg), 0)
        grad_w_up = reduced(n2_list, flat(gu), 0)
    for s in range(seqs):
        got = ring_scatter(piece_of(ffn[s]), tensor, rank)
        halves = [hidden_all[(s * chunks + k) * rows : (s * chunks + k + 1) * rows] for k in range(chunks)]
        out, stat = output_share(share_scalars(s), got, ffn[s], halves, order)
        out_shares.append(out)
        ffn_squares = ffn_squares + stat[0, 0]

    gain1_grad = jnp.zeros((1, width), F32)
    head_gain = jnp.zeros((2 * hd,), F32)
    dpres, in_shares = [], []
    for s in range(seqs):
        pre, everything, att, inv, seq_scal = saved[s]
        da_own, da_oth = branch_back(gb[s], out_w, core1)
        d_own, d_oth = attend_back(seq_scal, everything, att, inv, da_own, over_core(da_oth), groups)
        dpre, first, gain_part, hg = heads_back(
            d_own, over_core(d_oth), pre, cosine, sine, qgain, kgain, xr, s, qkv, core1, hd, nq, nk
        )
        gain1_grad = gain1_grad + gain_part
        head_gain = head_gain + hg[:, 0]
        dpres.append(dpre)
        got = ring_scatter(piece_of([first]), tensor, rank)
        in_shares.append(input_share(share_scalars(s), got, first, gh[s], xr, s, gain1, order))

    att_list = [tok[i * rows : (i + 1) * rows] for i in range(seqs * chunks)]
    grad_w_output = reduced(att_list, flat(gb), 1)
    grad_qkv = reduced([n1[s] for s in range(seqs)], dpres, 0)
    nqc, nkc = nq * hd, nk * hd
    grad_w_query = grad_qkv[:, :nqc]
    grad_w_key = grad_qkv[:, nqc : nqc + nkc]
    grad_w_value = grad_qkv[:, nqc + nkc :]

    gain2_grad = gain2_grad / tensor
    counts = jnp.sum(jnp.clip(lengths - start, 0, span)).astype(F32) / tensor
    small = jnp.concatenate([head_gain, stats / tensor, ffn_squares.reshape(1), counts.reshape(1)])
    small = jnp.pad(small, (0, (-small.shape[0]) % 128)).reshape(1, -1)
    lines = jnp.concatenate([gain1_grad, gain2_grad], axis=0)
    if dp == 4 and tensor == 4:
        half = width // 2
        quarter = half // 4

        def join(part):
            return jnp.concatenate([part.reshape(1, -1), small], axis=1)

        got = over_core(join(lines[:, half:]))
        lines = lines[:, :half] + got[:, : 2 * half].reshape(2, half)
        small = small + got[:, 2 * half :]
        lines = lines.reshape(2, 4, quarter)
        got = over_x(join(lines[:, 1::2]))
        lines = lines[:, 0::2] + got[:, : 4 * quarter].reshape(2, 2, quarter)
        small = small + got[:, 4 * quarter :]
        got = over_y(join(lines[:, 1]))
        lines = lines[:, 0] + got[:, : 2 * quarter].reshape(2, quarter)
        small = small + got[:, 2 * quarter :]
        for step in (1, 2):
            got = lax.ppermute(join(lines), "tensor", [(i, i ^ step) for i in range(4)])
            lines = lines + got[:, : 2 * quarter].reshape(2, quarter)
            small = small + got[:, 2 * quarter :]
    else:
        piece = width // (2 * dp)
        lines = to_absolute(lines, dp, core) if dp != 4 else lines.reshape(2, 2 * dp, piece)[:, jnp.argsort(ids)].reshape(2, width)
        lines, small = lax.psum((lines, small), ("dp", "context", "tensor"))
        lines = lax.dynamic_slice_in_dim(lines, lax.axis_index(("dp", "context")) * piece, piece, 1)
    small = small[0]
    rms_values = jnp.sqrt(small[2 * hd : 2 * hd + 3] / (small[2 * hd + 3] * width))

    output = jnp.stack(out_shares)
    grad_inputs = jnp.stack(in_shares)
    if order == 1:
        output, grad_inputs = to_absolute(output, dp, core), to_absolute(grad_inputs, dp, core)
    return (
        output,
        grad_inputs,
        grad_w_query,
        grad_w_key,
        grad_w_value,
        grad_w_output,
        grad_w_gate,
        grad_w_up,
        grad_w_down,
        lines[0],
        lines[1],
        small[:hd],
        small[hd : 2 * hd],
        rms_values,
    )


def solution(mesh):
    both = ("dp", "context")
    rows = P(both, "tensor")
    cols = P("tensor", both)
    shares = P("dp", ("context", "tensor"), None)
    acts = P("dp", "context", None)
    return jax.shard_map(
        per_device,
        mesh=mesh,
        in_specs=(acts, acts, P("dp"), rows, rows, rows, cols, rows, rows, cols, P(both), P(both), P(), P()),
        out_specs=(shares, shares, rows, rows, rows, cols, rows, rows, cols, P(both), P(both), P(), P(), P()),
        check_vma=False,
    )
```

```python
import functools
import math

import jax
import jax.numpy as jnp
from jax import lax
from jax.experimental import pallas as pl
from jax.experimental.pallas import tpu as pltpu
from jax.sharding import PartitionSpec as P

F32 = jnp.float32
BF16 = jnp.bfloat16
epsilon = 1e-05
rope_base = 1000000.0
log2e = 1.4426950408889634
VMEM_BYTES = 60 * 1024 * 1024
VMEM_MOST = 63 * 1024 * 1024
PARAMS = pltpu.CompilerParams(vmem_limit_bytes=VMEM_BYTES)
SMEM = pl.BlockSpec(memory_space=pltpu.SMEM)
SWAP = ((0, 1), (1, 0))


def shape(dims, dtype):
    return jax.ShapeDtypeStruct(tuple(dims), dtype)


def cost(flops, size, exps=0):
    return pl.CostEstimate(flops=int(flops), bytes_accessed=int(size), transcendentals=int(exps))


def dot_nn(a, b):
    return lax.dot_general(a, b, (((1,), (0,)), ((), ())), preferred_element_type=F32)


def dot_nt(a, b):
    return lax.dot_general(a, b, (((1,), (1,)), ((), ())), preferred_element_type=F32)


def dot_tn(a, b):
    return lax.dot_general(a, b, (((0,), (0,)), ((), ())), preferred_element_type=F32)


def inverse_rms(values):
    return lax.rsqrt(jnp.mean(values * values, axis=-1, keepdims=True) + epsilon)


def block_order(dp, core):
    return jnp.stack([jnp.int32(k) * 2 + (core ^ o) for o in range(2) for k in range(dp)]).astype(jnp.int32)


def to_relative(values, dp, core):
    lead = values.shape[:-1]
    parts = values.reshape(lead + (dp, 2, -1))
    parts = jnp.where(core == 0, parts, parts[..., ::-1, :])
    return jnp.swapaxes(parts, -3, -2).reshape(values.shape)


def to_absolute(values, dp, core):
    lead = values.shape[:-1]
    parts = jnp.swapaxes(values.reshape(lead + (2, dp, -1)), -3, -2)
    return jnp.where(core == 0, parts, parts[..., ::-1, :]).reshape(values.shape)


def over_core(value):
    return lax.ppermute(value, "context", SWAP)


def gather_blocks(weight, axis):
    own = lax.all_gather(weight, "dp", axis=axis, tiled=True)
    return jnp.stack([own, over_core(own)])


def scatter_blocks(total, axis):
    return lax.psum_scatter(total, "dp", scatter_dimension=axis, tiled=True).astype(F32)


def ring_scatter(piece, tensor, rank):
    ring = [(i, (i + 1) % tensor) for i in range(tensor)]
    moving = piece((rank + tensor - 1) % tensor)
    for step in range(1, tensor):
        moving = lax.ppermute(moving, "tensor", ring)
        if step < tensor - 1:
            moving = (moving.astype(F32) + piece((rank + tensor - 1 - step) % tensor).astype(F32)).astype(BF16)
    return moving


def begin_kernel(order, x_ref, cot_ref, gain_ref, scal_ref, xr_ref, n1_ref, gf_ref):
    seq, tile = pl.program_id(0), pl.program_id(1)
    rows, width = x_ref.shape[1:]
    seqs = pl.num_programs(0)
    place = scal_ref[seqs] + tile * rows + lax.broadcasted_iota(jnp.int32, (rows, 1), 0)
    valid = (place < scal_ref[seq]).astype(F32)
    x = x_ref[0].astype(F32)
    inv = inverse_rms(x)
    piece = width // order
    for k in range(order):
        src = pl.ds(pl.multiple_of(scal_ref[seqs + 1 + k] * piece, piece), piece) if order > 1 else slice(0, width)
        dst = slice(k * piece, (k + 1) * piece)
        part = x_ref[0, :, src]
        xr_ref[0, :, dst] = part
        n1_ref[0, :, dst] = (part.astype(F32) * inv * gain_ref[:, dst]).astype(BF16)
        gf_ref[0, :, dst] = (cot_ref[0, :, src].astype(F32) * valid).astype(BF16)


def begin(x, cot, gain, scalars, order):
    seqs, span, width = x.shape
    rows = min(256, span)
    spec = pl.BlockSpec((1, rows, width), lambda s, i: (s, i, 0))
    return pl.pallas_call(
        functools.partial(begin_kernel, order),
        grid=(seqs, span // rows),
        in_specs=[spec, spec, pl.BlockSpec((1, width), lambda s, i: (0, 0)), SMEM],
        out_specs=[spec] * 3,
        out_shape=[shape(x.shape, BF16)] * 3,
        compiler_params=PARAMS,
        cost_estimate=cost(8 * x.size, 10 * x.size),
        name="first_norm",
    )(x, cot, gain, scalars)


def heads_kernel(hd, nq, nk, n1_ref, w_ref, cos_ref, sin_ref, qg_ref, kg_ref, core_ref, pre_ref, own_ref, oth_ref):
    half = w_ref.shape[1]
    x = n1_ref[0]
    flat = dot_nn(x[:, :half], w_ref[0]) + dot_nn(x[:, half:], w_ref[1])
    turned = flat.T
    span = turned.shape[1]
    normed = turned[: (nq + nk) * hd]
    pre_ref[...] = normed
    core = core_ref[0]
    cosine, sine = cos_ref[...], sin_ref[...]
    done = []
    for h in range(nq + nk):
        v = normed[h * hd : (h + 1) * hd]
        inv = lax.rsqrt(jnp.mean(v * v, axis=0, keepdims=True) + epsilon)
        v = v * inv * (qg_ref[...] if h < nq else kg_ref[...])
        a, b = v[: hd // 2], v[hd // 2 :]
        done.append(jnp.concatenate([a * cosine - b * sine, b * cosine + a * sine], axis=0))
    for h in range(nk):
        lo = (nq + nk + h) * hd
        done.append(turned[lo : lo + hd])
    parts = [[], []]
    for start, count in ((0, nq), (nq, nk), (nq + nk, nk)):
        for side in range(2):
            parts[side] += done[start + side * count // 2 : start + (side + 1) * count // 2]
    low = jnp.concatenate(parts[0], axis=0)
    high = jnp.concatenate(parts[1], axis=0)
    first = core == 0
    own_ref[...] = jnp.where(first, low, high).astype(BF16)
    oth_ref[...] = jnp.where(first, high, low).astype(BF16)


def heads(n1, seq, weight, cosine, sine, qgain, kgain, core, hd, nq, nk):
    span, width = n1.shape[1:]
    sides = (nq + 2 * nk) * hd // 2
    full = pl.BlockSpec(memory_space=pltpu.VMEM)
    whole = lambda a: pl.BlockSpec(a.shape, lambda i: (0,) * a.ndim)
    outs = [shape(((nq + nk) * hd, span), F32), shape((sides, span), BF16), shape((sides, span), BF16)]
    return pl.pallas_call(
        functools.partial(heads_kernel, hd, nq, nk),
        grid=(1,),
        in_specs=[pl.BlockSpec((1, span, width), lambda i: (seq, 0, 0))]
        + [whole(a) for a in (weight, cosine, sine, qgain, kgain)]
        + [SMEM],
        out_specs=[whole(o) for o in outs],
        out_shape=outs,
        compiler_params=PARAMS,
        cost_estimate=cost(2 * span * width * weight.shape[2], 2 * span * width + 2 * weight.size),
        name="query_key_value",
    )(n1, weight, cosine, sine, qgain, kgain, core)


def join_positions(core, own, oth):
    first = core == 0
    return jnp.where(first, own, oth), jnp.where(first, oth, own)


def attend_kernel(block, groups, scal_ref, own_ref, got_ref, all_ref, att_ref, inv_ref, ao_ref, ax_ref):
    span = own_ref.shape[1]
    hd = own_ref.shape[0] // (groups + 2)
    length, core = scal_ref[0], scal_ref[1]
    low, high = join_positions(core, own_ref[...], got_ref[...])
    all_ref[:, :span] = low
    all_ref[:, span:] = high
    scale = log2e / math.sqrt(hd)
    krow = lax.broadcasted_iota(jnp.int32, (block, groups * block), 0)
    qcol = lax.broadcasted_iota(jnp.int32, (block, groups * block), 1) % block
    base = groups * hd
    for i in range(2 * span // block):
        cut = slice(i * block, (i + 1) * block)
        q = jnp.concatenate([all_ref[g * hd : (g + 1) * hd, cut] for g in range(groups)], axis=1)
        acc = jnp.zeros((hd, groups * block), F32)
        total = jnp.zeros((1, groups * block), F32)
        for j in range(i + 1):
            kcut = slice(j * block, (j + 1) * block)
            s = dot_tn(all_ref[base : base + hd, kcut], q) * scale
            ok = (krow + j * block) < length
            if j == i:
                ok = ok & (krow <= qcol)
            e = jnp.where(ok, jnp.exp2(s), 0.0)
            total = total + jnp.sum(e, axis=0, keepdims=True)
            acc = acc + dot_nn(all_ref[base + hd : base + 2 * hd, kcut], e.astype(BF16))
        inv = 1.0 / total
        att = (acc * inv).astype(BF16)
        for g in range(groups):
            att_ref[g * hd : (g + 1) * hd, cut] = att[:, g * block : (g + 1) * block]
            inv_ref[g : g + 1, cut] = inv[:, g * block : (g + 1) * block]
    mine, theirs = join_positions(core, att_ref[:, :span], att_ref[:, span:])
    ao_ref[...] = mine
    ax_ref[...] = theirs


def attend(scalars, own, got, groups):
    rows, span = own.shape
    hd = rows // (groups + 2)
    block = min(256, span)
    full = pl.BlockSpec(memory_space=pltpu.VMEM)
    return pl.pallas_call(
        functools.partial(attend_kernel, block, groups),
        in_specs=[SMEM, full, full],
        out_specs=[full] * 5,
        out_shape=[
            shape((rows, 2 * span), BF16),
            shape((groups * hd, 2 * span), BF16),
            shape((groups, 2 * span), F32),
            shape((groups * hd, span), BF16),
            shape((groups * hd, span), BF16),
        ],
        compiler_params=PARAMS,
        cost_estimate=cost(60 * groups * hd * span * span, 12 * rows * span, 4 * groups * span * span),
        name="attend_forward",
    )(scalars, own, got)


def branch_kernel(own_ref, got_ref, w_ref, core_ref, att_ref, *outs):
    half = w_ref.shape[2]
    low, high = join_positions(core_ref[0], own_ref[...], got_ref[...])
    att = jnp.concatenate([low, high], axis=0)
    att_ref[...] = att
    rows = outs[0].shape[0]
    for k, out in enumerate(outs):
        part = att[:, k * rows : (k + 1) * rows]
        out[:, :half] = dot_tn(part, w_ref[0]).astype(BF16)
        out[:, half:] = dot_tn(part, w_ref[1]).astype(BF16)


def branch(own, got, weight, core, chunks):
    rows, span = own.shape
    width = 2 * weight.shape[2]
    full = pl.BlockSpec(memory_space=pltpu.VMEM)
    return pl.pallas_call(
        branch_kernel,
        in_specs=[full] * 3 + [SMEM],
        out_specs=[full] * (1 + chunks),
        out_shape=[shape((2 * rows, span), BF16)] + [shape((span // chunks, width), BF16)] * chunks,
        compiler_params=PARAMS,
        cost_estimate=cost(4 * rows * span * width, 4 * rows * width + 2 * span * width),
        name="attention_branch",
    )(own, got, weight, core)


def second_norm_kernel(terms, scal_ref, x_ref, gain_ref, *refs):
    term_refs, (hidden_ref, n2_ref, stat_ref) = refs[:terms], refs[terms:]
    rows = hidden_ref.shape[0]
    branch_sum = term_refs[0][...].astype(F32)
    for ref in term_refs[1:]:
        branch_sum = branch_sum + ref[...].astype(F32)
    resid = x_ref[0].astype(F32)
    hidden = resid + branch_sum
    hidden_ref[...] = hidden
    n2_ref[...] = (hidden * inverse_rms(hidden) * gain_ref[...]).astype(BF16)
    place = scal_ref[1] + lax.broadcasted_iota(jnp.int32, (rows, 1), 0)
    valid = (place < scal_ref[0]).astype(F32)
    first = jnp.sum(valid * resid * resid, keepdims=True)
    second = jnp.sum(valid * branch_sum * branch_sum, keepdims=True)
    line = lax.broadcasted_iota(jnp.int32, (8, 128), 0)
    stat_ref[...] = jnp.where(line == 0, first, second)


def second_norm(scalars, xr, seq, part, gain, terms):
    rows, width = terms[0].shape
    flat = pl.BlockSpec((rows, width), lambda i: (0, 0))
    return pl.pallas_call(
        functools.partial(second_norm_kernel, len(terms)),
        grid=(1,),
        in_specs=[SMEM, pl.BlockSpec((1, rows, width), lambda i: (seq, part, 0)), pl.BlockSpec((1, width), lambda i: (0, 0))]
        + [flat] * len(terms),
        out_specs=[flat, flat, pl.BlockSpec((8, 128), lambda i: (0, 0))],
        out_shape=[shape((rows, width), F32), shape((rows, width), BF16), shape((8, 128), F32)],
        compiler_params=PARAMS,
        cost_estimate=cost(20 * rows * width, (8 + 2 * len(terms)) * rows * width),
        name="second_norm",
    )(scalars, xr, gain, *terms)


def feed_kernel(n_ref, g_ref, wgo, wgx, wuo, wux, wdo, wdx, inner_ref, gg_ref, gu_ref, ffn_ref, gn_ref, facc, gacc):
    step = pl.program_id(0)
    half = wgo.shape[0]
    no, nx = n_ref[:, :half], n_ref[:, half:]
    gate = dot_nn(no, wgo[...]) + dot_nn(nx, wgx[...])
    up = dot_nn(no, wuo[...]) + dot_nn(nx, wux[...])
    gi = dot_nt(g_ref[0, :, :half], wdo[...]) + dot_nt(g_ref[0, :, half:], wdx[...])
    sig = jax.nn.sigmoid(gate)
    silu = gate * sig
    inner = (silu * up).astype(BF16)
    gg = (gi * up * sig * (1.0 + gate * (1.0 - sig))).astype(BF16)
    gu = (gi * silu).astype(BF16)
    inner_ref[...] = inner
    gg_ref[...] = gg
    gu_ref[...] = gu

    @pl.when(step == 0)
    def _():
        facc[...] = jnp.zeros_like(facc)
        gacc[...] = jnp.zeros_like(gacc)

    facc[:, :half] += dot_nn(inner, wdo[...])
    facc[:, half:] += dot_nn(inner, wdx[...])
    gacc[:, :half] += dot_nt(gg, wgo[...]) + dot_nt(gu, wuo[...])
    gacc[:, half:] += dot_nt(gg, wgx[...]) + dot_nt(gu, wux[...])

    @pl.when(step == pl.num_programs(0) - 1)
    def _():
        ffn_ref[...] = facc[...].astype(BF16)
        gn_ref[...] = gacc[...].astype(BF16)


def feed(n2, chunk, rows, gf, seq, part, gate, up, down):
    width = n2.shape[1]
    _, half, hidden = gate.shape
    hb = min(512, hidden)
    row = [pl.BlockSpec((None, half, hb), lambda h, side=side: (side, 0, h)) for side in range(2)]
    col = [pl.BlockSpec((None, hb, half), lambda h, side=side: (side, h, 0)) for side in range(2)]
    whole = pl.BlockSpec((rows, width), lambda h: (0, 0))
    tile = pl.BlockSpec((rows, hb), lambda h: (0, h))
    return pl.pallas_call(
        feed_kernel,
        grid=(hidden // hb,),
        in_specs=[pl.BlockSpec((rows, width), lambda h: (chunk, 0)), pl.BlockSpec((1, rows, width), lambda h: (seq, part, 0))] + row + row + col,
        out_specs=[tile, tile, tile, whole, whole],
        out_shape=[shape((rows, hidden), BF16)] * 3 + [shape((rows, width), BF16)] * 2,
        scratch_shapes=[pltpu.VMEM((rows, width), F32), pltpu.VMEM((rows, width), F32)],
        compiler_params=PARAMS,
        cost_estimate=cost(12 * rows * width * hidden, 12 * half * hidden + 14 * rows * width, rows * hidden),
        name="feed_forward",
    )(n2, gf, gate, gate, up, up, down, down)


def second_back_kernel(terms, hidden_ref, gf_ref, gain_ref, *refs):
    term_refs, (gb_ref, gh_ref, gain_out) = refs[:terms], refs[terms:]
    e = term_refs[0][...].astype(F32)
    for ref in term_refs[1:]:
        e = e + ref[...].astype(F32)
    hidden = hidden_ref[...]
    inv = inverse_rms(hidden)
    hat = hidden * inv
    eg = e * gain_ref[...]
    gh = gf_ref[0].astype(F32) + inv * (eg - hat * jnp.mean(eg * hat, axis=-1, keepdims=True))
    gh_ref[...] = gh
    gb_ref[...] = gh.astype(BF16)
    gain_out[...] = jnp.sum(e * hat, axis=0, keepdims=True)


def second_back(hidden, chunk, gf, seq, part, gain, terms):
    rows, width = terms[0].shape
    flat = pl.BlockSpec((rows, width), lambda i: (0, 0))
    line = pl.BlockSpec((1, width), lambda i: (0, 0))
    return pl.pallas_call(
        functools.partial(second_back_kernel, len(terms)),
        grid=(1,),
        in_specs=[pl.BlockSpec((rows, width), lambda i: (chunk, 0)), pl.BlockSpec((1, rows, width), lambda i: (seq, part, 0)), line]
        + [flat] * len(terms),
        out_specs=[flat, flat, line],
        out_shape=[shape((rows, width), BF16), shape((rows, width), F32), shape((1, width), F32)],
        compiler_params=PARAMS,
        cost_estimate=cost(20 * rows * width, (12 + 2 * len(terms)) * rows * width),
        name="second_norm_back",
    )(hidden, gf, gain, *terms)


def branch_back_kernel(chunks, *refs):
    gb_refs, (w_ref, core_ref, own_ref, oth_ref) = refs[:chunks], refs[chunks:]
    half = w_ref.shape[2]
    rows = gb_refs[0].shape[0]
    heads_half = own_ref.shape[0]
    first = core_ref[0] == 0
    for k, ref in enumerate(gb_refs):
        da = dot_nt(w_ref[0], ref[:, :half]) + dot_nt(w_ref[1], ref[:, half:])
        da = da.astype(BF16)
        low, high = da[:heads_half], da[heads_half:]
        cut = slice(k * rows, (k + 1) * rows)
        own_ref[:, cut] = jnp.where(first, low, high)
        oth_ref[:, cut] = jnp.where(first, high, low)


def branch_back(gbs, weight, core):
    chunks = len(gbs)
    rows, width = gbs[0].shape
    dim = weight.shape[1]
    full = pl.BlockSpec(memory_space=pltpu.VMEM)
    return pl.pallas_call(
        functools.partial(branch_back_kernel, chunks),
        in_specs=[full] * (chunks + 1) + [SMEM],
        out_specs=[full] * 2,
        out_shape=[shape((dim // 2, chunks * rows), BF16)] * 2,
        compiler_params=PARAMS,
        cost_estimate=cost(2 * dim * chunks * rows * width, 2 * dim * width + 2 * chunks * rows * width),
        name="attention_branch_back",
    )(*gbs, weight, core)


def attend_back_kernel(block, groups, scal_ref, all_ref, att_ref, inv_ref, own_ref, got_ref, out_own, out_oth, da_all, grads):
    span = own_ref.shape[1]
    hd = all_ref.shape[0] // (groups + 2)
    length, core = scal_ref[0], scal_ref[1]
    low, high = join_positions(core, own_ref[...], got_ref[...])
    da_all[:, :span] = low
    da_all[:, span:] = high
    scale = log2e / math.sqrt(hd)
    back = 1.0 / math.sqrt(hd)
    krow = lax.broadcasted_iota(jnp.int32, (block, groups * block), 0)
    qcol = lax.broadcasted_iota(jnp.int32, (block, groups * block), 1) % block
    base = groups * hd
    grads[base:, :] = jnp.zeros((2 * hd, 2 * span), F32)
    for i in range(2 * span // block):
        cut = slice(i * block, (i + 1) * block)

        def rows(ref):
            return jnp.concatenate([ref[g * hd : (g + 1) * hd, cut] for g in range(groups)], axis=1)

        q = rows(all_ref)
        da = rows(da_all)
        inv = jnp.concatenate([inv_ref[g : g + 1, cut] for g in range(groups)], axis=1)
        delta = jnp.sum(rows(att_ref).astype(F32) * da.astype(F32), axis=0, keepdims=True)
        dq = jnp.zeros((hd, groups * block), F32)
        for j in range(i + 1):
            kcut = slice(j * block, (j + 1) * block)
            key = all_ref[base : base + hd, kcut]
            s = dot_tn(key, q) * scale
            ok = (krow + j * block) < length
            if j == i:
                ok = ok & (krow <= qcol)
            p = jnp.where(ok, jnp.exp2(s) * inv, 0.0)
            dp = dot_tn(all_ref[base + hd : base + 2 * hd, kcut], da)
            ds = (p * (dp - delta)).astype(BF16)
            dq = dq + dot_nn(key, ds)
            grads[base : base + hd, kcut] += dot_nt(q, ds) * back
            grads[base + hd : base + 2 * hd, kcut] += dot_nt(da, p.astype(BF16))
        dq = dq * back
        for g in range(groups):
            grads[g * hd : (g + 1) * hd, cut] = dq[:, g * block : (g + 1) * block]
    mine, theirs = join_positions(core, grads[:, :span], grads[:, span:])
    out_own[...] = mine.astype(BF16)
    out_oth[...] = theirs.astype(BF16)


def attend_back(scalars, everything, att, inv, own, got, groups):
    rows, slots = everything.shape
    span = slots // 2
    block = min(256, span)
    full = pl.BlockSpec(memory_space=pltpu.VMEM)
    return pl.pallas_call(
        functools.partial(attend_back_kernel, block, groups),
        in_specs=[SMEM] + [full] * 5,
        out_specs=[full] * 2,
        out_shape=[shape((rows, span), BF16)] * 2,
        scratch_shapes=[pltpu.VMEM(att.shape, BF16), pltpu.VMEM((rows, slots), F32)],
        compiler_params=PARAMS,
        cost_estimate=cost(30 * att.shape[0] * slots * slots, 12 * rows * slots, groups * slots * slots),
        name="attend_backward",
    )(scalars, everything, att, inv, own, got)


def heads_back_kernel(hd, nq, nk, own_ref, got_ref, pre_ref, cos_ref, sin_ref, qg_ref, kg_ref, x_ref, w_ref, core_ref, dpre_ref, first_ref, gain_ref, hgain_ref):
    half = w_ref.shape[1]
    low, high = join_positions(core_ref[0], own_ref[...].astype(F32), got_ref[...].astype(F32))
    sides = (nq // 2, nk // 2, nk // 2)
    grads = [[], [], []]
    for side in (low, high):
        at = 0
        for kind, count in enumerate(sides):
            for h in range(count):
                grads[kind].append(side[at : at + hd])
                at += hd
    cosine, sine = cos_ref[...], sin_ref[...]
    done = []
    sums = [0.0, 0.0]
    for h in range(nq + nk):
        kind = 0 if h < nq else 1
        g = grads[kind][h - kind * nq]
        a, b = g[: hd // 2], g[hd // 2 :]
        g = jnp.concatenate([a * cosine + b * sine, b * cosine - a * sine], axis=0)
        v = pre_ref[h * hd : (h + 1) * hd, :]
        inv = lax.rsqrt(jnp.mean(v * v, axis=0, keepdims=True) + epsilon)
        hat = v * inv
        sums[kind] = sums[kind] + jnp.sum(g * hat, axis=1, keepdims=True)
        gg = g * (qg_ref[...] if kind == 0 else kg_ref[...])
        done.append(inv * (gg - hat * jnp.mean(gg * hat, axis=0, keepdims=True)))
    done += grads[2]
    hgain_ref[:hd, :] = jnp.broadcast_to(sums[0], (hd, 128))
    hgain_ref[hd:, :] = jnp.broadcast_to(sums[1], (hd, 128))
    dpre = jnp.concatenate(done, axis=0).T.astype(BF16)
    dpre_ref[...] = dpre
    x = x_ref[0].astype(F32)
    hat = x * inverse_rms(x)
    for k in range(2):
        cut = slice(k * half, (k + 1) * half)
        part = dot_nt(dpre, w_ref[k])
        first_ref[:, cut] = part.astype(BF16)
        gain_ref[:, cut] = jnp.sum(part * hat[:, cut], axis=0, keepdims=True)


def heads_back(own, got, pre, cosine, sine, qgain, kgain, xr, seq, weight, core, hd, nq, nk):
    span = own.shape[1]
    _, half, cols = weight.shape
    width = 2 * half
    whole = lambda a: pl.BlockSpec(a.shape, lambda i: (0,) * len(a.shape))
    outs = [shape((span, cols), BF16), shape((span, width), BF16), shape((1, width), F32), shape((2 * hd, 128), F32)]
    return pl.pallas_call(
        functools.partial(heads_back_kernel, hd, nq, nk),
        grid=(1,),
        in_specs=[whole(a) for a in (own, got, pre, cosine, sine, qgain, kgain)]
        + [pl.BlockSpec((1, span, width), lambda i: (seq, 0, 0)), whole(weight), SMEM],
        out_specs=[whole(o) for o in outs],
        out_shape=outs,
        compiler_params=PARAMS,
        cost_estimate=cost(2 * span * width * cols, 4 * span * width + 4 * half * cols),
        name="query_key_value_back",
    )(own, got, pre, cosine, sine, qgain, kgain, xr, weight, core)


def place_blocks(order, ids, first_id, value, out_ref):
    piece = value.shape[-1] // order
    for k in range(order):
        if order == 1:
            out_ref[...] = value
        else:
            dst = pl.ds(pl.multiple_of(ids[first_id + k] * piece, piece), piece)
            out_ref[:, dst] = value[:, k * piece : (k + 1) * piece]


def output_kernel(order, scal_ref, got_ref, f0_ref, f1_ref, h0_ref, h1_ref, out_ref, stat_ref):
    low = scal_ref[0] * 2 < scal_ref[3]
    rows = out_ref.shape[0]
    ffn = got_ref[...].astype(F32) + jnp.where(low, f0_ref[...], f1_ref[...]).astype(F32)
    hidden = jnp.where(low, h0_ref[...], h1_ref[...])
    place = scal_ref[2] + lax.broadcasted_iota(jnp.int32, (rows, 1), 0)
    valid = (place < scal_ref[1]).astype(F32)
    stat_ref[...] = jnp.broadcast_to(jnp.sum(valid * ffn * ffn, keepdims=True), (8, 128))
    place_blocks(order, scal_ref, 4, (hidden + ffn).astype(BF16), out_ref)


def share_specs(rows, width, per):
    return [
        pl.BlockSpec((rows, width), lambda i, s: (jnp.minimum(s[0], per - 1), 0)),
        pl.BlockSpec((rows, width), lambda i, s: (jnp.maximum(s[0] - per, 0), 0)),
    ]


def output_share(scalars, got, ffns, hiddens, order):
    rows, width = got.shape
    pair = share_specs(rows, width, ffns[0].shape[0] // rows)
    flat = pl.BlockSpec((rows, width), lambda i, s: (0, 0))
    return pl.pallas_call(
        functools.partial(output_kernel, order),
        grid_spec=pltpu.PrefetchScalarGridSpec(
            num_scalar_prefetch=1,
            grid=(1,),
            in_specs=[flat] + pair + pair,
            out_specs=[flat, pl.BlockSpec((8, 128), lambda i, s: (0, 0))],
        ),
        out_shape=[shape((rows, width), BF16), shape((8, 128), F32)],
        compiler_params=PARAMS,
        cost_estimate=cost(6 * rows * width, 16 * rows * width),
        name="output_share",
    )(scalars, got, *ffns, *hiddens)


def input_kernel(order, scal_ref, got_ref, part_ref, g0_ref, g1_ref, x_ref, gain_ref, out_ref):
    low = scal_ref[0] * 2 < scal_ref[3]
    e = got_ref[...].astype(F32) + part_ref[...].astype(F32)
    gh = jnp.where(low, g0_ref[...], g1_ref[...])
    x = x_ref[0].astype(F32)
    inv = inverse_rms(x)
    hat = x * inv
    eg = e * gain_ref[...]
    value = gh + inv * (eg - hat * jnp.mean(eg * hat, axis=-1, keepdims=True))
    place_blocks(order, scal_ref, 4, value, out_ref)


def input_share(scalars, got, part, ghs, xr, seq, gain, order):
    rows, width = got.shape
    pair = share_specs(rows, width, ghs[0].shape[0] // rows)
    flat = pl.BlockSpec((rows, width), lambda i, s: (0, 0))
    return pl.pallas_call(
        functools.partial(input_kernel, order),
        grid_spec=pltpu.PrefetchScalarGridSpec(
            num_scalar_prefetch=1,
            grid=(1,),
            in_specs=[flat, pl.BlockSpec((rows, width), lambda i, s: (s[0], 0))]
            + pair
            + [pl.BlockSpec((1, rows, width), lambda i, s: (seq, s[0], 0)), pl.BlockSpec((1, width), lambda i, s: (0, 0))],
            out_specs=flat,
        ),
        out_shape=shape((rows, width), F32),
        compiler_params=PARAMS,
        cost_estimate=cost(12 * rows * width, 20 * rows * width),
        name="input_share",
    )(scalars, got, part, *ghs, xr, gain)


def weight_grad_kernel(count, extra, *refs):
    a_refs, b_refs, out = refs[:count], refs[count : 2 * count], refs[-1]
    total = dot_tn(a_refs[0][...], b_refs[0][...])
    for a, b in zip(a_refs[1:], b_refs[1:]):
        total = total + dot_tn(a[...], b[...])
    if extra:
        total = total + refs[2 * count][...].astype(F32)
    out[...] = total.astype(BF16)


def weight_grad(lefts, rights, side, axis, add=None):
    count = len(lefts)
    rows_all, cols_all = lefts[0].shape[1], rights[0].shape[1]
    dims = [rows_all, cols_all]
    dims[axis] //= 2
    rows, cols = min(512, dims[0]), min(2048, dims[1])
    row_at = side * (dims[0] // rows) if axis == 0 else 0
    col_at = side * (dims[1] // cols) if axis == 1 else 0
    specs = [pl.BlockSpec((a.shape[0], rows), lambda j, i: (0, i + row_at)) for a in lefts]
    specs += [pl.BlockSpec((b.shape[0], cols), lambda j, i: (0, j + col_at)) for b in rights]
    tile = pl.BlockSpec((rows, cols), lambda j, i: (i, j))
    tokens = sum(a.shape[0] for a in lefts)
    return pl.pallas_call(
        functools.partial(weight_grad_kernel, count, add is not None),
        grid=(dims[1] // cols, dims[0] // rows),
        in_specs=specs + ([tile] if add is not None else []),
        out_specs=tile,
        out_shape=shape(dims, BF16),
        compiler_params=PARAMS,
        cost_estimate=cost(2 * tokens * dims[0] * dims[1], 2 * tokens * sum(dims) + 2 * dims[0] * dims[1]),
        name="weight_grad",
    )(*lefts, *rights, *([add] if add is not None else []))


def xor_one(index):
    return index + 1 - 2 * (index % 2)


def remote(src, dst, send, recv, device):
    return pltpu.make_async_remote_copy(
        src_ref=src, dst_ref=dst, send_sem=send, recv_sem=recv, device_id=device, device_id_type=pl.DeviceIdType.MESH
    )


def greet(others):
    barrier = pltpu.get_barrier_semaphore()
    count = 0
    for needed, device in others:
        if needed is None:
            pl.semaphore_signal(barrier, inc=1, device_id=device, device_id_type=pl.DeviceIdType.MESH)
            count = count + 1
        else:

            @pl.when(needed)
            def _():
                pl.semaphore_signal(barrier, inc=1, device_id=device, device_id_type=pl.DeviceIdType.MESH)

            count = count + jnp.where(needed, 1, 0)
    pl.semaphore_wait(barrier, count)


class Gather:
    def __init__(self, shard, dst, axis, send, recv, local, near_x, near_y, near_core):
        piece = shard.shape[axis]
        half = shard.shape[0] // 2

        def block(side, k):
            cut = pl.ds(k * piece, piece)
            return dst.at[side, cut, :] if axis == 0 else dst.at[side, :, cut]

        def part(k, h):
            if axis == 0:
                return dst.at[0, pl.ds(k * piece + h * half, half), :]
            return dst.at[0, pl.ds(h * half, half), pl.ds(k * piece, piece)]

        sem = lambda k: (send.at[k], recv.at[k])
        self.local = pltpu.make_async_copy(shard, block(0, 0), local)
        self.x = remote(shard, block(0, 1), *sem(0), near_x)
        self.y = remote(shard, block(0, 2), *sem(1), near_y)
        self.dx = remote(part(2, 0), part(3, 0), *sem(2), near_x)
        self.dy = remote(part(1, 1), part(3, 1), *sem(3), near_y)
        self.cores = [remote(shard, block(1, 0), *sem(4), near_core)]
        self.cores += [remote(block(0, k), block(1, k), *sem(4 + k), near_core) for k in (1, 2, 3)]

    def first(self):
        self.x.start()
        self.y.start()
        self.cores[0].start()
        self.local.start()

    def second(self):
        self.y.wait_recv()
        self.dx.start()
        self.cores[2].start()
        self.x.wait_recv()
        self.dy.start()
        self.cores[1].start()

    def third(self):
        self.dx.wait_recv()
        self.dy.wait_recv()
        self.cores[3].start()

    def arrived(self):
        self.local.wait()
        for copy in self.cores:
            copy.wait_recv()

    def sent(self):
        for copy in [self.x, self.y, self.dx, self.dy] + self.cores:
            copy.wait_send()


def forward_kernel(
    hd, nq, nk, block, sub,
    len_ref, x_hbm, cot_hbm, wqkv, wout, wgate, wup, wdown, gain_ref, cos_ref, sin_ref, qg_ref, kg_ref,
    xr_hbm, n1_hbm, gf_hbm, qkv_hbm, out_hbm, gate_hbm, up_hbm, down_hbm, hidden_hbm, n2_hbm,
    gains_ref, pre_ref, all_ref, att_ref, inv_ref, tok_ref, stat_ref,
    xr_v, cot_v, n1_v, qkv_v, out_v, ex_own, ex_send, ex_got, at_own, at_send, at_got,
    part_v, in_v, back_v, total_v, hid_v, norm_v,
    load_sem, store_sem, wsend, wrecv, wloc, gsend, grecv, exsend, exrecv, zsend, zrecv, hid_sem,
):
    seqs, span, width = xr_v.shape
    groups = nq // nk
    row, core, rank = lax.axis_index("dp"), lax.axis_index("context"), lax.axis_index("tensor")
    start = core * span
    near = [row, xor_one(row), (row + 2) % 4, 3 - row]
    inner = (rank % 3) != 0
    near_x, near_y, near_core = {"dp": near[1]}, {"dp": near[2]}, {"context": 1 - core}
    z_side, z_mid = {"tensor": xor_one(rank)}, {"tensor": 3 - rank}
    piece = width // 8
    total_subs = part_v.shape[0]
    per = span // sub
    first_core = core == 0

    loads = []
    for at, (src, dst) in enumerate(((x_hbm, xr_v), (cot_hbm, cot_v))):
        for s in range(seqs):
            for o in range(2):
                for k in range(4):
                    b = near[k] * 2 + (core if o == 0 else 1 - core)
                    cut = pl.ds(pl.multiple_of(b * piece, piece), piece)
                    loads.append(
                        pltpu.make_async_copy(
                            src.at[s, :, cut], dst.at[s, :, pl.ds((o * 4 + k) * piece, piece)], load_sem.at[at, s, o * 4 + k]
                        )
                    )
    for copy in loads:
        copy.start()

    others = []
    for o in range(2):
        for k in range(4):
            if o or k:
                others.append((o * 4 + k, {"dp": near[k], "context": core if o == 0 else 1 - core}))
    greet([(None, d) for _, d in others] + [(None, z_side), (inner, z_mid)])

    gains = [remote(gain_ref, gains_ref.at[b], gsend.at[b], grecv.at[b], d) for b, d in others]
    for copy in gains:
        copy.start()
    weights = [
        Gather(shard, dst, axis, wsend.at[i], wrecv.at[i], wloc.at[i], near_x, near_y, near_core)
        for i, (shard, dst, axis) in enumerate(
            ((wqkv, qkv_v, 0), (wout, out_v, 1), (wgate, gate_hbm, 0), (wup, up_hbm, 0), (wdown, down_hbm, 1))
        )
    ]
    w_qkv, w_out, w_gate, w_up, w_down = weights
    w_qkv.first()
    w_out.first()
    gains_ref[0] = gain_ref[...]

    for copy in loads[len(loads) // 2 :]:
        copy.wait()

    def mask_rows(i, carry):
        s, t = i // (span // 16), i % (span // 16)
        cut = pl.ds(pl.multiple_of(t * 16, 16), 16)
        place = start + t * 16 + lax.broadcasted_iota(jnp.int32, (16, 1), 0)
        valid = (place < len_ref[s]).astype(F32)
        cot_v[s, cut, :] = (cot_v[s, cut, :].astype(F32) * valid).astype(BF16)
        return carry

    lax.fori_loop(0, seqs * span // 16, mask_rows, 0)
    store_gf = pltpu.make_async_copy(cot_v, gf_hbm, store_sem.at[0])
    store_gf.start()
    for copy in loads[: len(loads) // 2]:
        copy.wait()
    store_xr = pltpu.make_async_copy(xr_v, xr_hbm, store_sem.at[1])
    store_xr.start()
    for copy in gains:
        copy.wait_recv()
    gain1 = jnp.concatenate([gains_ref[b, 0:1, :] for b in range(8)], axis=1).astype(F32)
    gain2 = jnp.concatenate([gains_ref[b, 1:2, :] for b in range(8)], axis=1).astype(F32)

    def norm_rows(i, carry):
        s, t = i // (span // 16), i % (span // 16)
        cut = pl.ds(pl.multiple_of(t * 16, 16), 16)
        x = xr_v[s, cut, :].astype(F32)
        n1_v[s, cut, :] = (x * inverse_rms(x) * gain1).astype(BF16)
        return carry

    lax.fori_loop(0, seqs * span // 16, norm_rows, 0)
    store_n1 = pltpu.make_async_copy(n1_v, n1_hbm, store_sem.at[2])
    store_n1.start()
    w_qkv.second()
    w_out.second()
    w_gate.first()
    w_qkv.third()
    w_out.third()
    w_qkv.arrived()
    w_up.first()

    cosine, sine = cos_ref[...], sin_ref[...]
    half = width // 2

    def exchange(s):
        return remote(ex_send.at[s], ex_got.at[s], exsend.at[0, s], exrecv.at[0, s], near_core)

    def project(s, carry):
        x = n1_v[s]
        flat = dot_nn(x[:, :half], qkv_v[0]) + dot_nn(x[:, half:], qkv_v[1])
        turned = flat.T
        pre_ref[s] = turned[: (nq + nk) * hd]
        done = []
        for h in range(nq + nk):
            v = turned[h * hd : (h + 1) * hd]
            inv = lax.rsqrt(jnp.mean(v * v, axis=0, keepdims=True) + epsilon)
            v = v * inv * (qg_ref[...] if h < nq else kg_ref[...])
            a, b = v[: hd // 2], v[hd // 2 :]
            done.append(jnp.concatenate([a * cosine - b * sine, b * cosine + a * sine], axis=0))
        for h in range(nk):
            lo = (nq + nk + h) * hd
            done.append(turned[lo : lo + hd])
        parts = [[], []]
        for begin_at, count in ((0, nq), (nq, nk), (nq + nk, nk)):
            for side in range(2):
                parts[side] += done[begin_at + side * count // 2 : begin_at + (side + 1) * count // 2]
        low = jnp.concatenate(parts[0], axis=0)
        high = jnp.concatenate(parts[1], axis=0)
        ex_own[s] = jnp.where(first_core, low, high).astype(BF16)
        ex_send[s] = jnp.where(first_core, high, low).astype(BF16)
        exchange(s).start()
        return carry

    lax.fori_loop(0, seqs, project, 0)
    store_qkv = pltpu.make_async_copy(qkv_v, qkv_hbm, store_sem.at[3])
    store_qkv.start()

    scale = log2e / math.sqrt(hd)
    krow = lax.broadcasted_iota(jnp.int32, (block, groups * block), 0)
    qcol = lax.broadcasted_iota(jnp.int32, (block, groups * block), 1) % block
    base = groups * hd

    def give(s):
        return remote(at_send.at[s], at_got.at[s], exsend.at[1, s], exrecv.at[1, s], near_core)

    def attention(s, carry):
        exchange(s).wait_recv()
        low, high = join_positions(core, ex_own[s], ex_got[s])
        all_ref[s, :, :span] = low
        all_ref[s, :, span:] = high
        length = len_ref[s]
        for i in range(2 * span // block):
            cut = slice(i * block, (i + 1) * block)
            q = jnp.concatenate([all_ref[s, g * hd : (g + 1) * hd, cut] for g in range(groups)], axis=1)
            acc = jnp.zeros((hd, groups * block), F32)
            total = jnp.zeros((1, groups * block), F32)
            for j in range(i + 1):
                kcut = slice(j * block, (j + 1) * block)
                score = dot_tn(all_ref[s, base : base + hd, kcut], q) * scale
                ok = (krow + j * block) < length
                if j == i:
                    ok = ok & (krow <= qcol)
                e = jnp.where(ok, jnp.exp2(score), 0.0)
                total = total + jnp.sum(e, axis=0, keepdims=True)
                acc = acc + dot_nn(all_ref[s, base + hd : base + 2 * hd, kcut], e.astype(BF16))
            inv = 1.0 / total
            att = (acc * inv).astype(BF16)
            for g in range(groups):
                att_ref[s, g * hd : (g + 1) * hd, cut] = att[:, g * block : (g + 1) * block]
                inv_ref[s, g : g + 1, cut] = inv[:, g * block : (g + 1) * block]
        mine, theirs = join_positions(core, att_ref[s, :, :span], att_ref[s, :, span:])
        at_own[s] = mine
        at_send[s] = theirs
        give(s).start()
        return carry

    lax.fori_loop(0, seqs, attention, 0)
    w_out.arrived()
    store_out = pltpu.make_async_copy(out_v, out_hbm, store_sem.at[4])
    store_out.start()

    moving = Chain(rank, part_v, in_v, back_v, zsend, zrecv)

    def branch_rows(s, carry):
        give(s).wait_recv()
        low, high = join_positions(core, at_own[s], at_got[s])
        att = jnp.concatenate([low, high], axis=0).T
        tok_ref[s] = att
        for k in range(per):
            u = s * per + k
            rows = att[k * sub : (k + 1) * sub]
            part_v[u, :, :half] = dot_nn(rows, out_v[0]).astype(BF16)
            part_v[u, :, half:] = dot_nn(rows, out_v[1]).astype(BF16)

            moving.begin(u)
        return carry

    lax.fori_loop(0, seqs, branch_rows, 0)
    w_gate.second()
    w_down.first()
    stat_ref[...] = jnp.zeros_like(stat_ref)

    def hidden_store(u):
        cut = pl.ds(pl.multiple_of(u * sub, sub), sub)
        return (
            pltpu.make_async_copy(hid_v.at[u % 2], hidden_hbm.at[cut, :], hid_sem.at[0, u % 2]),
            pltpu.make_async_copy(norm_v.at[u % 2], n2_hbm.at[cut, :], hid_sem.at[1, u % 2]),
        )

    def finish(u):
        s, t = u // per, u % per
        cut = pl.ds(pl.multiple_of(t * sub, sub), sub)

        moving.total(u, total_v)

        @pl.when(u >= 2)
        def _():
            for copy in hidden_store(u - 2):
                copy.wait()

        length = len_ref[s]

        def body(piece_rows, first):
            total = total_v[piece_rows, :]
            resid = xr_v[s, pl.ds(pl.multiple_of(t * sub + first, 16), 16), :].astype(F32)
            hidden = resid + total
            hid_v[u % 2, piece_rows, :] = hidden
            norm_v[u % 2, piece_rows, :] = (hidden * inverse_rms(hidden) * gain2).astype(BF16)
            place = start + t * sub + first + lax.broadcasted_iota(jnp.int32, (16, 1), 0)
            valid = (place < length).astype(F32)
            stat_ref[0] += fold_lanes(valid * resid * resid)
            stat_ref[1] += fold_lanes(valid * total * total)

        by_pieces(sub, body)
        for copy in hidden_store(u):
            copy.start()

    def chain(i, carry):
        moving.middle(i)
        moving.outward(i - 1)

        @pl.when(i >= 2)
        def _():
            finish(i - 2)

        @pl.when(i == total_subs // 2 - 2)
        def _():
            w_gate.third()
            w_up.second()

        @pl.when(i == total_subs - 1)
        def _():
            w_up.third()
            w_down.second()

        return carry

    lax.fori_loop(0, total_subs + 2, chain, 0)
    w_down.third()
    for u in (total_subs - 2, total_subs - 1):
        for copy in hidden_store(u):
            copy.wait()

    moving.settle()
    for s in range(seqs):
        exchange(s).wait_send()
        give(s).wait_send()
    for copy in gains:
        copy.wait_send()
    for w in weights[2:]:
        w.arrived()
    for w in weights:
        w.sent()
    for copy in (store_gf, store_xr, store_n1, store_qkv, store_out):
        copy.wait()


def forward(lengths, x, cot, w_qkv, w_out, w_gate, w_up, w_down, gains, cosine, sine, qgain, kgain, hd, nq, nk):
    seqs, span, width = x.shape
    half = width // 2
    groups = nq // nk
    sub = min(128, span)
    subs = seqs * span // sub
    block = min(256, span)
    hidden = w_gate.shape[1]
    cols = w_qkv.shape[1]
    rows = cols // 2
    any_space = pl.BlockSpec(memory_space=pl.ANY)
    vmem = pl.BlockSpec(memory_space=pltpu.VMEM)
    wide = (seqs, span, width)
    large = [
        shape(wide, BF16), shape(wide, BF16), shape(wide, BF16),
        shape((2, half, cols), BF16), shape((2, w_out.shape[0], half), BF16),
        shape((2, half, hidden), BF16), shape((2, half, hidden), BF16), shape((2, hidden, half), BF16),
        shape((seqs * span, width), F32), shape((seqs * span, width), BF16),
    ]
    small = [
        shape((8,) + gains.shape, BF16), shape((seqs, (nq + nk) * hd, span), F32), shape((seqs, rows, 2 * span), BF16),
        shape((seqs, groups * hd, 2 * span), BF16), shape((seqs, groups, 2 * span), F32), shape((seqs, span, nq * hd), BF16),
        shape((2, 8, 128), F32),
    ]
    dma = pltpu.SemaphoreType.DMA
    ex = pltpu.VMEM((seqs, rows, span), BF16)
    at = pltpu.VMEM((seqs, groups * hd, span), BF16)
    moving = pltpu.VMEM((subs, sub, width), BF16)
    flops = 2 * seqs * span * width * (cols + nq * hd) + 16 * seqs * nq * hd * span * span
    return pl.pallas_call(
        functools.partial(forward_kernel, hd, nq, nk, block, sub),
        in_specs=[SMEM] + [any_space] * 7 + [vmem] * 5,
        out_specs=[any_space] * len(large) + [vmem] * len(small),
        out_shape=large + small,
        scratch_shapes=[
            pltpu.VMEM(wide, BF16), pltpu.VMEM(wide, BF16), pltpu.VMEM(wide, BF16),
            pltpu.VMEM((2, half, cols), BF16), pltpu.VMEM((2, w_out.shape[0], half), BF16),
            ex, ex, ex, at, at, at,
            moving, moving, moving,
            pltpu.VMEM((sub, width), F32), pltpu.VMEM((2, sub, width), F32), pltpu.VMEM((2, sub, width), BF16),
            dma((2, seqs, 8)), dma((5,)), dma((5, 8)), dma((5, 8)), dma((5,)), dma((8,)), dma((8,)),
            dma((2, seqs)), dma((2, seqs)), dma((3, subs)), dma((3, subs)), dma((2, 2)),
        ],
        compiler_params=pltpu.CompilerParams(vmem_limit_bytes=VMEM_BYTES, collective_id=1, has_side_effects=True),
        cost_estimate=cost(flops, 80 * seqs * span * width),
        name="attention_forward",
    )(lengths, x, cot, w_qkv, w_out, w_gate, w_up, w_down, gains, cosine, sine, qgain, kgain)


def by_pieces(count, body, size=16):
    def one(p, carry):
        body(pl.ds(pl.multiple_of(p * size, size), size), p * size)
        return carry

    lax.fori_loop(0, count // size, one, 0)


def fold_lanes(values):
    tiles = values[:8] + values[8:]
    return sum(tiles[:, k * 128 : (k + 1) * 128] for k in range(tiles.shape[1] // 128))


class Chain:
    def __init__(self, rank, part, arrive, back, send, recv):
        self.inner = (rank % 3) != 0
        self.outer = (rank % 3) == 0
        self.part, self.arrive, self.back = part, arrive, back
        self.send, self.recv = send, recv
        self.side, self.mid = {"tensor": xor_one(rank)}, {"tensor": 3 - rank}
        self.count = part.shape[0]

    def hop_in(self, u):
        return remote(self.part.at[u], self.arrive.at[u], self.send.at[0, u], self.recv.at[0, u], self.side)

    def hop_mid(self, u):
        return remote(self.arrive.at[u], self.back.at[u], self.send.at[1, u], self.recv.at[1, u], self.mid)

    def hop_out(self, u):
        return remote(self.part.at[u], self.back.at[u], self.send.at[2, u], self.recv.at[2, u], self.side)

    def add(self, into, one, two, u):
        def body(cut, first):
            into[u, cut, :] = (one[u, cut, :].astype(F32) + two[u, cut, :].astype(F32)).astype(BF16)

        by_pieces(self.part.shape[1], body)

    def begin(self, u):
        @pl.when(self.outer)
        def _():
            self.hop_in(u).start()

    def middle(self, u):
        @pl.when((u >= 0) & (u < self.count) & self.inner)
        def _():
            self.hop_in(u).wait_recv()
            self.add(self.arrive, self.part, self.arrive, u)
            self.hop_mid(u).start()

    def outward(self, u):
        @pl.when((u >= 0) & (u < self.count) & self.inner)
        def _():
            self.hop_mid(u).wait_recv()
            self.add(self.part, self.part, self.back, u)
            self.hop_out(u).start()

    def total(self, u, into):
        @pl.when(self.inner)
        def _():
            def body(cut, first):
                into[cut, :] = self.arrive[u, cut, :].astype(F32) + self.back[u, cut, :].astype(F32)

            by_pieces(self.part.shape[1], body)

        @pl.when(self.outer)
        def _():
            self.hop_out(u).wait_recv()

            def body(cut, first):
                into[cut, :] = self.part[u, cut, :].astype(F32) + self.back[u, cut, :].astype(F32)

            by_pieces(self.part.shape[1], body)

    def settle(self):
        def one(u, carry):
            @pl.when(self.outer)
            def _():
                self.hop_in(u).wait_send()

            @pl.when(self.inner)
            def _():
                self.hop_mid(u).wait_send()
                self.hop_out(u).wait_send()

            return carry

        lax.fori_loop(0, self.count, one, 0)


def feed_both_kernel(
    hb, sub, rows,
    n2_hbm, gf_hbm, gate_hbm, up_hbm, down_hbm, hidden_hbm, gain_ref,
    ffn_hbm, gb_hbm, gh_hbm, dgate_hbm, dup_hbm, ddown_hbm, gain_out,
    n2_v, gf_v, inner_v, gg_v, gu_v, facc, gacc, wrow, wcol, part_v, in_v, back_v, total_v, hid_v, gh_v, gb_v, ffn_v, stage_row, stage_col,
    load_sem, wsem, zsend, zrecv, hid_sem, out_sem, ffn_sem, csend, crecv, store_sem, free_sem,
):
    core, rank = lax.axis_index("context"), lax.axis_index("tensor")
    near_core = {"context": 1 - core}
    tokens, width = n2_v.shape
    half = width // 2
    hidden = inner_v.shape[1]
    hsteps = hidden // hb
    steps = tokens // rows * hsteps
    per = rows // sub
    chain = Chain(rank, part_v, in_v, back_v, zsend, zrecv)
    subs = chain.count

    def load_weights(i):
        slot, h = i % 2, i % hsteps
        cut = pl.ds(pl.multiple_of(h * hb, hb), hb)
        copies = []
        for side in range(2):
            copies.append(pltpu.make_async_copy(gate_hbm.at[side, :, cut], wrow.at[slot, 0, side], wsem.at[slot, side]))
            copies.append(pltpu.make_async_copy(up_hbm.at[side, :, cut], wrow.at[slot, 1, side], wsem.at[slot, 2 + side]))
            copies.append(pltpu.make_async_copy(down_hbm.at[side, cut, :], wcol.at[slot, side], wsem.at[slot, 4 + side]))
        return copies

    def load_hidden(u):
        cut = pl.ds(pl.multiple_of(u * sub, sub), sub)
        return pltpu.make_async_copy(hidden_hbm.at[cut, :], hid_v.at[u % 2], hid_sem.at[u % 2])

    loads = [pltpu.make_async_copy(n2_hbm, n2_v, load_sem.at[0]), pltpu.make_async_copy(gf_hbm, gf_v, load_sem.at[1])]
    for copy in loads + load_weights(0):
        copy.start()
    for u in range(2):
        load_hidden(u).start()
    greet([(None, chain.side), (chain.inner, chain.mid), (None, near_core)])
    gain_out[...] = jnp.zeros_like(gain_out)
    for copy in loads:
        copy.wait()

    def stores(u):
        cut = pl.ds(pl.multiple_of(u * sub, sub), sub)
        return (
            pltpu.make_async_copy(gh_v.at[u % 2], gh_hbm.at[cut, :], out_sem.at[0, u % 2]),
            pltpu.make_async_copy(gb_v.at[u % 2], gb_hbm.at[cut, :], out_sem.at[1, u % 2]),
        )

    def finish(u):
        chain.total(u, total_v)
        load_hidden(u).wait()

        @pl.when(u >= 2)
        def _():
            for copy in stores(u - 2):
                copy.wait()

        def body(piece_rows, first):
            e = total_v[piece_rows, :]
            hidden_rows = hid_v[u % 2, piece_rows, :]
            inv = inverse_rms(hidden_rows)
            hat = hidden_rows * inv
            eg = e * gain_ref[...]
            grad = gf_v[pl.ds(pl.multiple_of(u * sub + first, 16), 16), :].astype(F32)
            gh = grad + inv * (eg - hat * jnp.mean(eg * hat, axis=-1, keepdims=True))
            gh_v[u % 2, piece_rows, :] = gh
            gb_v[u % 2, piece_rows, :] = gh.astype(BF16)
            both = e * hat
            gain_out[...] += both[:8] + both[8:]

        by_pieces(sub, body)
        for copy in stores(u):
            copy.start()

        @pl.when(u + 2 < subs)
        def _():
            load_hidden(u + 2).start()

    def serve(k):
        chain.middle(k - 3)
        chain.outward(k - 4)

        @pl.when((k >= 5) & (k < 5 + subs))
        def _():
            finish(k - 5)

    def store_ffn(c):
        return pltpu.make_async_copy(ffn_v, ffn_hbm.at[pl.ds(pl.multiple_of(c * rows, rows), rows), :], ffn_sem)

    def step(i, carry):
        slot, c, h = i % 2, i // hsteps, i % hsteps
        for copy in load_weights(i):
            copy.wait()

        @pl.when(i + 1 < steps)
        def _():
            for copy in load_weights(i + 1):
                copy.start()

        here = pl.ds(pl.multiple_of(c * rows, rows), rows)
        cols = pl.ds(pl.multiple_of(h * hb, hb), hb)
        n, g = n2_v[here, :], gf_v[here, :]
        wide = min(256, hb)
        for q in range(hb // wide):
            part = slice(q * wide, (q + 1) * wide)
            gate = dot_nn(n[:, :half], wrow[slot, 0, 0, :, part]) + dot_nn(n[:, half:], wrow[slot, 0, 1, :, part])
            up = dot_nn(n[:, :half], wrow[slot, 1, 0, :, part]) + dot_nn(n[:, half:], wrow[slot, 1, 1, :, part])
            gi = dot_nt(g[:, :half], wcol[slot, 0, part, :]) + dot_nt(g[:, half:], wcol[slot, 1, part, :])
            sig = jax.nn.sigmoid(gate)
            silu = gate * sig
            at = pl.ds(pl.multiple_of(h * hb + q * wide, wide), wide)
            inner_v[here, at] = (silu * up).astype(BF16)
            gg_v[here, at] = (gi * up * sig * (1.0 + gate * (1.0 - sig))).astype(BF16)
            gu_v[here, at] = (gi * silu).astype(BF16)

        @pl.when(h == 0)
        def _():
            facc[...] = jnp.zeros_like(facc)
            gacc[...] = jnp.zeros_like(gacc)

        inner, gg, gu = inner_v[here, cols], gg_v[here, cols], gu_v[here, cols]
        span = min(512, half)
        for side in range(2):
            for q in range(half // span):
                part = slice(q * span, (q + 1) * span)
                cut = slice(side * half + q * span, side * half + (q + 1) * span)
                facc[:, cut] += dot_nn(inner, wcol[slot, side, :, part])
                gacc[:, cut] += dot_nt(gg, wrow[slot, 0, side, part, :]) + dot_nt(gu, wrow[slot, 1, side, part, :])

        @pl.when(h == hsteps - 1)
        def _():
            for k in range(per):
                part_v[c * per + k] = gacc[k * sub : (k + 1) * sub, :].astype(BF16)
                chain.begin(c * per + k)

            @pl.when(c > 0)
            def _():
                store_ffn(c - 1).wait()

            ffn_v[...] = facc[...].astype(BF16)
            store_ffn(c).start()

        @pl.when(i % 2 == 0)
        def _():
            serve(i // 2)

        return carry

    lax.fori_loop(0, steps, step, 0)

    pl.semaphore_signal(free_sem, inc=1, device_id=near_core, device_id_type=pl.DeviceIdType.MESH)
    outs = (dgate_hbm, dup_hbm, ddown_hbm)

    def landing(w, t):
        return wrow.at[t // 2, w, t % 2] if w < 2 else wcol.at[t // 2, t % 2]

    def landed(w, t, piece):
        return wrow[t // 2, w, t % 2, piece, :] if w < 2 else wcol[t // 2, t % 2, piece, :]

    def staging(w):
        return stage_row if w < 2 else stage_col

    def ship(w, t):
        return remote(staging(w).at[t % 2], landing(w, t), csend.at[w, t], crecv.at[w, t], near_core)

    def keep(w, t):
        cut = pl.ds(pl.multiple_of(t * hb, hb), hb)
        dst = outs[w].at[:, cut] if w < 2 else outs[w].at[cut, :]
        return pltpu.make_async_copy(staging(w).at[t % 2], dst, store_sem.at[w, t])

    def release(kind, w, t):
        if kind == 1:
            ship(w, t).wait_send()
        else:
            keep(w, t).wait()

    def group(kind, w, before):
        def one(t, carry):
            cut = pl.ds(pl.multiple_of(t * hb, hb), hb)
            mine = slice(kind * half, (kind + 1) * half)
            @pl.when(t >= 2)
            def _():
                release(kind, w, t - 2)

            if before is not None:

                @pl.when(t < 2)
                def _():
                    release(before[0], before[1], t + hsteps - 2)

            if kind == 0:
                ship(w, t).wait_recv()
            tall = staging(w).shape[1]
            size = min(256, tall)
            for q in range(tall // size):
                piece = slice(q * size, (q + 1) * size)
                if w == 2:
                    left = inner_v[:, pl.ds(pl.multiple_of(t * hb + q * size, size), size)]
                    value = dot_tn(left, gf_v[:, mine])
                else:
                    value = dot_tn(n2_v[:, kind * half + q * size : kind * half + (q + 1) * size], (gg_v, gu_v)[w][:, cut])
                if kind == 0:
                    value = value + landed(w, t, piece).astype(F32)
                staging(w)[t % 2, piece, :] = value.astype(BF16)
            if kind == 1:
                ship(w, t).start()
            else:
                keep(w, t).start()
            return carry

        lax.fori_loop(0, hsteps, one, 0)

    done = steps // 2
    serve(done)
    pl.semaphore_wait(free_sem, 1)
    group(1, 0, None)
    serve(done + 1)
    group(1, 1, (1, 0))
    group(0, 0, (1, 1))
    serve(done + 2)
    group(1, 2, None)
    group(0, 1, (0, 0))
    serve(done + 3)
    group(0, 2, (1, 2))
    for k in range(done + 4, 5 + subs):
        serve(k)
    for t in range(hsteps - 2, hsteps):
        keep(1, t).wait()
        keep(2, t).wait()
    store_ffn(steps // hsteps - 1).wait()
    for u in range(subs - 2, subs):
        for copy in stores(u):
            copy.wait()
    chain.settle()


def feed_both(n2, gf, gate, up, down, hidden_rows, gain):
    tokens, width = n2.shape
    _, half, hidden = gate.shape
    hb = hidden // 4
    sub, rows = tokens // 8, tokens // 4
    any_space = pl.BlockSpec(memory_space=pl.ANY)
    vmem = pl.BlockSpec(memory_space=pltpu.VMEM)
    dma = pltpu.SemaphoreType.DMA
    moving = pltpu.VMEM((8, sub, width), BF16)
    act = pltpu.VMEM((tokens, hidden), BF16)
    return pl.pallas_call(
        functools.partial(feed_both_kernel, hb, sub, rows),
        in_specs=[any_space] * 6 + [vmem],
        out_specs=[any_space] * 6 + [vmem],
        out_shape=[
            shape((tokens, width), BF16), shape((tokens, width), BF16), shape((tokens, width), F32),
            shape((half, hidden), BF16), shape((half, hidden), BF16), shape((hidden, half), BF16), shape((8, width), F32),
        ],
        scratch_shapes=[
            pltpu.VMEM((tokens, width), BF16), pltpu.VMEM((tokens, width), BF16), act, act, act,
            pltpu.VMEM((rows, width), F32), pltpu.VMEM((rows, width), F32),
            pltpu.VMEM((2, 2, 2, half, hb), BF16), pltpu.VMEM((2, 2, hb, half), BF16),
            moving, moving, moving, pltpu.VMEM((sub, width), F32),
            pltpu.VMEM((2, sub, width), F32), pltpu.VMEM((2, sub, width), F32), pltpu.VMEM((2, sub, width), BF16),
            pltpu.VMEM((rows, width), BF16), pltpu.VMEM((2, half, hb), BF16), pltpu.VMEM((2, hb, half), BF16),
            dma((2,)), dma((2, 6)), dma((3, 8)), dma((3, 8)), dma((2,)), dma((2, 2)), dma(()), dma((3, 4)), dma((3, 4)),
            dma((3, 4)), pltpu.SemaphoreType.REGULAR,
        ],
        compiler_params=pltpu.CompilerParams(vmem_limit_bytes=VMEM_MOST, collective_id=2, has_side_effects=True),
        cost_estimate=cost(18 * tokens * width * hidden, 60 * tokens * width),
        name="feed_forward_both",
    )(n2, gf, gate, up, down, hidden_rows, gain)


class Ring:
    def __init__(self, rank, source, own, slots, send, recv):
        self.source, self.own, self.slots, self.send, self.recv = source, own, slots, send, recv
        self.rank, self.right = rank, {"tensor": (rank + 1) % 4}

    def hop(self, j):
        src = self.source((self.rank + 3) % 4) if j == 0 else self.slots.at[j - 1]
        return remote(src, self.slots.at[j], self.send.at[j], self.recv.at[j], self.right)

    def begin(self):
        self.hop(0).start()

    def step(self, j):
        self.hop(j - 1).wait_recv()
        read = self.own((self.rank + 3 - j) % 4)

        def body(cut, first):
            self.slots[j - 1, cut, :] = (self.slots[j - 1, cut, :].astype(F32) + read(cut).astype(F32)).astype(BF16)

        by_pieces(self.slots.shape[1], body)
        self.hop(j).start()

    def arrived(self):
        self.hop(2).wait_recv()

    def settle(self):
        for j in range(3):
            self.hop(j).wait_send()


def tall(ref):
    return 16 * max(1, 2048 // ref.shape[1])


class Scatter:
    def __init__(self, block, from_x, from_y, land_x, land_y, temps, send, recv, load, near_x, near_y):
        self.block, self.from_x, self.from_y, self.land_x, self.land_y = block, from_x, from_y, land_x, land_y
        self.temps, self.load = temps, load
        sem = lambda k: (send.at[k], recv.at[k])
        self.first = [
            remote(block(3, 0), from_x, *sem(0), near_x),
            remote(block(3, 1), from_y, *sem(1), near_y),
            remote(block(1, 0), land_x(0), *sem(2), near_x),
            remote(block(2, 1), land_y(1), *sem(3), near_y),
        ]
        self.second = [
            remote(from_y, land_x(1), *sem(4), near_x),
            remote(from_x, land_y(0), *sem(5), near_y),
        ]

    def begin(self):
        for copy in self.first:
            copy.start()

    def pass_on(self):
        loads = [
            pltpu.make_async_copy(self.block(1, 1), self.temps.at[0], self.load.at[0]),
            pltpu.make_async_copy(self.block(2, 0), self.temps.at[1], self.load.at[1]),
        ]
        for copy in loads:
            copy.start()
        for which, into in ((1, self.from_y), (0, self.from_x)):
            self.first[which].wait_recv()
            loads[1 - which].wait()
            temp = 1 - which

            def body(cut, first):
                into[cut, :] = (into[cut, :].astype(F32) + self.temps[temp, cut, :].astype(F32)).astype(BF16)

            by_pieces(into.shape[0], body, tall(into))
            self.second[temp].start()

    def finish(self, stage, out, store):
        for copy in self.first[2:] + self.second:
            copy.wait_recv()
        for h in range(2):
            loads = [
                pltpu.make_async_copy(src, self.temps.at[k], self.load.at[k])
                for k, src in enumerate((self.block(0, h), self.land_x(h), self.land_y(h)))
            ]
            for copy in loads:
                copy.start()
            for copy in loads:
                copy.wait()

            def body(cut, first):
                stage[cut, :] = sum(self.temps[k, cut, :].astype(F32) for k in range(3))

            by_pieces(stage.shape[0], body, tall(stage))
            keep = pltpu.make_async_copy(stage, out(h), store)
            keep.start()
            keep.wait()

    def settle(self):
        for copy in self.first + self.second:
            copy.wait_send()


def backward_kernel(
    hd, nq, nk, block,
    len_ref, gb_hbm, gh_hbm, hidden_hbm, ffn_hbm, xr_hbm, n1_hbm, tok_hbm, outw_hbm, qkvw_hbm, all_hbm, att_hbm, inv_hbm, pre_hbm,
    dgate_hbm, dup_hbm, ddown_hbm, gain_ref, cos_ref, sin_ref, qg_ref, kg_ref, stat_ref, gain2_ref,
    out_hbm, gin_hbm, ggate_hbm, gup_hbm, gdown_hbm, gout_hbm, gqkv_hbm, landx0, landy0, landx1, landy1, landx2, landy2,
    lines_out, small_out,
    act_v, rows_v, qkvw_v, tok_v, all_v, att_v, inv_v, pre_v, grads, da_all, da_own, da_send, da_got, d_own, d_send, d_got, dpre_v,
    first_v, slots_v, piece_v, wide_a, wide_b, temp_a, temp_b, stage_a, stage_b,
    go_v, so_v, wide_o, land_o, temp_o, stage_o, gq_v, sq_v, wide_q, land_q, temp_q, stage_q,
    tile_v, xtile_v, otile_v, itile_v, lines_v, small_v, lin1, lin2, lin3, lin4, lin5, small_r,
    load_sem, zsend, zrecv, piece_sem, xsend, xrecv, xload, xstore, exsend, exrecv, osend, orecv, qsend, qrecv,
    tile_sem, outs_sem, smsend, smrecv,
):
    seqs, _, slots = all_v.shape
    span = slots // 2
    width = act_v.shape[1]
    half = width // 2
    groups = nq // nk
    share = span // 4
    row, core, rank = lax.axis_index("dp"), lax.axis_index("context"), lax.axis_index("tensor")
    start = core * span
    near = [row, xor_one(row), (row + 2) % 4, 3 - row]
    near_x, near_y, near_core = {"dp": near[1]}, {"dp": near[2]}, {"context": 1 - core}
    z_right, z_left, z_far = {"tensor": (rank + 1) % 4}, {"tensor": (rank + 3) % 4}, {"tensor": (rank + 2) % 4}
    first_core = core == 0

    def load(k, src, dst):
        copy = pltpu.make_async_copy(src, dst, load_sem.at[k])
        copy.start()
        return copy

    load_gb = load(0, gb_hbm, act_v)
    load_outw = load(1, outw_hbm, rows_v)
    load_att = [
        load(2, all_hbm, all_v), load(3, att_hbm, att_v), load(4, inv_hbm, inv_v), load(5, pre_hbm, pre_v),
    ]
    load_tok = load(6, tok_hbm, tok_v)
    load_qkvw = load(7, qkvw_hbm, qkvw_v)

    def piece_rows(s, m):
        return pl.ds(pl.multiple_of(s * span + m * share, share), share)

    def load_piece(s, m):
        return pltpu.make_async_copy(ffn_hbm.at[piece_rows(s, m), :], piece_v.at[s], piece_sem.at[s])

    greet([(None, d) for d in (near_x, near_y, near_core, z_right, z_left, z_far)])

    def ffn_own(s):
        def own(m):
            load_piece(s, m).wait()
            return lambda cut: piece_v[s, cut, :]

        return own

    def first_own(s):
        return lambda m: lambda cut: first_v[s, m, cut, :]

    ffn_rings = [
        Ring(rank, lambda m, s=s: ffn_hbm.at[piece_rows(s, m), :], ffn_own(s), slots_v.at[s], zsend.at[s], zrecv.at[s])
        for s in range(seqs)
    ]
    first_rings = [
        Ring(rank, lambda m, s=s: first_v.at[s, m], first_own(s), slots_v.at[seqs + s], zsend.at[seqs + s], zrecv.at[seqs + s])
        for s in range(seqs)
    ]
    for s in range(seqs):
        ffn_rings[s].begin()
        load_piece(s, (rank + 2) % 4).start()

    def ffn_step(s, j):
        ffn_rings[s].step(j)
        load_piece(s, (rank + 2 - j) % 4).start()

    def in_hbm(ref, axis):
        size = ref.shape[axis] // 4
        h2 = (size if axis == 0 else ref.shape[0]) // 2

        def get(k, h):
            if axis == 0:
                return ref.at[pl.ds(k * size + h * h2, h2), :]
            return ref.at[pl.ds(h * h2, h2), pl.ds(k * size, size)]

        return get

    def halves(ref):
        h2 = ref.shape[0] // 2
        return lambda h: ref.at[pl.ds(h * h2, h2), :]

    def in_vmem(ref):
        h2 = ref.shape[1] // 2
        return lambda k, h: ref.at[k, pl.ds(h * h2, h2), :]

    def scatter(i, get, wide, land_x, land_y, temps):
        return Scatter(get, wide.at[0], wide.at[1], land_x, land_y, temps, xsend.at[i], xrecv.at[i], xload.at[i], near_x, near_y)

    s_gate = scatter(0, in_hbm(dgate_hbm, 0), wide_a.at[0], halves(landx0), halves(landy0), temp_a)
    s_up = scatter(1, in_hbm(dup_hbm, 0), wide_a.at[1], halves(landx1), halves(landy1), temp_a)
    s_down = scatter(2, in_hbm(ddown_hbm, 1), wide_b, halves(landx2), halves(landy2), temp_b)
    s_out = scatter(3, in_vmem(go_v), wide_o, halves(land_o.at[0]), halves(land_o.at[1]), temp_o)
    s_qkv = scatter(4, in_vmem(gq_v), wide_q, halves(land_q.at[0]), halves(land_q.at[1]), temp_q)
    for item in (s_gate, s_up, s_down):
        item.begin()

    load_gb.wait()
    load_outw.wait()

    def give(s):
        return remote(da_send.at[s], da_got.at[s], exsend.at[0, s], exrecv.at[0, s], near_core)

    def exchange(s):
        return remote(d_send.at[s], d_got.at[s], exsend.at[1, s], exrecv.at[1, s], near_core)

    def branch_rows(s, carry):
        here = pl.ds(pl.multiple_of(s * span, span), span)
        parts = []
        for q in range(2):
            cut = slice(q * (nq * hd // 2), (q + 1) * (nq * hd // 2))
            da = dot_nt(rows_v[0, cut, :], act_v[here, :half]) + dot_nt(rows_v[1, cut, :], act_v[here, half:])
            parts.append(da.astype(BF16))
        da_own[s] = jnp.where(first_core, parts[0], parts[1])
        da_send[s] = jnp.where(first_core, parts[1], parts[0])
        give(s).start()
        return carry

    lax.fori_loop(0, seqs, branch_rows, 0)

    def load_x(s):
        return [pltpu.make_async_copy(xr_hbm.at[s, :, pl.ds(k * half, half)], rows_v.at[k], load_sem.at[8 + k]) for k in range(2)]

    for copy in load_x(0):
        copy.start()
    for copy in load_att:
        copy.wait()

    scale = log2e / math.sqrt(hd)
    back = 1.0 / math.sqrt(hd)
    krow = lax.broadcasted_iota(jnp.int32, (block, groups * block), 0)
    qcol = lax.broadcasted_iota(jnp.int32, (block, groups * block), 1) % block
    base = groups * hd

    def attention(s, carry):
        give(s).wait_recv()
        low, high = join_positions(core, da_own[s], da_got[s])
        da_all[:, :span] = low
        da_all[:, span:] = high
        length = len_ref[s]
        grads[base:, :] = jnp.zeros((2 * hd, slots), F32)
        for i in range(slots // block):
            cut = slice(i * block, (i + 1) * block)
            q = jnp.concatenate([all_v[s, g * hd : (g + 1) * hd, cut] for g in range(groups)], axis=1)
            da = jnp.concatenate([da_all[g * hd : (g + 1) * hd, cut] for g in range(groups)], axis=1)
            at = jnp.concatenate([att_v[s, g * hd : (g + 1) * hd, cut] for g in range(groups)], axis=1)
            inv = jnp.concatenate([inv_v[s, g : g + 1, cut] for g in range(groups)], axis=1)
            delta = jnp.sum(at.astype(F32) * da.astype(F32), axis=0, keepdims=True)
            dq = jnp.zeros((hd, groups * block), F32)
            for j in range(i + 1):
                kcut = slice(j * block, (j + 1) * block)
                key = all_v[s, base : base + hd, kcut]
                score = dot_tn(key, q) * scale
                ok = (krow + j * block) < length
                if j == i:
                    ok = ok & (krow <= qcol)
                p = jnp.where(ok, jnp.exp2(score) * inv, 0.0)
                dp = dot_tn(all_v[s, base + hd : base + 2 * hd, kcut], da)
                ds = (p * (dp - delta)).astype(BF16)
                dq = dq + dot_nn(key, ds)
                grads[base : base + hd, kcut] += dot_nt(q, ds) * back
                grads[base + hd : base + 2 * hd, kcut] += dot_nt(da, p.astype(BF16))
            dq = dq * back
            for g in range(groups):
                grads[g * hd : (g + 1) * hd, cut] = dq[:, g * block : (g + 1) * block]
        mine, theirs = join_positions(core, grads[:, :span], grads[:, span:])
        d_own[s] = mine.astype(BF16)
        d_send[s] = theirs.astype(BF16)
        exchange(s).start()

        @pl.when(s == 0)
        def _():
            ffn_step(0, 1)

        @pl.when(s == seqs - 1)
        def _():
            ffn_step(1, 1)
            s_gate.pass_on()

        return carry

    lax.fori_loop(0, seqs, attention, 0)

    load_tok.wait()
    blocks_o = [remote(so_v.at[k], go_v.at[k], osend.at[k], orecv.at[k], near_core) for k in range(4)]
    size_o = half // 4
    for k in range(4):
        cut = slice(half + k * size_o, half + (k + 1) * size_o)
        so_v[k] = dot_tn(tok_v[...], act_v[:, cut]).astype(BF16)
        blocks_o[k].start()

    cosine, sine = cos_ref[...], sin_ref[...]
    sides = (nq // 2, nk // 2, nk // 2)
    lines_v[:8, :] = jnp.zeros((8, width), F32)
    lines_v[8:, :] = gain2_ref[...] * (1.0 / lax.axis_size("tensor"))
    small_v[: 2 * hd, :] = jnp.zeros((2 * hd, 128), F32)
    for k in range(2):
        small_v[2 * hd + 8 * k : 2 * hd + 8 * k + 8, :] = stat_ref[k] * (1.0 / lax.axis_size("tensor"))
    small_v[2 * hd + 16 : 2 * hd + 24, :] = jnp.zeros((8, 128), F32)
    valid_slots = jnp.int32(0)
    for s in range(seqs):
        valid_slots = valid_slots + jnp.clip(len_ref[s] - start, 0, span)
    count = valid_slots.astype(F32) * (1.0 / (1024.0 * lax.axis_size("tensor")))
    small_v[2 * hd + 24 : 2 * hd + 32, :] = jnp.broadcast_to(count, (8, 128))
    load_qkvw.wait()

    def fold_columns(values):
        return sum(values[:, k * 128 : (k + 1) * 128] for k in range(values.shape[1] // 128))

    def heads_rows(s, carry):
        exchange(s).wait_recv()
        low, high = join_positions(core, d_own[s].astype(F32), d_got[s].astype(F32))
        parts = [[], [], []]
        for side in (low, high):
            at = 0
            for kind, number in enumerate(sides):
                for _ in range(number):
                    parts[kind].append(side[at : at + hd])
                    at += hd
        done = []
        for h in range(nq + nk):
            kind = 0 if h < nq else 1
            g = parts[kind][h - kind * nq]
            a, b = g[: hd // 2], g[hd // 2 :]
            g = jnp.concatenate([a * cosine + b * sine, b * cosine - a * sine], axis=0)
            v = pre_v[s, h * hd : (h + 1) * hd, :]
            inv = lax.rsqrt(jnp.mean(v * v, axis=0, keepdims=True) + epsilon)
            hat = v * inv
            small_v[kind * hd : (kind + 1) * hd, :] += fold_columns(g * hat)
            gg = g * (qg_ref[...] if kind == 0 else kg_ref[...])
            done.append(inv * (gg - hat * jnp.mean(gg * hat, axis=0, keepdims=True)))
        done += parts[2]
        for h in range(nq + 2 * nk):
            pair = h % 2
            if pair == 0:
                two = jnp.concatenate([done[h], done[h + 1]], axis=0).T.astype(BF16)
                dpre_v[pl.ds(pl.multiple_of(s * span, span), span), h * hd : (h + 2) * hd] = two
        for copy in load_x(s):
            copy.wait()
        for m in range(4):
            rows = slice(m * share, (m + 1) * share)
            xs = [rows_v[k, rows, :].astype(F32) for k in range(2)]
            mean = sum(jnp.sum(x * x, axis=-1, keepdims=True) for x in xs) * (1.0 / width)
            inv = lax.rsqrt(mean + epsilon)
            dpre = dpre_v[pl.ds(pl.multiple_of(s * span + m * share, share), share), :]
            for k in range(2):
                part = dot_nt(dpre, qkvw_v[k])
                cut = slice(k * half, (k + 1) * half)
                first_v[s, m, :, cut] = part.astype(BF16)
                both = part * (xs[k] * inv)
                lines_v[:8, cut] += sum(both[8 * r : 8 * r + 8] for r in range(share // 8))

        @pl.when(s == 0)
        def _():
            for copy in load_x(1):
                copy.start()
            first_rings[0].begin()
            ffn_step(0, 2)

        @pl.when(s == seqs - 1)
        def _():
            first_rings[1].begin()
            ffn_step(1, 2)
            s_up.pass_on()

        return carry

    lax.fori_loop(0, seqs, heads_rows, 0)

    for k in range(4):
        blocks_o[k].wait_recv()
        cut = slice(k * size_o, (k + 1) * size_o)
        go_v[k] = (dot_tn(tok_v[...], act_v[:, cut]) + go_v[k].astype(F32)).astype(BF16)
    s_out.begin()
    load_n1 = load(0, n1_hbm, act_v)
    first_rings[0].step(1)
    load_n1.wait()
    blocks_q = [remote(sq_v.at[k], gq_v.at[k], qsend.at[k], qrecv.at[k], near_core) for k in range(4)]
    size_q = half // 4
    for k in range(4):
        cut = slice(half + k * size_q, half + (k + 1) * size_q)
        sq_v[k] = dot_tn(act_v[:, cut], dpre_v[...]).astype(BF16)
        blocks_q[k].start()
    for k in range(4):
        blocks_q[k].wait_recv()
        cut = slice(k * size_q, (k + 1) * size_q)
        gq_v[k] = (dot_tn(act_v[:, cut], dpre_v[...]) + gq_v[k].astype(F32)).astype(BF16)
    s_qkv.begin()

    piece = width // 8

    def place(tile, dst, s):
        copies = []
        for o in range(2):
            for k in range(4):
                b = near[k] * 2 + (core if o == 0 else 1 - core)
                cut = pl.ds(pl.multiple_of(b * piece, piece), piece)
                copies.append(
                    pltpu.make_async_copy(tile.at[:, pl.ds((o * 4 + k) * piece, piece)], dst.at[s, :, cut], outs_sem.at[o * 4 + k])
                )
        return copies

    def out_share(s):
        keep = pltpu.make_async_copy(hidden_hbm.at[piece_rows(s, rank), :], tile_v, tile_sem.at[0])
        keep.start()
        ffn_rings[s].arrived()
        read = ffn_rings[s].own(rank)
        keep.wait()

        def body(cut, first):
            ffn = slots_v[s, 2, cut, :].astype(F32) + read(cut).astype(F32)
            otile_v[cut, :] = (tile_v[cut, :] + ffn).astype(BF16)
            spot = start + rank * share + first + lax.broadcasted_iota(jnp.int32, (16, 1), 0)
            valid = (spot < len_ref[s]).astype(F32)
            small_v[2 * hd + 16 : 2 * hd + 24, :] += fold_lanes(valid * ffn * ffn)

        by_pieces(share, body)
        copies = place(otile_v, out_hbm, s)
        for copy in copies:
            copy.start()
        for copy in copies:
            copy.wait()

    def in_share(s):
        loads = [
            pltpu.make_async_copy(gh_hbm.at[piece_rows(s, rank), :], tile_v, tile_sem.at[0]),
            pltpu.make_async_copy(xr_hbm.at[s, pl.ds(pl.multiple_of(rank * share, share), share), :], xtile_v, tile_sem.at[1]),
        ]
        for copy in loads:
            copy.start()
        for copy in loads:
            copy.wait()
        first_rings[s].arrived()

        def body(cut, first):
            e = slots_v[seqs + s, 2, cut, :].astype(F32) + first_v[s, rank, cut, :].astype(F32)
            x = xtile_v[cut, :].astype(F32)
            inv = inverse_rms(x)
            hat = x * inv
            eg = e * gain_ref[...]
            itile_v[cut, :] = tile_v[cut, :] + inv * (eg - hat * jnp.mean(eg * hat, axis=-1, keepdims=True))

        by_pieces(share, body)
        copies = place(itile_v, gin_hbm, s)
        for copy in copies:
            copy.start()
        for copy in copies:
            copy.wait()

    def lump(n, src, dst, device):
        return remote(src, dst, smsend.at[n], smrecv.at[n], device)

    def small_hop(n, device, pairs):
        copies = [lump(2 * n, small_v, small_r.at[n], device)]
        for i, (src, dst, _) in enumerate(pairs):
            copies.append(remote(src, dst, smsend.at[2 * n + 1 + 10 * i], smrecv.at[2 * n + 1 + 10 * i], device))
        for copy in copies:
            copy.start()
        for copy in copies:
            copy.wait()
        small_v[...] += small_r[n]
        for _, dst, into in pairs:
            lines_v[:, into] += dst[...]

    def columns(k):
        return slice(k * piece, (k + 1) * piece)

    out_share(0)
    first_rings[1].step(1)
    s_down.pass_on()
    out_share(1)
    first_rings[0].step(2)
    s_out.pass_on()
    small_hop(0, near_core, [(lines_v.at[:, pl.ds(half, half)], lin1, slice(0, half))])
    s_gate.finish(stage_a, in_out(ggate_hbm), xstore.at[0])
    first_rings[1].step(2)
    s_qkv.pass_on()
    small_hop(
        1, near_x,
        [(lines_v.at[:, pl.ds(piece, piece)], lin2.at[0], columns(0)), (lines_v.at[:, pl.ds(3 * piece, piece)], lin2.at[1], columns(2))],
    )
    small_hop(2, near_y, [(lines_v.at[:, pl.ds(2 * piece, piece)], lin3, columns(0))])
    s_up.finish(stage_a, in_out(gup_hbm), xstore.at[1])
    in_share(0)
    s_down.finish(stage_b, in_out(gdown_hbm), xstore.at[2])
    small_hop(3, {"tensor": xor_one(rank)}, [(lines_v.at[:, pl.ds(0, piece)], lin4, columns(0))])
    s_out.finish(stage_o, in_out(gout_hbm), xstore.at[3])
    small_hop(4, z_far, [(lines_v.at[:, pl.ds(0, piece)], lin5, columns(0))])
    lines_out[...] = lines_v[:, :piece]
    small_out[...] = small_v[...]
    s_qkv.finish(stage_q, in_out(gqkv_hbm), xstore.at[4])
    in_share(1)
    for ring in ffn_rings + first_rings:
        ring.settle()
    for item in (s_gate, s_up, s_down, s_out, s_qkv):
        item.settle()
    for copy in blocks_o + blocks_q:
        copy.wait_send()
    for s in range(seqs):
        give(s).wait_send()
        exchange(s).wait_send()


def in_out(ref):
    h2 = ref.shape[0] // 2
    return lambda h: ref.at[pl.ds(h * h2, h2), :]


def backward(
    lengths, gb, gh, hidden_rows, ffn, xr, n1, tok, outw, qkvw, everything, att, inv, pre, dgate, dup, ddown,
    gain1, cosine, sine, qgain, kgain, stat, gain2_part, hd, nq, nk,
):
    seqs, span, width = xr.shape
    half = width // 2
    groups = nq // nk
    share = span // 4
    piece = width // 8
    hidden = dgate.shape[1]
    cols = qkvw.shape[2]
    feat = nq * hd
    block = min(256, span)
    any_space = pl.BlockSpec(memory_space=pl.ANY)
    vmem = pl.BlockSpec(memory_space=pltpu.VMEM)
    dma = pltpu.SemaphoreType.DMA
    hold = lambda *dims: pltpu.VMEM(dims, BF16)
    wide = lambda *dims: pltpu.VMEM(dims, F32)
    big = [
        shape((seqs, share, width), BF16), shape((seqs, share, width), F32),
        shape((piece, hidden), F32), shape((piece, hidden), F32), shape((hidden, piece), F32), shape((feat, piece), F32), shape((piece, cols), F32),
    ]
    big += [shape((piece, hidden), BF16)] * 4 + [shape((hidden, piece), BF16)] * 2
    small_rows = 2 * hd + 32
    small = [shape((16, piece), F32), shape((small_rows, 128), F32)]
    rows = everything.shape[1]
    scratch = [
        hold(seqs * span, width), hold(2, span, half), hold(2, half, cols), hold(seqs * span, feat), hold(*everything.shape), hold(*att.shape),
        wide(*inv.shape), wide(*pre.shape), wide(rows, 2 * span), hold(groups * hd, 2 * span),
        hold(seqs, feat // 2, span), hold(seqs, feat // 2, span), hold(seqs, feat // 2, span),
        hold(seqs, rows, span), hold(seqs, rows, span), hold(seqs, rows, span), hold(seqs * span, cols),
        hold(seqs, 4, share, width), hold(2 * seqs, 3, share, width), hold(seqs, share, width),
        hold(2, 2, piece // 2, hidden), hold(2, hidden // 2, piece), hold(3, piece // 2, hidden), hold(3, hidden // 2, piece),
        wide(piece // 2, hidden), wide(hidden // 2, piece),
        hold(4, feat, piece), hold(4, feat, piece), hold(2, feat // 2, piece), hold(2, feat, piece), hold(3, feat // 2, piece), wide(feat // 2, piece),
        hold(4, piece, cols), hold(4, piece, cols), hold(2, piece // 2, cols), hold(2, piece, cols), hold(3, piece // 2, cols), wide(piece // 2, cols),
        wide(share, width), hold(share, width), hold(share, width), wide(share, width),
        wide(16, width), wide(small_rows, 128), wide(16, half), wide(2, 16, piece), wide(16, piece), wide(16, piece), wide(16, piece), wide(5, small_rows, 128),
        dma((10,)), dma((2 * seqs, 3)), dma((2 * seqs, 3)), dma((seqs,)), dma((5, 6)), dma((5, 6)), dma((5, 3)), dma((5,)),
        dma((2, seqs)), dma((2, seqs)), dma((4,)), dma((4,)), dma((4,)), dma((4,)), dma((2,)), dma((8,)), dma((20,)), dma((20,)),
    ]
    tokens = seqs * span
    return pl.pallas_call(
        functools.partial(backward_kernel, hd, nq, nk, block),
        in_specs=[SMEM] + [any_space] * 16 + [vmem] * 7,
        out_specs=[any_space] * len(big) + [vmem] * 2,
        out_shape=big + small,
        scratch_shapes=scratch,
        compiler_params=pltpu.CompilerParams(vmem_limit_bytes=VMEM_MOST, collective_id=3, has_side_effects=True),
        cost_estimate=cost(4 * tokens * width * (cols + feat), 60 * tokens * width),
        name="attention_backward",
    )(
        lengths, gb, gh, hidden_rows, ffn, xr, n1, tok, outw, qkvw, everything, att, inv, pre, dgate, dup, ddown,
        gain1, cosine, sine, qgain, kgain, stat, gain2_part,
    )


def per_device_general(
    inputs,
    cotangent,
    lengths,
    w_query,
    key_projection_weight,
    value_projection_weight,
    w_output,
    w_gate,
    w_up,
    w_down,
    attn_gain,
    ffn_gain,
    query_gain,
    key_gain,
):
    seqs, span, width = inputs.shape
    hd = query_gain.shape[0]
    nq = w_query.shape[1] // hd
    nk = key_projection_weight.shape[1] // hd
    groups = nq // nk
    dp = lax.axis_size("dp")
    tensor = lax.axis_size("tensor")
    core = lax.axis_index("context")
    rank = lax.axis_index("tensor")
    chunks = 2
    rows = span // chunks
    share = span // tensor
    lengths = lengths.astype(jnp.int32)
    start = (core * span).astype(jnp.int32)
    core1 = core.astype(jnp.int32).reshape(1)
    ids = block_order(dp, core)
    order = 2 * dp if (width // (2 * dp)) % 128 == 0 else 1

    positions = start + jnp.arange(span, dtype=jnp.int32)
    freqs = rope_base ** (-(jnp.arange(hd // 2, dtype=F32) * (2.0 / hd)))
    angles = freqs[:, None] * positions.astype(F32)[None, :]
    cosine, sine = jnp.cos(angles), jnp.sin(angles)
    qgain = query_gain.astype(F32).reshape(hd, 1)
    kgain = key_gain.astype(F32).reshape(hd, 1)

    w_qkv = jnp.concatenate([w_query, key_projection_weight, value_projection_weight], axis=1)
    saved = []
    gains = gather_blocks(jnp.stack([attn_gain, ffn_gain]), 1)
    gains = jnp.concatenate([gains[0], gains[1]], axis=1).astype(F32)
    gain1, gain2 = gains[0:1], gains[1:2]
    qkv = gather_blocks(w_qkv, 0)
    out_w = gather_blocks(w_output, 1)
    gate = gather_blocks(w_gate, 0)
    up = gather_blocks(w_up, 0)
    down = gather_blocks(w_down, 1)

    scal = jnp.concatenate([lengths, start.reshape(1), ids])
    x_in, cot_in = inputs, cotangent
    if order == 1:
        x_in, cot_in = to_relative(x_in, dp, core), to_relative(cot_in, dp, core)
    xr, n1, gf = begin(x_in, cot_in, gain1, scal, order)

    parts, tok = [], []
    for s in range(seqs):
        pre, own, oth = heads(n1, s, qkv, cosine, sine, qgain, kgain, core1, hd, nq, nk)
        seq_scal = jnp.stack([lengths[s], core.astype(jnp.int32)])
        everything, att, inv, mine, theirs = attend(seq_scal, own, over_core(oth), groups)
        branched = branch(mine, over_core(theirs), out_w, core1, chunks)
        saved.append((pre, everything, att, inv, seq_scal))
        tok.append(jnp.swapaxes(branched[0], 0, 1))
        parts.append(branched[1:])
    tok = jnp.concatenate(tok, axis=0)

    stats = jnp.zeros((2,), F32)
    hidden_all, n2_all = [], []
    for s in range(seqs):
        for k in range(chunks):
            terms = [lax.psum(parts[s][k], "tensor")]
            place = jnp.stack([lengths[s], start + k * rows])
            hidden, n2, stat = second_norm(place, xr, s, k, gain2, terms)
            hidden_all.append(hidden)
            n2_all.append(n2)
            stats = stats + stat[:2, 0]
    hidden_all, n2_all = jnp.concatenate(hidden_all), jnp.concatenate(n2_all)

    ffn_squares = jnp.zeros((), F32)
    out_shares = []

    def piece_of(arrays):
        per = arrays[0].shape[0] // share

        def piece(k):
            found = lax.dynamic_slice_in_dim(arrays[0], jnp.minimum(k, per - 1) * share, share, 0)
            for m in range(1, len(arrays)):
                here = lax.dynamic_slice_in_dim(arrays[m], jnp.clip(k - m * per, 0, per - 1) * share, share, 0)
                found = jnp.where(k >= m * per, here, found)
            return found

        return piece

    def share_scalars(s):
        head = jnp.stack([rank.astype(jnp.int32), lengths[s], start + rank.astype(jnp.int32) * share, jnp.int32(tensor)])
        return jnp.concatenate([head, ids])

    def flat(nested):
        return [item for inner_list in nested for item in inner_list]

    def slices(array, count):
        size = array.shape[0] // count
        return [array[i * size : (i + 1) * size] for i in range(count)]

    def reduced(lefts, rights, axis):
        oth = weight_grad(lefts, rights, 1, axis)
        own = weight_grad(lefts, rights, 0, axis, over_core(oth))
        return scatter_blocks(own, axis)

    inner, gg, gu, ffn, gn = [[[None] * chunks for _ in range(seqs)] for _ in range(5)]
    for s in range(seqs):
        for k in range(chunks):
            inner[s][k], gg[s][k], gu[s][k], ffn[s][k], gn[s][k] = feed(
                n2_all, s * chunks + k, rows, gf, s, k, gate, up, down
            )
    gain2_grad = jnp.zeros((1, width), F32)
    gb, gh = [[[None] * chunks for _ in range(seqs)] for _ in range(2)]
    for s in range(seqs):
        for k in range(chunks):
            terms = [lax.psum(gn[s][k], "tensor")]
            gb[s][k], gh[s][k], gain_part = second_back(hidden_all, s * chunks + k, gf, s, k, gain2, terms)
            gain2_grad = gain2_grad + gain_part
    gf_list = slices(gf.reshape(seqs * span, width), seqs * chunks)
    n2_list = slices(n2_all, seqs * chunks)
    grad_w_down = reduced(flat(inner), gf_list, 1)
    grad_w_gate = reduced(n2_list, flat(gg), 0)
    grad_w_up = reduced(n2_list, flat(gu), 0)
    for s in range(seqs):
        got = ring_scatter(piece_of(ffn[s]), tensor, rank)
        halves = [hidden_all[(s * chunks + k) * rows : (s * chunks + k + 1) * rows] for k in range(chunks)]
        out, stat = output_share(share_scalars(s), got, ffn[s], halves, order)
        out_shares.append(out)
        ffn_squares = ffn_squares + stat[0, 0]

    gain1_grad = jnp.zeros((1, width), F32)
    head_gain = jnp.zeros((2 * hd,), F32)
    dpres, in_shares = [], []
    for s in range(seqs):
        pre, everything, att, inv, seq_scal = saved[s]
        da_own, da_oth = branch_back(gb[s], out_w, core1)
        d_own, d_oth = attend_back(seq_scal, everything, att, inv, da_own, over_core(da_oth), groups)
        dpre, first, gain_part, hg = heads_back(
            d_own, over_core(d_oth), pre, cosine, sine, qgain, kgain, xr, s, qkv, core1, hd, nq, nk
        )
        gain1_grad = gain1_grad + gain_part
        head_gain = head_gain + hg[:, 0]
        dpres.append(dpre)
        got = ring_scatter(piece_of([first]), tensor, rank)
        in_shares.append(input_share(share_scalars(s), got, first, gh[s], xr, s, gain1, order))

    att_list = [tok[i * rows : (i + 1) * rows] for i in range(seqs * chunks)]
    grad_w_output = reduced(att_list, flat(gb), 1)
    grad_qkv = reduced([n1[s] for s in range(seqs)], dpres, 0)
    nqc, nkc = nq * hd, nk * hd
    grad_w_query = grad_qkv[:, :nqc]
    grad_w_key = grad_qkv[:, nqc : nqc + nkc]
    grad_w_value = grad_qkv[:, nqc + nkc :]

    gain2_grad = gain2_grad / tensor
    counts = jnp.sum(jnp.clip(lengths - start, 0, span)).astype(F32) / tensor
    small = jnp.concatenate([head_gain, stats / tensor, ffn_squares.reshape(1), counts.reshape(1)])
    small = jnp.pad(small, (0, (-small.shape[0]) % 128)).reshape(1, -1)
    lines = jnp.concatenate([gain1_grad, gain2_grad], axis=0)
    piece = width // (2 * dp)
    lines = to_absolute(lines, dp, core)
    lines, small = lax.psum((lines, small), ("dp", "context", "tensor"))
    lines = lax.dynamic_slice_in_dim(lines, lax.axis_index(("dp", "context")) * piece, piece, 1)
    small = small[0]
    rms_values = jnp.sqrt(small[2 * hd : 2 * hd + 3] / (small[2 * hd + 3] * width))

    output = jnp.stack(out_shares)
    grad_inputs = jnp.stack(in_shares)
    if order == 1:
        output, grad_inputs = to_absolute(output, dp, core), to_absolute(grad_inputs, dp, core)
    return (
        output,
        grad_inputs,
        grad_w_query,
        grad_w_key,
        grad_w_value,
        grad_w_output,
        grad_w_gate,
        grad_w_up,
        grad_w_down,
        lines[0],
        lines[1],
        small[:hd],
        small[hd : 2 * hd],
        rms_values,
    )


def per_device_square(
    inputs,
    cotangent,
    lengths,
    w_query,
    key_projection_weight,
    value_projection_weight,
    w_output,
    w_gate,
    w_up,
    w_down,
    attn_gain,
    ffn_gain,
    query_gain,
    key_gain,
):
    seqs, span, width = inputs.shape
    hd = query_gain.shape[0]
    nq = w_query.shape[1] // hd
    nk = key_projection_weight.shape[1] // hd
    lengths = lengths.astype(jnp.int32)
    positions = lax.axis_index("context") * span + jnp.arange(span, dtype=jnp.int32)
    freqs = rope_base ** (-(jnp.arange(hd // 2, dtype=F32) * (2.0 / hd)))
    angles = freqs[:, None] * positions.astype(F32)[None, :]
    cosine, sine = jnp.cos(angles), jnp.sin(angles)
    qgain = query_gain.astype(F32).reshape(hd, 1)
    kgain = key_gain.astype(F32).reshape(hd, 1)
    w_qkv = jnp.concatenate([w_query, key_projection_weight, value_projection_weight], axis=1)
    gains = jnp.pad(jnp.stack([attn_gain, ffn_gain]), ((0, 14), (0, 0)))

    (xr, n1, gf, qkv, out_w, gate, up, down, hidden, n2, gains, pre, everything, att, inv, tok, stat) = forward(
        lengths, inputs, cotangent, w_qkv, w_output, w_gate, w_up, w_down, gains, cosine, sine, qgain, kgain, hd, nq, nk
    )
    gains = jnp.swapaxes(gains[:, :2], 0, 1).reshape(2, width).astype(F32)
    tokens = seqs * span
    ffn, gb, gh, d_gate, d_up, d_down, gain2_part = feed_both(
        n2, gf.reshape(tokens, width), gate, up, down, hidden, gains[1:2]
    )
    results = backward(
        lengths, gb, gh, hidden, ffn, xr, n1.reshape(tokens, width), tok.reshape(tokens, nq * hd), out_w, qkv,
        everything, att, inv, pre, d_gate, d_up, d_down, gains[0:1], cosine, sine, qgain, kgain, stat, gain2_part, hd, nq, nk,
    )
    output, grad_inputs, grad_gate, grad_up, grad_down, grad_out, grad_qkv = results[:7]
    lines, small = results[-2:]
    nqc, nkc = nq * hd, nk * hd
    totals = jnp.sum(small[2 * hd :].reshape(4, -1), axis=1)
    return (
        output,
        grad_inputs,
        grad_qkv[:, :nqc],
        grad_qkv[:, nqc : nqc + nkc],
        grad_qkv[:, nqc + nkc :],
        grad_out,
        grad_gate,
        grad_up,
        grad_down,
        jnp.sum(lines[:8], axis=0),
        jnp.sum(lines[8:], axis=0),
        jnp.sum(small[:hd], axis=1),
        jnp.sum(small[hd : 2 * hd], axis=1),
        jnp.sqrt(totals[:3] / (totals[3] * width)),
    )


def per_device(*args):
    inputs, w_query = args[0], args[3]
    seqs, span, width = inputs.shape
    square = lax.axis_size("dp") == 4 and lax.axis_size("tensor") == 4 and lax.axis_size("context") == 2
    if square and width % 2048 == 0 and span % 512 == 0 and seqs == 2 and w_query.shape[1] == span:
        return per_device_square(*args)
    return per_device_general(*args)


def solution(mesh):
    both = ("dp", "context")
    rows = P(both, "tensor")
    cols = P("tensor", both)
    shares = P("dp", ("context", "tensor"), None)
    acts = P("dp", "context", None)
    return jax.shard_map(
        per_device,
        mesh=mesh,
        in_specs=(acts, acts, P("dp"), rows, rows, rows, cols, rows, rows, cols, P(both), P(both), P(), P()),
        out_specs=(shares, shares, rows, rows, rows, cols, rows, rows, cols, P(both), P(both), P(), P(), P()),
        check_vma=False,
    )
```

```python
import functools
import math

import jax
import jax.numpy as jnp
from jax import lax
from jax.experimental import pallas as pl
from jax.experimental.pallas import tpu as pltpu
from jax.sharding import PartitionSpec as P

F32 = jnp.float32
BF16 = jnp.bfloat16
epsilon = 1e-05
rope_base = 1000000.0
log2e = 1.4426950408889634
VMEM_BYTES = 60 * 1024 * 1024
VMEM_MOST = 63 * 1024 * 1024
PARAMS = pltpu.CompilerParams(vmem_limit_bytes=VMEM_BYTES)
SMEM = pl.BlockSpec(memory_space=pltpu.SMEM)
SWAP = ((0, 1), (1, 0))


def shape(dims, dtype):
    return jax.ShapeDtypeStruct(tuple(dims), dtype)


def cost(flops, size, exps=0):
    return pl.CostEstimate(flops=int(flops), bytes_accessed=int(size), transcendentals=int(exps))


def dot_nn(a, b):
    return lax.dot_general(a, b, (((1,), (0,)), ((), ())), preferred_element_type=F32)


def dot_nt(a, b):
    return lax.dot_general(a, b, (((1,), (1,)), ((), ())), preferred_element_type=F32)


def dot_tn(a, b):
    return lax.dot_general(a, b, (((0,), (0,)), ((), ())), preferred_element_type=F32)


def inverse_rms(values):
    return lax.rsqrt(jnp.mean(values * values, axis=-1, keepdims=True) + epsilon)


def block_order(dp, core):
    return jnp.stack([jnp.int32(k) * 2 + (core ^ o) for o in range(2) for k in range(dp)]).astype(jnp.int32)


def to_relative(values, dp, core):
    lead = values.shape[:-1]
    parts = values.reshape(lead + (dp, 2, -1))
    parts = jnp.where(core == 0, parts, parts[..., ::-1, :])
    return jnp.swapaxes(parts, -3, -2).reshape(values.shape)


def to_absolute(values, dp, core):
    lead = values.shape[:-1]
    parts = jnp.swapaxes(values.reshape(lead + (2, dp, -1)), -3, -2)
    return jnp.where(core == 0, parts, parts[..., ::-1, :]).reshape(values.shape)


def over_core(value):
    return lax.ppermute(value, "context", SWAP)


def gather_blocks(weight, axis):
    own = lax.all_gather(weight, "dp", axis=axis, tiled=True)
    return jnp.stack([own, over_core(own)])


def scatter_blocks(total, axis):
    return lax.psum_scatter(total, "dp", scatter_dimension=axis, tiled=True).astype(F32)


def ring_scatter(piece, tensor, rank):
    ring = [(i, (i + 1) % tensor) for i in range(tensor)]
    moving = piece((rank + tensor - 1) % tensor)
    for step in range(1, tensor):
        moving = lax.ppermute(moving, "tensor", ring)
        if step < tensor - 1:
            moving = (moving.astype(F32) + piece((rank + tensor - 1 - step) % tensor).astype(F32)).astype(BF16)
    return moving


def begin_kernel(order, x_ref, cot_ref, gain_ref, scal_ref, xr_ref, n1_ref, gf_ref):
    seq, tile = pl.program_id(0), pl.program_id(1)
    rows, width = x_ref.shape[1:]
    seqs = pl.num_programs(0)
    place = scal_ref[seqs] + tile * rows + lax.broadcasted_iota(jnp.int32, (rows, 1), 0)
    valid = (place < scal_ref[seq]).astype(F32)
    x = x_ref[0].astype(F32)
    inv = inverse_rms(x)
    piece = width // order
    for k in range(order):
        src = pl.ds(pl.multiple_of(scal_ref[seqs + 1 + k] * piece, piece), piece) if order > 1 else slice(0, width)
        dst = slice(k * piece, (k + 1) * piece)
        part = x_ref[0, :, src]
        xr_ref[0, :, dst] = part
        n1_ref[0, :, dst] = (part.astype(F32) * inv * gain_ref[:, dst]).astype(BF16)
        gf_ref[0, :, dst] = (cot_ref[0, :, src].astype(F32) * valid).astype(BF16)


def begin(x, cot, gain, scalars, order):
    seqs, span, width = x.shape
    rows = min(256, span)
    spec = pl.BlockSpec((1, rows, width), lambda s, i: (s, i, 0))
    return pl.pallas_call(
        functools.partial(begin_kernel, order),
        grid=(seqs, span // rows),
        in_specs=[spec, spec, pl.BlockSpec((1, width), lambda s, i: (0, 0)), SMEM],
        out_specs=[spec] * 3,
        out_shape=[shape(x.shape, BF16)] * 3,
        compiler_params=PARAMS,
        cost_estimate=cost(8 * x.size, 10 * x.size),
        name="first_norm",
    )(x, cot, gain, scalars)


def heads_kernel(hd, nq, nk, n1_ref, w_ref, cos_ref, sin_ref, qg_ref, kg_ref, core_ref, pre_ref, own_ref, oth_ref):
    half = w_ref.shape[1]
    x = n1_ref[0]
    flat = dot_nn(x[:, :half], w_ref[0]) + dot_nn(x[:, half:], w_ref[1])
    turned = flat.T
    span = turned.shape[1]
    normed = turned[: (nq + nk) * hd]
    pre_ref[...] = normed
    core = core_ref[0]
    cosine, sine = cos_ref[...], sin_ref[...]
    done = []
    for h in range(nq + nk):
        v = normed[h * hd : (h + 1) * hd]
        inv = lax.rsqrt(jnp.mean(v * v, axis=0, keepdims=True) + epsilon)
        v = v * inv * (qg_ref[...] if h < nq else kg_ref[...])
        a, b = v[: hd // 2], v[hd // 2 :]
        done.append(jnp.concatenate([a * cosine - b * sine, b * cosine + a * sine], axis=0))
    for h in range(nk):
        lo = (nq + nk + h) * hd
        done.append(turned[lo : lo + hd])
    parts = [[], []]
    for start, count in ((0, nq), (nq, nk), (nq + nk, nk)):
        for side in range(2):
            parts[side] += done[start + side * count // 2 : start + (side + 1) * count // 2]
    low = jnp.concatenate(parts[0], axis=0)
    high = jnp.concatenate(parts[1], axis=0)
    first = core == 0
    own_ref[...] = jnp.where(first, low, high).astype(BF16)
    oth_ref[...] = jnp.where(first, high, low).astype(BF16)


def heads(n1, seq, weight, cosine, sine, qgain, kgain, core, hd, nq, nk):
    span, width = n1.shape[1:]
    sides = (nq + 2 * nk) * hd // 2
    full = pl.BlockSpec(memory_space=pltpu.VMEM)
    whole = lambda a: pl.BlockSpec(a.shape, lambda i: (0,) * a.ndim)
    outs = [shape(((nq + nk) * hd, span), F32), shape((sides, span), BF16), shape((sides, span), BF16)]
    return pl.pallas_call(
        functools.partial(heads_kernel, hd, nq, nk),
        grid=(1,),
        in_specs=[pl.BlockSpec((1, span, width), lambda i: (seq, 0, 0))]
        + [whole(a) for a in (weight, cosine, sine, qgain, kgain)]
        + [SMEM],
        out_specs=[whole(o) for o in outs],
        out_shape=outs,
        compiler_params=PARAMS,
        cost_estimate=cost(2 * span * width * weight.shape[2], 2 * span * width + 2 * weight.size),
        name="query_key_value",
    )(n1, weight, cosine, sine, qgain, kgain, core)


def join_positions(core, own, oth):
    first = core == 0
    return jnp.where(first, own, oth), jnp.where(first, oth, own)


def attend_kernel(block, groups, scal_ref, own_ref, got_ref, all_ref, att_ref, inv_ref, ao_ref, ax_ref):
    span = own_ref.shape[1]
    hd = own_ref.shape[0] // (groups + 2)
    length, core = scal_ref[0], scal_ref[1]
    low, high = join_positions(core, own_ref[...], got_ref[...])
    all_ref[:, :span] = low
    all_ref[:, span:] = high
    scale = log2e / math.sqrt(hd)
    krow = lax.broadcasted_iota(jnp.int32, (block, groups * block), 0)
    qcol = lax.broadcasted_iota(jnp.int32, (block, groups * block), 1) % block
    base = groups * hd
    for i in range(2 * span // block):
        cut = slice(i * block, (i + 1) * block)
        q = jnp.concatenate([all_ref[g * hd : (g + 1) * hd, cut] for g in range(groups)], axis=1)
        acc = jnp.zeros((hd, groups * block), F32)
        total = jnp.zeros((1, groups * block), F32)
        for j in range(i + 1):
            kcut = slice(j * block, (j + 1) * block)
            s = dot_tn(all_ref[base : base + hd, kcut], q) * scale
            ok = (krow + j * block) < length
            if j == i:
                ok = ok & (krow <= qcol)
            e = jnp.where(ok, jnp.exp2(s), 0.0)
            total = total + jnp.sum(e, axis=0, keepdims=True)
            acc = acc + dot_nn(all_ref[base + hd : base + 2 * hd, kcut], e.astype(BF16))
        inv = 1.0 / total
        att = (acc * inv).astype(BF16)
        for g in range(groups):
            att_ref[g * hd : (g + 1) * hd, cut] = att[:, g * block : (g + 1) * block]
            inv_ref[g : g + 1, cut] = inv[:, g * block : (g + 1) * block]
    mine, theirs = join_positions(core, att_ref[:, :span], att_ref[:, span:])
    ao_ref[...] = mine
    ax_ref[...] = theirs


def attend(scalars, own, got, groups):
    rows, span = own.shape
    hd = rows // (groups + 2)
    block = min(256, span)
    full = pl.BlockSpec(memory_space=pltpu.VMEM)
    return pl.pallas_call(
        functools.partial(attend_kernel, block, groups),
        in_specs=[SMEM, full, full],
        out_specs=[full] * 5,
        out_shape=[
            shape((rows, 2 * span), BF16),
            shape((groups * hd, 2 * span), BF16),
            shape((groups, 2 * span), F32),
            shape((groups * hd, span), BF16),
            shape((groups * hd, span), BF16),
        ],
        compiler_params=PARAMS,
        cost_estimate=cost(60 * groups * hd * span * span, 12 * rows * span, 4 * groups * span * span),
        name="attend_forward",
    )(scalars, own, got)


def branch_kernel(own_ref, got_ref, w_ref, core_ref, att_ref, *outs):
    half = w_ref.shape[2]
    low, high = join_positions(core_ref[0], own_ref[...], got_ref[...])
    att = jnp.concatenate([low, high], axis=0)
    att_ref[...] = att
    rows = outs[0].shape[0]
    for k, out in enumerate(outs):
        part = att[:, k * rows : (k + 1) * rows]
        out[:, :half] = dot_tn(part, w_ref[0]).astype(BF16)
        out[:, half:] = dot_tn(part, w_ref[1]).astype(BF16)


def branch(own, got, weight, core, chunks):
    rows, span = own.shape
    width = 2 * weight.shape[2]
    full = pl.BlockSpec(memory_space=pltpu.VMEM)
    return pl.pallas_call(
        branch_kernel,
        in_specs=[full] * 3 + [SMEM],
        out_specs=[full] * (1 + chunks),
        out_shape=[shape((2 * rows, span), BF16)] + [shape((span // chunks, width), BF16)] * chunks,
        compiler_params=PARAMS,
        cost_estimate=cost(4 * rows * span * width, 4 * rows * width + 2 * span * width),
        name="attention_branch",
    )(own, got, weight, core)


def second_norm_kernel(terms, scal_ref, x_ref, gain_ref, *refs):
    term_refs, (hidden_ref, n2_ref, stat_ref) = refs[:terms], refs[terms:]
    rows = hidden_ref.shape[0]
    branch_sum = term_refs[0][...].astype(F32)
    for ref in term_refs[1:]:
        branch_sum = branch_sum + ref[...].astype(F32)
    resid = x_ref[0].astype(F32)
    hidden = resid + branch_sum
    hidden_ref[...] = hidden
    n2_ref[...] = (hidden * inverse_rms(hidden) * gain_ref[...]).astype(BF16)
    place = scal_ref[1] + lax.broadcasted_iota(jnp.int32, (rows, 1), 0)
    valid = (place < scal_ref[0]).astype(F32)
    first = jnp.sum(valid * resid * resid, keepdims=True)
    second = jnp.sum(valid * branch_sum * branch_sum, keepdims=True)
    line = lax.broadcasted_iota(jnp.int32, (8, 128), 0)
    stat_ref[...] = jnp.where(line == 0, first, second)


def second_norm(scalars, xr, seq, part, gain, terms):
    rows, width = terms[0].shape
    flat = pl.BlockSpec((rows, width), lambda i: (0, 0))
    return pl.pallas_call(
        functools.partial(second_norm_kernel, len(terms)),
        grid=(1,),
        in_specs=[SMEM, pl.BlockSpec((1, rows, width), lambda i: (seq, part, 0)), pl.BlockSpec((1, width), lambda i: (0, 0))]
        + [flat] * len(terms),
        out_specs=[flat, flat, pl.BlockSpec((8, 128), lambda i: (0, 0))],
        out_shape=[shape((rows, width), F32), shape((rows, width), BF16), shape((8, 128), F32)],
        compiler_params=PARAMS,
        cost_estimate=cost(20 * rows * width, (8 + 2 * len(terms)) * rows * width),
        name="second_norm",
    )(scalars, xr, gain, *terms)


def feed_kernel(n_ref, g_ref, wgo, wgx, wuo, wux, wdo, wdx, inner_ref, gg_ref, gu_ref, ffn_ref, gn_ref, facc, gacc):
    step = pl.program_id(0)
    half = wgo.shape[0]
    no, nx = n_ref[:, :half], n_ref[:, half:]
    gate = dot_nn(no, wgo[...]) + dot_nn(nx, wgx[...])
    up = dot_nn(no, wuo[...]) + dot_nn(nx, wux[...])
    gi = dot_nt(g_ref[0, :, :half], wdo[...]) + dot_nt(g_ref[0, :, half:], wdx[...])
    sig = jax.nn.sigmoid(gate)
    silu = gate * sig
    inner = (silu * up).astype(BF16)
    gg = (gi * up * sig * (1.0 + gate * (1.0 - sig))).astype(BF16)
    gu = (gi * silu).astype(BF16)
    inner_ref[...] = inner
    gg_ref[...] = gg
    gu_ref[...] = gu

    @pl.when(step == 0)
    def _():
        facc[...] = jnp.zeros_like(facc)
        gacc[...] = jnp.zeros_like(gacc)

    facc[:, :half] += dot_nn(inner, wdo[...])
    facc[:, half:] += dot_nn(inner, wdx[...])
    gacc[:, :half] += dot_nt(gg, wgo[...]) + dot_nt(gu, wuo[...])
    gacc[:, half:] += dot_nt(gg, wgx[...]) + dot_nt(gu, wux[...])

    @pl.when(step == pl.num_programs(0) - 1)
    def _():
        ffn_ref[...] = facc[...].astype(BF16)
        gn_ref[...] = gacc[...].astype(BF16)


def feed(n2, chunk, rows, gf, seq, part, gate, up, down):
    width = n2.shape[1]
    _, half, hidden = gate.shape
    hb = min(512, hidden)
    row = [pl.BlockSpec((None, half, hb), lambda h, side=side: (side, 0, h)) for side in range(2)]
    col = [pl.BlockSpec((None, hb, half), lambda h, side=side: (side, h, 0)) for side in range(2)]
    whole = pl.BlockSpec((rows, width), lambda h: (0, 0))
    tile = pl.BlockSpec((rows, hb), lambda h: (0, h))
    return pl.pallas_call(
        feed_kernel,
        grid=(hidden // hb,),
        in_specs=[pl.BlockSpec((rows, width), lambda h: (chunk, 0)), pl.BlockSpec((1, rows, width), lambda h: (seq, part, 0))] + row + row + col,
        out_specs=[tile, tile, tile, whole, whole],
        out_shape=[shape((rows, hidden), BF16)] * 3 + [shape((rows, width), BF16)] * 2,
        scratch_shapes=[pltpu.VMEM((rows, width), F32), pltpu.VMEM((rows, width), F32)],
        compiler_params=PARAMS,
        cost_estimate=cost(12 * rows * width * hidden, 12 * half * hidden + 14 * rows * width, rows * hidden),
        name="feed_forward",
    )(n2, gf, gate, gate, up, up, down, down)


def second_back_kernel(terms, hidden_ref, gf_ref, gain_ref, *refs):
    term_refs, (gb_ref, gh_ref, gain_out) = refs[:terms], refs[terms:]
    e = term_refs[0][...].astype(F32)
    for ref in term_refs[1:]:
        e = e + ref[...].astype(F32)
    hidden = hidden_ref[...]
    inv = inverse_rms(hidden)
    hat = hidden * inv
    eg = e * gain_ref[...]
    gh = gf_ref[0].astype(F32) + inv * (eg - hat * jnp.mean(eg * hat, axis=-1, keepdims=True))
    gh_ref[...] = gh
    gb_ref[...] = gh.astype(BF16)
    gain_out[...] = jnp.sum(e * hat, axis=0, keepdims=True)


def second_back(hidden, chunk, gf, seq, part, gain, terms):
    rows, width = terms[0].shape
    flat = pl.BlockSpec((rows, width), lambda i: (0, 0))
    line = pl.BlockSpec((1, width), lambda i: (0, 0))
    return pl.pallas_call(
        functools.partial(second_back_kernel, len(terms)),
        grid=(1,),
        in_specs=[pl.BlockSpec((rows, width), lambda i: (chunk, 0)), pl.BlockSpec((1, rows, width), lambda i: (seq, part, 0)), line]
        + [flat] * len(terms),
        out_specs=[flat, flat, line],
        out_shape=[shape((rows, width), BF16), shape((rows, width), F32), shape((1, width), F32)],
        compiler_params=PARAMS,
        cost_estimate=cost(20 * rows * width, (12 + 2 * len(terms)) * rows * width),
        name="second_norm_back",
    )(hidden, gf, gain, *terms)


def branch_back_kernel(chunks, *refs):
    gb_refs, (w_ref, core_ref, own_ref, oth_ref) = refs[:chunks], refs[chunks:]
    half = w_ref.shape[2]
    rows = gb_refs[0].shape[0]
    heads_half = own_ref.shape[0]
    first = core_ref[0] == 0
    for k, ref in enumerate(gb_refs):
        da = dot_nt(w_ref[0], ref[:, :half]) + dot_nt(w_ref[1], ref[:, half:])
        da = da.astype(BF16)
        low, high = da[:heads_half], da[heads_half:]
        cut = slice(k * rows, (k + 1) * rows)
        own_ref[:, cut] = jnp.where(first, low, high)
        oth_ref[:, cut] = jnp.where(first, high, low)


def branch_back(gbs, weight, core):
    chunks = len(gbs)
    rows, width = gbs[0].shape
    dim = weight.shape[1]
    full = pl.BlockSpec(memory_space=pltpu.VMEM)
    return pl.pallas_call(
        functools.partial(branch_back_kernel, chunks),
        in_specs=[full] * (chunks + 1) + [SMEM],
        out_specs=[full] * 2,
        out_shape=[shape((dim // 2, chunks * rows), BF16)] * 2,
        compiler_params=PARAMS,
        cost_estimate=cost(2 * dim * chunks * rows * width, 2 * dim * width + 2 * chunks * rows * width),
        name="attention_branch_back",
    )(*gbs, weight, core)


def attend_back_kernel(block, groups, scal_ref, all_ref, att_ref, inv_ref, own_ref, got_ref, out_own, out_oth, da_all, grads):
    span = own_ref.shape[1]
    hd = all_ref.shape[0] // (groups + 2)
    length, core = scal_ref[0], scal_ref[1]
    low, high = join_positions(core, own_ref[...], got_ref[...])
    da_all[:, :span] = low
    da_all[:, span:] = high
    scale = log2e / math.sqrt(hd)
    back = 1.0 / math.sqrt(hd)
    krow = lax.broadcasted_iota(jnp.int32, (block, groups * block), 0)
    qcol = lax.broadcasted_iota(jnp.int32, (block, groups * block), 1) % block
    base = groups * hd
    grads[base:, :] = jnp.zeros((2 * hd, 2 * span), F32)
    for i in range(2 * span // block):
        cut = slice(i * block, (i + 1) * block)

        def rows(ref):
            return jnp.concatenate([ref[g * hd : (g + 1) * hd, cut] for g in range(groups)], axis=1)

        q = rows(all_ref)
        da = rows(da_all)
        inv = jnp.concatenate([inv_ref[g : g + 1, cut] for g in range(groups)], axis=1)
        delta = jnp.sum(rows(att_ref).astype(F32) * da.astype(F32), axis=0, keepdims=True)
        dq = jnp.zeros((hd, groups * block), F32)
        for j in range(i + 1):
            kcut = slice(j * block, (j + 1) * block)
            key = all_ref[base : base + hd, kcut]
            s = dot_tn(key, q) * scale
            ok = (krow + j * block) < length
            if j == i:
                ok = ok & (krow <= qcol)
            p = jnp.where(ok, jnp.exp2(s) * inv, 0.0)
            dp = dot_tn(all_ref[base + hd : base + 2 * hd, kcut], da)
            ds = (p * (dp - delta)).astype(BF16)
            dq = dq + dot_nn(key, ds)
            grads[base : base + hd, kcut] += dot_nt(q, ds) * back
            grads[base + hd : base + 2 * hd, kcut] += dot_nt(da, p.astype(BF16))
        dq = dq * back
        for g in range(groups):
            grads[g * hd : (g + 1) * hd, cut] = dq[:, g * block : (g + 1) * block]
    mine, theirs = join_positions(core, grads[:, :span], grads[:, span:])
    out_own[...] = mine.astype(BF16)
    out_oth[...] = theirs.astype(BF16)


def attend_back(scalars, everything, att, inv, own, got, groups):
    rows, slots = everything.shape
    span = slots // 2
    block = min(256, span)
    full = pl.BlockSpec(memory_space=pltpu.VMEM)
    return pl.pallas_call(
        functools.partial(attend_back_kernel, block, groups),
        in_specs=[SMEM] + [full] * 5,
        out_specs=[full] * 2,
        out_shape=[shape((rows, span), BF16)] * 2,
        scratch_shapes=[pltpu.VMEM(att.shape, BF16), pltpu.VMEM((rows, slots), F32)],
        compiler_params=PARAMS,
        cost_estimate=cost(30 * att.shape[0] * slots * slots, 12 * rows * slots, groups * slots * slots),
        name="attend_backward",
    )(scalars, everything, att, inv, own, got)


def heads_back_kernel(hd, nq, nk, own_ref, got_ref, pre_ref, cos_ref, sin_ref, qg_ref, kg_ref, x_ref, w_ref, core_ref, dpre_ref, first_ref, gain_ref, hgain_ref):
    half = w_ref.shape[1]
    low, high = join_positions(core_ref[0], own_ref[...].astype(F32), got_ref[...].astype(F32))
    sides = (nq // 2, nk // 2, nk // 2)
    grads = [[], [], []]
    for side in (low, high):
        at = 0
        for kind, count in enumerate(sides):
            for h in range(count):
                grads[kind].append(side[at : at + hd])
                at += hd
    cosine, sine = cos_ref[...], sin_ref[...]
    done = []
    sums = [0.0, 0.0]
    for h in range(nq + nk):
        kind = 0 if h < nq else 1
        g = grads[kind][h - kind * nq]
        a, b = g[: hd // 2], g[hd // 2 :]
        g = jnp.concatenate([a * cosine + b * sine, b * cosine - a * sine], axis=0)
        v = pre_ref[h * hd : (h + 1) * hd, :]
        inv = lax.rsqrt(jnp.mean(v * v, axis=0, keepdims=True) + epsilon)
        hat = v * inv
        sums[kind] = sums[kind] + jnp.sum(g * hat, axis=1, keepdims=True)
        gg = g * (qg_ref[...] if kind == 0 else kg_ref[...])
        done.append(inv * (gg - hat * jnp.mean(gg * hat, axis=0, keepdims=True)))
    done += grads[2]
    hgain_ref[:hd, :] = jnp.broadcast_to(sums[0], (hd, 128))
    hgain_ref[hd:, :] = jnp.broadcast_to(sums[1], (hd, 128))
    dpre = jnp.concatenate(done, axis=0).T.astype(BF16)
    dpre_ref[...] = dpre
    x = x_ref[0].astype(F32)
    hat = x * inverse_rms(x)
    for k in range(2):
        cut = slice(k * half, (k + 1) * half)
        part = dot_nt(dpre, w_ref[k])
        first_ref[:, cut] = part.astype(BF16)
        gain_ref[:, cut] = jnp.sum(part * hat[:, cut], axis=0, keepdims=True)


def heads_back(own, got, pre, cosine, sine, qgain, kgain, xr, seq, weight, core, hd, nq, nk):
    span = own.shape[1]
    _, half, cols = weight.shape
    width = 2 * half
    whole = lambda a: pl.BlockSpec(a.shape, lambda i: (0,) * len(a.shape))
    outs = [shape((span, cols), BF16), shape((span, width), BF16), shape((1, width), F32), shape((2 * hd, 128), F32)]
    return pl.pallas_call(
        functools.partial(heads_back_kernel, hd, nq, nk),
        grid=(1,),
        in_specs=[whole(a) for a in (own, got, pre, cosine, sine, qgain, kgain)]
        + [pl.BlockSpec((1, span, width), lambda i: (seq, 0, 0)), whole(weight), SMEM],
        out_specs=[whole(o) for o in outs],
        out_shape=outs,
        compiler_params=PARAMS,
        cost_estimate=cost(2 * span * width * cols, 4 * span * width + 4 * half * cols),
        name="query_key_value_back",
    )(own, got, pre, cosine, sine, qgain, kgain, xr, weight, core)


def place_blocks(order, ids, first_id, value, out_ref):
    piece = value.shape[-1] // order
    for k in range(order):
        if order == 1:
            out_ref[...] = value
        else:
            dst = pl.ds(pl.multiple_of(ids[first_id + k] * piece, piece), piece)
            out_ref[:, dst] = value[:, k * piece : (k + 1) * piece]


def output_kernel(order, scal_ref, got_ref, f0_ref, f1_ref, h0_ref, h1_ref, out_ref, stat_ref):
    low = scal_ref[0] * 2 < scal_ref[3]
    rows = out_ref.shape[0]
    ffn = got_ref[...].astype(F32) + jnp.where(low, f0_ref[...], f1_ref[...]).astype(F32)
    hidden = jnp.where(low, h0_ref[...], h1_ref[...])
    place = scal_ref[2] + lax.broadcasted_iota(jnp.int32, (rows, 1), 0)
    valid = (place < scal_ref[1]).astype(F32)
    stat_ref[...] = jnp.broadcast_to(jnp.sum(valid * ffn * ffn, keepdims=True), (8, 128))
    place_blocks(order, scal_ref, 4, (hidden + ffn).astype(BF16), out_ref)


def share_specs(rows, width, per):
    return [
        pl.BlockSpec((rows, width), lambda i, s: (jnp.minimum(s[0], per - 1), 0)),
        pl.BlockSpec((rows, width), lambda i, s: (jnp.maximum(s[0] - per, 0), 0)),
    ]


def output_share(scalars, got, ffns, hiddens, order):
    rows, width = got.shape
    pair = share_specs(rows, width, ffns[0].shape[0] // rows)
    flat = pl.BlockSpec((rows, width), lambda i, s: (0, 0))
    return pl.pallas_call(
        functools.partial(output_kernel, order),
        grid_spec=pltpu.PrefetchScalarGridSpec(
            num_scalar_prefetch=1,
            grid=(1,),
            in_specs=[flat] + pair + pair,
            out_specs=[flat, pl.BlockSpec((8, 128), lambda i, s: (0, 0))],
        ),
        out_shape=[shape((rows, width), BF16), shape((8, 128), F32)],
        compiler_params=PARAMS,
        cost_estimate=cost(6 * rows * width, 16 * rows * width),
        name="output_share",
    )(scalars, got, *ffns, *hiddens)


def input_kernel(order, scal_ref, got_ref, part_ref, g0_ref, g1_ref, x_ref, gain_ref, out_ref):
    low = scal_ref[0] * 2 < scal_ref[3]
    e = got_ref[...].astype(F32) + part_ref[...].astype(F32)
    gh = jnp.where(low, g0_ref[...], g1_ref[...])
    x = x_ref[0].astype(F32)
    inv = inverse_rms(x)
    hat = x * inv
    eg = e * gain_ref[...]
    value = gh + inv * (eg - hat * jnp.mean(eg * hat, axis=-1, keepdims=True))
    place_blocks(order, scal_ref, 4, value, out_ref)


def input_share(scalars, got, part, ghs, xr, seq, gain, order):
    rows, width = got.shape
    pair = share_specs(rows, width, ghs[0].shape[0] // rows)
    flat = pl.BlockSpec((rows, width), lambda i, s: (0, 0))
    return pl.pallas_call(
        functools.partial(input_kernel, order),
        grid_spec=pltpu.PrefetchScalarGridSpec(
            num_scalar_prefetch=1,
            grid=(1,),
            in_specs=[flat, pl.BlockSpec((rows, width), lambda i, s: (s[0], 0))]
            + pair
            + [pl.BlockSpec((1, rows, width), lambda i, s: (seq, s[0], 0)), pl.BlockSpec((1, width), lambda i, s: (0, 0))],
            out_specs=flat,
        ),
        out_shape=shape((rows, width), F32),
        compiler_params=PARAMS,
        cost_estimate=cost(12 * rows * width, 20 * rows * width),
        name="input_share",
    )(scalars, got, part, *ghs, xr, gain)


def weight_grad_kernel(count, extra, *refs):
    a_refs, b_refs, out = refs[:count], refs[count : 2 * count], refs[-1]
    total = dot_tn(a_refs[0][...], b_refs[0][...])
    for a, b in zip(a_refs[1:], b_refs[1:]):
        total = total + dot_tn(a[...], b[...])
    if extra:
        total = total + refs[2 * count][...].astype(F32)
    out[...] = total.astype(BF16)


def weight_grad(lefts, rights, side, axis, add=None):
    count = len(lefts)
    rows_all, cols_all = lefts[0].shape[1], rights[0].shape[1]
    dims = [rows_all, cols_all]
    dims[axis] //= 2
    rows, cols = min(512, dims[0]), min(2048, dims[1])
    row_at = side * (dims[0] // rows) if axis == 0 else 0
    col_at = side * (dims[1] // cols) if axis == 1 else 0
    specs = [pl.BlockSpec((a.shape[0], rows), lambda j, i: (0, i + row_at)) for a in lefts]
    specs += [pl.BlockSpec((b.shape[0], cols), lambda j, i: (0, j + col_at)) for b in rights]
    tile = pl.BlockSpec((rows, cols), lambda j, i: (i, j))
    tokens = sum(a.shape[0] for a in lefts)
    return pl.pallas_call(
        functools.partial(weight_grad_kernel, count, add is not None),
        grid=(dims[1] // cols, dims[0] // rows),
        in_specs=specs + ([tile] if add is not None else []),
        out_specs=tile,
        out_shape=shape(dims, BF16),
        compiler_params=PARAMS,
        cost_estimate=cost(2 * tokens * dims[0] * dims[1], 2 * tokens * sum(dims) + 2 * dims[0] * dims[1]),
        name="weight_grad",
    )(*lefts, *rights, *([add] if add is not None else []))


def xor_one(index):
    return index + 1 - 2 * (index % 2)


def remote(src, dst, send, recv, device):
    return pltpu.make_async_remote_copy(
        src_ref=src, dst_ref=dst, send_sem=send, recv_sem=recv, device_id=device, device_id_type=pl.DeviceIdType.MESH
    )


def greet(others):
    barrier = pltpu.get_barrier_semaphore()
    count = 0
    for needed, device in others:
        if needed is None:
            pl.semaphore_signal(barrier, inc=1, device_id=device, device_id_type=pl.DeviceIdType.MESH)
            count = count + 1
        else:

            @pl.when(needed)
            def _():
                pl.semaphore_signal(barrier, inc=1, device_id=device, device_id_type=pl.DeviceIdType.MESH)

            count = count + jnp.where(needed, 1, 0)
    pl.semaphore_wait(barrier, count)


class Gather:
    def __init__(self, shard, dst, axis, send, recv, local, near_x, near_y, near_core):
        piece = shard.shape[axis]
        half = shard.shape[0] // 2

        def block(side, k):
            cut = pl.ds(k * piece, piece)
            return dst.at[side, cut, :] if axis == 0 else dst.at[side, :, cut]

        def part(k, h):
            if axis == 0:
                return dst.at[0, pl.ds(k * piece + h * half, half), :]
            return dst.at[0, pl.ds(h * half, half), pl.ds(k * piece, piece)]

        sem = lambda k: (send.at[k], recv.at[k])
        self.local = pltpu.make_async_copy(shard, block(0, 0), local)
        self.x = remote(shard, block(0, 1), *sem(0), near_x)
        self.y = remote(shard, block(0, 2), *sem(1), near_y)
        self.dx = remote(part(2, 0), part(3, 0), *sem(2), near_x)
        self.dy = remote(part(1, 1), part(3, 1), *sem(3), near_y)
        self.cores = [remote(shard, block(1, 0), *sem(4), near_core)]
        self.cores += [remote(block(0, k), block(1, k), *sem(4 + k), near_core) for k in (1, 2, 3)]

    def first(self):
        self.x.start()
        self.y.start()
        self.cores[0].start()
        self.local.start()

    def second(self):
        self.y.wait_recv()
        self.dx.start()
        self.cores[2].start()
        self.x.wait_recv()
        self.dy.start()
        self.cores[1].start()

    def third(self):
        self.dx.wait_recv()
        self.dy.wait_recv()
        self.cores[3].start()

    def arrived(self):
        self.local.wait()
        for copy in self.cores:
            copy.wait_recv()

    def sent(self):
        for copy in [self.x, self.y, self.dx, self.dy] + self.cores:
            copy.wait_send()


def forward_kernel(
    hd, nq, nk, block, sub,
    len_ref, x_hbm, cot_hbm, wq_hbm, wk_hbm, wv_hbm, wout, wgate, wup, wdown, small_ref,
    xr_hbm, n1_hbm, gf_hbm, qkv_hbm, out_hbm, gate_hbm, up_hbm, down_hbm, hidden_hbm, n2_hbm, rest_hbm, gi_hbm, pre_hbm, all_hbm, att_hbm, tok_hbm,
    gains_ref, table_ref, inv_ref, stat_ref,
    xr_v, cot_v, n1_v, qkv_v, out_v, ex_own, ex_send, ex_got, at_own, at_send, at_got,
    part_v, in_v, back_v, total_v, hid_v, norm_v, wqkv, gain_ref, down_v, gi_v, pre_ref, all_ref, att_ref, tok_ref,
    keep_sem, load_sem, store_sem, shard_sem, rest_sem, down_sem, gi_sem, wsend, wrecv, wloc, gsend, grecv, exsend, exrecv, zsend, zrecv, hid_sem,
):
    seqs, span, width = xr_v.shape
    groups = nq // nk
    row, core, rank = lax.axis_index("dp"), lax.axis_index("context"), lax.axis_index("tensor")
    start = core * span
    near = [row, xor_one(row), (row + 2) % 4, 3 - row]
    inner = (rank % 3) != 0
    near_x, near_y, near_core = {"dp": near[1]}, {"dp": near[2]}, {"context": 1 - core}
    z_side, z_mid = {"tensor": xor_one(rank)}, {"tensor": 3 - rank}
    piece = width // 8
    total_subs = part_v.shape[0]
    per = span // sub
    first_core = core == 0

    loads = []
    for at, (src, dst) in enumerate(((x_hbm, xr_v), (cot_hbm, cot_v))):
        for s in range(seqs):
            for o in range(2):
                for k in range(4):
                    b = near[k] * 2 + (core if o == 0 else 1 - core)
                    cut = pl.ds(pl.multiple_of(b * piece, piece), piece)
                    loads.append(
                        pltpu.make_async_copy(
                            src.at[s, :, cut], dst.at[s, :, pl.ds((o * 4 + k) * piece, piece)], load_sem.at[at, s, o * 4 + k]
                        )
                    )
    shards, at = [], 0
    for k, ref in enumerate((wq_hbm, wk_hbm, wv_hbm)):
        shards.append(pltpu.make_async_copy(ref, wqkv.at[:, pl.ds(at, ref.shape[1])], shard_sem.at[k]))
        at += ref.shape[1]
    for copy in shards + loads:
        copy.start()
    piece = width // 8
    gain_ref[...] = jnp.concatenate([small_ref[:, :piece], small_ref[:, piece : 2 * piece], jnp.zeros((14, piece), BF16)], axis=0)

    others = []
    for o in range(2):
        for k in range(4):
            if o or k:
                others.append((o * 4 + k, {"dp": near[k], "context": core if o == 0 else 1 - core}))
    greet([(None, d) for _, d in others] + [(None, z_side), (inner, z_mid)])

    gains = [remote(gain_ref, gains_ref.at[b], gsend.at[b], grecv.at[b], d) for b, d in others]
    for copy in gains:
        copy.start()
    weights = [
        Gather(shard, dst, axis, wsend.at[i], wrecv.at[i], wloc.at[i], near_x, near_y, near_core)
        for i, (shard, dst, axis) in enumerate(
            ((wqkv, qkv_v, 0), (wout, out_v, 1), (wgate, gate_hbm, 0), (wup, up_hbm, 0), (wdown, down_hbm, 1))
        )
    ]
    w_qkv, w_out, w_gate, w_up, w_down = weights
    for copy in shards:
        copy.wait()
    w_qkv.first()
    gains_ref[0] = gain_ref[...]

    quarter = hd // 2
    freqs = jnp.exp(lax.broadcasted_iota(jnp.int32, (quarter, span), 0).astype(F32) * (-2.0 * math.log(rope_base) / hd))
    angles = freqs * (start + lax.broadcasted_iota(jnp.int32, (quarter, span), 1)).astype(F32)
    cosine, sine = jnp.cos(angles), jnp.sin(angles)
    both_gains = jnp.broadcast_to(small_ref[:, 2 * piece :].astype(F32), (8, 2 * hd)).T
    qgain, kgain = both_gains[:hd, 0:1], both_gains[hd:, 0:1]
    table_ref[:quarter, :] = cosine
    table_ref[quarter : 2 * quarter, :] = sine
    table_ref[2 * quarter : 2 * quarter + hd, :128] = jnp.broadcast_to(qgain, (hd, 128))
    table_ref[2 * quarter + hd :, :128] = jnp.broadcast_to(kgain, (hd, 128))

    for copy in loads[len(loads) // 2 :]:
        copy.wait()

    def mask_rows(i, carry):
        s, t = i // (span // 16), i % (span // 16)
        cut = pl.ds(pl.multiple_of(t * 16, 16), 16)
        place = start + t * 16 + lax.broadcasted_iota(jnp.int32, (16, 1), 0)
        valid = (place < len_ref[s]).astype(F32)
        cot_v[s, cut, :] = (cot_v[s, cut, :].astype(F32) * valid).astype(BF16)
        return carry

    lax.fori_loop(0, seqs * span // 16, mask_rows, 0)
    store_gf = pltpu.make_async_copy(cot_v, gf_hbm, store_sem.at[0])
    store_gf.start()
    for copy in loads[: len(loads) // 2]:
        copy.wait()
    store_xr = pltpu.make_async_copy(xr_v, xr_hbm, store_sem.at[1])
    store_xr.start()
    for copy in gains:
        copy.wait_recv()
    gain1 = jnp.concatenate([gains_ref[b, 0:1, :] for b in range(8)], axis=1).astype(F32)
    gain2 = jnp.concatenate([gains_ref[b, 1:2, :] for b in range(8)], axis=1).astype(F32)

    def norm_rows(i, carry):
        s, t = i // (span // 16), i % (span // 16)
        cut = pl.ds(pl.multiple_of(t * 16, 16), 16)
        x = xr_v[s, cut, :].astype(F32)
        n1_v[s, cut, :] = (x * inverse_rms(x) * gain1).astype(BF16)
        return carry

    lax.fori_loop(0, span // 16, norm_rows, 0)
    w_qkv.second()
    w_out.first()
    lax.fori_loop(span // 16, seqs * span // 16, norm_rows, 0)
    store_n1 = pltpu.make_async_copy(n1_v, n1_hbm, store_sem.at[2])
    store_n1.start()
    w_qkv.third()
    w_qkv.arrived()

    half = width // 2

    def exchange(s):
        return remote(ex_send.at[s], ex_got.at[s], exsend.at[0, s], exrecv.at[0, s], near_core)

    def keep(k, s):
        ref, dst = ((pre_ref, pre_hbm), (all_ref, all_hbm), (att_ref, att_hbm), (tok_ref, tok_hbm))[k]
        return pltpu.make_async_copy(ref.at[s], dst.at[s], keep_sem.at[k, s])

    def project(s):
        x = n1_v[s]
        flat = dot_nn(x[:, :half], qkv_v[0]) + dot_nn(x[:, half:], qkv_v[1])
        turned = flat.T
        pre_ref[s] = turned[: (nq + nk) * hd]
        done = []
        for h in range(nq + nk):
            v = turned[h * hd : (h + 1) * hd]
            inv = lax.rsqrt(jnp.mean(v * v, axis=0, keepdims=True) + epsilon)
            v = v * inv * (qgain if h < nq else kgain)
            a, b = v[: hd // 2], v[hd // 2 :]
            done.append(jnp.concatenate([a * cosine - b * sine, b * cosine + a * sine], axis=0))
        for h in range(nk):
            lo = (nq + nk + h) * hd
            done.append(turned[lo : lo + hd])
        parts = [[], []]
        for begin_at, count in ((0, nq), (nq, nk), (nq + nk, nk)):
            for side in range(2):
                parts[side] += done[begin_at + side * count // 2 : begin_at + (side + 1) * count // 2]
        low = jnp.concatenate(parts[0], axis=0)
        high = jnp.concatenate(parts[1], axis=0)
        ex_own[s] = jnp.where(first_core, low, high).astype(BF16)
        ex_send[s] = jnp.where(first_core, high, low).astype(BF16)
        exchange(s).start()
        keep(0, s).start()

    store_qkv = pltpu.make_async_copy(qkv_v, qkv_hbm, store_sem.at[3])
    store_qkv.start()
    store_out = pltpu.make_async_copy(out_v, out_hbm, store_sem.at[4])

    scale = log2e / math.sqrt(hd)
    krow = lax.broadcasted_iota(jnp.int32, (block, groups * block), 0)
    qcol = lax.broadcasted_iota(jnp.int32, (block, groups * block), 1) % block
    base = groups * hd

    def give(s):
        return remote(at_send.at[s], at_got.at[s], exsend.at[1, s], exrecv.at[1, s], near_core)

    def attention(s):
        exchange(s).wait_recv()
        low, high = join_positions(core, ex_own[s], ex_got[s])
        all_ref[s, :, :span] = low
        all_ref[s, :, span:] = high
        length = len_ref[s]
        for i in range(2 * span // block):
            cut = slice(i * block, (i + 1) * block)
            q = jnp.concatenate([all_ref[s, g * hd : (g + 1) * hd, cut] for g in range(groups)], axis=1)
            acc = jnp.zeros((hd, groups * block), F32)
            total = jnp.zeros((1, groups * block), F32)
            for j in range(i + 1):
                kcut = slice(j * block, (j + 1) * block)
                score = dot_tn(all_ref[s, base : base + hd, kcut], q) * scale
                ok = (krow + j * block) < length
                if j == i:
                    ok = ok & (krow <= qcol)
                e = jnp.where(ok, jnp.exp2(score), 0.0)
                total = total + jnp.sum(e, axis=0, keepdims=True)
                acc = acc + dot_nn(all_ref[s, base + hd : base + 2 * hd, kcut], e.astype(BF16))
            inv = 1.0 / total
            att = (acc * inv).astype(BF16)
            for g in range(groups):
                att_ref[s, g * hd : (g + 1) * hd, cut] = att[:, g * block : (g + 1) * block]
                inv_ref[s, g : g + 1, cut] = inv[:, g * block : (g + 1) * block]
        mine, theirs = join_positions(core, att_ref[s, :, :span], att_ref[s, :, span:])
        at_own[s] = mine
        at_send[s] = theirs
        give(s).start()
        keep(1, s).start()
        keep(2, s).start()

    moving = Chain(rank, part_v, in_v, back_v, zsend, zrecv)
    subs = moving.count

    def branch_rows(s):
        give(s).wait_recv()
        low, high = join_positions(core, at_own[s], at_got[s])
        att = jnp.concatenate([low, high], axis=0).T
        tok_ref[s] = att
        keep(3, s).start()
        many = 2
        for k in range(0, per, many):
            rows = att[k * sub : (k + many) * sub]
            for side in range(2):
                part = dot_nn(rows, out_v[side]).astype(BF16)
                for m in range(many):
                    part_v[s * per + k + m, :, side * half : (side + 1) * half] = part[m * sub : (m + 1) * sub]
            for m in range(many):
                u = s * per + k + m

                @pl.when(u < subs)
                def _():
                    moving.begin(u)

    def sequence(s, carry):
        project(s)

        @pl.when(s == 0)
        def _():
            w_out.second()
            w_down.first()
            w_gate.first()

        attention(s)

        @pl.when(s == 0)
        def _():
            w_out.third()
            w_out.arrived()
            store_out.start()

        branch_rows(s)
        return carry

    lax.fori_loop(0, seqs, sequence, 0)
    rest = [pltpu.make_async_copy(part_v.at[u], rest_hbm.at[u - subs], rest_sem.at[u - subs]) for u in range(subs, total_subs)]
    for copy in rest:
        copy.start()
    stat_ref[...] = jnp.zeros_like(stat_ref)

    def hidden_store(u):
        cut = pl.ds(pl.multiple_of(u * sub, sub), sub)
        return (
            pltpu.make_async_copy(hid_v.at[u % 2], hidden_hbm.at[cut, :], hid_sem.at[0, u % 2]),
            pltpu.make_async_copy(norm_v.at[u % 2], n2_hbm.at[cut, :], hid_sem.at[1, u % 2]),
        )

    def finish(u):
        s, t = u // per, u % per
        cut = pl.ds(pl.multiple_of(t * sub, sub), sub)

        moving.total(u, total_v)

        @pl.when(u >= 2)
        def _():
            for copy in hidden_store(u - 2):
                copy.wait()

        length = len_ref[s]

        def body(piece_rows, first):
            total = total_v[piece_rows, :]
            resid = xr_v[s, pl.ds(pl.multiple_of(t * sub + first, 16), 16), :].astype(F32)
            hidden = resid + total
            hid_v[u % 2, piece_rows, :] = hidden
            norm_v[u % 2, piece_rows, :] = (hidden * inverse_rms(hidden) * gain2).astype(BF16)
            place = start + t * sub + first + lax.broadcasted_iota(jnp.int32, (16, 1), 0)
            valid = (place < length).astype(F32)
            stat_ref[0] += fold_lanes(valid * resid * resid)
            stat_ref[1] += fold_lanes(valid * total * total)

        by_pieces(sub, body)
        for copy in hidden_store(u):
            copy.start()

    hb = down_v.shape[2]
    blocks = down_hbm.shape[1] // hb

    def load_down(h):
        cut = pl.ds(pl.multiple_of(h * hb, hb), hb)
        return [pltpu.make_async_copy(down_hbm.at[side, cut, :], down_v.at[h % 2, side], down_sem.at[h % 2, side]) for side in range(2)]

    def store_gi(h):
        cut = pl.ds(pl.multiple_of(h * hb, hb), hb)
        return pltpu.make_async_copy(gi_v.at[h % 2], gi_hbm.at[:, cut], gi_sem.at[h % 2])

    def grad_inner(h):
        for copy in load_down(h):
            copy.wait()

        @pl.when(h + 1 < blocks)
        def _():
            for copy in load_down(h + 1):
                copy.start()

        @pl.when(h >= 2)
        def _():
            store_gi(h - 2).wait()

        for s in range(seqs):
            for q in range(span // 256):
                cut = slice(q * 256, (q + 1) * 256)
                g = dot_nt(cot_v[s, cut, :half], down_v[h % 2, 0]) + dot_nt(cot_v[s, cut, half:], down_v[h % 2, 1])
                gi_v[h % 2, s * span + q * 256 : s * span + (q + 1) * 256, :] = g.astype(BF16)
        store_gi(h).start()

    def chain(i, carry):
        moving.middle(i)
        moving.outward(i - 1)

        @pl.when(i >= 2)
        def _():
            finish(i - 2)

        @pl.when(i == 1)
        def _():
            w_down.second()
            w_up.first()

        @pl.when(i == 6)
        def _():
            w_gate.second()

        @pl.when(i == 8)
        def _():
            w_down.third()

        @pl.when(i == 9)
        def _():
            w_down.arrived()
            for copy in load_down(0):
                copy.start()

        @pl.when((i >= 10) & (i < 10 + blocks))
        def _():
            grad_inner(i - 10)

        @pl.when(i == 12)
        def _():
            w_up.second()

        @pl.when(i == 14)
        def _():
            w_gate.third()

        return carry

    lax.fori_loop(0, subs + 2, chain, 0)
    w_up.third()
    for u in (subs - 2, subs - 1):
        for copy in hidden_store(u):
            copy.wait()
    for h in (blocks - 2, blocks - 1):
        store_gi(h).wait()
    moving.settle()
    for s in range(seqs):
        exchange(s).wait_send()
        give(s).wait_send()
        for k in range(4):
            keep(k, s).wait()
    for copy in gains:
        copy.wait_send()
    w_gate.arrived()
    w_up.arrived()
    for w in weights:
        w.sent()
    for copy in [store_gf, store_xr, store_n1, store_qkv, store_out] + rest:
        copy.wait()


def forward(lengths, x, cot, w_query, w_key, w_value, w_out, w_gate, w_up, w_down, all_gains, hd, nq, nk):
    seqs, span, width = x.shape
    half = width // 2
    groups = nq // nk
    sub = span // 8
    subs = seqs * span // sub
    here = subs - 2
    block = min(256, span)
    hidden = w_gate.shape[1]
    hb = hidden // 4
    cols = w_query.shape[1] + w_key.shape[1] + w_value.shape[1]
    rows = cols // 2
    any_space = pl.BlockSpec(memory_space=pl.ANY)
    vmem = pl.BlockSpec(memory_space=pltpu.VMEM)
    wide = (seqs, span, width)
    large = [
        shape(wide, BF16), shape(wide, BF16), shape(wide, BF16),
        shape((2, half, cols), BF16), shape((2, w_out.shape[0], half), BF16),
        shape((2, half, hidden), BF16), shape((2, half, hidden), BF16), shape((2, hidden, half), BF16),
        shape((seqs * span, width), F32), shape((seqs * span, width), BF16), shape((subs - here, sub, width), BF16),
        shape((seqs * span, hidden), BF16),
    ]
    kept = [
        shape((seqs, (nq + nk) * hd, span), F32), shape((seqs, rows, 2 * span), BF16),
        shape((seqs, groups * hd, 2 * span), BF16), shape((seqs, span, nq * hd), BF16),
    ]
    large += kept
    small = [
        shape((8, 16, width // 8), BF16), shape((3 * hd, span), F32), shape((seqs, groups, 2 * span), F32), shape((2, 8, 128), F32),
    ]
    dma = pltpu.SemaphoreType.DMA
    ex = pltpu.VMEM((seqs, rows, span), BF16)
    at = pltpu.VMEM((seqs, groups * hd, span), BF16)
    moving = pltpu.VMEM((subs, sub, width), BF16)
    landing = pltpu.VMEM((here, sub, width), BF16)
    flops = 2 * seqs * span * width * (cols + nq * hd) + 16 * seqs * nq * hd * span * span
    return pl.pallas_call(
        functools.partial(forward_kernel, hd, nq, nk, block, sub),
        in_specs=[SMEM] + [any_space] * 9 + [vmem],
        out_specs=[any_space] * len(large) + [vmem] * len(small),
        out_shape=large + small,
        scratch_shapes=[
            pltpu.VMEM(wide, BF16), pltpu.VMEM(wide, BF16), pltpu.VMEM(wide, BF16),
            pltpu.VMEM((2, half, cols), BF16), pltpu.VMEM((2, w_out.shape[0], half), BF16),
            ex, ex, ex, at, at, at,
            moving, landing, landing,
            pltpu.VMEM((sub, width), F32), pltpu.VMEM((2, sub, width), F32), pltpu.VMEM((2, sub, width), BF16),
            pltpu.VMEM((w_query.shape[0], cols), BF16), pltpu.VMEM((16, width // 8), BF16),
            pltpu.VMEM((2, 2, hb, half), BF16), pltpu.VMEM((2, seqs * span, hb), BF16),
            *[pltpu.VMEM(a.shape, a.dtype) for a in kept],
            dma((4, seqs)), dma((2, seqs, 8)), dma((5,)), dma((3,)), dma((subs - here,)), dma((2, 2)), dma((2,)), dma((5, 8)), dma((5, 8)), dma((5,)), dma((8,)), dma((8,)),
            dma((2, seqs)), dma((2, seqs)), dma((3, subs)), dma((3, subs)), dma((2, 2)),
        ],
        compiler_params=pltpu.CompilerParams(vmem_limit_bytes=VMEM_MOST, collective_id=1, has_side_effects=True),
        cost_estimate=cost(flops, 80 * seqs * span * width),
        name="attention_forward",
    )(lengths, x, cot, w_query, w_key, w_value, w_out, w_gate, w_up, w_down, all_gains)


def by_pieces(count, body, size=16):
    def one(p, carry):
        body(pl.ds(pl.multiple_of(p * size, size), size), p * size)
        return carry

    lax.fori_loop(0, count // size, one, 0)


def fold_lanes(values):
    tiles = values[:8] + values[8:]
    return sum(tiles[:, k * 128 : (k + 1) * 128] for k in range(tiles.shape[1] // 128))


class Chain:
    def __init__(self, rank, part, arrive, back, send, recv):
        self.inner = (rank % 3) != 0
        self.outer = (rank % 3) == 0
        self.part, self.arrive, self.back = part, arrive, back
        self.send, self.recv = send, recv
        self.side, self.mid = {"tensor": xor_one(rank)}, {"tensor": 3 - rank}
        self.count = arrive.shape[0]

    def hop_in(self, u):
        return remote(self.part.at[u], self.arrive.at[u], self.send.at[0, u], self.recv.at[0, u], self.side)

    def hop_mid(self, u):
        return remote(self.arrive.at[u], self.back.at[u], self.send.at[1, u], self.recv.at[1, u], self.mid)

    def hop_out(self, u):
        return remote(self.part.at[u], self.back.at[u], self.send.at[2, u], self.recv.at[2, u], self.side)

    def add(self, into, one, two, u):
        def body(cut, first):
            into[u, cut, :] = (one[u, cut, :].astype(F32) + two[u, cut, :].astype(F32)).astype(BF16)

        by_pieces(self.part.shape[1], body)

    def begin(self, u):
        @pl.when(self.outer)
        def _():
            self.hop_in(u).start()

    def middle(self, u):
        @pl.when((u >= 0) & (u < self.count) & self.inner)
        def _():
            self.hop_in(u).wait_recv()
            self.add(self.arrive, self.part, self.arrive, u)
            self.hop_mid(u).start()

    def outward(self, u):
        @pl.when((u >= 0) & (u < self.count) & self.inner)
        def _():
            self.hop_mid(u).wait_recv()
            self.add(self.part, self.part, self.back, u)
            self.hop_out(u).start()

    def total(self, u, into):
        @pl.when(self.inner)
        def _():
            def body(cut, first):
                into[cut, :] = self.arrive[u, cut, :].astype(F32) + self.back[u, cut, :].astype(F32)

            by_pieces(self.part.shape[1], body)

        @pl.when(self.outer)
        def _():
            self.hop_out(u).wait_recv()

            def body(cut, first):
                into[cut, :] = self.part[u, cut, :].astype(F32) + self.back[u, cut, :].astype(F32)

            by_pieces(self.part.shape[1], body)

    def settle(self):
        def one(u, carry):
            @pl.when(self.outer)
            def _():
                self.hop_in(u).wait_send()

            @pl.when(self.inner)
            def _():
                self.hop_mid(u).wait_send()
                self.hop_out(u).wait_send()

            return carry

        lax.fori_loop(0, self.count, one, 0)


def feed_both_kernel(
    hb, sub, rows,
    len_ref, n2_hbm, gf_hbm, gate_hbm, up_hbm, down_hbm, gi_hbm, rest_hbm, xr_hbm, hidden_in, gains_ref,
    ffn_hbm, gb_hbm, gh_hbm, dgate_hbm, dup_hbm, ddown_hbm, hidden_hbm, landx, landy, gain_out, stat_ref,
    n2_v, gf_v, inner_v, gg_v, gu_v, facc, gacc, wrow, wcol, part_v, in_v, back_v, total_v, hid_v, gh_v, gb_v, stage_row, stage_col,
    late_p, late_a, late_b, xtile_v, gi_v, wide_v, temp_v, gain_ref,
    load_sem, wsem, zsend, zrecv, hid_sem, out_sem, ffn_sem, csend, crecv, store_sem, lsend, lrecv, xt_sem, xsend, xrecv, xload, free_sem,
):
    core, rank = lax.axis_index("context"), lax.axis_index("tensor")
    near_core = {"context": 1 - core}
    tokens, width = n2_v.shape
    half = width // 2
    hidden = inner_v.shape[1]
    hsteps = hidden // hb
    steps = tokens // rows * hsteps
    per = rows // sub
    chain = Chain(rank, part_v, in_v, back_v, zsend, zrecv)
    subs = chain.count
    late = Chain(rank, late_p, late_a, late_b, lsend, lrecv)
    known = subs - late.count
    start = core * (tokens // 2)

    def load_weights(i):
        slot, h = i % 2, i % hsteps
        cut = pl.ds(pl.multiple_of(h * hb, hb), hb)
        here = pl.ds(pl.multiple_of(i // hsteps * rows, rows), rows)
        copies = [pltpu.make_async_copy(gi_hbm.at[here, cut], gi_v.at[slot], wsem.at[slot, 6])]
        for side in range(2):
            copies.append(pltpu.make_async_copy(gate_hbm.at[side, :, cut], wrow.at[slot, 0, side], wsem.at[slot, side]))
            copies.append(pltpu.make_async_copy(up_hbm.at[side, :, cut], wrow.at[slot, 1, side], wsem.at[slot, 2 + side]))
            copies.append(pltpu.make_async_copy(down_hbm.at[side, cut, :], wcol.at[slot, side], wsem.at[slot, 4 + side]))
        return copies

    def load_hidden(u):
        cut = pl.ds(pl.multiple_of(u * sub, sub), sub)
        return pltpu.make_async_copy(hidden_hbm.at[cut, :], hid_v, hid_sem)

    ready = pl.ds(0, known * sub)
    loads = [
        pltpu.make_async_copy(n2_hbm.at[ready, :], n2_v.at[ready, :], load_sem.at[0]),
        pltpu.make_async_copy(rest_hbm, late_p, load_sem.at[1]),
    ]
    load_gf = pltpu.make_async_copy(gf_hbm, gf_v, load_sem.at[2])
    for copy in loads + load_weights(0) + [load_gf]:
        copy.start()
    load_hidden(0).start()
    row = lax.axis_index("dp")
    near_x, near_y = {"dp": xor_one(row)}, {"dp": (row + 2) % 4}
    greet([(None, near_core), (None, near_x), (None, near_y), (None, chain.side), (chain.inner, chain.mid)])
    for b in range(8):
        gain_ref[:, b * (width // 8) : (b + 1) * (width // 8)] = gains_ref[b, 1:2, :].astype(F32)
    gain_out[...] = jnp.zeros_like(gain_out)
    stat_ref[...] = jnp.zeros_like(stat_ref)
    for copy in loads:
        copy.wait()
    for u in range(late.count):
        late.begin(u)

    def load_x(u):
        at = pl.multiple_of((known + u) * sub, sub)
        return pltpu.make_async_copy(xr_hbm.at[pl.ds(at, sub), :], xtile_v, xt_sem)

    def late_store(u):
        return pltpu.make_async_copy(gh_v, hidden_hbm.at[pl.ds(pl.multiple_of((known + u) * sub, sub), sub), :], out_sem.at[0])

    def late_finish(u):
        load_x(u).start()
        late.total(u, total_v)
        load_x(u).wait()

        @pl.when(u >= 1)
        def _():
            late_store(u - 1).wait()

        length = len_ref[known * sub // (tokens // 2)]
        offset = start + known * sub % (tokens // 2) + u * sub

        def body(cut, first):
            total = total_v[cut, :]
            resid = xtile_v[cut, :].astype(F32)
            hidden_rows = resid + total
            gh_v[cut, :] = hidden_rows
            normed = (hidden_rows * inverse_rms(hidden_rows) * gain_ref[...]).astype(BF16)
            n2_v[pl.ds(pl.multiple_of((known + u) * sub + first, 16), 16), :] = normed
            spot = offset + first + lax.broadcasted_iota(jnp.int32, (16, 1), 0)
            valid = (spot < length).astype(F32)
            stat_ref[0] += fold_lanes(valid * resid * resid)
            stat_ref[1] += fold_lanes(valid * total * total)

        by_pieces(sub, body)
        late_store(u).start()

    def store_gb(u):
        cut = pl.ds(pl.multiple_of(u * sub, sub), sub)
        return pltpu.make_async_copy(gb_v, gb_hbm.at[cut, :], out_sem.at[1])

    def store_gh(u):
        at = pl.ds(pl.multiple_of(u % 2 * sub, sub), sub)
        return pltpu.make_async_copy(gh_v, gh_hbm.at[u // 8, at, :], out_sem.at[0])

    def finish(u):
        chain.total(u, total_v)
        load_hidden(u).wait()

        @pl.when(u >= 1)
        def _():
            store_gb(u - 1).wait()

        def body(piece_rows, first):
            e = total_v[piece_rows, :]
            hidden_rows = hid_v[piece_rows, :]
            inv = inverse_rms(hidden_rows)
            hat = hidden_rows * inv
            eg = e * gain_ref[...]
            grad = gf_v[pl.ds(pl.multiple_of(u * sub + first, 16), 16), :].astype(F32)
            gh = grad + inv * (eg - hat * jnp.mean(eg * hat, axis=-1, keepdims=True))
            gb_v[piece_rows, :] = gh.astype(BF16)

            @pl.when(u % 8 // 2 == rank)
            def _():
                gh_v[piece_rows, :] = gh

            both = e * hat
            gain_out[...] += both[:8] + both[8:]

        by_pieces(sub, body)
        store_gb(u).start()

        @pl.when(u % 8 // 2 == rank)
        def _():
            store_gh(u).start()
            store_gh(u).wait()

        @pl.when(u + 1 < subs)
        def _():
            load_hidden(u + 1).start()

    def serve(n):
        chain.middle(n)
        chain.outward(n - 2)

        @pl.when((n >= 4) & (n < 4 + subs))
        def _():
            finish(n - 4)

    quarter = width // 4

    def store_ffn(c):
        here = pl.ds(pl.multiple_of(c * rows, rows), rows)
        return [
            pltpu.make_async_copy(
                stage_row.at[c % 2, pl.ds(k * rows, rows), :], ffn_hbm.at[here, pl.ds(k * quarter, quarter)], ffn_sem.at[c % 2, k]
            )
            for k in range(4)
        ]

    def step(i, carry):
        slot, c, h = i % 2, i // hsteps, i % hsteps
        for copy in load_weights(i):
            copy.wait()

        @pl.when(i + 1 < steps)
        def _():
            for copy in load_weights(i + 1):
                copy.start()

        here = pl.ds(pl.multiple_of(c * rows, rows), rows)
        cols = pl.ds(pl.multiple_of(h * hb, hb), hb)
        n = n2_v[here, :]
        wide = min(256, hb)
        for q in range(hb // wide):
            part = slice(q * wide, (q + 1) * wide)
            gate = dot_nn(n[:, :half], wrow[slot, 0, 0, :, part]) + dot_nn(n[:, half:], wrow[slot, 0, 1, :, part])
            up = dot_nn(n[:, :half], wrow[slot, 1, 0, :, part]) + dot_nn(n[:, half:], wrow[slot, 1, 1, :, part])
            gi = gi_v[slot, :, part].astype(F32)
            sig = jax.nn.sigmoid(gate)
            silu = gate * sig
            at = pl.ds(pl.multiple_of(h * hb + q * wide, wide), wide)
            inner_v[here, at] = (silu * up).astype(BF16)
            gg_v[here, at] = (gi * up * sig * (1.0 + gate * (1.0 - sig))).astype(BF16)
            gu_v[here, at] = (gi * silu).astype(BF16)

        @pl.when(h == 0)
        def _():
            facc[...] = jnp.zeros_like(facc)
            gacc[...] = jnp.zeros_like(gacc)

        inner, gg, gu = inner_v[here, cols], gg_v[here, cols], gu_v[here, cols]
        span = min(512, half)
        for side in range(2):
            for q in range(half // span):
                part = slice(q * span, (q + 1) * span)
                cut = slice(side * half + q * span, side * half + (q + 1) * span)
                facc[:, cut] += dot_nn(inner, wcol[slot, side, :, part])
                gacc[:, cut] += dot_nt(gg, wrow[slot, 0, side, part, :]) + dot_nt(gu, wrow[slot, 1, side, part, :])

        @pl.when((h == hsteps - 1) & (c >= 2))
        def _():
            for copy in store_ffn(c - 2):
                copy.wait()

        @pl.when(h == hsteps - 1)
        def _():
            for k in range(per):
                part_v[c * per + k] = gacc[k * sub : (k + 1) * sub, :].astype(BF16)
                chain.begin(c * per + k)

            for k in range(4):
                stage_row[c % 2, k * rows : (k + 1) * rows, :] = facc[:, k * quarter : (k + 1) * quarter].astype(BF16)
            for copy in store_ffn(c):
                copy.start()

        @pl.when((i >= 2) & (i < 2 + late.count))
        def _():
            late.middle(i - 2)

        @pl.when((i >= 4) & (i < 4 + late.count))
        def _():
            late.outward(i - 4)

        @pl.when((i >= 6) & (i < 6 + late.count))
        def _():
            late_finish(i - 6)

        @pl.when(i == 9)
        def _():
            load_gf.wait()
            late_store(late.count - 1).wait()

        serve(i - 6)
        return carry

    lax.fori_loop(0, steps, step, 0)
    for c in range(2, steps // hsteps):
        for copy in store_ffn(c):
            copy.wait()

    pl.semaphore_signal(free_sem, inc=1, device_id=near_core, device_id_type=pl.DeviceIdType.MESH)
    outs = (dgate_hbm, dup_hbm, ddown_hbm)

    def landing(w, t):
        return wrow.at[t // 2, w, t % 2] if w < 2 else wcol.at[t // 2, t % 2]

    def landed(w, t, piece):
        return wrow[t // 2, w, t % 2, piece, :] if w < 2 else wcol[t // 2, t % 2, piece, :]

    def staging(w):
        return stage_row if w < 2 else stage_col

    def ship(w, t):
        return remote(staging(w).at[t % 2], landing(w, t), csend.at[w, t], crecv.at[w, t], near_core)

    def keep(w, t):
        cut = pl.ds(pl.multiple_of(t * hb, hb), hb)
        dst = outs[w].at[:, cut] if w < 2 else outs[w].at[cut, :]
        return pltpu.make_async_copy(staging(w).at[t % 2], dst, store_sem.at[w, t])

    def release(kind, w, t):
        if kind == 1:
            ship(w, t).wait_send()
        else:
            keep(w, t).wait()

    def group(kind, w, before, part):
        def one(t, carry):
            cut = pl.ds(pl.multiple_of(t * hb, hb), hb)
            mine = slice(kind * half, (kind + 1) * half)
            @pl.when(t >= 2)
            def _():
                release(kind, w, t - 2)

            if before is not None:

                @pl.when(t < 2)
                def _():
                    release(before[0], before[1], t + hsteps - 2)

            if kind == 0:
                ship(w, t).wait_recv()
            tall = staging(w).shape[1]
            size = min(256, tall)
            for q in range(tall // size):
                piece = slice(q * size, (q + 1) * size)
                if w == 2:
                    left = inner_v[:, pl.ds(pl.multiple_of(t * hb + q * size, size), size)]
                    value = dot_tn(left, gf_v[:, mine])
                else:
                    value = dot_tn(n2_v[:, kind * half + q * size : kind * half + (q + 1) * size], (gg_v, gu_v)[w][:, cut])
                if kind == 0:
                    value = value + landed(w, t, piece).astype(F32)
                staging(w)[t % 2, piece, :] = value.astype(BF16)
            if kind == 1:
                ship(w, t).start()
            else:
                keep(w, t).start()
            return carry

        lax.fori_loop(part * (hsteps // 2), (part + 1) * (hsteps // 2), one, 0)

    pl.semaphore_wait(free_sem, 1)
    after = iter(range(steps - 6, subs + 4))
    done = []

    def both(kind, w, before):
        for part in range(2):
            group(kind, w, before, part)
            done.append(part)
            if len(done) <= 8 or len(done) % 2 == 0:
                serve(next(after))

    both(1, 0, None)
    both(0, 0, (1, 0))
    for t in range(hsteps - 2, hsteps):
        keep(0, t).wait()
    gate_sum = Scatter(
        row_blocks(dgate_hbm), wide_v.at[0], wide_v.at[1], half_rows(landx), half_rows(landy), temp_v, xsend, xrecv, xload, near_x, near_y
    )
    gate_sum.begin()
    both(1, 1, None)
    both(1, 2, None)
    gate_sum.pass_on()
    both(0, 1, (1, 1))
    both(0, 2, (1, 2))
    for n in after:
        serve(n)
    for t in range(hsteps - 2, hsteps):
        keep(1, t).wait()
        keep(2, t).wait()
    store_gb(subs - 1).wait()
    gate_sum.arrived()
    gate_sum.settle()
    chain.settle()
    late.settle()


def row_blocks(ref):
    size = ref.shape[0] // 4
    return lambda k, h: ref.at[pl.ds(k * size + h * (size // 2), size // 2), :]


def half_rows(ref):
    size = ref.shape[0] // 2
    return lambda h: ref.at[pl.ds(h * size, size), :]


def feed_both(lengths, n2, gf, gate, up, down, gi, rest, xr, hidden_rows, gain):
    tokens, width = n2.shape
    _, half, hidden = gate.shape
    hb = hidden // 4
    sub, rows = tokens // 16, tokens // 4
    count = rest.shape[0]
    any_space = pl.BlockSpec(memory_space=pl.ANY)
    vmem = pl.BlockSpec(memory_space=pltpu.VMEM)
    dma = pltpu.SemaphoreType.DMA
    moving = pltpu.VMEM((16, sub, width), BF16)
    late = pltpu.VMEM((count, sub, width), BF16)
    act = pltpu.VMEM((tokens, hidden), BF16)
    return pl.pallas_call(
        functools.partial(feed_both_kernel, hb, sub, rows),
        in_specs=[SMEM] + [any_space] * 9 + [vmem],
        out_specs=[any_space] * 9 + [vmem] * 2,
        out_shape=[
            shape((tokens, width), BF16), shape((tokens, width), BF16), shape((2, 2 * sub, width), F32),
            shape((half, hidden), BF16), shape((half, hidden), BF16), shape((hidden, half), BF16),
            shape((tokens, width), F32), shape((half // 4, hidden), BF16), shape((half // 4, hidden), BF16),
            shape((8, width), F32), shape((2, 8, 128), F32),
        ],
        scratch_shapes=[
            pltpu.VMEM((tokens, width), BF16), pltpu.VMEM((tokens, width), BF16), act, act, act,
            pltpu.VMEM((rows, width), F32), pltpu.VMEM((rows, width), F32),
            pltpu.VMEM((2, 2, 2, half, hb), BF16), pltpu.VMEM((2, 2, hb, half), BF16),
            moving, moving, moving, pltpu.VMEM((sub, width), F32),
            pltpu.VMEM((sub, width), F32), pltpu.VMEM((sub, width), F32), pltpu.VMEM((sub, width), BF16),
            pltpu.VMEM((2, half, hb), BF16), pltpu.VMEM((2, hb, half), BF16),
            late, late, late, pltpu.VMEM((sub, width), BF16), pltpu.VMEM((2, rows, hb), BF16),
            pltpu.VMEM((2, half // 8, hidden), BF16), pltpu.VMEM((2, half // 8, hidden), BF16), pltpu.VMEM((1, width), F32),
            dma((3,)), dma((2, 7)), dma((3, 16)), dma((3, 16)), dma(()), dma((2,)), dma((2, 4)), dma((3, 4)), dma((3, 4)),
            dma((3, 4)), dma((3, count)), dma((3, count)), dma(()), dma((6,)), dma((6,)), dma((3,)), pltpu.SemaphoreType.REGULAR,
        ],
        input_output_aliases={9: 6},
        compiler_params=pltpu.CompilerParams(vmem_limit_bytes=VMEM_MOST, collective_id=2, has_side_effects=True),
        cost_estimate=cost(18 * tokens * width * hidden, 60 * tokens * width),
        name="feed_forward_both",
    )(lengths, n2, gf, gate, up, down, gi, rest, xr, hidden_rows, gain)


class Ring:
    def __init__(self, rank, source, own, slots, send, recv, last=None):
        self.source, self.own, self.slots, self.send, self.recv = source, own, slots, send, recv
        self.last = slots.at[2] if last is None else last
        self.rows = slots.shape[1]
        self.rank, self.right = rank, {"tensor": (rank + 1) % 4}

    def hop(self, j):
        src = self.source((self.rank + 3) % 4) if j == 0 else self.slots.at[j - 1]
        dst = self.last if j == 2 else self.slots.at[j]
        return remote(src, dst, self.send.at[j], self.recv.at[j], self.right)

    def begin(self):
        self.hop(0).start()

    def step(self, j):
        self.hop(j - 1).wait_recv()
        read = self.own((self.rank + 3 - j) % 4)

        def body(cut, first):
            self.slots[j - 1, cut, :] = (self.slots[j - 1, cut, :].astype(F32) + read(cut).astype(F32)).astype(BF16)

        by_pieces(self.rows, body)
        self.hop(j).start()

    def arrived(self):
        self.hop(2).wait_recv()

    def settle(self):
        for j in range(3):
            self.hop(j).wait_send()


def tall(ref):
    return 16 * max(1, 2048 // ref.shape[1])


class Scatter:
    def __init__(self, block, from_x, from_y, land_x, land_y, temps, send, recv, load, near_x, near_y):
        self.block, self.from_x, self.from_y, self.land_x, self.land_y = block, from_x, from_y, land_x, land_y
        self.temps, self.load = temps, load
        sem = lambda k: (send.at[k], recv.at[k])
        self.first = [
            remote(block(3, 0), from_x, *sem(0), near_x),
            remote(block(3, 1), from_y, *sem(1), near_y),
            remote(block(1, 0), land_x(0), *sem(2), near_x),
            remote(block(2, 1), land_y(1), *sem(3), near_y),
        ]
        self.second = [
            remote(from_y, land_x(1), *sem(4), near_x),
            remote(from_x, land_y(0), *sem(5), near_y),
        ]

    def begin(self):
        for copy in self.first:
            copy.start()

    def pass_on(self):
        loads = [
            pltpu.make_async_copy(self.block(1, 1), self.temps.at[0], self.load.at[0]),
            pltpu.make_async_copy(self.block(2, 0), self.temps.at[1], self.load.at[1]),
        ]
        for copy in loads:
            copy.start()
        for which, into in ((1, self.from_y), (0, self.from_x)):
            self.first[which].wait_recv()
            loads[1 - which].wait()
            temp = 1 - which

            def body(cut, first):
                into[cut, :] = (into[cut, :].astype(F32) + self.temps[temp, cut, :].astype(F32)).astype(BF16)

            by_pieces(into.shape[0], body, tall(into))
            self.second[temp].start()

    def arrived(self):
        for copy in self.first[2:] + self.second:
            copy.wait_recv()

    def finish(self, stage, out, store, landed=False):
        if not landed:
            self.arrived()
        for h in range(2):
            loads = [
                pltpu.make_async_copy(src, self.temps.at[k], self.load.at[k])
                for k, src in enumerate((self.block(0, h), self.land_x(h), self.land_y(h)))
            ]
            for copy in loads:
                copy.start()
            for copy in loads:
                copy.wait()

            def body(cut, first):
                stage[cut, :] = sum(self.temps[k, cut, :].astype(F32) for k in range(3))

            by_pieces(stage.shape[0], body, tall(stage))
            keep = pltpu.make_async_copy(stage, out(h), store)
            keep.start()
            keep.wait()

    def settle(self):
        for copy in self.first + self.second:
            copy.wait_send()


def backward_kernel(
    hd, nq, nk, block,
    len_ref, gb_hbm, hidden_hbm, ffn_hbm, xr_hbm, n1_hbm, tok_hbm, outw_hbm, qkvw_hbm, all_hbm, att_hbm, inv_hbm, pre_hbm,
    dup_hbm, ddown_hbm, table_ref, stat_ref, stat2_ref, gain2_ref,
    out_hbm, fin_hbm, own_hbm, mine_o, mine_q, landx1, landy1, landx2, landy2, landx3, landy3, landx4, landy4,
    lines_out, small_out,
    act_v, rows_v, qkvw_v, tok_v, all_v, att_v, inv_v, pre_v, grads, da_all, da_own, da_send, da_got, d_own, d_send, d_got, dpre_v,
    first_v, slots_v, piece_v, wide_a, wide_b, temp_a, temp_b,
    go_v, so_v, wide_o, temp_o, gq_v, sq_v, wide_q, temp_q,
    tile_v, otile_v, lines_v, small_v, heads_v, lin1, lin2, lin3, small_r,
    load_sem, zsend, zrecv, piece_sem, xsend, xrecv, xload, own_sem, exsend, exrecv, osend, orecv, qsend, qrecv,
    tile_sem, outs_sem, smsend, smrecv,
):
    seqs, _, slots = all_v.shape
    span = slots // 2
    width = act_v.shape[1]
    half = width // 2
    groups = nq // nk
    share = span // 4
    row, core, rank = lax.axis_index("dp"), lax.axis_index("context"), lax.axis_index("tensor")
    start = core * span
    near = [row, xor_one(row), (row + 2) % 4, 3 - row]
    near_x, near_y, near_core = {"dp": near[1]}, {"dp": near[2]}, {"context": 1 - core}
    z_right, z_left, z_far = {"tensor": (rank + 1) % 4}, {"tensor": (rank + 3) % 4}, {"tensor": (rank + 2) % 4}
    first_core = core == 0

    def load(k, src, dst):
        copy = pltpu.make_async_copy(src, dst, load_sem.at[k])
        copy.start()
        return copy

    load_gb = load(0, gb_hbm, act_v)
    load_outw = load(1, outw_hbm, rows_v)
    load_att = [
        load(2, all_hbm, all_v), load(3, att_hbm, att_v), load(4, inv_hbm, inv_v), load(5, pre_hbm, pre_v),
    ]
    load_tok = load(6, tok_hbm, tok_v)
    load_qkvw = load(7, qkvw_hbm, qkvw_v)

    def piece_rows(s, m):
        return pl.ds(pl.multiple_of(s * span + m * share, share), share)

    def load_piece(s, m):
        return pltpu.make_async_copy(ffn_hbm.at[piece_rows(s, m), :], piece_v.at[s], piece_sem.at[s])

    greet([(None, d) for d in (near_x, near_y, {"dp": near[3]}, near_core, z_right, z_left, z_far)])

    def ffn_own(s):
        def own(m):
            load_piece(s, m).wait()
            return lambda cut: piece_v[s, cut, :]

        return own

    def first_own(s):
        return lambda m: lambda cut: first_v[s, m, cut, :]

    ffn_rings = [
        Ring(rank, lambda m, s=s: ffn_hbm.at[piece_rows(s, m), :], ffn_own(s), slots_v.at[s], zsend.at[s], zrecv.at[s])
        for s in range(seqs)
    ]
    first_rings = [
        Ring(rank, lambda m, s=s: first_v.at[s, m], first_own(s), slots_v.at[seqs + s], zsend.at[seqs + s], zrecv.at[seqs + s], fin_hbm.at[s])
        for s in range(seqs)
    ]
    last = seqs - 1
    for s in range(seqs):
        ffn_rings[s].begin()
        load_piece(s, (rank + 2) % 4).start()

    def ffn_step(s, j):
        ffn_rings[s].step(j)
        load_piece(s, (rank + 2 - j) % 4).start()

    def in_hbm(ref, axis):
        size = ref.shape[axis] // 4
        h2 = (size if axis == 0 else ref.shape[0]) // 2

        def get(k, h):
            if axis == 0:
                return ref.at[pl.ds(k * size + h * h2, h2), :]
            return ref.at[pl.ds(h * h2, h2), pl.ds(k * size, size)]

        return get

    def halves(ref):
        h2 = ref.shape[0] // 2
        return lambda h: ref.at[pl.ds(h * h2, h2), :]

    def in_vmem(ref):
        h2 = ref.shape[1] // 2
        return lambda k, h: ref.at[k, pl.ds(h * h2, h2), :]

    def scatter(i, get, wide, land_x, land_y, temps):
        return Scatter(get, wide.at[0], wide.at[1], land_x, land_y, temps, xsend.at[i], xrecv.at[i], xload.at[i], near_x, near_y)

    s_up = scatter(0, in_hbm(dup_hbm, 0), wide_a, halves(landx1), halves(landy1), temp_a)
    s_down = scatter(1, in_hbm(ddown_hbm, 1), wide_b, halves(landx2), halves(landy2), temp_b)
    s_out = scatter(2, in_vmem(go_v), wide_o, halves(landx3), halves(landy3), temp_o)
    s_qkv = scatter(3, in_vmem(gq_v), wide_q, halves(landx4), halves(landy4), temp_q)
    s_up.begin()

    load_gb.wait()
    load_outw.wait()

    def give(s):
        return remote(da_send.at[s], da_got.at[s], exsend.at[0, s], exrecv.at[0, s], near_core)

    def exchange(s):
        return remote(d_send.at[s], d_got.at[s], exsend.at[1, s], exrecv.at[1, s], near_core)

    def branch_rows(s, carry):
        here = pl.ds(pl.multiple_of(s * span, span), span)
        parts = []
        for q in range(2):
            cut = slice(q * (nq * hd // 2), (q + 1) * (nq * hd // 2))
            da = dot_nt(rows_v[0, cut, :], act_v[here, :half]) + dot_nt(rows_v[1, cut, :], act_v[here, half:])
            parts.append(da.astype(BF16))
        da_own[s] = jnp.where(first_core, parts[0], parts[1])
        da_send[s] = jnp.where(first_core, parts[1], parts[0])
        give(s).start()
        return carry

    lax.fori_loop(0, seqs, branch_rows, 0)

    def load_x(s):
        return [pltpu.make_async_copy(xr_hbm.at[s, :, pl.ds(k * half, half)], rows_v.at[k], load_sem.at[8 + k]) for k in range(2)]

    for copy in load_x(0):
        copy.start()
    for copy in load_att:
        copy.wait()

    scale = log2e / math.sqrt(hd)
    back = 1.0 / math.sqrt(hd)
    krow = lax.broadcasted_iota(jnp.int32, (block, groups * block), 0)
    qcol = lax.broadcasted_iota(jnp.int32, (block, groups * block), 1) % block
    base = groups * hd

    def attention(s):
        give(s).wait_recv()
        low, high = join_positions(core, da_own[s], da_got[s])
        da_all[:, :span] = low
        da_all[:, span:] = high
        length = len_ref[s]
        grads[base:, :] = jnp.zeros((2 * hd, slots), F32)
        for i in range(slots // block):
            cut = slice(i * block, (i + 1) * block)
            q = jnp.concatenate([all_v[s, g * hd : (g + 1) * hd, cut] for g in range(groups)], axis=1)
            da = jnp.concatenate([da_all[g * hd : (g + 1) * hd, cut] for g in range(groups)], axis=1)
            at = jnp.concatenate([att_v[s, g * hd : (g + 1) * hd, cut] for g in range(groups)], axis=1)
            inv = jnp.concatenate([inv_v[s, g : g + 1, cut] for g in range(groups)], axis=1)
            delta = jnp.sum(at.astype(F32) * da.astype(F32), axis=0, keepdims=True)
            dq = jnp.zeros((hd, groups * block), F32)
            for j in range(i + 1):
                kcut = slice(j * block, (j + 1) * block)
                key = all_v[s, base : base + hd, kcut]
                score = dot_tn(key, q) * scale
                ok = (krow + j * block) < length
                if j == i:
                    ok = ok & (krow <= qcol)
                p = jnp.where(ok, jnp.exp2(score) * inv, 0.0)
                dp = dot_tn(all_v[s, base + hd : base + 2 * hd, kcut], da)
                ds = (p * (dp - delta)).astype(BF16)
                dq = dq + dot_nn(key, ds)
                grads[base : base + hd, kcut] += dot_nt(q, ds) * back
                grads[base + hd : base + 2 * hd, kcut] += dot_nt(da, p.astype(BF16))
            dq = dq * back
            for g in range(groups):
                grads[g * hd : (g + 1) * hd, cut] = dq[:, g * block : (g + 1) * block]
        mine, theirs = join_positions(core, grads[:, :span], grads[:, span:])
        d_own[s] = mine.astype(BF16)
        d_send[s] = theirs.astype(BF16)
        exchange(s).start()

    quarter = hd // 2
    cosine, sine = table_ref[:quarter, :], table_ref[quarter : 2 * quarter, :]
    qgain, kgain = table_ref[2 * quarter : 2 * quarter + hd, 0:1], table_ref[2 * quarter + hd :, 0:1]
    sides = (nq // 2, nk // 2, nk // 2)
    copies_in_tensor = 1.0 / lax.axis_size("tensor")
    lines_v[:8, :] = jnp.zeros((8, width), F32)
    lines_v[8:, :] = gain2_ref[...] * copies_in_tensor
    heads_v[...] = jnp.zeros_like(heads_v)
    valid_slots = jnp.int32(0)
    for s in range(seqs):
        valid_slots = valid_slots + jnp.clip(len_ref[s] - start, 0, span)
    count = valid_slots.astype(F32) * (copies_in_tensor / 128.0)
    small_v[...] = jnp.zeros_like(small_v)
    for k in range(2):
        both = stat_ref[k] + stat2_ref[k]
        small_v[1 + k : 2 + k, :] = jnp.sum(both, axis=0, keepdims=True) * copies_in_tensor
    small_v[4:5, :] = jnp.broadcast_to(count, (1, 128))
    load_qkvw.wait()

    def fold_columns(values):
        return sum(values[:, k * 128 : (k + 1) * 128] for k in range(values.shape[1] // 128))

    def heads_rows(s):
        exchange(s).wait_recv()
        low, high = join_positions(core, d_own[s].astype(F32), d_got[s].astype(F32))
        parts = [[], [], []]
        for side in (low, high):
            at = 0
            for kind, number in enumerate(sides):
                for _ in range(number):
                    parts[kind].append(side[at : at + hd])
                    at += hd
        done = []
        for h in range(nq + nk):
            kind = 0 if h < nq else 1
            g = parts[kind][h - kind * nq]
            a, b = g[: hd // 2], g[hd // 2 :]
            g = jnp.concatenate([a * cosine + b * sine, b * cosine - a * sine], axis=0)
            v = pre_v[s, h * hd : (h + 1) * hd, :]
            inv = lax.rsqrt(jnp.mean(v * v, axis=0, keepdims=True) + epsilon)
            hat = v * inv
            heads_v[kind * hd : (kind + 1) * hd, :] += fold_columns(g * hat)
            gg = g * (qgain if kind == 0 else kgain)
            done.append(inv * (gg - hat * jnp.mean(gg * hat, axis=0, keepdims=True)))
        done += parts[2]
        for h in range(nq + 2 * nk):
            pair = h % 2
            if pair == 0:
                two = jnp.concatenate([done[h], done[h + 1]], axis=0).T.astype(BF16)
                dpre_v[pl.ds(pl.multiple_of(s * span, span), span), h * hd : (h + 2) * hd] = two
        for copy in load_x(s):
            copy.wait()
        for m in range(4):
            rows = slice(m * share, (m + 1) * share)
            xs = [rows_v[k, rows, :].astype(F32) for k in range(2)]
            mean = sum(jnp.sum(x * x, axis=-1, keepdims=True) for x in xs) * (1.0 / width)
            inv = lax.rsqrt(mean + epsilon)
            dpre = dpre_v[pl.ds(pl.multiple_of(s * span + m * share, share), share), :]
            for k in range(2):
                part = dot_nt(dpre, qkvw_v[k])
                cut = slice(k * half, (k + 1) * half)
                first_v[s, m, :, cut] = part.astype(BF16)
                both = part * (xs[k] * inv)
                lines_v[:8, cut] += sum(both[8 * r : 8 * r + 8] for r in range(share // 8))

    def sequence(s, carry):
        attention(s)

        @pl.when(s == last)
        def _():
            s_up.pass_on()
            ffn_step(1, 1)

        heads_rows(s)

        @pl.when(s == 0)
        def _():
            for copy in load_x(1):
                copy.start()
            first_rings[0].begin()
            ffn_step(0, 1)
            s_down.begin()

        @pl.when(s == last)
        def _():
            first_rings[1].begin()

        return carry

    lax.fori_loop(0, seqs, sequence, 0)

    def hop_copies(n, items):
        return [remote(src, dst, smsend.at[n, i], smrecv.at[n, i], device) for i, (device, src, dst, _) in enumerate(items)]

    def hop_begin(n, items):
        for copy in hop_copies(n, items):
            copy.start()

    def hop_end(n, items):
        for copy in hop_copies(n, items):
            copy.wait()
        for _, _, dst, place_to in items:
            if place_to is None:
                small_v[...] += dst[...]
            else:
                lines_v[:, place_to] += dst[...]

    piece = width // 8

    def columns(k):
        return slice(k * piece, (k + 1) * piece)

    def view(k, count=1):
        return lines_v.at[:, pl.ds(k * piece, count * piece)]

    hop_core = [(near_core, view(4, 4), lin1, slice(0, half))]
    near_all = [near_x, near_y, {"dp": near[3]}]
    hop_lines = [(near_all[k], view(1 + k), lin2.at[k], columns(0)) for k in range(3)]
    hop_small = [(near_core, small_v, small_r.at[0], None)]
    hop_square = [(near_all[k], small_v, small_r.at[1 + k], None) for k in range(3)]
    z_all = [z_right, z_far, z_left]
    hop_chain = [(z_all[k], view(0), lin3.at[k], columns(0)) for k in range(3)]
    hop_chain += [(z_all[k], small_v, small_r.at[4 + k], None) for k in range(3)]
    hop_begin(0, hop_core)

    load_tok.wait()
    blocks_o = [remote(so_v.at[k], go_v.at[k], osend.at[k], orecv.at[k], near_core) for k in range(4)]
    size_o = half // 4
    for k in range(4):
        cut = slice(half + k * size_o, half + (k + 1) * size_o)
        so_v[k] = dot_tn(tok_v[...], act_v[:, cut]).astype(BF16)
        blocks_o[k].start()
    for k in range(4):
        blocks_o[k].wait_recv()
        cut = slice(k * size_o, (k + 1) * size_o)
        go_v[k] = (dot_tn(tok_v[...], act_v[:, cut]) + go_v[k].astype(F32)).astype(BF16)
    s_out.begin()
    load_n1 = load(0, n1_hbm, act_v)
    hop_end(0, hop_core)
    hop_begin(1, hop_lines)
    load_n1.wait()
    blocks_q = [remote(sq_v.at[k], gq_v.at[k], qsend.at[k], qrecv.at[k], near_core) for k in range(4)]
    size_q = half // 4
    for k in range(4):
        cut = slice(half + k * size_q, half + (k + 1) * size_q)
        sq_v[k] = dot_tn(act_v[:, cut], dpre_v[...]).astype(BF16)
        blocks_q[k].start()
    for k in range(4):
        blocks_q[k].wait_recv()
        cut = slice(k * size_q, (k + 1) * size_q)
        gq_v[k] = (dot_tn(act_v[:, cut], dpre_v[...]) + gq_v[k].astype(F32)).astype(BF16)
    s_qkv.begin()
    keeps = [
        pltpu.make_async_copy(go_v.at[0], mine_o, own_sem.at[0]),
        pltpu.make_async_copy(gq_v.at[0], mine_q, own_sem.at[1]),
    ]
    keeps += [pltpu.make_async_copy(first_v.at[s, rank], own_hbm.at[s], own_sem.at[2 + s]) for s in range(seqs)]
    for copy in keeps:
        copy.start()


    def place(tile, dst, s):
        copies = []
        for o in range(2):
            for k in range(4):
                b = near[k] * 2 + (core if o == 0 else 1 - core)
                cut = pl.ds(pl.multiple_of(b * piece, piece), piece)
                copies.append(
                    pltpu.make_async_copy(tile.at[:, pl.ds((o * 4 + k) * piece, piece)], dst.at[s, :, cut], outs_sem.at[o * 4 + k])
                )
        return copies

    def out_share(s):
        keep = pltpu.make_async_copy(hidden_hbm.at[piece_rows(s, rank), :], tile_v, tile_sem.at[0])
        keep.start()
        ffn_rings[s].arrived()
        read = ffn_rings[s].own(rank)
        keep.wait()

        def body(cut, first):
            ffn = slots_v[s, 2, cut, :].astype(F32) + read(cut).astype(F32)
            otile_v[cut, :] = (tile_v[cut, :] + ffn).astype(BF16)
            spot = start + rank * share + first + lax.broadcasted_iota(jnp.int32, (16, 1), 0)
            valid = (spot < len_ref[s]).astype(F32)
            small_v[3:4, :] += jnp.sum(fold_lanes(valid * ffn * ffn), axis=0, keepdims=True)

        by_pieces(share, body)
        copies = place(otile_v, out_hbm, s)
        for copy in copies:
            copy.start()
        for copy in copies:
            copy.wait()

    small_v[0:1, :] = jnp.sum(heads_v[...].T, axis=0, keepdims=True)
    ffn_step(0, 2)
    ffn_step(1, 2)
    first_rings[0].step(1)
    s_down.pass_on()
    first_rings[1].step(1)
    s_out.pass_on()
    s_qkv.pass_on()
    hop_end(1, hop_lines)
    out_share(0)
    out_share(1)
    hop_begin(2, hop_small)
    hop_end(2, hop_small)
    hop_begin(3, hop_square)
    hop_end(3, hop_square)
    hop_begin(4, hop_chain)
    first_rings[0].step(2)
    first_rings[1].step(2)
    hop_end(4, hop_chain)
    lines_out[...] = lines_v[:, :piece]
    small_out[...] = small_v[...]
    for item in (s_up, s_down, s_out, s_qkv):
        item.arrived()
    for ring in first_rings:
        ring.arrived()
    for copy in keeps:
        copy.wait()
    for ring in ffn_rings + first_rings:
        ring.settle()
    for item in (s_up, s_down, s_out, s_qkv):
        item.settle()
    for copy in blocks_o + blocks_q:
        copy.wait_send()
    for s in range(seqs):
        give(s).wait_send()
        exchange(s).wait_send()


def backward(
    lengths, gb, hidden_rows, ffn, xr, n1, tok, outw, qkvw, everything, att, inv, pre, dup, ddown,
    table, stat, stat2, gain2_part, hd, nq, nk,
):
    seqs, span, width = xr.shape
    half = width // 2
    groups = nq // nk
    share = span // 4
    piece = width // 8
    hidden = dup.shape[1]
    cols = qkvw.shape[2]
    feat = nq * hd
    block = min(256, span)
    any_space = pl.BlockSpec(memory_space=pl.ANY)
    vmem = pl.BlockSpec(memory_space=pltpu.VMEM)
    dma = pltpu.SemaphoreType.DMA
    hold = lambda *dims: pltpu.VMEM(dims, BF16)
    wide = lambda *dims: pltpu.VMEM(dims, F32)
    big = [shape((seqs, share, width), BF16)] * 3 + [shape((feat, piece), BF16), shape((piece, cols), BF16)]
    big += [shape((piece, hidden), BF16)] * 2 + [shape((hidden, piece), BF16)] * 2
    big += [shape((feat, piece), BF16)] * 2 + [shape((piece, cols), BF16)] * 2
    small = [shape((16, piece), F32), shape((8, 128), F32)]
    rows = everything.shape[1]
    scratch = [
        hold(seqs * span, width), hold(2, span, half), hold(2, half, cols), hold(seqs * span, feat), hold(*everything.shape), hold(*att.shape),
        wide(*inv.shape), wide(*pre.shape), wide(rows, 2 * span), hold(groups * hd, 2 * span),
        hold(seqs, feat // 2, span), hold(seqs, feat // 2, span), hold(seqs, feat // 2, span),
        hold(seqs, rows, span), hold(seqs, rows, span), hold(seqs, rows, span), hold(seqs * span, cols),
        hold(seqs, 4, share, width), hold(2 * seqs, 3, share, width), hold(seqs, share, width),
        hold(2, piece // 2, hidden), hold(2, hidden // 2, piece), hold(2, piece // 2, hidden), hold(2, hidden // 2, piece),
        hold(4, feat, piece), hold(4, feat, piece), hold(2, feat // 2, piece), hold(2, feat // 2, piece),
        hold(4, piece, cols), hold(4, piece, cols), hold(2, piece // 2, cols), hold(2, piece // 2, cols),
        wide(share, width), hold(share, width),
        wide(16, width), wide(8, 128), wide(2 * hd, 128), wide(16, half), wide(3, 16, piece), wide(3, 16, piece), wide(7, 8, 128),
        dma((10,)), dma((2 * seqs, 3)), dma((2 * seqs, 3)), dma((seqs,)), dma((4, 6)), dma((4, 6)), dma((4, 3)), dma((2 + seqs,)),
        dma((2, seqs)), dma((2, seqs)), dma((4,)), dma((4,)), dma((4,)), dma((4,)), dma((2,)), dma((8,)), dma((5, 6)), dma((5, 6)),
    ]
    tokens = seqs * span
    return pl.pallas_call(
        functools.partial(backward_kernel, hd, nq, nk, block),
        in_specs=[SMEM] + [any_space] * 14 + [vmem] * 4,
        out_specs=[any_space] * len(big) + [vmem] * 2,
        out_shape=big + small,
        scratch_shapes=scratch,
        compiler_params=pltpu.CompilerParams(vmem_limit_bytes=VMEM_MOST, collective_id=3, has_side_effects=True),
        cost_estimate=cost(4 * tokens * width * (cols + feat), 60 * tokens * width),
        name="attention_backward",
    )(
        lengths, gb, hidden_rows, ffn, xr, n1, tok, outw, qkvw, everything, att, inv, pre, dup, ddown,
        table, stat, stat2, gain2_part,
    )


def results_kernel(
    hd, nqc, nkc, count, scal_ref, dgate, lx0, ly0, dup, lx1, ly1, ddown, lx2, ly2, mine_o, lx3, ly3, mine_q, lx4, ly4,
    gh_ref, x_ref, fin_ref, own_ref, out_ref, gains_ref, lines_ref, small_ref,
    output, gin, ggate, gup, gdown, gout, gq, gk, gv, gain_a, gain_b, gain_q, gain_k, rms,
):
    def add(*refs):
        return sum(ref[...].astype(F32) for ref in refs)

    ggate[...] = add(dgate, lx0, ly0)
    gup[...] = add(dup, lx1, ly1)
    gdown[...] = add(ddown, lx2, ly2)
    gout[...] = add(mine_o, lx3, ly3)
    qkv = add(mine_q, lx4, ly4)
    gq[...] = qkv[:, :nqc]
    gk[...] = qkv[:, nqc : nqc + nkc]
    gv[...] = qkv[:, nqc + nkc :]
    output[...] = out_ref[...]
    width = x_ref.shape[-1]
    piece = width // 8
    rows = x_ref.shape[1]
    gain = jnp.concatenate([gains_ref[b, 0:1, :] for b in range(8)], axis=1).astype(F32)
    for r in range(0, rows, 16):
        cut = slice(r, r + 16)
        e = fin_ref[0, cut, :].astype(F32) + own_ref[0, cut, :].astype(F32)
        x = x_ref[0, cut, :].astype(F32)
        inv = inverse_rms(x)
        hat = x * inv
        eg = e * gain
        value = gh_ref[0, cut, :] + inv * (eg - hat * jnp.mean(eg * hat, axis=-1, keepdims=True))
        for k in range(8):
            gin[0, cut, pl.ds(pl.multiple_of(scal_ref[1 + k] * piece, piece), piece)] = value[:, k * piece : (k + 1) * piece]

    @pl.when(pl.program_id(0) == 0)
    def _():
        first = jnp.sum(lines_ref[:8, :], axis=0, keepdims=True)
        second = jnp.sum(lines_ref[8:, :], axis=0, keepdims=True)
        gain_a[...] = first.reshape(gain_a.shape)
        gain_b[...] = second.reshape(gain_b.shape)
        gain_q[...] = small_ref[0:1, :hd].reshape(gain_q.shape)
        gain_k[...] = small_ref[0:1, hd : 2 * hd].reshape(gain_k.shape)
        totals = [jnp.sum(small_ref[k, :]) for k in range(1, 5)]
        for k in range(3):
            rms[k] = totals[k] / (totals[3] * count)


def finish_results(rank, ids, pairs, mine_o, mine_q, lands_o, lands_q, gh, xr, fin, own, out, gains, lines, small, hd, nqc, nkc):
    (dgate, lx0, ly0), (dup, lx1, ly1), (ddown, lx2, ly2) = pairs
    steps = 8
    seqs, share, width = out.shape
    hidden = dgate.shape[1]
    piece = width // 8
    per = steps // seqs
    rows = share // per
    wide = lambda h, w: pl.BlockSpec((h, w), lambda i, s: (i, 0))
    token = pl.BlockSpec((1, rows, width), lambda i, s: (i // per, i % per, 0))
    mine = pl.BlockSpec((1, rows, width), lambda i, s: (i // per, s[0] * per + i % per, 0))
    fixed = lambda a: pl.BlockSpec(a.shape, lambda i, s: (0,) * a.ndim)
    g = wide(piece // steps, hidden)
    d = wide(hidden // steps, piece)
    o = wide(mine_o.shape[0] // steps, piece)
    q = wide(piece // steps, mine_q.shape[1])
    outs = [
        (shape(out.shape, BF16), token), (shape(out.shape, F32), token), (shape((piece, hidden), F32), g), (shape((piece, hidden), F32), g),
        (shape((hidden, piece), F32), d), (shape(mine_o.shape, F32), o), (shape((piece, nqc), F32), wide(piece // steps, nqc)),
        (shape((piece, nkc), F32), wide(piece // steps, nkc)), (shape((piece, nkc), F32), wide(piece // steps, nkc)),
        *[(shape((size,), F32), pl.BlockSpec((size,), lambda i, s: (0,))) for size in (piece, piece, hd, hd)],
        (shape((3,), F32), pl.BlockSpec(memory_space=pltpu.SMEM)),
    ]
    scalars = jnp.concatenate([rank.astype(jnp.int32).reshape(1), ids])
    return pl.pallas_call(
        functools.partial(results_kernel, hd, nqc, nkc, float(width)),
        grid_spec=pltpu.PrefetchScalarGridSpec(
            num_scalar_prefetch=1,
            grid=(steps,),
            in_specs=[g] * 6 + [d] * 3 + [o] * 3 + [q] * 3 + [token, mine, token, token, token, fixed(gains), fixed(lines), fixed(small)],
            out_specs=[spec for _, spec in outs],
        ),
        out_shape=[kind for kind, _ in outs],
        compiler_params=PARAMS,
        cost_estimate=cost(30 * piece * hidden, 60 * piece * hidden),
        name="results",
    )(scalars, dgate, lx0, ly0, dup, lx1, ly1, ddown, lx2, ly2, mine_o, *lands_o, mine_q, *lands_q, gh, xr, fin, own, out, gains, lines, small)


def per_device_general(
    inputs,
    cotangent,
    lengths,
    w_query,
    key_projection_weight,
    value_projection_weight,
    w_output,
    w_gate,
    w_up,
    w_down,
    attn_gain,
    ffn_gain,
    query_gain,
    key_gain,
):
    seqs, span, width = inputs.shape
    hd = query_gain.shape[0]
    nq = w_query.shape[1] // hd
    nk = key_projection_weight.shape[1] // hd
    groups = nq // nk
    dp = lax.axis_size("dp")
    tensor = lax.axis_size("tensor")
    core = lax.axis_index("context")
    rank = lax.axis_index("tensor")
    chunks = 2
    rows = span // chunks
    share = span // tensor
    lengths = lengths.astype(jnp.int32)
    start = (core * span).astype(jnp.int32)
    core1 = core.astype(jnp.int32).reshape(1)
    ids = block_order(dp, core)
    order = 2 * dp if (width // (2 * dp)) % 128 == 0 else 1

    positions = start + jnp.arange(span, dtype=jnp.int32)
    freqs = rope_base ** (-(jnp.arange(hd // 2, dtype=F32) * (2.0 / hd)))
    angles = freqs[:, None] * positions.astype(F32)[None, :]
    cosine, sine = jnp.cos(angles), jnp.sin(angles)
    qgain = query_gain.astype(F32).reshape(hd, 1)
    kgain = key_gain.astype(F32).reshape(hd, 1)

    w_qkv = jnp.concatenate([w_query, key_projection_weight, value_projection_weight], axis=1)
    saved = []
    gains = gather_blocks(jnp.stack([attn_gain, ffn_gain]), 1)
    gains = jnp.concatenate([gains[0], gains[1]], axis=1).astype(F32)
    gain1, gain2 = gains[0:1], gains[1:2]
    qkv = gather_blocks(w_qkv, 0)
    out_w = gather_blocks(w_output, 1)
    gate = gather_blocks(w_gate, 0)
    up = gather_blocks(w_up, 0)
    down = gather_blocks(w_down, 1)

    scal = jnp.concatenate([lengths, start.reshape(1), ids])
    x_in, cot_in = inputs, cotangent
    if order == 1:
        x_in, cot_in = to_relative(x_in, dp, core), to_relative(cot_in, dp, core)
    xr, n1, gf = begin(x_in, cot_in, gain1, scal, order)

    parts, tok = [], []
    for s in range(seqs):
        pre, own, oth = heads(n1, s, qkv, cosine, sine, qgain, kgain, core1, hd, nq, nk)
        seq_scal = jnp.stack([lengths[s], core.astype(jnp.int32)])
        everything, att, inv, mine, theirs = attend(seq_scal, own, over_core(oth), groups)
        branched = branch(mine, over_core(theirs), out_w, core1, chunks)
        saved.append((pre, everything, att, inv, seq_scal))
        tok.append(jnp.swapaxes(branched[0], 0, 1))
        parts.append(branched[1:])
    tok = jnp.concatenate(tok, axis=0)

    stats = jnp.zeros((2,), F32)
    hidden_all, n2_all = [], []
    for s in range(seqs):
        for k in range(chunks):
            terms = [lax.psum(parts[s][k], "tensor")]
            place = jnp.stack([lengths[s], start + k * rows])
            hidden, n2, stat = second_norm(place, xr, s, k, gain2, terms)
            hidden_all.append(hidden)
            n2_all.append(n2)
            stats = stats + stat[:2, 0]
    hidden_all, n2_all = jnp.concatenate(hidden_all), jnp.concatenate(n2_all)

    ffn_squares = jnp.zeros((), F32)
    out_shares = []

    def piece_of(arrays):
        per = arrays[0].shape[0] // share

        def piece(k):
            found = lax.dynamic_slice_in_dim(arrays[0], jnp.minimum(k, per - 1) * share, share, 0)
            for m in range(1, len(arrays)):
                here = lax.dynamic_slice_in_dim(arrays[m], jnp.clip(k - m * per, 0, per - 1) * share, share, 0)
                found = jnp.where(k >= m * per, here, found)
            return found

        return piece

    def share_scalars(s):
        head = jnp.stack([rank.astype(jnp.int32), lengths[s], start + rank.astype(jnp.int32) * share, jnp.int32(tensor)])
        return jnp.concatenate([head, ids])

    def flat(nested):
        return [item for inner_list in nested for item in inner_list]

    def slices(array, count):
        size = array.shape[0] // count
        return [array[i * size : (i + 1) * size] for i in range(count)]

    def reduced(lefts, rights, axis):
        oth = weight_grad(lefts, rights, 1, axis)
        own = weight_grad(lefts, rights, 0, axis, over_core(oth))
        return scatter_blocks(own, axis)

    inner, gg, gu, ffn, gn = [[[None] * chunks for _ in range(seqs)] for _ in range(5)]
    for s in range(seqs):
        for k in range(chunks):
            inner[s][k], gg[s][k], gu[s][k], ffn[s][k], gn[s][k] = feed(
                n2_all, s * chunks + k, rows, gf, s, k, gate, up, down
            )
    gain2_grad = jnp.zeros((1, width), F32)
    gb, gh = [[[None] * chunks for _ in range(seqs)] for _ in range(2)]
    for s in range(seqs):
        for k in range(chunks):
            terms = [lax.psum(gn[s][k], "tensor")]
            gb[s][k], gh[s][k], gain_part = second_back(hidden_all, s * chunks + k, gf, s, k, gain2, terms)
            gain2_grad = gain2_grad + gain_part
    gf_list = slices(gf.reshape(seqs * span, width), seqs * chunks)
    n2_list = slices(n2_all, seqs * chunks)
    grad_w_down = reduced(flat(inner), gf_list, 1)
    grad_w_gate = reduced(n2_list, flat(gg), 0)
    grad_w_up = reduced(n2_list, flat(gu), 0)
    for s in range(seqs):
        got = ring_scatter(piece_of(ffn[s]), tensor, rank)
        halves = [hidden_all[(s * chunks + k) * rows : (s * chunks + k + 1) * rows] for k in range(chunks)]
        out, stat = output_share(share_scalars(s), got, ffn[s], halves, order)
        out_shares.append(out)
        ffn_squares = ffn_squares + stat[0, 0]

    gain1_grad = jnp.zeros((1, width), F32)
    head_gain = jnp.zeros((2 * hd,), F32)
    dpres, in_shares = [], []
    for s in range(seqs):
        pre, everything, att, inv, seq_scal = saved[s]
        da_own, da_oth = branch_back(gb[s], out_w, core1)
        d_own, d_oth = attend_back(seq_scal, everything, att, inv, da_own, over_core(da_oth), groups)
        dpre, first, gain_part, hg = heads_back(
            d_own, over_core(d_oth), pre, cosine, sine, qgain, kgain, xr, s, qkv, core1, hd, nq, nk
        )
        gain1_grad = gain1_grad + gain_part
        head_gain = head_gain + hg[:, 0]
        dpres.append(dpre)
        got = ring_scatter(piece_of([first]), tensor, rank)
        in_shares.append(input_share(share_scalars(s), got, first, gh[s], xr, s, gain1, order))

    att_list = [tok[i * rows : (i + 1) * rows] for i in range(seqs * chunks)]
    grad_w_output = reduced(att_list, flat(gb), 1)
    grad_qkv = reduced([n1[s] for s in range(seqs)], dpres, 0)
    nqc, nkc = nq * hd, nk * hd
    grad_w_query = grad_qkv[:, :nqc]
    grad_w_key = grad_qkv[:, nqc : nqc + nkc]
    grad_w_value = grad_qkv[:, nqc + nkc :]

    gain2_grad = gain2_grad / tensor
    counts = jnp.sum(jnp.clip(lengths - start, 0, span)).astype(F32) / tensor
    small = jnp.concatenate([head_gain, stats / tensor, ffn_squares.reshape(1), counts.reshape(1)])
    small = jnp.pad(small, (0, (-small.shape[0]) % 128)).reshape(1, -1)
    lines = jnp.concatenate([gain1_grad, gain2_grad], axis=0)
    piece = width // (2 * dp)
    lines = to_absolute(lines, dp, core)
    lines, small = lax.psum((lines, small), ("dp", "context", "tensor"))
    lines = lax.dynamic_slice_in_dim(lines, lax.axis_index(("dp", "context")) * piece, piece, 1)
    small = small[0]
    rms_values = jnp.sqrt(small[2 * hd : 2 * hd + 3] / (small[2 * hd + 3] * width))

    output = jnp.stack(out_shares)
    grad_inputs = jnp.stack(in_shares)
    if order == 1:
        output, grad_inputs = to_absolute(output, dp, core), to_absolute(grad_inputs, dp, core)
    return (
        output,
        grad_inputs,
        grad_w_query,
        grad_w_key,
        grad_w_value,
        grad_w_output,
        grad_w_gate,
        grad_w_up,
        grad_w_down,
        lines[0],
        lines[1],
        small[:hd],
        small[hd : 2 * hd],
        rms_values,
    )


def per_device_square(
    inputs,
    cotangent,
    lengths,
    w_query,
    key_projection_weight,
    value_projection_weight,
    w_output,
    w_gate,
    w_up,
    w_down,
    attn_gain,
    ffn_gain,
    query_gain,
    key_gain,
):
    seqs, span, width = inputs.shape
    hd = query_gain.shape[0]
    nq = w_query.shape[1] // hd
    nk = key_projection_weight.shape[1] // hd
    lengths = lengths.astype(jnp.int32)
    all_gains = jnp.concatenate([attn_gain, ffn_gain, query_gain, key_gain]).reshape(1, -1)
    (
        xr, n1, gf, qkv, out_w, gate, up, down, hidden, n2, rest, gi, pre, everything, att, tok, gains, table, inv, stat
    ) = forward(
        lengths, inputs, cotangent, w_query, key_projection_weight, value_projection_weight, w_output, w_gate, w_up, w_down,
        all_gains, hd, nq, nk,
    )
    tokens = seqs * span
    flat = lambda a: a.reshape(tokens, -1)
    ffn, gb, gh, d_gate, d_up, d_down, hidden, landx, landy, gain2_part, stat2 = feed_both(
        lengths, n2, flat(gf), gate, up, down, gi, rest, flat(xr), hidden, gains
    )
    output, fin, own, mine_o, mine_q, lx1, ly1, lx2, ly2, lx3, ly3, lx4, ly4, lines, small = backward(
        lengths, gb, hidden, ffn, xr, flat(n1), flat(tok), out_w, qkv,
        everything, att, inv, pre, d_up, d_down, table, stat, stat2, gain2_part, hd, nq, nk,
    )
    row, core = lax.axis_index("dp"), lax.axis_index("context")
    near = [row, xor_one(row), (row + 2) % 4, 3 - row]
    ids = jnp.stack([near[k] * 2 + (core if o == 0 else 1 - core) for o in range(2) for k in range(4)]).astype(jnp.int32)
    nqc, nkc = nq * hd, nk * hd
    pairs = ((d_gate, landx, landy), (d_up, lx1, ly1), (d_down, lx2, ly2))
    output, grad_inputs, grad_gate, grad_up, grad_down, grad_out, grad_q, grad_k, grad_v, *small = finish_results(
        lax.axis_index("tensor"), ids, pairs, mine_o, mine_q, (lx3, ly3), (lx4, ly4), gh, xr, fin, own, output, gains,
        lines, small, hd, nqc, nkc,
    )
    return (output, grad_inputs, grad_q, grad_k, grad_v, grad_out, grad_gate, grad_up, grad_down, *small[:4], jnp.sqrt(small[4]))


def per_device(*args):
    inputs, w_query = args[0], args[3]
    seqs, span, width = inputs.shape
    square = lax.axis_size("dp") == 4 and lax.axis_size("tensor") == 4 and lax.axis_size("context") == 2
    if square and width % 2048 == 0 and span % 512 == 0 and seqs == 2 and w_query.shape[1] == span:
        return per_device_square(*args)
    return per_device_general(*args)


def solution(mesh):
    both = ("dp", "context")
    rows = P(both, "tensor")
    cols = P("tensor", both)
    shares = P("dp", ("context", "tensor"), None)
    acts = P("dp", "context", None)
    return jax.shard_map(
        per_device,
        mesh=mesh,
        in_specs=(acts, acts, P("dp"), rows, rows, rows, cols, rows, rows, cols, P(both), P(both), P(), P()),
        out_specs=(shares, shares, rows, rows, rows, cols, rows, rows, cols, P(both), P(both), P(), P(), P()),
        check_vma=False,
    )
```

```python
import functools
import math

import jax
import jax.numpy as jnp
from jax import lax
from jax.experimental import pallas as pl
from jax.experimental.pallas import tpu as pltpu
from jax.sharding import PartitionSpec as P

F32 = jnp.float32
BF16 = jnp.bfloat16
epsilon = 1e-05
rope_base = 1000000.0
log2e = 1.4426950408889634
VMEM_BYTES = 60 * 1024 * 1024
VMEM_MOST = 63 * 1024 * 1024
PARAMS = pltpu.CompilerParams(vmem_limit_bytes=VMEM_BYTES)
SMEM = pl.BlockSpec(memory_space=pltpu.SMEM)
SWAP = ((0, 1), (1, 0))


def shape(dims, dtype):
    return jax.ShapeDtypeStruct(tuple(dims), dtype)


def cost(flops, size, exps=0):
    return pl.CostEstimate(flops=int(flops), bytes_accessed=int(size), transcendentals=int(exps))


def dot_nn(a, b):
    return lax.dot_general(a, b, (((1,), (0,)), ((), ())), preferred_element_type=F32)


def dot_nt(a, b):
    return lax.dot_general(a, b, (((1,), (1,)), ((), ())), preferred_element_type=F32)


def dot_tn(a, b):
    return lax.dot_general(a, b, (((0,), (0,)), ((), ())), preferred_element_type=F32)


def inverse_rms(values):
    return lax.rsqrt(jnp.mean(values * values, axis=-1, keepdims=True) + epsilon)


def block_order(dp, core):
    return jnp.stack([jnp.int32(k) * 2 + (core ^ o) for o in range(2) for k in range(dp)]).astype(jnp.int32)


def to_relative(values, dp, core):
    lead = values.shape[:-1]
    parts = values.reshape(lead + (dp, 2, -1))
    parts = jnp.where(core == 0, parts, parts[..., ::-1, :])
    return jnp.swapaxes(parts, -3, -2).reshape(values.shape)


def to_absolute(values, dp, core):
    lead = values.shape[:-1]
    parts = jnp.swapaxes(values.reshape(lead + (2, dp, -1)), -3, -2)
    return jnp.where(core == 0, parts, parts[..., ::-1, :]).reshape(values.shape)


def over_core(value):
    return lax.ppermute(value, "context", SWAP)


def gather_blocks(weight, axis):
    own = lax.all_gather(weight, "dp", axis=axis, tiled=True)
    return jnp.stack([own, over_core(own)])


def scatter_blocks(total, axis):
    return lax.psum_scatter(total, "dp", scatter_dimension=axis, tiled=True).astype(F32)


def ring_scatter(piece, tensor, rank):
    ring = [(i, (i + 1) % tensor) for i in range(tensor)]
    moving = piece((rank + tensor - 1) % tensor)
    for step in range(1, tensor):
        moving = lax.ppermute(moving, "tensor", ring)
        if step < tensor - 1:
            moving = (moving.astype(F32) + piece((rank + tensor - 1 - step) % tensor).astype(F32)).astype(BF16)
    return moving


def begin_kernel(order, x_ref, cot_ref, gain_ref, scal_ref, xr_ref, n1_ref, gf_ref):
    seq, tile = pl.program_id(0), pl.program_id(1)
    rows, width = x_ref.shape[1:]
    seqs = pl.num_programs(0)
    place = scal_ref[seqs] + tile * rows + lax.broadcasted_iota(jnp.int32, (rows, 1), 0)
    valid = (place < scal_ref[seq]).astype(F32)
    x = x_ref[0].astype(F32)
    inv = inverse_rms(x)
    piece = width // order
    for k in range(order):
        src = pl.ds(pl.multiple_of(scal_ref[seqs + 1 + k] * piece, piece), piece) if order > 1 else slice(0, width)
        dst = slice(k * piece, (k + 1) * piece)
        part = x_ref[0, :, src]
        xr_ref[0, :, dst] = part
        n1_ref[0, :, dst] = (part.astype(F32) * inv * gain_ref[:, dst]).astype(BF16)
        gf_ref[0, :, dst] = (cot_ref[0, :, src].astype(F32) * valid).astype(BF16)


def begin(x, cot, gain, scalars, order):
    seqs, span, width = x.shape
    rows = min(256, span)
    spec = pl.BlockSpec((1, rows, width), lambda s, i: (s, i, 0))
    return pl.pallas_call(
        functools.partial(begin_kernel, order),
        grid=(seqs, span // rows),
        in_specs=[spec, spec, pl.BlockSpec((1, width), lambda s, i: (0, 0)), SMEM],
        out_specs=[spec] * 3,
        out_shape=[shape(x.shape, BF16)] * 3,
        compiler_params=PARAMS,
        cost_estimate=cost(8 * x.size, 10 * x.size),
        name="first_norm",
    )(x, cot, gain, scalars)


def heads_kernel(hd, nq, nk, n1_ref, w_ref, cos_ref, sin_ref, qg_ref, kg_ref, core_ref, pre_ref, own_ref, oth_ref):
    half = w_ref.shape[1]
    x = n1_ref[0]
    flat = dot_nn(x[:, :half], w_ref[0]) + dot_nn(x[:, half:], w_ref[1])
    turned = flat.T
    span = turned.shape[1]
    normed = turned[: (nq + nk) * hd]
    pre_ref[...] = normed
    core = core_ref[0]
    cosine, sine = cos_ref[...], sin_ref[...]
    done = []
    for h in range(nq + nk):
        v = normed[h * hd : (h + 1) * hd]
        inv = lax.rsqrt(jnp.mean(v * v, axis=0, keepdims=True) + epsilon)
        v = v * inv * (qg_ref[...] if h < nq else kg_ref[...])
        a, b = v[: hd // 2], v[hd // 2 :]
        done.append(jnp.concatenate([a * cosine - b * sine, b * cosine + a * sine], axis=0))
    for h in range(nk):
        lo = (nq + nk + h) * hd
        done.append(turned[lo : lo + hd])
    parts = [[], []]
    for start, count in ((0, nq), (nq, nk), (nq + nk, nk)):
        for side in range(2):
            parts[side] += done[start + side * count // 2 : start + (side + 1) * count // 2]
    low = jnp.concatenate(parts[0], axis=0)
    high = jnp.concatenate(parts[1], axis=0)
    first = core == 0
    own_ref[...] = jnp.where(first, low, high).astype(BF16)
    oth_ref[...] = jnp.where(first, high, low).astype(BF16)


def heads(n1, seq, weight, cosine, sine, qgain, kgain, core, hd, nq, nk):
    span, width = n1.shape[1:]
    sides = (nq + 2 * nk) * hd // 2
    full = pl.BlockSpec(memory_space=pltpu.VMEM)
    whole = lambda a: pl.BlockSpec(a.shape, lambda i: (0,) * a.ndim)
    outs = [shape(((nq + nk) * hd, span), F32), shape((sides, span), BF16), shape((sides, span), BF16)]
    return pl.pallas_call(
        functools.partial(heads_kernel, hd, nq, nk),
        grid=(1,),
        in_specs=[pl.BlockSpec((1, span, width), lambda i: (seq, 0, 0))]
        + [whole(a) for a in (weight, cosine, sine, qgain, kgain)]
        + [SMEM],
        out_specs=[whole(o) for o in outs],
        out_shape=outs,
        compiler_params=PARAMS,
        cost_estimate=cost(2 * span * width * weight.shape[2], 2 * span * width + 2 * weight.size),
        name="query_key_value",
    )(n1, weight, cosine, sine, qgain, kgain, core)


def join_positions(core, own, oth):
    first = core == 0
    return jnp.where(first, own, oth), jnp.where(first, oth, own)


def attend_kernel(block, groups, scal_ref, own_ref, got_ref, all_ref, att_ref, inv_ref, ao_ref, ax_ref):
    span = own_ref.shape[1]
    hd = own_ref.shape[0] // (groups + 2)
    length, core = scal_ref[0], scal_ref[1]
    low, high = join_positions(core, own_ref[...], got_ref[...])
    all_ref[:, :span] = low
    all_ref[:, span:] = high
    scale = log2e / math.sqrt(hd)
    krow = lax.broadcasted_iota(jnp.int32, (block, groups * block), 0)
    qcol = lax.broadcasted_iota(jnp.int32, (block, groups * block), 1) % block
    base = groups * hd
    for i in range(2 * span // block):
        cut = slice(i * block, (i + 1) * block)
        q = jnp.concatenate([all_ref[g * hd : (g + 1) * hd, cut] for g in range(groups)], axis=1)
        acc = jnp.zeros((hd, groups * block), F32)
        total = jnp.zeros((1, groups * block), F32)
        for j in range(i + 1):
            kcut = slice(j * block, (j + 1) * block)
            s = dot_tn(all_ref[base : base + hd, kcut], q) * scale
            ok = (krow + j * block) < length
            if j == i:
                ok = ok & (krow <= qcol)
            e = jnp.where(ok, jnp.exp2(s), 0.0)
            total = total + jnp.sum(e, axis=0, keepdims=True)
            acc = acc + dot_nn(all_ref[base + hd : base + 2 * hd, kcut], e.astype(BF16))
        inv = 1.0 / total
        att = (acc * inv).astype(BF16)
        for g in range(groups):
            att_ref[g * hd : (g + 1) * hd, cut] = att[:, g * block : (g + 1) * block]
            inv_ref[g : g + 1, cut] = inv[:, g * block : (g + 1) * block]
    mine, theirs = join_positions(core, att_ref[:, :span], att_ref[:, span:])
    ao_ref[...] = mine
    ax_ref[...] = theirs


def attend(scalars, own, got, groups):
    rows, span = own.shape
    hd = rows // (groups + 2)
    block = min(256, span)
    full = pl.BlockSpec(memory_space=pltpu.VMEM)
    return pl.pallas_call(
        functools.partial(attend_kernel, block, groups),
        in_specs=[SMEM, full, full],
        out_specs=[full] * 5,
        out_shape=[
            shape((rows, 2 * span), BF16),
            shape((groups * hd, 2 * span), BF16),
            shape((groups, 2 * span), F32),
            shape((groups * hd, span), BF16),
            shape((groups * hd, span), BF16),
        ],
        compiler_params=PARAMS,
        cost_estimate=cost(60 * groups * hd * span * span, 12 * rows * span, 4 * groups * span * span),
        name="attend_forward",
    )(scalars, own, got)


def branch_kernel(own_ref, got_ref, w_ref, core_ref, att_ref, *outs):
    half = w_ref.shape[2]
    low, high = join_positions(core_ref[0], own_ref[...], got_ref[...])
    att = jnp.concatenate([low, high], axis=0)
    att_ref[...] = att
    rows = outs[0].shape[0]
    for k, out in enumerate(outs):
        part = att[:, k * rows : (k + 1) * rows]
        out[:, :half] = dot_tn(part, w_ref[0]).astype(BF16)
        out[:, half:] = dot_tn(part, w_ref[1]).astype(BF16)


def branch(own, got, weight, core, chunks):
    rows, span = own.shape
    width = 2 * weight.shape[2]
    full = pl.BlockSpec(memory_space=pltpu.VMEM)
    return pl.pallas_call(
        branch_kernel,
        in_specs=[full] * 3 + [SMEM],
        out_specs=[full] * (1 + chunks),
        out_shape=[shape((2 * rows, span), BF16)] + [shape((span // chunks, width), BF16)] * chunks,
        compiler_params=PARAMS,
        cost_estimate=cost(4 * rows * span * width, 4 * rows * width + 2 * span * width),
        name="attention_branch",
    )(own, got, weight, core)


def second_norm_kernel(terms, scal_ref, x_ref, gain_ref, *refs):
    term_refs, (hidden_ref, n2_ref, stat_ref) = refs[:terms], refs[terms:]
    rows = hidden_ref.shape[0]
    branch_sum = term_refs[0][...].astype(F32)
    for ref in term_refs[1:]:
        branch_sum = branch_sum + ref[...].astype(F32)
    resid = x_ref[0].astype(F32)
    hidden = resid + branch_sum
    hidden_ref[...] = hidden
    n2_ref[...] = (hidden * inverse_rms(hidden) * gain_ref[...]).astype(BF16)
    place = scal_ref[1] + lax.broadcasted_iota(jnp.int32, (rows, 1), 0)
    valid = (place < scal_ref[0]).astype(F32)
    first = jnp.sum(valid * resid * resid, keepdims=True)
    second = jnp.sum(valid * branch_sum * branch_sum, keepdims=True)
    line = lax.broadcasted_iota(jnp.int32, (8, 128), 0)
    stat_ref[...] = jnp.where(line == 0, first, second)


def second_norm(scalars, xr, seq, part, gain, terms):
    rows, width = terms[0].shape
    flat = pl.BlockSpec((rows, width), lambda i: (0, 0))
    return pl.pallas_call(
        functools.partial(second_norm_kernel, len(terms)),
        grid=(1,),
        in_specs=[SMEM, pl.BlockSpec((1, rows, width), lambda i: (seq, part, 0)), pl.BlockSpec((1, width), lambda i: (0, 0))]
        + [flat] * len(terms),
        out_specs=[flat, flat, pl.BlockSpec((8, 128), lambda i: (0, 0))],
        out_shape=[shape((rows, width), F32), shape((rows, width), BF16), shape((8, 128), F32)],
        compiler_params=PARAMS,
        cost_estimate=cost(20 * rows * width, (8 + 2 * len(terms)) * rows * width),
        name="second_norm",
    )(scalars, xr, gain, *terms)


def feed_kernel(n_ref, g_ref, wgo, wgx, wuo, wux, wdo, wdx, inner_ref, gg_ref, gu_ref, ffn_ref, gn_ref, facc, gacc):
    step = pl.program_id(0)
    half = wgo.shape[0]
    no, nx = n_ref[:, :half], n_ref[:, half:]
    gate = dot_nn(no, wgo[...]) + dot_nn(nx, wgx[...])
    up = dot_nn(no, wuo[...]) + dot_nn(nx, wux[...])
    gi = dot_nt(g_ref[0, :, :half], wdo[...]) + dot_nt(g_ref[0, :, half:], wdx[...])
    sig = jax.nn.sigmoid(gate)
    silu = gate * sig
    inner = (silu * up).astype(BF16)
    gg = (gi * up * sig * (1.0 + gate * (1.0 - sig))).astype(BF16)
    gu = (gi * silu).astype(BF16)
    inner_ref[...] = inner
    gg_ref[...] = gg
    gu_ref[...] = gu

    @pl.when(step == 0)
    def _():
        facc[...] = jnp.zeros_like(facc)
        gacc[...] = jnp.zeros_like(gacc)

    facc[:, :half] += dot_nn(inner, wdo[...])
    facc[:, half:] += dot_nn(inner, wdx[...])
    gacc[:, :half] += dot_nt(gg, wgo[...]) + dot_nt(gu, wuo[...])
    gacc[:, half:] += dot_nt(gg, wgx[...]) + dot_nt(gu, wux[...])

    @pl.when(step == pl.num_programs(0) - 1)
    def _():
        ffn_ref[...] = facc[...].astype(BF16)
        gn_ref[...] = gacc[...].astype(BF16)


def feed(n2, chunk, rows, gf, seq, part, gate, up, down):
    width = n2.shape[1]
    _, half, hidden = gate.shape
    hb = min(512, hidden)
    row = [pl.BlockSpec((None, half, hb), lambda h, side=side: (side, 0, h)) for side in range(2)]
    col = [pl.BlockSpec((None, hb, half), lambda h, side=side: (side, h, 0)) for side in range(2)]
    whole = pl.BlockSpec((rows, width), lambda h: (0, 0))
    tile = pl.BlockSpec((rows, hb), lambda h: (0, h))
    return pl.pallas_call(
        feed_kernel,
        grid=(hidden // hb,),
        in_specs=[pl.BlockSpec((rows, width), lambda h: (chunk, 0)), pl.BlockSpec((1, rows, width), lambda h: (seq, part, 0))] + row + row + col,
        out_specs=[tile, tile, tile, whole, whole],
        out_shape=[shape((rows, hidden), BF16)] * 3 + [shape((rows, width), BF16)] * 2,
        scratch_shapes=[pltpu.VMEM((rows, width), F32), pltpu.VMEM((rows, width), F32)],
        compiler_params=PARAMS,
        cost_estimate=cost(12 * rows * width * hidden, 12 * half * hidden + 14 * rows * width, rows * hidden),
        name="feed_forward",
    )(n2, gf, gate, gate, up, up, down, down)


def second_back_kernel(terms, hidden_ref, gf_ref, gain_ref, *refs):
    term_refs, (gb_ref, gh_ref, gain_out) = refs[:terms], refs[terms:]
    e = term_refs[0][...].astype(F32)
    for ref in term_refs[1:]:
        e = e + ref[...].astype(F32)
    hidden = hidden_ref[...]
    inv = inverse_rms(hidden)
    hat = hidden * inv
    eg = e * gain_ref[...]
    gh = gf_ref[0].astype(F32) + inv * (eg - hat * jnp.mean(eg * hat, axis=-1, keepdims=True))
    gh_ref[...] = gh
    gb_ref[...] = gh.astype(BF16)
    gain_out[...] = jnp.sum(e * hat, axis=0, keepdims=True)


def second_back(hidden, chunk, gf, seq, part, gain, terms):
    rows, width = terms[0].shape
    flat = pl.BlockSpec((rows, width), lambda i: (0, 0))
    line = pl.BlockSpec((1, width), lambda i: (0, 0))
    return pl.pallas_call(
        functools.partial(second_back_kernel, len(terms)),
        grid=(1,),
        in_specs=[pl.BlockSpec((rows, width), lambda i: (chunk, 0)), pl.BlockSpec((1, rows, width), lambda i: (seq, part, 0)), line]
        + [flat] * len(terms),
        out_specs=[flat, flat, line],
        out_shape=[shape((rows, width), BF16), shape((rows, width), F32), shape((1, width), F32)],
        compiler_params=PARAMS,
        cost_estimate=cost(20 * rows * width, (12 + 2 * len(terms)) * rows * width),
        name="second_norm_back",
    )(hidden, gf, gain, *terms)


def branch_back_kernel(chunks, *refs):
    gb_refs, (w_ref, core_ref, own_ref, oth_ref) = refs[:chunks], refs[chunks:]
    half = w_ref.shape[2]
    rows = gb_refs[0].shape[0]
    heads_half = own_ref.shape[0]
    first = core_ref[0] == 0
    for k, ref in enumerate(gb_refs):
        da = dot_nt(w_ref[0], ref[:, :half]) + dot_nt(w_ref[1], ref[:, half:])
        da = da.astype(BF16)
        low, high = da[:heads_half], da[heads_half:]
        cut = slice(k * rows, (k + 1) * rows)
        own_ref[:, cut] = jnp.where(first, low, high)
        oth_ref[:, cut] = jnp.where(first, high, low)


def branch_back(gbs, weight, core):
    chunks = len(gbs)
    rows, width = gbs[0].shape
    dim = weight.shape[1]
    full = pl.BlockSpec(memory_space=pltpu.VMEM)
    return pl.pallas_call(
        functools.partial(branch_back_kernel, chunks),
        in_specs=[full] * (chunks + 1) + [SMEM],
        out_specs=[full] * 2,
        out_shape=[shape((dim // 2, chunks * rows), BF16)] * 2,
        compiler_params=PARAMS,
        cost_estimate=cost(2 * dim * chunks * rows * width, 2 * dim * width + 2 * chunks * rows * width),
        name="attention_branch_back",
    )(*gbs, weight, core)


def attend_back_kernel(block, groups, scal_ref, all_ref, att_ref, inv_ref, own_ref, got_ref, out_own, out_oth, da_all, grads):
    span = own_ref.shape[1]
    hd = all_ref.shape[0] // (groups + 2)
    length, core = scal_ref[0], scal_ref[1]
    low, high = join_positions(core, own_ref[...], got_ref[...])
    da_all[:, :span] = low
    da_all[:, span:] = high
    scale = log2e / math.sqrt(hd)
    back = 1.0 / math.sqrt(hd)
    krow = lax.broadcasted_iota(jnp.int32, (block, groups * block), 0)
    qcol = lax.broadcasted_iota(jnp.int32, (block, groups * block), 1) % block
    base = groups * hd
    grads[base:, :] = jnp.zeros((2 * hd, 2 * span), F32)
    for i in range(2 * span // block):
        cut = slice(i * block, (i + 1) * block)

        def rows(ref):
            return jnp.concatenate([ref[g * hd : (g + 1) * hd, cut] for g in range(groups)], axis=1)

        q = rows(all_ref)
        da = rows(da_all)
        inv = jnp.concatenate([inv_ref[g : g + 1, cut] for g in range(groups)], axis=1)
        delta = jnp.sum(rows(att_ref).astype(F32) * da.astype(F32), axis=0, keepdims=True)
        dq = jnp.zeros((hd, groups * block), F32)
        for j in range(i + 1):
            kcut = slice(j * block, (j + 1) * block)
            key = all_ref[base : base + hd, kcut]
            s = dot_tn(key, q) * scale
            ok = (krow + j * block) < length
            if j == i:
                ok = ok & (krow <= qcol)
            p = jnp.where(ok, jnp.exp2(s) * inv, 0.0)
            dp = dot_tn(all_ref[base + hd : base + 2 * hd, kcut], da)
            ds = (p * (dp - delta)).astype(BF16)
            dq = dq + dot_nn(key, ds)
            grads[base : base + hd, kcut] += dot_nt(q, ds) * back
            grads[base + hd : base + 2 * hd, kcut] += dot_nt(da, p.astype(BF16))
        dq = dq * back
        for g in range(groups):
            grads[g * hd : (g + 1) * hd, cut] = dq[:, g * block : (g + 1) * block]
    mine, theirs = join_positions(core, grads[:, :span], grads[:, span:])
    out_own[...] = mine.astype(BF16)
    out_oth[...] = theirs.astype(BF16)


def attend_back(scalars, everything, att, inv, own, got, groups):
    rows, slots = everything.shape
    span = slots // 2
    block = min(256, span)
    full = pl.BlockSpec(memory_space=pltpu.VMEM)
    return pl.pallas_call(
        functools.partial(attend_back_kernel, block, groups),
        in_specs=[SMEM] + [full] * 5,
        out_specs=[full] * 2,
        out_shape=[shape((rows, span), BF16)] * 2,
        scratch_shapes=[pltpu.VMEM(att.shape, BF16), pltpu.VMEM((rows, slots), F32)],
        compiler_params=PARAMS,
        cost_estimate=cost(30 * att.shape[0] * slots * slots, 12 * rows * slots, groups * slots * slots),
        name="attend_backward",
    )(scalars, everything, att, inv, own, got)


def heads_back_kernel(hd, nq, nk, own_ref, got_ref, pre_ref, cos_ref, sin_ref, qg_ref, kg_ref, x_ref, w_ref, core_ref, dpre_ref, first_ref, gain_ref, hgain_ref):
    half = w_ref.shape[1]
    low, high = join_positions(core_ref[0], own_ref[...].astype(F32), got_ref[...].astype(F32))
    sides = (nq // 2, nk // 2, nk // 2)
    grads = [[], [], []]
    for side in (low, high):
        at = 0
        for kind, count in enumerate(sides):
            for h in range(count):
                grads[kind].append(side[at : at + hd])
                at += hd
    cosine, sine = cos_ref[...], sin_ref[...]
    done = []
    sums = [0.0, 0.0]
    for h in range(nq + nk):
        kind = 0 if h < nq else 1
        g = grads[kind][h - kind * nq]
        a, b = g[: hd // 2], g[hd // 2 :]
        g = jnp.concatenate([a * cosine + b * sine, b * cosine - a * sine], axis=0)
        v = pre_ref[h * hd : (h + 1) * hd, :]
        inv = lax.rsqrt(jnp.mean(v * v, axis=0, keepdims=True) + epsilon)
        hat = v * inv
        sums[kind] = sums[kind] + jnp.sum(g * hat, axis=1, keepdims=True)
        gg = g * (qg_ref[...] if kind == 0 else kg_ref[...])
        done.append(inv * (gg - hat * jnp.mean(gg * hat, axis=0, keepdims=True)))
    done += grads[2]
    hgain_ref[:hd, :] = jnp.broadcast_to(sums[0], (hd, 128))
    hgain_ref[hd:, :] = jnp.broadcast_to(sums[1], (hd, 128))
    dpre = jnp.concatenate(done, axis=0).T.astype(BF16)
    dpre_ref[...] = dpre
    x = x_ref[0].astype(F32)
    hat = x * inverse_rms(x)
    for k in range(2):
        cut = slice(k * half, (k + 1) * half)
        part = dot_nt(dpre, w_ref[k])
        first_ref[:, cut] = part.astype(BF16)
        gain_ref[:, cut] = jnp.sum(part * hat[:, cut], axis=0, keepdims=True)


def heads_back(own, got, pre, cosine, sine, qgain, kgain, xr, seq, weight, core, hd, nq, nk):
    span = own.shape[1]
    _, half, cols = weight.shape
    width = 2 * half
    whole = lambda a: pl.BlockSpec(a.shape, lambda i: (0,) * len(a.shape))
    outs = [shape((span, cols), BF16), shape((span, width), BF16), shape((1, width), F32), shape((2 * hd, 128), F32)]
    return pl.pallas_call(
        functools.partial(heads_back_kernel, hd, nq, nk),
        grid=(1,),
        in_specs=[whole(a) for a in (own, got, pre, cosine, sine, qgain, kgain)]
        + [pl.BlockSpec((1, span, width), lambda i: (seq, 0, 0)), whole(weight), SMEM],
        out_specs=[whole(o) for o in outs],
        out_shape=outs,
        compiler_params=PARAMS,
        cost_estimate=cost(2 * span * width * cols, 4 * span * width + 4 * half * cols),
        name="query_key_value_back",
    )(own, got, pre, cosine, sine, qgain, kgain, xr, weight, core)


def place_blocks(order, ids, first_id, value, out_ref):
    piece = value.shape[-1] // order
    for k in range(order):
        if order == 1:
            out_ref[...] = value
        else:
            dst = pl.ds(pl.multiple_of(ids[first_id + k] * piece, piece), piece)
            out_ref[:, dst] = value[:, k * piece : (k + 1) * piece]


def output_kernel(order, scal_ref, got_ref, f0_ref, f1_ref, h0_ref, h1_ref, out_ref, stat_ref):
    low = scal_ref[0] * 2 < scal_ref[3]
    rows = out_ref.shape[0]
    ffn = got_ref[...].astype(F32) + jnp.where(low, f0_ref[...], f1_ref[...]).astype(F32)
    hidden = jnp.where(low, h0_ref[...], h1_ref[...])
    place = scal_ref[2] + lax.broadcasted_iota(jnp.int32, (rows, 1), 0)
    valid = (place < scal_ref[1]).astype(F32)
    stat_ref[...] = jnp.broadcast_to(jnp.sum(valid * ffn * ffn, keepdims=True), (8, 128))
    place_blocks(order, scal_ref, 4, (hidden + ffn).astype(BF16), out_ref)


def share_specs(rows, width, per):
    return [
        pl.BlockSpec((rows, width), lambda i, s: (jnp.minimum(s[0], per - 1), 0)),
        pl.BlockSpec((rows, width), lambda i, s: (jnp.maximum(s[0] - per, 0), 0)),
    ]


def output_share(scalars, got, ffns, hiddens, order):
    rows, width = got.shape
    pair = share_specs(rows, width, ffns[0].shape[0] // rows)
    flat = pl.BlockSpec((rows, width), lambda i, s: (0, 0))
    return pl.pallas_call(
        functools.partial(output_kernel, order),
        grid_spec=pltpu.PrefetchScalarGridSpec(
            num_scalar_prefetch=1,
            grid=(1,),
            in_specs=[flat] + pair + pair,
            out_specs=[flat, pl.BlockSpec((8, 128), lambda i, s: (0, 0))],
        ),
        out_shape=[shape((rows, width), BF16), shape((8, 128), F32)],
        compiler_params=PARAMS,
        cost_estimate=cost(6 * rows * width, 16 * rows * width),
        name="output_share",
    )(scalars, got, *ffns, *hiddens)


def input_kernel(order, scal_ref, got_ref, part_ref, g0_ref, g1_ref, x_ref, gain_ref, out_ref):
    low = scal_ref[0] * 2 < scal_ref[3]
    e = got_ref[...].astype(F32) + part_ref[...].astype(F32)
    gh = jnp.where(low, g0_ref[...], g1_ref[...])
    x = x_ref[0].astype(F32)
    inv = inverse_rms(x)
    hat = x * inv
    eg = e * gain_ref[...]
    value = gh + inv * (eg - hat * jnp.mean(eg * hat, axis=-1, keepdims=True))
    place_blocks(order, scal_ref, 4, value, out_ref)


def input_share(scalars, got, part, ghs, xr, seq, gain, order):
    rows, width = got.shape
    pair = share_specs(rows, width, ghs[0].shape[0] // rows)
    flat = pl.BlockSpec((rows, width), lambda i, s: (0, 0))
    return pl.pallas_call(
        functools.partial(input_kernel, order),
        grid_spec=pltpu.PrefetchScalarGridSpec(
            num_scalar_prefetch=1,
            grid=(1,),
            in_specs=[flat, pl.BlockSpec((rows, width), lambda i, s: (s[0], 0))]
            + pair
            + [pl.BlockSpec((1, rows, width), lambda i, s: (seq, s[0], 0)), pl.BlockSpec((1, width), lambda i, s: (0, 0))],
            out_specs=flat,
        ),
        out_shape=shape((rows, width), F32),
        compiler_params=PARAMS,
        cost_estimate=cost(12 * rows * width, 20 * rows * width),
        name="input_share",
    )(scalars, got, part, *ghs, xr, gain)


def weight_grad_kernel(count, extra, *refs):
    a_refs, b_refs, out = refs[:count], refs[count : 2 * count], refs[-1]
    total = dot_tn(a_refs[0][...], b_refs[0][...])
    for a, b in zip(a_refs[1:], b_refs[1:]):
        total = total + dot_tn(a[...], b[...])
    if extra:
        total = total + refs[2 * count][...].astype(F32)
    out[...] = total.astype(BF16)


def weight_grad(lefts, rights, side, axis, add=None):
    count = len(lefts)
    rows_all, cols_all = lefts[0].shape[1], rights[0].shape[1]
    dims = [rows_all, cols_all]
    dims[axis] //= 2
    rows, cols = min(512, dims[0]), min(2048, dims[1])
    row_at = side * (dims[0] // rows) if axis == 0 else 0
    col_at = side * (dims[1] // cols) if axis == 1 else 0
    specs = [pl.BlockSpec((a.shape[0], rows), lambda j, i: (0, i + row_at)) for a in lefts]
    specs += [pl.BlockSpec((b.shape[0], cols), lambda j, i: (0, j + col_at)) for b in rights]
    tile = pl.BlockSpec((rows, cols), lambda j, i: (i, j))
    tokens = sum(a.shape[0] for a in lefts)
    return pl.pallas_call(
        functools.partial(weight_grad_kernel, count, add is not None),
        grid=(dims[1] // cols, dims[0] // rows),
        in_specs=specs + ([tile] if add is not None else []),
        out_specs=tile,
        out_shape=shape(dims, BF16),
        compiler_params=PARAMS,
        cost_estimate=cost(2 * tokens * dims[0] * dims[1], 2 * tokens * sum(dims) + 2 * dims[0] * dims[1]),
        name="weight_grad",
    )(*lefts, *rights, *([add] if add is not None else []))


def xor_one(index):
    return index + 1 - 2 * (index % 2)


def remote(src, dst, send, recv, device):
    return pltpu.make_async_remote_copy(
        src_ref=src, dst_ref=dst, send_sem=send, recv_sem=recv, device_id=device, device_id_type=pl.DeviceIdType.MESH
    )


def greet(others):
    barrier = pltpu.get_barrier_semaphore()
    count = 0
    for needed, device in others:
        if needed is None:
            pl.semaphore_signal(barrier, inc=1, device_id=device, device_id_type=pl.DeviceIdType.MESH)
            count = count + 1
        else:

            @pl.when(needed)
            def _():
                pl.semaphore_signal(barrier, inc=1, device_id=device, device_id_type=pl.DeviceIdType.MESH)

            count = count + jnp.where(needed, 1, 0)
    pl.semaphore_wait(barrier, count)


class Gather:
    def __init__(self, shard, dst, axis, send, recv, local, near_x, near_y, near_core):
        piece = shard.shape[axis]
        half = shard.shape[0] // 2

        def block(side, k):
            cut = pl.ds(k * piece, piece)
            return dst.at[side, cut, :] if axis == 0 else dst.at[side, :, cut]

        def part(k, h):
            if axis == 0:
                return dst.at[0, pl.ds(k * piece + h * half, half), :]
            return dst.at[0, pl.ds(h * half, half), pl.ds(k * piece, piece)]

        sem = lambda k: (send.at[k], recv.at[k])
        self.local = pltpu.make_async_copy(shard, block(0, 0), local)
        self.x = remote(shard, block(0, 1), *sem(0), near_x)
        self.y = remote(shard, block(0, 2), *sem(1), near_y)
        self.dx = remote(part(2, 0), part(3, 0), *sem(2), near_x)
        self.dy = remote(part(1, 1), part(3, 1), *sem(3), near_y)
        self.cores = [remote(shard, block(1, 0), *sem(4), near_core)]
        self.cores += [remote(block(0, k), block(1, k), *sem(4 + k), near_core) for k in (1, 2, 3)]

    def first(self):
        self.x.start()
        self.y.start()
        self.cores[0].start()
        self.local.start()

    def second(self):
        self.y.wait_recv()
        self.dx.start()
        self.cores[2].start()
        self.x.wait_recv()
        self.dy.start()
        self.cores[1].start()

    def third(self):
        self.dx.wait_recv()
        self.dy.wait_recv()
        self.cores[3].start()

    def arrived(self):
        self.local.wait()
        for copy in self.cores:
            copy.wait_recv()

    def sent(self):
        for copy in [self.x, self.y, self.dx, self.dy] + self.cores:
            copy.wait_send()


def forward_kernel(
    hd, nq, nk, block, sub,
    len_ref, x_hbm, cot_hbm, wq_hbm, wk_hbm, wv_hbm, wout, wgate, wup, wdown, small_ref,
    xr_hbm, n1_hbm, gf_hbm, qkv_hbm, out_hbm, gate_hbm, up_hbm, down_hbm, hidden_hbm, n2_hbm, rest_hbm, gi_hbm, pre_hbm, all_hbm, att_hbm, tok_hbm,
    gains_ref, table_ref, inv_ref, stat_ref,
    xr_v, cot_v, n1_v, qkv_v, out_v, ex_own, ex_send, ex_got, at_own, at_send, at_got,
    part_v, in_v, back_v, total_v, hid_v, norm_v, wqkv, gain_ref, down_v, gi_v, pre_ref, all_ref, att_ref, tok_ref,
    keep_sem, load_sem, store_sem, shard_sem, rest_sem, down_sem, gi_sem, wsend, wrecv, wloc, gsend, grecv, exsend, exrecv, zsend, zrecv, hid_sem,
):
    seqs, span, width = xr_v.shape
    groups = nq // nk
    row, core, rank = lax.axis_index("dp"), lax.axis_index("context"), lax.axis_index("tensor")
    start = core * span
    near = [row, xor_one(row), (row + 2) % 4, 3 - row]
    inner = (rank % 3) != 0
    near_x, near_y, near_core = {"dp": near[1]}, {"dp": near[2]}, {"context": 1 - core}
    z_side, z_mid = {"tensor": xor_one(rank)}, {"tensor": 3 - rank}
    piece = width // 8
    total_subs = part_v.shape[0]
    per = span // sub
    first_core = core == 0

    loads = []
    for at, (src, dst) in enumerate(((x_hbm, xr_v), (cot_hbm, cot_v))):
        for s in range(seqs):
            for o in range(2):
                for k in range(4):
                    b = near[k] * 2 + (core if o == 0 else 1 - core)
                    cut = pl.ds(pl.multiple_of(b * piece, piece), piece)
                    loads.append(
                        pltpu.make_async_copy(
                            src.at[s, :, cut], dst.at[s, :, pl.ds((o * 4 + k) * piece, piece)], load_sem.at[at, s, o * 4 + k]
                        )
                    )
    shards, at = [], 0
    for k, ref in enumerate((wq_hbm, wk_hbm, wv_hbm)):
        shards.append(pltpu.make_async_copy(ref, wqkv.at[:, pl.ds(at, ref.shape[1])], shard_sem.at[k]))
        at += ref.shape[1]
    for copy in shards + loads:
        copy.start()
    piece = width // 8
    gain_ref[...] = jnp.concatenate([small_ref[:, :piece], small_ref[:, piece : 2 * piece], jnp.zeros((14, piece), BF16)], axis=0)

    others = []
    for o in range(2):
        for k in range(4):
            if o or k:
                others.append((o * 4 + k, {"dp": near[k], "context": core if o == 0 else 1 - core}))
    greet([(None, d) for _, d in others] + [(None, z_side), (inner, z_mid)])

    gains = [remote(gain_ref, gains_ref.at[b], gsend.at[b], grecv.at[b], d) for b, d in others]
    for copy in gains:
        copy.start()
    weights = [
        Gather(shard, dst, axis, wsend.at[i], wrecv.at[i], wloc.at[i], near_x, near_y, near_core)
        for i, (shard, dst, axis) in enumerate(
            ((wqkv, qkv_v, 0), (wout, out_v, 1), (wgate, gate_hbm, 0), (wup, up_hbm, 0), (wdown, down_hbm, 1))
        )
    ]
    w_qkv, w_out, w_gate, w_up, w_down = weights
    for copy in shards:
        copy.wait()
    w_qkv.first()
    gains_ref[0] = gain_ref[...]

    quarter = hd // 2
    freqs = jnp.exp(lax.broadcasted_iota(jnp.int32, (quarter, span), 0).astype(F32) * (-2.0 * math.log(rope_base) / hd))
    angles = freqs * (start + lax.broadcasted_iota(jnp.int32, (quarter, span), 1)).astype(F32)
    cosine, sine = jnp.cos(angles), jnp.sin(angles)
    both_gains = jnp.broadcast_to(small_ref[:, 2 * piece :].astype(F32), (8, 2 * hd)).T
    qgain, kgain = both_gains[:hd, 0:1], both_gains[hd:, 0:1]
    table_ref[:quarter, :] = cosine
    table_ref[quarter : 2 * quarter, :] = sine
    table_ref[2 * quarter : 2 * quarter + hd, :128] = jnp.broadcast_to(qgain, (hd, 128))
    table_ref[2 * quarter + hd :, :128] = jnp.broadcast_to(kgain, (hd, 128))

    for copy in loads[len(loads) // 2 :]:
        copy.wait()

    def mask_rows(i, carry):
        s, t = i // (span // 16), i % (span // 16)
        cut = pl.ds(pl.multiple_of(t * 16, 16), 16)
        place = start + t * 16 + lax.broadcasted_iota(jnp.int32, (16, 1), 0)
        valid = (place < len_ref[s]).astype(F32)
        cot_v[s, cut, :] = (cot_v[s, cut, :].astype(F32) * valid).astype(BF16)
        return carry

    lax.fori_loop(0, seqs * span // 16, mask_rows, 0)
    store_gf = pltpu.make_async_copy(cot_v, gf_hbm, store_sem.at[0])
    store_gf.start()
    for copy in loads[: len(loads) // 2]:
        copy.wait()
    store_xr = pltpu.make_async_copy(xr_v, xr_hbm, store_sem.at[1])
    store_xr.start()
    for copy in gains:
        copy.wait_recv()
    gain1 = jnp.concatenate([gains_ref[b, 0:1, :] for b in range(8)], axis=1).astype(F32)
    gain2 = jnp.concatenate([gains_ref[b, 1:2, :] for b in range(8)], axis=1).astype(F32)

    def norm_rows(i, carry):
        s, t = i // (span // 16), i % (span // 16)
        cut = pl.ds(pl.multiple_of(t * 16, 16), 16)
        x = xr_v[s, cut, :].astype(F32)
        n1_v[s, cut, :] = (x * inverse_rms(x) * gain1).astype(BF16)
        return carry

    lax.fori_loop(0, span // 16, norm_rows, 0)
    w_qkv.second()
    w_out.first()
    lax.fori_loop(span // 16, seqs * span // 16, norm_rows, 0)
    store_n1 = pltpu.make_async_copy(n1_v, n1_hbm, store_sem.at[2])
    store_n1.start()
    w_qkv.third()
    w_qkv.arrived()

    half = width // 2

    def exchange(s):
        return remote(ex_send.at[s], ex_got.at[s], exsend.at[0, s], exrecv.at[0, s], near_core)

    def keep(k, s):
        ref, dst = ((pre_ref, pre_hbm), (all_ref, all_hbm), (att_ref, att_hbm), (tok_ref, tok_hbm))[k]
        return pltpu.make_async_copy(ref.at[s], dst.at[s], keep_sem.at[k, s])

    def project(s):
        x = n1_v[s]
        flat = dot_nn(x[:, :half], qkv_v[0]) + dot_nn(x[:, half:], qkv_v[1])
        turned = flat.T
        pre_ref[s] = turned[: (nq + nk) * hd]
        done = []
        for h in range(nq + nk):
            v = turned[h * hd : (h + 1) * hd]
            inv = lax.rsqrt(jnp.mean(v * v, axis=0, keepdims=True) + epsilon)
            v = v * inv * (qgain if h < nq else kgain)
            a, b = v[: hd // 2], v[hd // 2 :]
            done.append(jnp.concatenate([a * cosine - b * sine, b * cosine + a * sine], axis=0))
        for h in range(nk):
            lo = (nq + nk + h) * hd
            done.append(turned[lo : lo + hd])
        parts = [[], []]
        for begin_at, count in ((0, nq), (nq, nk), (nq + nk, nk)):
            for side in range(2):
                parts[side] += done[begin_at + side * count // 2 : begin_at + (side + 1) * count // 2]
        low = jnp.concatenate(parts[0], axis=0)
        high = jnp.concatenate(parts[1], axis=0)
        ex_own[s] = jnp.where(first_core, low, high).astype(BF16)
        ex_send[s] = jnp.where(first_core, high, low).astype(BF16)
        exchange(s).start()
        keep(0, s).start()

    store_qkv = pltpu.make_async_copy(qkv_v, qkv_hbm, store_sem.at[3])
    store_qkv.start()
    store_out = pltpu.make_async_copy(out_v, out_hbm, store_sem.at[4])

    scale = log2e / math.sqrt(hd)
    krow = lax.broadcasted_iota(jnp.int32, (block, groups * block), 0)
    qcol = lax.broadcasted_iota(jnp.int32, (block, groups * block), 1) % block
    base = groups * hd

    def give(s):
        return remote(at_send.at[s], at_got.at[s], exsend.at[1, s], exrecv.at[1, s], near_core)

    def attention(s):
        exchange(s).wait_recv()
        low, high = join_positions(core, ex_own[s], ex_got[s])
        all_ref[s, :, :span] = low
        all_ref[s, :, span:] = high
        length = len_ref[s]
        for i in range(2 * span // block):
            cut = slice(i * block, (i + 1) * block)
            q = jnp.concatenate([all_ref[s, g * hd : (g + 1) * hd, cut] for g in range(groups)], axis=1)
            acc = jnp.zeros((hd, groups * block), F32)
            total = jnp.zeros((1, groups * block), F32)
            for j in range(i + 1):
                kcut = slice(j * block, (j + 1) * block)
                score = dot_tn(all_ref[s, base : base + hd, kcut], q) * scale
                ok = (krow + j * block) < length
                if j == i:
                    ok = ok & (krow <= qcol)
                e = jnp.where(ok, jnp.exp2(score), 0.0)
                total = total + jnp.sum(e, axis=0, keepdims=True)
                acc = acc + dot_nn(all_ref[s, base + hd : base + 2 * hd, kcut], e.astype(BF16))
            inv = 1.0 / total
            att = (acc * inv).astype(BF16)
            for g in range(groups):
                att_ref[s, g * hd : (g + 1) * hd, cut] = att[:, g * block : (g + 1) * block]
                inv_ref[s, g : g + 1, cut] = inv[:, g * block : (g + 1) * block]
        mine, theirs = join_positions(core, att_ref[s, :, :span], att_ref[s, :, span:])
        at_own[s] = mine
        at_send[s] = theirs
        give(s).start()
        keep(1, s).start()
        keep(2, s).start()

    moving = Chain(rank, part_v, in_v, back_v, zsend, zrecv)
    subs = moving.count

    def branch_rows(s):
        give(s).wait_recv()
        low, high = join_positions(core, at_own[s], at_got[s])
        att = jnp.concatenate([low, high], axis=0).T
        tok_ref[s] = att
        keep(3, s).start()
        many = 2
        for k in range(0, per, many):
            rows = att[k * sub : (k + many) * sub]
            for side in range(2):
                part = dot_nn(rows, out_v[side]).astype(BF16)
                for m in range(many):
                    part_v[s * per + k + m, :, side * half : (side + 1) * half] = part[m * sub : (m + 1) * sub]
            for m in range(many):
                u = s * per + k + m

                @pl.when(u < subs)
                def _():
                    moving.begin(u)

    def sequence(s, carry):
        project(s)

        @pl.when(s == 0)
        def _():
            w_out.second()
            w_down.first()
            w_gate.first()

        attention(s)

        @pl.when(s == 0)
        def _():
            w_out.third()
            w_out.arrived()
            store_out.start()

        branch_rows(s)
        return carry

    lax.fori_loop(0, seqs, sequence, 0)
    rest = [pltpu.make_async_copy(part_v.at[u], rest_hbm.at[u - subs], rest_sem.at[u - subs]) for u in range(subs, total_subs)]
    for copy in rest:
        copy.start()
    stat_ref[...] = jnp.zeros_like(stat_ref)

    def hidden_store(u):
        cut = pl.ds(pl.multiple_of(u * sub, sub), sub)
        return (
            pltpu.make_async_copy(hid_v.at[u % 2], hidden_hbm.at[cut, :], hid_sem.at[0, u % 2]),
            pltpu.make_async_copy(norm_v.at[u % 2], n2_hbm.at[cut, :], hid_sem.at[1, u % 2]),
        )

    def finish(u):
        s, t = u // per, u % per
        cut = pl.ds(pl.multiple_of(t * sub, sub), sub)

        moving.total(u, total_v)

        @pl.when(u >= 2)
        def _():
            for copy in hidden_store(u - 2):
                copy.wait()

        length = len_ref[s]

        def body(piece_rows, first):
            total = total_v[piece_rows, :]
            resid = xr_v[s, pl.ds(pl.multiple_of(t * sub + first, 16), 16), :].astype(F32)
            hidden = resid + total
            hid_v[u % 2, piece_rows, :] = hidden
            norm_v[u % 2, piece_rows, :] = (hidden * inverse_rms(hidden) * gain2).astype(BF16)
            place = start + t * sub + first + lax.broadcasted_iota(jnp.int32, (16, 1), 0)
            valid = (place < length).astype(F32)
            stat_ref[0] += fold_lanes(valid * resid * resid)
            stat_ref[1] += fold_lanes(valid * total * total)

        by_pieces(sub, body)
        for copy in hidden_store(u):
            copy.start()

    hb = down_v.shape[2]
    blocks = down_hbm.shape[1] // hb

    def load_down(h):
        cut = pl.ds(pl.multiple_of(h * hb, hb), hb)
        return [pltpu.make_async_copy(down_hbm.at[side, cut, :], down_v.at[h % 2, side], down_sem.at[h % 2, side]) for side in range(2)]

    def store_gi(h):
        cut = pl.ds(pl.multiple_of(h * hb, hb), hb)
        return pltpu.make_async_copy(gi_v.at[h % 2], gi_hbm.at[:, cut], gi_sem.at[h % 2])

    def grad_inner(h):
        for copy in load_down(h):
            copy.wait()

        @pl.when(h + 1 < blocks)
        def _():
            for copy in load_down(h + 1):
                copy.start()

        @pl.when(h >= 2)
        def _():
            store_gi(h - 2).wait()

        for s in range(seqs):
            for q in range(span // 256):
                cut = slice(q * 256, (q + 1) * 256)
                g = dot_nt(cot_v[s, cut, :half], down_v[h % 2, 0]) + dot_nt(cot_v[s, cut, half:], down_v[h % 2, 1])
                gi_v[h % 2, s * span + q * 256 : s * span + (q + 1) * 256, :] = g.astype(BF16)
        store_gi(h).start()

    def chain(i, carry):
        moving.middle(i)
        moving.outward(i - 1)

        @pl.when(i >= 2)
        def _():
            finish(i - 2)

        @pl.when(i == 1)
        def _():
            w_down.second()
            w_up.first()

        @pl.when(i == 6)
        def _():
            w_gate.second()

        @pl.when(i == 8)
        def _():
            w_down.third()

        @pl.when(i == 9)
        def _():
            w_down.arrived()
            for copy in load_down(0):
                copy.start()

        @pl.when((i >= 10) & (i < 10 + blocks))
        def _():
            grad_inner(i - 10)

        @pl.when(i == 12)
        def _():
            w_up.second()

        @pl.when(i == 14)
        def _():
            w_gate.third()

        return carry

    lax.fori_loop(0, subs + 2, chain, 0)
    w_up.third()
    for u in (subs - 2, subs - 1):
        for copy in hidden_store(u):
            copy.wait()
    for h in (blocks - 2, blocks - 1):
        store_gi(h).wait()
    moving.settle()
    for s in range(seqs):
        exchange(s).wait_send()
        give(s).wait_send()
        for k in range(4):
            keep(k, s).wait()
    for copy in gains:
        copy.wait_send()
    w_gate.arrived()
    w_up.arrived()
    for w in weights:
        w.sent()
    for copy in [store_gf, store_xr, store_n1, store_qkv, store_out] + rest:
        copy.wait()


def forward(lengths, x, cot, w_query, w_key, w_value, w_out, w_gate, w_up, w_down, all_gains, hd, nq, nk):
    seqs, span, width = x.shape
    half = width // 2
    groups = nq // nk
    sub = span // 8
    subs = seqs * span // sub
    here = subs - 2
    block = min(256, span)
    hidden = w_gate.shape[1]
    hb = hidden // 4
    cols = w_query.shape[1] + w_key.shape[1] + w_value.shape[1]
    rows = cols // 2
    any_space = pl.BlockSpec(memory_space=pl.ANY)
    vmem = pl.BlockSpec(memory_space=pltpu.VMEM)
    wide = (seqs, span, width)
    large = [
        shape(wide, BF16), shape(wide, BF16), shape(wide, BF16),
        shape((2, half, cols), BF16), shape((2, w_out.shape[0], half), BF16),
        shape((2, half, hidden), BF16), shape((2, half, hidden), BF16), shape((2, hidden, half), BF16),
        shape((seqs * span, width), F32), shape((seqs * span, width), BF16), shape((subs - here, sub, width), BF16),
        shape((seqs * span, hidden), BF16),
    ]
    kept = [
        shape((seqs, (nq + nk) * hd, span), F32), shape((seqs, rows, 2 * span), BF16),
        shape((seqs, groups * hd, 2 * span), BF16), shape((seqs, span, nq * hd), BF16),
    ]
    large += kept
    small = [
        shape((8, 16, width // 8), BF16), shape((3 * hd, span), F32), shape((seqs, groups, 2 * span), F32), shape((2, 8, 128), F32),
    ]
    dma = pltpu.SemaphoreType.DMA
    ex = pltpu.VMEM((seqs, rows, span), BF16)
    at = pltpu.VMEM((seqs, groups * hd, span), BF16)
    moving = pltpu.VMEM((subs, sub, width), BF16)
    landing = pltpu.VMEM((here, sub, width), BF16)
    flops = 2 * seqs * span * width * (cols + nq * hd) + 16 * seqs * nq * hd * span * span
    return pl.pallas_call(
        functools.partial(forward_kernel, hd, nq, nk, block, sub),
        in_specs=[SMEM] + [any_space] * 9 + [vmem],
        out_specs=[any_space] * len(large) + [vmem] * len(small),
        out_shape=large + small,
        scratch_shapes=[
            pltpu.VMEM(wide, BF16), pltpu.VMEM(wide, BF16), pltpu.VMEM(wide, BF16),
            pltpu.VMEM((2, half, cols), BF16), pltpu.VMEM((2, w_out.shape[0], half), BF16),
            ex, ex, ex, at, at, at,
            moving, landing, landing,
            pltpu.VMEM((sub, width), F32), pltpu.VMEM((2, sub, width), F32), pltpu.VMEM((2, sub, width), BF16),
            pltpu.VMEM((w_query.shape[0], cols), BF16), pltpu.VMEM((16, width // 8), BF16),
            pltpu.VMEM((2, 2, hb, half), BF16), pltpu.VMEM((2, seqs * span, hb), BF16),
            *[pltpu.VMEM(a.shape, a.dtype) for a in kept],
            dma((4, seqs)), dma((2, seqs, 8)), dma((5,)), dma((3,)), dma((subs - here,)), dma((2, 2)), dma((2,)), dma((5, 8)), dma((5, 8)), dma((5,)), dma((8,)), dma((8,)),
            dma((2, seqs)), dma((2, seqs)), dma((3, subs)), dma((3, subs)), dma((2, 2)),
        ],
        compiler_params=pltpu.CompilerParams(vmem_limit_bytes=VMEM_MOST, collective_id=1, has_side_effects=True),
        cost_estimate=cost(flops, 80 * seqs * span * width),
        name="attention_forward",
    )(lengths, x, cot, w_query, w_key, w_value, w_out, w_gate, w_up, w_down, all_gains)


def by_pieces(count, body, size=16):
    def one(p, carry):
        body(pl.ds(pl.multiple_of(p * size, size), size), p * size)
        return carry

    lax.fori_loop(0, count // size, one, 0, unroll=2)


def fold_lanes(values):
    tiles = values[:8] + values[8:]
    return sum(tiles[:, k * 128 : (k + 1) * 128] for k in range(tiles.shape[1] // 128))


class Chain:
    def __init__(self, rank, part, arrive, back, send, recv):
        self.inner = (rank % 3) != 0
        self.outer = (rank % 3) == 0
        self.part, self.arrive, self.back = part, arrive, back
        self.send, self.recv = send, recv
        self.side, self.mid = {"tensor": xor_one(rank)}, {"tensor": 3 - rank}
        self.count = arrive.shape[0]

    def hop_in(self, u):
        return remote(self.part.at[u], self.arrive.at[u], self.send.at[0, u], self.recv.at[0, u], self.side)

    def hop_mid(self, u):
        return remote(self.arrive.at[u], self.back.at[u], self.send.at[1, u], self.recv.at[1, u], self.mid)

    def hop_out(self, u):
        return remote(self.part.at[u], self.back.at[u], self.send.at[2, u], self.recv.at[2, u], self.side)

    def add(self, into, one, two, u):
        def body(cut, first):
            into[u, cut, :] = (one[u, cut, :].astype(F32) + two[u, cut, :].astype(F32)).astype(BF16)

        by_pieces(self.part.shape[1], body)

    def begin(self, u):
        @pl.when(self.outer)
        def _():
            self.hop_in(u).start()

    def middle(self, u):
        @pl.when((u >= 0) & (u < self.count) & self.inner)
        def _():
            self.hop_in(u).wait_recv()
            self.add(self.arrive, self.part, self.arrive, u)
            self.hop_mid(u).start()

    def outward(self, u):
        @pl.when((u >= 0) & (u < self.count) & self.inner)
        def _():
            self.hop_mid(u).wait_recv()
            self.add(self.part, self.part, self.back, u)
            self.hop_out(u).start()

    def total(self, u, into):
        @pl.when(self.inner)
        def _():
            def body(cut, first):
                into[cut, :] = self.arrive[u, cut, :].astype(F32) + self.back[u, cut, :].astype(F32)

            by_pieces(self.part.shape[1], body)

        @pl.when(self.outer)
        def _():
            self.hop_out(u).wait_recv()

            def body(cut, first):
                into[cut, :] = self.part[u, cut, :].astype(F32) + self.back[u, cut, :].astype(F32)

            by_pieces(self.part.shape[1], body)

    def settle(self):
        def one(u, carry):
            @pl.when(self.outer)
            def _():
                self.hop_in(u).wait_send()

            @pl.when(self.inner)
            def _():
                self.hop_mid(u).wait_send()
                self.hop_out(u).wait_send()

            return carry

        lax.fori_loop(0, self.count, one, 0)


def feed_both_kernel(
    hb, sub, rows,
    len_ref, n2_hbm, gf_hbm, gate_hbm, up_hbm, down_hbm, gi_hbm, rest_hbm, xr_hbm, hidden_in, gains_ref,
    ffn_hbm, gb_hbm, gh_hbm, dgate_hbm, dup_hbm, ddown_hbm, hidden_hbm, landx, landy, ring_hbm, gain_out, stat_ref,
    n2_v, gf_v, inner_v, gg_v, gu_v, facc, gacc, wrow, wcol, part_v, in_v, back_v, total_v, hid_v, gh_v, gb_v, stage_row, stage_col,
    late_p, late_a, late_b, xtile_v, gi_v, wide_v, temp_v, gain_ref,
    load_sem, wsem, zsend, zrecv, hid_sem, out_sem, ffn_sem, csend, crecv, store_sem, lsend, lrecv, xt_sem, xsend, xrecv, xload, rsend, rrecv, free_sem,
):
    core, rank = lax.axis_index("context"), lax.axis_index("tensor")
    near_core = {"context": 1 - core}
    tokens, width = n2_v.shape
    half = width // 2
    hidden = inner_v.shape[1]
    hsteps = hidden // hb
    steps = tokens // rows * hsteps
    per = rows // sub
    chain = Chain(rank, part_v, in_v, back_v, zsend, zrecv)
    subs = chain.count
    late = Chain(rank, late_p, late_a, late_b, lsend, lrecv)
    known = subs - late.count
    start = core * (tokens // 2)

    def load_weights(i):
        slot, h = i % 2, i % hsteps
        cut = pl.ds(pl.multiple_of(h * hb, hb), hb)
        here = pl.ds(pl.multiple_of(i // hsteps * rows, rows), rows)
        copies = [pltpu.make_async_copy(gi_hbm.at[here, cut], gi_v.at[slot], wsem.at[slot, 6])]
        for side in range(2):
            copies.append(pltpu.make_async_copy(gate_hbm.at[side, :, cut], wrow.at[slot, 0, side], wsem.at[slot, side]))
            copies.append(pltpu.make_async_copy(up_hbm.at[side, :, cut], wrow.at[slot, 1, side], wsem.at[slot, 2 + side]))
            copies.append(pltpu.make_async_copy(down_hbm.at[side, cut, :], wcol.at[slot, side], wsem.at[slot, 4 + side]))
        return copies

    def load_hidden(u):
        cut = pl.ds(pl.multiple_of(u * sub, sub), sub)
        return pltpu.make_async_copy(hidden_hbm.at[cut, :], hid_v, hid_sem)

    ready = pl.ds(0, known * sub)
    loads = [
        pltpu.make_async_copy(n2_hbm.at[ready, :], n2_v.at[ready, :], load_sem.at[0]),
        pltpu.make_async_copy(rest_hbm, late_p, load_sem.at[1]),
    ]
    load_gf = pltpu.make_async_copy(gf_hbm, gf_v, load_sem.at[2])
    for copy in loads + load_weights(0) + [load_gf]:
        copy.start()
    load_hidden(0).start()
    row = lax.axis_index("dp")
    near_x, near_y = {"dp": xor_one(row)}, {"dp": (row + 2) % 4}
    greet([(None, near_core), (None, near_x), (None, near_y), (None, chain.side), (chain.inner, chain.mid)])
    for b in range(8):
        gain_ref[:, b * (width // 8) : (b + 1) * (width // 8)] = gains_ref[b, 1:2, :].astype(F32)
    gain_out[...] = jnp.zeros_like(gain_out)
    stat_ref[...] = jnp.zeros_like(stat_ref)
    for copy in loads:
        copy.wait()
    for u in range(late.count):
        late.begin(u)

    def load_x(u):
        at = pl.multiple_of((known + u) * sub, sub)
        return pltpu.make_async_copy(xr_hbm.at[pl.ds(at, sub), :], xtile_v, xt_sem)

    def late_store(u):
        return pltpu.make_async_copy(gh_v, hidden_hbm.at[pl.ds(pl.multiple_of((known + u) * sub, sub), sub), :], out_sem.at[0])

    def late_finish(u):
        load_x(u).start()
        late.total(u, total_v)
        load_x(u).wait()

        @pl.when(u >= 1)
        def _():
            late_store(u - 1).wait()

        length = len_ref[known * sub // (tokens // 2)]
        offset = start + known * sub % (tokens // 2) + u * sub

        def body(cut, first):
            total = total_v[cut, :]
            resid = xtile_v[cut, :].astype(F32)
            hidden_rows = resid + total
            gh_v[cut, :] = hidden_rows
            normed = (hidden_rows * inverse_rms(hidden_rows) * gain_ref[...]).astype(BF16)
            n2_v[pl.ds(pl.multiple_of((known + u) * sub + first, 16), 16), :] = normed
            spot = offset + first + lax.broadcasted_iota(jnp.int32, (16, 1), 0)
            valid = (spot < length).astype(F32)
            stat_ref[0] += fold_lanes(valid * resid * resid)
            stat_ref[1] += fold_lanes(valid * total * total)

        by_pieces(sub, body)
        late_store(u).start()

    def store_gb(u):
        cut = pl.ds(pl.multiple_of(u * sub, sub), sub)
        return pltpu.make_async_copy(gb_v, gb_hbm.at[cut, :], out_sem.at[1])

    def store_gh(u):
        at = pl.ds(pl.multiple_of(u % 2 * sub, sub), sub)
        return pltpu.make_async_copy(gh_v, gh_hbm.at[u // 8, at, :], out_sem.at[0])

    def finish(u):
        chain.total(u, total_v)
        load_hidden(u).wait()

        @pl.when(u >= 1)
        def _():
            store_gb(u - 1).wait()

        def body(piece_rows, first):
            e = total_v[piece_rows, :]
            hidden_rows = hid_v[piece_rows, :]
            inv = inverse_rms(hidden_rows)
            hat = hidden_rows * inv
            eg = e * gain_ref[...]
            grad = gf_v[pl.ds(pl.multiple_of(u * sub + first, 16), 16), :].astype(F32)
            gh = grad + inv * (eg - hat * jnp.mean(eg * hat, axis=-1, keepdims=True))
            gb_v[piece_rows, :] = gh.astype(BF16)

            @pl.when(u % 8 // 2 == rank)
            def _():
                gh_v[piece_rows, :] = gh

            both = e * hat
            gain_out[...] += both[:8] + both[8:]

        by_pieces(sub, body)
        store_gb(u).start()

        @pl.when(u % 8 // 2 == rank)
        def _():
            store_gh(u).start()
            store_gh(u).wait()

        @pl.when(u + 1 < subs)
        def _():
            load_hidden(u + 1).start()

    def serve(n):
        chain.middle(n)
        chain.outward(n - 2)

        @pl.when((n >= 4) & (n < 4 + subs))
        def _():
            finish(n - 4)

    quarter = width // 4

    def store_ffn(c):
        here = pl.ds(pl.multiple_of(c * rows, rows), rows)
        return [
            pltpu.make_async_copy(
                stage_row.at[c % 2, pl.ds(k * rows, rows), :], ffn_hbm.at[here, pl.ds(k * quarter, quarter)], ffn_sem.at[c % 2, k]
            )
            for k in range(4)
        ]

    def step(i, carry):
        slot, c, h = i % 2, i // hsteps, i % hsteps
        for copy in load_weights(i):
            copy.wait()

        @pl.when(i + 1 < steps)
        def _():
            for copy in load_weights(i + 1):
                copy.start()

        here = pl.ds(pl.multiple_of(c * rows, rows), rows)
        cols = pl.ds(pl.multiple_of(h * hb, hb), hb)
        n = n2_v[here, :]
        wide = min(256, hb)
        for q in range(hb // wide):
            part = slice(q * wide, (q + 1) * wide)
            gate = dot_nn(n[:, :half], wrow[slot, 0, 0, :, part]) + dot_nn(n[:, half:], wrow[slot, 0, 1, :, part])
            up = dot_nn(n[:, :half], wrow[slot, 1, 0, :, part]) + dot_nn(n[:, half:], wrow[slot, 1, 1, :, part])
            gi = gi_v[slot, :, part].astype(F32)
            sig = jax.nn.sigmoid(gate)
            silu = gate * sig
            at = pl.ds(pl.multiple_of(h * hb + q * wide, wide), wide)
            inner_v[here, at] = (silu * up).astype(BF16)
            gg_v[here, at] = (gi * up * sig * (1.0 + gate * (1.0 - sig))).astype(BF16)
            gu_v[here, at] = (gi * silu).astype(BF16)

        @pl.when(h == 0)
        def _():
            facc[...] = jnp.zeros_like(facc)
            gacc[...] = jnp.zeros_like(gacc)

        inner, gg, gu = inner_v[here, cols], gg_v[here, cols], gu_v[here, cols]
        span = min(512, half)
        for side in range(2):
            for q in range(half // span):
                part = slice(q * span, (q + 1) * span)
                cut = slice(side * half + q * span, side * half + (q + 1) * span)
                facc[:, cut] += dot_nn(inner, wcol[slot, side, :, part])
                gacc[:, cut] += dot_nt(gg, wrow[slot, 0, side, part, :]) + dot_nt(gu, wrow[slot, 1, side, part, :])

        @pl.when((h == hsteps - 1) & (c >= 2))
        def _():
            for copy in store_ffn(c - 2):
                copy.wait()

        @pl.when(h == hsteps - 1)
        def _():
            for k in range(per):
                part_v[c * per + k] = gacc[k * sub : (k + 1) * sub, :].astype(BF16)
                chain.begin(c * per + k)

            for k in range(4):
                stage_row[c % 2, k * rows : (k + 1) * rows, :] = facc[:, k * quarter : (k + 1) * quarter].astype(BF16)
            for copy in store_ffn(c):
                copy.start()

        @pl.when((i >= 2) & (i < 2 + late.count))
        def _():
            late.middle(i - 2)

        @pl.when((i >= 4) & (i < 4 + late.count))
        def _():
            late.outward(i - 4)

        @pl.when((i >= 6) & (i < 6 + late.count))
        def _():
            late_finish(i - 6)

        @pl.when(i == 9)
        def _():
            load_gf.wait()
            late_store(late.count - 1).wait()

        serve(i - 6)
        return carry

    lax.fori_loop(0, steps, step, 0)
    for c in range(2, steps // hsteps):
        for copy in store_ffn(c):
            copy.wait()

    pl.semaphore_signal(free_sem, inc=1, device_id=near_core, device_id_type=pl.DeviceIdType.MESH)
    outs = (dgate_hbm, dup_hbm, ddown_hbm)

    def landing(w, t):
        return wrow.at[t // 2, w, t % 2] if w < 2 else wcol.at[t // 2, t % 2]

    def landed(w, t, piece):
        return wrow[t // 2, w, t % 2, piece, :] if w < 2 else wcol[t // 2, t % 2, piece, :]

    def staging(w):
        return stage_row if w < 2 else stage_col

    def ship(w, t):
        return remote(staging(w).at[t % 2], landing(w, t), csend.at[w, t], crecv.at[w, t], near_core)

    def keep(w, t):
        cut = pl.ds(pl.multiple_of(t * hb, hb), hb)
        dst = outs[w].at[:, cut] if w < 2 else outs[w].at[cut, :]
        return pltpu.make_async_copy(staging(w).at[t % 2], dst, store_sem.at[w, t])

    def release(kind, w, t):
        if kind == 1:
            ship(w, t).wait_send()
        else:
            keep(w, t).wait()

    def group(kind, w, before, part):
        def one(t, carry):
            cut = pl.ds(pl.multiple_of(t * hb, hb), hb)
            mine = slice(kind * half, (kind + 1) * half)
            @pl.when(t >= 2)
            def _():
                release(kind, w, t - 2)

            if before is not None:

                @pl.when(t < 2)
                def _():
                    release(before[0], before[1], t + hsteps - 2)

            if kind == 0:
                ship(w, t).wait_recv()
            tall = staging(w).shape[1]
            size = min(256, tall)
            for q in range(tall // size):
                piece = slice(q * size, (q + 1) * size)
                if w == 2:
                    left = inner_v[:, pl.ds(pl.multiple_of(t * hb + q * size, size), size)]
                    value = dot_tn(left, gf_v[:, mine])
                else:
                    value = dot_tn(n2_v[:, kind * half + q * size : kind * half + (q + 1) * size], (gg_v, gu_v)[w][:, cut])
                if kind == 0:
                    value = value + landed(w, t, piece).astype(F32)
                staging(w)[t % 2, piece, :] = value.astype(BF16)
            if kind == 1:
                ship(w, t).start()
            else:
                keep(w, t).start()
            return carry

        lax.fori_loop(part * (hsteps // 2), (part + 1) * (hsteps // 2), one, 0)

    pl.semaphore_wait(free_sem, 1)

    def term(m):
        return ffn_hbm.at[pl.ds(pl.multiple_of(m * (2 * sub), 2 * sub), 2 * sub), :]

    fold = Fold(rank, term, None, ring_hbm, (ring_hbm.at[2], None), rsend, rrecv)
    after = iter(range(steps - 6, subs + 4))
    done = []

    def both(kind, w, before):
        for part in range(2):
            group(kind, w, before, part)
            done.append(part)
            if len(done) <= 8 or len(done) % 2 == 0:
                serve(next(after))
            if len(done) == 5:
                fold.begin()

    both(1, 0, None)
    both(0, 0, (1, 0))
    for t in range(hsteps - 2, hsteps):
        keep(0, t).wait()
    gate_sum = Scatter(
        row_blocks(dgate_hbm), wide_v.at[0], wide_v.at[1], half_rows(landx), half_rows(landy), temp_v, xsend, xrecv, xload, near_x, near_y
    )
    gate_sum.begin()
    both(1, 1, None)
    both(1, 2, None)
    gate_sum.pass_on()
    both(0, 1, (1, 1))
    both(0, 2, (1, 2))
    for n in after:
        serve(n)
    for t in range(hsteps - 2, hsteps):
        keep(1, t).wait()
        keep(2, t).wait()
    store_gb(subs - 1).wait()
    gate_sum.arrived()
    gate_sum.settle()
    chain.settle()

    @pl.when(fold.inner)
    def _():
        for k in range(3):
            fold.come(k)

    @pl.when(fold.outer)
    def _():
        for k in range(3):
            fold.inward(k).wait_send()

    late.settle()


def row_blocks(ref):
    size = ref.shape[0] // 4
    return lambda k, h: ref.at[pl.ds(k * size + h * (size // 2), size // 2), :]


def half_rows(ref):
    size = ref.shape[0] // 2
    return lambda h: ref.at[pl.ds(h * size, size), :]


def feed_both(lengths, n2, gf, gate, up, down, gi, rest, xr, hidden_rows, gain):
    tokens, width = n2.shape
    _, half, hidden = gate.shape
    hb = hidden // 4
    sub, rows = tokens // 16, tokens // 4
    count = rest.shape[0]
    any_space = pl.BlockSpec(memory_space=pl.ANY)
    vmem = pl.BlockSpec(memory_space=pltpu.VMEM)
    dma = pltpu.SemaphoreType.DMA
    moving = pltpu.VMEM((16, sub, width), BF16)
    late = pltpu.VMEM((count, sub, width), BF16)
    act = pltpu.VMEM((tokens, hidden), BF16)
    return pl.pallas_call(
        functools.partial(feed_both_kernel, hb, sub, rows),
        in_specs=[SMEM] + [any_space] * 9 + [vmem],
        out_specs=[any_space] * 10 + [vmem] * 2,
        out_shape=[
            shape((tokens, width), BF16), shape((tokens, width), BF16), shape((2, 2 * sub, width), F32),
            shape((half, hidden), BF16), shape((half, hidden), BF16), shape((hidden, half), BF16),
            shape((tokens, width), F32), shape((half // 4, hidden), BF16), shape((half // 4, hidden), BF16),
            shape((3, 2 * sub, width), BF16), shape((8, width), F32), shape((2, 8, 128), F32),
        ],
        scratch_shapes=[
            pltpu.VMEM((tokens, width), BF16), pltpu.VMEM((tokens, width), BF16), act, act, act,
            pltpu.VMEM((rows, width), F32), pltpu.VMEM((rows, width), F32),
            pltpu.VMEM((2, 2, 2, half, hb), BF16), pltpu.VMEM((2, 2, hb, half), BF16),
            moving, moving, moving, pltpu.VMEM((sub, width), F32),
            pltpu.VMEM((sub, width), F32), pltpu.VMEM((sub, width), F32), pltpu.VMEM((sub, width), BF16),
            pltpu.VMEM((2, half, hb), BF16), pltpu.VMEM((2, hb, half), BF16),
            late, late, late, pltpu.VMEM((sub, width), BF16), pltpu.VMEM((2, rows, hb), BF16),
            pltpu.VMEM((2, half // 8, hidden), BF16), pltpu.VMEM((2, half // 8, hidden), BF16), pltpu.VMEM((1, width), F32),
            dma((3,)), dma((2, 7)), dma((3, 16)), dma((3, 16)), dma(()), dma((2,)), dma((2, 4)), dma((3, 4)), dma((3, 4)),
            dma((3, 4)), dma((3, count)), dma((3, count)), dma(()), dma((6,)), dma((6,)), dma((3,)), dma((6,)), dma((6,)), pltpu.SemaphoreType.REGULAR,
        ],
        input_output_aliases={9: 6},
        compiler_params=pltpu.CompilerParams(vmem_limit_bytes=VMEM_MOST, collective_id=2, has_side_effects=True),
        cost_estimate=cost(18 * tokens * width * hidden, 60 * tokens * width),
        name="feed_forward_both",
    )(lengths, n2, gf, gate, up, down, gi, rest, xr, hidden_rows, gain)


class Fold:
    def __init__(self, rank, source, own, slots, finals, send, recv, landed=None):
        self.inner, self.outer = (rank % 3) != 0, (rank % 3) == 0
        self.side, self.mid = {"tensor": xor_one(rank)}, {"tensor": 3 - rank}
        self.leaving = (3 - rank, xor_one(3 - rank), xor_one(rank))
        self.added = (xor_one(3 - rank), 3 - rank, xor_one(rank))
        self.source, self.own, self.slots, self.finals = source, own, slots, finals
        self.send, self.recv, self.landed = send, recv, landed

    def inward(self, k):
        dst = self.slots.at[k] if k < 2 else self.finals[0]
        return remote(self.source(self.leaving[k]), dst, self.send.at[k], self.recv.at[k], self.side)

    def across(self, k):
        dst = self.slots.at[2] if k == 0 else self.finals[1]
        return remote(self.slots.at[k], dst, self.send.at[3 + k], self.recv.at[3 + k], self.mid)

    def outward(self):
        return remote(self.slots.at[2], self.finals[0], self.send.at[5], self.recv.at[5], self.side)

    def begin(self):
        @pl.when(self.outer)
        def _():
            for k in range(3):
                self.inward(k).start()

    def come(self, k):
        (self.landed[k].wait if self.landed is not None else self.inward(k).wait_recv)()

    def step(self, k):
        @pl.when(self.inner)
        def _():
            if k < 2:
                self.come(k)
            else:
                self.across(0).wait_recv()
            read = self.own(self.added[k])

            def body(cut, first):
                self.slots[k, cut, :] = (self.slots[k, cut, :].astype(F32) + read(cut).astype(F32)).astype(BF16)

            by_pieces(self.slots.shape[1], body)
            (self.across(k) if k < 2 else self.outward()).start()

    def arrived(self):
        @pl.when(self.inner)
        def _():
            self.come(2)
            self.across(1).wait_recv()

        @pl.when(self.outer)
        def _():
            self.outward().wait_recv()

    def settle(self):
        @pl.when(self.inner)
        def _():
            for k in range(2):
                self.across(k).wait_send()
            self.outward().wait_send()

        if self.landed is None:

            @pl.when(self.outer)
            def _():
                for k in range(3):
                    self.inward(k).wait_send()


def tall(ref):
    return 16 * max(1, 2048 // ref.shape[1])


class Scatter:
    def __init__(self, block, from_x, from_y, land_x, land_y, temps, send, recv, load, near_x, near_y):
        self.block, self.from_x, self.from_y, self.land_x, self.land_y = block, from_x, from_y, land_x, land_y
        self.temps, self.load = temps, load
        sem = lambda k: (send.at[k], recv.at[k])
        self.first = [
            remote(block(3, 0), from_x, *sem(0), near_x),
            remote(block(3, 1), from_y, *sem(1), near_y),
            remote(block(1, 0), land_x(0), *sem(2), near_x),
            remote(block(2, 1), land_y(1), *sem(3), near_y),
        ]
        self.second = [
            remote(from_y, land_x(1), *sem(4), near_x),
            remote(from_x, land_y(0), *sem(5), near_y),
        ]

    def begin(self):
        for copy in self.first:
            copy.start()

    def pass_on(self):
        loads = [
            pltpu.make_async_copy(self.block(1, 1), self.temps.at[0], self.load.at[0]),
            pltpu.make_async_copy(self.block(2, 0), self.temps.at[1], self.load.at[1]),
        ]
        for copy in loads:
            copy.start()
        for which, into in ((1, self.from_y), (0, self.from_x)):
            self.first[which].wait_recv()
            loads[1 - which].wait()
            temp = 1 - which

            def body(cut, first):
                into[cut, :] = (into[cut, :].astype(F32) + self.temps[temp, cut, :].astype(F32)).astype(BF16)

            by_pieces(into.shape[0], body, tall(into))
            self.second[temp].start()

    def arrived(self):
        for copy in self.first[2:] + self.second:
            copy.wait_recv()

    def finish(self, stage, out, store, landed=False):
        if not landed:
            self.arrived()
        for h in range(2):
            loads = [
                pltpu.make_async_copy(src, self.temps.at[k], self.load.at[k])
                for k, src in enumerate((self.block(0, h), self.land_x(h), self.land_y(h)))
            ]
            for copy in loads:
                copy.start()
            for copy in loads:
                copy.wait()

            def body(cut, first):
                stage[cut, :] = sum(self.temps[k, cut, :].astype(F32) for k in range(3))

            by_pieces(stage.shape[0], body, tall(stage))
            keep = pltpu.make_async_copy(stage, out(h), store)
            keep.start()
            keep.wait()

    def settle(self):
        for copy in self.first + self.second:
            copy.wait_send()


def backward_kernel(
    hd, nq, nk, block,
    len_ref, gb_hbm, hidden_hbm, ffn_hbm, ring_hbm, xr_hbm, n1_hbm, tok_hbm, outw_hbm, qkvw_hbm, all_hbm, att_hbm, inv_hbm, pre_hbm,
    dup_hbm, ddown_hbm, table_ref, stat_ref, stat2_ref, gain2_ref,
    out_hbm, fin_hbm, finb_hbm, own_hbm, mine_o, mine_q, landx1, landy1, landx2, landy2, landx3, landy3, landx4, landy4,
    lines_out, small_out,
    act_v, rows_v, qkvw_v, tok_v, all_v, att_v, inv_v, pre_v, grads, da_all, da_own, da_send, da_got, d_own, d_send, d_got, dpre_v,
    first_v, slots_v, turns_v, piece_v, wide_a, wide_b, temp_a, temp_b,
    go_v, so_v, wide_o, temp_o, gq_v, sq_v, wide_q, temp_q,
    tile_v, otile_v, lines_v, small_v, heads_v, lin1, lin2, lin3, small_r,
    load_sem, zsend, zrecv, piece_sem, xsend, xrecv, xload, own_sem, exsend, exrecv, osend, orecv, qsend, qrecv,
    tile_sem, outs_sem, smsend, smrecv,
):
    seqs, _, slots = all_v.shape
    span = slots // 2
    width = act_v.shape[1]
    half = width // 2
    groups = nq // nk
    share = span // 4
    row, core, rank = lax.axis_index("dp"), lax.axis_index("context"), lax.axis_index("tensor")
    start = core * span
    near = [row, xor_one(row), (row + 2) % 4, 3 - row]
    near_x, near_y, near_core = {"dp": near[1]}, {"dp": near[2]}, {"context": 1 - core}
    z_right, z_left, z_far = {"tensor": (rank + 1) % 4}, {"tensor": (rank + 3) % 4}, {"tensor": (rank + 2) % 4}
    first_core = core == 0

    def load(k, src, dst):
        copy = pltpu.make_async_copy(src, dst, load_sem.at[k])
        copy.start()
        return copy

    load_gb = load(0, gb_hbm, act_v)
    load_outw = load(1, outw_hbm, rows_v)
    load_att = [
        load(2, all_hbm, all_v), load(3, att_hbm, att_v), load(4, inv_hbm, inv_v), load(5, pre_hbm, pre_v),
    ]
    load_tok = load(6, tok_hbm, tok_v)
    load_qkvw = load(7, qkvw_hbm, qkvw_v)

    def piece_rows(s, m):
        return pl.ds(pl.multiple_of(s * span + m * share, share), share)

    def load_piece(s, m):
        return pltpu.make_async_copy(ffn_hbm.at[piece_rows(s, m), :], piece_v.at[s], piece_sem.at[s])

    greet([(None, d) for d in (near_x, near_y, {"dp": near[3]}, near_core, z_right, z_left, z_far)])

    last = seqs - 1
    inner = (rank % 3) != 0
    came = []
    for k, slot in enumerate((0, 1, 3)):
        came.append(pltpu.make_async_copy(ring_hbm.at[k], slots_v.at[0, slot], load_sem.at[12 + k]))

    @pl.when(inner)
    def _():
        for copy in came:
            copy.start()

    def ffn_own(s):
        def own(m):
            load_piece(s, m).wait()
            return lambda cut: piece_v[s, cut, :]

        return own

    def first_own(s):
        return lambda m: lambda cut: first_v[s, m, cut, :]

    ffn_rings = [
        Fold(
            rank, lambda m, s=s: ffn_hbm.at[piece_rows(s, m), :], ffn_own(s), slots_v.at[s], (slots_v.at[s, 3], slots_v.at[s, 4]),
            zsend.at[s], zrecv.at[s], came if s == 0 else None,
        )
        for s in range(seqs)
    ]
    first_rings = [
        Fold(
            rank, lambda m, s=s: first_v.at[s, m], first_own(s), turns_v.at[s], (fin_hbm.at[s], finb_hbm.at[s]),
            zsend.at[seqs + s], zrecv.at[seqs + s],
        )
        for s in range(seqs)
    ]
    for s in range(1, seqs):
        ffn_rings[s].begin()
    for s in range(seqs):
        load_piece(s, jnp.where(inner, ffn_rings[s].added[0], rank)).start()

    def ffn_step(s, k):
        ffn_rings[s].step(k)

        @pl.when(inner)
        def _():
            load_piece(s, ffn_rings[s].added[k + 1] if k < 2 else rank).start()

    def in_hbm(ref, axis):
        size = ref.shape[axis] // 4
        h2 = (size if axis == 0 else ref.shape[0]) // 2

        def get(k, h):
            if axis == 0:
                return ref.at[pl.ds(k * size + h * h2, h2), :]
            return ref.at[pl.ds(h * h2, h2), pl.ds(k * size, size)]

        return get

    def halves(ref):
        h2 = ref.shape[0] // 2
        return lambda h: ref.at[pl.ds(h * h2, h2), :]

    def in_vmem(ref):
        h2 = ref.shape[1] // 2
        return lambda k, h: ref.at[k, pl.ds(h * h2, h2), :]

    def scatter(i, get, wide, land_x, land_y, temps):
        return Scatter(get, wide.at[0], wide.at[1], land_x, land_y, temps, xsend.at[i], xrecv.at[i], xload.at[i], near_x, near_y)

    s_up = scatter(0, in_hbm(dup_hbm, 0), wide_a, halves(landx1), halves(landy1), temp_a)
    s_down = scatter(1, in_hbm(ddown_hbm, 1), wide_b, halves(landx2), halves(landy2), temp_b)
    s_out = scatter(2, in_vmem(go_v), wide_o, halves(landx3), halves(landy3), temp_o)
    s_qkv = scatter(3, in_vmem(gq_v), wide_q, halves(landx4), halves(landy4), temp_q)
    s_up.begin()
    ffn_step(0, 0)
    ffn_step(0, 1)

    load_gb.wait()
    load_outw.wait()

    def give(s):
        return remote(da_send.at[s], da_got.at[s], exsend.at[0, s], exrecv.at[0, s], near_core)

    def exchange(s):
        return remote(d_send.at[s], d_got.at[s], exsend.at[1, s], exrecv.at[1, s], near_core)

    def branch_rows(s, carry):
        here = pl.ds(pl.multiple_of(s * span, span), span)
        parts = []
        for q in range(2):
            cut = slice(q * (nq * hd // 2), (q + 1) * (nq * hd // 2))
            da = dot_nt(rows_v[0, cut, :], act_v[here, :half]) + dot_nt(rows_v[1, cut, :], act_v[here, half:])
            parts.append(da.astype(BF16))
        da_own[s] = jnp.where(first_core, parts[0], parts[1])
        da_send[s] = jnp.where(first_core, parts[1], parts[0])
        give(s).start()
        return carry

    lax.fori_loop(0, seqs, branch_rows, 0)

    def load_x(s):
        return [pltpu.make_async_copy(xr_hbm.at[s, :, pl.ds(k * half, half)], rows_v.at[k], load_sem.at[10 + k]) for k in range(2)]

    for copy in load_x(0):
        copy.start()
    for copy in load_att:
        copy.wait()

    scale = log2e / math.sqrt(hd)
    back = 1.0 / math.sqrt(hd)
    krow = lax.broadcasted_iota(jnp.int32, (block, groups * block), 0)
    qcol = lax.broadcasted_iota(jnp.int32, (block, groups * block), 1) % block
    base = groups * hd

    def attention(s):
        give(s).wait_recv()
        low, high = join_positions(core, da_own[s], da_got[s])
        da_all[:, :span] = low
        da_all[:, span:] = high
        length = len_ref[s]
        grads[base:, :] = jnp.zeros((2 * hd, slots), F32)
        for i in range(slots // block):
            cut = slice(i * block, (i + 1) * block)
            q = jnp.concatenate([all_v[s, g * hd : (g + 1) * hd, cut] for g in range(groups)], axis=1)
            da = jnp.concatenate([da_all[g * hd : (g + 1) * hd, cut] for g in range(groups)], axis=1)
            at = jnp.concatenate([att_v[s, g * hd : (g + 1) * hd, cut] for g in range(groups)], axis=1)
            inv = jnp.concatenate([inv_v[s, g : g + 1, cut] for g in range(groups)], axis=1)
            delta = jnp.sum(at.astype(F32) * da.astype(F32), axis=0, keepdims=True)
            dq = jnp.zeros((hd, groups * block), F32)
            for j in range(i + 1):
                kcut = slice(j * block, (j + 1) * block)
                key = all_v[s, base : base + hd, kcut]
                score = dot_tn(key, q) * scale
                ok = (krow + j * block) < length
                if j == i:
                    ok = ok & (krow <= qcol)
                p = jnp.where(ok, jnp.exp2(score) * inv, 0.0)
                dp = dot_tn(all_v[s, base + hd : base + 2 * hd, kcut], da)
                ds = (p * (dp - delta)).astype(BF16)
                dq = dq + dot_nn(key, ds)
                grads[base : base + hd, kcut] += dot_nt(q, ds) * back
                grads[base + hd : base + 2 * hd, kcut] += dot_nt(da, p.astype(BF16))
            dq = dq * back
            for g in range(groups):
                grads[g * hd : (g + 1) * hd, cut] = dq[:, g * block : (g + 1) * block]
        mine, theirs = join_positions(core, grads[:, :span], grads[:, span:])
        d_own[s] = mine.astype(BF16)
        d_send[s] = theirs.astype(BF16)
        exchange(s).start()

    quarter = hd // 2
    cosine, sine = table_ref[:quarter, :], table_ref[quarter : 2 * quarter, :]
    qgain, kgain = table_ref[2 * quarter : 2 * quarter + hd, 0:1], table_ref[2 * quarter + hd :, 0:1]
    sides = (nq // 2, nk // 2, nk // 2)
    copies_in_tensor = 1.0 / lax.axis_size("tensor")
    lines_v[:8, :] = jnp.zeros((8, width), F32)
    lines_v[8:, :] = gain2_ref[...] * copies_in_tensor
    heads_v[...] = jnp.zeros_like(heads_v)
    valid_slots = jnp.int32(0)
    for s in range(seqs):
        valid_slots = valid_slots + jnp.clip(len_ref[s] - start, 0, span)
    count = valid_slots.astype(F32) * (copies_in_tensor / 128.0)
    small_v[...] = jnp.zeros_like(small_v)
    for k in range(2):
        both = stat_ref[k] + stat2_ref[k]
        small_v[1 + k : 2 + k, :] = jnp.sum(both, axis=0, keepdims=True) * copies_in_tensor
    small_v[4:5, :] = jnp.broadcast_to(count, (1, 128))
    load_qkvw.wait()

    def fold_columns(values):
        return sum(values[:, k * 128 : (k + 1) * 128] for k in range(values.shape[1] // 128))

    def heads_rows(s):
        exchange(s).wait_recv()
        low, high = join_positions(core, d_own[s].astype(F32), d_got[s].astype(F32))
        parts = [[], [], []]
        for side in (low, high):
            at = 0
            for kind, number in enumerate(sides):
                for _ in range(number):
                    parts[kind].append(side[at : at + hd])
                    at += hd
        done = []
        for h in range(nq + nk):
            kind = 0 if h < nq else 1
            g = parts[kind][h - kind * nq]
            a, b = g[: hd // 2], g[hd // 2 :]
            g = jnp.concatenate([a * cosine + b * sine, b * cosine - a * sine], axis=0)
            v = pre_v[s, h * hd : (h + 1) * hd, :]
            inv = lax.rsqrt(jnp.mean(v * v, axis=0, keepdims=True) + epsilon)
            hat = v * inv
            heads_v[kind * hd : (kind + 1) * hd, :] += fold_columns(g * hat)
            gg = g * (qgain if kind == 0 else kgain)
            done.append(inv * (gg - hat * jnp.mean(gg * hat, axis=0, keepdims=True)))
        done += parts[2]
        for h in range(nq + 2 * nk):
            pair = h % 2
            if pair == 0:
                two = jnp.concatenate([done[h], done[h + 1]], axis=0).T.astype(BF16)
                dpre_v[pl.ds(pl.multiple_of(s * span, span), span), h * hd : (h + 2) * hd] = two
        for copy in load_x(s):
            copy.wait()
        for m in range(4):
            rows = slice(m * share, (m + 1) * share)
            xs = [rows_v[k, rows, :].astype(F32) for k in range(2)]
            mean = sum(jnp.sum(x * x, axis=-1, keepdims=True) for x in xs) * (1.0 / width)
            inv = lax.rsqrt(mean + epsilon)
            dpre = dpre_v[pl.ds(pl.multiple_of(s * span + m * share, share), share), :]
            for k in range(2):
                part = dot_nt(dpre, qkvw_v[k])
                cut = slice(k * half, (k + 1) * half)
                first_v[s, m, :, cut] = part.astype(BF16)
                both = part * (xs[k] * inv)
                lines_v[:8, cut] += sum(both[8 * r : 8 * r + 8] for r in range(share // 8))

    def sequence(s, carry):
        attention(s)

        @pl.when(s == last)
        def _():
            ffn_step(1, 1)
            s_up.pass_on()

        heads_rows(s)

        @pl.when(s == 0)
        def _():
            for copy in load_x(1):
                copy.start()
            first_rings[0].begin()
            ffn_step(1, 0)
            ffn_step(0, 2)
            s_down.begin()

        @pl.when(s == last)
        def _():
            first_rings[1].begin()

        return carry

    lax.fori_loop(0, seqs, sequence, 0)

    def hop_copies(n, items):
        return [remote(src, dst, smsend.at[n, i], smrecv.at[n, i], device) for i, (device, src, dst, _) in enumerate(items)]

    def hop_begin(n, items):
        for copy in hop_copies(n, items):
            copy.start()

    def hop_end(n, items):
        for copy in hop_copies(n, items):
            copy.wait()
        for _, _, dst, place_to in items:
            if place_to is None:
                small_v[...] += dst[...]
            else:
                lines_v[:, place_to] += dst[...]

    piece = width // 8

    def columns(k):
        return slice(k * piece, (k + 1) * piece)

    def view(k, count=1):
        return lines_v.at[:, pl.ds(k * piece, count * piece)]

    hop_core = [(near_core, view(4, 4), lin1, slice(0, half))]
    near_all = [near_x, near_y, {"dp": near[3]}]
    hop_lines = [(near_all[k], view(1 + k), lin2.at[k], columns(0)) for k in range(3)]
    hop_small = [(near_core, small_v, small_r.at[0], None)]
    hop_square = [(near_all[k], small_v, small_r.at[1 + k], None) for k in range(3)]
    z_all = [z_right, z_far, z_left]
    hop_chain = [(z_all[k], view(0), lin3.at[k], columns(0)) for k in range(3)]
    hop_chain += [(z_all[k], small_v, small_r.at[4 + k], None) for k in range(3)]
    hop_begin(0, hop_core)

    load_tok.wait()
    blocks_o = [remote(so_v.at[k], go_v.at[k], osend.at[k], orecv.at[k], near_core) for k in range(4)]
    size_o = half // 4
    for k in range(4):
        cut = slice(half + k * size_o, half + (k + 1) * size_o)
        so_v[k] = dot_tn(tok_v[...], act_v[:, cut]).astype(BF16)
        blocks_o[k].start()
    ffn_step(1, 2)
    for k in range(4):
        blocks_o[k].wait_recv()
        cut = slice(k * size_o, (k + 1) * size_o)
        go_v[k] = (dot_tn(tok_v[...], act_v[:, cut]) + go_v[k].astype(F32)).astype(BF16)
    s_out.begin()
    load_n1 = load(0, n1_hbm, act_v)
    hop_end(0, hop_core)
    hop_begin(1, hop_lines)
    load_n1.wait()
    blocks_q = [remote(sq_v.at[k], gq_v.at[k], qsend.at[k], qrecv.at[k], near_core) for k in range(4)]
    size_q = half // 4
    for k in range(4):
        cut = slice(half + k * size_q, half + (k + 1) * size_q)
        sq_v[k] = dot_tn(act_v[:, cut], dpre_v[...]).astype(BF16)
        blocks_q[k].start()
    for k in range(4):
        blocks_q[k].wait_recv()
        cut = slice(k * size_q, (k + 1) * size_q)
        gq_v[k] = (dot_tn(act_v[:, cut], dpre_v[...]) + gq_v[k].astype(F32)).astype(BF16)
    s_qkv.begin()
    keeps = [
        pltpu.make_async_copy(go_v.at[0], mine_o, own_sem.at[0]),
        pltpu.make_async_copy(gq_v.at[0], mine_q, own_sem.at[1]),
    ]
    keeps += [pltpu.make_async_copy(first_v.at[s, rank], own_hbm.at[s], own_sem.at[2 + s]) for s in range(seqs)]
    for copy in keeps:
        copy.start()


    def place(tile, dst, s):
        copies = []
        for o in range(2):
            for k in range(4):
                b = near[k] * 2 + (core if o == 0 else 1 - core)
                cut = pl.ds(pl.multiple_of(b * piece, piece), piece)
                copies.append(
                    pltpu.make_async_copy(tile.at[:, pl.ds((o * 4 + k) * piece, piece)], dst.at[s, :, cut], outs_sem.at[o * 4 + k])
                )
        return copies

    def out_share(s):
        keep = pltpu.make_async_copy(hidden_hbm.at[piece_rows(s, rank), :], tile_v, tile_sem.at[0])
        keep.start()
        ffn_rings[s].arrived()
        read = ffn_rings[s].own(rank)
        keep.wait()

        def body(cut, first):
            ffn = slots_v[s, 3, cut, :].astype(F32) + read(cut).astype(F32)
            ffn = ffn + jnp.where(inner, slots_v[s, 4, cut, :].astype(F32), 0.0)
            otile_v[cut, :] = (tile_v[cut, :] + ffn).astype(BF16)
            spot = start + rank * share + first + lax.broadcasted_iota(jnp.int32, (16, 1), 0)
            valid = (spot < len_ref[s]).astype(F32)
            small_v[3:4, :] += jnp.sum(fold_lanes(valid * ffn * ffn), axis=0, keepdims=True)

        by_pieces(share, body)
        copies = place(otile_v, out_hbm, s)
        for copy in copies:
            copy.start()
        for copy in copies:
            copy.wait()

    small_v[0:1, :] = jnp.sum(heads_v[...].T, axis=0, keepdims=True)
    first_rings[0].step(0)
    out_share(0)
    s_down.pass_on()
    out_share(1)
    hop_end(1, hop_lines)
    hop_begin(2, hop_small)
    hop_end(2, hop_small)
    hop_begin(3, hop_square)
    first_rings[0].step(1)
    first_rings[0].step(2)
    s_out.pass_on()
    s_qkv.pass_on()
    first_rings[1].step(0)
    hop_end(3, hop_square)
    hop_begin(4, hop_chain)
    first_rings[1].step(1)
    first_rings[1].step(2)
    hop_end(4, hop_chain)
    lines_out[...] = lines_v[:, :piece]
    small_out[...] = small_v[...]
    for item in (s_up, s_down, s_out, s_qkv):
        item.arrived()
    for ring in first_rings:
        ring.arrived()
    for copy in keeps:
        copy.wait()
    for ring in ffn_rings + first_rings:
        ring.settle()
    for item in (s_up, s_down, s_out, s_qkv):
        item.settle()
    for copy in blocks_o + blocks_q:
        copy.wait_send()
    for s in range(seqs):
        give(s).wait_send()
        exchange(s).wait_send()


def backward(
    lengths, gb, hidden_rows, ffn, ring, xr, n1, tok, outw, qkvw, everything, att, inv, pre, dup, ddown,
    table, stat, stat2, gain2_part, hd, nq, nk,
):
    seqs, span, width = xr.shape
    half = width // 2
    groups = nq // nk
    share = span // 4
    piece = width // 8
    hidden = dup.shape[1]
    cols = qkvw.shape[2]
    feat = nq * hd
    block = min(256, span)
    any_space = pl.BlockSpec(memory_space=pl.ANY)
    vmem = pl.BlockSpec(memory_space=pltpu.VMEM)
    dma = pltpu.SemaphoreType.DMA
    hold = lambda *dims: pltpu.VMEM(dims, BF16)
    wide = lambda *dims: pltpu.VMEM(dims, F32)
    big = [shape((seqs, share, width), BF16)] * 4 + [shape((feat, piece), BF16), shape((piece, cols), BF16)]
    big += [shape((piece, hidden), BF16)] * 2 + [shape((hidden, piece), BF16)] * 2
    big += [shape((feat, piece), BF16)] * 2 + [shape((piece, cols), BF16)] * 2
    small = [shape((16, piece), F32), shape((8, 128), F32)]
    rows = everything.shape[1]
    scratch = [
        hold(seqs * span, width), hold(2, span, half), hold(2, half, cols), hold(seqs * span, feat), hold(*everything.shape), hold(*att.shape),
        wide(*inv.shape), wide(*pre.shape), wide(rows, 2 * span), hold(groups * hd, 2 * span),
        hold(seqs, feat // 2, span), hold(seqs, feat // 2, span), hold(seqs, feat // 2, span),
        hold(seqs, rows, span), hold(seqs, rows, span), hold(seqs, rows, span), hold(seqs * span, cols),
        hold(seqs, 4, share, width), hold(seqs, 5, share, width), hold(seqs, 3, share, width), hold(seqs, share, width),
        hold(2, piece // 2, hidden), hold(2, hidden // 2, piece), hold(2, piece // 2, hidden), hold(2, hidden // 2, piece),
        hold(4, feat, piece), hold(4, feat, piece), hold(2, feat // 2, piece), hold(2, feat // 2, piece),
        hold(4, piece, cols), hold(4, piece, cols), hold(2, piece // 2, cols), hold(2, piece // 2, cols),
        wide(share, width), hold(share, width),
        wide(16, width), wide(8, 128), wide(2 * hd, 128), wide(16, half), wide(3, 16, piece), wide(3, 16, piece), wide(7, 8, 128),
        dma((15,)), dma((2 * seqs, 6)), dma((2 * seqs, 6)), dma((seqs,)), dma((4, 6)), dma((4, 6)), dma((4, 3)), dma((2 + seqs,)),
        dma((2, seqs)), dma((2, seqs)), dma((4,)), dma((4,)), dma((4,)), dma((4,)), dma((2,)), dma((8,)), dma((5, 6)), dma((5, 6)),
    ]
    tokens = seqs * span
    return pl.pallas_call(
        functools.partial(backward_kernel, hd, nq, nk, block),
        in_specs=[SMEM] + [any_space] * 15 + [vmem] * 4,
        out_specs=[any_space] * len(big) + [vmem] * 2,
        out_shape=big + small,
        scratch_shapes=scratch,
        compiler_params=pltpu.CompilerParams(vmem_limit_bytes=VMEM_MOST, collective_id=3, has_side_effects=True),
        cost_estimate=cost(4 * tokens * width * (cols + feat), 60 * tokens * width),
        name="attention_backward",
    )(
        lengths, gb, hidden_rows, ffn, ring, xr, n1, tok, outw, qkvw, everything, att, inv, pre, dup, ddown,
        table, stat, stat2, gain2_part,
    )


def results_kernel(
    hd, nqc, nkc, count,
    dgate, lx0, ly0, dup, lx1, ly1, ddown, lx2, ly2, mine_o, lx3, ly3, mine_q, lx4, ly4, gh, xr, fin, finb, own, out, gains_ref, lines_ref, small_ref,
    output, gin, ggate, gup, gdown, gout, gq, gk, gv, gain_a, gain_b, gain_q, gain_k, rms,
    gate_i, up_i, down_i, o_i, q_i, gate_o, up_o, down_o, o_o, q_o, gh_v, x_v, fin_v, finb_v, own_v, gin_v, out_v, in_sem, token_sem, out_sem, place_sem, copy_sem,
):
    row, core, rank = lax.axis_index("dp"), lax.axis_index("context"), lax.axis_index("tensor")
    near = [row, xor_one(row), (row + 2) % 4, 3 - row]
    seqs, share, width = gin_v.shape
    piece = width // 8
    sums = (
        (dgate.at[pl.ds(0, piece), :], lx0, ly0, gate_i, gate_o, ((0, ggate),)),
        (dup.at[pl.ds(0, piece), :], lx1, ly1, up_i, up_o, ((0, gup),)),
        (ddown.at[:, pl.ds(0, piece)], lx2, ly2, down_i, down_o, ((0, gdown),)),
        (mine_o, lx3, ly3, o_i, o_o, ((0, gout),)),
        (mine_q, lx4, ly4, q_i, q_o, ((0, gq), (nqc, gk), (nqc + nkc, gv))),
    )
    into_out = pltpu.make_async_copy(out, out_v, copy_sem.at[0])
    into_out.start()
    through = pltpu.make_async_copy(out_v, output, copy_sem.at[1])

    def loads(i):
        one, two, three, into = sums[i][:4]
        return [pltpu.make_async_copy(src, into.at[k], in_sem.at[i, k]) for k, src in enumerate((one, two, three))]

    mine = pl.ds(pl.multiple_of(rank * share, share), share)
    tokens = [
        pltpu.make_async_copy(src, dst, token_sem.at[k])
        for k, (src, dst) in enumerate(((gh, gh_v), (xr.at[:, mine, :], x_v), (fin, fin_v), (finb, finb_v), (own, own_v)))
    ]
    for copy in tokens:
        copy.start()

    first = jnp.sum(lines_ref[:8, :], axis=0, keepdims=True)
    second = jnp.sum(lines_ref[8:, :], axis=0, keepdims=True)
    gain_a[...] = first.reshape(gain_a.shape)
    gain_b[...] = second.reshape(gain_b.shape)
    gain_q[...] = small_ref[0:1, :hd].reshape(gain_q.shape)
    gain_k[...] = small_ref[0:1, hd : 2 * hd].reshape(gain_k.shape)
    total = jnp.sum(small_ref[4:5, :], keepdims=True) * count
    for k in range(3):
        square = jnp.sum(small_ref[1 + k : 2 + k, :], keepdims=True) / total
        rms[k] = jnp.max(jnp.sqrt(jnp.broadcast_to(square, (8, 128))))

    into_out.wait()
    through.start()
    gain = jnp.concatenate([gains_ref[b, 0:1, :] for b in range(8)], axis=1).astype(F32)
    for copy in tokens:
        copy.wait()
    for i in range(len(sums)):
        for copy in loads(i):
            copy.start()
    inner = (rank % 3) != 0
    stores = []
    for s in range(seqs):

        def body(cut, at):
            e = fin_v[s, cut, :].astype(F32) + own_v[s, cut, :].astype(F32)
            e = e + jnp.where(inner, finb_v[s, cut, :].astype(F32), 0.0)
            x = x_v[s, cut, :].astype(F32)
            inv = inverse_rms(x)
            hat = x * inv
            eg = e * gain
            gin_v[s, cut, :] = gh_v[s, cut, :] + inv * (eg - hat * jnp.mean(eg * hat, axis=-1, keepdims=True))

        by_pieces(share, body)
        for o in range(2):
            for k in range(4):
                b = near[k] * 2 + (core if o == 0 else 1 - core)
                cut = pl.ds(pl.multiple_of(b * piece, piece), piece)
                src = gin_v.at[s, :, pl.ds((o * 4 + k) * piece, piece)]
                stores.append(pltpu.make_async_copy(src, gin.at[s, :, cut], place_sem.at[s, o * 4 + k]))
                stores[-1].start()

    for i, (_, _, _, came, total_v, parts) in enumerate(sums):
        for copy in loads(i):
            copy.wait()

        def body(cut, at):
            total_v[cut, :] = sum(came[k, cut, :].astype(F32) for k in range(3))

        by_pieces(total_v.shape[0], body, tall(total_v))
        for n, (at, dst) in enumerate(parts):
            stores.append(pltpu.make_async_copy(total_v.at[:, pl.ds(at, dst.shape[1])], dst, out_sem.at[i, n]))
            stores[-1].start()
    for copy in stores + [through]:
        copy.wait()


def finish_results(pairs, mine_o, mine_q, lands_o, lands_q, gh, xr, fin, finb, own, out, gains, lines, small, hd, nqc, nkc):
    (dgate, lx0, ly0), (dup, lx1, ly1), (ddown, lx2, ly2) = pairs
    seqs, share, width = out.shape
    hidden = dgate.shape[1]
    piece = width // 8
    any_space = pl.BlockSpec(memory_space=pl.ANY)
    vmem = pl.BlockSpec(memory_space=pltpu.VMEM)
    dma = pltpu.SemaphoreType.DMA
    blocks = [(piece, hidden), (piece, hidden), (hidden, piece), mine_o.shape, mine_q.shape]
    outs = [shape(out.shape, BF16), shape(out.shape, F32)] + [shape(b, F32) for b in blocks[:4]]
    outs += [shape((piece, size), F32) for size in (nqc, nkc, nkc)]
    tiny = [shape((size,), F32) for size in (piece, piece, hd, hd)]
    token = pltpu.VMEM(out.shape, BF16)
    return pl.pallas_call(
        functools.partial(results_kernel, hd, nqc, nkc, float(width)),
        in_specs=[any_space] * 21 + [vmem] * 3,
        out_specs=[any_space] * len(outs) + [vmem] * 4 + [SMEM],
        out_shape=outs + tiny + [shape((3,), F32)],
        scratch_shapes=[pltpu.VMEM((3,) + tuple(b), BF16) for b in blocks]
        + [pltpu.VMEM(b, F32) for b in blocks]
        + [pltpu.VMEM(out.shape, F32), token, token, token, token, pltpu.VMEM(out.shape, F32), token]
        + [dma((5, 3)), dma((5,)), dma((5, 3)), dma((seqs, 8)), dma((2,))],
        compiler_params=PARAMS,
        cost_estimate=cost(30 * piece * hidden, 60 * piece * hidden),
        name="results",
    )(dgate, lx0, ly0, dup, lx1, ly1, ddown, lx2, ly2, mine_o, *lands_o, mine_q, *lands_q, gh, xr, fin, finb, own, out, gains, lines, small)


def per_device_general(
    inputs,
    cotangent,
    lengths,
    w_query,
    key_projection_weight,
    value_projection_weight,
    w_output,
    w_gate,
    w_up,
    w_down,
    attn_gain,
    ffn_gain,
    query_gain,
    key_gain,
):
    seqs, span, width = inputs.shape
    hd = query_gain.shape[0]
    nq = w_query.shape[1] // hd
    nk = key_projection_weight.shape[1] // hd
    groups = nq // nk
    dp = lax.axis_size("dp")
    tensor = lax.axis_size("tensor")
    core = lax.axis_index("context")
    rank = lax.axis_index("tensor")
    chunks = 2
    rows = span // chunks
    share = span // tensor
    lengths = lengths.astype(jnp.int32)
    start = (core * span).astype(jnp.int32)
    core1 = core.astype(jnp.int32).reshape(1)
    ids = block_order(dp, core)
    order = 2 * dp if (width // (2 * dp)) % 128 == 0 else 1

    positions = start + jnp.arange(span, dtype=jnp.int32)
    freqs = rope_base ** (-(jnp.arange(hd // 2, dtype=F32) * (2.0 / hd)))
    angles = freqs[:, None] * positions.astype(F32)[None, :]
    cosine, sine = jnp.cos(angles), jnp.sin(angles)
    qgain = query_gain.astype(F32).reshape(hd, 1)
    kgain = key_gain.astype(F32).reshape(hd, 1)

    w_qkv = jnp.concatenate([w_query, key_projection_weight, value_projection_weight], axis=1)
    saved = []
    gains = gather_blocks(jnp.stack([attn_gain, ffn_gain]), 1)
    gains = jnp.concatenate([gains[0], gains[1]], axis=1).astype(F32)
    gain1, gain2 = gains[0:1], gains[1:2]
    qkv = gather_blocks(w_qkv, 0)
    out_w = gather_blocks(w_output, 1)
    gate = gather_blocks(w_gate, 0)
    up = gather_blocks(w_up, 0)
    down = gather_blocks(w_down, 1)

    scal = jnp.concatenate([lengths, start.reshape(1), ids])
    x_in, cot_in = inputs, cotangent
    if order == 1:
        x_in, cot_in = to_relative(x_in, dp, core), to_relative(cot_in, dp, core)
    xr, n1, gf = begin(x_in, cot_in, gain1, scal, order)

    parts, tok = [], []
    for s in range(seqs):
        pre, own, oth = heads(n1, s, qkv, cosine, sine, qgain, kgain, core1, hd, nq, nk)
        seq_scal = jnp.stack([lengths[s], core.astype(jnp.int32)])
        everything, att, inv, mine, theirs = attend(seq_scal, own, over_core(oth), groups)
        branched = branch(mine, over_core(theirs), out_w, core1, chunks)
        saved.append((pre, everything, att, inv, seq_scal))
        tok.append(jnp.swapaxes(branched[0], 0, 1))
        parts.append(branched[1:])
    tok = jnp.concatenate(tok, axis=0)

    stats = jnp.zeros((2,), F32)
    hidden_all, n2_all = [], []
    for s in range(seqs):
        for k in range(chunks):
            terms = [lax.psum(parts[s][k], "tensor")]
            place = jnp.stack([lengths[s], start + k * rows])
            hidden, n2, stat = second_norm(place, xr, s, k, gain2, terms)
            hidden_all.append(hidden)
            n2_all.append(n2)
            stats = stats + stat[:2, 0]
    hidden_all, n2_all = jnp.concatenate(hidden_all), jnp.concatenate(n2_all)

    ffn_squares = jnp.zeros((), F32)
    out_shares = []

    def piece_of(arrays):
        per = arrays[0].shape[0] // share

        def piece(k):
            found = lax.dynamic_slice_in_dim(arrays[0], jnp.minimum(k, per - 1) * share, share, 0)
            for m in range(1, len(arrays)):
                here = lax.dynamic_slice_in_dim(arrays[m], jnp.clip(k - m * per, 0, per - 1) * share, share, 0)
                found = jnp.where(k >= m * per, here, found)
            return found

        return piece

    def share_scalars(s):
        head = jnp.stack([rank.astype(jnp.int32), lengths[s], start + rank.astype(jnp.int32) * share, jnp.int32(tensor)])
        return jnp.concatenate([head, ids])

    def flat(nested):
        return [item for inner_list in nested for item in inner_list]

    def slices(array, count):
        size = array.shape[0] // count
        return [array[i * size : (i + 1) * size] for i in range(count)]

    def reduced(lefts, rights, axis):
        oth = weight_grad(lefts, rights, 1, axis)
        own = weight_grad(lefts, rights, 0, axis, over_core(oth))
        return scatter_blocks(own, axis)

    inner, gg, gu, ffn, gn = [[[None] * chunks for _ in range(seqs)] for _ in range(5)]
    for s in range(seqs):
        for k in range(chunks):
            inner[s][k], gg[s][k], gu[s][k], ffn[s][k], gn[s][k] = feed(
                n2_all, s * chunks + k, rows, gf, s, k, gate, up, down
            )
    gain2_grad = jnp.zeros((1, width), F32)
    gb, gh = [[[None] * chunks for _ in range(seqs)] for _ in range(2)]
    for s in range(seqs):
        for k in range(chunks):
            terms = [lax.psum(gn[s][k], "tensor")]
            gb[s][k], gh[s][k], gain_part = second_back(hidden_all, s * chunks + k, gf, s, k, gain2, terms)
            gain2_grad = gain2_grad + gain_part
    gf_list = slices(gf.reshape(seqs * span, width), seqs * chunks)
    n2_list = slices(n2_all, seqs * chunks)
    grad_w_down = reduced(flat(inner), gf_list, 1)
    grad_w_gate = reduced(n2_list, flat(gg), 0)
    grad_w_up = reduced(n2_list, flat(gu), 0)
    for s in range(seqs):
        got = ring_scatter(piece_of(ffn[s]), tensor, rank)
        halves = [hidden_all[(s * chunks + k) * rows : (s * chunks + k + 1) * rows] for k in range(chunks)]
        out, stat = output_share(share_scalars(s), got, ffn[s], halves, order)
        out_shares.append(out)
        ffn_squares = ffn_squares + stat[0, 0]

    gain1_grad = jnp.zeros((1, width), F32)
    head_gain = jnp.zeros((2 * hd,), F32)
    dpres, in_shares = [], []
    for s in range(seqs):
        pre, everything, att, inv, seq_scal = saved[s]
        da_own, da_oth = branch_back(gb[s], out_w, core1)
        d_own, d_oth = attend_back(seq_scal, everything, att, inv, da_own, over_core(da_oth), groups)
        dpre, first, gain_part, hg = heads_back(
            d_own, over_core(d_oth), pre, cosine, sine, qgain, kgain, xr, s, qkv, core1, hd, nq, nk
        )
        gain1_grad = gain1_grad + gain_part
        head_gain = head_gain + hg[:, 0]
        dpres.append(dpre)
        got = ring_scatter(piece_of([first]), tensor, rank)
        in_shares.append(input_share(share_scalars(s), got, first, gh[s], xr, s, gain1, order))

    att_list = [tok[i * rows : (i + 1) * rows] for i in range(seqs * chunks)]
    grad_w_output = reduced(att_list, flat(gb), 1)
    grad_qkv = reduced([n1[s] for s in range(seqs)], dpres, 0)
    nqc, nkc = nq * hd, nk * hd
    grad_w_query = grad_qkv[:, :nqc]
    grad_w_key = grad_qkv[:, nqc : nqc + nkc]
    grad_w_value = grad_qkv[:, nqc + nkc :]

    gain2_grad = gain2_grad / tensor
    counts = jnp.sum(jnp.clip(lengths - start, 0, span)).astype(F32) / tensor
    small = jnp.concatenate([head_gain, stats / tensor, ffn_squares.reshape(1), counts.reshape(1)])
    small = jnp.pad(small, (0, (-small.shape[0]) % 128)).reshape(1, -1)
    lines = jnp.concatenate([gain1_grad, gain2_grad], axis=0)
    piece = width // (2 * dp)
    lines = to_absolute(lines, dp, core)
    lines, small = lax.psum((lines, small), ("dp", "context", "tensor"))
    lines = lax.dynamic_slice_in_dim(lines, lax.axis_index(("dp", "context")) * piece, piece, 1)
    small = small[0]
    rms_values = jnp.sqrt(small[2 * hd : 2 * hd + 3] / (small[2 * hd + 3] * width))

    output = jnp.stack(out_shares)
    grad_inputs = jnp.stack(in_shares)
    if order == 1:
        output, grad_inputs = to_absolute(output, dp, core), to_absolute(grad_inputs, dp, core)
    return (
        output,
        grad_inputs,
        grad_w_query,
        grad_w_key,
        grad_w_value,
        grad_w_output,
        grad_w_gate,
        grad_w_up,
        grad_w_down,
        lines[0],
        lines[1],
        small[:hd],
        small[hd : 2 * hd],
        rms_values,
    )


def per_device_square(
    inputs,
    cotangent,
    lengths,
    w_query,
    key_projection_weight,
    value_projection_weight,
    w_output,
    w_gate,
    w_up,
    w_down,
    attn_gain,
    ffn_gain,
    query_gain,
    key_gain,
):
    seqs, span, width = inputs.shape
    hd = query_gain.shape[0]
    nq = w_query.shape[1] // hd
    nk = key_projection_weight.shape[1] // hd
    lengths = lengths.astype(jnp.int32)
    all_gains = jnp.concatenate([attn_gain, ffn_gain, query_gain, key_gain]).reshape(1, -1)
    (
        xr, n1, gf, qkv, out_w, gate, up, down, hidden, n2, rest, gi, pre, everything, att, tok, gains, table, inv, stat
    ) = forward(
        lengths, inputs, cotangent, w_query, key_projection_weight, value_projection_weight, w_output, w_gate, w_up, w_down,
        all_gains, hd, nq, nk,
    )
    tokens = seqs * span
    flat = lambda a: a.reshape(tokens, -1)
    ffn, gb, gh, d_gate, d_up, d_down, hidden, landx, landy, ring, gain2_part, stat2 = feed_both(
        lengths, n2, flat(gf), gate, up, down, gi, rest, flat(xr), hidden, gains
    )
    output, fin, finb, own, mine_o, mine_q, lx1, ly1, lx2, ly2, lx3, ly3, lx4, ly4, lines, small = backward(
        lengths, gb, hidden, ffn, ring, xr, flat(n1), flat(tok), out_w, qkv,
        everything, att, inv, pre, d_up, d_down, table, stat, stat2, gain2_part, hd, nq, nk,
    )
    nqc, nkc = nq * hd, nk * hd
    pairs = ((d_gate, landx, landy), (d_up, lx1, ly1), (d_down, lx2, ly2))
    output, grad_inputs, grad_gate, grad_up, grad_down, grad_out, grad_q, grad_k, grad_v, *small = finish_results(
        pairs, mine_o, mine_q, (lx3, ly3), (lx4, ly4), gh, xr, fin, finb, own, output, gains,
        lines, small, hd, nqc, nkc,
    )
    return (output, grad_inputs, grad_q, grad_k, grad_v, grad_out, grad_gate, grad_up, grad_down, *small)


def per_device(*args):
    inputs, w_query = args[0], args[3]
    seqs, span, width = inputs.shape
    square = lax.axis_size("dp") == 4 and lax.axis_size("tensor") == 4 and lax.axis_size("context") == 2
    if square and width % 2048 == 0 and span % 512 == 0 and seqs == 2 and w_query.shape[1] == span:
        return per_device_square(*args)
    return per_device_general(*args)


def solution(mesh):
    both = ("dp", "context")
    rows = P(both, "tensor")
    cols = P("tensor", both)
    shares = P("dp", ("context", "tensor"), None)
    acts = P("dp", "context", None)
    return jax.shard_map(
        per_device,
        mesh=mesh,
        in_specs=(acts, acts, P("dp"), rows, rows, rows, cols, rows, rows, cols, P(both), P(both), P(), P()),
        out_specs=(shares, shares, rows, rows, rows, cols, rows, rows, cols, P(both), P(both), P(), P(), P()),
        check_vma=False,
    )
```

```python
import functools
import math

import jax
import jax.numpy as jnp
from jax import lax
from jax.experimental import pallas as pl
from jax.experimental.pallas import tpu as pltpu
from jax.sharding import PartitionSpec as P

F32 = jnp.float32
BF16 = jnp.bfloat16
epsilon = 1e-05
rope_base = 1000000.0
log2e = 1.4426950408889634
VMEM_BYTES = 60 * 1024 * 1024
VMEM_MOST = 63 * 1024 * 1024
PARAMS = pltpu.CompilerParams(vmem_limit_bytes=VMEM_BYTES)
SMEM = pl.BlockSpec(memory_space=pltpu.SMEM)
SWAP = ((0, 1), (1, 0))


def shape(dims, dtype):
    return jax.ShapeDtypeStruct(tuple(dims), dtype)


def cost(flops, size, exps=0):
    return pl.CostEstimate(flops=int(flops), bytes_accessed=int(size), transcendentals=int(exps))


def dot_nn(a, b):
    return lax.dot_general(a, b, (((1,), (0,)), ((), ())), preferred_element_type=F32)


def dot_nt(a, b):
    return lax.dot_general(a, b, (((1,), (1,)), ((), ())), preferred_element_type=F32)


def dot_tn(a, b):
    return lax.dot_general(a, b, (((0,), (0,)), ((), ())), preferred_element_type=F32)


def inverse_rms(values):
    return lax.rsqrt(jnp.mean(values * values, axis=-1, keepdims=True) + epsilon)


def block_order(dp, core):
    return jnp.stack([jnp.int32(k) * 2 + (core ^ o) for o in range(2) for k in range(dp)]).astype(jnp.int32)


def to_relative(values, dp, core):
    lead = values.shape[:-1]
    parts = values.reshape(lead + (dp, 2, -1))
    parts = jnp.where(core == 0, parts, parts[..., ::-1, :])
    return jnp.swapaxes(parts, -3, -2).reshape(values.shape)


def to_absolute(values, dp, core):
    lead = values.shape[:-1]
    parts = jnp.swapaxes(values.reshape(lead + (2, dp, -1)), -3, -2)
    return jnp.where(core == 0, parts, parts[..., ::-1, :]).reshape(values.shape)


def over_core(value):
    return lax.ppermute(value, "context", SWAP)


def gather_blocks(weight, axis):
    own = lax.all_gather(weight, "dp", axis=axis, tiled=True)
    return jnp.stack([own, over_core(own)])


def scatter_blocks(total, axis):
    return lax.psum_scatter(total, "dp", scatter_dimension=axis, tiled=True).astype(F32)


def ring_scatter(piece, tensor, rank):
    ring = [(i, (i + 1) % tensor) for i in range(tensor)]
    moving = piece((rank + tensor - 1) % tensor)
    for step in range(1, tensor):
        moving = lax.ppermute(moving, "tensor", ring)
        if step < tensor - 1:
            moving = (moving.astype(F32) + piece((rank + tensor - 1 - step) % tensor).astype(F32)).astype(BF16)
    return moving


def begin_kernel(order, x_ref, cot_ref, gain_ref, scal_ref, xr_ref, n1_ref, gf_ref):
    seq, tile = pl.program_id(0), pl.program_id(1)
    rows, width = x_ref.shape[1:]
    seqs = pl.num_programs(0)
    place = scal_ref[seqs] + tile * rows + lax.broadcasted_iota(jnp.int32, (rows, 1), 0)
    valid = (place < scal_ref[seq]).astype(F32)
    x = x_ref[0].astype(F32)
    inv = inverse_rms(x)
    piece = width // order
    for k in range(order):
        src = pl.ds(pl.multiple_of(scal_ref[seqs + 1 + k] * piece, piece), piece) if order > 1 else slice(0, width)
        dst = slice(k * piece, (k + 1) * piece)
        part = x_ref[0, :, src]
        xr_ref[0, :, dst] = part
        n1_ref[0, :, dst] = (part.astype(F32) * inv * gain_ref[:, dst]).astype(BF16)
        gf_ref[0, :, dst] = (cot_ref[0, :, src].astype(F32) * valid).astype(BF16)


def begin(x, cot, gain, scalars, order):
    seqs, span, width = x.shape
    rows = min(256, span)
    spec = pl.BlockSpec((1, rows, width), lambda s, i: (s, i, 0))
    return pl.pallas_call(
        functools.partial(begin_kernel, order),
        grid=(seqs, span // rows),
        in_specs=[spec, spec, pl.BlockSpec((1, width), lambda s, i: (0, 0)), SMEM],
        out_specs=[spec] * 3,
        out_shape=[shape(x.shape, BF16)] * 3,
        compiler_params=PARAMS,
        cost_estimate=cost(8 * x.size, 10 * x.size),
        name="first_norm",
    )(x, cot, gain, scalars)


def heads_kernel(hd, nq, nk, n1_ref, w_ref, cos_ref, sin_ref, qg_ref, kg_ref, core_ref, pre_ref, own_ref, oth_ref):
    half = w_ref.shape[1]
    x = n1_ref[0]
    flat = dot_nn(x[:, :half], w_ref[0]) + dot_nn(x[:, half:], w_ref[1])
    turned = flat.T
    span = turned.shape[1]
    normed = turned[: (nq + nk) * hd]
    pre_ref[...] = normed
    core = core_ref[0]
    cosine, sine = cos_ref[...], sin_ref[...]
    done = []
    for h in range(nq + nk):
        v = normed[h * hd : (h + 1) * hd]
        inv = lax.rsqrt(jnp.mean(v * v, axis=0, keepdims=True) + epsilon)
        v = v * inv * (qg_ref[...] if h < nq else kg_ref[...])
        a, b = v[: hd // 2], v[hd // 2 :]
        done.append(jnp.concatenate([a * cosine - b * sine, b * cosine + a * sine], axis=0))
    for h in range(nk):
        lo = (nq + nk + h) * hd
        done.append(turned[lo : lo + hd])
    parts = [[], []]
    for start, count in ((0, nq), (nq, nk), (nq + nk, nk)):
        for side in range(2):
            parts[side] += done[start + side * count // 2 : start + (side + 1) * count // 2]
    low = jnp.concatenate(parts[0], axis=0)
    high = jnp.concatenate(parts[1], axis=0)
    first = core == 0
    own_ref[...] = jnp.where(first, low, high).astype(BF16)
    oth_ref[...] = jnp.where(first, high, low).astype(BF16)


def heads(n1, seq, weight, cosine, sine, qgain, kgain, core, hd, nq, nk):
    span, width = n1.shape[1:]
    sides = (nq + 2 * nk) * hd // 2
    full = pl.BlockSpec(memory_space=pltpu.VMEM)
    whole = lambda a: pl.BlockSpec(a.shape, lambda i: (0,) * a.ndim)
    outs = [shape(((nq + nk) * hd, span), F32), shape((sides, span), BF16), shape((sides, span), BF16)]
    return pl.pallas_call(
        functools.partial(heads_kernel, hd, nq, nk),
        grid=(1,),
        in_specs=[pl.BlockSpec((1, span, width), lambda i: (seq, 0, 0))]
        + [whole(a) for a in (weight, cosine, sine, qgain, kgain)]
        + [SMEM],
        out_specs=[whole(o) for o in outs],
        out_shape=outs,
        compiler_params=PARAMS,
        cost_estimate=cost(2 * span * width * weight.shape[2], 2 * span * width + 2 * weight.size),
        name="query_key_value",
    )(n1, weight, cosine, sine, qgain, kgain, core)


def join_positions(core, own, oth):
    first = core == 0
    return jnp.where(first, own, oth), jnp.where(first, oth, own)


def attend_kernel(block, groups, scal_ref, own_ref, got_ref, all_ref, att_ref, inv_ref, ao_ref, ax_ref):
    span = own_ref.shape[1]
    hd = own_ref.shape[0] // (groups + 2)
    length, core = scal_ref[0], scal_ref[1]
    low, high = join_positions(core, own_ref[...], got_ref[...])
    all_ref[:, :span] = low
    all_ref[:, span:] = high
    scale = log2e / math.sqrt(hd)
    krow = lax.broadcasted_iota(jnp.int32, (block, groups * block), 0)
    qcol = lax.broadcasted_iota(jnp.int32, (block, groups * block), 1) % block
    base = groups * hd
    for i in range(2 * span // block):
        cut = slice(i * block, (i + 1) * block)
        q = jnp.concatenate([all_ref[g * hd : (g + 1) * hd, cut] for g in range(groups)], axis=1)
        acc = jnp.zeros((hd, groups * block), F32)
        total = jnp.zeros((1, groups * block), F32)
        for j in range(i + 1):
            kcut = slice(j * block, (j + 1) * block)
            s = dot_tn(all_ref[base : base + hd, kcut], q) * scale
            ok = (krow + j * block) < length
            if j == i:
                ok = ok & (krow <= qcol)
            e = jnp.where(ok, jnp.exp2(s), 0.0)
            total = total + jnp.sum(e, axis=0, keepdims=True)
            acc = acc + dot_nn(all_ref[base + hd : base + 2 * hd, kcut], e.astype(BF16))
        inv = 1.0 / total
        att = (acc * inv).astype(BF16)
        for g in range(groups):
            att_ref[g * hd : (g + 1) * hd, cut] = att[:, g * block : (g + 1) * block]
            inv_ref[g : g + 1, cut] = inv[:, g * block : (g + 1) * block]
    mine, theirs = join_positions(core, att_ref[:, :span], att_ref[:, span:])
    ao_ref[...] = mine
    ax_ref[...] = theirs


def attend(scalars, own, got, groups):
    rows, span = own.shape
    hd = rows // (groups + 2)
    block = min(256, span)
    full = pl.BlockSpec(memory_space=pltpu.VMEM)
    return pl.pallas_call(
        functools.partial(attend_kernel, block, groups),
        in_specs=[SMEM, full, full],
        out_specs=[full] * 5,
        out_shape=[
            shape((rows, 2 * span), BF16),
            shape((groups * hd, 2 * span), BF16),
            shape((groups, 2 * span), F32),
            shape((groups * hd, span), BF16),
            shape((groups * hd, span), BF16),
        ],
        compiler_params=PARAMS,
        cost_estimate=cost(60 * groups * hd * span * span, 12 * rows * span, 4 * groups * span * span),
        name="attend_forward",
    )(scalars, own, got)


def branch_kernel(own_ref, got_ref, w_ref, core_ref, att_ref, *outs):
    half = w_ref.shape[2]
    low, high = join_positions(core_ref[0], own_ref[...], got_ref[...])
    att = jnp.concatenate([low, high], axis=0)
    att_ref[...] = att
    rows = outs[0].shape[0]
    for k, out in enumerate(outs):
        part = att[:, k * rows : (k + 1) * rows]
        out[:, :half] = dot_tn(part, w_ref[0]).astype(BF16)
        out[:, half:] = dot_tn(part, w_ref[1]).astype(BF16)


def branch(own, got, weight, core, chunks):
    rows, span = own.shape
    width = 2 * weight.shape[2]
    full = pl.BlockSpec(memory_space=pltpu.VMEM)
    return pl.pallas_call(
        branch_kernel,
        in_specs=[full] * 3 + [SMEM],
        out_specs=[full] * (1 + chunks),
        out_shape=[shape((2 * rows, span), BF16)] + [shape((span // chunks, width), BF16)] * chunks,
        compiler_params=PARAMS,
        cost_estimate=cost(4 * rows * span * width, 4 * rows * width + 2 * span * width),
        name="attention_branch",
    )(own, got, weight, core)


def second_norm_kernel(terms, scal_ref, x_ref, gain_ref, *refs):
    term_refs, (hidden_ref, n2_ref, stat_ref) = refs[:terms], refs[terms:]
    rows = hidden_ref.shape[0]
    branch_sum = term_refs[0][...].astype(F32)
    for ref in term_refs[1:]:
        branch_sum = branch_sum + ref[...].astype(F32)
    resid = x_ref[0].astype(F32)
    hidden = resid + branch_sum
    hidden_ref[...] = hidden
    n2_ref[...] = (hidden * inverse_rms(hidden) * gain_ref[...]).astype(BF16)
    place = scal_ref[1] + lax.broadcasted_iota(jnp.int32, (rows, 1), 0)
    valid = (place < scal_ref[0]).astype(F32)
    first = jnp.sum(valid * resid * resid, keepdims=True)
    second = jnp.sum(valid * branch_sum * branch_sum, keepdims=True)
    line = lax.broadcasted_iota(jnp.int32, (8, 128), 0)
    stat_ref[...] = jnp.where(line == 0, first, second)


def second_norm(scalars, xr, seq, part, gain, terms):
    rows, width = terms[0].shape
    flat = pl.BlockSpec((rows, width), lambda i: (0, 0))
    return pl.pallas_call(
        functools.partial(second_norm_kernel, len(terms)),
        grid=(1,),
        in_specs=[SMEM, pl.BlockSpec((1, rows, width), lambda i: (seq, part, 0)), pl.BlockSpec((1, width), lambda i: (0, 0))]
        + [flat] * len(terms),
        out_specs=[flat, flat, pl.BlockSpec((8, 128), lambda i: (0, 0))],
        out_shape=[shape((rows, width), F32), shape((rows, width), BF16), shape((8, 128), F32)],
        compiler_params=PARAMS,
        cost_estimate=cost(20 * rows * width, (8 + 2 * len(terms)) * rows * width),
        name="second_norm",
    )(scalars, xr, gain, *terms)


def feed_kernel(n_ref, g_ref, wgo, wgx, wuo, wux, wdo, wdx, inner_ref, gg_ref, gu_ref, ffn_ref, gn_ref, facc, gacc):
    step = pl.program_id(0)
    half = wgo.shape[0]
    no, nx = n_ref[:, :half], n_ref[:, half:]
    gate = dot_nn(no, wgo[...]) + dot_nn(nx, wgx[...])
    up = dot_nn(no, wuo[...]) + dot_nn(nx, wux[...])
    gi = dot_nt(g_ref[0, :, :half], wdo[...]) + dot_nt(g_ref[0, :, half:], wdx[...])
    sig = jax.nn.sigmoid(gate)
    silu = gate * sig
    inner = (silu * up).astype(BF16)
    gg = (gi * up * sig * (1.0 + gate * (1.0 - sig))).astype(BF16)
    gu = (gi * silu).astype(BF16)
    inner_ref[...] = inner
    gg_ref[...] = gg
    gu_ref[...] = gu

    @pl.when(step == 0)
    def _():
        facc[...] = jnp.zeros_like(facc)
        gacc[...] = jnp.zeros_like(gacc)

    facc[:, :half] += dot_nn(inner, wdo[...])
    facc[:, half:] += dot_nn(inner, wdx[...])
    gacc[:, :half] += dot_nt(gg, wgo[...]) + dot_nt(gu, wuo[...])
    gacc[:, half:] += dot_nt(gg, wgx[...]) + dot_nt(gu, wux[...])

    @pl.when(step == pl.num_programs(0) - 1)
    def _():
        ffn_ref[...] = facc[...].astype(BF16)
        gn_ref[...] = gacc[...].astype(BF16)


def feed(n2, chunk, rows, gf, seq, part, gate, up, down):
    width = n2.shape[1]
    _, half, hidden = gate.shape
    hb = min(512, hidden)
    row = [pl.BlockSpec((None, half, hb), lambda h, side=side: (side, 0, h)) for side in range(2)]
    col = [pl.BlockSpec((None, hb, half), lambda h, side=side: (side, h, 0)) for side in range(2)]
    whole = pl.BlockSpec((rows, width), lambda h: (0, 0))
    tile = pl.BlockSpec((rows, hb), lambda h: (0, h))
    return pl.pallas_call(
        feed_kernel,
        grid=(hidden // hb,),
        in_specs=[pl.BlockSpec((rows, width), lambda h: (chunk, 0)), pl.BlockSpec((1, rows, width), lambda h: (seq, part, 0))] + row + row + col,
        out_specs=[tile, tile, tile, whole, whole],
        out_shape=[shape((rows, hidden), BF16)] * 3 + [shape((rows, width), BF16)] * 2,
        scratch_shapes=[pltpu.VMEM((rows, width), F32), pltpu.VMEM((rows, width), F32)],
        compiler_params=PARAMS,
        cost_estimate=cost(12 * rows * width * hidden, 12 * half * hidden + 14 * rows * width, rows * hidden),
        name="feed_forward",
    )(n2, gf, gate, gate, up, up, down, down)


def second_back_kernel(terms, hidden_ref, gf_ref, gain_ref, *refs):
    term_refs, (gb_ref, gh_ref, gain_out) = refs[:terms], refs[terms:]
    e = term_refs[0][...].astype(F32)
    for ref in term_refs[1:]:
        e = e + ref[...].astype(F32)
    hidden = hidden_ref[...]
    inv = inverse_rms(hidden)
    hat = hidden * inv
    eg = e * gain_ref[...]
    gh = gf_ref[0].astype(F32) + inv * (eg - hat * jnp.mean(eg * hat, axis=-1, keepdims=True))
    gh_ref[...] = gh
    gb_ref[...] = gh.astype(BF16)
    gain_out[...] = jnp.sum(e * hat, axis=0, keepdims=True)


def second_back(hidden, chunk, gf, seq, part, gain, terms):
    rows, width = terms[0].shape
    flat = pl.BlockSpec((rows, width), lambda i: (0, 0))
    line = pl.BlockSpec((1, width), lambda i: (0, 0))
    return pl.pallas_call(
        functools.partial(second_back_kernel, len(terms)),
        grid=(1,),
        in_specs=[pl.BlockSpec((rows, width), lambda i: (chunk, 0)), pl.BlockSpec((1, rows, width), lambda i: (seq, part, 0)), line]
        + [flat] * len(terms),
        out_specs=[flat, flat, line],
        out_shape=[shape((rows, width), BF16), shape((rows, width), F32), shape((1, width), F32)],
        compiler_params=PARAMS,
        cost_estimate=cost(20 * rows * width, (12 + 2 * len(terms)) * rows * width),
        name="second_norm_back",
    )(hidden, gf, gain, *terms)


def branch_back_kernel(chunks, *refs):
    gb_refs, (w_ref, core_ref, own_ref, oth_ref) = refs[:chunks], refs[chunks:]
    half = w_ref.shape[2]
    rows = gb_refs[0].shape[0]
    heads_half = own_ref.shape[0]
    first = core_ref[0] == 0
    for k, ref in enumerate(gb_refs):
        da = dot_nt(w_ref[0], ref[:, :half]) + dot_nt(w_ref[1], ref[:, half:])
        da = da.astype(BF16)
        low, high = da[:heads_half], da[heads_half:]
        cut = slice(k * rows, (k + 1) * rows)
        own_ref[:, cut] = jnp.where(first, low, high)
        oth_ref[:, cut] = jnp.where(first, high, low)


def branch_back(gbs, weight, core):
    chunks = len(gbs)
    rows, width = gbs[0].shape
    dim = weight.shape[1]
    full = pl.BlockSpec(memory_space=pltpu.VMEM)
    return pl.pallas_call(
        functools.partial(branch_back_kernel, chunks),
        in_specs=[full] * (chunks + 1) + [SMEM],
        out_specs=[full] * 2,
        out_shape=[shape((dim // 2, chunks * rows), BF16)] * 2,
        compiler_params=PARAMS,
        cost_estimate=cost(2 * dim * chunks * rows * width, 2 * dim * width + 2 * chunks * rows * width),
        name="attention_branch_back",
    )(*gbs, weight, core)


def attend_back_kernel(block, groups, scal_ref, all_ref, att_ref, inv_ref, own_ref, got_ref, out_own, out_oth, da_all, grads):
    span = own_ref.shape[1]
    hd = all_ref.shape[0] // (groups + 2)
    length, core = scal_ref[0], scal_ref[1]
    low, high = join_positions(core, own_ref[...], got_ref[...])
    da_all[:, :span] = low
    da_all[:, span:] = high
    scale = log2e / math.sqrt(hd)
    back = 1.0 / math.sqrt(hd)
    krow = lax.broadcasted_iota(jnp.int32, (block, groups * block), 0)
    qcol = lax.broadcasted_iota(jnp.int32, (block, groups * block), 1) % block
    base = groups * hd
    grads[base:, :] = jnp.zeros((2 * hd, 2 * span), F32)
    for i in range(2 * span // block):
        cut = slice(i * block, (i + 1) * block)

        def rows(ref):
            return jnp.concatenate([ref[g * hd : (g + 1) * hd, cut] for g in range(groups)], axis=1)

        q = rows(all_ref)
        da = rows(da_all)
        inv = jnp.concatenate([inv_ref[g : g + 1, cut] for g in range(groups)], axis=1)
        delta = jnp.sum(rows(att_ref).astype(F32) * da.astype(F32), axis=0, keepdims=True)
        dq = jnp.zeros((hd, groups * block), F32)
        for j in range(i + 1):
            kcut = slice(j * block, (j + 1) * block)
            key = all_ref[base : base + hd, kcut]
            s = dot_tn(key, q) * scale
            ok = (krow + j * block) < length
            if j == i:
                ok = ok & (krow <= qcol)
            p = jnp.where(ok, jnp.exp2(s) * inv, 0.0)
            dp = dot_tn(all_ref[base + hd : base + 2 * hd, kcut], da)
            ds = (p * (dp - delta)).astype(BF16)
            dq = dq + dot_nn(key, ds)
            grads[base : base + hd, kcut] += dot_nt(q, ds) * back
            grads[base + hd : base + 2 * hd, kcut] += dot_nt(da, p.astype(BF16))
        dq = dq * back
        for g in range(groups):
            grads[g * hd : (g + 1) * hd, cut] = dq[:, g * block : (g + 1) * block]
    mine, theirs = join_positions(core, grads[:, :span], grads[:, span:])
    out_own[...] = mine.astype(BF16)
    out_oth[...] = theirs.astype(BF16)


def attend_back(scalars, everything, att, inv, own, got, groups):
    rows, slots = everything.shape
    span = slots // 2
    block = min(256, span)
    full = pl.BlockSpec(memory_space=pltpu.VMEM)
    return pl.pallas_call(
        functools.partial(attend_back_kernel, block, groups),
        in_specs=[SMEM] + [full] * 5,
        out_specs=[full] * 2,
        out_shape=[shape((rows, span), BF16)] * 2,
        scratch_shapes=[pltpu.VMEM(att.shape, BF16), pltpu.VMEM((rows, slots), F32)],
        compiler_params=PARAMS,
        cost_estimate=cost(30 * att.shape[0] * slots * slots, 12 * rows * slots, groups * slots * slots),
        name="attend_backward",
    )(scalars, everything, att, inv, own, got)


def heads_back_kernel(hd, nq, nk, own_ref, got_ref, pre_ref, cos_ref, sin_ref, qg_ref, kg_ref, x_ref, w_ref, core_ref, dpre_ref, first_ref, gain_ref, hgain_ref):
    half = w_ref.shape[1]
    low, high = join_positions(core_ref[0], own_ref[...].astype(F32), got_ref[...].astype(F32))
    sides = (nq // 2, nk // 2, nk // 2)
    grads = [[], [], []]
    for side in (low, high):
        at = 0
        for kind, count in enumerate(sides):
            for h in range(count):
                grads[kind].append(side[at : at + hd])
                at += hd
    cosine, sine = cos_ref[...], sin_ref[...]
    done = []
    sums = [0.0, 0.0]
    for h in range(nq + nk):
        kind = 0 if h < nq else 1
        g = grads[kind][h - kind * nq]
        a, b = g[: hd // 2], g[hd // 2 :]
        g = jnp.concatenate([a * cosine + b * sine, b * cosine - a * sine], axis=0)
        v = pre_ref[h * hd : (h + 1) * hd, :]
        inv = lax.rsqrt(jnp.mean(v * v, axis=0, keepdims=True) + epsilon)
        hat = v * inv
        sums[kind] = sums[kind] + jnp.sum(g * hat, axis=1, keepdims=True)
        gg = g * (qg_ref[...] if kind == 0 else kg_ref[...])
        done.append(inv * (gg - hat * jnp.mean(gg * hat, axis=0, keepdims=True)))
    done += grads[2]
    hgain_ref[:hd, :] = jnp.broadcast_to(sums[0], (hd, 128))
    hgain_ref[hd:, :] = jnp.broadcast_to(sums[1], (hd, 128))
    dpre = jnp.concatenate(done, axis=0).T.astype(BF16)
    dpre_ref[...] = dpre
    x = x_ref[0].astype(F32)
    hat = x * inverse_rms(x)
    for k in range(2):
        cut = slice(k * half, (k + 1) * half)
        part = dot_nt(dpre, w_ref[k])
        first_ref[:, cut] = part.astype(BF16)
        gain_ref[:, cut] = jnp.sum(part * hat[:, cut], axis=0, keepdims=True)


def heads_back(own, got, pre, cosine, sine, qgain, kgain, xr, seq, weight, core, hd, nq, nk):
    span = own.shape[1]
    _, half, cols = weight.shape
    width = 2 * half
    whole = lambda a: pl.BlockSpec(a.shape, lambda i: (0,) * len(a.shape))
    outs = [shape((span, cols), BF16), shape((span, width), BF16), shape((1, width), F32), shape((2 * hd, 128), F32)]
    return pl.pallas_call(
        functools.partial(heads_back_kernel, hd, nq, nk),
        grid=(1,),
        in_specs=[whole(a) for a in (own, got, pre, cosine, sine, qgain, kgain)]
        + [pl.BlockSpec((1, span, width), lambda i: (seq, 0, 0)), whole(weight), SMEM],
        out_specs=[whole(o) for o in outs],
        out_shape=outs,
        compiler_params=PARAMS,
        cost_estimate=cost(2 * span * width * cols, 4 * span * width + 4 * half * cols),
        name="query_key_value_back",
    )(own, got, pre, cosine, sine, qgain, kgain, xr, weight, core)


def place_blocks(order, ids, first_id, value, out_ref):
    piece = value.shape[-1] // order
    for k in range(order):
        if order == 1:
            out_ref[...] = value
        else:
            dst = pl.ds(pl.multiple_of(ids[first_id + k] * piece, piece), piece)
            out_ref[:, dst] = value[:, k * piece : (k + 1) * piece]


def output_kernel(order, scal_ref, got_ref, f0_ref, f1_ref, h0_ref, h1_ref, out_ref, stat_ref):
    low = scal_ref[0] * 2 < scal_ref[3]
    rows = out_ref.shape[0]
    ffn = got_ref[...].astype(F32) + jnp.where(low, f0_ref[...], f1_ref[...]).astype(F32)
    hidden = jnp.where(low, h0_ref[...], h1_ref[...])
    place = scal_ref[2] + lax.broadcasted_iota(jnp.int32, (rows, 1), 0)
    valid = (place < scal_ref[1]).astype(F32)
    stat_ref[...] = jnp.broadcast_to(jnp.sum(valid * ffn * ffn, keepdims=True), (8, 128))
    place_blocks(order, scal_ref, 4, (hidden + ffn).astype(BF16), out_ref)


def share_specs(rows, width, per):
    return [
        pl.BlockSpec((rows, width), lambda i, s: (jnp.minimum(s[0], per - 1), 0)),
        pl.BlockSpec((rows, width), lambda i, s: (jnp.maximum(s[0] - per, 0), 0)),
    ]


def output_share(scalars, got, ffns, hiddens, order):
    rows, width = got.shape
    pair = share_specs(rows, width, ffns[0].shape[0] // rows)
    flat = pl.BlockSpec((rows, width), lambda i, s: (0, 0))
    return pl.pallas_call(
        functools.partial(output_kernel, order),
        grid_spec=pltpu.PrefetchScalarGridSpec(
            num_scalar_prefetch=1,
            grid=(1,),
            in_specs=[flat] + pair + pair,
            out_specs=[flat, pl.BlockSpec((8, 128), lambda i, s: (0, 0))],
        ),
        out_shape=[shape((rows, width), BF16), shape((8, 128), F32)],
        compiler_params=PARAMS,
        cost_estimate=cost(6 * rows * width, 16 * rows * width),
        name="output_share",
    )(scalars, got, *ffns, *hiddens)


def input_kernel(order, scal_ref, got_ref, part_ref, g0_ref, g1_ref, x_ref, gain_ref, out_ref):
    low = scal_ref[0] * 2 < scal_ref[3]
    e = got_ref[...].astype(F32) + part_ref[...].astype(F32)
    gh = jnp.where(low, g0_ref[...], g1_ref[...])
    x = x_ref[0].astype(F32)
    inv = inverse_rms(x)
    hat = x * inv
    eg = e * gain_ref[...]
    value = gh + inv * (eg - hat * jnp.mean(eg * hat, axis=-1, keepdims=True))
    place_blocks(order, scal_ref, 4, value, out_ref)


def input_share(scalars, got, part, ghs, xr, seq, gain, order):
    rows, width = got.shape
    pair = share_specs(rows, width, ghs[0].shape[0] // rows)
    flat = pl.BlockSpec((rows, width), lambda i, s: (0, 0))
    return pl.pallas_call(
        functools.partial(input_kernel, order),
        grid_spec=pltpu.PrefetchScalarGridSpec(
            num_scalar_prefetch=1,
            grid=(1,),
            in_specs=[flat, pl.BlockSpec((rows, width), lambda i, s: (s[0], 0))]
            + pair
            + [pl.BlockSpec((1, rows, width), lambda i, s: (seq, s[0], 0)), pl.BlockSpec((1, width), lambda i, s: (0, 0))],
            out_specs=flat,
        ),
        out_shape=shape((rows, width), F32),
        compiler_params=PARAMS,
        cost_estimate=cost(12 * rows * width, 20 * rows * width),
        name="input_share",
    )(scalars, got, part, *ghs, xr, gain)


def weight_grad_kernel(count, extra, *refs):
    a_refs, b_refs, out = refs[:count], refs[count : 2 * count], refs[-1]
    total = dot_tn(a_refs[0][...], b_refs[0][...])
    for a, b in zip(a_refs[1:], b_refs[1:]):
        total = total + dot_tn(a[...], b[...])
    if extra:
        total = total + refs[2 * count][...].astype(F32)
    out[...] = total.astype(BF16)


def weight_grad(lefts, rights, side, axis, add=None):
    count = len(lefts)
    rows_all, cols_all = lefts[0].shape[1], rights[0].shape[1]
    dims = [rows_all, cols_all]
    dims[axis] //= 2
    rows, cols = min(512, dims[0]), min(2048, dims[1])
    row_at = side * (dims[0] // rows) if axis == 0 else 0
    col_at = side * (dims[1] // cols) if axis == 1 else 0
    specs = [pl.BlockSpec((a.shape[0], rows), lambda j, i: (0, i + row_at)) for a in lefts]
    specs += [pl.BlockSpec((b.shape[0], cols), lambda j, i: (0, j + col_at)) for b in rights]
    tile = pl.BlockSpec((rows, cols), lambda j, i: (i, j))
    tokens = sum(a.shape[0] for a in lefts)
    return pl.pallas_call(
        functools.partial(weight_grad_kernel, count, add is not None),
        grid=(dims[1] // cols, dims[0] // rows),
        in_specs=specs + ([tile] if add is not None else []),
        out_specs=tile,
        out_shape=shape(dims, BF16),
        compiler_params=PARAMS,
        cost_estimate=cost(2 * tokens * dims[0] * dims[1], 2 * tokens * sum(dims) + 2 * dims[0] * dims[1]),
        name="weight_grad",
    )(*lefts, *rights, *([add] if add is not None else []))


def xor_one(index):
    return index + 1 - 2 * (index % 2)


def remote(src, dst, send, recv, device):
    return pltpu.make_async_remote_copy(
        src_ref=src, dst_ref=dst, send_sem=send, recv_sem=recv, device_id=device, device_id_type=pl.DeviceIdType.MESH
    )


def greet(others):
    barrier = pltpu.get_barrier_semaphore()
    count = 0
    for needed, device in others:
        if needed is None:
            pl.semaphore_signal(barrier, inc=1, device_id=device, device_id_type=pl.DeviceIdType.MESH)
            count = count + 1
        else:

            @pl.when(needed)
            def _():
                pl.semaphore_signal(barrier, inc=1, device_id=device, device_id_type=pl.DeviceIdType.MESH)

            count = count + jnp.where(needed, 1, 0)
    pl.semaphore_wait(barrier, count)


class Gather:
    def __init__(self, shard, dst, axis, send, recv, local, near_x, near_y, near_core):
        piece = shard.shape[axis]
        half = shard.shape[0] // 2

        def block(side, k):
            cut = pl.ds(k * piece, piece)
            return dst.at[side, cut, :] if axis == 0 else dst.at[side, :, cut]

        def part(k, h):
            if axis == 0:
                return dst.at[0, pl.ds(k * piece + h * half, half), :]
            return dst.at[0, pl.ds(h * half, half), pl.ds(k * piece, piece)]

        link, cross = send.at[0], send.at[1]
        self.local = pltpu.make_async_copy(shard, block(0, 0), local)
        self.x = remote(shard, block(0, 1), link, recv.at[0], near_x)
        self.y = remote(shard, block(0, 2), link, recv.at[1], near_y)
        self.dx = remote(part(2, 0), part(3, 0), link, recv.at[2], near_x)
        self.dy = remote(part(1, 1), part(3, 1), link, recv.at[2], near_y)
        self.cores = [remote(shard if k == 0 else block(0, k), block(1, k), cross, recv.at[3], near_core) for k in range(4)]
        cut = pl.ds(0, 3 * piece)
        three = dst.at[0, cut, :] if axis == 0 else dst.at[0, :, cut]
        self.all_links = remote(three, three, link, recv.at[0], near_x)
        self.diagonal = remote(block(0, 3), block(0, 3), link, recv.at[2], near_x)
        self.all_cores = remote(dst.at[0], dst.at[1], cross, recv.at[3], near_core)

    def first(self):
        self.x.start()
        self.y.start()
        self.cores[0].start()
        self.local.start()

    def second(self):
        self.y.wait_recv()
        self.dx.start()
        self.cores[2].start()
        self.x.wait_recv()
        self.dy.start()
        self.cores[1].start()

    def third(self):
        self.diagonal.wait_recv()
        self.cores[3].start()

    def arrived(self):
        self.local.wait()
        self.all_cores.wait_recv()

    def sent(self):
        self.all_links.wait_send()
        self.all_cores.wait_send()


def forward_kernel(
    hd, nq, nk, block, sub,
    len_ref, x_hbm, cot_hbm, wq_hbm, wk_hbm, wv_hbm, wout, wgate, wup, wdown, again_ref, fgain_ref, qgain_ref, kgain_ref,
    xr_hbm, n1_hbm, gf_hbm, qkv_hbm, out_hbm, gate_hbm, up_hbm, down_hbm, hidden_hbm, n2_hbm, rest_hbm, gi_hbm, pre_hbm, all_hbm, att_hbm, tok_hbm,
    gains_ref, table_ref, inv_ref, stat_ref,
    xr_v, cot_v, n1_v, qkv_v, out_v, ex_own, ex_send, ex_got, at_own, at_send, at_got,
    part_v, in_v, back_v, total_v, hid_v, norm_v, wqkv, gain_ref, down_v, gi_v, pre_ref, all_ref, att_ref, tok_ref,
    keep_sem, load_sem, store_sem, shard_sem, rest_sem, down_sem, gi_sem, wsend, wrecv, wloc, gsend, grecv, exsend, exrecv, zsend, zrecv, hid_sem,
):
    seqs, span, width = xr_v.shape
    groups = nq // nk
    row, core, rank = lax.axis_index("dp"), lax.axis_index("context"), lax.axis_index("tensor")
    start = core * span
    near = [row, xor_one(row), (row + 2) % 4, 3 - row]
    inner = (rank % 3) != 0
    near_x, near_y, near_core = {"dp": near[1]}, {"dp": near[2]}, {"context": 1 - core}
    z_side, z_mid = {"tensor": xor_one(rank)}, {"tensor": 3 - rank}
    piece = width // 8
    total_subs = part_v.shape[0]
    per = span // sub
    first_core = core == 0

    loads = []
    for at, (src, dst) in enumerate(((x_hbm, xr_v), (cot_hbm, cot_v))):
        for s in range(seqs):
            for o in range(2):
                for k in range(4):
                    b = near[k] * 2 + (core if o == 0 else 1 - core)
                    cut = pl.ds(pl.multiple_of(b * piece, piece), piece)
                    loads.append(
                        pltpu.make_async_copy(
                            src.at[s, :, cut], dst.at[s, :, pl.ds((o * 4 + k) * piece, piece)], load_sem.at[at]
                        )
                    )
    shards, at = [], 0
    for k, ref in enumerate((wq_hbm, wk_hbm, wv_hbm)):
        shards.append(pltpu.make_async_copy(ref, wqkv.at[:, pl.ds(at, ref.shape[1])], shard_sem.at[k]))
        at += ref.shape[1]
    for copy in shards + loads:
        copy.start()
    piece = width // 8
    wide_gains = [ref[...].astype(F32).reshape(1, piece) for ref in (again_ref, fgain_ref)]
    gain_ref[...] = jnp.concatenate(wide_gains + [jnp.zeros((14, piece), F32)], axis=0).astype(BF16)

    others = []
    for o in range(2):
        for k in range(4):
            if o or k:
                others.append((o * 4 + k, {"dp": near[k], "context": core if o == 0 else 1 - core}))
    greet([(None, d) for _, d in others] + [(None, z_side), (inner, z_mid)])

    gains = [remote(gain_ref, gains_ref.at[b], gsend, grecv, d) for b, d in others]
    every_gain = remote(gains_ref.at[pl.ds(1, 7)], gains_ref.at[pl.ds(1, 7)], gsend, grecv, near_core)
    for copy in gains:
        copy.start()
    weights = [
        Gather(shard, dst, axis, wsend.at[i], wrecv.at[i], wloc.at[i], near_x, near_y, near_core)
        for i, (shard, dst, axis) in enumerate(
            ((wqkv, qkv_v, 0), (wout, out_v, 1), (wgate, gate_hbm, 0), (wup, up_hbm, 0), (wdown, down_hbm, 1))
        )
    ]
    w_qkv, w_out, w_gate, w_up, w_down = weights
    for copy in shards:
        copy.wait()
    w_qkv.first()
    gains_ref[0] = gain_ref[...]

    quarter = hd // 2
    freqs = jnp.exp(lax.broadcasted_iota(jnp.int32, (quarter, span), 0).astype(F32) * (-2.0 * math.log(rope_base) / hd))
    angles = freqs * (start + lax.broadcasted_iota(jnp.int32, (quarter, span), 1)).astype(F32)
    cosine, sine = jnp.cos(angles), jnp.sin(angles)
    turned = [jnp.broadcast_to(ref[...].astype(F32).reshape(1, hd), (8, hd)).T for ref in (qgain_ref, kgain_ref)]
    qgain, kgain = turned[0][:, 0:1], turned[1][:, 0:1]
    table_ref[:quarter, :] = cosine
    table_ref[quarter : 2 * quarter, :] = sine
    table_ref[2 * quarter : 2 * quarter + hd, :128] = jnp.broadcast_to(qgain, (hd, 128))
    table_ref[2 * quarter + hd :, :128] = jnp.broadcast_to(kgain, (hd, 128))

    pltpu.make_async_copy(cot_hbm, cot_v, load_sem.at[1]).wait()

    def mask_rows(i, carry):
        s, t = i // (span // 16), i % (span // 16)
        cut = pl.ds(pl.multiple_of(t * 16, 16), 16)
        place = start + t * 16 + lax.broadcasted_iota(jnp.int32, (16, 1), 0)
        valid = (place < len_ref[s]).astype(F32)
        cot_v[s, cut, :] = (cot_v[s, cut, :].astype(F32) * valid).astype(BF16)
        return carry

    lax.fori_loop(0, seqs * span // 16, mask_rows, 0)
    store_gf = pltpu.make_async_copy(cot_v, gf_hbm, store_sem.at[0])
    store_gf.start()
    pltpu.make_async_copy(x_hbm, xr_v, load_sem.at[0]).wait()
    store_xr = pltpu.make_async_copy(xr_v, xr_hbm, store_sem.at[1])
    store_xr.start()
    every_gain.wait_recv()
    gain1 = jnp.concatenate([gains_ref[b, 0:1, :] for b in range(8)], axis=1).astype(F32)
    gain2 = jnp.concatenate([gains_ref[b, 1:2, :] for b in range(8)], axis=1).astype(F32)

    def norm_rows(i, carry):
        s, t = i // (span // 16), i % (span // 16)
        cut = pl.ds(pl.multiple_of(t * 16, 16), 16)
        x = xr_v[s, cut, :].astype(F32)
        n1_v[s, cut, :] = (x * inverse_rms(x) * gain1).astype(BF16)
        return carry

    lax.fori_loop(0, span // 16, norm_rows, 0)
    w_qkv.second()
    w_out.first()
    lax.fori_loop(span // 16, seqs * span // 16, norm_rows, 0)
    store_n1 = pltpu.make_async_copy(n1_v, n1_hbm, store_sem.at[2])
    store_n1.start()
    w_qkv.third()
    w_qkv.arrived()

    half = width // 2

    def exchange(s):
        return remote(ex_send.at[s], ex_got.at[s], exsend.at[0, s], exrecv.at[0, s], near_core)

    def keep(k, s):
        ref, dst = ((pre_ref, pre_hbm), (all_ref, all_hbm), (att_ref, att_hbm), (tok_ref, tok_hbm))[k]
        return pltpu.make_async_copy(ref.at[s], dst.at[s], keep_sem.at[k, s])

    def project(s):
        x = n1_v[s]
        flat = dot_nn(x[:, :half], qkv_v[0]) + dot_nn(x[:, half:], qkv_v[1])
        turned = flat.T
        pre_ref[s] = turned[: (nq + nk) * hd]
        done = []
        for h in range(nq + nk):
            v = turned[h * hd : (h + 1) * hd]
            inv = lax.rsqrt(jnp.mean(v * v, axis=0, keepdims=True) + epsilon)
            v = v * inv * (qgain if h < nq else kgain)
            a, b = v[: hd // 2], v[hd // 2 :]
            done.append(jnp.concatenate([a * cosine - b * sine, b * cosine + a * sine], axis=0))
        for h in range(nk):
            lo = (nq + nk + h) * hd
            done.append(turned[lo : lo + hd])
        parts = [[], []]
        for begin_at, count in ((0, nq), (nq, nk), (nq + nk, nk)):
            for side in range(2):
                parts[side] += done[begin_at + side * count // 2 : begin_at + (side + 1) * count // 2]
        low = jnp.concatenate(parts[0], axis=0)
        high = jnp.concatenate(parts[1], axis=0)
        ex_own[s] = jnp.where(first_core, low, high).astype(BF16)
        ex_send[s] = jnp.where(first_core, high, low).astype(BF16)
        exchange(s).start()
        keep(0, s).start()

    store_qkv = pltpu.make_async_copy(qkv_v, qkv_hbm, store_sem.at[3])
    store_qkv.start()
    store_out = pltpu.make_async_copy(out_v, out_hbm, store_sem.at[4])

    scale = log2e / math.sqrt(hd)
    krow = lax.broadcasted_iota(jnp.int32, (block, groups * block), 0)
    qcol = lax.broadcasted_iota(jnp.int32, (block, groups * block), 1) % block
    base = groups * hd

    def give(s):
        return remote(at_send.at[s], at_got.at[s], exsend.at[1, s], exrecv.at[1, s], near_core)

    def attention(s):
        exchange(s).wait_recv()
        low, high = join_positions(core, ex_own[s], ex_got[s])
        all_ref[s, :, :span] = low
        all_ref[s, :, span:] = high
        length = len_ref[s]
        for i in range(2 * span // block):
            cut = slice(i * block, (i + 1) * block)
            q = jnp.concatenate([all_ref[s, g * hd : (g + 1) * hd, cut] for g in range(groups)], axis=1)
            acc = jnp.zeros((hd, groups * block), F32)
            total = jnp.zeros((1, groups * block), F32)
            for j in range(i + 1):
                kcut = slice(j * block, (j + 1) * block)
                score = dot_tn(all_ref[s, base : base + hd, kcut], q) * scale
                ok = (krow + j * block) < length
                if j == i:
                    ok = ok & (krow <= qcol)
                e = jnp.where(ok, jnp.exp2(score), 0.0)
                total = total + jnp.sum(e, axis=0, keepdims=True)
                acc = acc + dot_nn(all_ref[s, base + hd : base + 2 * hd, kcut], e.astype(BF16))
            inv = 1.0 / total
            att = (acc * inv).astype(BF16)
            for g in range(groups):
                att_ref[s, g * hd : (g + 1) * hd, cut] = att[:, g * block : (g + 1) * block]
                inv_ref[s, g : g + 1, cut] = inv[:, g * block : (g + 1) * block]
        mine, theirs = join_positions(core, att_ref[s, :, :span], att_ref[s, :, span:])
        at_own[s] = mine
        at_send[s] = theirs
        give(s).start()
        keep(1, s).start()
        keep(2, s).start()

    moving = Chain(rank, part_v, in_v, back_v, zsend, zrecv)
    subs = moving.count

    def branch_rows(s):
        give(s).wait_recv()
        low, high = join_positions(core, at_own[s], at_got[s])
        att = jnp.concatenate([low, high], axis=0).T
        tok_ref[s] = att
        keep(3, s).start()
        many = 2
        for k in range(0, per, many):
            rows = att[k * sub : (k + many) * sub]
            for side in range(2):
                part = dot_nn(rows, out_v[side]).astype(BF16)
                for m in range(many):
                    part_v[s * per + k + m, :, side * half : (side + 1) * half] = part[m * sub : (m + 1) * sub]
            for m in range(many):
                u = s * per + k + m

                @pl.when(u < subs)
                def _():
                    moving.begin(u)

    def sequence(s, carry):
        project(s)

        @pl.when(s == 0)
        def _():
            w_out.second()
            w_down.first()
            w_gate.first()

        attention(s)

        @pl.when(s == 0)
        def _():
            w_out.third()
            w_out.arrived()
            store_out.start()

        branch_rows(s)
        return carry

    lax.fori_loop(0, seqs, sequence, 0)
    rest = [pltpu.make_async_copy(part_v.at[u], rest_hbm.at[u - subs], rest_sem.at[u - subs]) for u in range(subs, total_subs)]
    for copy in rest:
        copy.start()
    stat_ref[...] = jnp.zeros_like(stat_ref)

    def hidden_store(u):
        cut = pl.ds(pl.multiple_of(u * sub, sub), sub)
        return (
            pltpu.make_async_copy(hid_v.at[u % 2], hidden_hbm.at[cut, :], hid_sem.at[0, u % 2]),
            pltpu.make_async_copy(norm_v.at[u % 2], n2_hbm.at[cut, :], hid_sem.at[1, u % 2]),
        )

    def finish(u):
        s, t = u // per, u % per
        cut = pl.ds(pl.multiple_of(t * sub, sub), sub)

        moving.total(u, total_v)

        @pl.when(u >= 2)
        def _():
            for copy in hidden_store(u - 2):
                copy.wait()

        length = len_ref[s]

        def body(piece_rows, first):
            total = total_v[piece_rows, :]
            resid = xr_v[s, pl.ds(pl.multiple_of(t * sub + first, 16), 16), :].astype(F32)
            hidden = resid + total
            hid_v[u % 2, piece_rows, :] = hidden
            norm_v[u % 2, piece_rows, :] = (hidden * inverse_rms(hidden) * gain2).astype(BF16)
            place = start + t * sub + first + lax.broadcasted_iota(jnp.int32, (16, 1), 0)
            valid = (place < length).astype(F32)
            stat_ref[0] += fold_lanes(valid * resid * resid)
            stat_ref[1] += fold_lanes(valid * total * total)

        by_pieces(sub, body)
        for copy in hidden_store(u):
            copy.start()

    hb = down_v.shape[2]
    blocks = down_hbm.shape[1] // hb

    def load_down(h):
        cut = pl.ds(pl.multiple_of(h * hb, hb), hb)
        return [pltpu.make_async_copy(down_hbm.at[side, cut, :], down_v.at[h % 2, side], down_sem.at[h % 2, side]) for side in range(2)]

    def store_gi(h):
        cut = pl.ds(pl.multiple_of(h * hb, hb), hb)
        return pltpu.make_async_copy(gi_v.at[h % 2], gi_hbm.at[:, cut], gi_sem.at[h % 2])

    def grad_inner(h):
        for copy in load_down(h):
            copy.wait()

        @pl.when(h + 1 < blocks)
        def _():
            for copy in load_down(h + 1):
                copy.start()

        @pl.when(h >= 2)
        def _():
            store_gi(h - 2).wait()

        for s in range(seqs):
            for q in range(span // 256):
                cut = slice(q * 256, (q + 1) * 256)
                g = dot_nt(cot_v[s, cut, :half], down_v[h % 2, 0]) + dot_nt(cot_v[s, cut, half:], down_v[h % 2, 1])
                gi_v[h % 2, s * span + q * 256 : s * span + (q + 1) * 256, :] = g.astype(BF16)
        store_gi(h).start()

    def chain(i, carry):
        moving.middle(i)
        moving.outward(i - 1)

        @pl.when(i == subs + 1)
        def _():
            w_up.third()

        @pl.when(i >= 2)
        def _():
            finish(i - 2)

        @pl.when(i == 1)
        def _():
            w_down.second()
            w_up.first()

        @pl.when(i == 6)
        def _():
            w_gate.second()

        @pl.when(i == 8)
        def _():
            w_down.third()

        @pl.when(i == 9)
        def _():
            w_down.arrived()
            for copy in load_down(0):
                copy.start()

        @pl.when((i >= 10) & (i < 10 + blocks))
        def _():
            grad_inner(i - 10)

        @pl.when(i == 12)
        def _():
            w_up.second()

        @pl.when(i == 14)
        def _():
            w_gate.third()

        return carry

    lax.fori_loop(0, subs + 2, chain, 0)
    for u in (subs - 2, subs - 1):
        for copy in hidden_store(u):
            copy.wait()
    for h in (blocks - 2, blocks - 1):
        store_gi(h).wait()
    moving.settle()
    for s in range(seqs):
        exchange(s).wait_send()
        give(s).wait_send()
        for k in range(4):
            keep(k, s).wait()
    every_gain.wait_send()
    w_gate.arrived()
    w_up.arrived()
    for w in weights:
        w.sent()
    for copy in [store_gf, store_xr, store_n1, store_qkv, store_out] + rest:
        copy.wait()


def forward(lengths, x, cot, w_query, w_key, w_value, w_out, w_gate, w_up, w_down, all_gains, hd, nq, nk):
    seqs, span, width = x.shape
    half = width // 2
    groups = nq // nk
    sub = span // 8
    subs = seqs * span // sub
    here = subs - 2
    block = min(256, span)
    hidden = w_gate.shape[1]
    hb = hidden // 4
    cols = w_query.shape[1] + w_key.shape[1] + w_value.shape[1]
    rows = cols // 2
    any_space = pl.BlockSpec(memory_space=pl.ANY)
    vmem = pl.BlockSpec(memory_space=pltpu.VMEM)
    wide = (seqs, span, width)
    large = [
        shape(wide, BF16), shape(wide, BF16), shape(wide, BF16),
        shape((2, half, cols), BF16), shape((2, w_out.shape[0], half), BF16),
        shape((2, half, hidden), BF16), shape((2, half, hidden), BF16), shape((2, hidden, half), BF16),
        shape((seqs * span, width), F32), shape((seqs * span, width), BF16), shape((subs - here, sub, width), BF16),
        shape((seqs * span, hidden), BF16),
    ]
    kept = [
        shape((seqs, (nq + nk) * hd, span), F32), shape((seqs, rows, 2 * span), BF16),
        shape((seqs, groups * hd, 2 * span), BF16), shape((seqs, span, nq * hd), BF16),
    ]
    large += kept
    small = [
        shape((8, 16, width // 8), BF16), shape((3 * hd, span), F32), shape((seqs, groups, 2 * span), F32), shape((2, 8, 128), F32),
    ]
    dma = pltpu.SemaphoreType.DMA
    ex = pltpu.VMEM((seqs, rows, span), BF16)
    at = pltpu.VMEM((seqs, groups * hd, span), BF16)
    moving = pltpu.VMEM((subs, sub, width), BF16)
    landing = pltpu.VMEM((here, sub, width), BF16)
    flops = 2 * seqs * span * width * (cols + nq * hd) + 16 * seqs * nq * hd * span * span
    return pl.pallas_call(
        functools.partial(forward_kernel, hd, nq, nk, block, sub),
        in_specs=[SMEM] + [any_space] * 9 + [vmem] * 4,
        out_specs=[any_space] * len(large) + [vmem] * len(small),
        out_shape=large + small,
        scratch_shapes=[
            pltpu.VMEM(wide, BF16), pltpu.VMEM(wide, BF16), pltpu.VMEM(wide, BF16),
            pltpu.VMEM((2, half, cols), BF16), pltpu.VMEM((2, w_out.shape[0], half), BF16),
            ex, ex, ex, at, at, at,
            moving, landing, landing,
            pltpu.VMEM((sub, width), F32), pltpu.VMEM((2, sub, width), F32), pltpu.VMEM((2, sub, width), BF16),
            pltpu.VMEM((w_query.shape[0], cols), BF16), pltpu.VMEM((16, width // 8), BF16),
            pltpu.VMEM((2, 2, hb, half), BF16), pltpu.VMEM((2, seqs * span, hb), BF16),
            *[pltpu.VMEM(a.shape, a.dtype) for a in kept],
            dma((4, seqs)), dma((2,)), dma((5,)), dma((3,)), dma((subs - here,)), dma((2, 2)), dma((2,)), dma((5, 2)), dma((5, 4)), dma((5,)), dma(()), dma(()),
            dma((2, seqs)), dma((2, seqs)), dma((2,)), dma((2, here)), dma((2, 2)),
        ],
        compiler_params=pltpu.CompilerParams(vmem_limit_bytes=VMEM_MOST, collective_id=1, has_side_effects=True),
        cost_estimate=cost(flops, 80 * seqs * span * width),
        name="attention_forward",
    )(lengths, x, cot, w_query, w_key, w_value, w_out, w_gate, w_up, w_down, *all_gains)


def by_pieces(count, body, size=16):
    def one(p, carry):
        body(pl.ds(pl.multiple_of(p * size, size), size), p * size)
        return carry

    lax.fori_loop(0, count // size, one, 0, unroll=2)


def fold_lanes(values):
    tiles = values[:8] + values[8:]
    return sum(tiles[:, k * 128 : (k + 1) * 128] for k in range(tiles.shape[1] // 128))


class Chain:
    def __init__(self, rank, part, arrive, back, send, recv):
        self.inner = (rank % 3) != 0
        self.outer = (rank % 3) == 0
        self.part, self.arrive, self.back = part, arrive, back
        self.send, self.recv = send, recv
        self.side, self.mid = {"tensor": xor_one(rank)}, {"tensor": 3 - rank}
        self.count = arrive.shape[0]

    def hop_in(self, u):
        return remote(self.part.at[u], self.arrive.at[u], self.send.at[0], self.recv.at[0, u], self.side)

    def hop_mid(self, u):
        return remote(self.arrive.at[u], self.back.at[u], self.send.at[1], self.recv.at[1, u], self.mid)

    def hop_out(self, u):
        return remote(self.part.at[u], self.back.at[u], self.send.at[0], self.recv.at[0, u], self.side)

    def add(self, into, one, two, u):
        def body(cut, first):
            into[u, cut, :] = (one[u, cut, :].astype(F32) + two[u, cut, :].astype(F32)).astype(BF16)

        by_pieces(self.part.shape[1], body)

    def begin(self, u):
        @pl.when(self.outer)
        def _():
            self.hop_in(u).start()

    def middle(self, u):
        @pl.when((u >= 0) & (u < self.count) & self.inner)
        def _():
            self.hop_in(u).wait_recv()
            self.add(self.arrive, self.part, self.arrive, u)
            self.hop_mid(u).start()

    def outward(self, u):
        @pl.when((u >= 0) & (u < self.count) & self.inner)
        def _():
            self.hop_mid(u).wait_recv()
            self.add(self.part, self.part, self.back, u)
            self.hop_out(u).start()

    def total(self, u, into):
        @pl.when(self.inner)
        def _():
            def body(cut, first):
                into[cut, :] = self.arrive[u, cut, :].astype(F32) + self.back[u, cut, :].astype(F32)

            by_pieces(self.part.shape[1], body)

        @pl.when(self.outer)
        def _():
            self.hop_out(u).wait_recv()

            def body(cut, first):
                into[cut, :] = self.part[u, cut, :].astype(F32) + self.back[u, cut, :].astype(F32)

            by_pieces(self.part.shape[1], body)

    def settle(self):
        every = self.part.at[pl.ds(0, self.count)]
        remote(every, self.back, self.send.at[0], self.recv.at[0, 0], self.side).wait_send()

        @pl.when(self.inner)
        def _():
            remote(self.arrive, self.back, self.send.at[1], self.recv.at[1, 0], self.mid).wait_send()


def feed_both_kernel(
    hb, sub, rows,
    len_ref, n2_hbm, gf_hbm, gate_hbm, up_hbm, down_hbm, gi_hbm, rest_hbm, xr_hbm, hidden_in, gains_ref,
    ffn_hbm, gb_hbm, gh_hbm, dgate_hbm, dup_hbm, ddown_hbm, hidden_hbm, landx, landy, ring_hbm, gain_out, stat_ref,
    n2_v, gf_v, inner_v, gg_v, gu_v, facc, gacc, wrow, wcol, part_v, in_v, back_v, total_v, hid_v, gh_v, gb_v, stage_row, stage_col,
    late_p, late_a, late_b, xtile_v, gi_v, wide_v, temp_v, gain_ref,
    load_sem, wsem, zsend, zrecv, hid_sem, out_sem, ffn_sem, csend, crecv, store_sem, lsend, lrecv, xt_sem, xsend, xrecv, xload, rsend, rrecv, free_sem,
):
    core, rank = lax.axis_index("context"), lax.axis_index("tensor")
    near_core = {"context": 1 - core}
    tokens, width = n2_v.shape
    half = width // 2
    hidden = inner_v.shape[1]
    hsteps = hidden // hb
    steps = tokens // rows * hsteps
    per = rows // sub
    chain = Chain(rank, part_v, in_v, back_v, zsend, zrecv)
    subs = chain.count
    late = Chain(rank, late_p, late_a, late_b, lsend, lrecv)
    known = subs - late.count
    start = core * (tokens // 2)

    def load_weights(i):
        slot, h = i % 2, i % hsteps
        cut = pl.ds(pl.multiple_of(h * hb, hb), hb)
        here = pl.ds(pl.multiple_of(i // hsteps * rows, rows), rows)
        copies = [pltpu.make_async_copy(gi_hbm.at[here, cut], gi_v.at[slot], wsem.at[slot, 6])]
        for side in range(2):
            copies.append(pltpu.make_async_copy(gate_hbm.at[side, :, cut], wrow.at[slot, 0, side], wsem.at[slot, side]))
            copies.append(pltpu.make_async_copy(up_hbm.at[side, :, cut], wrow.at[slot, 1, side], wsem.at[slot, 2 + side]))
            copies.append(pltpu.make_async_copy(down_hbm.at[side, cut, :], wcol.at[slot, side], wsem.at[slot, 4 + side]))
        return copies

    def load_hidden(u):
        cut = pl.ds(pl.multiple_of(u * sub, sub), sub)
        return pltpu.make_async_copy(hidden_hbm.at[cut, :], hid_v, hid_sem)

    ready = pl.ds(0, known * sub)
    loads = [
        pltpu.make_async_copy(n2_hbm.at[ready, :], n2_v.at[ready, :], load_sem.at[0]),
        pltpu.make_async_copy(rest_hbm, late_p, load_sem.at[1]),
    ]
    load_gf = pltpu.make_async_copy(gf_hbm, gf_v, load_sem.at[2])
    for copy in loads + load_weights(0) + [load_gf]:
        copy.start()
    load_hidden(0).start()
    row = lax.axis_index("dp")
    near_x, near_y = {"dp": xor_one(row)}, {"dp": (row + 2) % 4}
    greet([(None, near_core), (None, near_x), (None, near_y), (None, chain.side), (chain.inner, chain.mid)])
    for b in range(8):
        gain_ref[:, b * (width // 8) : (b + 1) * (width // 8)] = gains_ref[b, 1:2, :].astype(F32)
    gain_out[...] = jnp.zeros_like(gain_out)
    stat_ref[...] = jnp.zeros_like(stat_ref)
    for copy in loads:
        copy.wait()
    for u in range(late.count):
        late.begin(u)

    def load_x(u):
        at = pl.multiple_of((known + u) * sub, sub)
        return pltpu.make_async_copy(xr_hbm.at[pl.ds(at, sub), :], xtile_v, xt_sem)

    def late_store(u):
        return pltpu.make_async_copy(gh_v, hidden_hbm.at[pl.ds(pl.multiple_of((known + u) * sub, sub), sub), :], out_sem.at[0])

    def late_finish(u):
        load_x(u).start()
        late.total(u, total_v)
        load_x(u).wait()

        @pl.when(u >= 1)
        def _():
            late_store(u - 1).wait()

        length = len_ref[known * sub // (tokens // 2)]
        offset = start + known * sub % (tokens // 2) + u * sub

        def body(cut, first):
            total = total_v[cut, :]
            resid = xtile_v[cut, :].astype(F32)
            hidden_rows = resid + total
            gh_v[cut, :] = hidden_rows
            normed = (hidden_rows * inverse_rms(hidden_rows) * gain_ref[...]).astype(BF16)
            n2_v[pl.ds(pl.multiple_of((known + u) * sub + first, 16), 16), :] = normed
            spot = offset + first + lax.broadcasted_iota(jnp.int32, (16, 1), 0)
            valid = (spot < length).astype(F32)
            stat_ref[0] += fold_lanes(valid * resid * resid)
            stat_ref[1] += fold_lanes(valid * total * total)

        by_pieces(sub, body)
        late_store(u).start()

    def store_gb(u):
        cut = pl.ds(pl.multiple_of(u * sub, sub), sub)
        return pltpu.make_async_copy(gb_v, gb_hbm.at[cut, :], out_sem.at[1])

    def store_gh(u):
        at = pl.ds(pl.multiple_of(u % 2 * sub, sub), sub)
        return pltpu.make_async_copy(gh_v, gh_hbm.at[u // 8, at, :], out_sem.at[0])

    def finish(u):
        chain.total(u, total_v)
        load_hidden(u).wait()

        @pl.when(u >= 1)
        def _():
            store_gb(u - 1).wait()

        def body(piece_rows, first):
            e = total_v[piece_rows, :]
            hidden_rows = hid_v[piece_rows, :]
            inv = inverse_rms(hidden_rows)
            hat = hidden_rows * inv
            eg = e * gain_ref[...]
            grad = gf_v[pl.ds(pl.multiple_of(u * sub + first, 16), 16), :].astype(F32)
            gh = grad + inv * (eg - hat * jnp.mean(eg * hat, axis=-1, keepdims=True))
            gb_v[piece_rows, :] = gh.astype(BF16)

            @pl.when(u % 8 // 2 == rank)
            def _():
                gh_v[piece_rows, :] = gh

            both = e * hat
            gain_out[...] += both[:8] + both[8:]

        by_pieces(sub, body)
        store_gb(u).start()

        @pl.when(u % 8 // 2 == rank)
        def _():
            store_gh(u).start()
            store_gh(u).wait()

        @pl.when(u + 1 < subs)
        def _():
            load_hidden(u + 1).start()

    def serve(n):
        chain.middle(n)
        chain.outward(n - 2)

        @pl.when((n >= 4) & (n < 4 + subs))
        def _():
            finish(n - 4)

    quarter = width // 4

    def store_ffn(c):
        here = pl.ds(pl.multiple_of(c * rows, rows), rows)
        return [
            pltpu.make_async_copy(
                stage_row.at[c % 2, pl.ds(k * rows, rows), :], ffn_hbm.at[here, pl.ds(k * quarter, quarter)], ffn_sem.at[c % 2, k]
            )
            for k in range(4)
        ]

    def step(i, carry):
        slot, c, h = i % 2, i // hsteps, i % hsteps
        for copy in load_weights(i):
            copy.wait()

        @pl.when(i + 1 < steps)
        def _():
            for copy in load_weights(i + 1):
                copy.start()

        here = pl.ds(pl.multiple_of(c * rows, rows), rows)
        cols = pl.ds(pl.multiple_of(h * hb, hb), hb)
        n = n2_v[here, :]
        wide = min(256, hb)
        for q in range(hb // wide):
            part = slice(q * wide, (q + 1) * wide)
            gate = dot_nn(n[:, :half], wrow[slot, 0, 0, :, part]) + dot_nn(n[:, half:], wrow[slot, 0, 1, :, part])
            up = dot_nn(n[:, :half], wrow[slot, 1, 0, :, part]) + dot_nn(n[:, half:], wrow[slot, 1, 1, :, part])
            gi = gi_v[slot, :, part].astype(F32)
            sig = jax.nn.sigmoid(gate)
            silu = gate * sig
            at = pl.ds(pl.multiple_of(h * hb + q * wide, wide), wide)
            inner_v[here, at] = (silu * up).astype(BF16)
            gg_v[here, at] = (gi * up * sig * (1.0 + gate * (1.0 - sig))).astype(BF16)
            gu_v[here, at] = (gi * silu).astype(BF16)

        @pl.when(h == 0)
        def _():
            facc[...] = jnp.zeros_like(facc)
            gacc[...] = jnp.zeros_like(gacc)

        inner, gg, gu = inner_v[here, cols], gg_v[here, cols], gu_v[here, cols]
        span = min(512, half)
        for side in range(2):
            for q in range(half // span):
                part = slice(q * span, (q + 1) * span)
                cut = slice(side * half + q * span, side * half + (q + 1) * span)
                facc[:, cut] += dot_nn(inner, wcol[slot, side, :, part])
                gacc[:, cut] += dot_nt(gg, wrow[slot, 0, side, part, :]) + dot_nt(gu, wrow[slot, 1, side, part, :])

        @pl.when((h == hsteps - 1) & (c >= 2))
        def _():
            for copy in store_ffn(c - 2):
                copy.wait()

        @pl.when(h == hsteps - 1)
        def _():
            for k in range(per):
                part_v[c * per + k] = gacc[k * sub : (k + 1) * sub, :].astype(BF16)
                chain.begin(c * per + k)

            for k in range(4):
                stage_row[c % 2, k * rows : (k + 1) * rows, :] = facc[:, k * quarter : (k + 1) * quarter].astype(BF16)
            for copy in store_ffn(c):
                copy.start()

        @pl.when((i >= 2) & (i < 2 + late.count))
        def _():
            late.middle(i - 2)

        @pl.when((i >= 4) & (i < 4 + late.count))
        def _():
            late.outward(i - 4)

        @pl.when((i >= 6) & (i < 6 + late.count))
        def _():
            late_finish(i - 6)

        @pl.when(i == 9)
        def _():
            load_gf.wait()
            late_store(late.count - 1).wait()

        serve(i - 6)
        return carry

    lax.fori_loop(0, steps, step, 0)
    for c in range(2, steps // hsteps):
        for copy in store_ffn(c):
            copy.wait()

    pl.semaphore_signal(free_sem, inc=1, device_id=near_core, device_id_type=pl.DeviceIdType.MESH)
    outs = (dgate_hbm, dup_hbm, ddown_hbm)

    def landing(w, t):
        return wrow.at[t // 2, w, t % 2] if w < 2 else wcol.at[t // 2, t % 2]

    def landed(w, t, piece):
        return wrow[t // 2, w, t % 2, piece, :] if w < 2 else wcol[t // 2, t % 2, piece, :]

    def staging(w):
        return stage_row if w < 2 else stage_col

    def ship(w, t):
        return remote(staging(w).at[t % 2], landing(w, t), csend.at[w, t], crecv.at[w, t], near_core)

    def keep(w, t):
        cut = pl.ds(pl.multiple_of(t * hb, hb), hb)
        dst = outs[w].at[:, cut] if w < 2 else outs[w].at[cut, :]
        return pltpu.make_async_copy(staging(w).at[t % 2], dst, store_sem.at[w, t])

    def release(kind, w, t):
        if kind == 1:
            ship(w, t).wait_send()
        else:
            keep(w, t).wait()

    def group(kind, w, before, part):
        def one(t, carry):
            cut = pl.ds(pl.multiple_of(t * hb, hb), hb)
            mine = slice(kind * half, (kind + 1) * half)
            @pl.when(t >= 2)
            def _():
                release(kind, w, t - 2)

            if before is not None:

                @pl.when(t < 2)
                def _():
                    release(before[0], before[1], t + hsteps - 2)

            if kind == 0:
                ship(w, t).wait_recv()
            tall = staging(w).shape[1]
            size = min(256, tall)
            for q in range(tall // size):
                piece = slice(q * size, (q + 1) * size)
                if w == 2:
                    left = inner_v[:, pl.ds(pl.multiple_of(t * hb + q * size, size), size)]
                    value = dot_tn(left, gf_v[:, mine])
                else:
                    value = dot_tn(n2_v[:, kind * half + q * size : kind * half + (q + 1) * size], (gg_v, gu_v)[w][:, cut])
                if kind == 0:
                    value = value + landed(w, t, piece).astype(F32)
                staging(w)[t % 2, piece, :] = value.astype(BF16)
            if kind == 1:
                ship(w, t).start()
            else:
                keep(w, t).start()
            return carry

        lax.fori_loop(part * (hsteps // 2), (part + 1) * (hsteps // 2), one, 0)

    pl.semaphore_wait(free_sem, 1)

    def term(m):
        return ffn_hbm.at[pl.ds(pl.multiple_of(m * (2 * sub), 2 * sub), 2 * sub), :]

    fold = Fold(rank, term, None, ring_hbm, (ring_hbm.at[2], None), rsend, rrecv)
    after = iter(range(steps - 6, subs + 4))
    done = []

    def both(kind, w, before):
        for part in range(2):
            group(kind, w, before, part)
            done.append(part)
            if len(done) <= 8 or len(done) % 2 == 0:
                serve(next(after))
            if len(done) == 5:
                fold.begin()

    both(1, 0, None)
    both(0, 0, (1, 0))
    for t in range(hsteps - 2, hsteps):
        keep(0, t).wait()
    gate_sum = Scatter(
        row_blocks(dgate_hbm), wide_v.at[0], wide_v.at[1], half_rows(landx), half_rows(landy), temp_v, xsend, xrecv, xload, near_x, near_y
    )
    gate_sum.begin()
    both(1, 1, None)
    both(1, 2, None)
    gate_sum.pass_on()
    both(0, 1, (1, 1))
    both(0, 2, (1, 2))
    for n in after:
        serve(n)
    for t in range(hsteps - 2, hsteps):
        keep(1, t).wait()
        keep(2, t).wait()
    store_gb(subs - 1).wait()
    gate_sum.arrived()
    gate_sum.settle()
    chain.settle()

    @pl.when(fold.inner)
    def _():
        for k in range(3):
            fold.come(k)

    @pl.when(fold.outer)
    def _():
        fold.settle()

    late.settle()


def row_blocks(ref):
    size = ref.shape[0] // 4
    return lambda k, h: ref.at[pl.ds(k * size + h * (size // 2), size // 2), :]


def half_rows(ref):
    size = ref.shape[0] // 2
    return lambda h: ref.at[pl.ds(h * size, size), :]


def feed_both(lengths, n2, gf, gate, up, down, gi, rest, xr, hidden_rows, gain):
    tokens, width = n2.shape
    _, half, hidden = gate.shape
    hb = hidden // 4
    sub, rows = tokens // 16, tokens // 4
    count = rest.shape[0]
    any_space = pl.BlockSpec(memory_space=pl.ANY)
    vmem = pl.BlockSpec(memory_space=pltpu.VMEM)
    dma = pltpu.SemaphoreType.DMA
    moving = pltpu.VMEM((16, sub, width), BF16)
    late = pltpu.VMEM((count, sub, width), BF16)
    act = pltpu.VMEM((tokens, hidden), BF16)
    return pl.pallas_call(
        functools.partial(feed_both_kernel, hb, sub, rows),
        in_specs=[SMEM] + [any_space] * 9 + [vmem],
        out_specs=[any_space] * 10 + [vmem] * 2,
        out_shape=[
            shape((tokens, width), BF16), shape((tokens, width), BF16), shape((2, 2 * sub, width), F32),
            shape((half, hidden), BF16), shape((half, hidden), BF16), shape((hidden, half), BF16),
            shape((tokens, width), F32), shape((half // 4, hidden), BF16), shape((half // 4, hidden), BF16),
            shape((3, 2 * sub, width), BF16), shape((8, width), F32), shape((2, 8, 128), F32),
        ],
        scratch_shapes=[
            pltpu.VMEM((tokens, width), BF16), pltpu.VMEM((tokens, width), BF16), act, act, act,
            pltpu.VMEM((rows, width), F32), pltpu.VMEM((rows, width), F32),
            pltpu.VMEM((2, 2, 2, half, hb), BF16), pltpu.VMEM((2, 2, hb, half), BF16),
            moving, moving, moving, pltpu.VMEM((sub, width), F32),
            pltpu.VMEM((sub, width), F32), pltpu.VMEM((sub, width), F32), pltpu.VMEM((sub, width), BF16),
            pltpu.VMEM((2, half, hb), BF16), pltpu.VMEM((2, hb, half), BF16),
            late, late, late, pltpu.VMEM((sub, width), BF16), pltpu.VMEM((2, rows, hb), BF16),
            pltpu.VMEM((2, half // 8, hidden), BF16), pltpu.VMEM((2, half // 8, hidden), BF16), pltpu.VMEM((1, width), F32),
            dma((3,)), dma((2, 7)), dma((2,)), dma((2, 16)), dma(()), dma((2,)), dma((2, 4)), dma((3, 4)), dma((3, 4)),
            dma((3, 4)), dma((2,)), dma((2, count)), dma(()), dma((6,)), dma((6,)), dma((3,)), dma(()), dma((5,)), pltpu.SemaphoreType.REGULAR,
        ],
        input_output_aliases={9: 6},
        compiler_params=pltpu.CompilerParams(vmem_limit_bytes=VMEM_MOST, collective_id=2, has_side_effects=True),
        cost_estimate=cost(18 * tokens * width * hidden, 60 * tokens * width),
        name="feed_forward_both",
    )(lengths, n2, gf, gate, up, down, gi, rest, xr, hidden_rows, gain)


class Fold:
    def __init__(self, rank, source, own, slots, finals, send, recv, landed=None):
        self.inner, self.outer = (rank % 3) != 0, (rank % 3) == 0
        self.side, self.mid = {"tensor": xor_one(rank)}, {"tensor": 3 - rank}
        self.leaving = (3 - rank, xor_one(3 - rank), xor_one(rank))
        self.added = (xor_one(3 - rank), 3 - rank, xor_one(rank))
        self.source, self.own, self.slots, self.finals = source, own, slots, finals
        self.send, self.recv, self.landed = send, recv, landed

    def inward(self, k):
        dst = self.slots.at[k] if k < 2 else self.finals[0]
        return remote(self.source(self.leaving[k]), dst, self.send, self.recv.at[k], self.side)

    def across(self, k):
        dst = self.slots.at[2] if k == 0 else self.finals[1]
        return remote(self.slots.at[k], dst, self.send, self.recv.at[3 + k], self.mid)

    def outward(self):
        return remote(self.slots.at[2], self.finals[0], self.send, self.recv.at[0], self.side)

    def begin(self):
        @pl.when(self.outer)
        def _():
            for k in range(3):
                self.inward(k).start()

    def come(self, k):
        (self.landed[k].wait if self.landed is not None else self.inward(k).wait_recv)()

    def step(self, k):
        @pl.when(self.inner)
        def _():
            if k < 2:
                self.come(k)
            else:
                self.across(0).wait_recv()
            read = self.own(self.added[k])

            def body(cut, first):
                self.slots[k, cut, :] = (self.slots[k, cut, :].astype(F32) + read(cut).astype(F32)).astype(BF16)

            by_pieces(self.slots.shape[1], body)
            (self.across(k) if k < 2 else self.outward()).start()

    def arrived(self):
        @pl.when(self.inner)
        def _():
            self.come(2)
            self.across(1).wait_recv()

        @pl.when(self.outer)
        def _():
            self.outward().wait_recv()

    def settle(self):
        three = self.slots.at[pl.ds(0, 3)]
        every = remote(three, three, self.send, self.recv.at[0], self.side)
        if self.landed is None:
            every.wait_send()
        else:
            pl.when(self.inner)(every.wait_send)


def tall(ref):
    return 16 * max(1, 2048 // ref.shape[1])


class Scatter:
    def __init__(self, block, from_x, from_y, land_x, land_y, temps, send, recv, load, near_x, near_y):
        self.block, self.from_x, self.from_y, self.land_x, self.land_y = block, from_x, from_y, land_x, land_y
        self.temps, self.load = temps, load
        sem = lambda k: (send.at[k], recv.at[k])
        self.first = [
            remote(block(3, 0), from_x, *sem(0), near_x),
            remote(block(3, 1), from_y, *sem(1), near_y),
            remote(block(1, 0), land_x(0), *sem(2), near_x),
            remote(block(2, 1), land_y(1), *sem(3), near_y),
        ]
        self.second = [
            remote(from_y, land_x(1), *sem(4), near_x),
            remote(from_x, land_y(0), *sem(5), near_y),
        ]

    def begin(self):
        for copy in self.first:
            copy.start()

    def pass_on(self):
        loads = [
            pltpu.make_async_copy(self.block(1, 1), self.temps.at[0], self.load.at[0]),
            pltpu.make_async_copy(self.block(2, 0), self.temps.at[1], self.load.at[1]),
        ]
        for copy in loads:
            copy.start()
        for which, into in ((1, self.from_y), (0, self.from_x)):
            self.first[which].wait_recv()
            loads[1 - which].wait()
            temp = 1 - which

            def body(cut, first):
                into[cut, :] = (into[cut, :].astype(F32) + self.temps[temp, cut, :].astype(F32)).astype(BF16)

            by_pieces(into.shape[0], body, tall(into))
            self.second[temp].start()

    def arrived(self):
        for copy in self.first[2:] + self.second:
            copy.wait_recv()

    def keep(self, out, store):
        for h in range(2):
            loads = [
                pltpu.make_async_copy(src, self.temps.at[k], self.load.at[k])
                for k, src in enumerate((self.block(0, h), self.land_x(h), self.land_y(h)))
            ]
            for copy in loads:
                copy.start()
            for copy in loads:
                copy.wait()

            def body(cut, first):
                self.temps[0, cut, :] = sum(self.temps[k, cut, :].astype(F32) for k in range(3)).astype(BF16)

            by_pieces(self.temps.shape[1], body, tall(self.temps.at[0]))
            copy = pltpu.make_async_copy(self.temps.at[0], out(h), store)
            copy.start()
            copy.wait()

    def settle(self):
        for copy in self.first + self.second:
            copy.wait_send()


def backward_kernel(
    hd, nq, nk, block,
    len_ref, gb_hbm, hidden_hbm, ffn_hbm, ring_hbm, xr_hbm, n1_hbm, tok_hbm, outw_hbm, qkvw_hbm, all_hbm, att_hbm, inv_hbm, pre_hbm,
    gh_hbm, dgate_hbm, landx0, landy0, dup_hbm, ddown_hbm, table_ref, gains_ref, stat_ref, stat2_ref, gain2_ref,
    out_hbm, gin_hbm, fin_hbm, finb_hbm, own_hbm, sum_gate, sum_up, sum_down, mine_o, mine_q, landx1, landy1, landx2, landy2, landx3, landy3, landx4, landy4,
    lines_out, small_out,
    act_v, rows_v, qkvw_v, tok_v, all_v, att_v, inv_v, pre_v, grads, da_all, da_own, da_send, da_got, d_own, d_send, d_got, dpre_v,
    first_v, slots_v, turns_v, piece_v, wide_a, wide_b, temp_a, temp_b,
    go_v, so_v, wide_o, temp_o, gq_v, sq_v, wide_q, temp_q,
    tile_v, otile_v, lines_v, small_v, heads_v, lin1, lin2, lin3, small_r,
    load_sem, zsend, zrecv, piece_sem, xsend, xrecv, xload, own_sem, exsend, exrecv, osend, orecv, qsend, qrecv,
    tile_sem, outs_sem, sum_sem, smsend, smrecv,
):
    seqs, _, slots = all_v.shape
    span = slots // 2
    width = act_v.shape[1]
    half = width // 2
    groups = nq // nk
    share = span // 4
    row, core, rank = lax.axis_index("dp"), lax.axis_index("context"), lax.axis_index("tensor")
    start = core * span
    near = [row, xor_one(row), (row + 2) % 4, 3 - row]
    near_x, near_y, near_core = {"dp": near[1]}, {"dp": near[2]}, {"context": 1 - core}
    z_right, z_left, z_far = {"tensor": (rank + 1) % 4}, {"tensor": (rank + 3) % 4}, {"tensor": (rank + 2) % 4}
    first_core = core == 0

    def load(k, src, dst):
        copy = pltpu.make_async_copy(src, dst, load_sem.at[k])
        copy.start()
        return copy

    load_gb = load(0, gb_hbm, act_v)
    load_outw = load(1, outw_hbm, rows_v)
    load_att = [
        load(2, all_hbm, all_v), load(3, att_hbm, att_v), load(4, inv_hbm, inv_v), load(5, pre_hbm, pre_v),
    ]
    load_tok = load(6, tok_hbm, tok_v)
    load_qkvw = load(7, qkvw_hbm, qkvw_v)

    def piece_rows(s, m):
        return pl.ds(pl.multiple_of(s * span + m * share, share), share)

    def load_piece(s, m):
        return pltpu.make_async_copy(ffn_hbm.at[piece_rows(s, m), :], piece_v.at[s], piece_sem.at[s])

    greet([(None, d) for d in (near_x, near_y, {"dp": near[3]}, near_core, z_right, z_left, z_far)])

    last = seqs - 1
    inner = (rank % 3) != 0
    came = []
    for k, slot in enumerate((0, 1, 3)):
        came.append(pltpu.make_async_copy(ring_hbm.at[k], slots_v.at[0, slot], load_sem.at[12 + k]))

    @pl.when(inner)
    def _():
        for copy in came:
            copy.start()

    def ffn_own(s):
        def own(m):
            load_piece(s, m).wait()
            return lambda cut: piece_v[s, cut, :]

        return own

    def first_own(s):
        return lambda m: lambda cut: first_v[s, m, cut, :]

    ffn_rings = [
        Fold(
            rank, lambda m, s=s: ffn_hbm.at[piece_rows(s, m), :], ffn_own(s), slots_v.at[s], (slots_v.at[s, 3], slots_v.at[s, 4]),
            zsend.at[s], zrecv.at[s], came if s == 0 else None,
        )
        for s in range(seqs)
    ]
    first_rings = [
        Fold(
            rank, lambda m, s=s: first_v.at[s, m], first_own(s), turns_v.at[s], (fin_hbm.at[s], finb_hbm.at[s]),
            zsend.at[seqs + s], zrecv.at[seqs + s],
        )
        for s in range(seqs)
    ]
    for s in range(1, seqs):
        ffn_rings[s].begin()
    for s in range(seqs):
        load_piece(s, jnp.where(inner, ffn_rings[s].added[0], rank)).start()

    def ffn_step(s, k):
        ffn_rings[s].step(k)

        @pl.when(inner)
        def _():
            load_piece(s, ffn_rings[s].added[k + 1] if k < 2 else rank).start()

    def in_hbm(ref, axis):
        size = ref.shape[axis] // 4
        h2 = (size if axis == 0 else ref.shape[0]) // 2

        def get(k, h):
            if axis == 0:
                return ref.at[pl.ds(k * size + h * h2, h2), :]
            return ref.at[pl.ds(h * h2, h2), pl.ds(k * size, size)]

        return get

    def halves(ref):
        h2 = ref.shape[0] // 2
        return lambda h: ref.at[pl.ds(h * h2, h2), :]

    def in_vmem(ref):
        h2 = ref.shape[1] // 2
        return lambda k, h: ref.at[k, pl.ds(h * h2, h2), :]

    def scatter(i, get, wide, land_x, land_y, temps):
        return Scatter(get, wide.at[0], wide.at[1], land_x, land_y, temps, xsend.at[i], xrecv.at[i], xload.at[i], near_x, near_y)

    s_gate = scatter(0, in_hbm(dgate_hbm, 0), wide_a, halves(landx0), halves(landy0), temp_a)
    s_up = scatter(0, in_hbm(dup_hbm, 0), wide_a, halves(landx1), halves(landy1), temp_a)
    s_down = scatter(1, in_hbm(ddown_hbm, 1), wide_b, halves(landx2), halves(landy2), temp_b)
    s_out = scatter(2, in_vmem(go_v), wide_o, halves(landx3), halves(landy3), temp_o)
    s_qkv = scatter(3, in_vmem(gq_v), wide_q, halves(landx4), halves(landy4), temp_q)
    s_up.begin()
    ffn_step(0, 0)
    ffn_step(0, 1)

    load_gb.wait()
    load_outw.wait()

    def give(s):
        return remote(da_send.at[s], da_got.at[s], exsend.at[0, s], exrecv.at[0, s], near_core)

    def exchange(s):
        return remote(d_send.at[s], d_got.at[s], exsend.at[1, s], exrecv.at[1, s], near_core)

    def branch_rows(s, carry):
        here = pl.ds(pl.multiple_of(s * span, span), span)
        parts = []
        for q in range(2):
            cut = slice(q * (nq * hd // 2), (q + 1) * (nq * hd // 2))
            da = dot_nt(rows_v[0, cut, :], act_v[here, :half]) + dot_nt(rows_v[1, cut, :], act_v[here, half:])
            parts.append(da.astype(BF16))
        da_own[s] = jnp.where(first_core, parts[0], parts[1])
        da_send[s] = jnp.where(first_core, parts[1], parts[0])
        give(s).start()
        return carry

    lax.fori_loop(0, seqs, branch_rows, 0)

    def load_x(s):
        return [pltpu.make_async_copy(xr_hbm.at[s, :, pl.ds(k * half, half)], rows_v.at[k], load_sem.at[10 + k]) for k in range(2)]

    for copy in load_x(0):
        copy.start()
    for copy in load_att:
        copy.wait()

    scale = log2e / math.sqrt(hd)
    back = 1.0 / math.sqrt(hd)
    krow = lax.broadcasted_iota(jnp.int32, (block, groups * block), 0)
    qcol = lax.broadcasted_iota(jnp.int32, (block, groups * block), 1) % block
    base = groups * hd

    def attention(s):
        give(s).wait_recv()
        low, high = join_positions(core, da_own[s], da_got[s])
        da_all[:, :span] = low
        da_all[:, span:] = high
        length = len_ref[s]
        grads[base:, :] = jnp.zeros((2 * hd, slots), F32)
        for i in range(slots // block):
            cut = slice(i * block, (i + 1) * block)
            q = jnp.concatenate([all_v[s, g * hd : (g + 1) * hd, cut] for g in range(groups)], axis=1)
            da = jnp.concatenate([da_all[g * hd : (g + 1) * hd, cut] for g in range(groups)], axis=1)
            at = jnp.concatenate([att_v[s, g * hd : (g + 1) * hd, cut] for g in range(groups)], axis=1)
            inv = jnp.concatenate([inv_v[s, g : g + 1, cut] for g in range(groups)], axis=1)
            delta = jnp.sum(at.astype(F32) * da.astype(F32), axis=0, keepdims=True)
            dq = jnp.zeros((hd, groups * block), F32)
            for j in range(i + 1):
                kcut = slice(j * block, (j + 1) * block)
                key = all_v[s, base : base + hd, kcut]
                score = dot_tn(key, q) * scale
                ok = (krow + j * block) < length
                if j == i:
                    ok = ok & (krow <= qcol)
                p = jnp.where(ok, jnp.exp2(score) * inv, 0.0)
                dp = dot_tn(all_v[s, base + hd : base + 2 * hd, kcut], da)
                ds = (p * (dp - delta)).astype(BF16)
                dq = dq + dot_nn(key, ds)
                grads[base : base + hd, kcut] += dot_nt(q, ds) * back
                grads[base + hd : base + 2 * hd, kcut] += dot_nt(da, p.astype(BF16))
            dq = dq * back
            for g in range(groups):
                grads[g * hd : (g + 1) * hd, cut] = dq[:, g * block : (g + 1) * block]
        mine, theirs = join_positions(core, grads[:, :span], grads[:, span:])
        d_own[s] = mine.astype(BF16)
        d_send[s] = theirs.astype(BF16)
        exchange(s).start()

    quarter = hd // 2
    cosine, sine = table_ref[:quarter, :], table_ref[quarter : 2 * quarter, :]
    qgain, kgain = table_ref[2 * quarter : 2 * quarter + hd, 0:1], table_ref[2 * quarter + hd :, 0:1]
    sides = (nq // 2, nk // 2, nk // 2)
    copies_in_tensor = 1.0 / lax.axis_size("tensor")
    lines_v[:8, :] = jnp.zeros((8, width), F32)
    lines_v[8:, :] = gain2_ref[...] * copies_in_tensor
    heads_v[...] = jnp.zeros_like(heads_v)
    valid_slots = jnp.int32(0)
    for s in range(seqs):
        valid_slots = valid_slots + jnp.clip(len_ref[s] - start, 0, span)
    count = valid_slots.astype(F32) * (copies_in_tensor / 128.0)
    small_v[...] = jnp.zeros_like(small_v)
    for k in range(2):
        both = stat_ref[k] + stat2_ref[k]
        small_v[1 + k : 2 + k, :] = jnp.sum(both, axis=0, keepdims=True) * copies_in_tensor
    small_v[4:5, :] = jnp.broadcast_to(count, (1, 128))
    load_qkvw.wait()

    def fold_columns(values):
        return sum(values[:, k * 128 : (k + 1) * 128] for k in range(values.shape[1] // 128))

    def heads_rows(s):
        exchange(s).wait_recv()
        low, high = join_positions(core, d_own[s].astype(F32), d_got[s].astype(F32))
        parts = [[], [], []]
        for side in (low, high):
            at = 0
            for kind, number in enumerate(sides):
                for _ in range(number):
                    parts[kind].append(side[at : at + hd])
                    at += hd
        done = []
        for h in range(nq + nk):
            kind = 0 if h < nq else 1
            g = parts[kind][h - kind * nq]
            a, b = g[: hd // 2], g[hd // 2 :]
            g = jnp.concatenate([a * cosine + b * sine, b * cosine - a * sine], axis=0)
            v = pre_v[s, h * hd : (h + 1) * hd, :]
            inv = lax.rsqrt(jnp.mean(v * v, axis=0, keepdims=True) + epsilon)
            hat = v * inv
            heads_v[kind * hd : (kind + 1) * hd, :] += fold_columns(g * hat)
            gg = g * (qgain if kind == 0 else kgain)
            done.append(inv * (gg - hat * jnp.mean(gg * hat, axis=0, keepdims=True)))
        done += parts[2]
        for h in range(nq + 2 * nk):
            pair = h % 2
            if pair == 0:
                two = jnp.concatenate([done[h], done[h + 1]], axis=0).T.astype(BF16)
                dpre_v[pl.ds(pl.multiple_of(s * span, span), span), h * hd : (h + 2) * hd] = two
        for copy in load_x(s):
            copy.wait()
        for m in range(4):
            rows = slice(m * share, (m + 1) * share)
            xs = [rows_v[k, rows, :].astype(F32) for k in range(2)]
            mean = sum(jnp.sum(x * x, axis=-1, keepdims=True) for x in xs) * (1.0 / width)
            inv = lax.rsqrt(mean + epsilon)
            dpre = dpre_v[pl.ds(pl.multiple_of(s * span + m * share, share), share), :]
            for k in range(2):
                part = dot_nt(dpre, qkvw_v[k])
                cut = slice(k * half, (k + 1) * half)
                first_v[s, m, :, cut] = part.astype(BF16)
                both = part * (xs[k] * inv)
                lines_v[:8, cut] += sum(both[8 * r : 8 * r + 8] for r in range(share // 8))

    def sequence(s, carry):
        attention(s)

        @pl.when(s == last)
        def _():
            ffn_step(1, 1)
            s_up.pass_on()

        heads_rows(s)

        @pl.when(s == 0)
        def _():
            for copy in load_x(1):
                copy.start()
            first_rings[0].begin()
            ffn_step(1, 0)
            ffn_step(0, 2)
            s_down.begin()

        @pl.when(s == last)
        def _():
            first_rings[1].begin()

        return carry

    lax.fori_loop(0, seqs, sequence, 0)

    def hop_copies(n, items):
        base_at = (0, 1, 4, 5, 8)[n]
        return [
            remote(src, dst, smsend.at[base_at + i], smrecv.at[base_at + i], device) for i, (device, src, dst, _) in enumerate(items)
        ]

    def hop_begin(n, items):
        for copy in hop_copies(n, items):
            copy.start()

    def hop_end(n, items):
        for copy in hop_copies(n, items):
            copy.wait()
        for _, _, dst, place_to in items:
            if place_to is None:
                small_v[...] += dst[...]
            else:
                lines_v[:, place_to] += dst[...]

    piece = width // 8

    def columns(k):
        return slice(k * piece, (k + 1) * piece)

    def view(k, count=1):
        return lines_v.at[:, pl.ds(k * piece, count * piece)]

    hop_core = [(near_core, view(4, 4), lin1, slice(0, half))]
    near_all = [near_x, near_y, {"dp": near[3]}]
    hop_lines = [(near_all[k], view(1 + k), lin2.at[k], columns(0)) for k in range(3)]
    hop_small = [(near_core, small_v, small_r.at[0], None)]
    hop_square = [(near_all[k], small_v, small_r.at[1 + k], None) for k in range(3)]
    z_all = [z_right, z_far, z_left]
    hop_chain = [(z_all[k], view(0), lin3.at[k], columns(0)) for k in range(3)]
    hop_chain += [(z_all[k], small_v, small_r.at[4 + k], None) for k in range(3)]
    hop_begin(0, hop_core)

    load_tok.wait()
    blocks_o = [remote(so_v.at[k], go_v.at[k], osend.at[k], orecv.at[k], near_core) for k in range(4)]
    size_o = half // 4
    for k in range(4):
        cut = slice(half + k * size_o, half + (k + 1) * size_o)
        so_v[k] = dot_tn(tok_v[...], act_v[:, cut]).astype(BF16)
        blocks_o[k].start()
    ffn_step(1, 2)
    for k in range(4):
        blocks_o[k].wait_recv()
        cut = slice(k * size_o, (k + 1) * size_o)
        go_v[k] = (dot_tn(tok_v[...], act_v[:, cut]) + go_v[k].astype(F32)).astype(BF16)
    s_out.begin()
    load_n1 = load(0, n1_hbm, act_v)
    hop_end(0, hop_core)
    hop_begin(1, hop_lines)
    load_n1.wait()
    blocks_q = [remote(sq_v.at[k], gq_v.at[k], qsend.at[k], qrecv.at[k], near_core) for k in range(4)]
    size_q = half // 4
    for k in range(4):
        cut = slice(half + k * size_q, half + (k + 1) * size_q)
        sq_v[k] = dot_tn(act_v[:, cut], dpre_v[...]).astype(BF16)
        blocks_q[k].start()
    for k in range(4):
        blocks_q[k].wait_recv()
        cut = slice(k * size_q, (k + 1) * size_q)
        gq_v[k] = (dot_tn(act_v[:, cut], dpre_v[...]) + gq_v[k].astype(F32)).astype(BF16)
    s_qkv.begin()
    keeps = [
        pltpu.make_async_copy(go_v.at[0], mine_o, own_sem.at[0]),
        pltpu.make_async_copy(gq_v.at[0], mine_q, own_sem.at[1]),
    ]
    keeps += [pltpu.make_async_copy(first_v.at[s, rank], own_hbm.at[s], own_sem.at[2 + s]) for s in range(seqs)]
    for copy in keeps:
        copy.start()


    def place(tile, dst, s):
        for o in range(2):
            for k in range(4):
                b = near[k] * 2 + (core if o == 0 else 1 - core)
                cut = pl.ds(pl.multiple_of(b * piece, piece), piece)
                pltpu.make_async_copy(tile.at[:, pl.ds((o * 4 + k) * piece, piece)], dst.at[s, :, cut], outs_sem).start()
        pltpu.make_async_copy(tile, dst.at[s], outs_sem).wait()

    def out_share(s):
        keep = pltpu.make_async_copy(hidden_hbm.at[piece_rows(s, rank), :], tile_v, tile_sem.at[0])
        keep.start()
        ffn_rings[s].arrived()
        read = ffn_rings[s].own(rank)
        keep.wait()

        def body(cut, first):
            ffn = slots_v[s, 3, cut, :].astype(F32) + read(cut).astype(F32)
            ffn = ffn + jnp.where(inner, slots_v[s, 4, cut, :].astype(F32), 0.0)
            otile_v[cut, :] = (tile_v[cut, :] + ffn).astype(BF16)
            spot = start + rank * share + first + lax.broadcasted_iota(jnp.int32, (16, 1), 0)
            valid = (spot < len_ref[s]).astype(F32)
            small_v[3:4, :] += jnp.sum(fold_lanes(valid * ffn * ffn), axis=0, keepdims=True)

        by_pieces(share, body)
        place(otile_v, out_hbm, s)

    def in_share(s):
        first_rings[s].arrived()
        tiles = (piece_v.at[0], piece_v.at[1], otile_v)
        rows = pl.ds(pl.multiple_of(rank * share, share), share)
        loads = [
            pltpu.make_async_copy(src, dst, load_sem.at[k])
            for k, (src, dst) in enumerate(zip((fin_hbm.at[s], finb_hbm.at[s], xr_hbm.at[s, rows, :]), tiles))
        ]
        loads.append(pltpu.make_async_copy(gh_hbm.at[s], tile_v, load_sem.at[3]))
        for copy in loads:
            copy.start()
        gain = jnp.concatenate([gains_ref[b, 0:1, :] for b in range(8)], axis=1).astype(F32)
        for copy in loads:
            copy.wait()

        def body(cut, at):
            e = piece_v[0, cut, :].astype(F32) + first_v[s, rank, cut, :].astype(F32)
            e = e + jnp.where(inner, piece_v[1, cut, :].astype(F32), 0.0)
            x = otile_v[cut, :].astype(F32)
            inv = inverse_rms(x)
            hat = x * inv
            eg = e * gain
            tile_v[cut, :] = tile_v[cut, :] + inv * (eg - hat * jnp.mean(eg * hat, axis=-1, keepdims=True))

        by_pieces(share, body)
        place(tile_v, gin_hbm, s)

    small_v[0:1, :] = jnp.sum(heads_v[...].T, axis=0, keepdims=True)
    first_rings[0].step(0)
    out_share(0)
    s_down.pass_on()
    out_share(1)
    hop_end(1, hop_lines)
    hop_begin(2, hop_small)
    hop_end(2, hop_small)
    hop_begin(3, hop_square)
    first_rings[0].step(1)
    first_rings[0].step(2)
    s_out.pass_on()
    s_qkv.pass_on()
    s_gate.keep(halves(sum_gate), sum_sem)
    s_up.arrived()
    s_up.keep(halves(sum_up), sum_sem)
    first_rings[1].step(0)
    hop_end(3, hop_square)
    hop_begin(4, hop_chain)
    s_down.arrived()
    s_down.keep(halves(sum_down), sum_sem)
    first_rings[1].step(1)
    first_rings[1].step(2)
    for s in range(last):
        in_share(s)
    hop_end(4, hop_chain)
    lines_out[...] = lines_v[:, :piece]
    small_out[...] = small_v[...]
    for item in (s_out, s_qkv):
        item.arrived()
    first_rings[last].arrived()
    for copy in keeps:
        copy.wait()
    for ring in ffn_rings + first_rings:
        ring.settle()
    for item in (s_up, s_down, s_out, s_qkv):
        item.settle()
    for copy in blocks_o + blocks_q:
        copy.wait_send()
    for s in range(seqs):
        give(s).wait_send()
        exchange(s).wait_send()


def backward(
    lengths, gb, hidden_rows, ffn, ring, xr, n1, tok, outw, qkvw, everything, att, inv, pre, gh, dgate, landx, landy, dup, ddown,
    table, gains, stat, stat2, gain2_part, hd, nq, nk,
):
    seqs, span, width = xr.shape
    half = width // 2
    groups = nq // nk
    share = span // 4
    piece = width // 8
    hidden = dup.shape[1]
    cols = qkvw.shape[2]
    feat = nq * hd
    block = min(256, span)
    any_space = pl.BlockSpec(memory_space=pl.ANY)
    vmem = pl.BlockSpec(memory_space=pltpu.VMEM)
    dma = pltpu.SemaphoreType.DMA
    hold = lambda *dims: pltpu.VMEM(dims, BF16)
    wide = lambda *dims: pltpu.VMEM(dims, F32)
    token = shape((seqs, share, width), BF16)
    big = [token, shape((seqs - 1, share, width), F32)] + [token] * 3 + [shape((piece, hidden), BF16)] * 2 + [shape((hidden, piece), BF16)]
    big += [shape((feat, piece), BF16), shape((piece, cols), BF16)]
    big += [shape((piece, hidden), BF16)] * 2 + [shape((hidden, piece), BF16)] * 2
    big += [shape((feat, piece), BF16)] * 2 + [shape((piece, cols), BF16)] * 2
    small = [shape((16, piece), F32), shape((8, 128), F32)]
    rows = everything.shape[1]
    scratch = [
        hold(seqs * span, width), hold(2, span, half), hold(2, half, cols), hold(seqs * span, feat), hold(*everything.shape), hold(*att.shape),
        wide(*inv.shape), wide(*pre.shape), wide(rows, 2 * span), hold(groups * hd, 2 * span),
        hold(seqs, feat // 2, span), hold(seqs, feat // 2, span), hold(seqs, feat // 2, span),
        hold(seqs, rows, span), hold(seqs, rows, span), hold(seqs, rows, span), hold(seqs * span, cols),
        hold(seqs, 4, share, width), hold(seqs, 5, share, width), hold(seqs, 3, share, width), hold(seqs, share, width),
        hold(2, piece // 2, hidden), hold(2, hidden // 2, piece), hold(3, piece // 2, hidden), hold(3, hidden // 2, piece),
        hold(4, feat, piece), hold(4, feat, piece), hold(2, feat // 2, piece), hold(2, feat // 2, piece),
        hold(4, piece, cols), hold(4, piece, cols), hold(2, piece // 2, cols), hold(2, piece // 2, cols),
        wide(share, width), hold(share, width),
        wide(16, width), wide(8, 128), wide(2 * hd, 128), wide(16, half), wide(3, 16, piece), wide(3, 16, piece), wide(7, 8, 128),
        dma((15,)), dma((2 * seqs,)), dma((2 * seqs, 5)), dma((seqs,)), dma((4, 6)), dma((4, 6)), dma((4, 3)), dma((2 + seqs,)),
        dma((2, seqs)), dma((2, seqs)), dma((4,)), dma((4,)), dma((4,)), dma((4,)), dma((2,)), dma(()), dma(()), dma((14,)), dma((14,)),
    ]
    tokens = seqs * span
    return pl.pallas_call(
        functools.partial(backward_kernel, hd, nq, nk, block),
        in_specs=[SMEM] + [any_space] * 19 + [vmem] * 5,
        out_specs=[any_space] * len(big) + [vmem] * 2,
        out_shape=big + small,
        scratch_shapes=scratch,
        compiler_params=pltpu.CompilerParams(vmem_limit_bytes=VMEM_MOST, collective_id=3, has_side_effects=True),
        cost_estimate=cost(4 * tokens * width * (cols + feat), 60 * tokens * width),
        name="attention_backward",
    )(
        lengths, gb, hidden_rows, ffn, ring, xr, n1, tok, outw, qkvw, everything, att, inv, pre, gh, dgate, landx, landy, dup, ddown,
        table, gains, stat, stat2, gain2_part,
    )


def results_kernel(
    hd, nqc, nkc, count,
    sum_gate, sum_up, sum_down, mine_o, lx3, ly3, mine_q, lx4, ly4, gh, xr, fin, finb, own, out, early, gains_ref, lines_ref, small_ref,
    output, gin, ggate, gup, gdown, gout, gq, gk, gv, gain_a, gain_b, gain_q, gain_k, rms,
    gate_i, up_i, down_i, o_i, q_i, gate_o, up_o, down_o, o_o, q_o, gh_v, x_v, fin_v, finb_v, own_v, early_v, out_v,
    in_sem, token_sem, out_sem, place_sem, copy_sem,
):
    row, core, rank = lax.axis_index("dp"), lax.axis_index("context"), lax.axis_index("tensor")
    near = [row, xor_one(row), (row + 2) % 4, 3 - row]
    seqs, share, width = out_v.shape
    last = seqs - 1
    piece = width // 8
    sums = (
        ((sum_gate,), gate_i, gate_o, ((0, ggate),)),
        ((sum_up,), up_i, up_o, ((0, gup),)),
        ((sum_down,), down_i, down_o, ((0, gdown),)),
        ((mine_o, lx3, ly3), o_i, o_o, ((0, gout),)),
        ((mine_q, lx4, ly4), q_i, q_o, ((0, gq), (nqc, gk), (nqc + nkc, gv))),
    )
    simple = [
        (pltpu.make_async_copy(out, out_v, copy_sem.at[0]), pltpu.make_async_copy(out_v, output, copy_sem.at[1])),
        (pltpu.make_async_copy(early, early_v, copy_sem.at[2]), pltpu.make_async_copy(early_v, gin.at[pl.ds(0, last)], copy_sem.at[3])),
    ]

    def loads(i):
        return [pltpu.make_async_copy(src, sums[i][1].at[k], in_sem.at[i, k]) for k, src in enumerate(sums[i][0])]

    mine = pl.ds(pl.multiple_of(rank * share, share), share)
    tokens = [
        pltpu.make_async_copy(src, dst, token_sem.at[k])
        for k, (src, dst) in enumerate(
            ((gh.at[last], gh_v), (xr.at[last, mine, :], x_v), (fin.at[last], fin_v), (finb.at[last], finb_v), (own.at[last], own_v))
        )
    ]
    for i in range(len(sums)):
        for copy in loads(i):
            copy.start()
    for copy in tokens + [first for first, _ in simple]:
        copy.start()

    first = jnp.sum(lines_ref[:8, :], axis=0, keepdims=True)
    second = jnp.sum(lines_ref[8:, :], axis=0, keepdims=True)
    gain_a[...] = first.reshape(gain_a.shape)
    gain_b[...] = second.reshape(gain_b.shape)
    gain_q[...] = small_ref[0:1, :hd].reshape(gain_q.shape)
    gain_k[...] = small_ref[0:1, hd : 2 * hd].reshape(gain_k.shape)
    total = jnp.sum(small_ref[4:5, :], keepdims=True) * count
    for k in range(3):
        square = jnp.sum(small_ref[1 + k : 2 + k, :], keepdims=True) / total
        rms[k] = jnp.max(jnp.sqrt(jnp.broadcast_to(square, (8, 128))))

    stores = []
    for i, (terms, came, total_v, parts) in enumerate(sums):
        for copy in loads(i):
            copy.wait()

        def body(cut, at):
            total_v[cut, :] = sum(came[k, cut, :].astype(F32) for k in range(len(terms)))

        by_pieces(total_v.shape[0], body, tall(total_v))
        for n, (at, dst) in enumerate(parts):
            stores.append(pltpu.make_async_copy(total_v.at[:, pl.ds(at, dst.shape[1])], dst, out_sem.at[i, n]))
            stores[-1].start()
    for first, second in simple:
        first.wait()
        second.start()

    gain = jnp.concatenate([gains_ref[b, 0:1, :] for b in range(8)], axis=1).astype(F32)
    for copy in tokens:
        copy.wait()
    inner = (rank % 3) != 0

    def body(cut, at):
        e = fin_v[cut, :].astype(F32) + own_v[cut, :].astype(F32)
        e = e + jnp.where(inner, finb_v[cut, :].astype(F32), 0.0)
        x = x_v[cut, :].astype(F32)
        inv = inverse_rms(x)
        hat = x * inv
        eg = e * gain
        gh_v[cut, :] = gh_v[cut, :] + inv * (eg - hat * jnp.mean(eg * hat, axis=-1, keepdims=True))

    by_pieces(share, body)
    for o in range(2):
        for k in range(4):
            b = near[k] * 2 + (core if o == 0 else 1 - core)
            cut = pl.ds(pl.multiple_of(b * piece, piece), piece)
            src = gh_v.at[:, pl.ds((o * 4 + k) * piece, piece)]
            stores.append(pltpu.make_async_copy(src, gin.at[last, :, cut], place_sem.at[o * 4 + k]))
            stores[-1].start()
    for copy in stores + [second for _, second in simple]:
        copy.wait()


def finish_results(sums, mine_o, mine_q, lands_o, lands_q, gh, xr, fin, finb, own, out, early, gains, lines, small, hd, nqc, nkc):
    seqs, share, width = out.shape
    hidden = sums[0].shape[1]
    piece = width // 8
    any_space = pl.BlockSpec(memory_space=pl.ANY)
    vmem = pl.BlockSpec(memory_space=pltpu.VMEM)
    dma = pltpu.SemaphoreType.DMA
    blocks = [(piece, hidden), (piece, hidden), (hidden, piece), mine_o.shape, mine_q.shape]
    terms = (1, 1, 1, 3, 3)
    outs = [shape(out.shape, BF16), shape(out.shape, F32)] + [shape(b, F32) for b in blocks[:4]]
    outs += [shape((piece, size), F32) for size in (nqc, nkc, nkc)]
    tiny = [shape((size,), F32) for size in (piece, piece, hd, hd)]
    token = pltpu.VMEM((share, width), BF16)
    return pl.pallas_call(
        functools.partial(results_kernel, hd, nqc, nkc, float(width)),
        in_specs=[any_space] * 16 + [vmem] * 3,
        out_specs=[any_space] * len(outs) + [vmem] * 4 + [SMEM],
        out_shape=outs + tiny + [shape((3,), F32)],
        scratch_shapes=[pltpu.VMEM((n,) + tuple(b), BF16) for n, b in zip(terms, blocks)]
        + [pltpu.VMEM(b, F32) for b in blocks]
        + [pltpu.VMEM((share, width), F32), token, token, token, token, pltpu.VMEM(early.shape, F32), pltpu.VMEM(out.shape, BF16)]
        + [dma((5, 3)), dma((5,)), dma((5, 3)), dma((8,)), dma((4,))],
        compiler_params=PARAMS,
        cost_estimate=cost(30 * piece * hidden, 40 * piece * hidden),
        name="results",
    )(*sums, mine_o, *lands_o, mine_q, *lands_q, gh, xr, fin, finb, own, out, early, gains, lines, small)


def per_device_general(
    inputs,
    cotangent,
    lengths,
    w_query,
    key_projection_weight,
    value_projection_weight,
    w_output,
    w_gate,
    w_up,
    w_down,
    attn_gain,
    ffn_gain,
    query_gain,
    key_gain,
):
    seqs, span, width = inputs.shape
    hd = query_gain.shape[0]
    nq = w_query.shape[1] // hd
    nk = key_projection_weight.shape[1] // hd
    groups = nq // nk
    dp = lax.axis_size("dp")
    tensor = lax.axis_size("tensor")
    core = lax.axis_index("context")
    rank = lax.axis_index("tensor")
    chunks = 2
    rows = span // chunks
    share = span // tensor
    lengths = lengths.astype(jnp.int32)
    start = (core * span).astype(jnp.int32)
    core1 = core.astype(jnp.int32).reshape(1)
    ids = block_order(dp, core)
    order = 2 * dp if (width // (2 * dp)) % 128 == 0 else 1

    positions = start + jnp.arange(span, dtype=jnp.int32)
    freqs = rope_base ** (-(jnp.arange(hd // 2, dtype=F32) * (2.0 / hd)))
    angles = freqs[:, None] * positions.astype(F32)[None, :]
    cosine, sine = jnp.cos(angles), jnp.sin(angles)
    qgain = query_gain.astype(F32).reshape(hd, 1)
    kgain = key_gain.astype(F32).reshape(hd, 1)

    w_qkv = jnp.concatenate([w_query, key_projection_weight, value_projection_weight], axis=1)
    saved = []
    gains = gather_blocks(jnp.stack([attn_gain, ffn_gain]), 1)
    gains = jnp.concatenate([gains[0], gains[1]], axis=1).astype(F32)
    gain1, gain2 = gains[0:1], gains[1:2]
    qkv = gather_blocks(w_qkv, 0)
    out_w = gather_blocks(w_output, 1)
    gate = gather_blocks(w_gate, 0)
    up = gather_blocks(w_up, 0)
    down = gather_blocks(w_down, 1)

    scal = jnp.concatenate([lengths, start.reshape(1), ids])
    x_in, cot_in = inputs, cotangent
    if order == 1:
        x_in, cot_in = to_relative(x_in, dp, core), to_relative(cot_in, dp, core)
    xr, n1, gf = begin(x_in, cot_in, gain1, scal, order)

    parts, tok = [], []
    for s in range(seqs):
        pre, own, oth = heads(n1, s, qkv, cosine, sine, qgain, kgain, core1, hd, nq, nk)
        seq_scal = jnp.stack([lengths[s], core.astype(jnp.int32)])
        everything, att, inv, mine, theirs = attend(seq_scal, own, over_core(oth), groups)
        branched = branch(mine, over_core(theirs), out_w, core1, chunks)
        saved.append((pre, everything, att, inv, seq_scal))
        tok.append(jnp.swapaxes(branched[0], 0, 1))
        parts.append(branched[1:])
    tok = jnp.concatenate(tok, axis=0)

    stats = jnp.zeros((2,), F32)
    hidden_all, n2_all = [], []
    for s in range(seqs):
        for k in range(chunks):
            terms = [lax.psum(parts[s][k], "tensor")]
            place = jnp.stack([lengths[s], start + k * rows])
            hidden, n2, stat = second_norm(place, xr, s, k, gain2, terms)
            hidden_all.append(hidden)
            n2_all.append(n2)
            stats = stats + stat[:2, 0]
    hidden_all, n2_all = jnp.concatenate(hidden_all), jnp.concatenate(n2_all)

    ffn_squares = jnp.zeros((), F32)
    out_shares = []

    def piece_of(arrays):
        per = arrays[0].shape[0] // share

        def piece(k):
            found = lax.dynamic_slice_in_dim(arrays[0], jnp.minimum(k, per - 1) * share, share, 0)
            for m in range(1, len(arrays)):
                here = lax.dynamic_slice_in_dim(arrays[m], jnp.clip(k - m * per, 0, per - 1) * share, share, 0)
                found = jnp.where(k >= m * per, here, found)
            return found

        return piece

    def share_scalars(s):
        head = jnp.stack([rank.astype(jnp.int32), lengths[s], start + rank.astype(jnp.int32) * share, jnp.int32(tensor)])
        return jnp.concatenate([head, ids])

    def flat(nested):
        return [item for inner_list in nested for item in inner_list]

    def slices(array, count):
        size = array.shape[0] // count
        return [array[i * size : (i + 1) * size] for i in range(count)]

    def reduced(lefts, rights, axis):
        oth = weight_grad(lefts, rights, 1, axis)
        own = weight_grad(lefts, rights, 0, axis, over_core(oth))
        return scatter_blocks(own, axis)

    inner, gg, gu, ffn, gn = [[[None] * chunks for _ in range(seqs)] for _ in range(5)]
    for s in range(seqs):
        for k in range(chunks):
            inner[s][k], gg[s][k], gu[s][k], ffn[s][k], gn[s][k] = feed(
                n2_all, s * chunks + k, rows, gf, s, k, gate, up, down
            )
    gain2_grad = jnp.zeros((1, width), F32)
    gb, gh = [[[None] * chunks for _ in range(seqs)] for _ in range(2)]
    for s in range(seqs):
        for k in range(chunks):
            terms = [lax.psum(gn[s][k], "tensor")]
            gb[s][k], gh[s][k], gain_part = second_back(hidden_all, s * chunks + k, gf, s, k, gain2, terms)
            gain2_grad = gain2_grad + gain_part
    gf_list = slices(gf.reshape(seqs * span, width), seqs * chunks)
    n2_list = slices(n2_all, seqs * chunks)
    grad_w_down = reduced(flat(inner), gf_list, 1)
    grad_w_gate = reduced(n2_list, flat(gg), 0)
    grad_w_up = reduced(n2_list, flat(gu), 0)
    for s in range(seqs):
        got = ring_scatter(piece_of(ffn[s]), tensor, rank)
        halves = [hidden_all[(s * chunks + k) * rows : (s * chunks + k + 1) * rows] for k in range(chunks)]
        out, stat = output_share(share_scalars(s), got, ffn[s], halves, order)
        out_shares.append(out)
        ffn_squares = ffn_squares + stat[0, 0]

    gain1_grad = jnp.zeros((1, width), F32)
    head_gain = jnp.zeros((2 * hd,), F32)
    dpres, in_shares = [], []
    for s in range(seqs):
        pre, everything, att, inv, seq_scal = saved[s]
        da_own, da_oth = branch_back(gb[s], out_w, core1)
        d_own, d_oth = attend_back(seq_scal, everything, att, inv, da_own, over_core(da_oth), groups)
        dpre, first, gain_part, hg = heads_back(
            d_own, over_core(d_oth), pre, cosine, sine, qgain, kgain, xr, s, qkv, core1, hd, nq, nk
        )
        gain1_grad = gain1_grad + gain_part
        head_gain = head_gain + hg[:, 0]
        dpres.append(dpre)
        got = ring_scatter(piece_of([first]), tensor, rank)
        in_shares.append(input_share(share_scalars(s), got, first, gh[s], xr, s, gain1, order))

    att_list = [tok[i * rows : (i + 1) * rows] for i in range(seqs * chunks)]
    grad_w_output = reduced(att_list, flat(gb), 1)
    grad_qkv = reduced([n1[s] for s in range(seqs)], dpres, 0)
    nqc, nkc = nq * hd, nk * hd
    grad_w_query = grad_qkv[:, :nqc]
    grad_w_key = grad_qkv[:, nqc : nqc + nkc]
    grad_w_value = grad_qkv[:, nqc + nkc :]

    gain2_grad = gain2_grad / tensor
    counts = jnp.sum(jnp.clip(lengths - start, 0, span)).astype(F32) / tensor
    small = jnp.concatenate([head_gain, stats / tensor, ffn_squares.reshape(1), counts.reshape(1)])
    small = jnp.pad(small, (0, (-small.shape[0]) % 128)).reshape(1, -1)
    lines = jnp.concatenate([gain1_grad, gain2_grad], axis=0)
    piece = width // (2 * dp)
    lines = to_absolute(lines, dp, core)
    lines, small = lax.psum((lines, small), ("dp", "context", "tensor"))
    lines = lax.dynamic_slice_in_dim(lines, lax.axis_index(("dp", "context")) * piece, piece, 1)
    small = small[0]
    rms_values = jnp.sqrt(small[2 * hd : 2 * hd + 3] / (small[2 * hd + 3] * width))

    output = jnp.stack(out_shares)
    grad_inputs = jnp.stack(in_shares)
    if order == 1:
        output, grad_inputs = to_absolute(output, dp, core), to_absolute(grad_inputs, dp, core)
    return (
        output,
        grad_inputs,
        grad_w_query,
        grad_w_key,
        grad_w_value,
        grad_w_output,
        grad_w_gate,
        grad_w_up,
        grad_w_down,
        lines[0],
        lines[1],
        small[:hd],
        small[hd : 2 * hd],
        rms_values,
    )


def per_device_square(
    inputs,
    cotangent,
    lengths,
    w_query,
    key_projection_weight,
    value_projection_weight,
    w_output,
    w_gate,
    w_up,
    w_down,
    attn_gain,
    ffn_gain,
    query_gain,
    key_gain,
):
    seqs, span, width = inputs.shape
    hd = query_gain.shape[0]
    nq = w_query.shape[1] // hd
    nk = key_projection_weight.shape[1] // hd
    lengths = lengths.astype(jnp.int32)
    all_gains = (attn_gain, ffn_gain, query_gain, key_gain)
    (
        xr, n1, gf, qkv, out_w, gate, up, down, hidden, n2, rest, gi, pre, everything, att, tok, gains, table, inv, stat
    ) = forward(
        lengths, inputs, cotangent, w_query, key_projection_weight, value_projection_weight, w_output, w_gate, w_up, w_down,
        all_gains, hd, nq, nk,
    )
    tokens = seqs * span
    flat = lambda a: a.reshape(tokens, -1)
    ffn, gb, gh, d_gate, d_up, d_down, hidden, landx, landy, ring, gain2_part, stat2 = feed_both(
        lengths, n2, flat(gf), gate, up, down, gi, rest, flat(xr), hidden, gains
    )
    (
        output, early, fin, finb, own, sum_gate, sum_up, sum_down, mine_o, mine_q, _, _, _, _, lx3, ly3, lx4, ly4, lines, small
    ) = backward(
        lengths, gb, hidden, ffn, ring, xr, flat(n1), flat(tok), out_w, qkv,
        everything, att, inv, pre, gh, d_gate, landx, landy, d_up, d_down, table, gains, stat, stat2, gain2_part, hd, nq, nk,
    )
    nqc, nkc = nq * hd, nk * hd
    output, grad_inputs, grad_gate, grad_up, grad_down, grad_out, grad_q, grad_k, grad_v, *small = finish_results(
        (sum_gate, sum_up, sum_down), mine_o, mine_q, (lx3, ly3), (lx4, ly4), gh, xr, fin, finb, own, output, early, gains,
        lines, small, hd, nqc, nkc,
    )
    return (output, grad_inputs, grad_q, grad_k, grad_v, grad_out, grad_gate, grad_up, grad_down, *small)


def per_device(*args):
    inputs, w_query = args[0], args[3]
    seqs, span, width = inputs.shape
    square = lax.axis_size("dp") == 4 and lax.axis_size("tensor") == 4 and lax.axis_size("context") == 2
    if square and width % 2048 == 0 and span % 512 == 0 and seqs == 2 and w_query.shape[1] == span:
        return per_device_square(*args)
    return per_device_general(*args)


def solution(mesh):
    both = ("dp", "context")
    rows = P(both, "tensor")
    cols = P("tensor", both)
    shares = P("dp", ("context", "tensor"), None)
    acts = P("dp", "context", None)
    return jax.shard_map(
        per_device,
        mesh=mesh,
        in_specs=(acts, acts, P("dp"), rows, rows, rows, cols, rows, rows, cols, P(both), P(both), P(), P()),
        out_specs=(shares, shares, rows, rows, rows, cols, rows, rows, cols, P(both), P(both), P(), P(), P()),
        check_vma=False,
    )
```

```python
import functools
import math

import jax
import jax.numpy as jnp
from jax import lax
from jax.experimental import pallas as pl
from jax.experimental.pallas import tpu as pltpu
from jax.sharding import PartitionSpec as P

F32 = jnp.float32
BF16 = jnp.bfloat16
epsilon = 1e-05
rope_base = 1000000.0
log2e = 1.4426950408889634
VMEM_BYTES = 60 * 1024 * 1024
VMEM_MOST = 63 * 1024 * 1024
PARAMS = pltpu.CompilerParams(vmem_limit_bytes=VMEM_BYTES)
SMEM = pl.BlockSpec(memory_space=pltpu.SMEM)
SWAP = ((0, 1), (1, 0))


def shape(dims, dtype):
    return jax.ShapeDtypeStruct(tuple(dims), dtype)


def cost(flops, size, exps=0):
    return pl.CostEstimate(flops=int(flops), bytes_accessed=int(size), transcendentals=int(exps))


def dot_nn(a, b):
    return lax.dot_general(a, b, (((1,), (0,)), ((), ())), preferred_element_type=F32)


def dot_nt(a, b):
    return lax.dot_general(a, b, (((1,), (1,)), ((), ())), preferred_element_type=F32)


def dot_tn(a, b):
    return lax.dot_general(a, b, (((0,), (0,)), ((), ())), preferred_element_type=F32)


def inverse_rms(values):
    return lax.rsqrt(jnp.mean(values * values, axis=-1, keepdims=True) + epsilon)


def block_order(dp, core):
    return jnp.stack([jnp.int32(k) * 2 + (core ^ o) for o in range(2) for k in range(dp)]).astype(jnp.int32)


def to_relative(values, dp, core):
    lead = values.shape[:-1]
    parts = values.reshape(lead + (dp, 2, -1))
    parts = jnp.where(core == 0, parts, parts[..., ::-1, :])
    return jnp.swapaxes(parts, -3, -2).reshape(values.shape)


def to_absolute(values, dp, core):
    lead = values.shape[:-1]
    parts = jnp.swapaxes(values.reshape(lead + (2, dp, -1)), -3, -2)
    return jnp.where(core == 0, parts, parts[..., ::-1, :]).reshape(values.shape)


def over_core(value):
    return lax.ppermute(value, "context", SWAP)


def gather_blocks(weight, axis):
    own = lax.all_gather(weight, "dp", axis=axis, tiled=True)
    return jnp.stack([own, over_core(own)])


def scatter_blocks(total, axis):
    return lax.psum_scatter(total, "dp", scatter_dimension=axis, tiled=True).astype(F32)


def ring_scatter(piece, tensor, rank):
    ring = [(i, (i + 1) % tensor) for i in range(tensor)]
    moving = piece((rank + tensor - 1) % tensor)
    for step in range(1, tensor):
        moving = lax.ppermute(moving, "tensor", ring)
        if step < tensor - 1:
            moving = (moving.astype(F32) + piece((rank + tensor - 1 - step) % tensor).astype(F32)).astype(BF16)
    return moving


def begin_kernel(order, x_ref, cot_ref, gain_ref, scal_ref, xr_ref, n1_ref, gf_ref):
    seq, tile = pl.program_id(0), pl.program_id(1)
    rows, width = x_ref.shape[1:]
    seqs = pl.num_programs(0)
    place = scal_ref[seqs] + tile * rows + lax.broadcasted_iota(jnp.int32, (rows, 1), 0)
    valid = (place < scal_ref[seq]).astype(F32)
    x = x_ref[0].astype(F32)
    inv = inverse_rms(x)
    piece = width // order
    for k in range(order):
        src = pl.ds(pl.multiple_of(scal_ref[seqs + 1 + k] * piece, piece), piece) if order > 1 else slice(0, width)
        dst = slice(k * piece, (k + 1) * piece)
        part = x_ref[0, :, src]
        xr_ref[0, :, dst] = part
        n1_ref[0, :, dst] = (part.astype(F32) * inv * gain_ref[:, dst]).astype(BF16)
        gf_ref[0, :, dst] = (cot_ref[0, :, src].astype(F32) * valid).astype(BF16)


def begin(x, cot, gain, scalars, order):
    seqs, span, width = x.shape
    rows = min(256, span)
    spec = pl.BlockSpec((1, rows, width), lambda s, i: (s, i, 0))
    return pl.pallas_call(
        functools.partial(begin_kernel, order),
        grid=(seqs, span // rows),
        in_specs=[spec, spec, pl.BlockSpec((1, width), lambda s, i: (0, 0)), SMEM],
        out_specs=[spec] * 3,
        out_shape=[shape(x.shape, BF16)] * 3,
        compiler_params=PARAMS,
        cost_estimate=cost(8 * x.size, 10 * x.size),
        name="first_norm",
    )(x, cot, gain, scalars)


def heads_kernel(hd, nq, nk, n1_ref, w_ref, cos_ref, sin_ref, qg_ref, kg_ref, core_ref, pre_ref, own_ref, oth_ref):
    half = w_ref.shape[1]
    x = n1_ref[0]
    flat = dot_nn(x[:, :half], w_ref[0]) + dot_nn(x[:, half:], w_ref[1])
    turned = flat.T
    span = turned.shape[1]
    normed = turned[: (nq + nk) * hd]
    pre_ref[...] = normed
    core = core_ref[0]
    cosine, sine = cos_ref[...], sin_ref[...]
    done = []
    for h in range(nq + nk):
        v = normed[h * hd : (h + 1) * hd]
        inv = lax.rsqrt(jnp.mean(v * v, axis=0, keepdims=True) + epsilon)
        v = v * inv * (qg_ref[...] if h < nq else kg_ref[...])
        a, b = v[: hd // 2], v[hd // 2 :]
        done.append(jnp.concatenate([a * cosine - b * sine, b * cosine + a * sine], axis=0))
    for h in range(nk):
        lo = (nq + nk + h) * hd
        done.append(turned[lo : lo + hd])
    parts = [[], []]
    for start, count in ((0, nq), (nq, nk), (nq + nk, nk)):
        for side in range(2):
            parts[side] += done[start + side * count // 2 : start + (side + 1) * count // 2]
    low = jnp.concatenate(parts[0], axis=0)
    high = jnp.concatenate(parts[1], axis=0)
    first = core == 0
    own_ref[...] = jnp.where(first, low, high).astype(BF16)
    oth_ref[...] = jnp.where(first, high, low).astype(BF16)


def heads(n1, seq, weight, cosine, sine, qgain, kgain, core, hd, nq, nk):
    span, width = n1.shape[1:]
    sides = (nq + 2 * nk) * hd // 2
    full = pl.BlockSpec(memory_space=pltpu.VMEM)
    whole = lambda a: pl.BlockSpec(a.shape, lambda i: (0,) * a.ndim)
    outs = [shape(((nq + nk) * hd, span), F32), shape((sides, span), BF16), shape((sides, span), BF16)]
    return pl.pallas_call(
        functools.partial(heads_kernel, hd, nq, nk),
        grid=(1,),
        in_specs=[pl.BlockSpec((1, span, width), lambda i: (seq, 0, 0))]
        + [whole(a) for a in (weight, cosine, sine, qgain, kgain)]
        + [SMEM],
        out_specs=[whole(o) for o in outs],
        out_shape=outs,
        compiler_params=PARAMS,
        cost_estimate=cost(2 * span * width * weight.shape[2], 2 * span * width + 2 * weight.size),
        name="query_key_value",
    )(n1, weight, cosine, sine, qgain, kgain, core)


def join_positions(core, own, oth):
    first = core == 0
    return jnp.where(first, own, oth), jnp.where(first, oth, own)


def attend_kernel(block, groups, scal_ref, own_ref, got_ref, all_ref, att_ref, inv_ref, ao_ref, ax_ref):
    span = own_ref.shape[1]
    hd = own_ref.shape[0] // (groups + 2)
    length, core = scal_ref[0], scal_ref[1]
    low, high = join_positions(core, own_ref[...], got_ref[...])
    all_ref[:, :span] = low
    all_ref[:, span:] = high
    scale = log2e / math.sqrt(hd)
    krow = lax.broadcasted_iota(jnp.int32, (block, groups * block), 0)
    qcol = lax.broadcasted_iota(jnp.int32, (block, groups * block), 1) % block
    base = groups * hd
    for i in range(2 * span // block):
        cut = slice(i * block, (i + 1) * block)
        q = jnp.concatenate([all_ref[g * hd : (g + 1) * hd, cut] for g in range(groups)], axis=1)
        acc = jnp.zeros((hd, groups * block), F32)
        total = jnp.zeros((1, groups * block), F32)
        for j in range(i + 1):
            kcut = slice(j * block, (j + 1) * block)
            s = dot_tn(all_ref[base : base + hd, kcut], q) * scale
            ok = (krow + j * block) < length
            if j == i:
                ok = ok & (krow <= qcol)
            e = jnp.where(ok, jnp.exp2(s), 0.0)
            total = total + jnp.sum(e, axis=0, keepdims=True)
            acc = acc + dot_nn(all_ref[base + hd : base + 2 * hd, kcut], e.astype(BF16))
        inv = 1.0 / total
        att = (acc * inv).astype(BF16)
        for g in range(groups):
            att_ref[g * hd : (g + 1) * hd, cut] = att[:, g * block : (g + 1) * block]
            inv_ref[g : g + 1, cut] = inv[:, g * block : (g + 1) * block]
    mine, theirs = join_positions(core, att_ref[:, :span], att_ref[:, span:])
    ao_ref[...] = mine
    ax_ref[...] = theirs


def attend(scalars, own, got, groups):
    rows, span = own.shape
    hd = rows // (groups + 2)
    block = min(256, span)
    full = pl.BlockSpec(memory_space=pltpu.VMEM)
    return pl.pallas_call(
        functools.partial(attend_kernel, block, groups),
        in_specs=[SMEM, full, full],
        out_specs=[full] * 5,
        out_shape=[
            shape((rows, 2 * span), BF16),
            shape((groups * hd, 2 * span), BF16),
            shape((groups, 2 * span), F32),
            shape((groups * hd, span), BF16),
            shape((groups * hd, span), BF16),
        ],
        compiler_params=PARAMS,
        cost_estimate=cost(60 * groups * hd * span * span, 12 * rows * span, 4 * groups * span * span),
        name="attend_forward",
    )(scalars, own, got)


def branch_kernel(own_ref, got_ref, w_ref, core_ref, att_ref, *outs):
    half = w_ref.shape[2]
    low, high = join_positions(core_ref[0], own_ref[...], got_ref[...])
    att = jnp.concatenate([low, high], axis=0)
    att_ref[...] = att
    rows = outs[0].shape[0]
    for k, out in enumerate(outs):
        part = att[:, k * rows : (k + 1) * rows]
        out[:, :half] = dot_tn(part, w_ref[0]).astype(BF16)
        out[:, half:] = dot_tn(part, w_ref[1]).astype(BF16)


def branch(own, got, weight, core, chunks):
    rows, span = own.shape
    width = 2 * weight.shape[2]
    full = pl.BlockSpec(memory_space=pltpu.VMEM)
    return pl.pallas_call(
        branch_kernel,
        in_specs=[full] * 3 + [SMEM],
        out_specs=[full] * (1 + chunks),
        out_shape=[shape((2 * rows, span), BF16)] + [shape((span // chunks, width), BF16)] * chunks,
        compiler_params=PARAMS,
        cost_estimate=cost(4 * rows * span * width, 4 * rows * width + 2 * span * width),
        name="attention_branch",
    )(own, got, weight, core)


def second_norm_kernel(terms, scal_ref, x_ref, gain_ref, *refs):
    term_refs, (hidden_ref, n2_ref, stat_ref) = refs[:terms], refs[terms:]
    rows = hidden_ref.shape[0]
    branch_sum = term_refs[0][...].astype(F32)
    for ref in term_refs[1:]:
        branch_sum = branch_sum + ref[...].astype(F32)
    resid = x_ref[0].astype(F32)
    hidden = resid + branch_sum
    hidden_ref[...] = hidden
    n2_ref[...] = (hidden * inverse_rms(hidden) * gain_ref[...]).astype(BF16)
    place = scal_ref[1] + lax.broadcasted_iota(jnp.int32, (rows, 1), 0)
    valid = (place < scal_ref[0]).astype(F32)
    first = jnp.sum(valid * resid * resid, keepdims=True)
    second = jnp.sum(valid * branch_sum * branch_sum, keepdims=True)
    line = lax.broadcasted_iota(jnp.int32, (8, 128), 0)
    stat_ref[...] = jnp.where(line == 0, first, second)


def second_norm(scalars, xr, seq, part, gain, terms):
    rows, width = terms[0].shape
    flat = pl.BlockSpec((rows, width), lambda i: (0, 0))
    return pl.pallas_call(
        functools.partial(second_norm_kernel, len(terms)),
        grid=(1,),
        in_specs=[SMEM, pl.BlockSpec((1, rows, width), lambda i: (seq, part, 0)), pl.BlockSpec((1, width), lambda i: (0, 0))]
        + [flat] * len(terms),
        out_specs=[flat, flat, pl.BlockSpec((8, 128), lambda i: (0, 0))],
        out_shape=[shape((rows, width), F32), shape((rows, width), BF16), shape((8, 128), F32)],
        compiler_params=PARAMS,
        cost_estimate=cost(20 * rows * width, (8 + 2 * len(terms)) * rows * width),
        name="second_norm",
    )(scalars, xr, gain, *terms)


def feed_kernel(n_ref, g_ref, wgo, wgx, wuo, wux, wdo, wdx, inner_ref, gg_ref, gu_ref, ffn_ref, gn_ref, facc, gacc):
    step = pl.program_id(0)
    half = wgo.shape[0]
    no, nx = n_ref[:, :half], n_ref[:, half:]
    gate = dot_nn(no, wgo[...]) + dot_nn(nx, wgx[...])
    up = dot_nn(no, wuo[...]) + dot_nn(nx, wux[...])
    gi = dot_nt(g_ref[0, :, :half], wdo[...]) + dot_nt(g_ref[0, :, half:], wdx[...])
    sig = jax.nn.sigmoid(gate)
    silu = gate * sig
    inner = (silu * up).astype(BF16)
    gg = (gi * up * sig * (1.0 + gate * (1.0 - sig))).astype(BF16)
    gu = (gi * silu).astype(BF16)
    inner_ref[...] = inner
    gg_ref[...] = gg
    gu_ref[...] = gu

    @pl.when(step == 0)
    def _():
        facc[...] = jnp.zeros_like(facc)
        gacc[...] = jnp.zeros_like(gacc)

    facc[:, :half] += dot_nn(inner, wdo[...])
    facc[:, half:] += dot_nn(inner, wdx[...])
    gacc[:, :half] += dot_nt(gg, wgo[...]) + dot_nt(gu, wuo[...])
    gacc[:, half:] += dot_nt(gg, wgx[...]) + dot_nt(gu, wux[...])

    @pl.when(step == pl.num_programs(0) - 1)
    def _():
        ffn_ref[...] = facc[...].astype(BF16)
        gn_ref[...] = gacc[...].astype(BF16)


def feed(n2, chunk, rows, gf, seq, part, gate, up, down):
    width = n2.shape[1]
    _, half, hidden = gate.shape
    hb = min(512, hidden)
    row = [pl.BlockSpec((None, half, hb), lambda h, side=side: (side, 0, h)) for side in range(2)]
    col = [pl.BlockSpec((None, hb, half), lambda h, side=side: (side, h, 0)) for side in range(2)]
    whole = pl.BlockSpec((rows, width), lambda h: (0, 0))
    tile = pl.BlockSpec((rows, hb), lambda h: (0, h))
    return pl.pallas_call(
        feed_kernel,
        grid=(hidden // hb,),
        in_specs=[pl.BlockSpec((rows, width), lambda h: (chunk, 0)), pl.BlockSpec((1, rows, width), lambda h: (seq, part, 0))] + row + row + col,
        out_specs=[tile, tile, tile, whole, whole],
        out_shape=[shape((rows, hidden), BF16)] * 3 + [shape((rows, width), BF16)] * 2,
        scratch_shapes=[pltpu.VMEM((rows, width), F32), pltpu.VMEM((rows, width), F32)],
        compiler_params=PARAMS,
        cost_estimate=cost(12 * rows * width * hidden, 12 * half * hidden + 14 * rows * width, rows * hidden),
        name="feed_forward",
    )(n2, gf, gate, gate, up, up, down, down)


def second_back_kernel(terms, hidden_ref, gf_ref, gain_ref, *refs):
    term_refs, (gb_ref, gh_ref, gain_out) = refs[:terms], refs[terms:]
    e = term_refs[0][...].astype(F32)
    for ref in term_refs[1:]:
        e = e + ref[...].astype(F32)
    hidden = hidden_ref[...]
    inv = inverse_rms(hidden)
    hat = hidden * inv
    eg = e * gain_ref[...]
    gh = gf_ref[0].astype(F32) + inv * (eg - hat * jnp.mean(eg * hat, axis=-1, keepdims=True))
    gh_ref[...] = gh
    gb_ref[...] = gh.astype(BF16)
    gain_out[...] = jnp.sum(e * hat, axis=0, keepdims=True)


def second_back(hidden, chunk, gf, seq, part, gain, terms):
    rows, width = terms[0].shape
    flat = pl.BlockSpec((rows, width), lambda i: (0, 0))
    line = pl.BlockSpec((1, width), lambda i: (0, 0))
    return pl.pallas_call(
        functools.partial(second_back_kernel, len(terms)),
        grid=(1,),
        in_specs=[pl.BlockSpec((rows, width), lambda i: (chunk, 0)), pl.BlockSpec((1, rows, width), lambda i: (seq, part, 0)), line]
        + [flat] * len(terms),
        out_specs=[flat, flat, line],
        out_shape=[shape((rows, width), BF16), shape((rows, width), F32), shape((1, width), F32)],
        compiler_params=PARAMS,
        cost_estimate=cost(20 * rows * width, (12 + 2 * len(terms)) * rows * width),
        name="second_norm_back",
    )(hidden, gf, gain, *terms)


def branch_back_kernel(chunks, *refs):
    gb_refs, (w_ref, core_ref, own_ref, oth_ref) = refs[:chunks], refs[chunks:]
    half = w_ref.shape[2]
    rows = gb_refs[0].shape[0]
    heads_half = own_ref.shape[0]
    first = core_ref[0] == 0
    for k, ref in enumerate(gb_refs):
        da = dot_nt(w_ref[0], ref[:, :half]) + dot_nt(w_ref[1], ref[:, half:])
        da = da.astype(BF16)
        low, high = da[:heads_half], da[heads_half:]
        cut = slice(k * rows, (k + 1) * rows)
        own_ref[:, cut] = jnp.where(first, low, high)
        oth_ref[:, cut] = jnp.where(first, high, low)


def branch_back(gbs, weight, core):
    chunks = len(gbs)
    rows, width = gbs[0].shape
    dim = weight.shape[1]
    full = pl.BlockSpec(memory_space=pltpu.VMEM)
    return pl.pallas_call(
        functools.partial(branch_back_kernel, chunks),
        in_specs=[full] * (chunks + 1) + [SMEM],
        out_specs=[full] * 2,
        out_shape=[shape((dim // 2, chunks * rows), BF16)] * 2,
        compiler_params=PARAMS,
        cost_estimate=cost(2 * dim * chunks * rows * width, 2 * dim * width + 2 * chunks * rows * width),
        name="attention_branch_back",
    )(*gbs, weight, core)


def attend_back_kernel(block, groups, scal_ref, all_ref, att_ref, inv_ref, own_ref, got_ref, out_own, out_oth, da_all, grads):
    span = own_ref.shape[1]
    hd = all_ref.shape[0] // (groups + 2)
    length, core = scal_ref[0], scal_ref[1]
    low, high = join_positions(core, own_ref[...], got_ref[...])
    da_all[:, :span] = low
    da_all[:, span:] = high
    scale = log2e / math.sqrt(hd)
    back = 1.0 / math.sqrt(hd)
    krow = lax.broadcasted_iota(jnp.int32, (block, groups * block), 0)
    qcol = lax.broadcasted_iota(jnp.int32, (block, groups * block), 1) % block
    base = groups * hd
    grads[base:, :] = jnp.zeros((2 * hd, 2 * span), F32)
    for i in range(2 * span // block):
        cut = slice(i * block, (i + 1) * block)

        def rows(ref):
            return jnp.concatenate([ref[g * hd : (g + 1) * hd, cut] for g in range(groups)], axis=1)

        q = rows(all_ref)
        da = rows(da_all)
        inv = jnp.concatenate([inv_ref[g : g + 1, cut] for g in range(groups)], axis=1)
        delta = jnp.sum(rows(att_ref).astype(F32) * da.astype(F32), axis=0, keepdims=True)
        dq = jnp.zeros((hd, groups * block), F32)
        for j in range(i + 1):
            kcut = slice(j * block, (j + 1) * block)
            key = all_ref[base : base + hd, kcut]
            s = dot_tn(key, q) * scale
            ok = (krow + j * block) < length
            if j == i:
                ok = ok & (krow <= qcol)
            p = jnp.where(ok, jnp.exp2(s) * inv, 0.0)
            dp = dot_tn(all_ref[base + hd : base + 2 * hd, kcut], da)
            ds = (p * (dp - delta)).astype(BF16)
            dq = dq + dot_nn(key, ds)
            grads[base : base + hd, kcut] += dot_nt(q, ds) * back
            grads[base + hd : base + 2 * hd, kcut] += dot_nt(da, p.astype(BF16))
        dq = dq * back
        for g in range(groups):
            grads[g * hd : (g + 1) * hd, cut] = dq[:, g * block : (g + 1) * block]
    mine, theirs = join_positions(core, grads[:, :span], grads[:, span:])
    out_own[...] = mine.astype(BF16)
    out_oth[...] = theirs.astype(BF16)


def attend_back(scalars, everything, att, inv, own, got, groups):
    rows, slots = everything.shape
    span = slots // 2
    block = min(256, span)
    full = pl.BlockSpec(memory_space=pltpu.VMEM)
    return pl.pallas_call(
        functools.partial(attend_back_kernel, block, groups),
        in_specs=[SMEM] + [full] * 5,
        out_specs=[full] * 2,
        out_shape=[shape((rows, span), BF16)] * 2,
        scratch_shapes=[pltpu.VMEM(att.shape, BF16), pltpu.VMEM((rows, slots), F32)],
        compiler_params=PARAMS,
        cost_estimate=cost(30 * att.shape[0] * slots * slots, 12 * rows * slots, groups * slots * slots),
        name="attend_backward",
    )(scalars, everything, att, inv, own, got)


def heads_back_kernel(hd, nq, nk, own_ref, got_ref, pre_ref, cos_ref, sin_ref, qg_ref, kg_ref, x_ref, w_ref, core_ref, dpre_ref, first_ref, gain_ref, hgain_ref):
    half = w_ref.shape[1]
    low, high = join_positions(core_ref[0], own_ref[...].astype(F32), got_ref[...].astype(F32))
    sides = (nq // 2, nk // 2, nk // 2)
    grads = [[], [], []]
    for side in (low, high):
        at = 0
        for kind, count in enumerate(sides):
            for h in range(count):
                grads[kind].append(side[at : at + hd])
                at += hd
    cosine, sine = cos_ref[...], sin_ref[...]
    done = []
    sums = [0.0, 0.0]
    for h in range(nq + nk):
        kind = 0 if h < nq else 1
        g = grads[kind][h - kind * nq]
        a, b = g[: hd // 2], g[hd // 2 :]
        g = jnp.concatenate([a * cosine + b * sine, b * cosine - a * sine], axis=0)
        v = pre_ref[h * hd : (h + 1) * hd, :]
        inv = lax.rsqrt(jnp.mean(v * v, axis=0, keepdims=True) + epsilon)
        hat = v * inv
        sums[kind] = sums[kind] + jnp.sum(g * hat, axis=1, keepdims=True)
        gg = g * (qg_ref[...] if kind == 0 else kg_ref[...])
        done.append(inv * (gg - hat * jnp.mean(gg * hat, axis=0, keepdims=True)))
    done += grads[2]
    hgain_ref[:hd, :] = jnp.broadcast_to(sums[0], (hd, 128))
    hgain_ref[hd:, :] = jnp.broadcast_to(sums[1], (hd, 128))
    dpre = jnp.concatenate(done, axis=0).T.astype(BF16)
    dpre_ref[...] = dpre
    x = x_ref[0].astype(F32)
    hat = x * inverse_rms(x)
    for k in range(2):
        cut = slice(k * half, (k + 1) * half)
        part = dot_nt(dpre, w_ref[k])
        first_ref[:, cut] = part.astype(BF16)
        gain_ref[:, cut] = jnp.sum(part * hat[:, cut], axis=0, keepdims=True)


def heads_back(own, got, pre, cosine, sine, qgain, kgain, xr, seq, weight, core, hd, nq, nk):
    span = own.shape[1]
    _, half, cols = weight.shape
    width = 2 * half
    whole = lambda a: pl.BlockSpec(a.shape, lambda i: (0,) * len(a.shape))
    outs = [shape((span, cols), BF16), shape((span, width), BF16), shape((1, width), F32), shape((2 * hd, 128), F32)]
    return pl.pallas_call(
        functools.partial(heads_back_kernel, hd, nq, nk),
        grid=(1,),
        in_specs=[whole(a) for a in (own, got, pre, cosine, sine, qgain, kgain)]
        + [pl.BlockSpec((1, span, width), lambda i: (seq, 0, 0)), whole(weight), SMEM],
        out_specs=[whole(o) for o in outs],
        out_shape=outs,
        compiler_params=PARAMS,
        cost_estimate=cost(2 * span * width * cols, 4 * span * width + 4 * half * cols),
        name="query_key_value_back",
    )(own, got, pre, cosine, sine, qgain, kgain, xr, weight, core)


def place_blocks(order, ids, first_id, value, out_ref):
    piece = value.shape[-1] // order
    for k in range(order):
        if order == 1:
            out_ref[...] = value
        else:
            dst = pl.ds(pl.multiple_of(ids[first_id + k] * piece, piece), piece)
            out_ref[:, dst] = value[:, k * piece : (k + 1) * piece]


def output_kernel(order, scal_ref, got_ref, f0_ref, f1_ref, h0_ref, h1_ref, out_ref, stat_ref):
    low = scal_ref[0] * 2 < scal_ref[3]
    rows = out_ref.shape[0]
    ffn = got_ref[...].astype(F32) + jnp.where(low, f0_ref[...], f1_ref[...]).astype(F32)
    hidden = jnp.where(low, h0_ref[...], h1_ref[...])
    place = scal_ref[2] + lax.broadcasted_iota(jnp.int32, (rows, 1), 0)
    valid = (place < scal_ref[1]).astype(F32)
    stat_ref[...] = jnp.broadcast_to(jnp.sum(valid * ffn * ffn, keepdims=True), (8, 128))
    place_blocks(order, scal_ref, 4, (hidden + ffn).astype(BF16), out_ref)


def share_specs(rows, width, per):
    return [
        pl.BlockSpec((rows, width), lambda i, s: (jnp.minimum(s[0], per - 1), 0)),
        pl.BlockSpec((rows, width), lambda i, s: (jnp.maximum(s[0] - per, 0), 0)),
    ]


def output_share(scalars, got, ffns, hiddens, order):
    rows, width = got.shape
    pair = share_specs(rows, width, ffns[0].shape[0] // rows)
    flat = pl.BlockSpec((rows, width), lambda i, s: (0, 0))
    return pl.pallas_call(
        functools.partial(output_kernel, order),
        grid_spec=pltpu.PrefetchScalarGridSpec(
            num_scalar_prefetch=1,
            grid=(1,),
            in_specs=[flat] + pair + pair,
            out_specs=[flat, pl.BlockSpec((8, 128), lambda i, s: (0, 0))],
        ),
        out_shape=[shape((rows, width), BF16), shape((8, 128), F32)],
        compiler_params=PARAMS,
        cost_estimate=cost(6 * rows * width, 16 * rows * width),
        name="output_share",
    )(scalars, got, *ffns, *hiddens)


def input_kernel(order, scal_ref, got_ref, part_ref, g0_ref, g1_ref, x_ref, gain_ref, out_ref):
    low = scal_ref[0] * 2 < scal_ref[3]
    e = got_ref[...].astype(F32) + part_ref[...].astype(F32)
    gh = jnp.where(low, g0_ref[...], g1_ref[...])
    x = x_ref[0].astype(F32)
    inv = inverse_rms(x)
    hat = x * inv
    eg = e * gain_ref[...]
    value = gh + inv * (eg - hat * jnp.mean(eg * hat, axis=-1, keepdims=True))
    place_blocks(order, scal_ref, 4, value, out_ref)


def input_share(scalars, got, part, ghs, xr, seq, gain, order):
    rows, width = got.shape
    pair = share_specs(rows, width, ghs[0].shape[0] // rows)
    flat = pl.BlockSpec((rows, width), lambda i, s: (0, 0))
    return pl.pallas_call(
        functools.partial(input_kernel, order),
        grid_spec=pltpu.PrefetchScalarGridSpec(
            num_scalar_prefetch=1,
            grid=(1,),
            in_specs=[flat, pl.BlockSpec((rows, width), lambda i, s: (s[0], 0))]
            + pair
            + [pl.BlockSpec((1, rows, width), lambda i, s: (seq, s[0], 0)), pl.BlockSpec((1, width), lambda i, s: (0, 0))],
            out_specs=flat,
        ),
        out_shape=shape((rows, width), F32),
        compiler_params=PARAMS,
        cost_estimate=cost(12 * rows * width, 20 * rows * width),
        name="input_share",
    )(scalars, got, part, *ghs, xr, gain)


def weight_grad_kernel(count, extra, *refs):
    a_refs, b_refs, out = refs[:count], refs[count : 2 * count], refs[-1]
    total = dot_tn(a_refs[0][...], b_refs[0][...])
    for a, b in zip(a_refs[1:], b_refs[1:]):
        total = total + dot_tn(a[...], b[...])
    if extra:
        total = total + refs[2 * count][...].astype(F32)
    out[...] = total.astype(BF16)


def weight_grad(lefts, rights, side, axis, add=None):
    count = len(lefts)
    rows_all, cols_all = lefts[0].shape[1], rights[0].shape[1]
    dims = [rows_all, cols_all]
    dims[axis] //= 2
    rows, cols = min(512, dims[0]), min(2048, dims[1])
    row_at = side * (dims[0] // rows) if axis == 0 else 0
    col_at = side * (dims[1] // cols) if axis == 1 else 0
    specs = [pl.BlockSpec((a.shape[0], rows), lambda j, i: (0, i + row_at)) for a in lefts]
    specs += [pl.BlockSpec((b.shape[0], cols), lambda j, i: (0, j + col_at)) for b in rights]
    tile = pl.BlockSpec((rows, cols), lambda j, i: (i, j))
    tokens = sum(a.shape[0] for a in lefts)
    return pl.pallas_call(
        functools.partial(weight_grad_kernel, count, add is not None),
        grid=(dims[1] // cols, dims[0] // rows),
        in_specs=specs + ([tile] if add is not None else []),
        out_specs=tile,
        out_shape=shape(dims, BF16),
        compiler_params=PARAMS,
        cost_estimate=cost(2 * tokens * dims[0] * dims[1], 2 * tokens * sum(dims) + 2 * dims[0] * dims[1]),
        name="weight_grad",
    )(*lefts, *rights, *([add] if add is not None else []))


def xor_one(index):
    return index + 1 - 2 * (index % 2)


def remote(src, dst, send, recv, device):
    return pltpu.make_async_remote_copy(
        src_ref=src, dst_ref=dst, send_sem=send, recv_sem=recv, device_id=device, device_id_type=pl.DeviceIdType.MESH
    )


def greet(others):
    barrier = pltpu.get_barrier_semaphore()
    count = 0
    for needed, device in others:
        if needed is None:
            pl.semaphore_signal(barrier, inc=1, device_id=device, device_id_type=pl.DeviceIdType.MESH)
            count = count + 1
        else:

            @pl.when(needed)
            def _():
                pl.semaphore_signal(barrier, inc=1, device_id=device, device_id_type=pl.DeviceIdType.MESH)

            count = count + jnp.where(needed, 1, 0)
    pl.semaphore_wait(barrier, count)


class Gather:
    def __init__(self, shard, dst, axis, send, recv, local, near_x, near_y, near_core):
        piece = shard.shape[axis]
        half = shard.shape[0] // 2

        def block(side, k):
            cut = pl.ds(k * piece, piece)
            return dst.at[side, cut, :] if axis == 0 else dst.at[side, :, cut]

        def part(k, h):
            if axis == 0:
                return dst.at[0, pl.ds(k * piece + h * half, half), :]
            return dst.at[0, pl.ds(h * half, half), pl.ds(k * piece, piece)]

        link, cross = send.at[0], send.at[1]
        self.local = pltpu.make_async_copy(shard, block(0, 0), local)
        self.x = remote(shard, block(0, 1), link, recv.at[0], near_x)
        self.y = remote(shard, block(0, 2), link, recv.at[1], near_y)
        self.dx = remote(part(2, 0), part(3, 0), link, recv.at[2], near_x)
        self.dy = remote(part(1, 1), part(3, 1), link, recv.at[2], near_y)
        self.cores = [remote(shard if k == 0 else block(0, k), block(1, k), cross, recv.at[3], near_core) for k in range(4)]
        cut = pl.ds(0, 3 * piece)
        three = dst.at[0, cut, :] if axis == 0 else dst.at[0, :, cut]
        self.all_links = remote(three, three, link, recv.at[0], near_x)
        self.diagonal = remote(block(0, 3), block(0, 3), link, recv.at[2], near_x)
        self.all_cores = remote(dst.at[0], dst.at[1], cross, recv.at[3], near_core)

    def first(self):
        self.x.start()
        self.y.start()
        self.cores[0].start()
        self.local.start()

    def second(self):
        self.y.wait_recv()
        self.dx.start()
        self.cores[2].start()
        self.x.wait_recv()
        self.dy.start()
        self.cores[1].start()

    def third(self):
        self.diagonal.wait_recv()
        self.cores[3].start()

    def arrived(self):
        self.local.wait()
        self.all_cores.wait_recv()

    def sent(self):
        self.all_links.wait_send()
        self.all_cores.wait_send()


def forward_kernel(
    hd, nq, nk, block, sub,
    len_ref, x_hbm, cot_hbm, wq_hbm, wk_hbm, wv_hbm, wout, wgate, wup, wdown, again_ref, fgain_ref, qgain_ref, kgain_ref,
    xr_hbm, n1_hbm, gf_hbm, qkv_hbm, out_hbm, gate_hbm, up_hbm, down_hbm, hidden_hbm, n2_hbm, rest_hbm, resta_hbm, gi_hbm, pre_hbm, all_hbm, att_hbm, tok_hbm,
    gains_ref, table_ref, inv_ref, stat_ref,
    xr_v, cot_v, n1_v, qkv_v, out_v, ex_own, ex_send, ex_got, at_own, at_send, at_got,
    part_v, in_v, back_v, hid_v, norm_v, wqkv, gain_ref, down_v, gi_v, pre_ref, all_ref, att_ref, tok_ref,
    keep_sem, load_sem, store_sem, shard_sem, rest_sem, down_sem, gi_sem, wsend, wrecv, wloc, gsend, grecv, exsend, exrecv, zsend, zrecv, hid_sem,
):
    seqs, span, width = xr_v.shape
    groups = nq // nk
    row, core, rank = lax.axis_index("dp"), lax.axis_index("context"), lax.axis_index("tensor")
    start = core * span
    near = [row, xor_one(row), (row + 2) % 4, 3 - row]
    inner = (rank % 3) != 0
    near_x, near_y, near_core = {"dp": near[1]}, {"dp": near[2]}, {"context": 1 - core}
    z_side, z_mid = {"tensor": xor_one(rank)}, {"tensor": 3 - rank}
    piece = width // 8
    total_subs = part_v.shape[0]
    per = span // sub
    first_core = core == 0

    loads = []
    for at, (src, dst) in enumerate(((x_hbm, xr_v), (cot_hbm, cot_v))):
        for s in range(seqs):
            for o in range(2):
                for k in range(4):
                    b = near[k] * 2 + (core if o == 0 else 1 - core)
                    cut = pl.ds(pl.multiple_of(b * piece, piece), piece)
                    loads.append(
                        pltpu.make_async_copy(
                            src.at[s, :, cut], dst.at[s, :, pl.ds((o * 4 + k) * piece, piece)], load_sem.at[at]
                        )
                    )
    shards, at = [], 0
    for k, ref in enumerate((wq_hbm, wk_hbm, wv_hbm)):
        shards.append(pltpu.make_async_copy(ref, wqkv.at[:, pl.ds(at, ref.shape[1])], shard_sem.at[k]))
        at += ref.shape[1]
    for copy in shards + loads:
        copy.start()
    piece = width // 8
    wide_gains = [ref[...].astype(F32).reshape(1, piece) for ref in (again_ref, fgain_ref)]
    gain_ref[...] = jnp.concatenate(wide_gains + [jnp.zeros((14, piece), F32)], axis=0).astype(BF16)

    others = []
    for o in range(2):
        for k in range(4):
            if o or k:
                others.append((o * 4 + k, {"dp": near[k], "context": core if o == 0 else 1 - core}))
    greet([(None, d) for _, d in others] + [(None, z_side), (inner, z_mid)])

    gains = [remote(gain_ref, gains_ref.at[b], gsend, grecv, d) for b, d in others]
    every_gain = remote(gains_ref.at[pl.ds(1, 7)], gains_ref.at[pl.ds(1, 7)], gsend, grecv, near_core)
    for copy in gains:
        copy.start()
    weights = [
        Gather(shard, dst, axis, wsend.at[i], wrecv.at[i], wloc.at[i], near_x, near_y, near_core)
        for i, (shard, dst, axis) in enumerate(
            ((wqkv, qkv_v, 0), (wout, out_v, 1), (wgate, gate_hbm, 0), (wup, up_hbm, 0), (wdown, down_hbm, 1))
        )
    ]
    w_qkv, w_out, w_gate, w_up, w_down = weights
    for copy in shards:
        copy.wait()
    w_qkv.first()
    w_out.first()
    gains_ref[0] = gain_ref[...]

    quarter = hd // 2
    freqs = jnp.exp(lax.broadcasted_iota(jnp.int32, (quarter, span), 0).astype(F32) * (-2.0 * math.log(rope_base) / hd))
    angles = freqs * (start + lax.broadcasted_iota(jnp.int32, (quarter, span), 1)).astype(F32)
    cosine, sine = jnp.cos(angles), jnp.sin(angles)
    turned = [jnp.broadcast_to(ref[...].astype(F32).reshape(1, hd), (8, hd)).T for ref in (qgain_ref, kgain_ref)]
    qgain, kgain = turned[0][:, 0:1], turned[1][:, 0:1]
    table_ref[:quarter, :] = cosine
    table_ref[quarter : 2 * quarter, :] = sine
    table_ref[2 * quarter : 2 * quarter + hd, :128] = jnp.broadcast_to(qgain, (hd, 128))
    table_ref[2 * quarter + hd :, :128] = jnp.broadcast_to(kgain, (hd, 128))

    pltpu.make_async_copy(cot_hbm, cot_v, load_sem.at[1]).wait()

    def mask_rows(i, carry):
        s, t = i // (span // 16), i % (span // 16)
        cut = pl.ds(pl.multiple_of(t * 16, 16), 16)
        place = start + t * 16 + lax.broadcasted_iota(jnp.int32, (16, 1), 0)
        valid = (place < len_ref[s]).astype(F32)
        cot_v[s, cut, :] = (cot_v[s, cut, :].astype(F32) * valid).astype(BF16)
        return carry

    lax.fori_loop(0, seqs * span // 16, mask_rows, 0)
    store_gf = pltpu.make_async_copy(cot_v, gf_hbm, store_sem.at[0])
    store_gf.start()
    pltpu.make_async_copy(x_hbm, xr_v, load_sem.at[0]).wait()
    store_xr = pltpu.make_async_copy(xr_v, xr_hbm, store_sem.at[1])
    store_xr.start()
    every_gain.wait_recv()
    gain1 = jnp.concatenate([gains_ref[b, 0:1, :] for b in range(8)], axis=1).astype(F32)
    gain2 = jnp.concatenate([gains_ref[b, 1:2, :] for b in range(8)], axis=1).astype(F32)

    def norm_rows(i, carry):
        s, t = i // (span // 16), i % (span // 16)
        cut = pl.ds(pl.multiple_of(t * 16, 16), 16)
        x = xr_v[s, cut, :].astype(F32)
        n1_v[s, cut, :] = (x * inverse_rms(x) * gain1).astype(BF16)
        return carry

    lax.fori_loop(0, span // 16, norm_rows, 0)
    w_qkv.second()
    lax.fori_loop(span // 16, seqs * span // 16, norm_rows, 0)
    store_n1 = pltpu.make_async_copy(n1_v, n1_hbm, store_sem.at[2])
    store_n1.start()
    w_out.second()
    w_down.first()
    w_gate.first()
    w_qkv.third()
    w_qkv.arrived()

    half = width // 2

    def exchange(s):
        return remote(ex_send.at[s], ex_got.at[s], exsend.at[0, s], exrecv.at[0, s], near_core)

    def keep(k, s):
        ref, dst = ((pre_ref, pre_hbm), (all_ref, all_hbm), (att_ref, att_hbm), (tok_ref, tok_hbm))[k]
        return pltpu.make_async_copy(ref.at[s], dst.at[s], keep_sem.at[k, s])

    def project(s):
        x = n1_v[s]
        flat = dot_nn(x[:, :half], qkv_v[0]) + dot_nn(x[:, half:], qkv_v[1])
        turned = flat.T
        pre_ref[s] = turned[: (nq + nk) * hd]
        done = []
        for h in range(nq + nk):
            v = turned[h * hd : (h + 1) * hd]
            inv = lax.rsqrt(jnp.mean(v * v, axis=0, keepdims=True) + epsilon)
            v = v * inv * (qgain if h < nq else kgain)
            a, b = v[: hd // 2], v[hd // 2 :]
            done.append(jnp.concatenate([a * cosine - b * sine, b * cosine + a * sine], axis=0))
        for h in range(nk):
            lo = (nq + nk + h) * hd
            done.append(turned[lo : lo + hd])
        parts = [[], []]
        for begin_at, count in ((0, nq), (nq, nk), (nq + nk, nk)):
            for side in range(2):
                parts[side] += done[begin_at + side * count // 2 : begin_at + (side + 1) * count // 2]
        low = jnp.concatenate(parts[0], axis=0)
        high = jnp.concatenate(parts[1], axis=0)
        ex_own[s] = jnp.where(first_core, low, high).astype(BF16)
        ex_send[s] = jnp.where(first_core, high, low).astype(BF16)
        exchange(s).start()
        keep(0, s).start()

    store_qkv = pltpu.make_async_copy(qkv_v, qkv_hbm, store_sem.at[3])
    store_qkv.start()
    store_out = pltpu.make_async_copy(out_v, out_hbm, store_sem.at[4])

    scale = log2e / math.sqrt(hd)
    krow = lax.broadcasted_iota(jnp.int32, (block, groups * block), 0)
    qcol = lax.broadcasted_iota(jnp.int32, (block, groups * block), 1) % block
    base = groups * hd

    def give(s):
        return remote(at_send.at[s], at_got.at[s], exsend.at[1, s], exrecv.at[1, s], near_core)

    def attention(s):
        exchange(s).wait_recv()
        low, high = join_positions(core, ex_own[s], ex_got[s])
        all_ref[s, :, :span] = low
        all_ref[s, :, span:] = high
        length = len_ref[s]
        for i in range(2 * span // block):
            cut = slice(i * block, (i + 1) * block)
            q = jnp.concatenate([all_ref[s, g * hd : (g + 1) * hd, cut] for g in range(groups)], axis=1)
            acc = jnp.zeros((hd, groups * block), F32)
            total = jnp.zeros((1, groups * block), F32)
            for j in range(i + 1):
                kcut = slice(j * block, (j + 1) * block)
                score = dot_tn(all_ref[s, base : base + hd, kcut], q) * scale
                ok = (krow + j * block) < length
                if j == i:
                    ok = ok & (krow <= qcol)
                e = jnp.where(ok, jnp.exp2(score), 0.0)
                total = total + jnp.sum(e, axis=0, keepdims=True)
                acc = acc + dot_nn(all_ref[s, base + hd : base + 2 * hd, kcut], e.astype(BF16))
            inv = 1.0 / total
            att = (acc * inv).astype(BF16)
            for g in range(groups):
                att_ref[s, g * hd : (g + 1) * hd, cut] = att[:, g * block : (g + 1) * block]
                inv_ref[s, g : g + 1, cut] = inv[:, g * block : (g + 1) * block]
        mine, theirs = join_positions(core, att_ref[s, :, :span], att_ref[s, :, span:])
        at_own[s] = mine
        at_send[s] = theirs
        give(s).start()
        keep(1, s).start()
        keep(2, s).start()

    moving = Chain(rank, part_v, in_v, back_v, zsend, zrecv)
    subs = moving.count

    def branch_rows(s):
        give(s).wait_recv()
        low, high = join_positions(core, at_own[s], at_got[s])
        att = jnp.concatenate([low, high], axis=0).T
        tok_ref[s] = att
        keep(3, s).start()
        many = 2
        for k in range(0, per, many):
            rows = att[k * sub : (k + many) * sub]
            for side in range(2):
                part = dot_nn(rows, out_v[side]).astype(BF16)
                for m in range(many):
                    part_v[s * per + k + m, :, side * half : (side + 1) * half] = part[m * sub : (m + 1) * sub]
            for m in range(many):
                u = s * per + k + m

                moving.begin(u)

    def sequence(s, carry):
        project(s)

        attention(s)

        @pl.when(s == 0)
        def _():
            w_out.third()
            w_out.arrived()
            store_out.start()

        branch_rows(s)
        return carry

    lax.fori_loop(0, seqs, sequence, 0)
    tail = pl.ds(subs, total_subs - subs)
    rest = [pltpu.make_async_copy(part_v.at[tail], rest_hbm, rest_sem.at[0])]
    rest[0].start()
    stat_ref[...] = jnp.zeros_like(stat_ref)

    def hidden_store(u):
        cut = pl.ds(pl.multiple_of(u * sub, sub), sub)
        return (
            pltpu.make_async_copy(hid_v.at[u % 2], hidden_hbm.at[cut, :], hid_sem.at[0, u % 2]),
            pltpu.make_async_copy(norm_v.at[u % 2], n2_hbm.at[cut, :], hid_sem.at[1, u % 2]),
        )

    def finish(u):
        s, t = u // per, u % per
        cut = pl.ds(pl.multiple_of(t * sub, sub), sub)

        moving.ready(u)

        @pl.when(u >= 2)
        def _():
            for copy in hidden_store(u - 2):
                copy.wait()

        length = len_ref[s]

        def body(piece_rows, first):
            total = moving.total(u, piece_rows)
            resid = xr_v[s, pl.ds(pl.multiple_of(t * sub + first, 16), 16), :].astype(F32)
            hidden = resid + total
            hid_v[u % 2, piece_rows, :] = hidden
            norm_v[u % 2, piece_rows, :] = (hidden * inverse_rms(hidden) * gain2).astype(BF16)
            place = start + t * sub + first + lax.broadcasted_iota(jnp.int32, (16, 1), 0)
            valid = (place < length).astype(F32)
            stat_ref[0] += fold_lanes(valid * resid * resid)
            stat_ref[1] += fold_lanes(valid * total * total)

        by_pieces(sub, body)
        for copy in hidden_store(u):
            copy.start()

    hb = down_v.shape[2]
    blocks = down_hbm.shape[1] // hb

    def load_down(h):
        cut = pl.ds(pl.multiple_of(h * hb, hb), hb)
        return [pltpu.make_async_copy(down_hbm.at[side, cut, :], down_v.at[h % 2, side], down_sem.at[h % 2, side]) for side in range(2)]

    def store_gi(h):
        cut = pl.ds(pl.multiple_of(h * hb, hb), hb)
        return pltpu.make_async_copy(gi_v.at[h % 2], gi_hbm.at[:, cut], gi_sem.at[h % 2])

    def grad_inner(h):
        for copy in load_down(h):
            copy.wait()

        @pl.when(h + 1 < blocks)
        def _():
            for copy in load_down(h + 1):
                copy.start()

        @pl.when(h >= 2)
        def _():
            store_gi(h - 2).wait()

        for s in range(seqs):
            for q in range(span // 256):
                cut = slice(q * 256, (q + 1) * 256)
                g = dot_nt(cot_v[s, cut, :half], down_v[h % 2, 0]) + dot_nt(cot_v[s, cut, half:], down_v[h % 2, 1])
                gi_v[h % 2, s * span + q * 256 : s * span + (q + 1) * 256, :] = g.astype(BF16)
        store_gi(h).start()

    def chain(i, carry):
        moving.middle(i)
        moving.outward(i - 1)

        @pl.when(i == 1)
        def _():
            w_down.second()
            w_up.first()

        @pl.when(i == 6)
        def _():
            w_gate.second()

        @pl.when(i == 7)
        def _():
            w_down.third()

        @pl.when(i == 8)
        def _():
            w_down.arrived()
            for copy in load_down(0):
                copy.start()

        @pl.when(i == 10)
        def _():
            w_up.second()

        @pl.when(i >= 2)
        def _():
            finish(i - 2)

        @pl.when((i >= 9) & (i < 9 + blocks))
        def _():
            grad_inner(i - 9)

        return carry

    lax.fori_loop(0, subs + 2, chain, 0)
    w_gate.third()
    came = pltpu.make_async_copy(in_v.at[tail], resta_hbm, rest_sem.at[1])

    @pl.when(inner)
    def _():
        for u in range(subs, total_subs):
            moving.hop_in(u).wait_recv()
        came.start()

    w_up.third()
    for u in (subs - 2, subs - 1):
        for copy in hidden_store(u):
            copy.wait()
    for h in (blocks - 2, blocks - 1):
        store_gi(h).wait()
    moving.settle()
    for s in range(seqs):
        exchange(s).wait_send()
        give(s).wait_send()
        for k in range(4):
            keep(k, s).wait()
    every_gain.wait_send()
    w_gate.arrived()
    w_up.arrived()
    pl.when(inner)(came.wait)
    for w in weights:
        w.sent()
    for copy in [store_gf, store_xr, store_n1, store_qkv, store_out] + rest:
        copy.wait()


def forward(lengths, x, cot, w_query, w_key, w_value, w_out, w_gate, w_up, w_down, all_gains, hd, nq, nk):
    seqs, span, width = x.shape
    half = width // 2
    groups = nq // nk
    sub = span // 8
    subs = seqs * span // sub
    here = subs - 4
    block = min(256, span)
    hidden = w_gate.shape[1]
    hb = hidden // 4
    cols = w_query.shape[1] + w_key.shape[1] + w_value.shape[1]
    rows = cols // 2
    any_space = pl.BlockSpec(memory_space=pl.ANY)
    vmem = pl.BlockSpec(memory_space=pltpu.VMEM)
    wide = (seqs, span, width)
    large = [
        shape(wide, BF16), shape(wide, BF16), shape(wide, BF16),
        shape((2, half, cols), BF16), shape((2, w_out.shape[0], half), BF16),
        shape((2, half, hidden), BF16), shape((2, half, hidden), BF16), shape((2, hidden, half), BF16),
        shape((seqs * span, width), F32), shape((seqs * span, width), BF16), shape((subs - here, sub, width), BF16),
        shape((subs - here, sub, width), BF16), shape((seqs * span, hidden), BF16),
    ]
    kept = [
        shape((seqs, (nq + nk) * hd, span), F32), shape((seqs, rows, 2 * span), BF16),
        shape((seqs, groups * hd, 2 * span), BF16), shape((seqs, span, nq * hd), BF16),
    ]
    large += kept
    small = [
        shape((8, 16, width // 8), BF16), shape((3 * hd, span), F32), shape((seqs, groups, 2 * span), F32), shape((2, 8, 128), F32),
    ]
    dma = pltpu.SemaphoreType.DMA
    ex = pltpu.VMEM((seqs, rows, span), BF16)
    at = pltpu.VMEM((seqs, groups * hd, span), BF16)
    moving = pltpu.VMEM((subs, sub, width), BF16)
    landing = pltpu.VMEM((here, sub, width), BF16)
    arriving = pltpu.VMEM((subs, sub, width), BF16)
    flops = 2 * seqs * span * width * (cols + nq * hd) + 16 * seqs * nq * hd * span * span
    return pl.pallas_call(
        functools.partial(forward_kernel, hd, nq, nk, block, sub),
        in_specs=[SMEM] + [any_space] * 9 + [vmem] * 4,
        out_specs=[any_space] * len(large) + [vmem] * len(small),
        out_shape=large + small,
        scratch_shapes=[
            pltpu.VMEM(wide, BF16), pltpu.VMEM(wide, BF16), pltpu.VMEM(wide, BF16),
            pltpu.VMEM((2, half, cols), BF16), pltpu.VMEM((2, w_out.shape[0], half), BF16),
            ex, ex, ex, at, at, at,
            moving, arriving, landing,
            pltpu.VMEM((2, sub, width), F32), pltpu.VMEM((2, sub, width), BF16),
            pltpu.VMEM((w_query.shape[0], cols), BF16), pltpu.VMEM((16, width // 8), BF16),
            pltpu.VMEM((2, 2, hb, half), BF16), pltpu.VMEM((2, seqs * span, hb), BF16),
            *[pltpu.VMEM(a.shape, a.dtype) for a in kept],
            dma((4, seqs)), dma((2,)), dma((5,)), dma((3,)), dma((2,)), dma((2, 2)), dma((2,)), dma((5, 2)), dma((5, 4)), dma((5,)), dma(()), dma(()),
            dma((2, seqs)), dma((2, seqs)), dma((2,)), dma((2, subs)), dma((2, 2)),
        ],
        compiler_params=pltpu.CompilerParams(vmem_limit_bytes=VMEM_MOST, collective_id=1, has_side_effects=True),
        cost_estimate=cost(flops, 80 * seqs * span * width),
        name="attention_forward",
    )(lengths, x, cot, w_query, w_key, w_value, w_out, w_gate, w_up, w_down, *all_gains)


def by_pieces(count, body, size=16):
    def one(p, carry):
        body(pl.ds(pl.multiple_of(p * size, size), size), p * size)
        return carry

    lax.fori_loop(0, count // size, one, 0, unroll=2)


def fold_lanes(values):
    tiles = values[:8] + values[8:]
    return sum(tiles[:, k * 128 : (k + 1) * 128] for k in range(tiles.shape[1] // 128))


class Chain:
    def __init__(self, rank, part, arrive, back, send, recv, landed=False):
        self.landed = landed
        self.inner = (rank % 3) != 0
        self.outer = (rank % 3) == 0
        self.part, self.arrive, self.back = part, arrive, back
        self.send, self.recv = send, recv
        self.side, self.mid = {"tensor": xor_one(rank)}, {"tensor": 3 - rank}
        self.count = back.shape[0]

    def hop_in(self, u):
        return remote(self.part.at[u], self.arrive.at[u], self.send.at[0], self.recv.at[0, u], self.side)

    def hop_mid(self, u):
        return remote(self.arrive.at[u], self.back.at[u], self.send.at[1], self.recv.at[1, u], self.mid)

    def hop_out(self, u):
        return remote(self.part.at[u], self.back.at[u], self.send.at[0], self.recv.at[0, u], self.side)

    def add(self, into, one, two, u):
        def body(cut, first):
            into[u, cut, :] = (one[u, cut, :].astype(F32) + two[u, cut, :].astype(F32)).astype(BF16)

        by_pieces(self.part.shape[1], body)

    def begin(self, u):
        @pl.when(self.outer)
        def _():
            self.hop_in(u).start()

    def middle(self, u):
        @pl.when((u >= 0) & (u < self.count) & self.inner)
        def _():
            if not self.landed:
                self.hop_in(u).wait_recv()
            self.add(self.arrive, self.part, self.arrive, u)
            self.hop_mid(u).start()

    def outward(self, u):
        @pl.when((u >= 0) & (u < self.count) & self.inner)
        def _():
            self.hop_mid(u).wait_recv()
            self.add(self.part, self.part, self.back, u)
            self.hop_out(u).start()

    def ready(self, u):
        @pl.when(self.outer)
        def _():
            self.hop_out(u).wait_recv()

    def total(self, u, cut):
        near = jnp.where(self.inner, self.arrive[u, cut, :], self.part[u, cut, :])
        return near.astype(F32) + self.back[u, cut, :].astype(F32)

    def settle(self):
        def all_sent(ref, count, sem):
            every = ref.at[pl.ds(0, count)]
            remote(every, every, self.send.at[sem], self.recv.at[0, 0], self.side).wait_send()

        @pl.when(self.inner)
        def _():
            all_sent(self.part, self.count, 0)
            all_sent(self.arrive, self.count, 1)

        if not self.landed:

            @pl.when(self.outer)
            def _():
                all_sent(self.part, self.arrive.shape[0], 0)


def feed_both_kernel(
    hb, sub, rows,
    len_ref, n2_hbm, gf_hbm, gate_hbm, up_hbm, down_hbm, gi_hbm, rest_hbm, resta_hbm, xr_hbm, hidden_in, gains_ref,
    ffn_hbm, gb_hbm, gh_hbm, dgate_hbm, dup_hbm, ddown_hbm, hidden_hbm, landx, landy, ring_hbm, gain_out, stat_ref,
    n2_v, gf_v, inner_v, gg_v, gu_v, facc, gacc, wrow, wcol, part_v, in_v, back_v, hid_v, gh_v, gb_v, stage_row, stage_col,
    xtile_v, gi_v, wide_v, temp_v, gain_ref,
    load_sem, wsem, zsend, zrecv, hid_sem, out_sem, ffn_sem, csend, crecv, store_sem, lsend, lrecv, xt_sem, xsend, xrecv, xload, rsend, rrecv, free_sem, done_sem,
):
    core, rank = lax.axis_index("context"), lax.axis_index("tensor")
    near_core = {"context": 1 - core}
    tokens, width = n2_v.shape
    half = width // 2
    hidden = inner_v.shape[1]
    hsteps = hidden // hb
    steps = tokens // rows * hsteps
    per = rows // sub
    chain = Chain(rank, part_v, in_v, back_v, zsend, zrecv)
    subs = chain.count
    known = subs - rest_hbm.shape[0]
    tail = pl.ds(known, subs - known)
    late = Chain(rank, part_v.at[tail], in_v.at[tail], back_v.at[tail], lsend, lrecv, True)
    start = core * (tokens // 2)

    def load_weights(i):
        slot, h = i % 2, i % hsteps
        cut = pl.ds(pl.multiple_of(h * hb, hb), hb)
        here = pl.ds(pl.multiple_of(i // hsteps * rows, rows), rows)
        copies = [pltpu.make_async_copy(gi_hbm.at[here, cut], gi_v.at[slot], wsem.at[slot, 6])]
        for side in range(2):
            copies.append(pltpu.make_async_copy(gate_hbm.at[side, :, cut], wrow.at[slot, 0, side], wsem.at[slot, side]))
            copies.append(pltpu.make_async_copy(up_hbm.at[side, :, cut], wrow.at[slot, 1, side], wsem.at[slot, 2 + side]))
            copies.append(pltpu.make_async_copy(down_hbm.at[side, cut, :], wcol.at[slot, side], wsem.at[slot, 4 + side]))
        return copies

    def load_hidden(u):
        cut = pl.ds(pl.multiple_of(u * sub, sub), sub)
        return pltpu.make_async_copy(hidden_hbm.at[cut, :], hid_v, hid_sem)

    ready = pl.ds(rows, known * sub - rows)
    head = pl.ds(0, rows)
    load_head = pltpu.make_async_copy(n2_hbm.at[head, :], n2_v.at[head, :], load_sem.at[4])
    loads = [
        pltpu.make_async_copy(n2_hbm.at[ready, :], n2_v.at[ready, :], load_sem.at[0]),
        pltpu.make_async_copy(rest_hbm, late.part, load_sem.at[1]),
        pltpu.make_async_copy(resta_hbm, late.arrive, load_sem.at[3]),
    ]
    load_gf = pltpu.make_async_copy(gf_hbm, gf_v, load_sem.at[2])
    for copy in load_weights(0) + [load_head] + loads + [load_gf]:
        copy.start()
    load_hidden(0).start()
    row = lax.axis_index("dp")
    near_x, near_y = {"dp": xor_one(row)}, {"dp": (row + 2) % 4}
    greet([(None, near_core), (None, near_x), (None, near_y), (None, chain.side), (chain.inner, chain.mid)])
    for b in range(8):
        gain_ref[:, b * (width // 8) : (b + 1) * (width // 8)] = gains_ref[b, 1:2, :].astype(F32)
    gain_out[...] = jnp.zeros_like(gain_out)
    stat_ref[...] = jnp.zeros_like(stat_ref)
    load_head.wait()

    def load_x(u):
        at = pl.multiple_of((known + u) * sub, sub)
        return pltpu.make_async_copy(xr_hbm.at[pl.ds(at, sub), :], xtile_v, xt_sem)

    def late_store(u):
        return pltpu.make_async_copy(gh_v, hidden_hbm.at[pl.ds(pl.multiple_of((known + u) * sub, sub), sub), :], out_sem.at[0])

    def late_finish(u):
        load_x(u).start()
        late.ready(u)
        load_x(u).wait()

        @pl.when(u >= 1)
        def _():
            late_store(u - 1).wait()

        length = len_ref[known * sub // (tokens // 2)]
        offset = start + known * sub % (tokens // 2) + u * sub

        def body(cut, first):
            total = late.total(u, cut)
            resid = xtile_v[cut, :].astype(F32)
            hidden_rows = resid + total
            gh_v[cut, :] = hidden_rows
            normed = (hidden_rows * inverse_rms(hidden_rows) * gain_ref[...]).astype(BF16)
            n2_v[pl.ds(pl.multiple_of((known + u) * sub + first, 16), 16), :] = normed
            spot = offset + first + lax.broadcasted_iota(jnp.int32, (16, 1), 0)
            valid = (spot < length).astype(F32)
            stat_ref[0] += fold_lanes(valid * resid * resid)
            stat_ref[1] += fold_lanes(valid * total * total)

        by_pieces(sub, body)
        late_store(u).start()

    def store_gb(u):
        cut = pl.ds(pl.multiple_of(u * sub, sub), sub)
        return pltpu.make_async_copy(gb_v, gb_hbm.at[cut, :], out_sem.at[1])

    def store_gh(u):
        at = pl.ds(pl.multiple_of(u % 2 * sub, sub), sub)
        return pltpu.make_async_copy(gh_v, gh_hbm.at[u // 8, at, :], out_sem.at[0])

    def finish(u):
        chain.ready(u)
        load_hidden(u).wait()

        @pl.when(u >= 1)
        def _():
            store_gb(u - 1).wait()

        def body(piece_rows, first):
            e = chain.total(u, piece_rows)
            hidden_rows = hid_v[piece_rows, :]
            inv = inverse_rms(hidden_rows)
            hat = hidden_rows * inv
            eg = e * gain_ref[...]
            grad = gf_v[pl.ds(pl.multiple_of(u * sub + first, 16), 16), :].astype(F32)
            gh = grad + inv * (eg - hat * jnp.mean(eg * hat, axis=-1, keepdims=True))
            gb_v[piece_rows, :] = gh.astype(BF16)

            @pl.when(u % 8 // 2 == rank)
            def _():
                gh_v[piece_rows, :] = gh

            both = e * hat
            gain_out[...] += both[:8] + both[8:]

        by_pieces(sub, body)
        store_gb(u).start()

        @pl.when(u % 8 // 2 == rank)
        def _():
            store_gh(u).start()
            store_gh(u).wait()

        @pl.when(u + 1 < subs)
        def _():
            load_hidden(u + 1).start()

    def serve(n):
        chain.middle(n)
        chain.outward(n - 2)

        @pl.when((n >= 4) & (n < 4 + subs))
        def _():
            finish(n - 4)

    quarter = width // 4

    def store_ffn(c):
        here = pl.ds(pl.multiple_of(c * rows, rows), rows)
        return [
            pltpu.make_async_copy(
                stage_row.at[c % 2, pl.ds(k * rows, rows), :], ffn_hbm.at[here, pl.ds(k * quarter, quarter)], ffn_sem.at[c % 2, k]
            )
            for k in range(4)
        ]

    def step(i, carry):
        slot, c, h = i % 2, i // hsteps, i % hsteps
        for copy in load_weights(i):
            copy.wait()

        @pl.when(i + 1 < steps)
        def _():
            for copy in load_weights(i + 1):
                copy.start()

        here = pl.ds(pl.multiple_of(c * rows, rows), rows)
        cols = pl.ds(pl.multiple_of(h * hb, hb), hb)
        n = n2_v[here, :]
        wide = min(256, hb)
        for q in range(hb // wide):
            part = slice(q * wide, (q + 1) * wide)
            gate = dot_nn(n[:, :half], wrow[slot, 0, 0, :, part]) + dot_nn(n[:, half:], wrow[slot, 0, 1, :, part])
            up = dot_nn(n[:, :half], wrow[slot, 1, 0, :, part]) + dot_nn(n[:, half:], wrow[slot, 1, 1, :, part])
            gi = gi_v[slot, :, part].astype(F32)
            sig = jax.nn.sigmoid(gate)
            silu = gate * sig
            at = pl.ds(pl.multiple_of(h * hb + q * wide, wide), wide)
            inner_v[here, at] = (silu * up).astype(BF16)
            gg_v[here, at] = (gi * up * sig * (1.0 + gate * (1.0 - sig))).astype(BF16)
            gu_v[here, at] = (gi * silu).astype(BF16)

        @pl.when(h == 0)
        def _():
            gacc[...] = jnp.zeros_like(gacc)

        gg, gu = gg_v[here, cols], gu_v[here, cols]
        span = min(512, half)
        for side in range(2):
            for q in range(half // span):
                part = slice(q * span, (q + 1) * span)
                cut = slice(side * half + q * span, side * half + (q + 1) * span)
                gacc[:, cut] += dot_nt(gg, wrow[slot, 0, side, part, :]) + dot_nt(gu, wrow[slot, 1, side, part, :])

        @pl.when(h == hsteps - 1)
        def _():
            for k in range(per):
                part_v[c * per + k] = gacc[k * sub : (k + 1) * sub, :].astype(BF16)
                chain.begin(c * per + k)

        @pl.when(c % 2 == 1)
        def _():
            pair = pl.ds(pl.multiple_of((c - 1) * rows, rows), 2 * rows)
            inner = inner_v[pair, cols]

            @pl.when(h == 0)
            def _():
                facc[...] = jnp.zeros_like(facc)

            for side in range(2):
                for q in range(half // span):
                    part = slice(q * span, (q + 1) * span)
                    cut = slice(side * half + q * span, side * half + (q + 1) * span)
                    facc[:, cut] += dot_nn(inner, wcol[slot, side, :, part])

            @pl.when(h == hsteps - 1)
            def _():
                for m in range(2):

                    @pl.when(c >= 2)
                    def _():
                        for copy in store_ffn(c - 3 + m):
                            copy.wait()

                    for k in range(4):
                        stage_row[m, k * rows : (k + 1) * rows, :] = facc[
                            m * rows : (m + 1) * rows, k * quarter : (k + 1) * quarter
                        ].astype(BF16)
                    for copy in store_ffn(c - 1 + m):
                        copy.start()

        @pl.when(i == 0)
        def _():
            for copy in loads:
                copy.wait()

        late.middle(i)
        late.outward(i - 3)

        @pl.when((i >= 6) & (i < 6 + late.count))
        def _():
            late_finish(i - 6)

        @pl.when(i == 9)
        def _():
            load_gf.wait()
            late_store(late.count - 1).wait()
            late.settle()
            pl.semaphore_signal(done_sem, inc=1, device_id=chain.side, device_id_type=pl.DeviceIdType.MESH)

            @pl.when(chain.inner)
            def _():
                pl.semaphore_signal(done_sem, inc=1, device_id=chain.mid, device_id_type=pl.DeviceIdType.MESH)

        @pl.when(i == steps - 2)
        def _():
            pl.semaphore_wait(done_sem, jnp.where(chain.inner, 2, 1))

        serve(i - 6)
        return carry

    lax.fori_loop(0, steps, step, 0)
    for c in range(2, steps // hsteps):
        for copy in store_ffn(c):
            copy.wait()

    pl.semaphore_signal(free_sem, inc=1, device_id=near_core, device_id_type=pl.DeviceIdType.MESH)
    outs = (dgate_hbm, dup_hbm, ddown_hbm)

    def landing(w, t):
        return wrow.at[t // 2, w, t % 2] if w < 2 else wcol.at[t // 2, t % 2]

    def landed(w, t, piece):
        return wrow[t // 2, w, t % 2, piece, :] if w < 2 else wcol[t // 2, t % 2, piece, :]

    def staging(w):
        return stage_row if w < 2 else stage_col

    def ship(w, t):
        return remote(staging(w).at[t % 2], landing(w, t), csend.at[w, t], crecv.at[w, t], near_core)

    def keep(w, t):
        cut = pl.ds(pl.multiple_of(t * hb, hb), hb)
        dst = outs[w].at[:, cut] if w < 2 else outs[w].at[cut, :]
        return pltpu.make_async_copy(staging(w).at[t % 2], dst, store_sem.at[w, t])

    def release(kind, w, t):
        if kind == 1:
            ship(w, t).wait_send()
        else:
            keep(w, t).wait()

    def group(kind, w, before, part):
        def one(t, carry):
            cut = pl.ds(pl.multiple_of(t * hb, hb), hb)
            mine = slice(kind * half, (kind + 1) * half)
            @pl.when(t >= 2)
            def _():
                release(kind, w, t - 2)

            if before is not None:

                @pl.when(t < 2)
                def _():
                    release(before[0], before[1], t + hsteps - 2)

            if kind == 0:
                ship(w, t).wait_recv()
            tall = staging(w).shape[1]
            size = min(256, tall)
            for q in range(tall // size):
                piece = slice(q * size, (q + 1) * size)
                if w == 2:
                    left = inner_v[:, pl.ds(pl.multiple_of(t * hb + q * size, size), size)]
                    value = dot_tn(left, gf_v[:, mine])
                else:
                    value = dot_tn(n2_v[:, kind * half + q * size : kind * half + (q + 1) * size], (gg_v, gu_v)[w][:, cut])
                if kind == 0:
                    value = value + landed(w, t, piece).astype(F32)
                staging(w)[t % 2, piece, :] = value.astype(BF16)
            if kind == 1:
                ship(w, t).start()
            else:
                keep(w, t).start()
            return carry

        lax.fori_loop(part * (hsteps // 2), (part + 1) * (hsteps // 2), one, 0)

    pl.semaphore_wait(free_sem, 1)

    def term(m):
        return ffn_hbm.at[pl.ds(pl.multiple_of(m * (2 * sub), 2 * sub), 2 * sub), :]

    fold = Fold(rank, term, None, ring_hbm, (ring_hbm.at[2], None), rsend, rrecv)
    after = iter(range(steps - 6, subs + 4))
    done = []

    def both(kind, w, before):
        for part in range(2):
            group(kind, w, before, part)
            done.append(part)
            if len(done) <= 8 or len(done) % 2 == 0:
                serve(next(after))
            if len(done) == 5:
                fold.begin()

    both(1, 0, None)
    both(0, 0, (1, 0))
    for t in range(hsteps - 2, hsteps):
        keep(0, t).wait()
    gate_sum = Scatter(
        row_blocks(dgate_hbm), wide_v.at[0], wide_v.at[1], half_rows(landx), half_rows(landy), temp_v, xsend, xrecv, xload, near_x, near_y
    )
    gate_sum.begin()
    both(1, 1, None)
    both(1, 2, None)
    gate_sum.pass_on()
    both(0, 1, (1, 1))
    both(0, 2, (1, 2))
    for n in after:
        serve(n)
    for t in range(hsteps - 2, hsteps):
        keep(1, t).wait()
        keep(2, t).wait()
    store_gb(subs - 1).wait()
    gate_sum.arrived()
    gate_sum.settle()
    chain.settle()

    @pl.when(fold.inner)
    def _():
        for k in range(3):
            fold.come(k)

    @pl.when(fold.outer)
    def _():
        fold.settle()


def row_blocks(ref):
    size = ref.shape[0] // 4
    return lambda k, h: ref.at[pl.ds(k * size + h * (size // 2), size // 2), :]


def half_rows(ref):
    size = ref.shape[0] // 2
    return lambda h: ref.at[pl.ds(h * size, size), :]


def feed_both(lengths, n2, gf, gate, up, down, gi, rest, came, xr, hidden_rows, gain):
    tokens, width = n2.shape
    _, half, hidden = gate.shape
    hb = hidden // 4
    sub, rows = tokens // 16, tokens // 4
    count = rest.shape[0]
    any_space = pl.BlockSpec(memory_space=pl.ANY)
    vmem = pl.BlockSpec(memory_space=pltpu.VMEM)
    dma = pltpu.SemaphoreType.DMA
    moving = pltpu.VMEM((16, sub, width), BF16)
    act = pltpu.VMEM((tokens, hidden), BF16)
    return pl.pallas_call(
        functools.partial(feed_both_kernel, hb, sub, rows),
        in_specs=[SMEM] + [any_space] * 10 + [vmem],
        out_specs=[any_space] * 10 + [vmem] * 2,
        out_shape=[
            shape((tokens, width), BF16), shape((tokens, width), BF16), shape((2, 2 * sub, width), F32),
            shape((half, hidden), BF16), shape((half, hidden), BF16), shape((hidden, half), BF16),
            shape((tokens, width), F32), shape((half // 4, hidden), BF16), shape((half // 4, hidden), BF16),
            shape((3, 2 * sub, width), BF16), shape((8, width), F32), shape((2, 8, 128), F32),
        ],
        scratch_shapes=[
            pltpu.VMEM((tokens, width), BF16), pltpu.VMEM((tokens, width), BF16), act, act, act,
            pltpu.VMEM((2 * rows, width), F32), pltpu.VMEM((rows, width), F32),
            pltpu.VMEM((2, 2, 2, half, hb), BF16), pltpu.VMEM((2, 2, hb, half), BF16),
            moving, moving, moving,
            pltpu.VMEM((sub, width), F32), pltpu.VMEM((sub, width), F32), pltpu.VMEM((sub, width), BF16),
            pltpu.VMEM((2, half, hb), BF16), pltpu.VMEM((2, hb, half), BF16),
            pltpu.VMEM((sub, width), BF16), pltpu.VMEM((2, rows, hb), BF16),
            pltpu.VMEM((2, half // 8, hidden), BF16), pltpu.VMEM((2, half // 8, hidden), BF16), pltpu.VMEM((1, width), F32),
            dma((5,)), dma((2, 7)), dma((2,)), dma((2, 16)), dma(()), dma((2,)), dma((2, 4)), dma((3, 4)), dma((3, 4)),
            dma((3, 4)), dma((2,)), dma((2, count)), dma(()), dma((6,)), dma((6,)), dma((3,)), dma(()), dma((5,)), pltpu.SemaphoreType.REGULAR, pltpu.SemaphoreType.REGULAR,
        ],
        input_output_aliases={10: 6},
        compiler_params=pltpu.CompilerParams(vmem_limit_bytes=VMEM_MOST, collective_id=2, has_side_effects=True),
        cost_estimate=cost(18 * tokens * width * hidden, 60 * tokens * width),
        name="feed_forward_both",
    )(lengths, n2, gf, gate, up, down, gi, rest, came, xr, hidden_rows, gain)


class Fold:
    def __init__(self, rank, source, own, slots, finals, send, recv, landed=None):
        self.inner, self.outer = (rank % 3) != 0, (rank % 3) == 0
        self.side, self.mid = {"tensor": xor_one(rank)}, {"tensor": 3 - rank}
        self.leaving = (3 - rank, xor_one(3 - rank), xor_one(rank))
        self.added = (xor_one(3 - rank), 3 - rank, xor_one(rank))
        self.source, self.own, self.slots, self.finals = source, own, slots, finals
        self.send, self.recv, self.landed = send, recv, landed

    def inward(self, k):
        dst = self.slots.at[k] if k < 2 else self.finals[0]
        return remote(self.source(self.leaving[k]), dst, self.send, self.recv.at[k], self.side)

    def across(self, k):
        dst = self.slots.at[2] if k == 0 else self.finals[1]
        return remote(self.slots.at[k], dst, self.send, self.recv.at[3 + k], self.mid)

    def outward(self):
        return remote(self.slots.at[2], self.finals[0], self.send, self.recv.at[0], self.side)

    def begin(self):
        @pl.when(self.outer)
        def _():
            for k in range(3):
                self.inward(k).start()

    def come(self, k):
        (self.landed[k].wait if self.landed is not None else self.inward(k).wait_recv)()

    def step(self, k):
        @pl.when(self.inner)
        def _():
            if k < 2:
                self.come(k)
            else:
                self.across(0).wait_recv()
            read = self.own(self.added[k])

            def body(cut, first):
                self.slots[k, cut, :] = (self.slots[k, cut, :].astype(F32) + read(cut).astype(F32)).astype(BF16)

            by_pieces(self.slots.shape[1], body)
            (self.across(k) if k < 2 else self.outward()).start()

    def arrived(self):
        @pl.when(self.inner)
        def _():
            self.come(2)
            self.across(1).wait_recv()

        @pl.when(self.outer)
        def _():
            self.outward().wait_recv()

    def settle(self):
        three = self.slots.at[pl.ds(0, 3)]
        every = remote(three, three, self.send, self.recv.at[0], self.side)
        if self.landed is None:
            every.wait_send()
        else:
            pl.when(self.inner)(every.wait_send)


def tall(ref):
    return 16 * max(1, 2048 // ref.shape[1])


class Scatter:
    def __init__(self, block, from_x, from_y, land_x, land_y, temps, send, recv, load, near_x, near_y):
        self.block, self.from_x, self.from_y, self.land_x, self.land_y = block, from_x, from_y, land_x, land_y
        self.temps, self.load = temps, load
        sem = lambda k: (send.at[k], recv.at[k])
        self.first = [
            remote(block(3, 0), from_x, *sem(0), near_x),
            remote(block(3, 1), from_y, *sem(1), near_y),
            remote(block(1, 0), land_x(0), *sem(2), near_x),
            remote(block(2, 1), land_y(1), *sem(3), near_y),
        ]
        self.second = [
            remote(from_y, land_x(1), *sem(4), near_x),
            remote(from_x, land_y(0), *sem(5), near_y),
        ]

    def begin(self):
        for copy in self.first:
            copy.start()

    def pass_on(self):
        loads = [
            pltpu.make_async_copy(self.block(1, 1), self.temps.at[0], self.load.at[0]),
            pltpu.make_async_copy(self.block(2, 0), self.temps.at[1], self.load.at[1]),
        ]
        for copy in loads:
            copy.start()
        for which, into in ((1, self.from_y), (0, self.from_x)):
            self.first[which].wait_recv()
            loads[1 - which].wait()
            temp = 1 - which

            def body(cut, first):
                into[cut, :] = (into[cut, :].astype(F32) + self.temps[temp, cut, :].astype(F32)).astype(BF16)

            by_pieces(into.shape[0], body, tall(into))
            self.second[temp].start()

    def arrived(self):
        for copy in self.first[2:] + self.second:
            copy.wait_recv()

    def keep(self, out, store):
        for h in range(2):
            loads = [
                pltpu.make_async_copy(src, self.temps.at[k], self.load.at[k])
                for k, src in enumerate((self.block(0, h), self.land_x(h), self.land_y(h)))
            ]
            for copy in loads:
                copy.start()
            for copy in loads:
                copy.wait()

            def body(cut, first):
                self.temps[0, cut, :] = sum(self.temps[k, cut, :].astype(F32) for k in range(3)).astype(BF16)

            by_pieces(self.temps.shape[1], body, tall(self.temps.at[0]))
            copy = pltpu.make_async_copy(self.temps.at[0], out(h), store)
            copy.start()
            copy.wait()

    def settle(self):
        for copy in self.first + self.second:
            copy.wait_send()


def backward_kernel(
    hd, nq, nk, block,
    len_ref, gb_hbm, hidden_hbm, ffn_hbm, ring_hbm, xr_hbm, n1_hbm, tok_hbm, outw_hbm, qkvw_hbm, all_hbm, att_hbm, inv_hbm, pre_hbm,
    gh_hbm, dgate_hbm, landx0, landy0, dup_hbm, ddown_hbm, table_ref, gains_ref, stat_ref, stat2_ref, gain2_ref,
    out_hbm, gin_hbm, fin_hbm, finb_hbm, own_hbm, sum_gate, sum_up, sum_down, mine_o, mine_q, landx1, landy1, landx2, landy2, landx3, landy3, landx4, landy4,
    lines_out, small_out,
    act_v, rows_v, qkvw_v, tok_v, all_v, att_v, inv_v, pre_v, grads, da_all, da_own, da_send, da_got, d_own, d_send, d_got, dpre_v,
    first_v, slots_v, turns_v, piece_v, wide_a, wide_b, temp_a, temp_b,
    go_v, so_v, wide_o, temp_o, gq_v, sq_v, wide_q, temp_q,
    tile_v, otile_v, lines_v, small_v, heads_v, lin1, lin2, lin3, small_r,
    load_sem, zsend, zrecv, piece_sem, xsend, xrecv, xload, own_sem, exsend, exrecv, osend, orecv, qsend, qrecv,
    tile_sem, outs_sem, sum_sem, smsend, smrecv,
):
    seqs, _, slots = all_v.shape
    span = slots // 2
    width = act_v.shape[1]
    half = width // 2
    groups = nq // nk
    share = span // 4
    row, core, rank = lax.axis_index("dp"), lax.axis_index("context"), lax.axis_index("tensor")
    start = core * span
    near = [row, xor_one(row), (row + 2) % 4, 3 - row]
    near_x, near_y, near_core = {"dp": near[1]}, {"dp": near[2]}, {"context": 1 - core}
    z_right, z_left, z_far = {"tensor": (rank + 1) % 4}, {"tensor": (rank + 3) % 4}, {"tensor": (rank + 2) % 4}
    first_core = core == 0

    def load(k, src, dst):
        copy = pltpu.make_async_copy(src, dst, load_sem.at[k])
        copy.start()
        return copy

    load_gb = load(0, gb_hbm, act_v)
    load_outw = load(1, outw_hbm, rows_v)
    load_att = [
        load(2, all_hbm, all_v), load(3, att_hbm, att_v), load(4, inv_hbm, inv_v), load(5, pre_hbm, pre_v),
    ]
    load_tok = load(6, tok_hbm, tok_v)
    load_qkvw = load(7, qkvw_hbm, qkvw_v)

    def piece_rows(s, m):
        return pl.ds(pl.multiple_of(s * span + m * share, share), share)

    def load_piece(s, m):
        return pltpu.make_async_copy(ffn_hbm.at[piece_rows(s, m), :], piece_v.at[s], piece_sem.at[s])

    greet([(None, d) for d in (near_x, near_y, {"dp": near[3]}, near_core, z_right, z_left, z_far)])

    last = seqs - 1
    inner = (rank % 3) != 0
    came = []
    for k, slot in enumerate((0, 1, 3)):
        came.append(pltpu.make_async_copy(ring_hbm.at[k], slots_v.at[0, slot], load_sem.at[12 + k]))

    @pl.when(inner)
    def _():
        for copy in came:
            copy.start()

    def ffn_own(s):
        def own(m):
            load_piece(s, m).wait()
            return lambda cut: piece_v[s, cut, :]

        return own

    def first_own(s):
        return lambda m: lambda cut: first_v[s, m, cut, :]

    ffn_rings = [
        Fold(
            rank, lambda m, s=s: ffn_hbm.at[piece_rows(s, m), :], ffn_own(s), slots_v.at[s], (slots_v.at[s, 3], slots_v.at[s, 4]),
            zsend.at[s], zrecv.at[s], came if s == 0 else None,
        )
        for s in range(seqs)
    ]
    first_rings = [
        Fold(
            rank, lambda m, s=s: first_v.at[s, m], first_own(s), turns_v.at[s], (fin_hbm.at[s], finb_hbm.at[s]),
            zsend.at[seqs + s], zrecv.at[seqs + s],
        )
        for s in range(seqs)
    ]
    for s in range(1, seqs):
        ffn_rings[s].begin()
    for s in range(seqs):
        load_piece(s, jnp.where(inner, ffn_rings[s].added[0], rank)).start()

    def ffn_step(s, k):
        ffn_rings[s].step(k)

        @pl.when(inner)
        def _():
            load_piece(s, ffn_rings[s].added[k + 1] if k < 2 else rank).start()

    def in_hbm(ref, axis):
        size = ref.shape[axis] // 4
        h2 = (size if axis == 0 else ref.shape[0]) // 2

        def get(k, h):
            if axis == 0:
                return ref.at[pl.ds(k * size + h * h2, h2), :]
            return ref.at[pl.ds(h * h2, h2), pl.ds(k * size, size)]

        return get

    def halves(ref):
        h2 = ref.shape[0] // 2
        return lambda h: ref.at[pl.ds(h * h2, h2), :]

    def in_vmem(ref):
        h2 = ref.shape[1] // 2
        return lambda k, h: ref.at[k, pl.ds(h * h2, h2), :]

    def scatter(i, get, wide, land_x, land_y, temps):
        return Scatter(get, wide.at[0], wide.at[1], land_x, land_y, temps, xsend.at[i], xrecv.at[i], xload.at[i], near_x, near_y)

    s_gate = scatter(0, in_hbm(dgate_hbm, 0), wide_a, halves(landx0), halves(landy0), temp_a)
    s_up = scatter(0, in_hbm(dup_hbm, 0), wide_a, halves(landx1), halves(landy1), temp_a)
    s_down = scatter(1, in_hbm(ddown_hbm, 1), wide_b, halves(landx2), halves(landy2), temp_b)
    s_out = scatter(2, in_vmem(go_v), wide_o, halves(landx3), halves(landy3), temp_o)
    s_qkv = scatter(3, in_vmem(gq_v), wide_q, halves(landx4), halves(landy4), temp_q)
    s_up.begin()
    ffn_step(0, 0)
    ffn_step(0, 1)

    load_gb.wait()
    load_outw.wait()

    def give(s):
        return remote(da_send.at[s], da_got.at[s], exsend.at[0, s], exrecv.at[0, s], near_core)

    def exchange(s):
        return remote(d_send.at[s], d_got.at[s], exsend.at[1, s], exrecv.at[1, s], near_core)

    def branch_rows(s, carry):
        here = pl.ds(pl.multiple_of(s * span, span), span)
        parts = []
        for q in range(2):
            cut = slice(q * (nq * hd // 2), (q + 1) * (nq * hd // 2))
            da = dot_nt(rows_v[0, cut, :], act_v[here, :half]) + dot_nt(rows_v[1, cut, :], act_v[here, half:])
            parts.append(da.astype(BF16))
        da_own[s] = jnp.where(first_core, parts[0], parts[1])
        da_send[s] = jnp.where(first_core, parts[1], parts[0])
        give(s).start()
        return carry

    lax.fori_loop(0, seqs, branch_rows, 0)

    def load_x(s):
        return [pltpu.make_async_copy(xr_hbm.at[s, :, pl.ds(k * half, half)], rows_v.at[k], load_sem.at[10 + k]) for k in range(2)]

    for copy in load_x(0):
        copy.start()
    for copy in load_att:
        copy.wait()

    scale = log2e / math.sqrt(hd)
    back = 1.0 / math.sqrt(hd)
    krow = lax.broadcasted_iota(jnp.int32, (block, groups * block), 0)
    qcol = lax.broadcasted_iota(jnp.int32, (block, groups * block), 1) % block
    base = groups * hd

    def attention(s):
        give(s).wait_recv()
        low, high = join_positions(core, da_own[s], da_got[s])
        da_all[:, :span] = low
        da_all[:, span:] = high
        length = len_ref[s]
        grads[base:, :] = jnp.zeros((2 * hd, slots), F32)
        for i in range(slots // block):
            cut = slice(i * block, (i + 1) * block)
            q = jnp.concatenate([all_v[s, g * hd : (g + 1) * hd, cut] for g in range(groups)], axis=1)
            da = jnp.concatenate([da_all[g * hd : (g + 1) * hd, cut] for g in range(groups)], axis=1)
            at = jnp.concatenate([att_v[s, g * hd : (g + 1) * hd, cut] for g in range(groups)], axis=1)
            inv = jnp.concatenate([inv_v[s, g : g + 1, cut] for g in range(groups)], axis=1)
            delta = jnp.sum(at.astype(F32) * da.astype(F32), axis=0, keepdims=True)
            dq = jnp.zeros((hd, groups * block), F32)
            for j in range(i + 1):
                kcut = slice(j * block, (j + 1) * block)
                key = all_v[s, base : base + hd, kcut]
                score = dot_tn(key, q) * scale
                ok = (krow + j * block) < length
                if j == i:
                    ok = ok & (krow <= qcol)
                p = jnp.where(ok, jnp.exp2(score) * inv, 0.0)
                dp = dot_tn(all_v[s, base + hd : base + 2 * hd, kcut], da)
                ds = (p * (dp - delta)).astype(BF16)
                dq = dq + dot_nn(key, ds)
                grads[base : base + hd, kcut] += dot_nt(q, ds) * back
                grads[base + hd : base + 2 * hd, kcut] += dot_nt(da, p.astype(BF16))
            dq = dq * back
            for g in range(groups):
                grads[g * hd : (g + 1) * hd, cut] = dq[:, g * block : (g + 1) * block]
        mine, theirs = join_positions(core, grads[:, :span], grads[:, span:])
        d_own[s] = mine.astype(BF16)
        d_send[s] = theirs.astype(BF16)
        exchange(s).start()

    quarter = hd // 2
    cosine, sine = table_ref[:quarter, :], table_ref[quarter : 2 * quarter, :]
    qgain, kgain = table_ref[2 * quarter : 2 * quarter + hd, 0:1], table_ref[2 * quarter + hd :, 0:1]
    sides = (nq // 2, nk // 2, nk // 2)
    copies_in_tensor = 1.0 / lax.axis_size("tensor")
    lines_v[:8, :] = jnp.zeros((8, width), F32)
    lines_v[8:, :] = gain2_ref[...] * copies_in_tensor
    heads_v[...] = jnp.zeros_like(heads_v)
    valid_slots = jnp.int32(0)
    for s in range(seqs):
        valid_slots = valid_slots + jnp.clip(len_ref[s] - start, 0, span)
    count = valid_slots.astype(F32) * (copies_in_tensor / 128.0)
    small_v[...] = jnp.zeros_like(small_v)
    for k in range(2):
        both = stat_ref[k] + stat2_ref[k]
        small_v[1 + k : 2 + k, :] = jnp.sum(both, axis=0, keepdims=True) * copies_in_tensor
    small_v[4:5, :] = jnp.broadcast_to(count, (1, 128))
    load_qkvw.wait()

    def fold_columns(values):
        return sum(values[:, k * 128 : (k + 1) * 128] for k in range(values.shape[1] // 128))

    def heads_rows(s):
        exchange(s).wait_recv()
        low, high = join_positions(core, d_own[s].astype(F32), d_got[s].astype(F32))
        parts = [[], [], []]
        for side in (low, high):
            at = 0
            for kind, number in enumerate(sides):
                for _ in range(number):
                    parts[kind].append(side[at : at + hd])
                    at += hd
        done = []
        for h in range(nq + nk):
            kind = 0 if h < nq else 1
            g = parts[kind][h - kind * nq]
            a, b = g[: hd // 2], g[hd // 2 :]
            g = jnp.concatenate([a * cosine + b * sine, b * cosine - a * sine], axis=0)
            v = pre_v[s, h * hd : (h + 1) * hd, :]
            inv = lax.rsqrt(jnp.mean(v * v, axis=0, keepdims=True) + epsilon)
            hat = v * inv
            heads_v[kind * hd : (kind + 1) * hd, :] += fold_columns(g * hat)
            gg = g * (qgain if kind == 0 else kgain)
            done.append(inv * (gg - hat * jnp.mean(gg * hat, axis=0, keepdims=True)))
        done += parts[2]
        for h in range(nq + 2 * nk):
            pair = h % 2
            if pair == 0:
                two = jnp.concatenate([done[h], done[h + 1]], axis=0).T.astype(BF16)
                dpre_v[pl.ds(pl.multiple_of(s * span, span), span), h * hd : (h + 2) * hd] = two
        for copy in load_x(s):
            copy.wait()
        for m in range(4):
            rows = slice(m * share, (m + 1) * share)
            xs = [rows_v[k, rows, :].astype(F32) for k in range(2)]
            mean = sum(jnp.sum(x * x, axis=-1, keepdims=True) for x in xs) * (1.0 / width)
            inv = lax.rsqrt(mean + epsilon)
            dpre = dpre_v[pl.ds(pl.multiple_of(s * span + m * share, share), share), :]
            for k in range(2):
                part = dot_nt(dpre, qkvw_v[k])
                cut = slice(k * half, (k + 1) * half)
                first_v[s, m, :, cut] = part.astype(BF16)
                both = part * (xs[k] * inv)
                lines_v[:8, cut] += sum(both[8 * r : 8 * r + 8] for r in range(share // 8))

    def sequence(s, carry):
        attention(s)

        @pl.when(s == last)
        def _():
            ffn_step(1, 1)
            s_up.pass_on()

        heads_rows(s)

        @pl.when(s == 0)
        def _():
            for copy in load_x(1):
                copy.start()
            first_rings[0].begin()
            ffn_step(1, 0)
            ffn_step(0, 2)
            s_down.begin()

        @pl.when(s == last)
        def _():
            first_rings[1].begin()

        return carry

    lax.fori_loop(0, seqs, sequence, 0)

    def hop_copies(n, items):
        base_at = (0, 1, 4, 5, 8)[n]
        return [
            remote(src, dst, smsend.at[base_at + i], smrecv.at[base_at + i], device) for i, (device, src, dst, _) in enumerate(items)
        ]

    def hop_begin(n, items):
        for copy in hop_copies(n, items):
            copy.start()

    def hop_end(n, items):
        for copy in hop_copies(n, items):
            copy.wait()
        for _, _, dst, place_to in items:
            if place_to is None:
                small_v[...] += dst[...]
            else:
                lines_v[:, place_to] += dst[...]

    piece = width // 8

    def columns(k):
        return slice(k * piece, (k + 1) * piece)

    def view(k, count=1):
        return lines_v.at[:, pl.ds(k * piece, count * piece)]

    hop_core = [(near_core, view(4, 4), lin1, slice(0, half))]
    near_all = [near_x, near_y, {"dp": near[3]}]
    hop_lines = [(near_all[k], view(1 + k), lin2.at[k], columns(0)) for k in range(3)]
    hop_small = [(near_core, small_v, small_r.at[0], None)]
    hop_square = [(near_all[k], small_v, small_r.at[1 + k], None) for k in range(3)]
    z_all = [z_right, z_far, z_left]
    hop_chain = [(z_all[k], view(0), lin3.at[k], columns(0)) for k in range(3)]
    hop_chain += [(z_all[k], small_v, small_r.at[4 + k], None) for k in range(3)]
    hop_begin(0, hop_core)

    load_tok.wait()
    blocks_o = [remote(so_v.at[k], go_v.at[k], osend.at[k], orecv.at[k], near_core) for k in range(4)]
    size_o = half // 4
    for k in range(4):
        cut = slice(half + k * size_o, half + (k + 1) * size_o)
        so_v[k] = dot_tn(tok_v[...], act_v[:, cut]).astype(BF16)
        blocks_o[k].start()
    ffn_step(1, 2)
    for k in range(4):
        blocks_o[k].wait_recv()
        cut = slice(k * size_o, (k + 1) * size_o)
        go_v[k] = (dot_tn(tok_v[...], act_v[:, cut]) + go_v[k].astype(F32)).astype(BF16)
    s_out.begin()
    load_n1 = load(0, n1_hbm, act_v)
    hop_end(0, hop_core)
    hop_begin(1, hop_lines)
    load_n1.wait()
    blocks_q = [remote(sq_v.at[k], gq_v.at[k], qsend.at[k], qrecv.at[k], near_core) for k in range(4)]
    size_q = half // 4
    for k in range(4):
        cut = slice(half + k * size_q, half + (k + 1) * size_q)
        sq_v[k] = dot_tn(act_v[:, cut], dpre_v[...]).astype(BF16)
        blocks_q[k].start()
    for k in range(4):
        blocks_q[k].wait_recv()
        cut = slice(k * size_q, (k + 1) * size_q)
        gq_v[k] = (dot_tn(act_v[:, cut], dpre_v[...]) + gq_v[k].astype(F32)).astype(BF16)
    s_qkv.begin()
    keeps = [
        pltpu.make_async_copy(go_v.at[0], mine_o, own_sem.at[0]),
        pltpu.make_async_copy(gq_v.at[0], mine_q, own_sem.at[1]),
    ]
    keeps += [pltpu.make_async_copy(first_v.at[s, rank], own_hbm.at[s], own_sem.at[2 + s]) for s in range(seqs)]
    for copy in keeps:
        copy.start()


    def place(tile, dst, s):
        for o in range(2):
            for k in range(4):
                b = near[k] * 2 + (core if o == 0 else 1 - core)
                cut = pl.ds(pl.multiple_of(b * piece, piece), piece)
                pltpu.make_async_copy(tile.at[:, pl.ds((o * 4 + k) * piece, piece)], dst.at[s, :, cut], outs_sem).start()
        pltpu.make_async_copy(tile, dst.at[s], outs_sem).wait()

    def out_share(s):
        keep = pltpu.make_async_copy(hidden_hbm.at[piece_rows(s, rank), :], tile_v, tile_sem.at[0])
        keep.start()
        ffn_rings[s].arrived()
        read = ffn_rings[s].own(rank)
        keep.wait()

        def body(cut, first):
            ffn = slots_v[s, 3, cut, :].astype(F32) + read(cut).astype(F32)
            ffn = ffn + jnp.where(inner, slots_v[s, 4, cut, :].astype(F32), 0.0)
            otile_v[cut, :] = (tile_v[cut, :] + ffn).astype(BF16)
            spot = start + rank * share + first + lax.broadcasted_iota(jnp.int32, (16, 1), 0)
            valid = (spot < len_ref[s]).astype(F32)
            small_v[3:4, :] += jnp.sum(fold_lanes(valid * ffn * ffn), axis=0, keepdims=True)

        by_pieces(share, body)
        place(otile_v, out_hbm, s)

    def in_share(s):
        first_rings[s].arrived()
        tiles = (piece_v.at[0], piece_v.at[1], otile_v)
        rows = pl.ds(pl.multiple_of(rank * share, share), share)
        loads = [
            pltpu.make_async_copy(src, dst, load_sem.at[k])
            for k, (src, dst) in enumerate(zip((fin_hbm.at[s], finb_hbm.at[s], xr_hbm.at[s, rows, :]), tiles))
        ]
        loads.append(pltpu.make_async_copy(gh_hbm.at[s], tile_v, load_sem.at[3]))
        for copy in loads:
            copy.start()
        gain = jnp.concatenate([gains_ref[b, 0:1, :] for b in range(8)], axis=1).astype(F32)
        for copy in loads:
            copy.wait()

        def body(cut, at):
            e = piece_v[0, cut, :].astype(F32) + first_v[s, rank, cut, :].astype(F32)
            e = e + jnp.where(inner, piece_v[1, cut, :].astype(F32), 0.0)
            x = otile_v[cut, :].astype(F32)
            inv = inverse_rms(x)
            hat = x * inv
            eg = e * gain
            tile_v[cut, :] = tile_v[cut, :] + inv * (eg - hat * jnp.mean(eg * hat, axis=-1, keepdims=True))

        by_pieces(share, body)
        place(tile_v, gin_hbm, s)

    small_v[0:1, :] = jnp.sum(heads_v[...].T, axis=0, keepdims=True)
    first_rings[0].step(0)
    out_share(0)
    s_down.pass_on()
    out_share(1)
    hop_end(1, hop_lines)
    hop_begin(2, hop_small)
    hop_end(2, hop_small)
    hop_begin(3, hop_square)
    first_rings[0].step(1)
    first_rings[0].step(2)
    s_out.pass_on()
    s_qkv.pass_on()
    s_gate.keep(halves(sum_gate), sum_sem)
    s_up.arrived()
    s_up.keep(halves(sum_up), sum_sem)
    first_rings[1].step(0)
    hop_end(3, hop_square)
    hop_begin(4, hop_chain)
    s_down.arrived()
    s_down.keep(halves(sum_down), sum_sem)
    first_rings[1].step(1)
    first_rings[1].step(2)
    for s in range(last):
        in_share(s)
    hop_end(4, hop_chain)
    lines_out[...] = lines_v[:, :piece]
    small_out[...] = small_v[...]
    for item in (s_out, s_qkv):
        item.arrived()
    first_rings[last].arrived()
    for copy in keeps:
        copy.wait()
    for ring in ffn_rings + first_rings:
        ring.settle()
    for item in (s_up, s_down, s_out, s_qkv):
        item.settle()
    for copy in blocks_o + blocks_q:
        copy.wait_send()
    for s in range(seqs):
        give(s).wait_send()
        exchange(s).wait_send()


def backward(
    lengths, gb, hidden_rows, ffn, ring, xr, n1, tok, outw, qkvw, everything, att, inv, pre, gh, dgate, landx, landy, dup, ddown,
    table, gains, stat, stat2, gain2_part, hd, nq, nk,
):
    seqs, span, width = xr.shape
    half = width // 2
    groups = nq // nk
    share = span // 4
    piece = width // 8
    hidden = dup.shape[1]
    cols = qkvw.shape[2]
    feat = nq * hd
    block = min(256, span)
    any_space = pl.BlockSpec(memory_space=pl.ANY)
    vmem = pl.BlockSpec(memory_space=pltpu.VMEM)
    dma = pltpu.SemaphoreType.DMA
    hold = lambda *dims: pltpu.VMEM(dims, BF16)
    wide = lambda *dims: pltpu.VMEM(dims, F32)
    token = shape((seqs, share, width), BF16)
    big = [token, shape((seqs - 1, share, width), F32)] + [token] * 3 + [shape((piece, hidden), BF16)] * 2 + [shape((hidden, piece), BF16)]
    big += [shape((feat, piece), BF16), shape((piece, cols), BF16)]
    big += [shape((piece, hidden), BF16)] * 2 + [shape((hidden, piece), BF16)] * 2
    big += [shape((feat, piece), BF16)] * 2 + [shape((piece, cols), BF16)] * 2
    small = [shape((16, piece), F32), shape((8, 128), F32)]
    rows = everything.shape[1]
    scratch = [
        hold(seqs * span, width), hold(2, span, half), hold(2, half, cols), hold(seqs * span, feat), hold(*everything.shape), hold(*att.shape),
        wide(*inv.shape), wide(*pre.shape), wide(rows, 2 * span), hold(groups * hd, 2 * span),
        hold(seqs, feat // 2, span), hold(seqs, feat // 2, span), hold(seqs, feat // 2, span),
        hold(seqs, rows, span), hold(seqs, rows, span), hold(seqs, rows, span), hold(seqs * span, cols),
        hold(seqs, 4, share, width), hold(seqs, 5, share, width), hold(seqs, 3, share, width), hold(seqs, share, width),
        hold(2, piece // 2, hidden), hold(2, hidden // 2, piece), hold(3, piece // 2, hidden), hold(3, hidden // 2, piece),
        hold(4, feat, piece), hold(4, feat, piece), hold(2, feat // 2, piece), hold(2, feat // 2, piece),
        hold(4, piece, cols), hold(4, piece, cols), hold(2, piece // 2, cols), hold(2, piece // 2, cols),
        wide(share, width), hold(share, width),
        wide(16, width), wide(8, 128), wide(2 * hd, 128), wide(16, half), wide(3, 16, piece), wide(3, 16, piece), wide(7, 8, 128),
        dma((15,)), dma((2 * seqs,)), dma((2 * seqs, 5)), dma((seqs,)), dma((4, 6)), dma((4, 6)), dma((4, 3)), dma((2 + seqs,)),
        dma((2, seqs)), dma((2, seqs)), dma((4,)), dma((4,)), dma((4,)), dma((4,)), dma((2,)), dma(()), dma(()), dma((14,)), dma((14,)),
    ]
    tokens = seqs * span
    return pl.pallas_call(
        functools.partial(backward_kernel, hd, nq, nk, block),
        in_specs=[SMEM] + [any_space] * 19 + [vmem] * 5,
        out_specs=[any_space] * len(big) + [vmem] * 2,
        out_shape=big + small,
        scratch_shapes=scratch,
        compiler_params=pltpu.CompilerParams(vmem_limit_bytes=VMEM_MOST, collective_id=3, has_side_effects=True),
        cost_estimate=cost(4 * tokens * width * (cols + feat), 60 * tokens * width),
        name="attention_backward",
    )(
        lengths, gb, hidden_rows, ffn, ring, xr, n1, tok, outw, qkvw, everything, att, inv, pre, gh, dgate, landx, landy, dup, ddown,
        table, gains, stat, stat2, gain2_part,
    )


def results_kernel(
    hd, nqc, nkc, count,
    sum_gate, sum_up, sum_down, mine_o, lx3, ly3, mine_q, lx4, ly4, gh, xr, fin, finb, own, out, early, gains_ref, lines_ref, small_ref,
    output, gin, ggate, gup, gdown, gout, gq, gk, gv, gain_a, gain_b, gain_q, gain_k, rms,
    gate_i, up_i, down_i, o_i, q_i, gate_o, up_o, down_o, o_o, q_o, gh_v, x_v, fin_v, finb_v, own_v, early_v, out_v,
    in_sem, token_sem, out_sem, place_sem, copy_sem,
):
    row, core, rank = lax.axis_index("dp"), lax.axis_index("context"), lax.axis_index("tensor")
    near = [row, xor_one(row), (row + 2) % 4, 3 - row]
    seqs, share, width = out_v.shape
    last = seqs - 1
    piece = width // 8
    sums = (
        ((sum_gate,), gate_i, gate_o, ((0, ggate),)),
        ((sum_up,), up_i, up_o, ((0, gup),)),
        ((sum_down,), down_i, down_o, ((0, gdown),)),
        ((mine_o, lx3, ly3), o_i, o_o, ((0, gout),)),
        ((mine_q, lx4, ly4), q_i, q_o, ((0, gq), (nqc, gk), (nqc + nkc, gv))),
    )
    simple = [
        (pltpu.make_async_copy(out, out_v, copy_sem.at[0]), pltpu.make_async_copy(out_v, output, copy_sem.at[1])),
        (pltpu.make_async_copy(early, early_v, copy_sem.at[2]), pltpu.make_async_copy(early_v, gin.at[pl.ds(0, last)], copy_sem.at[3])),
    ]

    def loads(i):
        return [pltpu.make_async_copy(src, sums[i][1].at[k], in_sem.at[i, k]) for k, src in enumerate(sums[i][0])]

    mine = pl.ds(pl.multiple_of(rank * share, share), share)
    tokens = [
        pltpu.make_async_copy(src, dst, token_sem.at[k])
        for k, (src, dst) in enumerate(
            ((gh.at[last], gh_v), (xr.at[last, mine, :], x_v), (fin.at[last], fin_v), (finb.at[last], finb_v), (own.at[last], own_v))
        )
    ]
    for i in range(len(sums)):
        for copy in loads(i):
            copy.start()
    for copy in tokens + [first for first, _ in simple]:
        copy.start()

    first = jnp.sum(lines_ref[:8, :], axis=0, keepdims=True)
    second = jnp.sum(lines_ref[8:, :], axis=0, keepdims=True)
    gain_a[...] = first.reshape(gain_a.shape)
    gain_b[...] = second.reshape(gain_b.shape)
    gain_q[...] = small_ref[0:1, :hd].reshape(gain_q.shape)
    gain_k[...] = small_ref[0:1, hd : 2 * hd].reshape(gain_k.shape)
    total = jnp.sum(small_ref[4:5, :], keepdims=True) * count
    for k in range(3):
        square = jnp.sum(small_ref[1 + k : 2 + k, :], keepdims=True) / total
        rms[k] = jnp.max(jnp.sqrt(jnp.broadcast_to(square, (8, 128))))

    stores = []
    for i, (terms, came, total_v, parts) in enumerate(sums):
        for copy in loads(i):
            copy.wait()

        def body(cut, at):
            total_v[cut, :] = sum(came[k, cut, :].astype(F32) for k in range(len(terms)))

        by_pieces(total_v.shape[0], body, tall(total_v))
        for n, (at, dst) in enumerate(parts):
            stores.append(pltpu.make_async_copy(total_v.at[:, pl.ds(at, dst.shape[1])], dst, out_sem.at[i, n]))
            stores[-1].start()
    for first, second in simple:
        first.wait()
        second.start()

    gain = jnp.concatenate([gains_ref[b, 0:1, :] for b in range(8)], axis=1).astype(F32)
    for copy in tokens:
        copy.wait()
    inner = (rank % 3) != 0

    def body(cut, at):
        e = fin_v[cut, :].astype(F32) + own_v[cut, :].astype(F32)
        e = e + jnp.where(inner, finb_v[cut, :].astype(F32), 0.0)
        x = x_v[cut, :].astype(F32)
        inv = inverse_rms(x)
        hat = x * inv
        eg = e * gain
        gh_v[cut, :] = gh_v[cut, :] + inv * (eg - hat * jnp.mean(eg * hat, axis=-1, keepdims=True))

    by_pieces(share, body)
    for o in range(2):
        for k in range(4):
            b = near[k] * 2 + (core if o == 0 else 1 - core)
            cut = pl.ds(pl.multiple_of(b * piece, piece), piece)
            src = gh_v.at[:, pl.ds((o * 4 + k) * piece, piece)]
            stores.append(pltpu.make_async_copy(src, gin.at[last, :, cut], place_sem.at[o * 4 + k]))
            stores[-1].start()
    for copy in stores + [second for _, second in simple]:
        copy.wait()


def finish_results(sums, mine_o, mine_q, lands_o, lands_q, gh, xr, fin, finb, own, out, early, gains, lines, small, hd, nqc, nkc):
    seqs, share, width = out.shape
    hidden = sums[0].shape[1]
    piece = width // 8
    any_space = pl.BlockSpec(memory_space=pl.ANY)
    vmem = pl.BlockSpec(memory_space=pltpu.VMEM)
    dma = pltpu.SemaphoreType.DMA
    blocks = [(piece, hidden), (piece, hidden), (hidden, piece), mine_o.shape, mine_q.shape]
    terms = (1, 1, 1, 3, 3)
    outs = [shape(out.shape, BF16), shape(out.shape, F32)] + [shape(b, F32) for b in blocks[:4]]
    outs += [shape((piece, size), F32) for size in (nqc, nkc, nkc)]
    tiny = [shape((size,), F32) for size in (piece, piece, hd, hd)]
    token = pltpu.VMEM((share, width), BF16)
    return pl.pallas_call(
        functools.partial(results_kernel, hd, nqc, nkc, float(width)),
        in_specs=[any_space] * 16 + [vmem] * 3,
        out_specs=[any_space] * len(outs) + [vmem] * 4 + [SMEM],
        out_shape=outs + tiny + [shape((3,), F32)],
        scratch_shapes=[pltpu.VMEM((n,) + tuple(b), BF16) for n, b in zip(terms, blocks)]
        + [pltpu.VMEM(b, F32) for b in blocks]
        + [pltpu.VMEM((share, width), F32), token, token, token, token, pltpu.VMEM(early.shape, F32), pltpu.VMEM(out.shape, BF16)]
        + [dma((5, 3)), dma((5,)), dma((5, 3)), dma((8,)), dma((4,))],
        compiler_params=PARAMS,
        cost_estimate=cost(30 * piece * hidden, 40 * piece * hidden),
        name="results",
    )(*sums, mine_o, *lands_o, mine_q, *lands_q, gh, xr, fin, finb, own, out, early, gains, lines, small)


def per_device_general(
    inputs,
    cotangent,
    lengths,
    w_query,
    key_projection_weight,
    value_projection_weight,
    w_output,
    w_gate,
    w_up,
    w_down,
    attn_gain,
    ffn_gain,
    query_gain,
    key_gain,
):
    seqs, span, width = inputs.shape
    hd = query_gain.shape[0]
    nq = w_query.shape[1] // hd
    nk = key_projection_weight.shape[1] // hd
    groups = nq // nk
    dp = lax.axis_size("dp")
    tensor = lax.axis_size("tensor")
    core = lax.axis_index("context")
    rank = lax.axis_index("tensor")
    chunks = 2
    rows = span // chunks
    share = span // tensor
    lengths = lengths.astype(jnp.int32)
    start = (core * span).astype(jnp.int32)
    core1 = core.astype(jnp.int32).reshape(1)
    ids = block_order(dp, core)
    order = 2 * dp if (width // (2 * dp)) % 128 == 0 else 1

    positions = start + jnp.arange(span, dtype=jnp.int32)
    freqs = rope_base ** (-(jnp.arange(hd // 2, dtype=F32) * (2.0 / hd)))
    angles = freqs[:, None] * positions.astype(F32)[None, :]
    cosine, sine = jnp.cos(angles), jnp.sin(angles)
    qgain = query_gain.astype(F32).reshape(hd, 1)
    kgain = key_gain.astype(F32).reshape(hd, 1)

    w_qkv = jnp.concatenate([w_query, key_projection_weight, value_projection_weight], axis=1)
    saved = []
    gains = gather_blocks(jnp.stack([attn_gain, ffn_gain]), 1)
    gains = jnp.concatenate([gains[0], gains[1]], axis=1).astype(F32)
    gain1, gain2 = gains[0:1], gains[1:2]
    qkv = gather_blocks(w_qkv, 0)
    out_w = gather_blocks(w_output, 1)
    gate = gather_blocks(w_gate, 0)
    up = gather_blocks(w_up, 0)
    down = gather_blocks(w_down, 1)

    scal = jnp.concatenate([lengths, start.reshape(1), ids])
    x_in, cot_in = inputs, cotangent
    if order == 1:
        x_in, cot_in = to_relative(x_in, dp, core), to_relative(cot_in, dp, core)
    xr, n1, gf = begin(x_in, cot_in, gain1, scal, order)

    parts, tok = [], []
    for s in range(seqs):
        pre, own, oth = heads(n1, s, qkv, cosine, sine, qgain, kgain, core1, hd, nq, nk)
        seq_scal = jnp.stack([lengths[s], core.astype(jnp.int32)])
        everything, att, inv, mine, theirs = attend(seq_scal, own, over_core(oth), groups)
        branched = branch(mine, over_core(theirs), out_w, core1, chunks)
        saved.append((pre, everything, att, inv, seq_scal))
        tok.append(jnp.swapaxes(branched[0], 0, 1))
        parts.append(branched[1:])
    tok = jnp.concatenate(tok, axis=0)

    stats = jnp.zeros((2,), F32)
    hidden_all, n2_all = [], []
    for s in range(seqs):
        for k in range(chunks):
            terms = [lax.psum(parts[s][k], "tensor")]
            place = jnp.stack([lengths[s], start + k * rows])
            hidden, n2, stat = second_norm(place, xr, s, k, gain2, terms)
            hidden_all.append(hidden)
            n2_all.append(n2)
            stats = stats + stat[:2, 0]
    hidden_all, n2_all = jnp.concatenate(hidden_all), jnp.concatenate(n2_all)

    ffn_squares = jnp.zeros((), F32)
    out_shares = []

    def piece_of(arrays):
        per = arrays[0].shape[0] // share

        def piece(k):
            found = lax.dynamic_slice_in_dim(arrays[0], jnp.minimum(k, per - 1) * share, share, 0)
            for m in range(1, len(arrays)):
                here = lax.dynamic_slice_in_dim(arrays[m], jnp.clip(k - m * per, 0, per - 1) * share, share, 0)
                found = jnp.where(k >= m * per, here, found)
            return found

        return piece

    def share_scalars(s):
        head = jnp.stack([rank.astype(jnp.int32), lengths[s], start + rank.astype(jnp.int32) * share, jnp.int32(tensor)])
        return jnp.concatenate([head, ids])

    def flat(nested):
        return [item for inner_list in nested for item in inner_list]

    def slices(array, count):
        size = array.shape[0] // count
        return [array[i * size : (i + 1) * size] for i in range(count)]

    def reduced(lefts, rights, axis):
        oth = weight_grad(lefts, rights, 1, axis)
        own = weight_grad(lefts, rights, 0, axis, over_core(oth))
        return scatter_blocks(own, axis)

    inner, gg, gu, ffn, gn = [[[None] * chunks for _ in range(seqs)] for _ in range(5)]
    for s in range(seqs):
        for k in range(chunks):
            inner[s][k], gg[s][k], gu[s][k], ffn[s][k], gn[s][k] = feed(
                n2_all, s * chunks + k, rows, gf, s, k, gate, up, down
            )
    gain2_grad = jnp.zeros((1, width), F32)
    gb, gh = [[[None] * chunks for _ in range(seqs)] for _ in range(2)]
    for s in range(seqs):
        for k in range(chunks):
            terms = [lax.psum(gn[s][k], "tensor")]
            gb[s][k], gh[s][k], gain_part = second_back(hidden_all, s * chunks + k, gf, s, k, gain2, terms)
            gain2_grad = gain2_grad + gain_part
    gf_list = slices(gf.reshape(seqs * span, width), seqs * chunks)
    n2_list = slices(n2_all, seqs * chunks)
    grad_w_down = reduced(flat(inner), gf_list, 1)
    grad_w_gate = reduced(n2_list, flat(gg), 0)
    grad_w_up = reduced(n2_list, flat(gu), 0)
    for s in range(seqs):
        got = ring_scatter(piece_of(ffn[s]), tensor, rank)
        halves = [hidden_all[(s * chunks + k) * rows : (s * chunks + k + 1) * rows] for k in range(chunks)]
        out, stat = output_share(share_scalars(s), got, ffn[s], halves, order)
        out_shares.append(out)
        ffn_squares = ffn_squares + stat[0, 0]

    gain1_grad = jnp.zeros((1, width), F32)
    head_gain = jnp.zeros((2 * hd,), F32)
    dpres, in_shares = [], []
    for s in range(seqs):
        pre, everything, att, inv, seq_scal = saved[s]
        da_own, da_oth = branch_back(gb[s], out_w, core1)
        d_own, d_oth = attend_back(seq_scal, everything, att, inv, da_own, over_core(da_oth), groups)
        dpre, first, gain_part, hg = heads_back(
            d_own, over_core(d_oth), pre, cosine, sine, qgain, kgain, xr, s, qkv, core1, hd, nq, nk
        )
        gain1_grad = gain1_grad + gain_part
        head_gain = head_gain + hg[:, 0]
        dpres.append(dpre)
        got = ring_scatter(piece_of([first]), tensor, rank)
        in_shares.append(input_share(share_scalars(s), got, first, gh[s], xr, s, gain1, order))

    att_list = [tok[i * rows : (i + 1) * rows] for i in range(seqs * chunks)]
    grad_w_output = reduced(att_list, flat(gb), 1)
    grad_qkv = reduced([n1[s] for s in range(seqs)], dpres, 0)
    nqc, nkc = nq * hd, nk * hd
    grad_w_query = grad_qkv[:, :nqc]
    grad_w_key = grad_qkv[:, nqc : nqc + nkc]
    grad_w_value = grad_qkv[:, nqc + nkc :]

    gain2_grad = gain2_grad / tensor
    counts = jnp.sum(jnp.clip(lengths - start, 0, span)).astype(F32) / tensor
    small = jnp.concatenate([head_gain, stats / tensor, ffn_squares.reshape(1), counts.reshape(1)])
    small = jnp.pad(small, (0, (-small.shape[0]) % 128)).reshape(1, -1)
    lines = jnp.concatenate([gain1_grad, gain2_grad], axis=0)
    piece = width // (2 * dp)
    lines = to_absolute(lines, dp, core)
    lines, small = lax.psum((lines, small), ("dp", "context", "tensor"))
    lines = lax.dynamic_slice_in_dim(lines, lax.axis_index(("dp", "context")) * piece, piece, 1)
    small = small[0]
    rms_values = jnp.sqrt(small[2 * hd : 2 * hd + 3] / (small[2 * hd + 3] * width))

    output = jnp.stack(out_shares)
    grad_inputs = jnp.stack(in_shares)
    if order == 1:
        output, grad_inputs = to_absolute(output, dp, core), to_absolute(grad_inputs, dp, core)
    return (
        output,
        grad_inputs,
        grad_w_query,
        grad_w_key,
        grad_w_value,
        grad_w_output,
        grad_w_gate,
        grad_w_up,
        grad_w_down,
        lines[0],
        lines[1],
        small[:hd],
        small[hd : 2 * hd],
        rms_values,
    )


def per_device_square(
    inputs,
    cotangent,
    lengths,
    w_query,
    key_projection_weight,
    value_projection_weight,
    w_output,
    w_gate,
    w_up,
    w_down,
    attn_gain,
    ffn_gain,
    query_gain,
    key_gain,
):
    seqs, span, width = inputs.shape
    hd = query_gain.shape[0]
    nq = w_query.shape[1] // hd
    nk = key_projection_weight.shape[1] // hd
    lengths = lengths.astype(jnp.int32)
    all_gains = (attn_gain, ffn_gain, query_gain, key_gain)
    (
        xr, n1, gf, qkv, out_w, gate, up, down, hidden, n2, rest, came, gi, pre, everything, att, tok, gains, table, inv, stat
    ) = forward(
        lengths, inputs, cotangent, w_query, key_projection_weight, value_projection_weight, w_output, w_gate, w_up, w_down,
        all_gains, hd, nq, nk,
    )
    tokens = seqs * span
    flat = lambda a: a.reshape(tokens, -1)
    ffn, gb, gh, d_gate, d_up, d_down, hidden, landx, landy, ring, gain2_part, stat2 = feed_both(
        lengths, n2, flat(gf), gate, up, down, gi, rest, came, flat(xr), hidden, gains
    )
    (
        output, early, fin, finb, own, sum_gate, sum_up, sum_down, mine_o, mine_q, _, _, _, _, lx3, ly3, lx4, ly4, lines, small
    ) = backward(
        lengths, gb, hidden, ffn, ring, xr, flat(n1), flat(tok), out_w, qkv,
        everything, att, inv, pre, gh, d_gate, landx, landy, d_up, d_down, table, gains, stat, stat2, gain2_part, hd, nq, nk,
    )
    nqc, nkc = nq * hd, nk * hd
    output, grad_inputs, grad_gate, grad_up, grad_down, grad_out, grad_q, grad_k, grad_v, *small = finish_results(
        (sum_gate, sum_up, sum_down), mine_o, mine_q, (lx3, ly3), (lx4, ly4), gh, xr, fin, finb, own, output, early, gains,
        lines, small, hd, nqc, nkc,
    )
    return (output, grad_inputs, grad_q, grad_k, grad_v, grad_out, grad_gate, grad_up, grad_down, *small)


def per_device(*args):
    inputs, w_query = args[0], args[3]
    seqs, span, width = inputs.shape
    square = lax.axis_size("dp") == 4 and lax.axis_size("tensor") == 4 and lax.axis_size("context") == 2
    if square and width % 2048 == 0 and span % 512 == 0 and seqs == 2 and w_query.shape[1] == span:
        return per_device_square(*args)
    return per_device_general(*args)


def solution(mesh):
    both = ("dp", "context")
    rows = P(both, "tensor")
    cols = P("tensor", both)
    shares = P("dp", ("context", "tensor"), None)
    acts = P("dp", "context", None)
    return jax.shard_map(
        per_device,
        mesh=mesh,
        in_specs=(acts, acts, P("dp"), rows, rows, rows, cols, rows, rows, cols, P(both), P(both), P(), P()),
        out_specs=(shares, shares, rows, rows, rows, cols, rows, rows, cols, P(both), P(both), P(), P(), P()),
        check_vma=False,
    )
```

```python
import functools
import math

import jax
import jax.numpy as jnp
from jax import lax
from jax.experimental import pallas as pl
from jax.experimental.pallas import tpu as pltpu
from jax.sharding import PartitionSpec as P

F32 = jnp.float32
BF16 = jnp.bfloat16
epsilon = 1e-05
rope_base = 1000000.0
log2e = 1.4426950408889634
VMEM_BYTES = 60 * 1024 * 1024
VMEM_MOST = 63 * 1024 * 1024
PARAMS = pltpu.CompilerParams(vmem_limit_bytes=VMEM_BYTES)
SMEM = pl.BlockSpec(memory_space=pltpu.SMEM)
SWAP = ((0, 1), (1, 0))


def shape(dims, dtype):
    return jax.ShapeDtypeStruct(tuple(dims), dtype)


def cost(flops, size, exps=0):
    return pl.CostEstimate(flops=int(flops), bytes_accessed=int(size), transcendentals=int(exps))


def dot_nn(a, b):
    return lax.dot_general(a, b, (((1,), (0,)), ((), ())), preferred_element_type=F32)


def dot_nt(a, b):
    return lax.dot_general(a, b, (((1,), (1,)), ((), ())), preferred_element_type=F32)


def dot_tn(a, b):
    return lax.dot_general(a, b, (((0,), (0,)), ((), ())), preferred_element_type=F32)


def inverse_rms(values):
    return lax.rsqrt(jnp.mean(values * values, axis=-1, keepdims=True) + epsilon)


def block_order(dp, core):
    return jnp.stack([jnp.int32(k) * 2 + (core ^ o) for o in range(2) for k in range(dp)]).astype(jnp.int32)


def to_relative(values, dp, core):
    lead = values.shape[:-1]
    parts = values.reshape(lead + (dp, 2, -1))
    parts = jnp.where(core == 0, parts, parts[..., ::-1, :])
    return jnp.swapaxes(parts, -3, -2).reshape(values.shape)


def to_absolute(values, dp, core):
    lead = values.shape[:-1]
    parts = jnp.swapaxes(values.reshape(lead + (2, dp, -1)), -3, -2)
    return jnp.where(core == 0, parts, parts[..., ::-1, :]).reshape(values.shape)


def over_core(value):
    return lax.ppermute(value, "context", SWAP)


def gather_blocks(weight, axis):
    own = lax.all_gather(weight, "dp", axis=axis, tiled=True)
    return jnp.stack([own, over_core(own)])


def scatter_blocks(total, axis):
    return lax.psum_scatter(total, "dp", scatter_dimension=axis, tiled=True).astype(F32)


def ring_scatter(piece, tensor, rank):
    ring = [(i, (i + 1) % tensor) for i in range(tensor)]
    moving = piece((rank + tensor - 1) % tensor)
    for step in range(1, tensor):
        moving = lax.ppermute(moving, "tensor", ring)
        if step < tensor - 1:
            moving = (moving.astype(F32) + piece((rank + tensor - 1 - step) % tensor).astype(F32)).astype(BF16)
    return moving


def begin_kernel(order, x_ref, cot_ref, gain_ref, scal_ref, xr_ref, n1_ref, gf_ref):
    seq, tile = pl.program_id(0), pl.program_id(1)
    rows, width = x_ref.shape[1:]
    seqs = pl.num_programs(0)
    place = scal_ref[seqs] + tile * rows + lax.broadcasted_iota(jnp.int32, (rows, 1), 0)
    valid = (place < scal_ref[seq]).astype(F32)
    x = x_ref[0].astype(F32)
    inv = inverse_rms(x)
    piece = width // order
    for k in range(order):
        src = pl.ds(pl.multiple_of(scal_ref[seqs + 1 + k] * piece, piece), piece) if order > 1 else slice(0, width)
        dst = slice(k * piece, (k + 1) * piece)
        part = x_ref[0, :, src]
        xr_ref[0, :, dst] = part
        n1_ref[0, :, dst] = (part.astype(F32) * inv * gain_ref[:, dst]).astype(BF16)
        gf_ref[0, :, dst] = (cot_ref[0, :, src].astype(F32) * valid).astype(BF16)


def begin(x, cot, gain, scalars, order):
    seqs, span, width = x.shape
    rows = min(256, span)
    spec = pl.BlockSpec((1, rows, width), lambda s, i: (s, i, 0))
    return pl.pallas_call(
        functools.partial(begin_kernel, order),
        grid=(seqs, span // rows),
        in_specs=[spec, spec, pl.BlockSpec((1, width), lambda s, i: (0, 0)), SMEM],
        out_specs=[spec] * 3,
        out_shape=[shape(x.shape, BF16)] * 3,
        compiler_params=PARAMS,
        cost_estimate=cost(8 * x.size, 10 * x.size),
        name="first_norm",
    )(x, cot, gain, scalars)


def heads_kernel(hd, nq, nk, n1_ref, w_ref, cos_ref, sin_ref, qg_ref, kg_ref, core_ref, pre_ref, own_ref, oth_ref):
    half = w_ref.shape[1]
    x = n1_ref[0]
    flat = dot_nn(x[:, :half], w_ref[0]) + dot_nn(x[:, half:], w_ref[1])
    turned = flat.T
    span = turned.shape[1]
    normed = turned[: (nq + nk) * hd]
    pre_ref[...] = normed
    core = core_ref[0]
    cosine, sine = cos_ref[...], sin_ref[...]
    done = []
    for h in range(nq + nk):
        v = normed[h * hd : (h + 1) * hd]
        inv = lax.rsqrt(jnp.mean(v * v, axis=0, keepdims=True) + epsilon)
        v = v * inv * (qg_ref[...] if h < nq else kg_ref[...])
        a, b = v[: hd // 2], v[hd // 2 :]
        done.append(jnp.concatenate([a * cosine - b * sine, b * cosine + a * sine], axis=0))
    for h in range(nk):
        lo = (nq + nk + h) * hd
        done.append(turned[lo : lo + hd])
    parts = [[], []]
    for start, count in ((0, nq), (nq, nk), (nq + nk, nk)):
        for side in range(2):
            parts[side] += done[start + side * count // 2 : start + (side + 1) * count // 2]
    low = jnp.concatenate(parts[0], axis=0)
    high = jnp.concatenate(parts[1], axis=0)
    first = core == 0
    own_ref[...] = jnp.where(first, low, high).astype(BF16)
    oth_ref[...] = jnp.where(first, high, low).astype(BF16)


def heads(n1, seq, weight, cosine, sine, qgain, kgain, core, hd, nq, nk):
    span, width = n1.shape[1:]
    sides = (nq + 2 * nk) * hd // 2
    full = pl.BlockSpec(memory_space=pltpu.VMEM)
    whole = lambda a: pl.BlockSpec(a.shape, lambda i: (0,) * a.ndim)
    outs = [shape(((nq + nk) * hd, span), F32), shape((sides, span), BF16), shape((sides, span), BF16)]
    return pl.pallas_call(
        functools.partial(heads_kernel, hd, nq, nk),
        grid=(1,),
        in_specs=[pl.BlockSpec((1, span, width), lambda i: (seq, 0, 0))]
        + [whole(a) for a in (weight, cosine, sine, qgain, kgain)]
        + [SMEM],
        out_specs=[whole(o) for o in outs],
        out_shape=outs,
        compiler_params=PARAMS,
        cost_estimate=cost(2 * span * width * weight.shape[2], 2 * span * width + 2 * weight.size),
        name="query_key_value",
    )(n1, weight, cosine, sine, qgain, kgain, core)


def join_positions(core, own, oth):
    first = core == 0
    return jnp.where(first, own, oth), jnp.where(first, oth, own)


def attend_kernel(block, groups, scal_ref, own_ref, got_ref, all_ref, att_ref, inv_ref, ao_ref, ax_ref):
    span = own_ref.shape[1]
    hd = own_ref.shape[0] // (groups + 2)
    length, core = scal_ref[0], scal_ref[1]
    low, high = join_positions(core, own_ref[...], got_ref[...])
    all_ref[:, :span] = low
    all_ref[:, span:] = high
    scale = log2e / math.sqrt(hd)
    krow = lax.broadcasted_iota(jnp.int32, (block, groups * block), 0)
    qcol = lax.broadcasted_iota(jnp.int32, (block, groups * block), 1) % block
    base = groups * hd
    for i in range(2 * span // block):
        cut = slice(i * block, (i + 1) * block)
        q = jnp.concatenate([all_ref[g * hd : (g + 1) * hd, cut] for g in range(groups)], axis=1)
        acc = jnp.zeros((hd, groups * block), F32)
        total = jnp.zeros((1, groups * block), F32)
        for j in range(i + 1):
            kcut = slice(j * block, (j + 1) * block)
            s = dot_tn(all_ref[base : base + hd, kcut], q) * scale
            ok = (krow + j * block) < length
            if j == i:
                ok = ok & (krow <= qcol)
            e = jnp.where(ok, jnp.exp2(s), 0.0)
            total = total + jnp.sum(e, axis=0, keepdims=True)
            acc = acc + dot_nn(all_ref[base + hd : base + 2 * hd, kcut], e.astype(BF16))
        inv = 1.0 / total
        att = (acc * inv).astype(BF16)
        for g in range(groups):
            att_ref[g * hd : (g + 1) * hd, cut] = att[:, g * block : (g + 1) * block]
            inv_ref[g : g + 1, cut] = inv[:, g * block : (g + 1) * block]
    mine, theirs = join_positions(core, att_ref[:, :span], att_ref[:, span:])
    ao_ref[...] = mine
    ax_ref[...] = theirs


def attend(scalars, own, got, groups):
    rows, span = own.shape
    hd = rows // (groups + 2)
    block = min(256, span)
    full = pl.BlockSpec(memory_space=pltpu.VMEM)
    return pl.pallas_call(
        functools.partial(attend_kernel, block, groups),
        in_specs=[SMEM, full, full],
        out_specs=[full] * 5,
        out_shape=[
            shape((rows, 2 * span), BF16),
            shape((groups * hd, 2 * span), BF16),
            shape((groups, 2 * span), F32),
            shape((groups * hd, span), BF16),
            shape((groups * hd, span), BF16),
        ],
        compiler_params=PARAMS,
        cost_estimate=cost(60 * groups * hd * span * span, 12 * rows * span, 4 * groups * span * span),
        name="attend_forward",
    )(scalars, own, got)


def branch_kernel(own_ref, got_ref, w_ref, core_ref, att_ref, *outs):
    half = w_ref.shape[2]
    low, high = join_positions(core_ref[0], own_ref[...], got_ref[...])
    att = jnp.concatenate([low, high], axis=0)
    att_ref[...] = att
    rows = outs[0].shape[0]
    for k, out in enumerate(outs):
        part = att[:, k * rows : (k + 1) * rows]
        out[:, :half] = dot_tn(part, w_ref[0]).astype(BF16)
        out[:, half:] = dot_tn(part, w_ref[1]).astype(BF16)


def branch(own, got, weight, core, chunks):
    rows, span = own.shape
    width = 2 * weight.shape[2]
    full = pl.BlockSpec(memory_space=pltpu.VMEM)
    return pl.pallas_call(
        branch_kernel,
        in_specs=[full] * 3 + [SMEM],
        out_specs=[full] * (1 + chunks),
        out_shape=[shape((2 * rows, span), BF16)] + [shape((span // chunks, width), BF16)] * chunks,
        compiler_params=PARAMS,
        cost_estimate=cost(4 * rows * span * width, 4 * rows * width + 2 * span * width),
        name="attention_branch",
    )(own, got, weight, core)


def second_norm_kernel(terms, scal_ref, x_ref, gain_ref, *refs):
    term_refs, (hidden_ref, n2_ref, stat_ref) = refs[:terms], refs[terms:]
    rows = hidden_ref.shape[0]
    branch_sum = term_refs[0][...].astype(F32)
    for ref in term_refs[1:]:
        branch_sum = branch_sum + ref[...].astype(F32)
    resid = x_ref[0].astype(F32)
    hidden = resid + branch_sum
    hidden_ref[...] = hidden
    n2_ref[...] = (hidden * inverse_rms(hidden) * gain_ref[...]).astype(BF16)
    place = scal_ref[1] + lax.broadcasted_iota(jnp.int32, (rows, 1), 0)
    valid = (place < scal_ref[0]).astype(F32)
    first = jnp.sum(valid * resid * resid, keepdims=True)
    second = jnp.sum(valid * branch_sum * branch_sum, keepdims=True)
    line = lax.broadcasted_iota(jnp.int32, (8, 128), 0)
    stat_ref[...] = jnp.where(line == 0, first, second)


def second_norm(scalars, xr, seq, part, gain, terms):
    rows, width = terms[0].shape
    flat = pl.BlockSpec((rows, width), lambda i: (0, 0))
    return pl.pallas_call(
        functools.partial(second_norm_kernel, len(terms)),
        grid=(1,),
        in_specs=[SMEM, pl.BlockSpec((1, rows, width), lambda i: (seq, part, 0)), pl.BlockSpec((1, width), lambda i: (0, 0))]
        + [flat] * len(terms),
        out_specs=[flat, flat, pl.BlockSpec((8, 128), lambda i: (0, 0))],
        out_shape=[shape((rows, width), F32), shape((rows, width), BF16), shape((8, 128), F32)],
        compiler_params=PARAMS,
        cost_estimate=cost(20 * rows * width, (8 + 2 * len(terms)) * rows * width),
        name="second_norm",
    )(scalars, xr, gain, *terms)


def feed_kernel(n_ref, g_ref, wgo, wgx, wuo, wux, wdo, wdx, inner_ref, gg_ref, gu_ref, ffn_ref, gn_ref, facc, gacc):
    step = pl.program_id(0)
    half = wgo.shape[0]
    no, nx = n_ref[:, :half], n_ref[:, half:]
    gate = dot_nn(no, wgo[...]) + dot_nn(nx, wgx[...])
    up = dot_nn(no, wuo[...]) + dot_nn(nx, wux[...])
    gi = dot_nt(g_ref[0, :, :half], wdo[...]) + dot_nt(g_ref[0, :, half:], wdx[...])
    sig = jax.nn.sigmoid(gate)
    silu = gate * sig
    inner = (silu * up).astype(BF16)
    gg = (gi * up * sig * (1.0 + gate * (1.0 - sig))).astype(BF16)
    gu = (gi * silu).astype(BF16)
    inner_ref[...] = inner
    gg_ref[...] = gg
    gu_ref[...] = gu

    @pl.when(step == 0)
    def _():
        facc[...] = jnp.zeros_like(facc)
        gacc[...] = jnp.zeros_like(gacc)

    facc[:, :half] += dot_nn(inner, wdo[...])
    facc[:, half:] += dot_nn(inner, wdx[...])
    gacc[:, :half] += dot_nt(gg, wgo[...]) + dot_nt(gu, wuo[...])
    gacc[:, half:] += dot_nt(gg, wgx[...]) + dot_nt(gu, wux[...])

    @pl.when(step == pl.num_programs(0) - 1)
    def _():
        ffn_ref[...] = facc[...].astype(BF16)
        gn_ref[...] = gacc[...].astype(BF16)


def feed(n2, chunk, rows, gf, seq, part, gate, up, down):
    width = n2.shape[1]
    _, half, hidden = gate.shape
    hb = min(512, hidden)
    row = [pl.BlockSpec((None, half, hb), lambda h, side=side: (side, 0, h)) for side in range(2)]
    col = [pl.BlockSpec((None, hb, half), lambda h, side=side: (side, h, 0)) for side in range(2)]
    whole = pl.BlockSpec((rows, width), lambda h: (0, 0))
    tile = pl.BlockSpec((rows, hb), lambda h: (0, h))
    return pl.pallas_call(
        feed_kernel,
        grid=(hidden // hb,),
        in_specs=[pl.BlockSpec((rows, width), lambda h: (chunk, 0)), pl.BlockSpec((1, rows, width), lambda h: (seq, part, 0))] + row + row + col,
        out_specs=[tile, tile, tile, whole, whole],
        out_shape=[shape((rows, hidden), BF16)] * 3 + [shape((rows, width), BF16)] * 2,
        scratch_shapes=[pltpu.VMEM((rows, width), F32), pltpu.VMEM((rows, width), F32)],
        compiler_params=PARAMS,
        cost_estimate=cost(12 * rows * width * hidden, 12 * half * hidden + 14 * rows * width, rows * hidden),
        name="feed_forward",
    )(n2, gf, gate, gate, up, up, down, down)


def second_back_kernel(terms, hidden_ref, gf_ref, gain_ref, *refs):
    term_refs, (gb_ref, gh_ref, gain_out) = refs[:terms], refs[terms:]
    e = term_refs[0][...].astype(F32)
    for ref in term_refs[1:]:
        e = e + ref[...].astype(F32)
    hidden = hidden_ref[...]
    inv = inverse_rms(hidden)
    hat = hidden * inv
    eg = e * gain_ref[...]
    gh = gf_ref[0].astype(F32) + inv * (eg - hat * jnp.mean(eg * hat, axis=-1, keepdims=True))
    gh_ref[...] = gh
    gb_ref[...] = gh.astype(BF16)
    gain_out[...] = jnp.sum(e * hat, axis=0, keepdims=True)


def second_back(hidden, chunk, gf, seq, part, gain, terms):
    rows, width = terms[0].shape
    flat = pl.BlockSpec((rows, width), lambda i: (0, 0))
    line = pl.BlockSpec((1, width), lambda i: (0, 0))
    return pl.pallas_call(
        functools.partial(second_back_kernel, len(terms)),
        grid=(1,),
        in_specs=[pl.BlockSpec((rows, width), lambda i: (chunk, 0)), pl.BlockSpec((1, rows, width), lambda i: (seq, part, 0)), line]
        + [flat] * len(terms),
        out_specs=[flat, flat, line],
        out_shape=[shape((rows, width), BF16), shape((rows, width), F32), shape((1, width), F32)],
        compiler_params=PARAMS,
        cost_estimate=cost(20 * rows * width, (12 + 2 * len(terms)) * rows * width),
        name="second_norm_back",
    )(hidden, gf, gain, *terms)


def branch_back_kernel(chunks, *refs):
    gb_refs, (w_ref, core_ref, own_ref, oth_ref) = refs[:chunks], refs[chunks:]
    half = w_ref.shape[2]
    rows = gb_refs[0].shape[0]
    heads_half = own_ref.shape[0]
    first = core_ref[0] == 0
    for k, ref in enumerate(gb_refs):
        da = dot_nt(w_ref[0], ref[:, :half]) + dot_nt(w_ref[1], ref[:, half:])
        da = da.astype(BF16)
        low, high = da[:heads_half], da[heads_half:]
        cut = slice(k * rows, (k + 1) * rows)
        own_ref[:, cut] = jnp.where(first, low, high)
        oth_ref[:, cut] = jnp.where(first, high, low)


def branch_back(gbs, weight, core):
    chunks = len(gbs)
    rows, width = gbs[0].shape
    dim = weight.shape[1]
    full = pl.BlockSpec(memory_space=pltpu.VMEM)
    return pl.pallas_call(
        functools.partial(branch_back_kernel, chunks),
        in_specs=[full] * (chunks + 1) + [SMEM],
        out_specs=[full] * 2,
        out_shape=[shape((dim // 2, chunks * rows), BF16)] * 2,
        compiler_params=PARAMS,
        cost_estimate=cost(2 * dim * chunks * rows * width, 2 * dim * width + 2 * chunks * rows * width),
        name="attention_branch_back",
    )(*gbs, weight, core)


def attend_back_kernel(block, groups, scal_ref, all_ref, att_ref, inv_ref, own_ref, got_ref, out_own, out_oth, da_all, grads):
    span = own_ref.shape[1]
    hd = all_ref.shape[0] // (groups + 2)
    length, core = scal_ref[0], scal_ref[1]
    low, high = join_positions(core, own_ref[...], got_ref[...])
    da_all[:, :span] = low
    da_all[:, span:] = high
    scale = log2e / math.sqrt(hd)
    back = 1.0 / math.sqrt(hd)
    krow = lax.broadcasted_iota(jnp.int32, (block, groups * block), 0)
    qcol = lax.broadcasted_iota(jnp.int32, (block, groups * block), 1) % block
    base = groups * hd
    grads[base:, :] = jnp.zeros((2 * hd, 2 * span), F32)
    for i in range(2 * span // block):
        cut = slice(i * block, (i + 1) * block)

        def rows(ref):
            return jnp.concatenate([ref[g * hd : (g + 1) * hd, cut] for g in range(groups)], axis=1)

        q = rows(all_ref)
        da = rows(da_all)
        inv = jnp.concatenate([inv_ref[g : g + 1, cut] for g in range(groups)], axis=1)
        delta = jnp.sum(rows(att_ref).astype(F32) * da.astype(F32), axis=0, keepdims=True)
        dq = jnp.zeros((hd, groups * block), F32)
        for j in range(i + 1):
            kcut = slice(j * block, (j + 1) * block)
            key = all_ref[base : base + hd, kcut]
            s = dot_tn(key, q) * scale
            ok = (krow + j * block) < length
            if j == i:
                ok = ok & (krow <= qcol)
            p = jnp.where(ok, jnp.exp2(s) * inv, 0.0)
            dp = dot_tn(all_ref[base + hd : base + 2 * hd, kcut], da)
            ds = (p * (dp - delta)).astype(BF16)
            dq = dq + dot_nn(key, ds)
            grads[base : base + hd, kcut] += dot_nt(q, ds) * back
            grads[base + hd : base + 2 * hd, kcut] += dot_nt(da, p.astype(BF16))
        dq = dq * back
        for g in range(groups):
            grads[g * hd : (g + 1) * hd, cut] = dq[:, g * block : (g + 1) * block]
    mine, theirs = join_positions(core, grads[:, :span], grads[:, span:])
    out_own[...] = mine.astype(BF16)
    out_oth[...] = theirs.astype(BF16)


def attend_back(scalars, everything, att, inv, own, got, groups):
    rows, slots = everything.shape
    span = slots // 2
    block = min(256, span)
    full = pl.BlockSpec(memory_space=pltpu.VMEM)
    return pl.pallas_call(
        functools.partial(attend_back_kernel, block, groups),
        in_specs=[SMEM] + [full] * 5,
        out_specs=[full] * 2,
        out_shape=[shape((rows, span), BF16)] * 2,
        scratch_shapes=[pltpu.VMEM(att.shape, BF16), pltpu.VMEM((rows, slots), F32)],
        compiler_params=PARAMS,
        cost_estimate=cost(30 * att.shape[0] * slots * slots, 12 * rows * slots, groups * slots * slots),
        name="attend_backward",
    )(scalars, everything, att, inv, own, got)


def heads_back_kernel(hd, nq, nk, own_ref, got_ref, pre_ref, cos_ref, sin_ref, qg_ref, kg_ref, x_ref, w_ref, core_ref, dpre_ref, first_ref, gain_ref, hgain_ref):
    half = w_ref.shape[1]
    low, high = join_positions(core_ref[0], own_ref[...].astype(F32), got_ref[...].astype(F32))
    sides = (nq // 2, nk // 2, nk // 2)
    grads = [[], [], []]
    for side in (low, high):
        at = 0
        for kind, count in enumerate(sides):
            for h in range(count):
                grads[kind].append(side[at : at + hd])
                at += hd
    cosine, sine = cos_ref[...], sin_ref[...]
    done = []
    sums = [0.0, 0.0]
    for h in range(nq + nk):
        kind = 0 if h < nq else 1
        g = grads[kind][h - kind * nq]
        a, b = g[: hd // 2], g[hd // 2 :]
        g = jnp.concatenate([a * cosine + b * sine, b * cosine - a * sine], axis=0)
        v = pre_ref[h * hd : (h + 1) * hd, :]
        inv = lax.rsqrt(jnp.mean(v * v, axis=0, keepdims=True) + epsilon)
        hat = v * inv
        sums[kind] = sums[kind] + jnp.sum(g * hat, axis=1, keepdims=True)
        gg = g * (qg_ref[...] if kind == 0 else kg_ref[...])
        done.append(inv * (gg - hat * jnp.mean(gg * hat, axis=0, keepdims=True)))
    done += grads[2]
    hgain_ref[:hd, :] = jnp.broadcast_to(sums[0], (hd, 128))
    hgain_ref[hd:, :] = jnp.broadcast_to(sums[1], (hd, 128))
    dpre = jnp.concatenate(done, axis=0).T.astype(BF16)
    dpre_ref[...] = dpre
    x = x_ref[0].astype(F32)
    hat = x * inverse_rms(x)
    for k in range(2):
        cut = slice(k * half, (k + 1) * half)
        part = dot_nt(dpre, w_ref[k])
        first_ref[:, cut] = part.astype(BF16)
        gain_ref[:, cut] = jnp.sum(part * hat[:, cut], axis=0, keepdims=True)


def heads_back(own, got, pre, cosine, sine, qgain, kgain, xr, seq, weight, core, hd, nq, nk):
    span = own.shape[1]
    _, half, cols = weight.shape
    width = 2 * half
    whole = lambda a: pl.BlockSpec(a.shape, lambda i: (0,) * len(a.shape))
    outs = [shape((span, cols), BF16), shape((span, width), BF16), shape((1, width), F32), shape((2 * hd, 128), F32)]
    return pl.pallas_call(
        functools.partial(heads_back_kernel, hd, nq, nk),
        grid=(1,),
        in_specs=[whole(a) for a in (own, got, pre, cosine, sine, qgain, kgain)]
        + [pl.BlockSpec((1, span, width), lambda i: (seq, 0, 0)), whole(weight), SMEM],
        out_specs=[whole(o) for o in outs],
        out_shape=outs,
        compiler_params=PARAMS,
        cost_estimate=cost(2 * span * width * cols, 4 * span * width + 4 * half * cols),
        name="query_key_value_back",
    )(own, got, pre, cosine, sine, qgain, kgain, xr, weight, core)


def place_blocks(order, ids, first_id, value, out_ref):
    piece = value.shape[-1] // order
    for k in range(order):
        if order == 1:
            out_ref[...] = value
        else:
            dst = pl.ds(pl.multiple_of(ids[first_id + k] * piece, piece), piece)
            out_ref[:, dst] = value[:, k * piece : (k + 1) * piece]


def output_kernel(order, scal_ref, got_ref, f0_ref, f1_ref, h0_ref, h1_ref, out_ref, stat_ref):
    low = scal_ref[0] * 2 < scal_ref[3]
    rows = out_ref.shape[0]
    ffn = got_ref[...].astype(F32) + jnp.where(low, f0_ref[...], f1_ref[...]).astype(F32)
    hidden = jnp.where(low, h0_ref[...], h1_ref[...])
    place = scal_ref[2] + lax.broadcasted_iota(jnp.int32, (rows, 1), 0)
    valid = (place < scal_ref[1]).astype(F32)
    stat_ref[...] = jnp.broadcast_to(jnp.sum(valid * ffn * ffn, keepdims=True), (8, 128))
    place_blocks(order, scal_ref, 4, (hidden + ffn).astype(BF16), out_ref)


def share_specs(rows, width, per):
    return [
        pl.BlockSpec((rows, width), lambda i, s: (jnp.minimum(s[0], per - 1), 0)),
        pl.BlockSpec((rows, width), lambda i, s: (jnp.maximum(s[0] - per, 0), 0)),
    ]


def output_share(scalars, got, ffns, hiddens, order):
    rows, width = got.shape
    pair = share_specs(rows, width, ffns[0].shape[0] // rows)
    flat = pl.BlockSpec((rows, width), lambda i, s: (0, 0))
    return pl.pallas_call(
        functools.partial(output_kernel, order),
        grid_spec=pltpu.PrefetchScalarGridSpec(
            num_scalar_prefetch=1,
            grid=(1,),
            in_specs=[flat] + pair + pair,
            out_specs=[flat, pl.BlockSpec((8, 128), lambda i, s: (0, 0))],
        ),
        out_shape=[shape((rows, width), BF16), shape((8, 128), F32)],
        compiler_params=PARAMS,
        cost_estimate=cost(6 * rows * width, 16 * rows * width),
        name="output_share",
    )(scalars, got, *ffns, *hiddens)


def input_kernel(order, scal_ref, got_ref, part_ref, g0_ref, g1_ref, x_ref, gain_ref, out_ref):
    low = scal_ref[0] * 2 < scal_ref[3]
    e = got_ref[...].astype(F32) + part_ref[...].astype(F32)
    gh = jnp.where(low, g0_ref[...], g1_ref[...])
    x = x_ref[0].astype(F32)
    inv = inverse_rms(x)
    hat = x * inv
    eg = e * gain_ref[...]
    value = gh + inv * (eg - hat * jnp.mean(eg * hat, axis=-1, keepdims=True))
    place_blocks(order, scal_ref, 4, value, out_ref)


def input_share(scalars, got, part, ghs, xr, seq, gain, order):
    rows, width = got.shape
    pair = share_specs(rows, width, ghs[0].shape[0] // rows)
    flat = pl.BlockSpec((rows, width), lambda i, s: (0, 0))
    return pl.pallas_call(
        functools.partial(input_kernel, order),
        grid_spec=pltpu.PrefetchScalarGridSpec(
            num_scalar_prefetch=1,
            grid=(1,),
            in_specs=[flat, pl.BlockSpec((rows, width), lambda i, s: (s[0], 0))]
            + pair
            + [pl.BlockSpec((1, rows, width), lambda i, s: (seq, s[0], 0)), pl.BlockSpec((1, width), lambda i, s: (0, 0))],
            out_specs=flat,
        ),
        out_shape=shape((rows, width), F32),
        compiler_params=PARAMS,
        cost_estimate=cost(12 * rows * width, 20 * rows * width),
        name="input_share",
    )(scalars, got, part, *ghs, xr, gain)


def weight_grad_kernel(count, extra, *refs):
    a_refs, b_refs, out = refs[:count], refs[count : 2 * count], refs[-1]
    total = dot_tn(a_refs[0][...], b_refs[0][...])
    for a, b in zip(a_refs[1:], b_refs[1:]):
        total = total + dot_tn(a[...], b[...])
    if extra:
        total = total + refs[2 * count][...].astype(F32)
    out[...] = total.astype(BF16)


def weight_grad(lefts, rights, side, axis, add=None):
    count = len(lefts)
    rows_all, cols_all = lefts[0].shape[1], rights[0].shape[1]
    dims = [rows_all, cols_all]
    dims[axis] //= 2
    rows, cols = min(512, dims[0]), min(2048, dims[1])
    row_at = side * (dims[0] // rows) if axis == 0 else 0
    col_at = side * (dims[1] // cols) if axis == 1 else 0
    specs = [pl.BlockSpec((a.shape[0], rows), lambda j, i: (0, i + row_at)) for a in lefts]
    specs += [pl.BlockSpec((b.shape[0], cols), lambda j, i: (0, j + col_at)) for b in rights]
    tile = pl.BlockSpec((rows, cols), lambda j, i: (i, j))
    tokens = sum(a.shape[0] for a in lefts)
    return pl.pallas_call(
        functools.partial(weight_grad_kernel, count, add is not None),
        grid=(dims[1] // cols, dims[0] // rows),
        in_specs=specs + ([tile] if add is not None else []),
        out_specs=tile,
        out_shape=shape(dims, BF16),
        compiler_params=PARAMS,
        cost_estimate=cost(2 * tokens * dims[0] * dims[1], 2 * tokens * sum(dims) + 2 * dims[0] * dims[1]),
        name="weight_grad",
    )(*lefts, *rights, *([add] if add is not None else []))


def xor_one(index):
    return index + 1 - 2 * (index % 2)


def remote(src, dst, send, recv, device):
    return pltpu.make_async_remote_copy(
        src_ref=src, dst_ref=dst, send_sem=send, recv_sem=recv, device_id=device, device_id_type=pl.DeviceIdType.MESH
    )


def greet(others):
    barrier = pltpu.get_barrier_semaphore()
    count = 0
    for needed, device in others:
        if needed is None:
            pl.semaphore_signal(barrier, inc=1, device_id=device, device_id_type=pl.DeviceIdType.MESH)
            count = count + 1
        else:

            @pl.when(needed)
            def _():
                pl.semaphore_signal(barrier, inc=1, device_id=device, device_id_type=pl.DeviceIdType.MESH)

            count = count + jnp.where(needed, 1, 0)
    pl.semaphore_wait(barrier, count)


class Gather:
    def __init__(self, shard, dst, axis, send, recv, local, near_x, near_y, near_core):
        piece = shard.shape[axis]
        half = shard.shape[0] // 2

        def block(side, k):
            cut = pl.ds(k * piece, piece)
            return dst.at[side, cut, :] if axis == 0 else dst.at[side, :, cut]

        def part(k, h):
            if axis == 0:
                return dst.at[0, pl.ds(k * piece + h * half, half), :]
            return dst.at[0, pl.ds(h * half, half), pl.ds(k * piece, piece)]

        link, cross = send.at[0], send.at[1]
        self.local = pltpu.make_async_copy(shard, block(0, 0), local)
        self.x = remote(shard, block(0, 1), link, recv.at[0], near_x)
        self.y = remote(shard, block(0, 2), link, recv.at[1], near_y)
        self.dx = remote(part(2, 0), part(3, 0), link, recv.at[2], near_x)
        self.dy = remote(part(1, 1), part(3, 1), link, recv.at[2], near_y)
        self.cores = [remote(shard if k == 0 else block(0, k), block(1, k), cross, recv.at[3], near_core) for k in range(4)]
        cut = pl.ds(0, 3 * piece)
        three = dst.at[0, cut, :] if axis == 0 else dst.at[0, :, cut]
        self.all_links = remote(three, three, link, recv.at[0], near_x)
        self.diagonal = remote(block(0, 3), block(0, 3), link, recv.at[2], near_x)
        self.all_cores = remote(dst.at[0], dst.at[1], cross, recv.at[3], near_core)

    def first(self):
        self.x.start()
        self.y.start()
        self.cores[0].start()
        self.local.start()

    def second(self):
        self.y.wait_recv()
        self.dx.start()
        self.cores[2].start()
        self.x.wait_recv()
        self.dy.start()
        self.cores[1].start()

    def third(self):
        self.diagonal.wait_recv()
        self.cores[3].start()

    def arrived(self):
        self.local.wait()
        self.all_cores.wait_recv()

    def sent(self):
        self.all_links.wait_send()
        self.all_cores.wait_send()


def forward_kernel(
    hd, nq, nk, block, sub,
    len_ref, x_hbm, cot_hbm, wq_hbm, wk_hbm, wv_hbm, wout, wgate, wup, wdown, again_ref, fgain_ref, qgain_ref, kgain_ref,
    xr_hbm, n1_hbm, gf_hbm, qkv_hbm, out_hbm, gate_hbm, up_hbm, down_hbm, hidden_hbm, n2_hbm, rest_hbm, resta_hbm, gi_hbm, pre_hbm, all_hbm, att_hbm, tok_hbm,
    gains_ref, table_ref, inv_ref, stat_ref,
    xr_v, cot_v, n1_v, qkv_v, out_v, ex_own, ex_send, ex_got, at_own, at_send, at_got,
    part_v, in_v, back_v, hid_v, norm_v, wqkv, gain_ref, down_v, gi_v, pre_ref, all_ref, att_ref, tok_ref,
    keep_sem, load_sem, store_sem, shard_sem, rest_sem, down_sem, gi_sem, wsend, wrecv, wloc, gsend, grecv, exsend, exrecv, zsend, zrecv, hid_sem,
):
    seqs, span, width = xr_v.shape
    groups = nq // nk
    row, core, rank = lax.axis_index("dp"), lax.axis_index("context"), lax.axis_index("tensor")
    start = core * span
    near = [row, xor_one(row), (row + 2) % 4, 3 - row]
    inner = (rank % 3) != 0
    near_x, near_y, near_core = {"dp": near[1]}, {"dp": near[2]}, {"context": 1 - core}
    z_side, z_mid = {"tensor": xor_one(rank)}, {"tensor": 3 - rank}
    piece = width // 8
    total_subs = part_v.shape[0]
    per = span // sub
    first_core = core == 0

    loads = []
    for at, (src, dst) in enumerate(((x_hbm, xr_v), (cot_hbm, cot_v))):
        for s in range(seqs):
            for o in range(2):
                for k in range(4):
                    b = near[k] * 2 + (core if o == 0 else 1 - core)
                    cut = pl.ds(pl.multiple_of(b * piece, piece), piece)
                    loads.append(
                        pltpu.make_async_copy(
                            src.at[s, :, cut], dst.at[s, :, pl.ds((o * 4 + k) * piece, piece)], load_sem.at[at]
                        )
                    )
    shards, at = [], 0
    for k, ref in enumerate((wq_hbm, wk_hbm, wv_hbm)):
        shards.append(pltpu.make_async_copy(ref, wqkv.at[:, pl.ds(at, ref.shape[1])], shard_sem.at[k]))
        at += ref.shape[1]
    for copy in shards + loads:
        copy.start()
    piece = width // 8
    wide_gains = [ref[...].astype(F32).reshape(1, piece) for ref in (again_ref, fgain_ref)]
    gain_ref[...] = jnp.concatenate(wide_gains + [jnp.zeros((14, piece), F32)], axis=0).astype(BF16)

    others = []
    for o in range(2):
        for k in range(4):
            if o or k:
                others.append((o * 4 + k, {"dp": near[k], "context": core if o == 0 else 1 - core}))
    greet([(None, d) for _, d in others] + [(None, z_side), (inner, z_mid)])

    gains = [remote(gain_ref, gains_ref.at[b], gsend, grecv, d) for b, d in others]
    every_gain = remote(gains_ref.at[pl.ds(1, 7)], gains_ref.at[pl.ds(1, 7)], gsend, grecv, near_core)
    for copy in gains:
        copy.start()
    weights = [
        Gather(shard, dst, axis, wsend.at[i], wrecv.at[i], wloc.at[i], near_x, near_y, near_core)
        for i, (shard, dst, axis) in enumerate(
            ((wqkv, qkv_v, 0), (wout, out_v, 1), (wgate, gate_hbm, 0), (wup, up_hbm, 0), (wdown, down_hbm, 1))
        )
    ]
    w_qkv, w_out, w_gate, w_up, w_down = weights
    for copy in shards:
        copy.wait()
    w_qkv.first()
    w_out.first()
    gains_ref[0] = gain_ref[...]

    quarter = hd // 2
    freqs = jnp.exp(lax.broadcasted_iota(jnp.int32, (quarter, span), 0).astype(F32) * (-2.0 * math.log(rope_base) / hd))
    angles = freqs * (start + lax.broadcasted_iota(jnp.int32, (quarter, span), 1)).astype(F32)
    cosine, sine = jnp.cos(angles), jnp.sin(angles)
    turned = [jnp.broadcast_to(ref[...].astype(F32).reshape(1, hd), (8, hd)).T for ref in (qgain_ref, kgain_ref)]
    qgain, kgain = turned[0][:, 0:1], turned[1][:, 0:1]
    table_ref[:quarter, :] = cosine
    table_ref[quarter : 2 * quarter, :] = sine
    table_ref[2 * quarter : 2 * quarter + hd, :128] = jnp.broadcast_to(qgain, (hd, 128))
    table_ref[2 * quarter + hd :, :128] = jnp.broadcast_to(kgain, (hd, 128))

    pltpu.make_async_copy(cot_hbm, cot_v, load_sem.at[1]).wait()

    def mask_rows(i, carry):
        s, t = i // (span // 16), i % (span // 16)
        cut = pl.ds(pl.multiple_of(t * 16, 16), 16)
        place = start + t * 16 + lax.broadcasted_iota(jnp.int32, (16, 1), 0)
        valid = (place < len_ref[s]).astype(F32)
        cot_v[s, cut, :] = (cot_v[s, cut, :].astype(F32) * valid).astype(BF16)
        return carry

    lax.fori_loop(0, seqs * span // 16, mask_rows, 0)
    store_gf = pltpu.make_async_copy(cot_v, gf_hbm, store_sem.at[0])
    store_gf.start()
    pltpu.make_async_copy(x_hbm, xr_v, load_sem.at[0]).wait()
    store_xr = pltpu.make_async_copy(xr_v, xr_hbm, store_sem.at[1])
    store_xr.start()
    every_gain.wait_recv()
    gain1 = jnp.concatenate([gains_ref[b, 0:1, :] for b in range(8)], axis=1).astype(F32)
    gain2 = jnp.concatenate([gains_ref[b, 1:2, :] for b in range(8)], axis=1).astype(F32)

    def norm_rows(i, carry):
        s, t = i // (span // 16), i % (span // 16)
        cut = pl.ds(pl.multiple_of(t * 16, 16), 16)
        x = xr_v[s, cut, :].astype(F32)
        n1_v[s, cut, :] = (x * inverse_rms(x) * gain1).astype(BF16)
        return carry

    lax.fori_loop(0, span // 16, norm_rows, 0)
    w_qkv.second()
    lax.fori_loop(span // 16, seqs * span // 16, norm_rows, 0)
    store_n1 = pltpu.make_async_copy(n1_v, n1_hbm, store_sem.at[2])
    store_n1.start()
    w_out.second()
    w_down.first()
    w_gate.first()
    w_qkv.third()
    w_qkv.arrived()

    half = width // 2

    def exchange(s):
        return remote(ex_send.at[s], ex_got.at[s], exsend.at[0, s], exrecv.at[0, s], near_core)

    def keep(k, s):
        ref, dst = ((pre_ref, pre_hbm), (all_ref, all_hbm), (att_ref, att_hbm), (tok_ref, tok_hbm))[k]
        return pltpu.make_async_copy(ref.at[s], dst.at[s], keep_sem.at[k, s])

    def project(s):
        x = n1_v[s]
        flat = dot_nn(x[:, :half], qkv_v[0]) + dot_nn(x[:, half:], qkv_v[1])
        turned = flat.T
        pre_ref[s] = turned[: (nq + nk) * hd]
        done = []
        for h in range(nq + nk):
            v = turned[h * hd : (h + 1) * hd]
            inv = lax.rsqrt(jnp.mean(v * v, axis=0, keepdims=True) + epsilon)
            v = v * inv * (qgain if h < nq else kgain)
            a, b = v[: hd // 2], v[hd // 2 :]
            done.append(jnp.concatenate([a * cosine - b * sine, b * cosine + a * sine], axis=0))
        for h in range(nk):
            lo = (nq + nk + h) * hd
            done.append(turned[lo : lo + hd])
        parts = [[], []]
        for begin_at, count in ((0, nq), (nq, nk), (nq + nk, nk)):
            for side in range(2):
                parts[side] += done[begin_at + side * count // 2 : begin_at + (side + 1) * count // 2]
        low = jnp.concatenate(parts[0], axis=0)
        high = jnp.concatenate(parts[1], axis=0)
        ex_own[s] = jnp.where(first_core, low, high).astype(BF16)
        ex_send[s] = jnp.where(first_core, high, low).astype(BF16)
        exchange(s).start()
        keep(0, s).start()

    store_qkv = pltpu.make_async_copy(qkv_v, qkv_hbm, store_sem.at[3])
    store_qkv.start()
    store_out = pltpu.make_async_copy(out_v, out_hbm, store_sem.at[4])

    scale = log2e / math.sqrt(hd)
    krow = lax.broadcasted_iota(jnp.int32, (block, groups * block), 0)
    qcol = lax.broadcasted_iota(jnp.int32, (block, groups * block), 1) % block
    base = groups * hd

    def give(s):
        return remote(at_send.at[s], at_got.at[s], exsend.at[1, s], exrecv.at[1, s], near_core)

    def attention(s):
        exchange(s).wait_recv()
        low, high = join_positions(core, ex_own[s], ex_got[s])
        all_ref[s, :, :span] = low
        all_ref[s, :, span:] = high
        length = len_ref[s]
        for i in range(2 * span // block):
            cut = slice(i * block, (i + 1) * block)
            q = jnp.concatenate([all_ref[s, g * hd : (g + 1) * hd, cut] for g in range(groups)], axis=1)
            acc = jnp.zeros((hd, groups * block), F32)
            total = jnp.zeros((1, groups * block), F32)
            for j in range(i + 1):
                kcut = slice(j * block, (j + 1) * block)
                score = dot_tn(all_ref[s, base : base + hd, kcut], q) * scale
                ok = (krow + j * block) < length
                if j == i:
                    ok = ok & (krow <= qcol)
                e = jnp.where(ok, jnp.exp2(score), 0.0)
                total = total + jnp.sum(e, axis=0, keepdims=True)
                acc = acc + dot_nn(all_ref[s, base + hd : base + 2 * hd, kcut], e.astype(BF16))
            inv = 1.0 / total
            att = (acc * inv).astype(BF16)
            for g in range(groups):
                att_ref[s, g * hd : (g + 1) * hd, cut] = att[:, g * block : (g + 1) * block]
                inv_ref[s, g : g + 1, cut] = inv[:, g * block : (g + 1) * block]
        mine, theirs = join_positions(core, att_ref[s, :, :span], att_ref[s, :, span:])
        at_own[s] = mine
        at_send[s] = theirs
        give(s).start()
        keep(1, s).start()
        keep(2, s).start()

    moving = Chain(rank, part_v, in_v, back_v, zsend, zrecv)
    subs = moving.count

    def branch_rows(s):
        give(s).wait_recv()
        low, high = join_positions(core, at_own[s], at_got[s])
        att = jnp.concatenate([low, high], axis=0).T
        tok_ref[s] = att
        keep(3, s).start()
        many = 2
        for k in range(0, per, many):
            rows = att[k * sub : (k + many) * sub]
            for side in range(2):
                part = dot_nn(rows, out_v[side]).astype(BF16)
                for m in range(many):
                    part_v[s * per + k + m, :, side * half : (side + 1) * half] = part[m * sub : (m + 1) * sub]
            for m in range(many):
                u = s * per + k + m

                moving.begin(u)

    def sequence(s, carry):
        project(s)

        attention(s)

        @pl.when(s == 0)
        def _():
            w_out.third()
            w_out.arrived()
            store_out.start()

        branch_rows(s)
        return carry

    lax.fori_loop(0, seqs, sequence, 0)
    tail = pl.ds(subs, total_subs - subs)
    rest = [pltpu.make_async_copy(part_v.at[tail], rest_hbm, rest_sem.at[0])]
    rest[0].start()
    stat_ref[...] = jnp.zeros_like(stat_ref)

    def hidden_store(u):
        cut = pl.ds(pl.multiple_of(u * sub, sub), sub)
        return (
            pltpu.make_async_copy(hid_v.at[u % 2], hidden_hbm.at[cut, :], hid_sem.at[0, u % 2]),
            pltpu.make_async_copy(norm_v.at[u % 2], n2_hbm.at[cut, :], hid_sem.at[1, u % 2]),
        )

    def finish(u):
        s, t = u // per, u % per
        cut = pl.ds(pl.multiple_of(t * sub, sub), sub)

        moving.ready(u)

        @pl.when(u >= 2)
        def _():
            for copy in hidden_store(u - 2):
                copy.wait()

        length = len_ref[s]

        def body(piece_rows, first):
            total = moving.total(u, piece_rows)
            resid = xr_v[s, pl.ds(pl.multiple_of(t * sub + first, 16), 16), :].astype(F32)
            hidden = resid + total
            hid_v[u % 2, piece_rows, :] = hidden
            norm_v[u % 2, piece_rows, :] = (hidden * inverse_rms(hidden) * gain2).astype(BF16)
            place = start + t * sub + first + lax.broadcasted_iota(jnp.int32, (16, 1), 0)
            valid = (place < length).astype(F32)
            stat_ref[0] += fold_lanes(valid * resid * resid)
            stat_ref[1] += fold_lanes(valid * total * total)

        by_pieces(sub, body)
        for copy in hidden_store(u):
            copy.start()

    hb = down_v.shape[2]
    blocks = down_hbm.shape[1] // hb

    def load_down(h):
        cut = pl.ds(pl.multiple_of(h * hb, hb), hb)
        return [pltpu.make_async_copy(down_hbm.at[side, cut, :], down_v.at[h % 2, side], down_sem.at[h % 2, side]) for side in range(2)]

    def store_gi(h):
        cut = pl.ds(pl.multiple_of(h * hb, hb), hb)
        return pltpu.make_async_copy(gi_v.at[h % 2], gi_hbm.at[:, cut], gi_sem.at[h % 2])

    def grad_inner(h):
        for copy in load_down(h):
            copy.wait()

        @pl.when(h + 1 < blocks)
        def _():
            for copy in load_down(h + 1):
                copy.start()

        @pl.when(h >= 2)
        def _():
            store_gi(h - 2).wait()

        for s in range(seqs):
            for q in range(span // 256):
                cut = slice(q * 256, (q + 1) * 256)
                g = dot_nt(cot_v[s, cut, :half], down_v[h % 2, 0]) + dot_nt(cot_v[s, cut, half:], down_v[h % 2, 1])
                gi_v[h % 2, s * span + q * 256 : s * span + (q + 1) * 256, :] = g.astype(BF16)
        store_gi(h).start()

    def chain(i, carry):
        moving.middle(i)
        moving.outward(i - 1)

        @pl.when(i == 1)
        def _():
            w_down.second()
            w_up.first()

        @pl.when(i == 6)
        def _():
            w_gate.second()

        @pl.when(i == 7)
        def _():
            w_down.third()

        @pl.when(i == 8)
        def _():
            w_down.arrived()
            for copy in load_down(0):
                copy.start()

        @pl.when(i == 10)
        def _():
            w_up.second()

        @pl.when(i >= 2)
        def _():
            finish(i - 2)

        @pl.when((i >= 9) & (i < 9 + blocks))
        def _():
            grad_inner(i - 9)

        return carry

    lax.fori_loop(0, subs + 2, chain, 0)
    w_gate.third()
    came = pltpu.make_async_copy(in_v.at[tail], resta_hbm, rest_sem.at[1])

    @pl.when(inner)
    def _():
        for u in range(subs, total_subs):
            moving.hop_in(u).wait_recv()
        came.start()

    w_up.third()
    for u in (subs - 2, subs - 1):
        for copy in hidden_store(u):
            copy.wait()
    for h in (blocks - 2, blocks - 1):
        store_gi(h).wait()
    moving.settle()
    for s in range(seqs):
        exchange(s).wait_send()
        give(s).wait_send()
        for k in range(4):
            keep(k, s).wait()
    every_gain.wait_send()
    w_gate.arrived()
    w_up.arrived()
    pl.when(inner)(came.wait)
    for w in weights:
        w.sent()
    for copy in [store_gf, store_xr, store_n1, store_qkv, store_out] + rest:
        copy.wait()


def forward(lengths, x, cot, w_query, w_key, w_value, w_out, w_gate, w_up, w_down, all_gains, hd, nq, nk):
    seqs, span, width = x.shape
    half = width // 2
    groups = nq // nk
    sub = span // 8
    subs = seqs * span // sub
    here = subs - 4
    block = min(256, span)
    hidden = w_gate.shape[1]
    hb = hidden // 4
    cols = w_query.shape[1] + w_key.shape[1] + w_value.shape[1]
    rows = cols // 2
    any_space = pl.BlockSpec(memory_space=pl.ANY)
    vmem = pl.BlockSpec(memory_space=pltpu.VMEM)
    wide = (seqs, span, width)
    large = [
        shape(wide, BF16), shape(wide, BF16), shape(wide, BF16),
        shape((2, half, cols), BF16), shape((2, w_out.shape[0], half), BF16),
        shape((2, half, hidden), BF16), shape((2, half, hidden), BF16), shape((2, hidden, half), BF16),
        shape((seqs * span, width), F32), shape((seqs * span, width), BF16), shape((subs - here, sub, width), BF16),
        shape((subs - here, sub, width), BF16), shape((seqs * span, hidden), BF16),
    ]
    kept = [
        shape((seqs, (nq + nk) * hd, span), F32), shape((seqs, rows, 2 * span), BF16),
        shape((seqs, groups * hd, 2 * span), BF16), shape((seqs, span, nq * hd), BF16),
    ]
    large += kept
    small = [
        shape((8, 16, width // 8), BF16), shape((3 * hd, span), F32), shape((seqs, groups, 2 * span), F32), shape((2, 8, 128), F32),
    ]
    dma = pltpu.SemaphoreType.DMA
    ex = pltpu.VMEM((seqs, rows, span), BF16)
    at = pltpu.VMEM((seqs, groups * hd, span), BF16)
    moving = pltpu.VMEM((subs, sub, width), BF16)
    landing = pltpu.VMEM((here, sub, width), BF16)
    arriving = pltpu.VMEM((subs, sub, width), BF16)
    flops = 2 * seqs * span * width * (cols + nq * hd) + 16 * seqs * nq * hd * span * span
    return pl.pallas_call(
        functools.partial(forward_kernel, hd, nq, nk, block, sub),
        in_specs=[SMEM] + [any_space] * 9 + [vmem] * 4,
        out_specs=[any_space] * len(large) + [vmem] * len(small),
        out_shape=large + small,
        scratch_shapes=[
            pltpu.VMEM(wide, BF16), pltpu.VMEM(wide, BF16), pltpu.VMEM(wide, BF16),
            pltpu.VMEM((2, half, cols), BF16), pltpu.VMEM((2, w_out.shape[0], half), BF16),
            ex, ex, ex, at, at, at,
            moving, arriving, landing,
            pltpu.VMEM((2, sub, width), F32), pltpu.VMEM((2, sub, width), BF16),
            pltpu.VMEM((w_query.shape[0], cols), BF16), pltpu.VMEM((16, width // 8), BF16),
            pltpu.VMEM((2, 2, hb, half), BF16), pltpu.VMEM((2, seqs * span, hb), BF16),
            *[pltpu.VMEM(a.shape, a.dtype) for a in kept],
            dma((4, seqs)), dma((2,)), dma((5,)), dma((3,)), dma((2,)), dma((2, 2)), dma((2,)), dma((5, 2)), dma((5, 4)), dma((5,)), dma(()), dma(()),
            dma((2, seqs)), dma((2, seqs)), dma((2,)), dma((2, subs)), dma((2, 2)),
        ],
        compiler_params=pltpu.CompilerParams(vmem_limit_bytes=VMEM_MOST, collective_id=1, has_side_effects=True),
        cost_estimate=cost(flops, 80 * seqs * span * width),
        name="attention_forward",
    )(lengths, x, cot, w_query, w_key, w_value, w_out, w_gate, w_up, w_down, *all_gains)


def by_pieces(count, body, size=16):
    def one(p, carry):
        body(pl.ds(pl.multiple_of(p * size, size), size), p * size)
        return carry

    lax.fori_loop(0, count // size, one, 0, unroll=2)


def fold_lanes(values):
    tiles = values[:8] + values[8:]
    return sum(tiles[:, k * 128 : (k + 1) * 128] for k in range(tiles.shape[1] // 128))


class Chain:
    def __init__(self, rank, part, arrive, back, send, recv, landed=False):
        self.landed = landed
        self.inner = (rank % 3) != 0
        self.outer = (rank % 3) == 0
        self.part, self.arrive, self.back = part, arrive, back
        self.send, self.recv = send, recv
        self.side, self.mid = {"tensor": xor_one(rank)}, {"tensor": 3 - rank}
        self.count = back.shape[0]

    def hop_in(self, u):
        return remote(self.part.at[u], self.arrive.at[u], self.send.at[0], self.recv.at[0, u], self.side)

    def hop_mid(self, u):
        return remote(self.arrive.at[u], self.back.at[u], self.send.at[1], self.recv.at[1, u], self.mid)

    def hop_out(self, u):
        return remote(self.part.at[u], self.back.at[u], self.send.at[0], self.recv.at[0, u], self.side)

    def add(self, into, one, two, u):
        def body(cut, first):
            into[u, cut, :] = (one[u, cut, :].astype(F32) + two[u, cut, :].astype(F32)).astype(BF16)

        by_pieces(self.part.shape[1], body)

    def begin(self, u):
        @pl.when(self.outer)
        def _():
            self.hop_in(u).start()

    def middle(self, u):
        @pl.when((u >= 0) & (u < self.count) & self.inner)
        def _():
            if not self.landed:
                self.hop_in(u).wait_recv()
            self.add(self.arrive, self.part, self.arrive, u)
            self.hop_mid(u).start()

    def outward(self, u):
        @pl.when((u >= 0) & (u < self.count) & self.inner)
        def _():
            self.hop_mid(u).wait_recv()
            self.add(self.part, self.part, self.back, u)
            self.hop_out(u).start()

    def ready(self, u):
        @pl.when(self.outer)
        def _():
            self.hop_out(u).wait_recv()

    def total(self, u, cut):
        near = jnp.where(self.inner, self.arrive[u, cut, :], self.part[u, cut, :])
        return near.astype(F32) + self.back[u, cut, :].astype(F32)

    def settle(self):
        def all_sent(ref, count, sem):
            every = ref.at[pl.ds(0, count)]
            remote(every, every, self.send.at[sem], self.recv.at[0, 0], self.side).wait_send()

        @pl.when(self.inner)
        def _():
            all_sent(self.part, self.count, 0)
            all_sent(self.arrive, self.count, 1)

        if not self.landed:

            @pl.when(self.outer)
            def _():
                all_sent(self.part, self.arrive.shape[0], 0)


def feed_both_kernel(
    hb, sub, rows,
    len_ref, n2_hbm, gf_hbm, gate_hbm, up_hbm, down_hbm, gi_hbm, rest_hbm, resta_hbm, xr_hbm, hidden_in, gains_ref,
    ffn_hbm, gb_hbm, gh_hbm, dgate_hbm, dup_hbm, ddown_hbm, hidden_hbm, landx, landy, ring_hbm, gain_out, stat_ref,
    n2_v, gf_v, inner_v, gg_v, gu_v, facc, gacc, wrow, wcol, part_v, in_v, back_v, hid_v, gh_v, gb_v, stage_row, stage_col,
    xtile_v, gi_v, wide_v, temp_v, gain_ref,
    load_sem, wsem, zsend, zrecv, hid_sem, out_sem, ffn_sem, csend, crecv, store_sem, lsend, lrecv, xt_sem, xsend, xrecv, xload, rsend, rrecv, free_sem, done_sem,
):
    core, rank = lax.axis_index("context"), lax.axis_index("tensor")
    near_core = {"context": 1 - core}
    tokens, width = n2_v.shape
    half = width // 2
    hidden = inner_v.shape[1]
    hsteps = hidden // hb
    steps = tokens // rows * hsteps
    per = rows // sub
    chain = Chain(rank, part_v, in_v, back_v, zsend, zrecv)
    subs = chain.count
    known = subs - rest_hbm.shape[0]
    tail = pl.ds(known, subs - known)
    late = Chain(rank, part_v.at[tail], in_v.at[tail], back_v.at[tail], lsend, lrecv, True)
    start = core * (tokens // 2)

    def load_weights(i):
        slot, h = i % 2, i % hsteps
        cut = pl.ds(pl.multiple_of(h * hb, hb), hb)
        here = pl.ds(pl.multiple_of(i // hsteps * rows, rows), rows)
        copies = [pltpu.make_async_copy(gi_hbm.at[here, cut], gi_v.at[slot], wsem.at[slot, 6])]
        for side in range(2):
            copies.append(pltpu.make_async_copy(gate_hbm.at[side, :, cut], wrow.at[slot, 0, side], wsem.at[slot, side]))
            copies.append(pltpu.make_async_copy(up_hbm.at[side, :, cut], wrow.at[slot, 1, side], wsem.at[slot, 2 + side]))
        return copies

    def load_down(i):
        slot, h = i % 2, i % hsteps
        cut = pl.ds(pl.multiple_of(h * hb, hb), hb)
        return [pltpu.make_async_copy(down_hbm.at[side, cut, :], wcol.at[slot, side], wsem.at[slot, 4 + side]) for side in range(2)]

    def load_hidden(u):
        cut = pl.ds(pl.multiple_of(u * sub, sub), sub)
        return pltpu.make_async_copy(hidden_hbm.at[cut, :], hid_v, hid_sem)

    ready = pl.ds(rows, known * sub - rows)
    head = pl.ds(0, rows)
    load_head = pltpu.make_async_copy(n2_hbm.at[head, :], n2_v.at[head, :], load_sem.at[4])
    loads = [
        pltpu.make_async_copy(n2_hbm.at[ready, :], n2_v.at[ready, :], load_sem.at[0]),
        pltpu.make_async_copy(rest_hbm, late.part, load_sem.at[1]),
        pltpu.make_async_copy(resta_hbm, late.arrive, load_sem.at[3]),
    ]
    load_gf = pltpu.make_async_copy(gf_hbm, gf_v, load_sem.at[2])
    for copy in load_weights(0) + [load_head] + loads + [load_gf]:
        copy.start()
    load_hidden(0).start()
    row = lax.axis_index("dp")
    near_x, near_y = {"dp": xor_one(row)}, {"dp": (row + 2) % 4}
    greet([(None, near_core), (None, near_x), (None, near_y), (None, chain.side), (chain.inner, chain.mid)])
    for b in range(8):
        gain_ref[:, b * (width // 8) : (b + 1) * (width // 8)] = gains_ref[b, 1:2, :].astype(F32)
    gain_out[...] = jnp.zeros_like(gain_out)
    stat_ref[...] = jnp.zeros_like(stat_ref)
    load_head.wait()

    def load_x(u):
        at = pl.multiple_of((known + u) * sub, sub)
        return pltpu.make_async_copy(xr_hbm.at[pl.ds(at, sub), :], xtile_v, xt_sem)

    def late_store(u):
        return pltpu.make_async_copy(gh_v, hidden_hbm.at[pl.ds(pl.multiple_of((known + u) * sub, sub), sub), :], out_sem.at[0])

    def late_finish(u):
        load_x(u).start()
        late.ready(u)
        load_x(u).wait()

        @pl.when(u >= 1)
        def _():
            late_store(u - 1).wait()

        length = len_ref[known * sub // (tokens // 2)]
        offset = start + known * sub % (tokens // 2) + u * sub

        def body(cut, first):
            total = late.total(u, cut)
            resid = xtile_v[cut, :].astype(F32)
            hidden_rows = resid + total
            gh_v[cut, :] = hidden_rows
            normed = (hidden_rows * inverse_rms(hidden_rows) * gain_ref[...]).astype(BF16)
            n2_v[pl.ds(pl.multiple_of((known + u) * sub + first, 16), 16), :] = normed
            spot = offset + first + lax.broadcasted_iota(jnp.int32, (16, 1), 0)
            valid = (spot < length).astype(F32)
            stat_ref[0] += fold_lanes(valid * resid * resid)
            stat_ref[1] += fold_lanes(valid * total * total)

        by_pieces(sub, body)
        late_store(u).start()

    def store_gb(u):
        cut = pl.ds(pl.multiple_of(u * sub, sub), sub)
        return pltpu.make_async_copy(gb_v, gb_hbm.at[cut, :], out_sem.at[1])

    def store_gh(u):
        at = pl.ds(pl.multiple_of(u % 2 * sub, sub), sub)
        return pltpu.make_async_copy(gh_v, gh_hbm.at[u // 8, at, :], out_sem.at[0])

    def finish(u):
        chain.ready(u)
        load_hidden(u).wait()

        @pl.when(u >= 1)
        def _():
            store_gb(u - 1).wait()

        def body(piece_rows, first):
            e = chain.total(u, piece_rows)
            hidden_rows = hid_v[piece_rows, :]
            inv = inverse_rms(hidden_rows)
            hat = hidden_rows * inv
            eg = e * gain_ref[...]
            grad = gf_v[pl.ds(pl.multiple_of(u * sub + first, 16), 16), :].astype(F32)
            gh = grad + inv * (eg - hat * jnp.mean(eg * hat, axis=-1, keepdims=True))
            gb_v[piece_rows, :] = gh.astype(BF16)

            @pl.when(u % 8 // 2 == rank)
            def _():
                gh_v[piece_rows, :] = gh

            both = e * hat
            gain_out[...] += both[:8] + both[8:]

        by_pieces(sub, body)
        store_gb(u).start()

        @pl.when(u % 8 // 2 == rank)
        def _():
            store_gh(u).start()
            store_gh(u).wait()

        @pl.when(u + 1 < subs)
        def _():
            load_hidden(u + 1).start()

    def serve(n):
        chain.middle(n)
        chain.outward(n - 2)

        @pl.when((n >= 4) & (n < 4 + subs))
        def _():
            finish(n - 4)

    quarter = width // 4

    def store_ffn(c):
        here = pl.ds(pl.multiple_of(c * rows, rows), rows)
        return [
            pltpu.make_async_copy(
                stage_row.at[c % 2, pl.ds(k * rows, rows), :], ffn_hbm.at[here, pl.ds(k * quarter, quarter)], ffn_sem.at[c % 2, k]
            )
            for k in range(4)
        ]

    def step(i, carry):
        slot, c, h = i % 2, i // hsteps, i % hsteps
        for copy in load_weights(i):
            copy.wait()

        @pl.when(i + 1 < steps)
        def _():
            for copy in load_weights(i + 1):
                copy.start()

            @pl.when((i + 1) // hsteps % 2 == 1)
            def _():
                for copy in load_down(i + 1):
                    copy.start()

        here = pl.ds(pl.multiple_of(c * rows, rows), rows)
        cols = pl.ds(pl.multiple_of(h * hb, hb), hb)
        n = n2_v[here, :]
        wide = min(256, hb)
        for q in range(hb // wide):
            part = slice(q * wide, (q + 1) * wide)
            gate = dot_nn(n[:, :half], wrow[slot, 0, 0, :, part]) + dot_nn(n[:, half:], wrow[slot, 0, 1, :, part])
            up = dot_nn(n[:, :half], wrow[slot, 1, 0, :, part]) + dot_nn(n[:, half:], wrow[slot, 1, 1, :, part])
            gi = gi_v[slot, :, part].astype(F32)
            sig = jax.nn.sigmoid(gate)
            silu = gate * sig
            at = pl.ds(pl.multiple_of(h * hb + q * wide, wide), wide)
            inner_v[here, at] = (silu * up).astype(BF16)
            gg_v[here, at] = (gi * up * sig * (1.0 + gate * (1.0 - sig))).astype(BF16)
            gu_v[here, at] = (gi * silu).astype(BF16)

        @pl.when(h == 0)
        def _():
            gacc[...] = jnp.zeros_like(gacc)

        gg, gu = gg_v[here, cols], gu_v[here, cols]
        span = min(512, half)
        for side in range(2):
            for q in range(half // span):
                part = slice(q * span, (q + 1) * span)
                cut = slice(side * half + q * span, side * half + (q + 1) * span)
                gacc[:, cut] += dot_nt(gg, wrow[slot, 0, side, part, :]) + dot_nt(gu, wrow[slot, 1, side, part, :])

        @pl.when(h == hsteps - 1)
        def _():
            for k in range(per):
                part_v[c * per + k] = gacc[k * sub : (k + 1) * sub, :].astype(BF16)
                chain.begin(c * per + k)

        @pl.when(c % 2 == 1)
        def _():
            pair = pl.ds(pl.multiple_of((c - 1) * rows, rows), 2 * rows)
            inner = inner_v[pair, cols]
            for copy in load_down(i):
                copy.wait()

            @pl.when(h == 0)
            def _():
                facc[...] = jnp.zeros_like(facc)

            for side in range(2):
                for q in range(half // span):
                    part = slice(q * span, (q + 1) * span)
                    cut = slice(side * half + q * span, side * half + (q + 1) * span)
                    facc[:, cut] += dot_nn(inner, wcol[slot, side, :, part])

            @pl.when(h == hsteps - 1)
            def _():
                for m in range(2):

                    @pl.when(c >= 2)
                    def _():
                        for copy in store_ffn(c - 3 + m):
                            copy.wait()

                    for k in range(4):
                        stage_row[m, k * rows : (k + 1) * rows, :] = facc[
                            m * rows : (m + 1) * rows, k * quarter : (k + 1) * quarter
                        ].astype(BF16)
                    for copy in store_ffn(c - 1 + m):
                        copy.start()

        @pl.when(i == 0)
        def _():
            for copy in loads:
                copy.wait()

        late.middle(i)
        late.outward(i - 3)

        @pl.when((i >= 6) & (i < 6 + late.count))
        def _():
            late_finish(i - 6)

        @pl.when(i == 9)
        def _():
            load_gf.wait()
            late_store(late.count - 1).wait()
            late.settle()
            pl.semaphore_signal(done_sem, inc=1, device_id=chain.side, device_id_type=pl.DeviceIdType.MESH)

            @pl.when(chain.inner)
            def _():
                pl.semaphore_signal(done_sem, inc=1, device_id=chain.mid, device_id_type=pl.DeviceIdType.MESH)

        @pl.when(i == steps - 2)
        def _():
            pl.semaphore_wait(done_sem, jnp.where(chain.inner, 2, 1))

        serve(i - 6)
        return carry

    lax.fori_loop(0, steps, step, 0)
    for c in range(2, steps // hsteps):
        for copy in store_ffn(c):
            copy.wait()

    pl.semaphore_signal(free_sem, inc=1, device_id=near_core, device_id_type=pl.DeviceIdType.MESH)
    outs = (dgate_hbm, dup_hbm, ddown_hbm)

    def landing(w, t):
        return wrow.at[t // 2, w, t % 2] if w < 2 else wcol.at[t // 2, t % 2]

    def landed(w, t, piece):
        return wrow[t // 2, w, t % 2, piece, :] if w < 2 else wcol[t // 2, t % 2, piece, :]

    def staging(w):
        return stage_row if w < 2 else stage_col

    def ship(w, t):
        return remote(staging(w).at[t % 2], landing(w, t), csend.at[w, t], crecv.at[w, t], near_core)

    def keep(w, t):
        cut = pl.ds(pl.multiple_of(t * hb, hb), hb)
        dst = outs[w].at[:, cut] if w < 2 else outs[w].at[cut, :]
        return pltpu.make_async_copy(staging(w).at[t % 2], dst, store_sem.at[w, t])

    def release(kind, w, t):
        if kind == 1:
            ship(w, t).wait_send()
        else:
            keep(w, t).wait()

    def group(kind, w, before, part):
        def one(t, carry):
            cut = pl.ds(pl.multiple_of(t * hb, hb), hb)
            mine = slice(kind * half, (kind + 1) * half)
            @pl.when(t >= 2)
            def _():
                release(kind, w, t - 2)

            if before is not None:

                @pl.when(t < 2)
                def _():
                    release(before[0], before[1], t + hsteps - 2)

            if kind == 0:
                ship(w, t).wait_recv()
            tall = staging(w).shape[1]
            size = min(256, tall)
            for q in range(tall // size):
                piece = slice(q * size, (q + 1) * size)
                if w == 2:
                    left = inner_v[:, pl.ds(pl.multiple_of(t * hb + q * size, size), size)]
                    value = dot_tn(left, gf_v[:, mine])
                else:
                    value = dot_tn(n2_v[:, kind * half + q * size : kind * half + (q + 1) * size], (gg_v, gu_v)[w][:, cut])
                if kind == 0:
                    value = value + landed(w, t, piece).astype(F32)
                staging(w)[t % 2, piece, :] = value.astype(BF16)
            if kind == 1:
                ship(w, t).start()
            else:
                keep(w, t).start()
            return carry

        lax.fori_loop(part * (hsteps // 2), (part + 1) * (hsteps // 2), one, 0)

    pl.semaphore_wait(free_sem, 1)

    def term(m):
        return ffn_hbm.at[pl.ds(pl.multiple_of(m * (2 * sub), 2 * sub), 2 * sub), :]

    fold = Fold(rank, term, None, ring_hbm, (ring_hbm.at[2], None), rsend, rrecv)
    after = iter(range(steps - 6, subs + 4))
    done = []

    def both(kind, w, before):
        for part in range(2):
            group(kind, w, before, part)
            done.append(part)
            if len(done) <= 8 or len(done) % 2 == 0:
                serve(next(after))
            if len(done) == 4:
                fold.begin()

    both(1, 0, None)
    both(0, 0, (1, 0))
    for t in range(hsteps - 2, hsteps):
        keep(0, t).wait()
    gate_sum = Scatter(
        row_blocks(dgate_hbm), wide_v.at[0], wide_v.at[1], half_rows(landx), half_rows(landy), temp_v, xsend, xrecv, xload, near_x, near_y
    )
    gate_sum.begin()
    both(1, 1, None)
    both(1, 2, None)
    gate_sum.pass_on()
    both(0, 1, (1, 1))
    both(0, 2, (1, 2))
    for n in after:
        serve(n)
    for t in range(hsteps - 2, hsteps):
        keep(1, t).wait()
        keep(2, t).wait()
    store_gb(subs - 1).wait()
    gate_sum.arrived()
    gate_sum.settle()
    chain.settle()

    @pl.when(fold.inner)
    def _():
        for k in range(3):
            fold.come(k)

    @pl.when(fold.outer)
    def _():
        fold.settle()


def row_blocks(ref):
    size = ref.shape[0] // 4
    return lambda k, h: ref.at[pl.ds(k * size + h * (size // 2), size // 2), :]


def half_rows(ref):
    size = ref.shape[0] // 2
    return lambda h: ref.at[pl.ds(h * size, size), :]


def feed_both(lengths, n2, gf, gate, up, down, gi, rest, came, xr, hidden_rows, gain):
    tokens, width = n2.shape
    _, half, hidden = gate.shape
    hb = hidden // 4
    sub, rows = tokens // 16, tokens // 4
    count = rest.shape[0]
    any_space = pl.BlockSpec(memory_space=pl.ANY)
    vmem = pl.BlockSpec(memory_space=pltpu.VMEM)
    dma = pltpu.SemaphoreType.DMA
    moving = pltpu.VMEM((16, sub, width), BF16)
    act = pltpu.VMEM((tokens, hidden), BF16)
    return pl.pallas_call(
        functools.partial(feed_both_kernel, hb, sub, rows),
        in_specs=[SMEM] + [any_space] * 10 + [vmem],
        out_specs=[any_space] * 10 + [vmem] * 2,
        out_shape=[
            shape((tokens, width), BF16), shape((tokens, width), BF16), shape((2, 2 * sub, width), F32),
            shape((half, hidden), BF16), shape((half, hidden), BF16), shape((hidden, half), BF16),
            shape((tokens, width), F32), shape((half // 4, hidden), BF16), shape((half // 4, hidden), BF16),
            shape((3, 2 * sub, width), BF16), shape((8, width), F32), shape((2, 8, 128), F32),
        ],
        scratch_shapes=[
            pltpu.VMEM((tokens, width), BF16), pltpu.VMEM((tokens, width), BF16), act, act, act,
            pltpu.VMEM((2 * rows, width), F32), pltpu.VMEM((rows, width), F32),
            pltpu.VMEM((2, 2, 2, half, hb), BF16), pltpu.VMEM((2, 2, hb, half), BF16),
            moving, moving, moving,
            pltpu.VMEM((sub, width), F32), pltpu.VMEM((sub, width), F32), pltpu.VMEM((sub, width), BF16),
            pltpu.VMEM((2, half, hb), BF16), pltpu.VMEM((2, hb, half), BF16),
            pltpu.VMEM((sub, width), BF16), pltpu.VMEM((2, rows, hb), BF16),
            pltpu.VMEM((2, half // 8, hidden), BF16), pltpu.VMEM((2, half // 8, hidden), BF16), pltpu.VMEM((1, width), F32),
            dma((5,)), dma((2, 7)), dma((2,)), dma((2, 16)), dma(()), dma((2,)), dma((2, 4)), dma((3, 4)), dma((3, 4)),
            dma((3, 4)), dma((2,)), dma((2, count)), dma(()), dma((6,)), dma((6,)), dma((3,)), dma(()), dma((5,)), pltpu.SemaphoreType.REGULAR, pltpu.SemaphoreType.REGULAR,
        ],
        input_output_aliases={10: 6},
        compiler_params=pltpu.CompilerParams(vmem_limit_bytes=VMEM_MOST, collective_id=2, has_side_effects=True),
        cost_estimate=cost(18 * tokens * width * hidden, 60 * tokens * width),
        name="feed_forward_both",
    )(lengths, n2, gf, gate, up, down, gi, rest, came, xr, hidden_rows, gain)


class Fold:
    def __init__(self, rank, source, own, slots, finals, send, recv, landed=None):
        self.inner, self.outer = (rank % 3) != 0, (rank % 3) == 0
        self.side, self.mid = {"tensor": xor_one(rank)}, {"tensor": 3 - rank}
        self.leaving = (3 - rank, xor_one(3 - rank), xor_one(rank))
        self.added = (xor_one(3 - rank), 3 - rank, xor_one(rank))
        self.source, self.own, self.slots, self.finals = source, own, slots, finals
        self.send, self.recv, self.landed = send, recv, landed

    def inward(self, k):
        dst = self.slots.at[k] if k < 2 else self.finals[0]
        return remote(self.source(self.leaving[k]), dst, self.send, self.recv.at[k], self.side)

    def across(self, k):
        dst = self.slots.at[2] if k == 0 else self.finals[1]
        return remote(self.slots.at[k], dst, self.send, self.recv.at[3 + k], self.mid)

    def outward(self):
        return remote(self.slots.at[2], self.finals[0], self.send, self.recv.at[0], self.side)

    def begin(self):
        @pl.when(self.outer)
        def _():
            for k in range(3):
                self.inward(k).start()

    def come(self, k):
        (self.landed[k].wait if self.landed is not None else self.inward(k).wait_recv)()

    def step(self, k):
        @pl.when(self.inner)
        def _():
            if k < 2:
                self.come(k)
            else:
                self.across(0).wait_recv()
            read = self.own(self.added[k])

            def body(cut, first):
                self.slots[k, cut, :] = (self.slots[k, cut, :].astype(F32) + read(cut).astype(F32)).astype(BF16)

            by_pieces(self.slots.shape[1], body)
            (self.across(k) if k < 2 else self.outward()).start()

    def arrived(self):
        @pl.when(self.inner)
        def _():
            self.come(2)
            self.across(1).wait_recv()

        @pl.when(self.outer)
        def _():
            self.outward().wait_recv()

    def settle(self):
        three = self.slots.at[pl.ds(0, 3)]
        every = remote(three, three, self.send, self.recv.at[0], self.side)
        if self.landed is None:
            every.wait_send()
        else:
            pl.when(self.inner)(every.wait_send)


def tall(ref):
    return 16 * max(1, 2048 // ref.shape[1])


class Scatter:
    def __init__(self, block, from_x, from_y, land_x, land_y, temps, send, recv, load, near_x, near_y):
        self.block, self.from_x, self.from_y, self.land_x, self.land_y = block, from_x, from_y, land_x, land_y
        self.temps, self.load = temps, load
        sem = lambda k: (send.at[k], recv.at[k])
        self.first = [
            remote(block(3, 0), from_x, *sem(0), near_x),
            remote(block(3, 1), from_y, *sem(1), near_y),
            remote(block(1, 0), land_x(0), *sem(2), near_x),
            remote(block(2, 1), land_y(1), *sem(3), near_y),
        ]
        self.second = [
            remote(from_y, land_x(1), *sem(4), near_x),
            remote(from_x, land_y(0), *sem(5), near_y),
        ]

    def begin(self):
        for copy in self.first:
            copy.start()

    def pass_on(self):
        loads = [
            pltpu.make_async_copy(self.block(1, 1), self.temps.at[0], self.load.at[0]),
            pltpu.make_async_copy(self.block(2, 0), self.temps.at[1], self.load.at[1]),
        ]
        for copy in loads:
            copy.start()
        for which, into in ((1, self.from_y), (0, self.from_x)):
            self.first[which].wait_recv()
            loads[1 - which].wait()
            temp = 1 - which

            def body(cut, first):
                into[cut, :] = (into[cut, :].astype(F32) + self.temps[temp, cut, :].astype(F32)).astype(BF16)

            by_pieces(into.shape[0], body, tall(into))
            self.second[temp].start()

    def arrived(self):
        for copy in self.first[2:] + self.second:
            copy.wait_recv()

    def keep(self, out, store):
        for h in range(2):
            loads = [
                pltpu.make_async_copy(src, self.temps.at[k], self.load.at[k])
                for k, src in enumerate((self.block(0, h), self.land_x(h), self.land_y(h)))
            ]
            for copy in loads:
                copy.start()
            for copy in loads:
                copy.wait()

            def body(cut, first):
                self.temps[0, cut, :] = sum(self.temps[k, cut, :].astype(F32) for k in range(3)).astype(BF16)

            by_pieces(self.temps.shape[1], body, tall(self.temps.at[0]))
            copy = pltpu.make_async_copy(self.temps.at[0], out(h), store)
            copy.start()
            copy.wait()

    def settle(self):
        for copy in self.first + self.second:
            copy.wait_send()


def backward_kernel(
    hd, nq, nk, block,
    len_ref, gb_hbm, hidden_hbm, ffn_hbm, ring_hbm, xr_hbm, n1_hbm, tok_hbm, outw_hbm, qkvw_hbm, all_hbm, att_hbm, inv_hbm, pre_hbm,
    gh_hbm, dgate_hbm, landx0, landy0, dup_hbm, ddown_hbm, table_ref, gains_ref, stat_ref, stat2_ref, gain2_ref,
    out_hbm, gin_hbm, fin_hbm, finb_hbm, own_hbm, sum_gate, sum_up, sum_down, mine_o, mine_q, landx1, landy1, landx2, landy2, landx3, landy3, landx4, landy4,
    lines_out, small_out,
    act_v, rows_v, qkvw_v, tok_v, all_v, att_v, inv_v, pre_v, grads, da_all, da_own, da_send, da_got, d_own, d_send, d_got, dpre_v,
    first_v, slots_v, turns_v, piece_v, wide_a, wide_b, temp_a, temp_b,
    go_v, so_v, wide_o, temp_o, gq_v, sq_v, wide_q, temp_q,
    tile_v, otile_v, lines_v, small_v, heads_v, lin1, lin2, lin3, small_r,
    load_sem, zsend, zrecv, piece_sem, xsend, xrecv, xload, own_sem, exsend, exrecv, osend, orecv, qsend, qrecv,
    tile_sem, outs_sem, sum_sem, smsend, smrecv,
):
    seqs, _, slots = all_v.shape
    span = slots // 2
    width = act_v.shape[1]
    half = width // 2
    groups = nq // nk
    share = span // 4
    row, core, rank = lax.axis_index("dp"), lax.axis_index("context"), lax.axis_index("tensor")
    start = core * span
    near = [row, xor_one(row), (row + 2) % 4, 3 - row]
    near_x, near_y, near_core = {"dp": near[1]}, {"dp": near[2]}, {"context": 1 - core}
    z_right, z_left, z_far = {"tensor": (rank + 1) % 4}, {"tensor": (rank + 3) % 4}, {"tensor": (rank + 2) % 4}
    first_core = core == 0

    def load(k, src, dst):
        copy = pltpu.make_async_copy(src, dst, load_sem.at[k])
        copy.start()
        return copy

    load_gb = load(0, gb_hbm, act_v)
    load_outw = load(1, outw_hbm, rows_v)
    load_att = [
        load(2, all_hbm, all_v), load(3, att_hbm, att_v), load(4, inv_hbm, inv_v), load(5, pre_hbm, pre_v),
    ]
    load_tok = load(6, tok_hbm, tok_v)
    load_qkvw = load(7, qkvw_hbm, qkvw_v)

    def piece_rows(s, m):
        return pl.ds(pl.multiple_of(s * span + m * share, share), share)

    def load_piece(s, m):
        return pltpu.make_async_copy(ffn_hbm.at[piece_rows(s, m), :], piece_v.at[s], piece_sem.at[s])

    greet([(None, d) for d in (near_x, near_y, {"dp": near[3]}, near_core, z_right, z_left, z_far)])

    last = seqs - 1
    inner = (rank % 3) != 0
    came = []
    for k, slot in enumerate((0, 1, 3)):
        came.append(pltpu.make_async_copy(ring_hbm.at[k], slots_v.at[0, slot], load_sem.at[12 + k]))

    @pl.when(inner)
    def _():
        for copy in came:
            copy.start()

    def ffn_own(s):
        def own(m):
            load_piece(s, m).wait()
            return lambda cut: piece_v[s, cut, :]

        return own

    def first_own(s):
        return lambda m: lambda cut: first_v[s, m, cut, :]

    ffn_rings = [
        Fold(
            rank, lambda m, s=s: ffn_hbm.at[piece_rows(s, m), :], ffn_own(s), slots_v.at[s], (slots_v.at[s, 3], slots_v.at[s, 4]),
            zsend.at[s], zrecv.at[s], came if s == 0 else None,
        )
        for s in range(seqs)
    ]
    first_rings = [
        Fold(
            rank, lambda m, s=s: first_v.at[s, m], first_own(s), turns_v.at[s], (fin_hbm.at[s], finb_hbm.at[s]),
            zsend.at[seqs + s], zrecv.at[seqs + s],
        )
        for s in range(seqs)
    ]
    for s in range(1, seqs):
        ffn_rings[s].begin()
    for s in range(seqs):
        load_piece(s, jnp.where(inner, ffn_rings[s].added[0], rank)).start()

    def ffn_step(s, k):
        ffn_rings[s].step(k)

        @pl.when(inner)
        def _():
            load_piece(s, ffn_rings[s].added[k + 1] if k < 2 else rank).start()

    def in_hbm(ref, axis):
        size = ref.shape[axis] // 4
        h2 = (size if axis == 0 else ref.shape[0]) // 2

        def get(k, h):
            if axis == 0:
                return ref.at[pl.ds(k * size + h * h2, h2), :]
            return ref.at[pl.ds(h * h2, h2), pl.ds(k * size, size)]

        return get

    def halves(ref):
        h2 = ref.shape[0] // 2
        return lambda h: ref.at[pl.ds(h * h2, h2), :]

    def in_vmem(ref):
        h2 = ref.shape[1] // 2
        return lambda k, h: ref.at[k, pl.ds(h * h2, h2), :]

    def scatter(i, get, wide, land_x, land_y, temps):
        return Scatter(get, wide.at[0], wide.at[1], land_x, land_y, temps, xsend.at[i], xrecv.at[i], xload.at[i], near_x, near_y)

    s_gate = scatter(0, in_hbm(dgate_hbm, 0), wide_a, halves(landx0), halves(landy0), temp_a)
    s_up = scatter(0, in_hbm(dup_hbm, 0), wide_a, halves(landx1), halves(landy1), temp_a)
    s_down = scatter(1, in_hbm(ddown_hbm, 1), wide_b, halves(landx2), halves(landy2), temp_b)
    s_out = scatter(2, in_vmem(go_v), wide_o, halves(landx3), halves(landy3), temp_o)
    s_qkv = scatter(3, in_vmem(gq_v), wide_q, halves(landx4), halves(landy4), temp_q)
    s_up.begin()
    ffn_step(0, 0)
    ffn_step(0, 1)

    load_gb.wait()
    load_outw.wait()

    def give(s):
        return remote(da_send.at[s], da_got.at[s], exsend.at[0, s], exrecv.at[0, s], near_core)

    def exchange(s):
        return remote(d_send.at[s], d_got.at[s], exsend.at[1, s], exrecv.at[1, s], near_core)

    def branch_rows(s, carry):
        here = pl.ds(pl.multiple_of(s * span, span), span)
        parts = []
        for q in range(2):
            cut = slice(q * (nq * hd // 2), (q + 1) * (nq * hd // 2))
            da = dot_nt(rows_v[0, cut, :], act_v[here, :half]) + dot_nt(rows_v[1, cut, :], act_v[here, half:])
            parts.append(da.astype(BF16))
        da_own[s] = jnp.where(first_core, parts[0], parts[1])
        da_send[s] = jnp.where(first_core, parts[1], parts[0])
        give(s).start()
        return carry

    lax.fori_loop(0, seqs, branch_rows, 0)

    def load_x(s):
        return [pltpu.make_async_copy(xr_hbm.at[s, :, pl.ds(k * half, half)], rows_v.at[k], load_sem.at[10 + k]) for k in range(2)]

    for copy in load_x(0):
        copy.start()
    for copy in load_att:
        copy.wait()

    scale = log2e / math.sqrt(hd)
    back = 1.0 / math.sqrt(hd)
    krow = lax.broadcasted_iota(jnp.int32, (block, groups * block), 0)
    qcol = lax.broadcasted_iota(jnp.int32, (block, groups * block), 1) % block
    base = groups * hd

    def attention(s):
        give(s).wait_recv()
        low, high = join_positions(core, da_own[s], da_got[s])
        da_all[:, :span] = low
        da_all[:, span:] = high
        length = len_ref[s]
        grads[base:, :] = jnp.zeros((2 * hd, slots), F32)
        for i in range(slots // block):
            cut = slice(i * block, (i + 1) * block)
            q = jnp.concatenate([all_v[s, g * hd : (g + 1) * hd, cut] for g in range(groups)], axis=1)
            da = jnp.concatenate([da_all[g * hd : (g + 1) * hd, cut] for g in range(groups)], axis=1)
            at = jnp.concatenate([att_v[s, g * hd : (g + 1) * hd, cut] for g in range(groups)], axis=1)
            inv = jnp.concatenate([inv_v[s, g : g + 1, cut] for g in range(groups)], axis=1)
            delta = jnp.sum(at.astype(F32) * da.astype(F32), axis=0, keepdims=True)
            dq = jnp.zeros((hd, groups * block), F32)
            for j in range(i + 1):
                kcut = slice(j * block, (j + 1) * block)
                key = all_v[s, base : base + hd, kcut]
                score = dot_tn(key, q) * scale
                ok = (krow + j * block) < length
                if j == i:
                    ok = ok & (krow <= qcol)
                p = jnp.where(ok, jnp.exp2(score) * inv, 0.0)
                dp = dot_tn(all_v[s, base + hd : base + 2 * hd, kcut], da)
                ds = (p * (dp - delta)).astype(BF16)
                dq = dq + dot_nn(key, ds)
                grads[base : base + hd, kcut] += dot_nt(q, ds) * back
                grads[base + hd : base + 2 * hd, kcut] += dot_nt(da, p.astype(BF16))
            dq = dq * back
            for g in range(groups):
                grads[g * hd : (g + 1) * hd, cut] = dq[:, g * block : (g + 1) * block]
        mine, theirs = join_positions(core, grads[:, :span], grads[:, span:])
        d_own[s] = mine.astype(BF16)
        d_send[s] = theirs.astype(BF16)
        exchange(s).start()

    quarter = hd // 2
    cosine, sine = table_ref[:quarter, :], table_ref[quarter : 2 * quarter, :]
    qgain, kgain = table_ref[2 * quarter : 2 * quarter + hd, 0:1], table_ref[2 * quarter + hd :, 0:1]
    sides = (nq // 2, nk // 2, nk // 2)
    copies_in_tensor = 1.0 / lax.axis_size("tensor")
    lines_v[:8, :] = jnp.zeros((8, width), F32)
    lines_v[8:, :] = gain2_ref[...] * copies_in_tensor
    heads_v[...] = jnp.zeros_like(heads_v)
    valid_slots = jnp.int32(0)
    for s in range(seqs):
        valid_slots = valid_slots + jnp.clip(len_ref[s] - start, 0, span)
    count = valid_slots.astype(F32) * (copies_in_tensor / 128.0)
    small_v[...] = jnp.zeros_like(small_v)
    for k in range(2):
        both = stat_ref[k] + stat2_ref[k]
        small_v[1 + k : 2 + k, :] = jnp.sum(both, axis=0, keepdims=True) * copies_in_tensor
    small_v[4:5, :] = jnp.broadcast_to(count, (1, 128))
    load_qkvw.wait()

    def fold_columns(values):
        return sum(values[:, k * 128 : (k + 1) * 128] for k in range(values.shape[1] // 128))

    def heads_rows(s):
        exchange(s).wait_recv()
        low, high = join_positions(core, d_own[s].astype(F32), d_got[s].astype(F32))
        parts = [[], [], []]
        for side in (low, high):
            at = 0
            for kind, number in enumerate(sides):
                for _ in range(number):
                    parts[kind].append(side[at : at + hd])
                    at += hd
        done = []
        for h in range(nq + nk):
            kind = 0 if h < nq else 1
            g = parts[kind][h - kind * nq]
            a, b = g[: hd // 2], g[hd // 2 :]
            g = jnp.concatenate([a * cosine + b * sine, b * cosine - a * sine], axis=0)
            v = pre_v[s, h * hd : (h + 1) * hd, :]
            inv = lax.rsqrt(jnp.mean(v * v, axis=0, keepdims=True) + epsilon)
            hat = v * inv
            heads_v[kind * hd : (kind + 1) * hd, :] += fold_columns(g * hat)
            gg = g * (qgain if kind == 0 else kgain)
            done.append(inv * (gg - hat * jnp.mean(gg * hat, axis=0, keepdims=True)))
        done += parts[2]
        for h in range(nq + 2 * nk):
            pair = h % 2
            if pair == 0:
                two = jnp.concatenate([done[h], done[h + 1]], axis=0).T.astype(BF16)
                dpre_v[pl.ds(pl.multiple_of(s * span, span), span), h * hd : (h + 2) * hd] = two
        for copy in load_x(s):
            copy.wait()
        for m in range(4):
            rows = slice(m * share, (m + 1) * share)
            xs = [rows_v[k, rows, :].astype(F32) for k in range(2)]
            mean = sum(jnp.sum(x * x, axis=-1, keepdims=True) for x in xs) * (1.0 / width)
            inv = lax.rsqrt(mean + epsilon)
            dpre = dpre_v[pl.ds(pl.multiple_of(s * span + m * share, share), share), :]
            for k in range(2):
                part = dot_nt(dpre, qkvw_v[k])
                cut = slice(k * half, (k + 1) * half)
                first_v[s, m, :, cut] = part.astype(BF16)
                both = part * (xs[k] * inv)
                lines_v[:8, cut] += sum(both[8 * r : 8 * r + 8] for r in range(share // 8))

    def sequence(s, carry):
        attention(s)

        @pl.when(s == last)
        def _():
            ffn_step(1, 1)
            s_up.pass_on()

        heads_rows(s)

        @pl.when(s == 0)
        def _():
            for copy in load_x(1):
                copy.start()
            first_rings[0].begin()
            ffn_step(1, 0)
            ffn_step(0, 2)
            s_down.begin()

        @pl.when(s == last)
        def _():
            first_rings[1].begin()

        return carry

    lax.fori_loop(0, seqs, sequence, 0)

    def hop_copies(n, items):
        base_at = (0, 1, 4, 5, 8)[n]
        return [
            remote(src, dst, smsend.at[base_at + i], smrecv.at[base_at + i], device) for i, (device, src, dst, _) in enumerate(items)
        ]

    def hop_begin(n, items):
        for copy in hop_copies(n, items):
            copy.start()

    def hop_end(n, items):
        for copy in hop_copies(n, items):
            copy.wait()
        for _, _, dst, place_to in items:
            if place_to is None:
                small_v[...] += dst[...]
            else:
                lines_v[:, place_to] += dst[...]

    piece = width // 8

    def columns(k):
        return slice(k * piece, (k + 1) * piece)

    def view(k, count=1):
        return lines_v.at[:, pl.ds(k * piece, count * piece)]

    hop_core = [(near_core, view(4, 4), lin1, slice(0, half))]
    near_all = [near_x, near_y, {"dp": near[3]}]
    hop_lines = [(near_all[k], view(1 + k), lin2.at[k], columns(0)) for k in range(3)]
    hop_small = [(near_core, small_v, small_r.at[0], None)]
    hop_square = [(near_all[k], small_v, small_r.at[1 + k], None) for k in range(3)]
    z_all = [z_right, z_far, z_left]
    hop_chain = [(z_all[k], view(0), lin3.at[k], columns(0)) for k in range(3)]
    hop_chain += [(z_all[k], small_v, small_r.at[4 + k], None) for k in range(3)]
    hop_begin(0, hop_core)

    load_tok.wait()
    blocks_o = [remote(so_v.at[k], go_v.at[k], osend.at[k], orecv.at[k], near_core) for k in range(4)]
    size_o = half // 4
    for k in range(4):
        cut = slice(half + k * size_o, half + (k + 1) * size_o)
        so_v[k] = dot_tn(tok_v[...], act_v[:, cut]).astype(BF16)
        blocks_o[k].start()
    ffn_step(1, 2)
    for k in range(4):
        blocks_o[k].wait_recv()
        cut = slice(k * size_o, (k + 1) * size_o)
        go_v[k] = (dot_tn(tok_v[...], act_v[:, cut]) + go_v[k].astype(F32)).astype(BF16)
    s_out.begin()
    load_n1 = load(0, n1_hbm, act_v)
    hop_end(0, hop_core)
    hop_begin(1, hop_lines)
    load_n1.wait()
    blocks_q = [remote(sq_v.at[k], gq_v.at[k], qsend.at[k], qrecv.at[k], near_core) for k in range(4)]
    size_q = half // 4
    for k in range(4):
        cut = slice(half + k * size_q, half + (k + 1) * size_q)
        sq_v[k] = dot_tn(act_v[:, cut], dpre_v[...]).astype(BF16)
        blocks_q[k].start()
    for k in range(4):
        blocks_q[k].wait_recv()
        cut = slice(k * size_q, (k + 1) * size_q)
        gq_v[k] = (dot_tn(act_v[:, cut], dpre_v[...]) + gq_v[k].astype(F32)).astype(BF16)
    s_qkv.begin()
    keeps = [
        pltpu.make_async_copy(go_v.at[0], mine_o, own_sem.at[0]),
        pltpu.make_async_copy(gq_v.at[0], mine_q, own_sem.at[1]),
    ]
    keeps += [pltpu.make_async_copy(first_v.at[s, rank], own_hbm.at[s], own_sem.at[2 + s]) for s in range(seqs)]
    for copy in keeps:
        copy.start()


    def place(tile, dst, s):
        for o in range(2):
            for k in range(4):
                b = near[k] * 2 + (core if o == 0 else 1 - core)
                cut = pl.ds(pl.multiple_of(b * piece, piece), piece)
                pltpu.make_async_copy(tile.at[:, pl.ds((o * 4 + k) * piece, piece)], dst.at[s, :, cut], outs_sem).start()
        pltpu.make_async_copy(tile, dst.at[s], outs_sem).wait()

    def out_share(s):
        keep = pltpu.make_async_copy(hidden_hbm.at[piece_rows(s, rank), :], tile_v, tile_sem.at[0])
        keep.start()
        ffn_rings[s].arrived()
        read = ffn_rings[s].own(rank)
        keep.wait()

        def body(cut, first):
            ffn = slots_v[s, 3, cut, :].astype(F32) + read(cut).astype(F32)
            ffn = ffn + jnp.where(inner, slots_v[s, 4, cut, :].astype(F32), 0.0)
            otile_v[cut, :] = (tile_v[cut, :] + ffn).astype(BF16)
            spot = start + rank * share + first + lax.broadcasted_iota(jnp.int32, (16, 1), 0)
            valid = (spot < len_ref[s]).astype(F32)
            small_v[3:4, :] += jnp.sum(fold_lanes(valid * ffn * ffn), axis=0, keepdims=True)

        by_pieces(share, body)
        place(otile_v, out_hbm, s)

    def in_share(s):
        first_rings[s].arrived()
        tiles = (piece_v.at[0], piece_v.at[1], otile_v)
        rows = pl.ds(pl.multiple_of(rank * share, share), share)
        loads = [
            pltpu.make_async_copy(src, dst, load_sem.at[k])
            for k, (src, dst) in enumerate(zip((fin_hbm.at[s], finb_hbm.at[s], xr_hbm.at[s, rows, :]), tiles))
        ]
        loads.append(pltpu.make_async_copy(gh_hbm.at[s], tile_v, load_sem.at[3]))
        for copy in loads:
            copy.start()
        gain = jnp.concatenate([gains_ref[b, 0:1, :] for b in range(8)], axis=1).astype(F32)
        for copy in loads:
            copy.wait()

        def body(cut, at):
            e = piece_v[0, cut, :].astype(F32) + first_v[s, rank, cut, :].astype(F32)
            e = e + jnp.where(inner, piece_v[1, cut, :].astype(F32), 0.0)
            x = otile_v[cut, :].astype(F32)
            inv = inverse_rms(x)
            hat = x * inv
            eg = e * gain
            tile_v[cut, :] = tile_v[cut, :] + inv * (eg - hat * jnp.mean(eg * hat, axis=-1, keepdims=True))

        by_pieces(share, body)
        place(tile_v, gin_hbm, s)

    small_v[0:1, :] = jnp.sum(heads_v[...].T, axis=0, keepdims=True)
    first_rings[0].step(0)
    out_share(0)
    s_down.pass_on()
    out_share(1)
    hop_end(1, hop_lines)
    hop_begin(2, hop_small)
    hop_end(2, hop_small)
    hop_begin(3, hop_square)
    first_rings[0].step(1)
    first_rings[0].step(2)
    s_out.pass_on()
    s_qkv.pass_on()
    s_gate.keep(halves(sum_gate), sum_sem)
    s_up.arrived()
    s_up.keep(halves(sum_up), sum_sem)
    first_rings[1].step(0)
    hop_end(3, hop_square)
    hop_begin(4, hop_chain)
    s_down.arrived()
    s_down.keep(halves(sum_down), sum_sem)
    first_rings[1].step(1)
    first_rings[1].step(2)
    for s in range(last):
        in_share(s)
    hop_end(4, hop_chain)
    lines_out[...] = lines_v[:, :piece]
    small_out[...] = small_v[...]
    for item in (s_out, s_qkv):
        item.arrived()
    first_rings[last].arrived()
    for copy in keeps:
        copy.wait()
    for ring in ffn_rings + first_rings:
        ring.settle()
    for item in (s_up, s_down, s_out, s_qkv):
        item.settle()
    for copy in blocks_o + blocks_q:
        copy.wait_send()
    for s in range(seqs):
        give(s).wait_send()
        exchange(s).wait_send()


def backward(
    lengths, gb, hidden_rows, ffn, ring, xr, n1, tok, outw, qkvw, everything, att, inv, pre, gh, dgate, landx, landy, dup, ddown,
    table, gains, stat, stat2, gain2_part, hd, nq, nk,
):
    seqs, span, width = xr.shape
    half = width // 2
    groups = nq // nk
    share = span // 4
    piece = width // 8
    hidden = dup.shape[1]
    cols = qkvw.shape[2]
    feat = nq * hd
    block = min(256, span)
    any_space = pl.BlockSpec(memory_space=pl.ANY)
    vmem = pl.BlockSpec(memory_space=pltpu.VMEM)
    dma = pltpu.SemaphoreType.DMA
    hold = lambda *dims: pltpu.VMEM(dims, BF16)
    wide = lambda *dims: pltpu.VMEM(dims, F32)
    token = shape((seqs, share, width), BF16)
    big = [token, shape((seqs - 1, share, width), F32)] + [token] * 3 + [shape((piece, hidden), BF16)] * 2 + [shape((hidden, piece), BF16)]
    big += [shape((feat, piece), BF16), shape((piece, cols), BF16)]
    big += [shape((piece, hidden), BF16)] * 2 + [shape((hidden, piece), BF16)] * 2
    big += [shape((feat, piece), BF16)] * 2 + [shape((piece, cols), BF16)] * 2
    small = [shape((16, piece), F32), shape((8, 128), F32)]
    rows = everything.shape[1]
    scratch = [
        hold(seqs * span, width), hold(2, span, half), hold(2, half, cols), hold(seqs * span, feat), hold(*everything.shape), hold(*att.shape),
        wide(*inv.shape), wide(*pre.shape), wide(rows, 2 * span), hold(groups * hd, 2 * span),
        hold(seqs, feat // 2, span), hold(seqs, feat // 2, span), hold(seqs, feat // 2, span),
        hold(seqs, rows, span), hold(seqs, rows, span), hold(seqs, rows, span), hold(seqs * span, cols),
        hold(seqs, 4, share, width), hold(seqs, 5, share, width), hold(seqs, 3, share, width), hold(seqs, share, width),
        hold(2, piece // 2, hidden), hold(2, hidden // 2, piece), hold(3, piece // 2, hidden), hold(3, hidden // 2, piece),
        hold(4, feat, piece), hold(4, feat, piece), hold(2, feat // 2, piece), hold(2, feat // 2, piece),
        hold(4, piece, cols), hold(4, piece, cols), hold(2, piece // 2, cols), hold(2, piece // 2, cols),
        wide(share, width), hold(share, width),
        wide(16, width), wide(8, 128), wide(2 * hd, 128), wide(16, half), wide(3, 16, piece), wide(3, 16, piece), wide(7, 8, 128),
        dma((15,)), dma((2 * seqs,)), dma((2 * seqs, 5)), dma((seqs,)), dma((4, 6)), dma((4, 6)), dma((4, 3)), dma((2 + seqs,)),
        dma((2, seqs)), dma((2, seqs)), dma((4,)), dma((4,)), dma((4,)), dma((4,)), dma((2,)), dma(()), dma(()), dma((14,)), dma((14,)),
    ]
    tokens = seqs * span
    return pl.pallas_call(
        functools.partial(backward_kernel, hd, nq, nk, block),
        in_specs=[SMEM] + [any_space] * 19 + [vmem] * 5,
        out_specs=[any_space] * len(big) + [vmem] * 2,
        out_shape=big + small,
        scratch_shapes=scratch,
        compiler_params=pltpu.CompilerParams(vmem_limit_bytes=VMEM_MOST, collective_id=3, has_side_effects=True),
        cost_estimate=cost(4 * tokens * width * (cols + feat), 60 * tokens * width),
        name="attention_backward",
    )(
        lengths, gb, hidden_rows, ffn, ring, xr, n1, tok, outw, qkvw, everything, att, inv, pre, gh, dgate, landx, landy, dup, ddown,
        table, gains, stat, stat2, gain2_part,
    )


def results_kernel(
    hd, nqc, nkc, count,
    sum_gate, sum_up, sum_down, mine_o, lx3, ly3, mine_q, lx4, ly4, gh, xr, fin, finb, own, out, early, gains_ref, lines_ref, small_ref,
    output, gin, ggate, gup, gdown, gout, gq, gk, gv, gain_a, gain_b, gain_q, gain_k, rms,
    gate_i, up_i, down_i, o_i, q_i, gate_o, up_o, down_o, o_o, q_o, gh_v, x_v, fin_v, finb_v, own_v, early_v, out_v,
    in_sem, token_sem, out_sem, place_sem, copy_sem,
):
    row, core, rank = lax.axis_index("dp"), lax.axis_index("context"), lax.axis_index("tensor")
    near = [row, xor_one(row), (row + 2) % 4, 3 - row]
    seqs, share, width = out_v.shape
    last = seqs - 1
    piece = width // 8
    sums = (
        ((sum_gate,), gate_i, gate_o, ((0, ggate),)),
        ((sum_up,), up_i, up_o, ((0, gup),)),
        ((sum_down,), down_i, down_o, ((0, gdown),)),
        ((mine_o, lx3, ly3), o_i, o_o, ((0, gout),)),
        ((mine_q, lx4, ly4), q_i, q_o, ((0, gq), (nqc, gk), (nqc + nkc, gv))),
    )
    simple = [
        (pltpu.make_async_copy(out, out_v, copy_sem.at[0]), pltpu.make_async_copy(out_v, output, copy_sem.at[1])),
        (pltpu.make_async_copy(early, early_v, copy_sem.at[2]), pltpu.make_async_copy(early_v, gin.at[pl.ds(0, last)], copy_sem.at[3])),
    ]

    def loads(i):
        return [pltpu.make_async_copy(src, sums[i][1].at[k], in_sem.at[i, k]) for k, src in enumerate(sums[i][0])]

    mine = pl.ds(pl.multiple_of(rank * share, share), share)
    tokens = [
        pltpu.make_async_copy(src, dst, token_sem.at[k])
        for k, (src, dst) in enumerate(
            ((gh.at[last], gh_v), (xr.at[last, mine, :], x_v), (fin.at[last], fin_v), (finb.at[last], finb_v), (own.at[last], own_v))
        )
    ]
    for i in range(len(sums)):
        for copy in loads(i):
            copy.start()
    for copy in tokens + [first for first, _ in simple]:
        copy.start()

    first = jnp.sum(lines_ref[:8, :], axis=0, keepdims=True)
    second = jnp.sum(lines_ref[8:, :], axis=0, keepdims=True)
    gain_a[...] = first.reshape(gain_a.shape)
    gain_b[...] = second.reshape(gain_b.shape)
    gain_q[...] = small_ref[0:1, :hd].reshape(gain_q.shape)
    gain_k[...] = small_ref[0:1, hd : 2 * hd].reshape(gain_k.shape)
    total = jnp.sum(small_ref[4:5, :], keepdims=True) * count
    for k in range(3):
        square = jnp.sum(small_ref[1 + k : 2 + k, :], keepdims=True) / total
        rms[k] = jnp.max(jnp.sqrt(jnp.broadcast_to(square, (8, 128))))

    stores = []
    for i, (terms, came, total_v, parts) in enumerate(sums):
        for copy in loads(i):
            copy.wait()

        def body(cut, at):
            total_v[cut, :] = sum(came[k, cut, :].astype(F32) for k in range(len(terms)))

        by_pieces(total_v.shape[0], body, tall(total_v))
        for n, (at, dst) in enumerate(parts):
            stores.append(pltpu.make_async_copy(total_v.at[:, pl.ds(at, dst.shape[1])], dst, out_sem.at[i, n]))
            stores[-1].start()
    for first, second in simple:
        first.wait()
        second.start()

    gain = jnp.concatenate([gains_ref[b, 0:1, :] for b in range(8)], axis=1).astype(F32)
    for copy in tokens:
        copy.wait()
    inner = (rank % 3) != 0

    def body(cut, at):
        e = fin_v[cut, :].astype(F32) + own_v[cut, :].astype(F32)
        e = e + jnp.where(inner, finb_v[cut, :].astype(F32), 0.0)
        x = x_v[cut, :].astype(F32)
        inv = inverse_rms(x)
        hat = x * inv
        eg = e * gain
        gh_v[cut, :] = gh_v[cut, :] + inv * (eg - hat * jnp.mean(eg * hat, axis=-1, keepdims=True))

    by_pieces(share, body)
    for o in range(2):
        for k in range(4):
            b = near[k] * 2 + (core if o == 0 else 1 - core)
            cut = pl.ds(pl.multiple_of(b * piece, piece), piece)
            src = gh_v.at[:, pl.ds((o * 4 + k) * piece, piece)]
            stores.append(pltpu.make_async_copy(src, gin.at[last, :, cut], place_sem.at[o * 4 + k]))
            stores[-1].start()
    for copy in stores + [second for _, second in simple]:
        copy.wait()


def finish_results(sums, mine_o, mine_q, lands_o, lands_q, gh, xr, fin, finb, own, out, early, gains, lines, small, hd, nqc, nkc):
    seqs, share, width = out.shape
    hidden = sums[0].shape[1]
    piece = width // 8
    any_space = pl.BlockSpec(memory_space=pl.ANY)
    vmem = pl.BlockSpec(memory_space=pltpu.VMEM)
    dma = pltpu.SemaphoreType.DMA
    blocks = [(piece, hidden), (piece, hidden), (hidden, piece), mine_o.shape, mine_q.shape]
    terms = (1, 1, 1, 3, 3)
    outs = [shape(out.shape, BF16), shape(out.shape, F32)] + [shape(b, F32) for b in blocks[:4]]
    outs += [shape((piece, size), F32) for size in (nqc, nkc, nkc)]
    tiny = [shape((size,), F32) for size in (piece, piece, hd, hd)]
    token = pltpu.VMEM((share, width), BF16)
    return pl.pallas_call(
        functools.partial(results_kernel, hd, nqc, nkc, float(width)),
        in_specs=[any_space] * 16 + [vmem] * 3,
        out_specs=[any_space] * len(outs) + [vmem] * 4 + [SMEM],
        out_shape=outs + tiny + [shape((3,), F32)],
        scratch_shapes=[pltpu.VMEM((n,) + tuple(b), BF16) for n, b in zip(terms, blocks)]
        + [pltpu.VMEM(b, F32) for b in blocks]
        + [pltpu.VMEM((share, width), F32), token, token, token, token, pltpu.VMEM(early.shape, F32), pltpu.VMEM(out.shape, BF16)]
        + [dma((5, 3)), dma((5,)), dma((5, 3)), dma((8,)), dma((4,))],
        compiler_params=PARAMS,
        cost_estimate=cost(30 * piece * hidden, 40 * piece * hidden),
        name="results",
    )(*sums, mine_o, *lands_o, mine_q, *lands_q, gh, xr, fin, finb, own, out, early, gains, lines, small)


def per_device_general(
    inputs,
    cotangent,
    lengths,
    w_query,
    key_projection_weight,
    value_projection_weight,
    w_output,
    w_gate,
    w_up,
    w_down,
    attn_gain,
    ffn_gain,
    query_gain,
    key_gain,
):
    seqs, span, width = inputs.shape
    hd = query_gain.shape[0]
    nq = w_query.shape[1] // hd
    nk = key_projection_weight.shape[1] // hd
    groups = nq // nk
    dp = lax.axis_size("dp")
    tensor = lax.axis_size("tensor")
    core = lax.axis_index("context")
    rank = lax.axis_index("tensor")
    chunks = 2
    rows = span // chunks
    share = span // tensor
    lengths = lengths.astype(jnp.int32)
    start = (core * span).astype(jnp.int32)
    core1 = core.astype(jnp.int32).reshape(1)
    ids = block_order(dp, core)
    order = 2 * dp if (width // (2 * dp)) % 128 == 0 else 1

    positions = start + jnp.arange(span, dtype=jnp.int32)
    freqs = rope_base ** (-(jnp.arange(hd // 2, dtype=F32) * (2.0 / hd)))
    angles = freqs[:, None] * positions.astype(F32)[None, :]
    cosine, sine = jnp.cos(angles), jnp.sin(angles)
    qgain = query_gain.astype(F32).reshape(hd, 1)
    kgain = key_gain.astype(F32).reshape(hd, 1)

    w_qkv = jnp.concatenate([w_query, key_projection_weight, value_projection_weight], axis=1)
    saved = []
    gains = gather_blocks(jnp.stack([attn_gain, ffn_gain]), 1)
    gains = jnp.concatenate([gains[0], gains[1]], axis=1).astype(F32)
    gain1, gain2 = gains[0:1], gains[1:2]
    qkv = gather_blocks(w_qkv, 0)
    out_w = gather_blocks(w_output, 1)
    gate = gather_blocks(w_gate, 0)
    up = gather_blocks(w_up, 0)
    down = gather_blocks(w_down, 1)

    scal = jnp.concatenate([lengths, start.reshape(1), ids])
    x_in, cot_in = inputs, cotangent
    if order == 1:
        x_in, cot_in = to_relative(x_in, dp, core), to_relative(cot_in, dp, core)
    xr, n1, gf = begin(x_in, cot_in, gain1, scal, order)

    parts, tok = [], []
    for s in range(seqs):
        pre, own, oth = heads(n1, s, qkv, cosine, sine, qgain, kgain, core1, hd, nq, nk)
        seq_scal = jnp.stack([lengths[s], core.astype(jnp.int32)])
        everything, att, inv, mine, theirs = attend(seq_scal, own, over_core(oth), groups)
        branched = branch(mine, over_core(theirs), out_w, core1, chunks)
        saved.append((pre, everything, att, inv, seq_scal))
        tok.append(jnp.swapaxes(branched[0], 0, 1))
        parts.append(branched[1:])
    tok = jnp.concatenate(tok, axis=0)

    stats = jnp.zeros((2,), F32)
    hidden_all, n2_all = [], []
    for s in range(seqs):
        for k in range(chunks):
            terms = [lax.psum(parts[s][k], "tensor")]
            place = jnp.stack([lengths[s], start + k * rows])
            hidden, n2, stat = second_norm(place, xr, s, k, gain2, terms)
            hidden_all.append(hidden)
            n2_all.append(n2)
            stats = stats + stat[:2, 0]
    hidden_all, n2_all = jnp.concatenate(hidden_all), jnp.concatenate(n2_all)

    ffn_squares = jnp.zeros((), F32)
    out_shares = []

    def piece_of(arrays):
        per = arrays[0].shape[0] // share

        def piece(k):
            found = lax.dynamic_slice_in_dim(arrays[0], jnp.minimum(k, per - 1) * share, share, 0)
            for m in range(1, len(arrays)):
                here = lax.dynamic_slice_in_dim(arrays[m], jnp.clip(k - m * per, 0, per - 1) * share, share, 0)
                found = jnp.where(k >= m * per, here, found)
            return found

        return piece

    def share_scalars(s):
        head = jnp.stack([rank.astype(jnp.int32), lengths[s], start + rank.astype(jnp.int32) * share, jnp.int32(tensor)])
        return jnp.concatenate([head, ids])

    def flat(nested):
        return [item for inner_list in nested for item in inner_list]

    def slices(array, count):
        size = array.shape[0] // count
        return [array[i * size : (i + 1) * size] for i in range(count)]

    def reduced(lefts, rights, axis):
        oth = weight_grad(lefts, rights, 1, axis)
        own = weight_grad(lefts, rights, 0, axis, over_core(oth))
        return scatter_blocks(own, axis)

    inner, gg, gu, ffn, gn = [[[None] * chunks for _ in range(seqs)] for _ in range(5)]
    for s in range(seqs):
        for k in range(chunks):
            inner[s][k], gg[s][k], gu[s][k], ffn[s][k], gn[s][k] = feed(
                n2_all, s * chunks + k, rows, gf, s, k, gate, up, down
            )
    gain2_grad = jnp.zeros((1, width), F32)
    gb, gh = [[[None] * chunks for _ in range(seqs)] for _ in range(2)]
    for s in range(seqs):
        for k in range(chunks):
            terms = [lax.psum(gn[s][k], "tensor")]
            gb[s][k], gh[s][k], gain_part = second_back(hidden_all, s * chunks + k, gf, s, k, gain2, terms)
            gain2_grad = gain2_grad + gain_part
    gf_list = slices(gf.reshape(seqs * span, width), seqs * chunks)
    n2_list = slices(n2_all, seqs * chunks)
    grad_w_down = reduced(flat(inner), gf_list, 1)
    grad_w_gate = reduced(n2_list, flat(gg), 0)
    grad_w_up = reduced(n2_list, flat(gu), 0)
    for s in range(seqs):
        got = ring_scatter(piece_of(ffn[s]), tensor, rank)
        halves = [hidden_all[(s * chunks + k) * rows : (s * chunks + k + 1) * rows] for k in range(chunks)]
        out, stat = output_share(share_scalars(s), got, ffn[s], halves, order)
        out_shares.append(out)
        ffn_squares = ffn_squares + stat[0, 0]

    gain1_grad = jnp.zeros((1, width), F32)
    head_gain = jnp.zeros((2 * hd,), F32)
    dpres, in_shares = [], []
    for s in range(seqs):
        pre, everything, att, inv, seq_scal = saved[s]
        da_own, da_oth = branch_back(gb[s], out_w, core1)
        d_own, d_oth = attend_back(seq_scal, everything, att, inv, da_own, over_core(da_oth), groups)
        dpre, first, gain_part, hg = heads_back(
            d_own, over_core(d_oth), pre, cosine, sine, qgain, kgain, xr, s, qkv, core1, hd, nq, nk
        )
        gain1_grad = gain1_grad + gain_part
        head_gain = head_gain + hg[:, 0]
        dpres.append(dpre)
        got = ring_scatter(piece_of([first]), tensor, rank)
        in_shares.append(input_share(share_scalars(s), got, first, gh[s], xr, s, gain1, order))

    att_list = [tok[i * rows : (i + 1) * rows] for i in range(seqs * chunks)]
    grad_w_output = reduced(att_list, flat(gb), 1)
    grad_qkv = reduced([n1[s] for s in range(seqs)], dpres, 0)
    nqc, nkc = nq * hd, nk * hd
    grad_w_query = grad_qkv[:, :nqc]
    grad_w_key = grad_qkv[:, nqc : nqc + nkc]
    grad_w_value = grad_qkv[:, nqc + nkc :]

    gain2_grad = gain2_grad / tensor
    counts = jnp.sum(jnp.clip(lengths - start, 0, span)).astype(F32) / tensor
    small = jnp.concatenate([head_gain, stats / tensor, ffn_squares.reshape(1), counts.reshape(1)])
    small = jnp.pad(small, (0, (-small.shape[0]) % 128)).reshape(1, -1)
    lines = jnp.concatenate([gain1_grad, gain2_grad], axis=0)
    piece = width // (2 * dp)
    lines = to_absolute(lines, dp, core)
    lines, small = lax.psum((lines, small), ("dp", "context", "tensor"))
    lines = lax.dynamic_slice_in_dim(lines, lax.axis_index(("dp", "context")) * piece, piece, 1)
    small = small[0]
    rms_values = jnp.sqrt(small[2 * hd : 2 * hd + 3] / (small[2 * hd + 3] * width))

    output = jnp.stack(out_shares)
    grad_inputs = jnp.stack(in_shares)
    if order == 1:
        output, grad_inputs = to_absolute(output, dp, core), to_absolute(grad_inputs, dp, core)
    return (
        output,
        grad_inputs,
        grad_w_query,
        grad_w_key,
        grad_w_value,
        grad_w_output,
        grad_w_gate,
        grad_w_up,
        grad_w_down,
        lines[0],
        lines[1],
        small[:hd],
        small[hd : 2 * hd],
        rms_values,
    )


def per_device_square(
    inputs,
    cotangent,
    lengths,
    w_query,
    key_projection_weight,
    value_projection_weight,
    w_output,
    w_gate,
    w_up,
    w_down,
    attn_gain,
    ffn_gain,
    query_gain,
    key_gain,
):
    seqs, span, width = inputs.shape
    hd = query_gain.shape[0]
    nq = w_query.shape[1] // hd
    nk = key_projection_weight.shape[1] // hd
    lengths = lengths.astype(jnp.int32)
    all_gains = (attn_gain, ffn_gain, query_gain, key_gain)
    (
        xr, n1, gf, qkv, out_w, gate, up, down, hidden, n2, rest, came, gi, pre, everything, att, tok, gains, table, inv, stat
    ) = forward(
        lengths, inputs, cotangent, w_query, key_projection_weight, value_projection_weight, w_output, w_gate, w_up, w_down,
        all_gains, hd, nq, nk,
    )
    tokens = seqs * span
    flat = lambda a: a.reshape(tokens, -1)
    ffn, gb, gh, d_gate, d_up, d_down, hidden, landx, landy, ring, gain2_part, stat2 = feed_both(
        lengths, n2, flat(gf), gate, up, down, gi, rest, came, flat(xr), hidden, gains
    )
    (
        output, early, fin, finb, own, sum_gate, sum_up, sum_down, mine_o, mine_q, _, _, _, _, lx3, ly3, lx4, ly4, lines, small
    ) = backward(
        lengths, gb, hidden, ffn, ring, xr, flat(n1), flat(tok), out_w, qkv,
        everything, att, inv, pre, gh, d_gate, landx, landy, d_up, d_down, table, gains, stat, stat2, gain2_part, hd, nq, nk,
    )
    nqc, nkc = nq * hd, nk * hd
    output, grad_inputs, grad_gate, grad_up, grad_down, grad_out, grad_q, grad_k, grad_v, *small = finish_results(
        (sum_gate, sum_up, sum_down), mine_o, mine_q, (lx3, ly3), (lx4, ly4), gh, xr, fin, finb, own, output, early, gains,
        lines, small, hd, nqc, nkc,
    )
    return (output, grad_inputs, grad_q, grad_k, grad_v, grad_out, grad_gate, grad_up, grad_down, *small)


def per_device(*args):
    inputs, w_query = args[0], args[3]
    seqs, span, width = inputs.shape
    square = lax.axis_size("dp") == 4 and lax.axis_size("tensor") == 4 and lax.axis_size("context") == 2
    if square and width % 2048 == 0 and span % 512 == 0 and seqs == 2 and w_query.shape[1] == span:
        return per_device_square(*args)
    return per_device_general(*args)


def solution(mesh):
    both = ("dp", "context")
    rows = P(both, "tensor")
    cols = P("tensor", both)
    shares = P("dp", ("context", "tensor"), None)
    acts = P("dp", "context", None)
    return jax.shard_map(
        per_device,
        mesh=mesh,
        in_specs=(acts, acts, P("dp"), rows, rows, rows, cols, rows, rows, cols, P(both), P(both), P(), P()),
        out_specs=(shares, shares, rows, rows, rows, cols, rows, rows, cols, P(both), P(both), P(), P(), P()),
        check_vma=False,
    )
```

```python
import functools
import math

import jax
import jax.numpy as jnp
from jax import lax
from jax.experimental import pallas as pl
from jax.experimental.pallas import tpu as pltpu
from jax.sharding import PartitionSpec as P

F32 = jnp.float32
BF16 = jnp.bfloat16
epsilon = 1e-05
rope_base = 1000000.0
log2e = 1.4426950408889634
VMEM_BYTES = 60 * 1024 * 1024
VMEM_MOST = 63 * 1024 * 1024
PARAMS = pltpu.CompilerParams(vmem_limit_bytes=VMEM_BYTES)
SMEM = pl.BlockSpec(memory_space=pltpu.SMEM)
SWAP = ((0, 1), (1, 0))


def shape(dims, dtype):
    return jax.ShapeDtypeStruct(tuple(dims), dtype)


def cost(flops, size, exps=0):
    return pl.CostEstimate(flops=int(flops), bytes_accessed=int(size), transcendentals=int(exps))


def dot_nn(a, b):
    return lax.dot_general(a, b, (((1,), (0,)), ((), ())), preferred_element_type=F32)


def dot_nt(a, b):
    return lax.dot_general(a, b, (((1,), (1,)), ((), ())), preferred_element_type=F32)


def dot_tn(a, b):
    return lax.dot_general(a, b, (((0,), (0,)), ((), ())), preferred_element_type=F32)


def inverse_rms(values):
    return lax.rsqrt(jnp.mean(values * values, axis=-1, keepdims=True) + epsilon)


def block_order(dp, core):
    return jnp.stack([jnp.int32(k) * 2 + (core ^ o) for o in range(2) for k in range(dp)]).astype(jnp.int32)


def to_relative(values, dp, core):
    lead = values.shape[:-1]
    parts = values.reshape(lead + (dp, 2, -1))
    parts = jnp.where(core == 0, parts, parts[..., ::-1, :])
    return jnp.swapaxes(parts, -3, -2).reshape(values.shape)


def to_absolute(values, dp, core):
    lead = values.shape[:-1]
    parts = jnp.swapaxes(values.reshape(lead + (2, dp, -1)), -3, -2)
    return jnp.where(core == 0, parts, parts[..., ::-1, :]).reshape(values.shape)


def over_core(value):
    return lax.ppermute(value, "context", SWAP)


def gather_blocks(weight, axis):
    own = lax.all_gather(weight, "dp", axis=axis, tiled=True)
    return jnp.stack([own, over_core(own)])


def scatter_blocks(total, axis):
    return lax.psum_scatter(total, "dp", scatter_dimension=axis, tiled=True).astype(F32)


def ring_scatter(piece, tensor, rank):
    ring = [(i, (i + 1) % tensor) for i in range(tensor)]
    moving = piece((rank + tensor - 1) % tensor)
    for step in range(1, tensor):
        moving = lax.ppermute(moving, "tensor", ring)
        if step < tensor - 1:
            moving = (moving.astype(F32) + piece((rank + tensor - 1 - step) % tensor).astype(F32)).astype(BF16)
    return moving


def begin_kernel(order, x_ref, cot_ref, gain_ref, scal_ref, xr_ref, n1_ref, gf_ref):
    seq, tile = pl.program_id(0), pl.program_id(1)
    rows, width = x_ref.shape[1:]
    seqs = pl.num_programs(0)
    place = scal_ref[seqs] + tile * rows + lax.broadcasted_iota(jnp.int32, (rows, 1), 0)
    valid = (place < scal_ref[seq]).astype(F32)
    x = x_ref[0].astype(F32)
    inv = inverse_rms(x)
    piece = width // order
    for k in range(order):
        src = pl.ds(pl.multiple_of(scal_ref[seqs + 1 + k] * piece, piece), piece) if order > 1 else slice(0, width)
        dst = slice(k * piece, (k + 1) * piece)
        part = x_ref[0, :, src]
        xr_ref[0, :, dst] = part
        n1_ref[0, :, dst] = (part.astype(F32) * inv * gain_ref[:, dst]).astype(BF16)
        gf_ref[0, :, dst] = (cot_ref[0, :, src].astype(F32) * valid).astype(BF16)


def begin(x, cot, gain, scalars, order):
    seqs, span, width = x.shape
    rows = min(256, span)
    spec = pl.BlockSpec((1, rows, width), lambda s, i: (s, i, 0))
    return pl.pallas_call(
        functools.partial(begin_kernel, order),
        grid=(seqs, span // rows),
        in_specs=[spec, spec, pl.BlockSpec((1, width), lambda s, i: (0, 0)), SMEM],
        out_specs=[spec] * 3,
        out_shape=[shape(x.shape, BF16)] * 3,
        compiler_params=PARAMS,
        cost_estimate=cost(8 * x.size, 10 * x.size),
        name="first_norm",
    )(x, cot, gain, scalars)


def heads_kernel(hd, nq, nk, n1_ref, w_ref, cos_ref, sin_ref, qg_ref, kg_ref, core_ref, pre_ref, own_ref, oth_ref):
    half = w_ref.shape[1]
    x = n1_ref[0]
    flat = dot_nn(x[:, :half], w_ref[0]) + dot_nn(x[:, half:], w_ref[1])
    turned = flat.T
    span = turned.shape[1]
    normed = turned[: (nq + nk) * hd]
    pre_ref[...] = normed
    core = core_ref[0]
    cosine, sine = cos_ref[...], sin_ref[...]
    done = []
    for h in range(nq + nk):
        v = normed[h * hd : (h + 1) * hd]
        inv = lax.rsqrt(jnp.mean(v * v, axis=0, keepdims=True) + epsilon)
        v = v * inv * (qg_ref[...] if h < nq else kg_ref[...])
        a, b = v[: hd // 2], v[hd // 2 :]
        done.append(jnp.concatenate([a * cosine - b * sine, b * cosine + a * sine], axis=0))
    for h in range(nk):
        lo = (nq + nk + h) * hd
        done.append(turned[lo : lo + hd])
    parts = [[], []]
    for start, count in ((0, nq), (nq, nk), (nq + nk, nk)):
        for side in range(2):
            parts[side] += done[start + side * count // 2 : start + (side + 1) * count // 2]
    low = jnp.concatenate(parts[0], axis=0)
    high = jnp.concatenate(parts[1], axis=0)
    first = core == 0
    own_ref[...] = jnp.where(first, low, high).astype(BF16)
    oth_ref[...] = jnp.where(first, high, low).astype(BF16)


def heads(n1, seq, weight, cosine, sine, qgain, kgain, core, hd, nq, nk):
    span, width = n1.shape[1:]
    sides = (nq + 2 * nk) * hd // 2
    full = pl.BlockSpec(memory_space=pltpu.VMEM)
    whole = lambda a: pl.BlockSpec(a.shape, lambda i: (0,) * a.ndim)
    outs = [shape(((nq + nk) * hd, span), F32), shape((sides, span), BF16), shape((sides, span), BF16)]
    return pl.pallas_call(
        functools.partial(heads_kernel, hd, nq, nk),
        grid=(1,),
        in_specs=[pl.BlockSpec((1, span, width), lambda i: (seq, 0, 0))]
        + [whole(a) for a in (weight, cosine, sine, qgain, kgain)]
        + [SMEM],
        out_specs=[whole(o) for o in outs],
        out_shape=outs,
        compiler_params=PARAMS,
        cost_estimate=cost(2 * span * width * weight.shape[2], 2 * span * width + 2 * weight.size),
        name="query_key_value",
    )(n1, weight, cosine, sine, qgain, kgain, core)


def join_positions(core, own, oth):
    first = core == 0
    return jnp.where(first, own, oth), jnp.where(first, oth, own)


def attend_kernel(block, groups, scal_ref, own_ref, got_ref, all_ref, att_ref, inv_ref, ao_ref, ax_ref):
    span = own_ref.shape[1]
    hd = own_ref.shape[0] // (groups + 2)
    length, core = scal_ref[0], scal_ref[1]
    low, high = join_positions(core, own_ref[...], got_ref[...])
    all_ref[:, :span] = low
    all_ref[:, span:] = high
    scale = log2e / math.sqrt(hd)
    krow = lax.broadcasted_iota(jnp.int32, (block, groups * block), 0)
    qcol = lax.broadcasted_iota(jnp.int32, (block, groups * block), 1) % block
    base = groups * hd
    for i in range(2 * span // block):
        cut = slice(i * block, (i + 1) * block)
        q = jnp.concatenate([all_ref[g * hd : (g + 1) * hd, cut] for g in range(groups)], axis=1)
        acc = jnp.zeros((hd, groups * block), F32)
        total = jnp.zeros((1, groups * block), F32)
        for j in range(i + 1):
            kcut = slice(j * block, (j + 1) * block)
            s = dot_tn(all_ref[base : base + hd, kcut], q) * scale
            ok = (krow + j * block) < length
            if j == i:
                ok = ok & (krow <= qcol)
            e = jnp.where(ok, jnp.exp2(s), 0.0)
            total = total + jnp.sum(e, axis=0, keepdims=True)
            acc = acc + dot_nn(all_ref[base + hd : base + 2 * hd, kcut], e.astype(BF16))
        inv = 1.0 / total
        att = (acc * inv).astype(BF16)
        for g in range(groups):
            att_ref[g * hd : (g + 1) * hd, cut] = att[:, g * block : (g + 1) * block]
            inv_ref[g : g + 1, cut] = inv[:, g * block : (g + 1) * block]
    mine, theirs = join_positions(core, att_ref[:, :span], att_ref[:, span:])
    ao_ref[...] = mine
    ax_ref[...] = theirs


def attend(scalars, own, got, groups):
    rows, span = own.shape
    hd = rows // (groups + 2)
    block = min(256, span)
    full = pl.BlockSpec(memory_space=pltpu.VMEM)
    return pl.pallas_call(
        functools.partial(attend_kernel, block, groups),
        in_specs=[SMEM, full, full],
        out_specs=[full] * 5,
        out_shape=[
            shape((rows, 2 * span), BF16),
            shape((groups * hd, 2 * span), BF16),
            shape((groups, 2 * span), F32),
            shape((groups * hd, span), BF16),
            shape((groups * hd, span), BF16),
        ],
        compiler_params=PARAMS,
        cost_estimate=cost(60 * groups * hd * span * span, 12 * rows * span, 4 * groups * span * span),
        name="attend_forward",
    )(scalars, own, got)


def branch_kernel(own_ref, got_ref, w_ref, core_ref, att_ref, *outs):
    half = w_ref.shape[2]
    low, high = join_positions(core_ref[0], own_ref[...], got_ref[...])
    att = jnp.concatenate([low, high], axis=0)
    att_ref[...] = att
    rows = outs[0].shape[0]
    for k, out in enumerate(outs):
        part = att[:, k * rows : (k + 1) * rows]
        out[:, :half] = dot_tn(part, w_ref[0]).astype(BF16)
        out[:, half:] = dot_tn(part, w_ref[1]).astype(BF16)


def branch(own, got, weight, core, chunks):
    rows, span = own.shape
    width = 2 * weight.shape[2]
    full = pl.BlockSpec(memory_space=pltpu.VMEM)
    return pl.pallas_call(
        branch_kernel,
        in_specs=[full] * 3 + [SMEM],
        out_specs=[full] * (1 + chunks),
        out_shape=[shape((2 * rows, span), BF16)] + [shape((span // chunks, width), BF16)] * chunks,
        compiler_params=PARAMS,
        cost_estimate=cost(4 * rows * span * width, 4 * rows * width + 2 * span * width),
        name="attention_branch",
    )(own, got, weight, core)


def second_norm_kernel(terms, scal_ref, x_ref, gain_ref, *refs):
    term_refs, (hidden_ref, n2_ref, stat_ref) = refs[:terms], refs[terms:]
    rows = hidden_ref.shape[0]
    branch_sum = term_refs[0][...].astype(F32)
    for ref in term_refs[1:]:
        branch_sum = branch_sum + ref[...].astype(F32)
    resid = x_ref[0].astype(F32)
    hidden = resid + branch_sum
    hidden_ref[...] = hidden
    n2_ref[...] = (hidden * inverse_rms(hidden) * gain_ref[...]).astype(BF16)
    place = scal_ref[1] + lax.broadcasted_iota(jnp.int32, (rows, 1), 0)
    valid = (place < scal_ref[0]).astype(F32)
    first = jnp.sum(valid * resid * resid, keepdims=True)
    second = jnp.sum(valid * branch_sum * branch_sum, keepdims=True)
    line = lax.broadcasted_iota(jnp.int32, (8, 128), 0)
    stat_ref[...] = jnp.where(line == 0, first, second)


def second_norm(scalars, xr, seq, part, gain, terms):
    rows, width = terms[0].shape
    flat = pl.BlockSpec((rows, width), lambda i: (0, 0))
    return pl.pallas_call(
        functools.partial(second_norm_kernel, len(terms)),
        grid=(1,),
        in_specs=[SMEM, pl.BlockSpec((1, rows, width), lambda i: (seq, part, 0)), pl.BlockSpec((1, width), lambda i: (0, 0))]
        + [flat] * len(terms),
        out_specs=[flat, flat, pl.BlockSpec((8, 128), lambda i: (0, 0))],
        out_shape=[shape((rows, width), F32), shape((rows, width), BF16), shape((8, 128), F32)],
        compiler_params=PARAMS,
        cost_estimate=cost(20 * rows * width, (8 + 2 * len(terms)) * rows * width),
        name="second_norm",
    )(scalars, xr, gain, *terms)


def feed_kernel(n_ref, g_ref, wgo, wgx, wuo, wux, wdo, wdx, inner_ref, gg_ref, gu_ref, ffn_ref, gn_ref, facc, gacc):
    step = pl.program_id(0)
    half = wgo.shape[0]
    no, nx = n_ref[:, :half], n_ref[:, half:]
    gate = dot_nn(no, wgo[...]) + dot_nn(nx, wgx[...])
    up = dot_nn(no, wuo[...]) + dot_nn(nx, wux[...])
    gi = dot_nt(g_ref[0, :, :half], wdo[...]) + dot_nt(g_ref[0, :, half:], wdx[...])
    sig = jax.nn.sigmoid(gate)
    silu = gate * sig
    inner = (silu * up).astype(BF16)
    gg = (gi * up * sig * (1.0 + gate * (1.0 - sig))).astype(BF16)
    gu = (gi * silu).astype(BF16)
    inner_ref[...] = inner
    gg_ref[...] = gg
    gu_ref[...] = gu

    @pl.when(step == 0)
    def _():
        facc[...] = jnp.zeros_like(facc)
        gacc[...] = jnp.zeros_like(gacc)

    facc[:, :half] += dot_nn(inner, wdo[...])
    facc[:, half:] += dot_nn(inner, wdx[...])
    gacc[:, :half] += dot_nt(gg, wgo[...]) + dot_nt(gu, wuo[...])
    gacc[:, half:] += dot_nt(gg, wgx[...]) + dot_nt(gu, wux[...])

    @pl.when(step == pl.num_programs(0) - 1)
    def _():
        ffn_ref[...] = facc[...].astype(BF16)
        gn_ref[...] = gacc[...].astype(BF16)


def feed(n2, chunk, rows, gf, seq, part, gate, up, down):
    width = n2.shape[1]
    _, half, hidden = gate.shape
    hb = min(512, hidden)
    row = [pl.BlockSpec((None, half, hb), lambda h, side=side: (side, 0, h)) for side in range(2)]
    col = [pl.BlockSpec((None, hb, half), lambda h, side=side: (side, h, 0)) for side in range(2)]
    whole = pl.BlockSpec((rows, width), lambda h: (0, 0))
    tile = pl.BlockSpec((rows, hb), lambda h: (0, h))
    return pl.pallas_call(
        feed_kernel,
        grid=(hidden // hb,),
        in_specs=[pl.BlockSpec((rows, width), lambda h: (chunk, 0)), pl.BlockSpec((1, rows, width), lambda h: (seq, part, 0))] + row + row + col,
        out_specs=[tile, tile, tile, whole, whole],
        out_shape=[shape((rows, hidden), BF16)] * 3 + [shape((rows, width), BF16)] * 2,
        scratch_shapes=[pltpu.VMEM((rows, width), F32), pltpu.VMEM((rows, width), F32)],
        compiler_params=PARAMS,
        cost_estimate=cost(12 * rows * width * hidden, 12 * half * hidden + 14 * rows * width, rows * hidden),
        name="feed_forward",
    )(n2, gf, gate, gate, up, up, down, down)


def second_back_kernel(terms, hidden_ref, gf_ref, gain_ref, *refs):
    term_refs, (gb_ref, gh_ref, gain_out) = refs[:terms], refs[terms:]
    e = term_refs[0][...].astype(F32)
    for ref in term_refs[1:]:
        e = e + ref[...].astype(F32)
    hidden = hidden_ref[...]
    inv = inverse_rms(hidden)
    hat = hidden * inv
    eg = e * gain_ref[...]
    gh = gf_ref[0].astype(F32) + inv * (eg - hat * jnp.mean(eg * hat, axis=-1, keepdims=True))
    gh_ref[...] = gh
    gb_ref[...] = gh.astype(BF16)
    gain_out[...] = jnp.sum(e * hat, axis=0, keepdims=True)


def second_back(hidden, chunk, gf, seq, part, gain, terms):
    rows, width = terms[0].shape
    flat = pl.BlockSpec((rows, width), lambda i: (0, 0))
    line = pl.BlockSpec((1, width), lambda i: (0, 0))
    return pl.pallas_call(
        functools.partial(second_back_kernel, len(terms)),
        grid=(1,),
        in_specs=[pl.BlockSpec((rows, width), lambda i: (chunk, 0)), pl.BlockSpec((1, rows, width), lambda i: (seq, part, 0)), line]
        + [flat] * len(terms),
        out_specs=[flat, flat, line],
        out_shape=[shape((rows, width), BF16), shape((rows, width), F32), shape((1, width), F32)],
        compiler_params=PARAMS,
        cost_estimate=cost(20 * rows * width, (12 + 2 * len(terms)) * rows * width),
        name="second_norm_back",
    )(hidden, gf, gain, *terms)


def branch_back_kernel(chunks, *refs):
    gb_refs, (w_ref, core_ref, own_ref, oth_ref) = refs[:chunks], refs[chunks:]
    half = w_ref.shape[2]
    rows = gb_refs[0].shape[0]
    heads_half = own_ref.shape[0]
    first = core_ref[0] == 0
    for k, ref in enumerate(gb_refs):
        da = dot_nt(w_ref[0], ref[:, :half]) + dot_nt(w_ref[1], ref[:, half:])
        da = da.astype(BF16)
        low, high = da[:heads_half], da[heads_half:]
        cut = slice(k * rows, (k + 1) * rows)
        own_ref[:, cut] = jnp.where(first, low, high)
        oth_ref[:, cut] = jnp.where(first, high, low)


def branch_back(gbs, weight, core):
    chunks = len(gbs)
    rows, width = gbs[0].shape
    dim = weight.shape[1]
    full = pl.BlockSpec(memory_space=pltpu.VMEM)
    return pl.pallas_call(
        functools.partial(branch_back_kernel, chunks),
        in_specs=[full] * (chunks + 1) + [SMEM],
        out_specs=[full] * 2,
        out_shape=[shape((dim // 2, chunks * rows), BF16)] * 2,
        compiler_params=PARAMS,
        cost_estimate=cost(2 * dim * chunks * rows * width, 2 * dim * width + 2 * chunks * rows * width),
        name="attention_branch_back",
    )(*gbs, weight, core)


def attend_back_kernel(block, groups, scal_ref, all_ref, att_ref, inv_ref, own_ref, got_ref, out_own, out_oth, da_all, grads):
    span = own_ref.shape[1]
    hd = all_ref.shape[0] // (groups + 2)
    length, core = scal_ref[0], scal_ref[1]
    low, high = join_positions(core, own_ref[...], got_ref[...])
    da_all[:, :span] = low
    da_all[:, span:] = high
    scale = log2e / math.sqrt(hd)
    back = 1.0 / math.sqrt(hd)
    krow = lax.broadcasted_iota(jnp.int32, (block, groups * block), 0)
    qcol = lax.broadcasted_iota(jnp.int32, (block, groups * block), 1) % block
    base = groups * hd
    grads[base:, :] = jnp.zeros((2 * hd, 2 * span), F32)
    for i in range(2 * span // block):
        cut = slice(i * block, (i + 1) * block)

        def rows(ref):
            return jnp.concatenate([ref[g * hd : (g + 1) * hd, cut] for g in range(groups)], axis=1)

        q = rows(all_ref)
        da = rows(da_all)
        inv = jnp.concatenate([inv_ref[g : g + 1, cut] for g in range(groups)], axis=1)
        delta = jnp.sum(rows(att_ref).astype(F32) * da.astype(F32), axis=0, keepdims=True)
        dq = jnp.zeros((hd, groups * block), F32)
        for j in range(i + 1):
            kcut = slice(j * block, (j + 1) * block)
            key = all_ref[base : base + hd, kcut]
            s = dot_tn(key, q) * scale
            ok = (krow + j * block) < length
            if j == i:
                ok = ok & (krow <= qcol)
            p = jnp.where(ok, jnp.exp2(s) * inv, 0.0)
            dp = dot_tn(all_ref[base + hd : base + 2 * hd, kcut], da)
            ds = (p * (dp - delta)).astype(BF16)
            dq = dq + dot_nn(key, ds)
            grads[base : base + hd, kcut] += dot_nt(q, ds) * back
            grads[base + hd : base + 2 * hd, kcut] += dot_nt(da, p.astype(BF16))
        dq = dq * back
        for g in range(groups):
            grads[g * hd : (g + 1) * hd, cut] = dq[:, g * block : (g + 1) * block]
    mine, theirs = join_positions(core, grads[:, :span], grads[:, span:])
    out_own[...] = mine.astype(BF16)
    out_oth[...] = theirs.astype(BF16)


def attend_back(scalars, everything, att, inv, own, got, groups):
    rows, slots = everything.shape
    span = slots // 2
    block = min(256, span)
    full = pl.BlockSpec(memory_space=pltpu.VMEM)
    return pl.pallas_call(
        functools.partial(attend_back_kernel, block, groups),
        in_specs=[SMEM] + [full] * 5,
        out_specs=[full] * 2,
        out_shape=[shape((rows, span), BF16)] * 2,
        scratch_shapes=[pltpu.VMEM(att.shape, BF16), pltpu.VMEM((rows, slots), F32)],
        compiler_params=PARAMS,
        cost_estimate=cost(30 * att.shape[0] * slots * slots, 12 * rows * slots, groups * slots * slots),
        name="attend_backward",
    )(scalars, everything, att, inv, own, got)


def heads_back_kernel(hd, nq, nk, own_ref, got_ref, pre_ref, cos_ref, sin_ref, qg_ref, kg_ref, x_ref, w_ref, core_ref, dpre_ref, first_ref, gain_ref, hgain_ref):
    half = w_ref.shape[1]
    low, high = join_positions(core_ref[0], own_ref[...].astype(F32), got_ref[...].astype(F32))
    sides = (nq // 2, nk // 2, nk // 2)
    grads = [[], [], []]
    for side in (low, high):
        at = 0
        for kind, count in enumerate(sides):
            for h in range(count):
                grads[kind].append(side[at : at + hd])
                at += hd
    cosine, sine = cos_ref[...], sin_ref[...]
    done = []
    sums = [0.0, 0.0]
    for h in range(nq + nk):
        kind = 0 if h < nq else 1
        g = grads[kind][h - kind * nq]
        a, b = g[: hd // 2], g[hd // 2 :]
        g = jnp.concatenate([a * cosine + b * sine, b * cosine - a * sine], axis=0)
        v = pre_ref[h * hd : (h + 1) * hd, :]
        inv = lax.rsqrt(jnp.mean(v * v, axis=0, keepdims=True) + epsilon)
        hat = v * inv
        sums[kind] = sums[kind] + jnp.sum(g * hat, axis=1, keepdims=True)
        gg = g * (qg_ref[...] if kind == 0 else kg_ref[...])
        done.append(inv * (gg - hat * jnp.mean(gg * hat, axis=0, keepdims=True)))
    done += grads[2]
    hgain_ref[:hd, :] = jnp.broadcast_to(sums[0], (hd, 128))
    hgain_ref[hd:, :] = jnp.broadcast_to(sums[1], (hd, 128))
    dpre = jnp.concatenate(done, axis=0).T.astype(BF16)
    dpre_ref[...] = dpre
    x = x_ref[0].astype(F32)
    hat = x * inverse_rms(x)
    for k in range(2):
        cut = slice(k * half, (k + 1) * half)
        part = dot_nt(dpre, w_ref[k])
        first_ref[:, cut] = part.astype(BF16)
        gain_ref[:, cut] = jnp.sum(part * hat[:, cut], axis=0, keepdims=True)


def heads_back(own, got, pre, cosine, sine, qgain, kgain, xr, seq, weight, core, hd, nq, nk):
    span = own.shape[1]
    _, half, cols = weight.shape
    width = 2 * half
    whole = lambda a: pl.BlockSpec(a.shape, lambda i: (0,) * len(a.shape))
    outs = [shape((span, cols), BF16), shape((span, width), BF16), shape((1, width), F32), shape((2 * hd, 128), F32)]
    return pl.pallas_call(
        functools.partial(heads_back_kernel, hd, nq, nk),
        grid=(1,),
        in_specs=[whole(a) for a in (own, got, pre, cosine, sine, qgain, kgain)]
        + [pl.BlockSpec((1, span, width), lambda i: (seq, 0, 0)), whole(weight), SMEM],
        out_specs=[whole(o) for o in outs],
        out_shape=outs,
        compiler_params=PARAMS,
        cost_estimate=cost(2 * span * width * cols, 4 * span * width + 4 * half * cols),
        name="query_key_value_back",
    )(own, got, pre, cosine, sine, qgain, kgain, xr, weight, core)


def place_blocks(order, ids, first_id, value, out_ref):
    piece = value.shape[-1] // order
    for k in range(order):
        if order == 1:
            out_ref[...] = value
        else:
            dst = pl.ds(pl.multiple_of(ids[first_id + k] * piece, piece), piece)
            out_ref[:, dst] = value[:, k * piece : (k + 1) * piece]


def output_kernel(order, scal_ref, got_ref, f0_ref, f1_ref, h0_ref, h1_ref, out_ref, stat_ref):
    low = scal_ref[0] * 2 < scal_ref[3]
    rows = out_ref.shape[0]
    ffn = got_ref[...].astype(F32) + jnp.where(low, f0_ref[...], f1_ref[...]).astype(F32)
    hidden = jnp.where(low, h0_ref[...], h1_ref[...])
    place = scal_ref[2] + lax.broadcasted_iota(jnp.int32, (rows, 1), 0)
    valid = (place < scal_ref[1]).astype(F32)
    stat_ref[...] = jnp.broadcast_to(jnp.sum(valid * ffn * ffn, keepdims=True), (8, 128))
    place_blocks(order, scal_ref, 4, (hidden + ffn).astype(BF16), out_ref)


def share_specs(rows, width, per):
    return [
        pl.BlockSpec((rows, width), lambda i, s: (jnp.minimum(s[0], per - 1), 0)),
        pl.BlockSpec((rows, width), lambda i, s: (jnp.maximum(s[0] - per, 0), 0)),
    ]


def output_share(scalars, got, ffns, hiddens, order):
    rows, width = got.shape
    pair = share_specs(rows, width, ffns[0].shape[0] // rows)
    flat = pl.BlockSpec((rows, width), lambda i, s: (0, 0))
    return pl.pallas_call(
        functools.partial(output_kernel, order),
        grid_spec=pltpu.PrefetchScalarGridSpec(
            num_scalar_prefetch=1,
            grid=(1,),
            in_specs=[flat] + pair + pair,
            out_specs=[flat, pl.BlockSpec((8, 128), lambda i, s: (0, 0))],
        ),
        out_shape=[shape((rows, width), BF16), shape((8, 128), F32)],
        compiler_params=PARAMS,
        cost_estimate=cost(6 * rows * width, 16 * rows * width),
        name="output_share",
    )(scalars, got, *ffns, *hiddens)


def input_kernel(order, scal_ref, got_ref, part_ref, g0_ref, g1_ref, x_ref, gain_ref, out_ref):
    low = scal_ref[0] * 2 < scal_ref[3]
    e = got_ref[...].astype(F32) + part_ref[...].astype(F32)
    gh = jnp.where(low, g0_ref[...], g1_ref[...])
    x = x_ref[0].astype(F32)
    inv = inverse_rms(x)
    hat = x * inv
    eg = e * gain_ref[...]
    value = gh + inv * (eg - hat * jnp.mean(eg * hat, axis=-1, keepdims=True))
    place_blocks(order, scal_ref, 4, value, out_ref)


def input_share(scalars, got, part, ghs, xr, seq, gain, order):
    rows, width = got.shape
    pair = share_specs(rows, width, ghs[0].shape[0] // rows)
    flat = pl.BlockSpec((rows, width), lambda i, s: (0, 0))
    return pl.pallas_call(
        functools.partial(input_kernel, order),
        grid_spec=pltpu.PrefetchScalarGridSpec(
            num_scalar_prefetch=1,
            grid=(1,),
            in_specs=[flat, pl.BlockSpec((rows, width), lambda i, s: (s[0], 0))]
            + pair
            + [pl.BlockSpec((1, rows, width), lambda i, s: (seq, s[0], 0)), pl.BlockSpec((1, width), lambda i, s: (0, 0))],
            out_specs=flat,
        ),
        out_shape=shape((rows, width), F32),
        compiler_params=PARAMS,
        cost_estimate=cost(12 * rows * width, 20 * rows * width),
        name="input_share",
    )(scalars, got, part, *ghs, xr, gain)


def weight_grad_kernel(count, extra, *refs):
    a_refs, b_refs, out = refs[:count], refs[count : 2 * count], refs[-1]
    total = dot_tn(a_refs[0][...], b_refs[0][...])
    for a, b in zip(a_refs[1:], b_refs[1:]):
        total = total + dot_tn(a[...], b[...])
    if extra:
        total = total + refs[2 * count][...].astype(F32)
    out[...] = total.astype(BF16)


def weight_grad(lefts, rights, side, axis, add=None):
    count = len(lefts)
    rows_all, cols_all = lefts[0].shape[1], rights[0].shape[1]
    dims = [rows_all, cols_all]
    dims[axis] //= 2
    rows, cols = min(512, dims[0]), min(2048, dims[1])
    row_at = side * (dims[0] // rows) if axis == 0 else 0
    col_at = side * (dims[1] // cols) if axis == 1 else 0
    specs = [pl.BlockSpec((a.shape[0], rows), lambda j, i: (0, i + row_at)) for a in lefts]
    specs += [pl.BlockSpec((b.shape[0], cols), lambda j, i: (0, j + col_at)) for b in rights]
    tile = pl.BlockSpec((rows, cols), lambda j, i: (i, j))
    tokens = sum(a.shape[0] for a in lefts)
    return pl.pallas_call(
        functools.partial(weight_grad_kernel, count, add is not None),
        grid=(dims[1] // cols, dims[0] // rows),
        in_specs=specs + ([tile] if add is not None else []),
        out_specs=tile,
        out_shape=shape(dims, BF16),
        compiler_params=PARAMS,
        cost_estimate=cost(2 * tokens * dims[0] * dims[1], 2 * tokens * sum(dims) + 2 * dims[0] * dims[1]),
        name="weight_grad",
    )(*lefts, *rights, *([add] if add is not None else []))


def xor_one(index):
    return index + 1 - 2 * (index % 2)


def remote(src, dst, send, recv, device):
    return pltpu.make_async_remote_copy(
        src_ref=src, dst_ref=dst, send_sem=send, recv_sem=recv, device_id=device, device_id_type=pl.DeviceIdType.MESH
    )


def greet(others):
    barrier = pltpu.get_barrier_semaphore()
    count = 0
    for needed, device in others:
        if needed is None:
            pl.semaphore_signal(barrier, inc=1, device_id=device, device_id_type=pl.DeviceIdType.MESH)
            count = count + 1
        else:

            @pl.when(needed)
            def _():
                pl.semaphore_signal(barrier, inc=1, device_id=device, device_id_type=pl.DeviceIdType.MESH)

            count = count + jnp.where(needed, 1, 0)
    pl.semaphore_wait(barrier, count)


class Gather:
    def __init__(self, shard, dst, axis, send, recv, local, near_x, near_y, near_core):
        piece = shard.shape[axis]
        half = shard.shape[0] // 2

        def block(side, k):
            cut = pl.ds(k * piece, piece)
            return dst.at[side, cut, :] if axis == 0 else dst.at[side, :, cut]

        def part(k, h):
            if axis == 0:
                return dst.at[0, pl.ds(k * piece + h * half, half), :]
            return dst.at[0, pl.ds(h * half, half), pl.ds(k * piece, piece)]

        link, cross = send.at[0], send.at[1]
        self.local = pltpu.make_async_copy(shard, block(0, 0), local)
        self.x = remote(shard, block(0, 1), link, recv.at[0], near_x)
        self.y = remote(shard, block(0, 2), link, recv.at[1], near_y)
        self.dx = remote(part(2, 0), part(3, 0), link, recv.at[2], near_x)
        self.dy = remote(part(1, 1), part(3, 1), link, recv.at[2], near_y)
        self.cores = [remote(shard if k == 0 else block(0, k), block(1, k), cross, recv.at[3], near_core) for k in range(4)]
        cut = pl.ds(0, 3 * piece)
        three = dst.at[0, cut, :] if axis == 0 else dst.at[0, :, cut]
        self.all_links = remote(three, three, link, recv.at[0], near_x)
        self.diagonal = remote(block(0, 3), block(0, 3), link, recv.at[2], near_x)
        self.all_cores = remote(dst.at[0], dst.at[1], cross, recv.at[3], near_core)

    def first(self):
        self.x.start()
        self.y.start()
        self.cores[0].start()
        self.local.start()

    def second(self):
        self.y.wait_recv()
        self.dx.start()
        self.cores[2].start()
        self.x.wait_recv()
        self.dy.start()
        self.cores[1].start()

    def third(self):
        self.diagonal.wait_recv()
        self.cores[3].start()

    def arrived(self):
        self.local.wait()
        self.all_cores.wait_recv()

    def sent(self):
        self.all_links.wait_send()
        self.all_cores.wait_send()


def forward_kernel(
    hd, nq, nk, block, sub,
    len_ref, x_hbm, cot_hbm, wq_hbm, wk_hbm, wv_hbm, wout, wgate, wup, wdown, again_ref, fgain_ref, qgain_ref, kgain_ref,
    xr_hbm, n1_hbm, gf_hbm, qkv_hbm, out_hbm, gate_hbm, up_hbm, down_hbm, hidden_hbm, n2_hbm, rest_hbm, resta_hbm, gi_hbm, pre_hbm, all_hbm, att_hbm, tok_hbm,
    gains_ref, table_ref, inv_ref, stat_ref,
    xr_v, cot_v, n1_v, qkv_v, out_v, ex_own, ex_send, ex_got, at_own, at_send, at_got,
    part_v, in_v, back_v, hid_v, norm_v, wqkv, gain_ref, down_v, gi_v, pre_ref, all_ref, att_ref, tok_ref,
    keep_sem, load_sem, store_sem, shard_sem, rest_sem, down_sem, gi_sem, wsend, wrecv, wloc, gsend, grecv, exsend, exrecv, zsend, zrecv, hid_sem,
):
    seqs, span, width = xr_v.shape
    groups = nq // nk
    row, core, rank = lax.axis_index("dp"), lax.axis_index("context"), lax.axis_index("tensor")
    start = core * span
    near = [row, xor_one(row), (row + 2) % 4, 3 - row]
    inner = (rank % 3) != 0
    near_x, near_y, near_core = {"dp": near[1]}, {"dp": near[2]}, {"context": 1 - core}
    z_side, z_mid = {"tensor": xor_one(rank)}, {"tensor": 3 - rank}
    piece = width // 8
    total_subs = part_v.shape[0]
    per = span // sub
    first_core = core == 0

    loads = []
    for at, (src, dst) in enumerate(((x_hbm, xr_v), (cot_hbm, cot_v))):
        for s in range(seqs):
            for o in range(2):
                for k in range(4):
                    b = near[k] * 2 + (core if o == 0 else 1 - core)
                    cut = pl.ds(pl.multiple_of(b * piece, piece), piece)
                    loads.append(
                        pltpu.make_async_copy(
                            src.at[s, :, cut], dst.at[s, :, pl.ds((o * 4 + k) * piece, piece)], load_sem.at[at]
                        )
                    )
    shards, at = [], 0
    for k, ref in enumerate((wq_hbm, wk_hbm, wv_hbm)):
        shards.append(pltpu.make_async_copy(ref, wqkv.at[:, pl.ds(at, ref.shape[1])], shard_sem.at[k]))
        at += ref.shape[1]
    for copy in shards + loads:
        copy.start()
    piece = width // 8
    wide_gains = [ref[...].astype(F32).reshape(1, piece) for ref in (again_ref, fgain_ref)]
    gain_ref[...] = jnp.concatenate(wide_gains + [jnp.zeros((14, piece), F32)], axis=0).astype(BF16)

    others = []
    for o in range(2):
        for k in range(4):
            if o or k:
                others.append((o * 4 + k, {"dp": near[k], "context": core if o == 0 else 1 - core}))
    greet([(None, d) for _, d in others] + [(None, z_side), (inner, z_mid)])

    gains = [remote(gain_ref, gains_ref.at[b], gsend, grecv, d) for b, d in others]
    every_gain = remote(gains_ref.at[pl.ds(1, 7)], gains_ref.at[pl.ds(1, 7)], gsend, grecv, near_core)
    for copy in gains:
        copy.start()
    weights = [
        Gather(shard, dst, axis, wsend.at[i], wrecv.at[i], wloc.at[i], near_x, near_y, near_core)
        for i, (shard, dst, axis) in enumerate(
            ((wqkv, qkv_v, 0), (wout, out_v, 1), (wgate, gate_hbm, 0), (wup, up_hbm, 0), (wdown, down_hbm, 1))
        )
    ]
    w_qkv, w_out, w_gate, w_up, w_down = weights
    for copy in shards:
        copy.wait()
    w_qkv.first()
    w_out.first()
    gains_ref[0] = gain_ref[...]

    quarter = hd // 2
    freqs = jnp.exp(lax.broadcasted_iota(jnp.int32, (quarter, span), 0).astype(F32) * (-2.0 * math.log(rope_base) / hd))
    angles = freqs * (start + lax.broadcasted_iota(jnp.int32, (quarter, span), 1)).astype(F32)
    cosine, sine = jnp.cos(angles), jnp.sin(angles)
    turned = [jnp.broadcast_to(ref[...].astype(F32).reshape(1, hd), (8, hd)).T for ref in (qgain_ref, kgain_ref)]
    qgain, kgain = turned[0][:, 0:1], turned[1][:, 0:1]
    table_ref[:quarter, :] = cosine
    table_ref[quarter : 2 * quarter, :] = sine
    table_ref[2 * quarter : 2 * quarter + hd, :128] = jnp.broadcast_to(qgain, (hd, 128))
    table_ref[2 * quarter + hd :, :128] = jnp.broadcast_to(kgain, (hd, 128))

    pltpu.make_async_copy(cot_hbm, cot_v, load_sem.at[1]).wait()

    def mask_rows(i, carry):
        s, t = i // (span // 16), i % (span // 16)
        cut = pl.ds(pl.multiple_of(t * 16, 16), 16)
        place = start + t * 16 + lax.broadcasted_iota(jnp.int32, (16, 1), 0)
        valid = (place < len_ref[s]).astype(F32)
        cot_v[s, cut, :] = (cot_v[s, cut, :].astype(F32) * valid).astype(BF16)
        return carry

    lax.fori_loop(0, seqs * span // 16, mask_rows, 0)
    store_gf = pltpu.make_async_copy(cot_v, gf_hbm, store_sem.at[0])
    store_gf.start()
    pltpu.make_async_copy(x_hbm, xr_v, load_sem.at[0]).wait()
    store_xr = pltpu.make_async_copy(xr_v, xr_hbm, store_sem.at[1])
    store_xr.start()
    every_gain.wait_recv()
    gain1 = jnp.concatenate([gains_ref[b, 0:1, :] for b in range(8)], axis=1).astype(F32)
    gain2 = jnp.concatenate([gains_ref[b, 1:2, :] for b in range(8)], axis=1).astype(F32)

    def norm_rows(i, carry):
        s, t = i // (span // 16), i % (span // 16)
        cut = pl.ds(pl.multiple_of(t * 16, 16), 16)
        x = xr_v[s, cut, :].astype(F32)
        n1_v[s, cut, :] = (x * inverse_rms(x) * gain1).astype(BF16)
        return carry

    lax.fori_loop(0, span // 16, norm_rows, 0)
    w_qkv.second()
    lax.fori_loop(span // 16, seqs * span // 16, norm_rows, 0)
    store_n1 = pltpu.make_async_copy(n1_v, n1_hbm, store_sem.at[2])
    store_n1.start()
    w_out.second()
    w_down.first()
    w_gate.first()
    w_qkv.third()
    w_qkv.arrived()

    half = width // 2

    def exchange(s):
        return remote(ex_send.at[s], ex_got.at[s], exsend.at[0, s], exrecv.at[0, s], near_core)

    def keep(k, s):
        ref, dst = ((pre_ref, pre_hbm), (all_ref, all_hbm), (att_ref, att_hbm), (tok_ref, tok_hbm))[k]
        return pltpu.make_async_copy(ref.at[s], dst.at[s], keep_sem.at[k, s])

    def project(s):
        x = n1_v[s]
        flat = dot_nn(x[:, :half], qkv_v[0]) + dot_nn(x[:, half:], qkv_v[1])
        turned = flat.T
        pre_ref[s] = turned[: (nq + nk) * hd]
        done = []
        for h in range(nq + nk):
            v = turned[h * hd : (h + 1) * hd]
            inv = lax.rsqrt(jnp.mean(v * v, axis=0, keepdims=True) + epsilon)
            v = v * inv * (qgain if h < nq else kgain)
            a, b = v[: hd // 2], v[hd // 2 :]
            done.append(jnp.concatenate([a * cosine - b * sine, b * cosine + a * sine], axis=0))
        for h in range(nk):
            lo = (nq + nk + h) * hd
            done.append(turned[lo : lo + hd])
        parts = [[], []]
        for begin_at, count in ((0, nq), (nq, nk), (nq + nk, nk)):
            for side in range(2):
                parts[side] += done[begin_at + side * count // 2 : begin_at + (side + 1) * count // 2]
        low = jnp.concatenate(parts[0], axis=0)
        high = jnp.concatenate(parts[1], axis=0)
        ex_own[s] = jnp.where(first_core, low, high).astype(BF16)
        ex_send[s] = jnp.where(first_core, high, low).astype(BF16)
        exchange(s).start()
        keep(0, s).start()

    store_qkv = pltpu.make_async_copy(qkv_v, qkv_hbm, store_sem.at[3])
    store_qkv.start()
    store_out = pltpu.make_async_copy(out_v, out_hbm, store_sem.at[4])

    scale = log2e / math.sqrt(hd)
    krow = lax.broadcasted_iota(jnp.int32, (block, groups * block), 0)
    qcol = lax.broadcasted_iota(jnp.int32, (block, groups * block), 1) % block
    base = groups * hd

    def give(s):
        return remote(at_send.at[s], at_got.at[s], exsend.at[1, s], exrecv.at[1, s], near_core)

    def attention(s):
        exchange(s).wait_recv()
        low, high = join_positions(core, ex_own[s], ex_got[s])
        all_ref[s, :, :span] = low
        all_ref[s, :, span:] = high
        length = len_ref[s]
        for i in range(2 * span // block):
            cut = slice(i * block, (i + 1) * block)
            q = jnp.concatenate([all_ref[s, g * hd : (g + 1) * hd, cut] for g in range(groups)], axis=1)
            acc = jnp.zeros((hd, groups * block), F32)
            total = jnp.zeros((1, groups * block), F32)
            for j in range(i + 1):
                kcut = slice(j * block, (j + 1) * block)
                score = dot_tn(all_ref[s, base : base + hd, kcut], q) * scale
                ok = (krow + j * block) < length
                if j == i:
                    ok = ok & (krow <= qcol)
                e = jnp.where(ok, jnp.exp2(score), 0.0)
                total = total + jnp.sum(e, axis=0, keepdims=True)
                acc = acc + dot_nn(all_ref[s, base + hd : base + 2 * hd, kcut], e.astype(BF16))
            inv = 1.0 / total
            att = (acc * inv).astype(BF16)
            for g in range(groups):
                att_ref[s, g * hd : (g + 1) * hd, cut] = att[:, g * block : (g + 1) * block]
                inv_ref[s, g : g + 1, cut] = inv[:, g * block : (g + 1) * block]
        mine, theirs = join_positions(core, att_ref[s, :, :span], att_ref[s, :, span:])
        at_own[s] = mine
        at_send[s] = theirs
        give(s).start()
        keep(1, s).start()
        keep(2, s).start()

    moving = Chain(rank, part_v, in_v, back_v, zsend, zrecv)
    subs = moving.count

    def branch_rows(s):
        give(s).wait_recv()
        low, high = join_positions(core, at_own[s], at_got[s])
        att = jnp.concatenate([low, high], axis=0).T
        tok_ref[s] = att
        keep(3, s).start()
        many = 2
        for k in range(0, per, many):
            rows = att[k * sub : (k + many) * sub]
            for side in range(2):
                part = dot_nn(rows, out_v[side]).astype(BF16)
                for m in range(many):
                    part_v[s * per + k + m, :, side * half : (side + 1) * half] = part[m * sub : (m + 1) * sub]
            for m in range(many):
                u = s * per + k + m

                moving.begin(u)

    def sequence(s, carry):
        project(s)

        attention(s)

        @pl.when(s == 0)
        def _():
            w_out.third()
            w_out.arrived()
            store_out.start()

        branch_rows(s)
        return carry

    lax.fori_loop(0, seqs, sequence, 0)
    tail = pl.ds(subs, total_subs - subs)
    rest = [pltpu.make_async_copy(part_v.at[tail], rest_hbm, rest_sem.at[0])]
    rest[0].start()
    stat_ref[...] = jnp.zeros_like(stat_ref)

    def hidden_store(u):
        cut = pl.ds(pl.multiple_of(u * sub, sub), sub)
        return (
            pltpu.make_async_copy(hid_v.at[u % 2], hidden_hbm.at[cut, :], hid_sem.at[0, u % 2]),
            pltpu.make_async_copy(norm_v.at[u % 2], n2_hbm.at[cut, :], hid_sem.at[1, u % 2]),
        )

    def finish(u):
        s, t = u // per, u % per
        cut = pl.ds(pl.multiple_of(t * sub, sub), sub)

        moving.ready(u)

        @pl.when(u >= 2)
        def _():
            for copy in hidden_store(u - 2):
                copy.wait()

        length = len_ref[s]

        def body(piece_rows, first):
            total = moving.total(u, piece_rows)
            resid = xr_v[s, pl.ds(pl.multiple_of(t * sub + first, 16), 16), :].astype(F32)
            hidden = resid + total
            hid_v[u % 2, piece_rows, :] = hidden
            norm_v[u % 2, piece_rows, :] = (hidden * inverse_rms(hidden) * gain2).astype(BF16)
            place = start + t * sub + first + lax.broadcasted_iota(jnp.int32, (16, 1), 0)
            valid = (place < length).astype(F32)
            stat_ref[0] += fold_lanes(valid * resid * resid)
            stat_ref[1] += fold_lanes(valid * total * total)

        by_pieces(sub, body)
        for copy in hidden_store(u):
            copy.start()

    hb = down_v.shape[2]
    blocks = down_hbm.shape[1] // hb

    def load_down(h):
        cut = pl.ds(pl.multiple_of(h * hb, hb), hb)
        return [pltpu.make_async_copy(down_hbm.at[side, cut, :], down_v.at[h % 2, side], down_sem.at[h % 2, side]) for side in range(2)]

    def store_gi(h):
        cut = pl.ds(pl.multiple_of(h * hb, hb), hb)
        return pltpu.make_async_copy(gi_v.at[h % 2], gi_hbm.at[:, cut], gi_sem.at[h % 2])

    def grad_inner(h):
        for copy in load_down(h):
            copy.wait()

        @pl.when(h + 1 < blocks)
        def _():
            for copy in load_down(h + 1):
                copy.start()

        @pl.when(h >= 2)
        def _():
            store_gi(h - 2).wait()

        for s in range(seqs):
            for q in range(span // 256):
                cut = slice(q * 256, (q + 1) * 256)
                g = dot_nt(cot_v[s, cut, :half], down_v[h % 2, 0]) + dot_nt(cot_v[s, cut, half:], down_v[h % 2, 1])
                gi_v[h % 2, s * span + q * 256 : s * span + (q + 1) * 256, :] = g.astype(BF16)
        store_gi(h).start()

    def chain(i, carry):
        moving.middle(i)
        moving.outward(i - 1)

        @pl.when(i == 1)
        def _():
            w_down.second()
            w_up.first()

        @pl.when(i == 6)
        def _():
            w_gate.second()

        @pl.when(i == 7)
        def _():
            w_down.third()

        @pl.when(i == 8)
        def _():
            w_down.arrived()
            for copy in load_down(0):
                copy.start()

        @pl.when(i == 10)
        def _():
            w_up.second()

        @pl.when(i >= 2)
        def _():
            finish(i - 2)

        @pl.when((i >= 9) & (i < 9 + blocks))
        def _():
            grad_inner(i - 9)

        return carry

    lax.fori_loop(0, subs + 2, chain, 0)
    w_gate.third()
    came = pltpu.make_async_copy(in_v.at[tail], resta_hbm, rest_sem.at[1])

    @pl.when(inner)
    def _():
        for u in range(subs, total_subs):
            moving.hop_in(u).wait_recv()
        came.start()

    w_up.third()
    for u in (subs - 2, subs - 1):
        for copy in hidden_store(u):
            copy.wait()
    for h in (blocks - 2, blocks - 1):
        store_gi(h).wait()
    moving.settle()
    for s in range(seqs):
        exchange(s).wait_send()
        give(s).wait_send()
        for k in range(4):
            keep(k, s).wait()
    every_gain.wait_send()
    w_gate.arrived()
    w_up.arrived()
    pl.when(inner)(came.wait)
    for w in weights:
        w.sent()
    for copy in [store_gf, store_xr, store_n1, store_qkv, store_out] + rest:
        copy.wait()


def forward(lengths, x, cot, w_query, w_key, w_value, w_out, w_gate, w_up, w_down, all_gains, hd, nq, nk):
    seqs, span, width = x.shape
    half = width // 2
    groups = nq // nk
    sub = span // 8
    subs = seqs * span // sub
    here = subs - 4
    block = min(256, span)
    hidden = w_gate.shape[1]
    hb = hidden // 4
    cols = w_query.shape[1] + w_key.shape[1] + w_value.shape[1]
    rows = cols // 2
    any_space = pl.BlockSpec(memory_space=pl.ANY)
    vmem = pl.BlockSpec(memory_space=pltpu.VMEM)
    wide = (seqs, span, width)
    large = [
        shape(wide, BF16), shape(wide, BF16), shape(wide, BF16),
        shape((2, half, cols), BF16), shape((2, w_out.shape[0], half), BF16),
        shape((2, half, hidden), BF16), shape((2, half, hidden), BF16), shape((2, hidden, half), BF16),
        shape((seqs * span, width), F32), shape((seqs * span, width), BF16), shape((subs - here, sub, width), BF16),
        shape((subs - here, sub, width), BF16), shape((seqs * span, hidden), BF16),
    ]
    kept = [
        shape((seqs, (nq + nk) * hd, span), F32), shape((seqs, rows, 2 * span), BF16),
        shape((seqs, groups * hd, 2 * span), BF16), shape((seqs, span, nq * hd), BF16),
    ]
    large += kept
    small = [
        shape((8, 16, width // 8), BF16), shape((3 * hd, span), F32), shape((seqs, groups, 2 * span), F32), shape((2, 8, 128), F32),
    ]
    dma = pltpu.SemaphoreType.DMA
    ex = pltpu.VMEM((seqs, rows, span), BF16)
    at = pltpu.VMEM((seqs, groups * hd, span), BF16)
    moving = pltpu.VMEM((subs, sub, width), BF16)
    landing = pltpu.VMEM((here, sub, width), BF16)
    arriving = pltpu.VMEM((subs, sub, width), BF16)
    flops = 2 * seqs * span * width * (cols + nq * hd) + 16 * seqs * nq * hd * span * span
    return pl.pallas_call(
        functools.partial(forward_kernel, hd, nq, nk, block, sub),
        in_specs=[SMEM] + [any_space] * 9 + [vmem] * 4,
        out_specs=[any_space] * len(large) + [vmem] * len(small),
        out_shape=large + small,
        scratch_shapes=[
            pltpu.VMEM(wide, BF16), pltpu.VMEM(wide, BF16), pltpu.VMEM(wide, BF16),
            pltpu.VMEM((2, half, cols), BF16), pltpu.VMEM((2, w_out.shape[0], half), BF16),
            ex, ex, ex, at, at, at,
            moving, arriving, landing,
            pltpu.VMEM((2, sub, width), F32), pltpu.VMEM((2, sub, width), BF16),
            pltpu.VMEM((w_query.shape[0], cols), BF16), pltpu.VMEM((16, width // 8), BF16),
            pltpu.VMEM((2, 2, hb, half), BF16), pltpu.VMEM((2, seqs * span, hb), BF16),
            *[pltpu.VMEM(a.shape, a.dtype) for a in kept],
            dma((4, seqs)), dma((2,)), dma((5,)), dma((3,)), dma((2,)), dma((2, 2)), dma((2,)), dma((5, 2)), dma((5, 4)), dma((5,)), dma(()), dma(()),
            dma((2, seqs)), dma((2, seqs)), dma((2,)), dma((2, subs)), dma((2, 2)),
        ],
        compiler_params=pltpu.CompilerParams(vmem_limit_bytes=VMEM_MOST, collective_id=1, has_side_effects=True),
        cost_estimate=cost(flops, 80 * seqs * span * width),
        name="attention_forward",
    )(lengths, x, cot, w_query, w_key, w_value, w_out, w_gate, w_up, w_down, *all_gains)


def by_pieces(count, body, size=16):
    def one(p, carry):
        body(pl.ds(pl.multiple_of(p * size, size), size), p * size)
        return carry

    lax.fori_loop(0, count // size, one, 0, unroll=2)


def fold_lanes(values):
    tiles = values[:8] + values[8:]
    return sum(tiles[:, k * 128 : (k + 1) * 128] for k in range(tiles.shape[1] // 128))


class Chain:
    def __init__(self, rank, part, arrive, back, send, recv, landed=False):
        self.landed = landed
        self.inner = (rank % 3) != 0
        self.outer = (rank % 3) == 0
        self.part, self.arrive, self.back = part, arrive, back
        self.send, self.recv = send, recv
        self.side, self.mid = {"tensor": xor_one(rank)}, {"tensor": 3 - rank}
        self.count = back.shape[0]

    def hop_in(self, u):
        return remote(self.part.at[u], self.arrive.at[u], self.send.at[0], self.recv.at[0, u], self.side)

    def hop_mid(self, u):
        return remote(self.arrive.at[u], self.back.at[u], self.send.at[1], self.recv.at[1, u], self.mid)

    def hop_out(self, u):
        return remote(self.part.at[u], self.back.at[u], self.send.at[0], self.recv.at[0, u], self.side)

    def add(self, into, one, two, u):
        def body(cut, first):
            into[u, cut, :] = (one[u, cut, :].astype(F32) + two[u, cut, :].astype(F32)).astype(BF16)

        by_pieces(self.part.shape[1], body)

    def begin(self, u):
        @pl.when(self.outer)
        def _():
            self.hop_in(u).start()

    def middle(self, u):
        @pl.when((u >= 0) & (u < self.count) & self.inner)
        def _():
            if not self.landed:
                self.hop_in(u).wait_recv()
            self.add(self.arrive, self.part, self.arrive, u)
            self.hop_mid(u).start()

    def outward(self, u):
        @pl.when((u >= 0) & (u < self.count) & self.inner)
        def _():
            self.hop_mid(u).wait_recv()
            self.add(self.part, self.part, self.back, u)
            self.hop_out(u).start()

    def ready(self, u):
        @pl.when(self.outer)
        def _():
            self.hop_out(u).wait_recv()

    def total(self, u, cut):
        near = jnp.where(self.inner, self.arrive[u, cut, :], self.part[u, cut, :])
        return near.astype(F32) + self.back[u, cut, :].astype(F32)

    def settle(self):
        def all_sent(ref, count, sem):
            every = ref.at[pl.ds(0, count)]
            remote(every, every, self.send.at[sem], self.recv.at[0, 0], self.side).wait_send()

        @pl.when(self.inner)
        def _():
            all_sent(self.part, self.count, 0)
            all_sent(self.arrive, self.count, 1)

        if not self.landed:

            @pl.when(self.outer)
            def _():
                all_sent(self.part, self.arrive.shape[0], 0)


def feed_both_kernel(
    hb, sub, rows,
    len_ref, n2_hbm, gf_hbm, gate_hbm, up_hbm, down_hbm, gi_hbm, rest_hbm, resta_hbm, xr_hbm, hidden_in, gains_ref,
    ffn_hbm, gb_hbm, gh_hbm, dgate_hbm, dup_hbm, ddown_hbm, hidden_hbm, landx, landy, ring_hbm, gain_out, stat_ref,
    n2_v, gf_v, inner_v, gg_v, gu_v, facc, gacc, wrow, wcol, part_v, in_v, back_v, hid_v, gh_v, gb_v, stage_row, stage_col,
    xtile_v, gi_v, wide_v, temp_v, gain_ref,
    load_sem, wsem, zsend, zrecv, hid_sem, out_sem, ffn_sem, csend, crecv, store_sem, lsend, lrecv, xt_sem, xsend, xrecv, xload, rsend, rrecv, free_sem, done_sem,
):
    core, rank = lax.axis_index("context"), lax.axis_index("tensor")
    near_core = {"context": 1 - core}
    tokens, width = n2_v.shape
    half = width // 2
    hidden = inner_v.shape[1]
    hsteps = hidden // hb
    steps = tokens // rows * hsteps
    per = rows // sub
    chain = Chain(rank, part_v, in_v, back_v, zsend, zrecv)
    subs = chain.count
    known = subs - rest_hbm.shape[0]
    tail = pl.ds(known, subs - known)
    late = Chain(rank, part_v.at[tail], in_v.at[tail], back_v.at[tail], lsend, lrecv, True)
    start = core * (tokens // 2)

    def load_weights(i):
        slot, h = i % 2, i % hsteps
        cut = pl.ds(pl.multiple_of(h * hb, hb), hb)
        here = pl.ds(pl.multiple_of(i // hsteps * rows, rows), rows)
        copies = [pltpu.make_async_copy(gi_hbm.at[here, cut], gi_v.at[slot], wsem.at[slot, 6])]
        for side in range(2):
            copies.append(pltpu.make_async_copy(gate_hbm.at[side, :, cut], wrow.at[slot, 0, side], wsem.at[slot, side]))
            copies.append(pltpu.make_async_copy(up_hbm.at[side, :, cut], wrow.at[slot, 1, side], wsem.at[slot, 2 + side]))
        return copies

    def load_down(i):
        slot, h = i % 2, i % hsteps
        cut = pl.ds(pl.multiple_of(h * hb, hb), hb)
        return [pltpu.make_async_copy(down_hbm.at[side, cut, :], wcol.at[slot, side], wsem.at[slot, 4 + side]) for side in range(2)]

    def load_hidden(u):
        cut = pl.ds(pl.multiple_of(u * sub, sub), sub)
        return pltpu.make_async_copy(hidden_hbm.at[cut, :], hid_v, hid_sem)

    ready = pl.ds(rows, known * sub - rows)
    head = pl.ds(0, rows)
    load_head = pltpu.make_async_copy(n2_hbm.at[head, :], n2_v.at[head, :], load_sem.at[4])
    loads = [
        pltpu.make_async_copy(n2_hbm.at[ready, :], n2_v.at[ready, :], load_sem.at[0]),
        pltpu.make_async_copy(rest_hbm, late.part, load_sem.at[1]),
        pltpu.make_async_copy(resta_hbm, late.arrive, load_sem.at[3]),
    ]
    load_gf = pltpu.make_async_copy(gf_hbm, gf_v, load_sem.at[2])
    for copy in load_weights(0) + [load_head] + loads[1:]:
        copy.start()
    load_hidden(0).start()
    row = lax.axis_index("dp")
    near_x, near_y = {"dp": xor_one(row)}, {"dp": (row + 2) % 4}
    greet([(None, near_core), (None, near_x), (None, near_y), (None, chain.side), (chain.inner, chain.mid)])
    for b in range(8):
        gain_ref[:, b * (width // 8) : (b + 1) * (width // 8)] = gains_ref[b, 1:2, :].astype(F32)
    gain_out[...] = jnp.zeros_like(gain_out)
    stat_ref[...] = jnp.zeros_like(stat_ref)
    load_head.wait()

    def load_x(u):
        at = pl.multiple_of((known + u) * sub, sub)
        return pltpu.make_async_copy(xr_hbm.at[pl.ds(at, sub), :], xtile_v, xt_sem)

    def late_store(u):
        return pltpu.make_async_copy(gh_v, hidden_hbm.at[pl.ds(pl.multiple_of((known + u) * sub, sub), sub), :], out_sem.at[0])

    def late_finish(u):
        load_x(u).start()
        late.ready(u)
        load_x(u).wait()

        @pl.when(u >= 1)
        def _():
            late_store(u - 1).wait()

        length = len_ref[known * sub // (tokens // 2)]
        offset = start + known * sub % (tokens // 2) + u * sub

        def body(cut, first):
            total = late.total(u, cut)
            resid = xtile_v[cut, :].astype(F32)
            hidden_rows = resid + total
            gh_v[cut, :] = hidden_rows
            normed = (hidden_rows * inverse_rms(hidden_rows) * gain_ref[...]).astype(BF16)
            n2_v[pl.ds(pl.multiple_of((known + u) * sub + first, 16), 16), :] = normed
            spot = offset + first + lax.broadcasted_iota(jnp.int32, (16, 1), 0)
            valid = (spot < length).astype(F32)
            stat_ref[0] += fold_lanes(valid * resid * resid)
            stat_ref[1] += fold_lanes(valid * total * total)

        by_pieces(sub, body)
        late_store(u).start()

    def store_gb(u):
        cut = pl.ds(pl.multiple_of(u * sub, sub), sub)
        return pltpu.make_async_copy(gb_v, gb_hbm.at[cut, :], out_sem.at[1])

    def store_gh(u):
        at = pl.ds(pl.multiple_of(u % 2 * sub, sub), sub)
        return pltpu.make_async_copy(gh_v, gh_hbm.at[u // 8, at, :], out_sem.at[0])

    def finish(u):
        chain.ready(u)
        load_hidden(u).wait()

        @pl.when(u >= 1)
        def _():
            store_gb(u - 1).wait()

        def body(piece_rows, first):
            e = chain.total(u, piece_rows)
            hidden_rows = hid_v[piece_rows, :]
            inv = inverse_rms(hidden_rows)
            hat = hidden_rows * inv
            eg = e * gain_ref[...]
            grad = gf_v[pl.ds(pl.multiple_of(u * sub + first, 16), 16), :].astype(F32)
            gh = grad + inv * (eg - hat * jnp.mean(eg * hat, axis=-1, keepdims=True))
            gb_v[piece_rows, :] = gh.astype(BF16)

            @pl.when(u % 8 // 2 == rank)
            def _():
                gh_v[piece_rows, :] = gh

            both = e * hat
            gain_out[...] += both[:8] + both[8:]

        by_pieces(sub, body)
        store_gb(u).start()

        @pl.when(u % 8 // 2 == rank)
        def _():
            store_gh(u).start()
            store_gh(u).wait()

        @pl.when(u + 1 < subs)
        def _():
            load_hidden(u + 1).start()

    def serve(n):
        chain.middle(n)
        chain.outward(n - 2)

        @pl.when((n >= 4) & (n < 4 + subs))
        def _():
            finish(n - 4)

    quarter = width // 4

    def store_ffn(c):
        here = pl.ds(pl.multiple_of(c * rows, rows), rows)
        return [
            pltpu.make_async_copy(
                stage_row.at[c % 2, pl.ds(k * rows, rows), :], ffn_hbm.at[here, pl.ds(k * quarter, quarter)], ffn_sem.at[c % 2, k]
            )
            for k in range(4)
        ]

    def step(i, carry):
        slot, c, h = i % 2, i // hsteps, i % hsteps
        for copy in load_weights(i):
            copy.wait()

        @pl.when(i + 1 < steps)
        def _():
            for copy in load_weights(i + 1):
                copy.start()

            @pl.when((i + 1) // hsteps % 2 == 1)
            def _():
                for copy in load_down(i + 1):
                    copy.start()

        here = pl.ds(pl.multiple_of(c * rows, rows), rows)
        cols = pl.ds(pl.multiple_of(h * hb, hb), hb)
        n = n2_v[here, :]
        wide = min(256, hb)
        for q in range(hb // wide):
            part = slice(q * wide, (q + 1) * wide)
            gate = dot_nn(n[:, :half], wrow[slot, 0, 0, :, part]) + dot_nn(n[:, half:], wrow[slot, 0, 1, :, part])
            up = dot_nn(n[:, :half], wrow[slot, 1, 0, :, part]) + dot_nn(n[:, half:], wrow[slot, 1, 1, :, part])
            gi = gi_v[slot, :, part].astype(F32)
            sig = jax.nn.sigmoid(gate)
            silu = gate * sig
            at = pl.ds(pl.multiple_of(h * hb + q * wide, wide), wide)
            inner_v[here, at] = (silu * up).astype(BF16)
            gg_v[here, at] = (gi * up * sig * (1.0 + gate * (1.0 - sig))).astype(BF16)
            gu_v[here, at] = (gi * silu).astype(BF16)

        @pl.when(h == 0)
        def _():
            gacc[...] = jnp.zeros_like(gacc)

        gg, gu = gg_v[here, cols], gu_v[here, cols]
        span = min(512, half)
        for side in range(2):
            for q in range(half // span):
                part = slice(q * span, (q + 1) * span)
                cut = slice(side * half + q * span, side * half + (q + 1) * span)
                gacc[:, cut] += dot_nt(gg, wrow[slot, 0, side, part, :]) + dot_nt(gu, wrow[slot, 1, side, part, :])

        @pl.when(h == hsteps - 1)
        def _():
            for k in range(per):
                part_v[c * per + k] = gacc[k * sub : (k + 1) * sub, :].astype(BF16)
                chain.begin(c * per + k)

        @pl.when(c % 2 == 1)
        def _():
            pair = pl.ds(pl.multiple_of((c - 1) * rows, rows), 2 * rows)
            inner = inner_v[pair, cols]
            for copy in load_down(i):
                copy.wait()

            @pl.when(h == 0)
            def _():
                facc[...] = jnp.zeros_like(facc)

            for side in range(2):
                for q in range(half // span):
                    part = slice(q * span, (q + 1) * span)
                    cut = slice(side * half + q * span, side * half + (q + 1) * span)
                    facc[:, cut] += dot_nn(inner, wcol[slot, side, :, part])

            @pl.when(h == hsteps - 1)
            def _():
                for m in range(2):

                    @pl.when(c >= 2)
                    def _():
                        for copy in store_ffn(c - 3 + m):
                            copy.wait()

                    for k in range(4):
                        stage_row[m, k * rows : (k + 1) * rows, :] = facc[
                            m * rows : (m + 1) * rows, k * quarter : (k + 1) * quarter
                        ].astype(BF16)
                    for copy in store_ffn(c - 1 + m):
                        copy.start()

        @pl.when(i == 0)
        def _():
            for copy in loads[1:]:
                copy.wait()

        @pl.when(i == 1)
        def _():
            loads[0].start()

        @pl.when(i == hsteps - 1)
        def _():
            loads[0].wait()
            load_gf.start()

        late.middle(i)
        late.outward(i - 3)

        @pl.when((i >= 6) & (i < 6 + late.count))
        def _():
            late_finish(i - 6)

        @pl.when(i == 9)
        def _():
            load_gf.wait()
            late_store(late.count - 1).wait()
            late.settle()
            pl.semaphore_signal(done_sem, inc=1, device_id=chain.side, device_id_type=pl.DeviceIdType.MESH)

            @pl.when(chain.inner)
            def _():
                pl.semaphore_signal(done_sem, inc=1, device_id=chain.mid, device_id_type=pl.DeviceIdType.MESH)

        @pl.when(i == steps - 2)
        def _():
            pl.semaphore_wait(done_sem, jnp.where(chain.inner, 2, 1))

        serve(i - 6)
        return carry

    lax.fori_loop(0, steps, step, 0)
    for c in range(2, steps // hsteps):
        for copy in store_ffn(c):
            copy.wait()

    pl.semaphore_signal(free_sem, inc=1, device_id=near_core, device_id_type=pl.DeviceIdType.MESH)
    outs = (dgate_hbm, dup_hbm, ddown_hbm)

    def landing(w, t):
        return wrow.at[t // 2, w, t % 2] if w < 2 else wcol.at[t // 2, t % 2]

    def landed(w, t, piece):
        return wrow[t // 2, w, t % 2, piece, :] if w < 2 else wcol[t // 2, t % 2, piece, :]

    def staging(w):
        return stage_row if w < 2 else stage_col

    def ship(w, t):
        return remote(staging(w).at[t % 2], landing(w, t), csend.at[w, t], crecv.at[w, t], near_core)

    def keep(w, t):
        cut = pl.ds(pl.multiple_of(t * hb, hb), hb)
        dst = outs[w].at[:, cut] if w < 2 else outs[w].at[cut, :]
        return pltpu.make_async_copy(staging(w).at[t % 2], dst, store_sem.at[w, t])

    def release(kind, w, t):
        if kind == 1:
            ship(w, t).wait_send()
        else:
            keep(w, t).wait()

    def group(kind, w, before, part):
        def one(t, carry):
            cut = pl.ds(pl.multiple_of(t * hb, hb), hb)
            mine = slice(kind * half, (kind + 1) * half)
            @pl.when(t >= 2)
            def _():
                release(kind, w, t - 2)

            if before is not None:

                @pl.when(t < 2)
                def _():
                    release(before[0], before[1], t + hsteps - 2)

            if kind == 0:
                ship(w, t).wait_recv()
            tall = staging(w).shape[1]
            size = min(256, tall)
            for q in range(tall // size):
                piece = slice(q * size, (q + 1) * size)
                if w == 2:
                    left = inner_v[:, pl.ds(pl.multiple_of(t * hb + q * size, size), size)]
                    value = dot_tn(left, gf_v[:, mine])
                else:
                    value = dot_tn(n2_v[:, kind * half + q * size : kind * half + (q + 1) * size], (gg_v, gu_v)[w][:, cut])
                if kind == 0:
                    value = value + landed(w, t, piece).astype(F32)
                staging(w)[t % 2, piece, :] = value.astype(BF16)
            if kind == 1:
                ship(w, t).start()
            else:
                keep(w, t).start()
            return carry

        lax.fori_loop(part * (hsteps // 2), (part + 1) * (hsteps // 2), one, 0)

    pl.semaphore_wait(free_sem, 1)

    def term(m):
        return ffn_hbm.at[pl.ds(pl.multiple_of(m * (2 * sub), 2 * sub), 2 * sub), :]

    fold = Fold(rank, term, None, ring_hbm, (ring_hbm.at[2], None), rsend, rrecv)
    after = iter(range(steps - 6, subs + 4))
    done = []

    def both(kind, w, before):
        for part in range(2):
            group(kind, w, before, part)
            done.append(part)
            if len(done) <= 8 or len(done) % 2 == 0:
                serve(next(after))
            if len(done) == 4:
                fold.begin()

    both(1, 0, None)
    both(0, 0, (1, 0))
    for t in range(hsteps - 2, hsteps):
        keep(0, t).wait()
    gate_sum = Scatter(
        row_blocks(dgate_hbm), wide_v.at[0], wide_v.at[1], half_rows(landx), half_rows(landy), temp_v, xsend, xrecv, xload, near_x, near_y
    )
    gate_sum.begin()
    both(1, 1, None)
    both(1, 2, None)
    gate_sum.pass_on()
    both(0, 1, (1, 1))
    both(0, 2, (1, 2))
    for n in after:
        serve(n)
    for t in range(hsteps - 2, hsteps):
        keep(1, t).wait()
        keep(2, t).wait()
    store_gb(subs - 1).wait()
    gate_sum.arrived()
    gate_sum.settle()
    chain.settle()

    @pl.when(fold.inner)
    def _():
        for k in range(3):
            fold.come(k)

    @pl.when(fold.outer)
    def _():
        fold.settle()


def row_blocks(ref):
    size = ref.shape[0] // 4
    return lambda k, h: ref.at[pl.ds(k * size + h * (size // 2), size // 2), :]


def half_rows(ref):
    size = ref.shape[0] // 2
    return lambda h: ref.at[pl.ds(h * size, size), :]


def feed_both(lengths, n2, gf, gate, up, down, gi, rest, came, xr, hidden_rows, gain):
    tokens, width = n2.shape
    _, half, hidden = gate.shape
    hb = hidden // 4
    sub, rows = tokens // 16, tokens // 4
    count = rest.shape[0]
    any_space = pl.BlockSpec(memory_space=pl.ANY)
    vmem = pl.BlockSpec(memory_space=pltpu.VMEM)
    dma = pltpu.SemaphoreType.DMA
    moving = pltpu.VMEM((16, sub, width), BF16)
    act = pltpu.VMEM((tokens, hidden), BF16)
    return pl.pallas_call(
        functools.partial(feed_both_kernel, hb, sub, rows),
        in_specs=[SMEM] + [any_space] * 10 + [vmem],
        out_specs=[any_space] * 10 + [vmem] * 2,
        out_shape=[
            shape((tokens, width), BF16), shape((tokens, width), BF16), shape((2, 2 * sub, width), F32),
            shape((half, hidden), BF16), shape((half, hidden), BF16), shape((hidden, half), BF16),
            shape((tokens, width), F32), shape((half // 4, hidden), BF16), shape((half // 4, hidden), BF16),
            shape((3, 2 * sub, width), BF16), shape((8, width), F32), shape((2, 8, 128), F32),
        ],
        scratch_shapes=[
            pltpu.VMEM((tokens, width), BF16), pltpu.VMEM((tokens, width), BF16), act, act, act,
            pltpu.VMEM((2 * rows, width), F32), pltpu.VMEM((rows, width), F32),
            pltpu.VMEM((2, 2, 2, half, hb), BF16), pltpu.VMEM((2, 2, hb, half), BF16),
            moving, moving, moving,
            pltpu.VMEM((sub, width), F32), pltpu.VMEM((sub, width), F32), pltpu.VMEM((sub, width), BF16),
            pltpu.VMEM((2, half, hb), BF16), pltpu.VMEM((2, hb, half), BF16),
            pltpu.VMEM((sub, width), BF16), pltpu.VMEM((2, rows, hb), BF16),
            pltpu.VMEM((2, half // 8, hidden), BF16), pltpu.VMEM((2, half // 8, hidden), BF16), pltpu.VMEM((1, width), F32),
            dma((5,)), dma((2, 7)), dma((2,)), dma((2, 16)), dma(()), dma((2,)), dma((2, 4)), dma((3, 4)), dma((3, 4)),
            dma((3, 4)), dma((2,)), dma((2, count)), dma(()), dma((6,)), dma((6,)), dma((3,)), dma(()), dma((5,)), pltpu.SemaphoreType.REGULAR, pltpu.SemaphoreType.REGULAR,
        ],
        input_output_aliases={10: 6},
        compiler_params=pltpu.CompilerParams(vmem_limit_bytes=VMEM_MOST, collective_id=2, has_side_effects=True),
        cost_estimate=cost(18 * tokens * width * hidden, 60 * tokens * width),
        name="feed_forward_both",
    )(lengths, n2, gf, gate, up, down, gi, rest, came, xr, hidden_rows, gain)


class Fold:
    def __init__(self, rank, source, own, slots, finals, send, recv, landed=None):
        self.inner, self.outer = (rank % 3) != 0, (rank % 3) == 0
        self.side, self.mid = {"tensor": xor_one(rank)}, {"tensor": 3 - rank}
        self.leaving = (3 - rank, xor_one(3 - rank), xor_one(rank))
        self.added = (xor_one(3 - rank), 3 - rank, xor_one(rank))
        self.source, self.own, self.slots, self.finals = source, own, slots, finals
        self.send, self.recv, self.landed = send, recv, landed

    def inward(self, k):
        dst = self.slots.at[k] if k < 2 else self.finals[0]
        return remote(self.source(self.leaving[k]), dst, self.send, self.recv.at[k], self.side)

    def across(self, k):
        dst = self.slots.at[2] if k == 0 else self.finals[1]
        return remote(self.slots.at[k], dst, self.send, self.recv.at[3 + k], self.mid)

    def outward(self):
        return remote(self.slots.at[2], self.finals[0], self.send, self.recv.at[0], self.side)

    def begin(self):
        @pl.when(self.outer)
        def _():
            for k in range(3):
                self.inward(k).start()

    def come(self, k):
        (self.landed[k].wait if self.landed is not None else self.inward(k).wait_recv)()

    def step(self, k):
        @pl.when(self.inner)
        def _():
            if k < 2:
                self.come(k)
            else:
                self.across(0).wait_recv()
            read = self.own(self.added[k])

            def body(cut, first):
                self.slots[k, cut, :] = (self.slots[k, cut, :].astype(F32) + read(cut).astype(F32)).astype(BF16)

            by_pieces(self.slots.shape[1], body)
            (self.across(k) if k < 2 else self.outward()).start()

    def arrived(self):
        @pl.when(self.inner)
        def _():
            self.come(2)
            self.across(1).wait_recv()

        @pl.when(self.outer)
        def _():
            self.outward().wait_recv()

    def settle(self):
        three = self.slots.at[pl.ds(0, 3)]
        every = remote(three, three, self.send, self.recv.at[0], self.side)
        if self.landed is None:
            every.wait_send()
        else:
            pl.when(self.inner)(every.wait_send)


def tall(ref):
    return 16 * max(1, 2048 // ref.shape[1])


class Scatter:
    def __init__(self, block, from_x, from_y, land_x, land_y, temps, send, recv, load, near_x, near_y):
        self.block, self.from_x, self.from_y, self.land_x, self.land_y = block, from_x, from_y, land_x, land_y
        self.temps, self.load = temps, load
        sem = lambda k: (send.at[k], recv.at[k])
        self.first = [
            remote(block(3, 0), from_x, *sem(0), near_x),
            remote(block(3, 1), from_y, *sem(1), near_y),
            remote(block(1, 0), land_x(0), *sem(2), near_x),
            remote(block(2, 1), land_y(1), *sem(3), near_y),
        ]
        self.second = [
            remote(from_y, land_x(1), *sem(4), near_x),
            remote(from_x, land_y(0), *sem(5), near_y),
        ]

    def begin(self):
        for copy in self.first:
            copy.start()

    def pass_on(self):
        loads = [
            pltpu.make_async_copy(self.block(1, 1), self.temps.at[0], self.load.at[0]),
            pltpu.make_async_copy(self.block(2, 0), self.temps.at[1], self.load.at[1]),
        ]
        for copy in loads:
            copy.start()
        for which, into in ((1, self.from_y), (0, self.from_x)):
            self.first[which].wait_recv()
            loads[1 - which].wait()
            temp = 1 - which

            def body(cut, first):
                into[cut, :] = (into[cut, :].astype(F32) + self.temps[temp, cut, :].astype(F32)).astype(BF16)

            by_pieces(into.shape[0], body, tall(into))
            self.second[temp].start()

    def arrived(self):
        for copy in self.first[2:] + self.second:
            copy.wait_recv()

    def keep(self, out, store):
        for h in range(2):
            loads = [
                pltpu.make_async_copy(src, self.temps.at[k], self.load.at[k])
                for k, src in enumerate((self.block(0, h), self.land_x(h), self.land_y(h)))
            ]
            for copy in loads:
                copy.start()
            for copy in loads:
                copy.wait()

            def body(cut, first):
                self.temps[0, cut, :] = sum(self.temps[k, cut, :].astype(F32) for k in range(3)).astype(BF16)

            by_pieces(self.temps.shape[1], body, tall(self.temps.at[0]))
            copy = pltpu.make_async_copy(self.temps.at[0], out(h), store)
            copy.start()
            copy.wait()

    def settle(self):
        for copy in self.first + self.second:
            copy.wait_send()


def backward_kernel(
    hd, nq, nk, block,
    len_ref, gb_hbm, hidden_hbm, ffn_hbm, ring_hbm, xr_hbm, n1_hbm, tok_hbm, outw_hbm, qkvw_hbm, all_hbm, att_hbm, inv_hbm, pre_hbm,
    gh_hbm, dgate_hbm, landx0, landy0, dup_hbm, ddown_hbm, table_ref, gains_ref, stat_ref, stat2_ref, gain2_ref,
    out_hbm, gin_hbm, fin_hbm, finb_hbm, own_hbm, sum_gate, sum_up, sum_down, mine_o, mine_q, landx1, landy1, landx2, landy2, landx3, landy3, landx4, landy4,
    lines_out, small_out,
    act_v, rows_v, qkvw_v, tok_v, all_v, att_v, inv_v, pre_v, grads, da_all, da_own, da_send, da_got, d_own, d_send, d_got, dpre_v,
    first_v, slots_v, turns_v, piece_v, wide_a, wide_b, temp_a, temp_b,
    go_v, so_v, wide_o, temp_o, gq_v, sq_v, wide_q, temp_q,
    tile_v, otile_v, lines_v, small_v, heads_v, lin1, lin2, lin3, small_r,
    load_sem, zsend, zrecv, piece_sem, xsend, xrecv, xload, own_sem, exsend, exrecv, osend, orecv, qsend, qrecv,
    tile_sem, outs_sem, sum_sem, smsend, smrecv,
):
    seqs, _, slots = all_v.shape
    span = slots // 2
    width = act_v.shape[1]
    half = width // 2
    groups = nq // nk
    share = span // 4
    row, core, rank = lax.axis_index("dp"), lax.axis_index("context"), lax.axis_index("tensor")
    start = core * span
    near = [row, xor_one(row), (row + 2) % 4, 3 - row]
    near_x, near_y, near_core = {"dp": near[1]}, {"dp": near[2]}, {"context": 1 - core}
    z_right, z_left, z_far = {"tensor": (rank + 1) % 4}, {"tensor": (rank + 3) % 4}, {"tensor": (rank + 2) % 4}
    first_core = core == 0

    def load(k, src, dst):
        copy = pltpu.make_async_copy(src, dst, load_sem.at[k])
        copy.start()
        return copy

    load_gb = load(0, gb_hbm, act_v)
    load_outw = load(1, outw_hbm, rows_v)
    load_att = [
        load(2, all_hbm, all_v), load(3, att_hbm, att_v), load(4, inv_hbm, inv_v), load(5, pre_hbm, pre_v),
    ]
    load_tok = load(6, tok_hbm, tok_v)
    load_qkvw = load(7, qkvw_hbm, qkvw_v)

    def piece_rows(s, m):
        return pl.ds(pl.multiple_of(s * span + m * share, share), share)

    def load_piece(s, m):
        return pltpu.make_async_copy(ffn_hbm.at[piece_rows(s, m), :], piece_v.at[s], piece_sem.at[s])

    greet([(None, d) for d in (near_x, near_y, {"dp": near[3]}, near_core, z_right, z_left, z_far)])

    last = seqs - 1
    inner = (rank % 3) != 0
    came = []
    for k, slot in enumerate((0, 1, 3)):
        came.append(pltpu.make_async_copy(ring_hbm.at[k], slots_v.at[0, slot], load_sem.at[12 + k]))

    @pl.when(inner)
    def _():
        for copy in came:
            copy.start()

    def ffn_own(s):
        def own(m):
            load_piece(s, m).wait()
            return lambda cut: piece_v[s, cut, :]

        return own

    def first_own(s):
        return lambda m: lambda cut: first_v[s, m, cut, :]

    ffn_rings = [
        Fold(
            rank, lambda m, s=s: ffn_hbm.at[piece_rows(s, m), :], ffn_own(s), slots_v.at[s], (slots_v.at[s, 3], slots_v.at[s, 4]),
            zsend.at[s], zrecv.at[s], came if s == 0 else None,
        )
        for s in range(seqs)
    ]
    first_rings = [
        Fold(
            rank, lambda m, s=s: first_v.at[s, m], first_own(s), turns_v.at[s], (fin_hbm.at[s], finb_hbm.at[s]),
            zsend.at[seqs + s], zrecv.at[seqs + s],
        )
        for s in range(seqs)
    ]
    for s in range(1, seqs):
        ffn_rings[s].begin()
    for s in range(seqs):
        load_piece(s, jnp.where(inner, ffn_rings[s].added[0], rank)).start()

    def ffn_step(s, k):
        ffn_rings[s].step(k)

        @pl.when(inner)
        def _():
            load_piece(s, ffn_rings[s].added[k + 1] if k < 2 else rank).start()

    def in_hbm(ref, axis):
        size = ref.shape[axis] // 4
        h2 = (size if axis == 0 else ref.shape[0]) // 2

        def get(k, h):
            if axis == 0:
                return ref.at[pl.ds(k * size + h * h2, h2), :]
            return ref.at[pl.ds(h * h2, h2), pl.ds(k * size, size)]

        return get

    def halves(ref):
        h2 = ref.shape[0] // 2
        return lambda h: ref.at[pl.ds(h * h2, h2), :]

    def in_vmem(ref):
        h2 = ref.shape[1] // 2
        return lambda k, h: ref.at[k, pl.ds(h * h2, h2), :]

    def scatter(i, get, wide, land_x, land_y, temps):
        return Scatter(get, wide.at[0], wide.at[1], land_x, land_y, temps, xsend.at[i], xrecv.at[i], xload.at[i], near_x, near_y)

    s_gate = scatter(0, in_hbm(dgate_hbm, 0), wide_a, halves(landx0), halves(landy0), temp_a)
    s_up = scatter(0, in_hbm(dup_hbm, 0), wide_a, halves(landx1), halves(landy1), temp_a)
    s_down = scatter(1, in_hbm(ddown_hbm, 1), wide_b, halves(landx2), halves(landy2), temp_b)
    s_out = scatter(2, in_vmem(go_v), wide_o, halves(landx3), halves(landy3), temp_o)
    s_qkv = scatter(3, in_vmem(gq_v), wide_q, halves(landx4), halves(landy4), temp_q)
    s_up.begin()
    ffn_step(0, 0)
    ffn_step(0, 1)

    load_gb.wait()
    load_outw.wait()

    def give(s):
        return remote(da_send.at[s], da_got.at[s], exsend.at[0, s], exrecv.at[0, s], near_core)

    def exchange(s):
        return remote(d_send.at[s], d_got.at[s], exsend.at[1, s], exrecv.at[1, s], near_core)

    def branch_rows(s, carry):
        here = pl.ds(pl.multiple_of(s * span, span), span)
        parts = []
        for q in range(2):
            cut = slice(q * (nq * hd // 2), (q + 1) * (nq * hd // 2))
            da = dot_nt(rows_v[0, cut, :], act_v[here, :half]) + dot_nt(rows_v[1, cut, :], act_v[here, half:])
            parts.append(da.astype(BF16))
        da_own[s] = jnp.where(first_core, parts[0], parts[1])
        da_send[s] = jnp.where(first_core, parts[1], parts[0])
        give(s).start()
        return carry

    lax.fori_loop(0, seqs, branch_rows, 0)

    def load_x(s):
        return [pltpu.make_async_copy(xr_hbm.at[s, :, pl.ds(k * half, half)], rows_v.at[k], load_sem.at[10 + k]) for k in range(2)]

    for copy in load_x(0):
        copy.start()
    for copy in load_att:
        copy.wait()

    scale = log2e / math.sqrt(hd)
    back = 1.0 / math.sqrt(hd)
    krow = lax.broadcasted_iota(jnp.int32, (block, groups * block), 0)
    qcol = lax.broadcasted_iota(jnp.int32, (block, groups * block), 1) % block
    base = groups * hd

    def attention(s):
        give(s).wait_recv()
        low, high = join_positions(core, da_own[s], da_got[s])
        da_all[:, :span] = low
        da_all[:, span:] = high
        length = len_ref[s]
        grads[base:, :] = jnp.zeros((2 * hd, slots), F32)
        for i in range(slots // block):
            cut = slice(i * block, (i + 1) * block)
            q = jnp.concatenate([all_v[s, g * hd : (g + 1) * hd, cut] for g in range(groups)], axis=1)
            da = jnp.concatenate([da_all[g * hd : (g + 1) * hd, cut] for g in range(groups)], axis=1)
            at = jnp.concatenate([att_v[s, g * hd : (g + 1) * hd, cut] for g in range(groups)], axis=1)
            inv = jnp.concatenate([inv_v[s, g : g + 1, cut] for g in range(groups)], axis=1)
            delta = jnp.sum(at.astype(F32) * da.astype(F32), axis=0, keepdims=True)
            dq = jnp.zeros((hd, groups * block), F32)
            for j in range(i + 1):
                kcut = slice(j * block, (j + 1) * block)
                key = all_v[s, base : base + hd, kcut]
                score = dot_tn(key, q) * scale
                ok = (krow + j * block) < length
                if j == i:
                    ok = ok & (krow <= qcol)
                p = jnp.where(ok, jnp.exp2(score) * inv, 0.0)
                dp = dot_tn(all_v[s, base + hd : base + 2 * hd, kcut], da)
                ds = (p * (dp - delta)).astype(BF16)
                dq = dq + dot_nn(key, ds)
                grads[base : base + hd, kcut] += dot_nt(q, ds) * back
                grads[base + hd : base + 2 * hd, kcut] += dot_nt(da, p.astype(BF16))
            dq = dq * back
            for g in range(groups):
                grads[g * hd : (g + 1) * hd, cut] = dq[:, g * block : (g + 1) * block]
        mine, theirs = join_positions(core, grads[:, :span], grads[:, span:])
        d_own[s] = mine.astype(BF16)
        d_send[s] = theirs.astype(BF16)
        exchange(s).start()

    quarter = hd // 2
    cosine, sine = table_ref[:quarter, :], table_ref[quarter : 2 * quarter, :]
    qgain, kgain = table_ref[2 * quarter : 2 * quarter + hd, 0:1], table_ref[2 * quarter + hd :, 0:1]
    sides = (nq // 2, nk // 2, nk // 2)
    copies_in_tensor = 1.0 / lax.axis_size("tensor")
    lines_v[:8, :] = jnp.zeros((8, width), F32)
    lines_v[8:, :] = gain2_ref[...] * copies_in_tensor
    heads_v[...] = jnp.zeros_like(heads_v)
    valid_slots = jnp.int32(0)
    for s in range(seqs):
        valid_slots = valid_slots + jnp.clip(len_ref[s] - start, 0, span)
    count = valid_slots.astype(F32) * (copies_in_tensor / 128.0)
    small_v[...] = jnp.zeros_like(small_v)
    for k in range(2):
        both = stat_ref[k] + stat2_ref[k]
        small_v[1 + k : 2 + k, :] = jnp.sum(both, axis=0, keepdims=True) * copies_in_tensor
    small_v[4:5, :] = jnp.broadcast_to(count, (1, 128))
    load_qkvw.wait()

    def fold_columns(values):
        return sum(values[:, k * 128 : (k + 1) * 128] for k in range(values.shape[1] // 128))

    def heads_rows(s):
        exchange(s).wait_recv()
        low, high = join_positions(core, d_own[s].astype(F32), d_got[s].astype(F32))
        parts = [[], [], []]
        for side in (low, high):
            at = 0
            for kind, number in enumerate(sides):
                for _ in range(number):
                    parts[kind].append(side[at : at + hd])
                    at += hd
        done = []
        for h in range(nq + nk):
            kind = 0 if h < nq else 1
            g = parts[kind][h - kind * nq]
            a, b = g[: hd // 2], g[hd // 2 :]
            g = jnp.concatenate([a * cosine + b * sine, b * cosine - a * sine], axis=0)
            v = pre_v[s, h * hd : (h + 1) * hd, :]
            inv = lax.rsqrt(jnp.mean(v * v, axis=0, keepdims=True) + epsilon)
            hat = v * inv
            heads_v[kind * hd : (kind + 1) * hd, :] += fold_columns(g * hat)
            gg = g * (qgain if kind == 0 else kgain)
            done.append(inv * (gg - hat * jnp.mean(gg * hat, axis=0, keepdims=True)))
        done += parts[2]
        for h in range(nq + 2 * nk):
            pair = h % 2
            if pair == 0:
                two = jnp.concatenate([done[h], done[h + 1]], axis=0).T.astype(BF16)
                dpre_v[pl.ds(pl.multiple_of(s * span, span), span), h * hd : (h + 2) * hd] = two
        for copy in load_x(s):
            copy.wait()
        for m in range(4):
            rows = slice(m * share, (m + 1) * share)
            xs = [rows_v[k, rows, :].astype(F32) for k in range(2)]
            mean = sum(jnp.sum(x * x, axis=-1, keepdims=True) for x in xs) * (1.0 / width)
            inv = lax.rsqrt(mean + epsilon)
            dpre = dpre_v[pl.ds(pl.multiple_of(s * span + m * share, share), share), :]
            for k in range(2):
                part = dot_nt(dpre, qkvw_v[k])
                cut = slice(k * half, (k + 1) * half)
                first_v[s, m, :, cut] = part.astype(BF16)
                both = part * (xs[k] * inv)
                lines_v[:8, cut] += sum(both[8 * r : 8 * r + 8] for r in range(share // 8))

    def sequence(s, carry):
        attention(s)

        @pl.when(s == last)
        def _():
            ffn_step(1, 1)
            s_up.pass_on()

        heads_rows(s)

        @pl.when(s == 0)
        def _():
            for copy in load_x(1):
                copy.start()
            first_rings[0].begin()
            ffn_step(1, 0)
            ffn_step(0, 2)
            s_down.begin()

        @pl.when(s == last)
        def _():
            first_rings[1].begin()

        return carry

    lax.fori_loop(0, seqs, sequence, 0)

    def hop_copies(n, items):
        base_at = (0, 1, 4, 5, 8)[n]
        return [
            remote(src, dst, smsend.at[base_at + i], smrecv.at[base_at + i], device) for i, (device, src, dst, _) in enumerate(items)
        ]

    def hop_begin(n, items):
        for copy in hop_copies(n, items):
            copy.start()

    def hop_end(n, items):
        for copy in hop_copies(n, items):
            copy.wait()
        for _, _, dst, place_to in items:
            if place_to is None:
                small_v[...] += dst[...]
            else:
                lines_v[:, place_to] += dst[...]

    piece = width // 8

    def columns(k):
        return slice(k * piece, (k + 1) * piece)

    def view(k, count=1):
        return lines_v.at[:, pl.ds(k * piece, count * piece)]

    hop_core = [(near_core, view(4, 4), lin1, slice(0, half))]
    near_all = [near_x, near_y, {"dp": near[3]}]
    hop_lines = [(near_all[k], view(1 + k), lin2.at[k], columns(0)) for k in range(3)]
    hop_small = [(near_core, small_v, small_r.at[0], None)]
    hop_square = [(near_all[k], small_v, small_r.at[1 + k], None) for k in range(3)]
    z_all = [z_right, z_far, z_left]
    hop_chain = [(z_all[k], view(0), lin3.at[k], columns(0)) for k in range(3)]
    hop_chain += [(z_all[k], small_v, small_r.at[4 + k], None) for k in range(3)]
    hop_begin(0, hop_core)

    load_tok.wait()
    blocks_o = [remote(so_v.at[k], go_v.at[k], osend.at[k], orecv.at[k], near_core) for k in range(4)]
    size_o = half // 4
    for k in range(4):
        cut = slice(half + k * size_o, half + (k + 1) * size_o)
        so_v[k] = dot_tn(tok_v[...], act_v[:, cut]).astype(BF16)
        blocks_o[k].start()
    ffn_step(1, 2)
    for k in range(4):
        blocks_o[k].wait_recv()
        cut = slice(k * size_o, (k + 1) * size_o)
        go_v[k] = (dot_tn(tok_v[...], act_v[:, cut]) + go_v[k].astype(F32)).astype(BF16)
    s_out.begin()
    load_n1 = load(0, n1_hbm, act_v)
    hop_end(0, hop_core)
    hop_begin(1, hop_lines)
    load_n1.wait()
    blocks_q = [remote(sq_v.at[k], gq_v.at[k], qsend.at[k], qrecv.at[k], near_core) for k in range(4)]
    size_q = half // 4
    for k in range(4):
        cut = slice(half + k * size_q, half + (k + 1) * size_q)
        sq_v[k] = dot_tn(act_v[:, cut], dpre_v[...]).astype(BF16)
        blocks_q[k].start()
    for k in range(4):
        blocks_q[k].wait_recv()
        cut = slice(k * size_q, (k + 1) * size_q)
        gq_v[k] = (dot_tn(act_v[:, cut], dpre_v[...]) + gq_v[k].astype(F32)).astype(BF16)
    s_qkv.begin()
    keeps = [
        pltpu.make_async_copy(go_v.at[0], mine_o, own_sem.at[0]),
        pltpu.make_async_copy(gq_v.at[0], mine_q, own_sem.at[1]),
    ]
    keeps += [pltpu.make_async_copy(first_v.at[s, rank], own_hbm.at[s], own_sem.at[2 + s]) for s in range(seqs)]
    for copy in keeps:
        copy.start()


    def place(tile, dst, s):
        for o in range(2):
            for k in range(4):
                b = near[k] * 2 + (core if o == 0 else 1 - core)
                cut = pl.ds(pl.multiple_of(b * piece, piece), piece)
                pltpu.make_async_copy(tile.at[:, pl.ds((o * 4 + k) * piece, piece)], dst.at[s, :, cut], outs_sem).start()
        pltpu.make_async_copy(tile, dst.at[s], outs_sem).wait()

    def out_share(s):
        keep = pltpu.make_async_copy(hidden_hbm.at[piece_rows(s, rank), :], tile_v, tile_sem.at[0])
        keep.start()
        ffn_rings[s].arrived()
        read = ffn_rings[s].own(rank)
        keep.wait()

        def body(cut, first):
            ffn = slots_v[s, 3, cut, :].astype(F32) + read(cut).astype(F32)
            ffn = ffn + jnp.where(inner, slots_v[s, 4, cut, :].astype(F32), 0.0)
            otile_v[cut, :] = (tile_v[cut, :] + ffn).astype(BF16)
            spot = start + rank * share + first + lax.broadcasted_iota(jnp.int32, (16, 1), 0)
            valid = (spot < len_ref[s]).astype(F32)
            small_v[3:4, :] += jnp.sum(fold_lanes(valid * ffn * ffn), axis=0, keepdims=True)

        by_pieces(share, body)
        place(otile_v, out_hbm, s)

    def in_share(s):
        first_rings[s].arrived()
        tiles = (piece_v.at[0], piece_v.at[1], otile_v)
        rows = pl.ds(pl.multiple_of(rank * share, share), share)
        loads = [
            pltpu.make_async_copy(src, dst, load_sem.at[k])
            for k, (src, dst) in enumerate(zip((fin_hbm.at[s], finb_hbm.at[s], xr_hbm.at[s, rows, :]), tiles))
        ]
        loads.append(pltpu.make_async_copy(gh_hbm.at[s], tile_v, load_sem.at[3]))
        for copy in loads:
            copy.start()
        gain = jnp.concatenate([gains_ref[b, 0:1, :] for b in range(8)], axis=1).astype(F32)
        for copy in loads:
            copy.wait()

        def body(cut, at):
            e = piece_v[0, cut, :].astype(F32) + first_v[s, rank, cut, :].astype(F32)
            e = e + jnp.where(inner, piece_v[1, cut, :].astype(F32), 0.0)
            x = otile_v[cut, :].astype(F32)
            inv = inverse_rms(x)
            hat = x * inv
            eg = e * gain
            tile_v[cut, :] = tile_v[cut, :] + inv * (eg - hat * jnp.mean(eg * hat, axis=-1, keepdims=True))

        by_pieces(share, body)
        place(tile_v, gin_hbm, s)

    small_v[0:1, :] = jnp.sum(heads_v[...].T, axis=0, keepdims=True)
    first_rings[0].step(0)
    out_share(0)
    s_down.pass_on()
    out_share(1)
    hop_end(1, hop_lines)
    hop_begin(2, hop_small)
    hop_end(2, hop_small)
    hop_begin(3, hop_square)
    first_rings[0].step(1)
    first_rings[0].step(2)
    s_out.pass_on()
    s_qkv.pass_on()
    s_gate.keep(halves(sum_gate), sum_sem)
    s_up.arrived()
    s_up.keep(halves(sum_up), sum_sem)
    first_rings[1].step(0)
    hop_end(3, hop_square)
    hop_begin(4, hop_chain)
    s_down.arrived()
    s_down.keep(halves(sum_down), sum_sem)
    first_rings[1].step(1)
    first_rings[1].step(2)
    for s in range(last):
        in_share(s)
    hop_end(4, hop_chain)
    lines_out[...] = lines_v[:, :piece]
    small_out[...] = small_v[...]
    for item in (s_out, s_qkv):
        item.arrived()
    first_rings[last].arrived()
    for copy in keeps:
        copy.wait()
    for ring in ffn_rings + first_rings:
        ring.settle()
    for item in (s_up, s_down, s_out, s_qkv):
        item.settle()
    for copy in blocks_o + blocks_q:
        copy.wait_send()
    for s in range(seqs):
        give(s).wait_send()
        exchange(s).wait_send()


def backward(
    lengths, gb, hidden_rows, ffn, ring, xr, n1, tok, outw, qkvw, everything, att, inv, pre, gh, dgate, landx, landy, dup, ddown,
    table, gains, stat, stat2, gain2_part, hd, nq, nk,
):
    seqs, span, width = xr.shape
    half = width // 2
    groups = nq // nk
    share = span // 4
    piece = width // 8
    hidden = dup.shape[1]
    cols = qkvw.shape[2]
    feat = nq * hd
    block = min(256, span)
    any_space = pl.BlockSpec(memory_space=pl.ANY)
    vmem = pl.BlockSpec(memory_space=pltpu.VMEM)
    dma = pltpu.SemaphoreType.DMA
    hold = lambda *dims: pltpu.VMEM(dims, BF16)
    wide = lambda *dims: pltpu.VMEM(dims, F32)
    token = shape((seqs, share, width), BF16)
    big = [token, shape((seqs - 1, share, width), F32)] + [token] * 3 + [shape((piece, hidden), BF16)] * 2 + [shape((hidden, piece), BF16)]
    big += [shape((feat, piece), BF16), shape((piece, cols), BF16)]
    big += [shape((piece, hidden), BF16)] * 2 + [shape((hidden, piece), BF16)] * 2
    big += [shape((feat, piece), BF16)] * 2 + [shape((piece, cols), BF16)] * 2
    small = [shape((16, piece), F32), shape((8, 128), F32)]
    rows = everything.shape[1]
    scratch = [
        hold(seqs * span, width), hold(2, span, half), hold(2, half, cols), hold(seqs * span, feat), hold(*everything.shape), hold(*att.shape),
        wide(*inv.shape), wide(*pre.shape), wide(rows, 2 * span), hold(groups * hd, 2 * span),
        hold(seqs, feat // 2, span), hold(seqs, feat // 2, span), hold(seqs, feat // 2, span),
        hold(seqs, rows, span), hold(seqs, rows, span), hold(seqs, rows, span), hold(seqs * span, cols),
        hold(seqs, 4, share, width), hold(seqs, 5, share, width), hold(seqs, 3, share, width), hold(seqs, share, width),
        hold(2, piece // 2, hidden), hold(2, hidden // 2, piece), hold(3, piece // 2, hidden), hold(3, hidden // 2, piece),
        hold(4, feat, piece), hold(4, feat, piece), hold(2, feat // 2, piece), hold(2, feat // 2, piece),
        hold(4, piece, cols), hold(4, piece, cols), hold(2, piece // 2, cols), hold(2, piece // 2, cols),
        wide(share, width), hold(share, width),
        wide(16, width), wide(8, 128), wide(2 * hd, 128), wide(16, half), wide(3, 16, piece), wide(3, 16, piece), wide(7, 8, 128),
        dma((15,)), dma((2 * seqs,)), dma((2 * seqs, 5)), dma((seqs,)), dma((4, 6)), dma((4, 6)), dma((4, 3)), dma((2 + seqs,)),
        dma((2, seqs)), dma((2, seqs)), dma((4,)), dma((4,)), dma((4,)), dma((4,)), dma((2,)), dma(()), dma(()), dma((14,)), dma((14,)),
    ]
    tokens = seqs * span
    return pl.pallas_call(
        functools.partial(backward_kernel, hd, nq, nk, block),
        in_specs=[SMEM] + [any_space] * 19 + [vmem] * 5,
        out_specs=[any_space] * len(big) + [vmem] * 2,
        out_shape=big + small,
        scratch_shapes=scratch,
        compiler_params=pltpu.CompilerParams(vmem_limit_bytes=VMEM_MOST, collective_id=3, has_side_effects=True),
        cost_estimate=cost(4 * tokens * width * (cols + feat), 60 * tokens * width),
        name="attention_backward",
    )(
        lengths, gb, hidden_rows, ffn, ring, xr, n1, tok, outw, qkvw, everything, att, inv, pre, gh, dgate, landx, landy, dup, ddown,
        table, gains, stat, stat2, gain2_part,
    )


def results_kernel(
    hd, nqc, nkc, count,
    sum_gate, sum_up, sum_down, mine_o, lx3, ly3, mine_q, lx4, ly4, gh, xr, fin, finb, own, out, early, gains_ref, lines_ref, small_ref,
    output, gin, ggate, gup, gdown, gout, gq, gk, gv, gain_a, gain_b, gain_q, gain_k, rms,
    gate_i, up_i, down_i, o_i, q_i, gate_o, up_o, down_o, o_o, q_o, gh_v, x_v, fin_v, finb_v, own_v, early_v, out_v,
    in_sem, token_sem, out_sem, place_sem, copy_sem,
):
    row, core, rank = lax.axis_index("dp"), lax.axis_index("context"), lax.axis_index("tensor")
    near = [row, xor_one(row), (row + 2) % 4, 3 - row]
    seqs, share, width = out_v.shape
    last = seqs - 1
    piece = width // 8
    sums = (
        ((sum_gate,), gate_i, gate_o, ((0, ggate),)),
        ((sum_up,), up_i, up_o, ((0, gup),)),
        ((sum_down,), down_i, down_o, ((0, gdown),)),
        ((mine_o, lx3, ly3), o_i, o_o, ((0, gout),)),
        ((mine_q, lx4, ly4), q_i, q_o, ((0, gq), (nqc, gk), (nqc + nkc, gv))),
    )
    simple = [
        (pltpu.make_async_copy(out, out_v, copy_sem.at[0]), pltpu.make_async_copy(out_v, output, copy_sem.at[1])),
        (pltpu.make_async_copy(early, early_v, copy_sem.at[2]), pltpu.make_async_copy(early_v, gin.at[pl.ds(0, last)], copy_sem.at[3])),
    ]

    def loads(i):
        return [pltpu.make_async_copy(src, sums[i][1].at[k], in_sem.at[i, k]) for k, src in enumerate(sums[i][0])]

    mine = pl.ds(pl.multiple_of(rank * share, share), share)
    tokens = [
        pltpu.make_async_copy(src, dst, token_sem.at[k])
        for k, (src, dst) in enumerate(
            ((gh.at[last], gh_v), (xr.at[last, mine, :], x_v), (fin.at[last], fin_v), (finb.at[last], finb_v), (own.at[last], own_v))
        )
    ]
    for i in range(len(sums)):
        for copy in loads(i):
            copy.start()
    for copy in tokens + [first for first, _ in simple]:
        copy.start()

    first = jnp.sum(lines_ref[:8, :], axis=0, keepdims=True)
    second = jnp.sum(lines_ref[8:, :], axis=0, keepdims=True)
    gain_a[...] = first.reshape(gain_a.shape)
    gain_b[...] = second.reshape(gain_b.shape)
    gain_q[...] = small_ref[0:1, :hd].reshape(gain_q.shape)
    gain_k[...] = small_ref[0:1, hd : 2 * hd].reshape(gain_k.shape)
    total = jnp.sum(small_ref[4:5, :], keepdims=True) * count
    for k in range(3):
        square = jnp.sum(small_ref[1 + k : 2 + k, :], keepdims=True) / total
        rms[k] = jnp.max(jnp.sqrt(jnp.broadcast_to(square, (8, 128))))

    stores = []
    for i, (terms, came, total_v, parts) in enumerate(sums):
        for copy in loads(i):
            copy.wait()

        def body(cut, at):
            total_v[cut, :] = sum(came[k, cut, :].astype(F32) for k in range(len(terms)))

        by_pieces(total_v.shape[0], body, tall(total_v))
        for n, (at, dst) in enumerate(parts):
            stores.append(pltpu.make_async_copy(total_v.at[:, pl.ds(at, dst.shape[1])], dst, out_sem.at[i, n]))
            stores[-1].start()
    for first, second in simple:
        first.wait()
        second.start()

    gain = jnp.concatenate([gains_ref[b, 0:1, :] for b in range(8)], axis=1).astype(F32)
    for copy in tokens:
        copy.wait()
    inner = (rank % 3) != 0

    def body(cut, at):
        e = fin_v[cut, :].astype(F32) + own_v[cut, :].astype(F32)
        e = e + jnp.where(inner, finb_v[cut, :].astype(F32), 0.0)
        x = x_v[cut, :].astype(F32)
        inv = inverse_rms(x)
        hat = x * inv
        eg = e * gain
        gh_v[cut, :] = gh_v[cut, :] + inv * (eg - hat * jnp.mean(eg * hat, axis=-1, keepdims=True))

    by_pieces(share, body)
    for o in range(2):
        for k in range(4):
            b = near[k] * 2 + (core if o == 0 else 1 - core)
            cut = pl.ds(pl.multiple_of(b * piece, piece), piece)
            src = gh_v.at[:, pl.ds((o * 4 + k) * piece, piece)]
            stores.append(pltpu.make_async_copy(src, gin.at[last, :, cut], place_sem.at[o * 4 + k]))
            stores[-1].start()
    for copy in stores + [second for _, second in simple]:
        copy.wait()


def finish_results(sums, mine_o, mine_q, lands_o, lands_q, gh, xr, fin, finb, own, out, early, gains, lines, small, hd, nqc, nkc):
    seqs, share, width = out.shape
    hidden = sums[0].shape[1]
    piece = width // 8
    any_space = pl.BlockSpec(memory_space=pl.ANY)
    vmem = pl.BlockSpec(memory_space=pltpu.VMEM)
    dma = pltpu.SemaphoreType.DMA
    blocks = [(piece, hidden), (piece, hidden), (hidden, piece), mine_o.shape, mine_q.shape]
    terms = (1, 1, 1, 3, 3)
    outs = [shape(out.shape, BF16), shape(out.shape, F32)] + [shape(b, F32) for b in blocks[:4]]
    outs += [shape((piece, size), F32) for size in (nqc, nkc, nkc)]
    tiny = [shape((size,), F32) for size in (piece, piece, hd, hd)]
    token = pltpu.VMEM((share, width), BF16)
    return pl.pallas_call(
        functools.partial(results_kernel, hd, nqc, nkc, float(width)),
        in_specs=[any_space] * 16 + [vmem] * 3,
        out_specs=[any_space] * len(outs) + [vmem] * 4 + [SMEM],
        out_shape=outs + tiny + [shape((3,), F32)],
        scratch_shapes=[pltpu.VMEM((n,) + tuple(b), BF16) for n, b in zip(terms, blocks)]
        + [pltpu.VMEM(b, F32) for b in blocks]
        + [pltpu.VMEM((share, width), F32), token, token, token, token, pltpu.VMEM(early.shape, F32), pltpu.VMEM(out.shape, BF16)]
        + [dma((5, 3)), dma((5,)), dma((5, 3)), dma((8,)), dma((4,))],
        compiler_params=PARAMS,
        cost_estimate=cost(30 * piece * hidden, 40 * piece * hidden),
        name="results",
    )(*sums, mine_o, *lands_o, mine_q, *lands_q, gh, xr, fin, finb, own, out, early, gains, lines, small)


def per_device_general(
    inputs,
    cotangent,
    lengths,
    w_query,
    key_projection_weight,
    value_projection_weight,
    w_output,
    w_gate,
    w_up,
    w_down,
    attn_gain,
    ffn_gain,
    query_gain,
    key_gain,
):
    seqs, span, width = inputs.shape
    hd = query_gain.shape[0]
    nq = w_query.shape[1] // hd
    nk = key_projection_weight.shape[1] // hd
    groups = nq // nk
    dp = lax.axis_size("dp")
    tensor = lax.axis_size("tensor")
    core = lax.axis_index("context")
    rank = lax.axis_index("tensor")
    chunks = 2
    rows = span // chunks
    share = span // tensor
    lengths = lengths.astype(jnp.int32)
    start = (core * span).astype(jnp.int32)
    core1 = core.astype(jnp.int32).reshape(1)
    ids = block_order(dp, core)
    order = 2 * dp if (width // (2 * dp)) % 128 == 0 else 1

    positions = start + jnp.arange(span, dtype=jnp.int32)
    freqs = rope_base ** (-(jnp.arange(hd // 2, dtype=F32) * (2.0 / hd)))
    angles = freqs[:, None] * positions.astype(F32)[None, :]
    cosine, sine = jnp.cos(angles), jnp.sin(angles)
    qgain = query_gain.astype(F32).reshape(hd, 1)
    kgain = key_gain.astype(F32).reshape(hd, 1)

    w_qkv = jnp.concatenate([w_query, key_projection_weight, value_projection_weight], axis=1)
    saved = []
    gains = gather_blocks(jnp.stack([attn_gain, ffn_gain]), 1)
    gains = jnp.concatenate([gains[0], gains[1]], axis=1).astype(F32)
    gain1, gain2 = gains[0:1], gains[1:2]
    qkv = gather_blocks(w_qkv, 0)
    out_w = gather_blocks(w_output, 1)
    gate = gather_blocks(w_gate, 0)
    up = gather_blocks(w_up, 0)
    down = gather_blocks(w_down, 1)

    scal = jnp.concatenate([lengths, start.reshape(1), ids])
    x_in, cot_in = inputs, cotangent
    if order == 1:
        x_in, cot_in = to_relative(x_in, dp, core), to_relative(cot_in, dp, core)
    xr, n1, gf = begin(x_in, cot_in, gain1, scal, order)

    parts, tok = [], []
    for s in range(seqs):
        pre, own, oth = heads(n1, s, qkv, cosine, sine, qgain, kgain, core1, hd, nq, nk)
        seq_scal = jnp.stack([lengths[s], core.astype(jnp.int32)])
        everything, att, inv, mine, theirs = attend(seq_scal, own, over_core(oth), groups)
        branched = branch(mine, over_core(theirs), out_w, core1, chunks)
        saved.append((pre, everything, att, inv, seq_scal))
        tok.append(jnp.swapaxes(branched[0], 0, 1))
        parts.append(branched[1:])
    tok = jnp.concatenate(tok, axis=0)

    stats = jnp.zeros((2,), F32)
    hidden_all, n2_all = [], []
    for s in range(seqs):
        for k in range(chunks):
            terms = [lax.psum(parts[s][k], "tensor")]
            place = jnp.stack([lengths[s], start + k * rows])
            hidden, n2, stat = second_norm(place, xr, s, k, gain2, terms)
            hidden_all.append(hidden)
            n2_all.append(n2)
            stats = stats + stat[:2, 0]
    hidden_all, n2_all = jnp.concatenate(hidden_all), jnp.concatenate(n2_all)

    ffn_squares = jnp.zeros((), F32)
    out_shares = []

    def piece_of(arrays):
        per = arrays[0].shape[0] // share

        def piece(k):
            found = lax.dynamic_slice_in_dim(arrays[0], jnp.minimum(k, per - 1) * share, share, 0)
            for m in range(1, len(arrays)):
                here = lax.dynamic_slice_in_dim(arrays[m], jnp.clip(k - m * per, 0, per - 1) * share, share, 0)
                found = jnp.where(k >= m * per, here, found)
            return found

        return piece

    def share_scalars(s):
        head = jnp.stack([rank.astype(jnp.int32), lengths[s], start + rank.astype(jnp.int32) * share, jnp.int32(tensor)])
        return jnp.concatenate([head, ids])

    def flat(nested):
        return [item for inner_list in nested for item in inner_list]

    def slices(array, count):
        size = array.shape[0] // count
        return [array[i * size : (i + 1) * size] for i in range(count)]

    def reduced(lefts, rights, axis):
        oth = weight_grad(lefts, rights, 1, axis)
        own = weight_grad(lefts, rights, 0, axis, over_core(oth))
        return scatter_blocks(own, axis)

    inner, gg, gu, ffn, gn = [[[None] * chunks for _ in range(seqs)] for _ in range(5)]
    for s in range(seqs):
        for k in range(chunks):
            inner[s][k], gg[s][k], gu[s][k], ffn[s][k], gn[s][k] = feed(
                n2_all, s * chunks + k, rows, gf, s, k, gate, up, down
            )
    gain2_grad = jnp.zeros((1, width), F32)
    gb, gh = [[[None] * chunks for _ in range(seqs)] for _ in range(2)]
    for s in range(seqs):
        for k in range(chunks):
            terms = [lax.psum(gn[s][k], "tensor")]
            gb[s][k], gh[s][k], gain_part = second_back(hidden_all, s * chunks + k, gf, s, k, gain2, terms)
            gain2_grad = gain2_grad + gain_part
    gf_list = slices(gf.reshape(seqs * span, width), seqs * chunks)
    n2_list = slices(n2_all, seqs * chunks)
    grad_w_down = reduced(flat(inner), gf_list, 1)
    grad_w_gate = reduced(n2_list, flat(gg), 0)
    grad_w_up = reduced(n2_list, flat(gu), 0)
    for s in range(seqs):
        got = ring_scatter(piece_of(ffn[s]), tensor, rank)
        halves = [hidden_all[(s * chunks + k) * rows : (s * chunks + k + 1) * rows] for k in range(chunks)]
        out, stat = output_share(share_scalars(s), got, ffn[s], halves, order)
        out_shares.append(out)
        ffn_squares = ffn_squares + stat[0, 0]

    gain1_grad = jnp.zeros((1, width), F32)
    head_gain = jnp.zeros((2 * hd,), F32)
    dpres, in_shares = [], []
    for s in range(seqs):
        pre, everything, att, inv, seq_scal = saved[s]
        da_own, da_oth = branch_back(gb[s], out_w, core1)
        d_own, d_oth = attend_back(seq_scal, everything, att, inv, da_own, over_core(da_oth), groups)
        dpre, first, gain_part, hg = heads_back(
            d_own, over_core(d_oth), pre, cosine, sine, qgain, kgain, xr, s, qkv, core1, hd, nq, nk
        )
        gain1_grad = gain1_grad + gain_part
        head_gain = head_gain + hg[:, 0]
        dpres.append(dpre)
        got = ring_scatter(piece_of([first]), tensor, rank)
        in_shares.append(input_share(share_scalars(s), got, first, gh[s], xr, s, gain1, order))

    att_list = [tok[i * rows : (i + 1) * rows] for i in range(seqs * chunks)]
    grad_w_output = reduced(att_list, flat(gb), 1)
    grad_qkv = reduced([n1[s] for s in range(seqs)], dpres, 0)
    nqc, nkc = nq * hd, nk * hd
    grad_w_query = grad_qkv[:, :nqc]
    grad_w_key = grad_qkv[:, nqc : nqc + nkc]
    grad_w_value = grad_qkv[:, nqc + nkc :]

    gain2_grad = gain2_grad / tensor
    counts = jnp.sum(jnp.clip(lengths - start, 0, span)).astype(F32) / tensor
    small = jnp.concatenate([head_gain, stats / tensor, ffn_squares.reshape(1), counts.reshape(1)])
    small = jnp.pad(small, (0, (-small.shape[0]) % 128)).reshape(1, -1)
    lines = jnp.concatenate([gain1_grad, gain2_grad], axis=0)
    piece = width // (2 * dp)
    lines = to_absolute(lines, dp, core)
    lines, small = lax.psum((lines, small), ("dp", "context", "tensor"))
    lines = lax.dynamic_slice_in_dim(lines, lax.axis_index(("dp", "context")) * piece, piece, 1)
    small = small[0]
    rms_values = jnp.sqrt(small[2 * hd : 2 * hd + 3] / (small[2 * hd + 3] * width))

    output = jnp.stack(out_shares)
    grad_inputs = jnp.stack(in_shares)
    if order == 1:
        output, grad_inputs = to_absolute(output, dp, core), to_absolute(grad_inputs, dp, core)
    return (
        output,
        grad_inputs,
        grad_w_query,
        grad_w_key,
        grad_w_value,
        grad_w_output,
        grad_w_gate,
        grad_w_up,
        grad_w_down,
        lines[0],
        lines[1],
        small[:hd],
        small[hd : 2 * hd],
        rms_values,
    )


def per_device_square(
    inputs,
    cotangent,
    lengths,
    w_query,
    key_projection_weight,
    value_projection_weight,
    w_output,
    w_gate,
    w_up,
    w_down,
    attn_gain,
    ffn_gain,
    query_gain,
    key_gain,
):
    seqs, span, width = inputs.shape
    hd = query_gain.shape[0]
    nq = w_query.shape[1] // hd
    nk = key_projection_weight.shape[1] // hd
    lengths = lengths.astype(jnp.int32)
    all_gains = (attn_gain, ffn_gain, query_gain, key_gain)
    (
        xr, n1, gf, qkv, out_w, gate, up, down, hidden, n2, rest, came, gi, pre, everything, att, tok, gains, table, inv, stat
    ) = forward(
        lengths, inputs, cotangent, w_query, key_projection_weight, value_projection_weight, w_output, w_gate, w_up, w_down,
        all_gains, hd, nq, nk,
    )
    tokens = seqs * span
    flat = lambda a: a.reshape(tokens, -1)
    ffn, gb, gh, d_gate, d_up, d_down, hidden, landx, landy, ring, gain2_part, stat2 = feed_both(
        lengths, n2, flat(gf), gate, up, down, gi, rest, came, flat(xr), hidden, gains
    )
    (
        output, early, fin, finb, own, sum_gate, sum_up, sum_down, mine_o, mine_q, _, _, _, _, lx3, ly3, lx4, ly4, lines, small
    ) = backward(
        lengths, gb, hidden, ffn, ring, xr, flat(n1), flat(tok), out_w, qkv,
        everything, att, inv, pre, gh, d_gate, landx, landy, d_up, d_down, table, gains, stat, stat2, gain2_part, hd, nq, nk,
    )
    nqc, nkc = nq * hd, nk * hd
    output, grad_inputs, grad_gate, grad_up, grad_down, grad_out, grad_q, grad_k, grad_v, *small = finish_results(
        (sum_gate, sum_up, sum_down), mine_o, mine_q, (lx3, ly3), (lx4, ly4), gh, xr, fin, finb, own, output, early, gains,
        lines, small, hd, nqc, nkc,
    )
    return (output, grad_inputs, grad_q, grad_k, grad_v, grad_out, grad_gate, grad_up, grad_down, *small)


def per_device(*args):
    inputs, w_query = args[0], args[3]
    seqs, span, width = inputs.shape
    square = lax.axis_size("dp") == 4 and lax.axis_size("tensor") == 4 and lax.axis_size("context") == 2
    if square and width % 2048 == 0 and span % 512 == 0 and seqs == 2 and w_query.shape[1] == span:
        return per_device_square(*args)
    return per_device_general(*args)


def solution(mesh):
    both = ("dp", "context")
    rows = P(both, "tensor")
    cols = P("tensor", both)
    shares = P("dp", ("context", "tensor"), None)
    acts = P("dp", "context", None)
    return jax.shard_map(
        per_device,
        mesh=mesh,
        in_specs=(acts, acts, P("dp"), rows, rows, rows, cols, rows, rows, cols, P(both), P(both), P(), P()),
        out_specs=(shares, shares, rows, rows, rows, cols, rows, rows, cols, P(both), P(both), P(), P(), P()),
        check_vma=False,
    )
```
